32 devices in a mesh: dp: 4 (over y, x), tensor: 8 (over z, core).
Axes of the slice: x: 2, y: 2, z: 4, core: 2. Of those that a mesh axis runs over, the one named last changes fastest.
Arguments:
- hidden_states: bfloat16 [1024, 2048], P(('dp', 'tensor')), may hold values from -36 to 36
- attention_gain: float32 [2048], replicated, may hold values from 0.4 to 2.5
- feedforward_gain: float32 [2048], replicated, may hold values from 0.4 to 2.5
- heads_weight: bfloat16 [2048, 6144], P(None, 'tensor'), may hold values from -1.9887378 to 1.9887378
- output_weight: bfloat16 [2048, 2048], P('tensor'), may hold values from -0.125 to 0.125
- upward_weight: bfloat16 [2048, 8192], P(None, 'tensor'), may hold values from -0.125 to 0.125
- downward_weight: bfloat16 [8192, 2048], P('tensor'), may hold values from -0.0625 to 0.0625
- segments: int32 [4, 256], P('dp'), may hold values from 0 to 7, never falling along the last dimension, each value on 1 to 128 neighbouring positions
- page_targets: int32 [64, 1], P('dp'), may hold values from 0 to 3; in each aligned block of 16 rows (0 to 15, 16 to 31, ...) at most 8 rows name the same one
Outputs:
- layer_output: float32 [1024, 2048], P(('dp', 'tensor'))
- cache_pages: bfloat16 [4, 4, 8, 16, 4096], P('dp', None, None, None, 'tensor')
The draws below stay inside these ranges and needn't reach their ends.
Inputs may be any that keep to these rules, and one draw needn't show every extreme that they name: `segments`: in each group's row the numbers never fall, every number below 8 occurs, no prompt has more than 128 tokens, and one has exactly 128. `page_targets`: among the 16 pages of one request group no target is named more than 8 times, a bound that some block reaches.
All inputs are finite; a program needn't handle non-finite values.
Results may differ from the reference program's by a relative error of at most 0.011.
Values may be sent and summed in bfloat16 or wider, within the bound.
No kernel may reach another device: no remote copies, remote signals or barrier semaphores. Data moves between devices by JAX's collectives and lax.ppermute only.
A program may use at most 64 MiB of HBM per device.

```python
import math
import jax
import jax.numpy as jnp
import numpy as np
from jax import lax

D = 2048
H = 8
HD = 256
FF = 8192
ROT = 64
TOK = 256
NSEG = 8
PAGE = 16
TOKENS = 1024
SEGMAX = 128
PAGES = 16
MOST = 8
QUARTERS = 1
HQ = 256
FF_DEV = 1024
N_DP = 4
N_TENSOR = 8


def draw_hidden_states(key, part):
    normal_key = jax.random.fold_in(key, 11)
    row_key = jax.random.fold_in(key, 12)
    column_key = jax.random.fold_in(key, 13)
    column_scale = jnp.exp(jax.random.uniform(column_key, (1, D), jnp.float32, math.log(0.3), math.log(3.0)))
    row_scale = jnp.exp(jax.random.uniform(row_key, (TOKENS, 1), jnp.float32, math.log(0.5), math.log(2.0)))
    values = jax.random.truncated_normal(normal_key, -4.0, 4.0, (TOKENS, D), jnp.float32)
    return (values * row_scale * column_scale).astype(jnp.bfloat16)


def draw_heads_weight(key, part):
    query_key = jax.random.fold_in(key, 21)
    keys_key = jax.random.fold_in(key, 22)
    value_key = jax.random.fold_in(key, 23)
    factor = D ** (-0.5)
    query_part = jax.random.truncated_normal(query_key, -4.0, 4.0, (D, H, HD), jnp.float32) * factor
    keys_part = jax.random.truncated_normal(keys_key, -4.0, 4.0, (D, H, HD), jnp.float32) * factor
    value_part = jax.random.truncated_normal(value_key, -4.0, 4.0, (D, H, HD), jnp.float32) * factor
    stacked = jnp.stack([query_part.reshape(D, H, QUARTERS, HQ), keys_part.reshape(D, H, QUARTERS, HQ), value_part.reshape(D, H, QUARTERS, HQ)], axis=3)
    return stacked.reshape(D, 3 * H * HD).astype(jnp.bfloat16)


def block_scale(rng, extent, shards, least, high):
    level, own = 1.0, jax.random.fold_in(rng, 6)
    for position, parts in shards:
        draws = jnp.exp(jax.random.uniform(jax.random.fold_in(own, position), (parts,), jnp.float32, least / len(shards), high / len(shards)))
        level = level * jnp.repeat(draws, extent[position] // parts).reshape([-1 if axis == position else 1 for axis in range(len(extent))])
    return level


def split_up(count, total, reach, skew):
    portions = [(1 << 20) // math.isqrt(standing ** skew) + 1 for standing in range(2, count + 1)]
    spare, given = total - reach - (count - 1), [1] * (count - 1)
    while spare > 0:
        free = [i for i in range(count - 1) if given[i] < reach]
        whole, left = sum([portions[i] for i in free]), spare
        for i in free:
            addition = min(reach - given[i], max(1, left * portions[i] // whole), spare)
            given[i] = given[i] + addition
            spare = spare - addition
    return np.array([reach] + given)


def ragged(rng, amount, total, limit, slope):
    if amount == 2:
        one = jax.random.randint(rng, (), max(1, total - limit), min(limit, total - 1) + 1)
        return jnp.stack([one, total - one])
    tallies = jnp.asarray(split_up(amount, total, limit, slope), jnp.int32)
    twos = (amount - 1) // 2
    source_of, sink = tallies[1:1 + 2 * twos:2], tallies[2:2 + 2 * twos:2]
    room = jnp.minimum(source_of - 1, limit - sink)
    moved = jax.random.randint(jax.random.fold_in(rng, 1), (twos,), 0, 1 << 20) % (room + 1)
    tallies = tallies.at[1:1 + 2 * twos:2].set(source_of - moved).at[2:2 + 2 * twos:2].set(sink + moved)
    return tallies[jax.random.permutation(jax.random.fold_in(rng, 2), amount)]


def shared_out(key, own, number, rows, count, top, reach, lean):
    sequence = jax.random.permutation(key, count)
    packed, ordinary = shares(count, rows * top, reach, lean, True), shares(count, rows * top, reach, lean, False)
    places = jnp.arange(count)

    def named(tallies, offset_by):
        used = int((tallies > 0).sum())
        fixed = max(1, used // 4)
        moved = fixed + (places - fixed + offset_by * (used - fixed)) % max(1, count - fixed)
        return jnp.zeros((count,), jnp.int32).at[sequence[jnp.where(places < fixed, places, moved)]].set(jnp.asarray(tallies, jnp.int32))

    tallies = jnp.where(number % 4 == 0, named(packed, number // 4), named(ordinary, number - number // 4 - 1))
    mixed = jax.random.permutation(jax.random.fold_in(own, 3), count)
    donor, taker = mixed[0:count // 2 * 2:2], mixed[1:count // 2 * 2:2]
    slack = jnp.minimum(tallies[donor] - 1, reach - tallies[taker]) // 2
    slack = jnp.where((donor == sequence[0]) | (taker == sequence[0]) | (tallies[taker] == 0), 0, jnp.maximum(slack, 0))
    moved = jax.random.randint(jax.random.fold_in(own, 4), (count // 2,), 0, 1 << 20) % (slack + 1)
    tallies = tallies.at[donor].add(-moved).at[taker].add(moved)
    items = jnp.searchsorted(jnp.cumsum(tallies), jnp.arange(rows * top), side="right").astype(jnp.int32)
    listing = items.reshape(top, rows).T
    listing = listing[jax.random.permutation(jax.random.fold_in(own, 1), rows)]
    offset_by = jax.random.randint(jax.random.fold_in(own, 2), (rows, 1), 0, top)
    return jnp.take_along_axis(listing, (jnp.arange(top)[None, :] + offset_by) % top, axis=1)


def shares(number_of, total, most, lean, full):
    portions = [(1 << 20) // math.isqrt(standing ** lean) + 1 for standing in range(1, number_of + 1)]
    largest = most if full else min(most, max(-(-total // number_of), total * portions[0] // sum(portions)))
    least = 1 if total - largest >= number_of - 1 else 0
    counts, rest = [largest] + [least] * (number_of - 1), total - largest - least * (number_of - 1)
    while rest > 0:
        free = [i for i in range(1, number_of) if counts[i] < largest] or [i for i in range(1, number_of) if counts[i] < most]
        pool, budget = sum([portions[i] for i in free]), rest
        for i in free:
            more = min(most - counts[i], max(1, budget * portions[i] // pool), rest)
            counts[i] = counts[i] + more
            rest = rest - more
    return np.array(counts)


def gaussian(key, dims, scale, bound, cuts=(), kind=jnp.bfloat16):
    drawn = jax.random.normal(key, dims, jnp.float32) * scale
    if len(cuts) > 0:
        drawn = block_scale(key, dims, cuts, -0.22, 0.18) * drawn
    return jnp.clip(drawn, min=-bound, max=bound).astype(kind)


def setup_inputs(seed: int = 0) -> dict:
    splits = jax.random.split(jax.random.key(seed), 10)
    hidden_states = draw_hidden_states(jax.random.fold_in(splits[9], 71), 0)
    attention_gain = jnp.clip(jnp.exp(jax.random.uniform(splits[1], (D,), jnp.float32, math.log(0.4), math.log(2.5))), 0.4, 2.5)
    feedforward_gain = jnp.clip(jnp.exp(jax.random.uniform(splits[2], (D,), jnp.float32, math.log(0.4), math.log(2.5))), 0.4, 2.5)
    heads_weight = draw_heads_weight(jax.random.fold_in(splits[9], 71), 0)
    output_weight = gaussian(splits[4], (H * HD, D), (H * HD) ** -0.5, 0.125, ((0, 8),))
    upward_weight = gaussian(splits[5], (D, FF), D ** -0.5, 0.125, ((1, 8),))
    downward_weight = gaussian(splits[6], (FF, D), FF ** -0.5, 0.0625, ((0, 8),))
    segments = jax.vmap(lambda own: jnp.searchsorted(jnp.cumsum(ragged(own, NSEG, TOK, SEGMAX, 2)), jnp.arange(TOK), side="right"))(jax.random.split(splits[7], N_DP)).reshape((N_DP, TOK)).astype(jnp.int32)
    page_targets_keys = jax.random.split(jax.random.fold_in(splits[8], 1), (N_DP * PAGES) // PAGES)
    page_targets_turns = jax.random.permutation(jax.random.fold_in(splits[8], 3), (N_DP * PAGES) // PAGES)
    page_targets = jax.vmap(lambda own, number: shared_out(jax.random.fold_in(splits[8], 2), own, number, PAGES, N_DP, 1, MOST, 1))(page_targets_keys, page_targets_turns).reshape((N_DP * PAGES, 1))
    return dict(hidden_states=hidden_states, attention_gain=attention_gain, feedforward_gain=feedforward_gain, heads_weight=heads_weight, output_weight=output_weight, upward_weight=upward_weight, downward_weight=downward_weight, segments=segments, page_targets=page_targets)


epsilon = 1e-05
rotary_base = 10000.0

def layer_norm(values, gain):
    floats = values.astype(jnp.float32)
    center = lax.optimization_barrier(jnp.mean(floats, axis=-1, keepdims=True))
    shifted = floats - center
    spread = lax.optimization_barrier(jnp.mean(shifted * shifted, axis=-1, keepdims=True))
    return (shifted * lax.rsqrt(spread + epsilon) * gain).astype(jnp.bfloat16)

def positions_of(stream):
    indices = jnp.arange(stream.shape[0], dtype=jnp.int32)
    boundary = jnp.concatenate([jnp.ones((1,), dtype=bool), stream[1:] != stream[:-1]])
    starting = lax.cummax(jnp.where(boundary, indices, jnp.zeros_like(indices)), axis=0)
    return (indices, starting)

def rotate_heads(vectors, offsets, rotary_dims):
    half_dims = rotary_dims // 2
    frequency = jnp.exp(jnp.arange(half_dims, dtype=jnp.float32) * (-2.0 * math.log(rotary_base) / rotary_dims))
    angles = offsets.astype(jnp.float32)[:, None] * frequency[None, :]
    cosine = jnp.cos(angles)
    sine = jnp.sin(angles)
    floats = vectors.astype(jnp.float32)
    leading = floats[..., :half_dims]
    trailing = floats[..., half_dims:rotary_dims]
    rotated = jnp.concatenate([leading * cosine - trailing * sine, trailing * cosine + leading * sine, floats[..., rotary_dims:]], axis=-1)
    return rotated.astype(jnp.bfloat16)

def attend_head(queries, keys, values, stream, indices):
    scores = jnp.dot(queries, keys.T, preferred_element_type=jnp.float32) * HD ** (-0.5)
    allowed = (stream[None, :] == stream[:, None]) & (indices[None, :] <= indices[:, None])
    peak = lax.optimization_barrier(jnp.max(jnp.where(allowed, scores, -jnp.inf), axis=1, keepdims=True))
    weights = jnp.where(allowed, jnp.exp(scores - peak), 0.0)
    weight_sum = lax.optimization_barrier(jnp.sum(weights, axis=1, keepdims=True))
    mixed = jnp.dot(weights.astype(jnp.bfloat16), values, preferred_element_type=jnp.float32) / weight_sum
    return mixed.astype(jnp.bfloat16)

def reference(hidden_states, attention_gain, feedforward_gain, heads_weight, output_weight, upward_weight, downward_weight, segments, page_targets):
    group_tokens = hidden_states.reshape(N_DP, TOK, D)
    group_targets = page_targets.reshape(N_DP, PAGES)

    def one_group(inputs):
        tokens, stream, targets = inputs
        normed_attention = layer_norm(tokens, attention_gain)
        normed_feedforward = layer_norm(tokens, feedforward_gain)
        joined = jnp.dot(normed_attention, heads_weight, preferred_element_type=jnp.float32).astype(jnp.bfloat16)
        components = joined.reshape(TOK, H, QUARTERS, 3, HQ).transpose(3, 1, 0, 2, 4).reshape(3, H, TOK, HD)
        indices, starting = positions_of(stream)
        offsets = indices - starting
        queries = rotate_heads(components[0], offsets, ROT)
        keys = rotate_heads(components[1], offsets, ROT)
        values = components[2]

        def per_head(trio):
            return attend_head(trio[0], trio[1], trio[2], stream, indices)
        mixed = lax.map(per_head, (queries, keys, values))
        attended = mixed.transpose(1, 0, 2).reshape(TOK, H * HD)
        hidden = jax.nn.gelu(jnp.dot(normed_feedforward, upward_weight, preferred_element_type=jnp.float32), approximate=False).astype(jnp.bfloat16)
        groups = (attended.reshape(TOK, N_TENSOR, HQ).transpose(1, 0, 2), output_weight.reshape(N_TENSOR, HQ, D), hidden.reshape(TOK, N_TENSOR, FF_DEV).transpose(1, 0, 2), downward_weight.reshape(N_TENSOR, FF_DEV, D))

        def add_group(running, group):
            term = jnp.dot(group[0], group[1], preferred_element_type=jnp.float32) + jnp.dot(group[2], group[3], preferred_element_type=jnp.float32)
            rounded = lax.optimization_barrier(term.astype(jnp.bfloat16))
            return (running + rounded.astype(jnp.float32), None)
        summed, unused = lax.scan(add_group, jnp.zeros((TOK, D), jnp.float32), groups)
        output = tokens.astype(jnp.float32) + summed
        keyed = keys.reshape(H, TOK, QUARTERS, HQ)
        valued = values.reshape(H, TOK, QUARTERS, HQ)
        rows = jnp.stack([keyed, valued], axis=3).transpose(1, 0, 2, 3, 4).reshape(PAGES, PAGE, 2 * H * HD)
        page_numbers = jnp.arange(PAGES, dtype=jnp.int32)
        earlier = lax.optimization_barrier(jnp.sum(((targets[None, :] == targets[:, None]) & (page_numbers[None, :] < page_numbers[:, None])).astype(jnp.int32), axis=1)).astype(jnp.int32)
        slots = jnp.zeros((N_DP, MOST, PAGE, 2 * H * HD), jnp.bfloat16).at[targets, earlier].set(rows)
        return (output, slots)
    outputs, slots = lax.map(one_group, (group_tokens, segments, group_targets))
    return (outputs.reshape(TOKENS, D), slots.transpose(1, 0, 2, 3, 4))
```

```python
import functools
import math

import jax
import jax.numpy as jnp
from jax import lax
from jax.experimental import pallas as pl
from jax.experimental.pallas import tpu as pltpu
from jax.sharding import PartitionSpec as P

H = 8
HD = 256
ROT = 64
PAGE = 16


epsilon = 1e-05
rotary_base = 10000.0
key_block = 256


def shortened(array):

    def short(part):
        return part.astype(jnp.bfloat16) if part.dtype == jnp.float32 else part

    return jax.tree.map(short, array)


def swapped(block, axis, apart):
    count = lax.axis_size(axis)
    route = []
    for low in range(count):
        high = low | 1 << apart
        if high != low and high < count:
            route += [(low, high), (high, low)]
    return lax.ppermute(block, axis, route)


def layer_norm(values, gain):
    floats = values.astype(jnp.float32)
    center = jnp.mean(floats, axis=-1, keepdims=True)
    shifted = floats - center
    spread = jnp.mean(shifted * shifted, axis=-1, keepdims=True)
    return (shifted * lax.rsqrt(spread + epsilon) * gain).astype(jnp.bfloat16)


def positions_of(stream):
    indices = jnp.arange(stream.shape[0], dtype=jnp.int32)
    boundary = jnp.concatenate([jnp.ones((1,), dtype=bool), stream[1:] != stream[:-1]])
    starting = lax.cummax(jnp.where(boundary, indices, jnp.zeros_like(indices)), axis=0)
    return (indices, starting)


def rotate_heads(vectors, offsets, rotary_dims):
    half_dims = rotary_dims // 2
    frequency = jnp.exp(
        jnp.arange(half_dims, dtype=jnp.float32) * (-2.0 * math.log(rotary_base) / rotary_dims)
    )
    angles = offsets.astype(jnp.float32)[:, None] * frequency[None, :]
    cosine = jnp.cos(angles)
    sine = jnp.sin(angles)
    floats = vectors.astype(jnp.float32)
    leading = floats[..., :half_dims]
    trailing = floats[..., half_dims:rotary_dims]
    rotated = jnp.concatenate(
        [
            leading * cosine - trailing * sine,
            trailing * cosine + leading * sine,
            floats[..., rotary_dims:],
        ],
        axis=-1,
    )
    return rotated.astype(jnp.bfloat16)


def shards_split_heads(
    hidden_states,
    attention_gain,
    feedforward_gain,
    heads_weight,
    output_weight,
    upward_weight,
    downward_weight,
    segments,
    page_targets,
):
    tensor_count = lax.axis_size("tensor")
    replica_count = lax.axis_size("dp")
    tensor_index = lax.axis_index("tensor")
    quarters = tensor_count // H
    quarter_width = HD // quarters
    quarter_index = tensor_index % quarters
    stream = segments[0]
    tokens_total = stream.shape[0]
    level_count = quarters.bit_length() - 1
    normed_attention = layer_norm(hidden_states, attention_gain)
    normed_feedforward = layer_norm(hidden_states, feedforward_gain)
    shard_rows = lax.all_gather(
        (normed_attention, normed_feedforward), "tensor", axis=0, tiled=True
    )
    joined_rows = jnp.dot(shard_rows[0], heads_weight, preferred_element_type=jnp.float32).astype(
        jnp.bfloat16
    )
    upward = jnp.dot(shard_rows[1], upward_weight, preferred_element_type=jnp.float32)
    hidden_rows = jax.nn.gelu(upward, approximate=False).astype(jnp.bfloat16)
    hidden = hidden_rows
    pieces = (
        joined_rows.reshape(tokens_total, 3, quarter_width)
        .transpose(1, 0, 2)
        .reshape(1, 3, tokens_total * quarter_width)
    )
    for bit_number in range(level_count):
        partner = swapped(shortened(pieces), "tensor", bit_number).astype(pieces.dtype)
        lower = tensor_index >> bit_number & 1 == 0
        pieces = jnp.where(
            lower, jnp.concatenate([pieces, partner], 0), jnp.concatenate([partner, pieces], 0)
        )
    whole_head = (
        pieces.reshape(quarters, 3, tokens_total, quarter_width)
        .transpose(1, 2, 0, 3)
        .reshape(3, tokens_total, HD)
    )
    indices, starting = positions_of(stream)
    offsets = indices - starting
    queries = rotate_heads(whole_head[0], offsets, ROT)
    keys = rotate_heads(whole_head[1], offsets, ROT)
    values = whole_head[2]
    block_rows = tokens_total // (2 * quarters)
    score_scale = HD ** (-0.5)

    def attend_block(block_number):
        first_row = block_number * block_rows
        block_queries = lax.dynamic_slice_in_dim(queries, first_row, block_rows, 0)
        query_segments = lax.dynamic_slice_in_dim(stream, first_row, block_rows, 0)
        query_indices = first_row + jnp.arange(block_rows, dtype=jnp.int32)
        lowest = lax.dynamic_index_in_dim(starting, first_row, 0, keepdims=False) // key_block
        highest = (first_row + block_rows + key_block - 1) // key_block

        def scores_of(key_number):
            key_first = key_number * key_block
            key_indices = key_first + jnp.arange(key_block, dtype=jnp.int32)
            scores = (
                jnp.dot(block_queries, keys.T, preferred_element_type=jnp.float32) * score_scale
            )
            allowed = (stream[None, :] == query_segments[:, None]) & (
                key_indices[None, :] <= query_indices[:, None]
            )
            return (scores, allowed)

        def find_peak(key_number, peak):
            scores, allowed = scores_of(key_number)
            return jnp.maximum(peak, jnp.max(jnp.where(allowed, scores, -jnp.inf), axis=1))

        peak = lax.fori_loop(
            lowest, highest, find_peak, jnp.full((block_rows,), -jnp.inf, jnp.float32)
        )

        def accumulate(key_number, state):
            weight_sum, mixed_sum = state
            scores, allowed = scores_of(key_number)
            weights = jnp.where(allowed, jnp.exp(scores - peak[:, None]), 0.0)
            mixed_next = mixed_sum + jnp.dot(
                weights.astype(jnp.bfloat16), values, preferred_element_type=jnp.float32
            )
            return (weight_sum + jnp.sum(weights, axis=1), mixed_next)

        start_state = (
            jnp.zeros((block_rows,), jnp.float32),
            jnp.zeros((block_rows, HD), jnp.float32),
        )
        weight_sum, mixed_sum = lax.fori_loop(lowest, highest, accumulate, start_state)
        return (mixed_sum / weight_sum[:, None]).astype(jnp.bfloat16)

    own_blocks = (2 * quarter_index, 2 * quarter_index + 1)
    own_rows = jnp.concatenate([attend_block(own_blocks[0]), attend_block(own_blocks[1])], 0)[None]
    for bit_number in range(level_count):
        partner = swapped(own_rows, "tensor", bit_number)
        lower = tensor_index >> bit_number & 1 == 0
        own_rows = jnp.where(
            lower, jnp.concatenate([own_rows, partner], 0), jnp.concatenate([partner, own_rows], 0)
        )
    attended = own_rows.reshape(tokens_total, HD)
    attended_quarter = lax.dynamic_slice_in_dim(
        attended, quarter_index * quarter_width, quarter_width, 1
    )
    hidden_rows = hidden
    summed = lax.psum_scatter(
        (
            jnp.dot(attended_quarter, output_weight, preferred_element_type=jnp.float32)
            + jnp.dot(hidden_rows, downward_weight, preferred_element_type=jnp.float32)
        ).astype(jnp.bfloat16),
        "tensor",
        scatter_dimension=0,
        tiled=True,
    ).astype(jnp.float32)
    layer_output = hidden_states.astype(jnp.float32) + summed
    key_quarter = lax.dynamic_slice_in_dim(keys, quarter_index * quarter_width, quarter_width, 1)
    value_quarter = joined_rows[:, 2 * quarter_width :]
    page_count = tokens_total // PAGE
    page_rows = jnp.concatenate([key_quarter, value_quarter], 1).reshape(
        page_count, PAGE * 2 * quarter_width
    )
    targets = page_targets[:, 0]
    page_numbers = jnp.arange(page_count, dtype=jnp.int32)
    earlier = jnp.sum(
        (
            (targets[None, :] == targets[:, None]) & (page_numbers[None, :] < page_numbers[:, None])
        ).astype(jnp.int32),
        axis=1,
    )
    capacity = 2 * page_count // replica_count
    slot_numbers = targets * capacity + earlier
    placing = (
        jnp.arange(replica_count * capacity, dtype=jnp.int32)[:, None] == slot_numbers[None, :]
    ).astype(jnp.bfloat16)
    outgoing = jnp.dot(placing, page_rows, preferred_element_type=jnp.float32).astype(jnp.bfloat16)
    outgoing = outgoing.reshape(replica_count, capacity, PAGE * 2 * quarter_width)
    incoming = lax.all_to_all(outgoing, "dp", split_axis=0, concat_axis=0, tiled=True)
    cache_pages = incoming.reshape(1, replica_count, capacity, PAGE, 2 * quarter_width)
    return (layer_output, cache_pages)


CORES = 2
MIB = 1 << 20


def in_vmem(array):
    return pltpu.with_memory_space_constraint(array, pltpu.VMEM)


def exchanged(block, axis, mask):
    count = lax.axis_size(axis)
    return lax.ppermute(block, axis, [(member, member ^ mask) for member in range(count)])


def vmem_specs(count):
    return [pl.BlockSpec(memory_space=pltpu.VMEM)] * count


def prepare_kernel(segments_ref, offsets_ref, cosine_ref, sine_down_ref, sine_up_ref):
    tokens = segments_ref.shape[1]
    shape = (tokens, tokens)
    rows = lax.broadcasted_iota(jnp.int32, shape, 0)
    columns = lax.broadcasted_iota(jnp.int32, shape, 1)
    across = jnp.broadcast_to(segments_ref[...], shape).astype(jnp.float32)
    down = jnp.sum(jnp.where(rows == columns, across, 0.0), axis=1, keepdims=True)
    earlier = (across == down) & (columns < rows)
    offsets = jnp.sum(jnp.where(earlier, 1.0, 0.0), axis=1, keepdims=True)
    offsets_ref[...] = jnp.broadcast_to(offsets, offsets_ref.shape)
    half = ROT // 2
    lane = lax.broadcasted_iota(jnp.int32, (tokens, 128), 1)
    step = (lane & (half - 1)).astype(jnp.float32)
    frequency = jnp.exp(step * (-2.0 * math.log(rotary_base) / ROT))
    angles = offsets * frequency
    sine = jnp.sin(angles)
    cosine_ref[...] = jnp.where(lane < ROT, jnp.cos(angles), 1.0)
    sine_down_ref[...] = jnp.where(lane < half, -sine, 0.0)
    sine_up_ref[...] = jnp.where((lane >= half) & (lane < ROT), sine, 0.0)


def prepare(segments):
    tokens = segments.shape[1]
    table = jax.ShapeDtypeStruct((tokens, 128), jnp.float32)
    return pl.pallas_call(
        prepare_kernel,
        out_shape=[table] * 4,
        in_specs=vmem_specs(1),
        out_specs=vmem_specs(4),
        compiler_params=pltpu.CompilerParams(vmem_limit_bytes=8 * MIB),
        name="prepare",
    )(segments)


def layer_kernel(
    chips,
    *refs,
):
    blocks = refs[: CORES * chips]
    (
        attention_gain_ref,
        feedforward_gain_ref,
        heads_ref,
        output_ref,
        upward_ref,
        downward_ref,
        offsets_ref,
        cosine_ref,
        sine_down_ref,
        sine_up_ref,
        targets_ref,
        sibling_ref,
        own_ref,
        *pages_refs,
    ) = refs[CORES * chips : -6]
    attention_scr, feedforward_scr, joined_scr, hidden_scr, attended_scr, counts_ref = refs[-6:]
    member = lax.axis_index("tensor")
    chip = member // CORES
    core = member % CORES
    group = lax.axis_index("dp")
    block_rows = blocks[0].shape[0]
    tokens = block_rows * CORES * chips
    piece = 16

    gain_a = attention_gain_ref[...]
    gain_f = feedforward_gain_ref[...]
    for mask in range(chips):
        for away in range(CORES):
            block_ref = blocks[mask * CORES + away]
            first = ((chip ^ mask) * CORES + (core ^ away)) * block_rows
            for part in range(block_rows // piece):
                floats = block_ref[part * piece : (part + 1) * piece, :].astype(jnp.float32)
                center = jnp.mean(floats, axis=-1, keepdims=True)
                shifted = floats - center
                spread = jnp.mean(shifted * shifted, axis=-1, keepdims=True)
                scaled = shifted * lax.rsqrt(spread + epsilon)
                place = pl.ds(pl.multiple_of(first + part * piece, piece), piece)
                attention_scr[place, :] = (scaled * gain_a).astype(jnp.bfloat16)
                feedforward_scr[place, :] = (scaled * gain_f).astype(jnp.bfloat16)

    normed = attention_scr[...]
    cosine = cosine_ref[...]
    sine_down = sine_down_ref[...]
    sine_up = sine_up_ref[...]
    for component in range(3):
        columns = slice(component * HD, (component + 1) * HD)
        joined = jnp.dot(
            normed, heads_ref[:, columns], preferred_element_type=jnp.float32
        ).astype(jnp.bfloat16)
        joined_scr[:, columns] = joined
        if component < 2:
            turning = joined[:, :128].astype(jnp.float32)
            turned = (
                turning * cosine
                + pltpu.roll(turning, 128 - ROT // 2, 1) * sine_down
                + pltpu.roll(turning, ROT // 2, 1) * sine_up
            )
            joined_scr[:, component * HD : component * HD + 128] = turned.astype(jnp.bfloat16)

    for page_ref in pages_refs:
        page_ref[...] = jnp.zeros(page_ref.shape, page_ref.dtype)
    capacity = pages_refs[0].shape[0]
    for target in range(len(pages_refs)):
        counts_ref[target] = 0
    for page in range(tokens // PAGE):
        target = targets_ref[page]
        slot = counts_ref[target]
        counts_ref[target] = slot + 1
        slot = jnp.minimum(slot, capacity - 1)
        rows = joined_scr[page * PAGE : (page + 1) * PAGE, HD:]
        for mask, page_ref in enumerate(pages_refs):

            @pl.when(target == (group ^ mask))
            def _():
                page_ref[pl.ds(slot, 1)] = rows[None]

    shape = (tokens, tokens)
    row = lax.broadcasted_iota(jnp.int32, shape, 0)
    column = lax.broadcasted_iota(jnp.int32, shape, 1)
    reach = offsets_ref[:, :1].astype(jnp.int32)
    allowed = (column <= row) & (column >= row - reach)
    scores = lax.dot_general(
        joined_scr[:, :HD],
        joined_scr[:, HD : 2 * HD],
        (((1,), (1,)), ((), ())),
        preferred_element_type=jnp.float32,
    ) * (HD ** (-0.5))
    peak = jnp.max(jnp.where(allowed, scores, -jnp.inf), axis=1, keepdims=True)
    weights = jnp.where(allowed, jnp.exp(scores - peak), 0.0)
    weight_sum = jnp.sum(weights, axis=1, keepdims=True)
    mixed = jnp.dot(
        weights.astype(jnp.bfloat16), joined_scr[:, 2 * HD :], preferred_element_type=jnp.float32
    )
    attended_scr[...] = (mixed / weight_sum).astype(jnp.bfloat16)

    normed = feedforward_scr[...]
    chunk = 256
    for first in range(0, upward_ref.shape[1], chunk):
        columns = slice(first, first + chunk)
        upward = jnp.dot(normed, upward_ref[:, columns], preferred_element_type=jnp.float32)
        hidden = 0.5 * upward * (1.0 + lax.erf(upward * (0.5**0.5)))
        hidden_scr[:, columns] = hidden.astype(jnp.bfloat16)

    hidden = hidden_scr[...]
    attended = attended_scr[...]
    for first in range(0, downward_ref.shape[1], chunk):
        columns = slice(first, first + chunk)
        partial = jnp.dot(
            attended, output_ref[:, columns], preferred_element_type=jnp.float32
        ) + jnp.dot(hidden, downward_ref[:, columns], preferred_element_type=jnp.float32)
        partial = partial.reshape(chips, CORES, block_rows, chunk)
        even, odd = partial[:, 0], partial[:, 1]
        own = jnp.where(core == 0, even, odd)
        sibling = jnp.where(core == 0, odd, even)
        own_ref[:, :, columns] = own
        sibling_ref[:, :, columns] = sibling.astype(jnp.bfloat16)


def layer(blocks, gains, weights, tables, targets, replica_count):
    count = len(blocks)
    chips = count // CORES
    block_rows, width = blocks[0].shape
    tokens = block_rows * count
    capacity = 2 * (tokens // PAGE) // replica_count
    hidden_width = weights[2].shape[1]
    out_shape = [
        jax.ShapeDtypeStruct((chips, block_rows, width), jnp.bfloat16),
        jax.ShapeDtypeStruct((chips, block_rows, width), jnp.float32),
    ] + [jax.ShapeDtypeStruct((capacity, PAGE, 2 * HD), jnp.bfloat16)] * replica_count
    return pl.pallas_call(
        functools.partial(layer_kernel, chips),
        out_shape=out_shape,
        in_specs=vmem_specs(count + 2 + 4 + 4) + [pl.BlockSpec(memory_space=pltpu.SMEM)],
        out_specs=vmem_specs(len(out_shape)),
        scratch_shapes=[
            pltpu.VMEM((tokens, width), jnp.bfloat16),
            pltpu.VMEM((tokens, width), jnp.bfloat16),
            pltpu.VMEM((tokens, 3 * HD), jnp.bfloat16),
            pltpu.VMEM((tokens, hidden_width), jnp.bfloat16),
            pltpu.VMEM((tokens, HD), jnp.bfloat16),
            pltpu.SMEM((replica_count,), jnp.int32),
        ],
        compiler_params=pltpu.CompilerParams(vmem_limit_bytes=32 * MIB),
        cost_estimate=pl.CostEstimate(
            flops=2 * tokens * width * (3 * HD + HD + 2 * hidden_width),
            bytes_accessed=16 * MIB,
            transcendentals=tokens * (hidden_width + tokens),
        ),
        name="layer",
    )(*blocks, *gains, *weights, *tables, targets)


def reduce_kernel(chips, own_ref, sibling_ref, hidden_ref, base_ref, *out_refs):
    chip = lax.axis_index("tensor") // CORES
    base_ref[...] = (
        hidden_ref[...].astype(jnp.float32)
        + own_ref[chip]
        + sibling_ref[chip].astype(jnp.float32)
    )
    for mask in range(1, chips):
        other = chip ^ mask
        out_refs[mask - 1][...] = (
            own_ref[other] + sibling_ref[other].astype(jnp.float32)
        ).astype(jnp.bfloat16)


def reduced(own, sibling, hidden_states):
    chips, block_rows, width = own.shape
    return pl.pallas_call(
        functools.partial(reduce_kernel, chips),
        out_shape=[jax.ShapeDtypeStruct((block_rows, width), jnp.float32)]
        + [jax.ShapeDtypeStruct((block_rows, width), jnp.bfloat16)] * (chips - 1),
        in_specs=vmem_specs(3),
        out_specs=vmem_specs(chips),
        compiler_params=pltpu.CompilerParams(vmem_limit_bytes=16 * MIB),
        name="reduced",
    )(own, sibling, hidden_states)


def finish_kernel(base_ref, *refs):
    total = base_ref[...]
    for ref in refs[:-1]:
        total = total + ref[...].astype(jnp.float32)
    refs[-1][...] = total


def finished(base, parts):
    return pl.pallas_call(
        finish_kernel,
        out_shape=jax.ShapeDtypeStruct(base.shape, base.dtype),
        in_specs=vmem_specs(1 + len(parts)),
        out_specs=pl.BlockSpec(memory_space=pltpu.VMEM),
        compiler_params=pltpu.CompilerParams(vmem_limit_bytes=8 * MIB),
        name="finished",
    )(base, *parts)


def place_kernel(*refs):
    group = lax.axis_index("dp")
    page_refs, cache_ref, sems = refs[:-2], refs[-2], refs[-1]
    copies = [
        pltpu.make_async_copy(page_ref, cache_ref.at[0, group ^ mask], sems.at[mask])
        for mask, page_ref in enumerate(page_refs)
    ]
    for copy in copies:
        copy.start()
    for copy in copies:
        copy.wait()


def placed(pages):
    count = len(pages)
    return pl.pallas_call(
        place_kernel,
        out_shape=jax.ShapeDtypeStruct((1, count) + pages[0].shape, pages[0].dtype),
        in_specs=[pl.BlockSpec(memory_space=pl.ANY)] * count,
        out_specs=pl.BlockSpec(memory_space=pl.ANY),
        scratch_shapes=[pltpu.SemaphoreType.DMA((count,))],
        compiler_params=pltpu.CompilerParams(vmem_limit_bytes=8 * MIB),
        name="placed",
    )(*pages)


def shards_whole_heads(
    hidden_states,
    attention_gain,
    feedforward_gain,
    heads_weight,
    output_weight,
    upward_weight,
    downward_weight,
    segments,
    page_targets,
):
    chips = lax.axis_size("tensor") // CORES
    replica_count = lax.axis_size("dp")
    near = [hidden_states] + [
        exchanged(hidden_states, "tensor", mask * CORES) for mask in range(1, chips)
    ]
    blocks = []
    for block in near:
        blocks += [block, exchanged(block, "tensor", 1)]
    tables = prepare(segments)
    weights = (heads_weight, output_weight, upward_weight, downward_weight)
    sibling, own, *pages = layer(
        blocks,
        (attention_gain[None], feedforward_gain[None]),
        [in_vmem(weight) for weight in weights],
        tables,
        page_targets[:, 0],
        replica_count,
    )
    received = exchanged(sibling, "tensor", 1)
    base, *outgoing = reduced(own, received, hidden_states)
    incoming = [
        exchanged(block, "tensor", (mask + 1) * CORES) for mask, block in enumerate(outgoing)
    ]
    cache_pages = placed(
        [pages[0]] + [exchanged(pages[mask], "dp", mask) for mask in range(1, replica_count)]
    )
    return (finished(base, incoming), cache_pages)


def solution(mesh):
    whole_heads = mesh.shape["tensor"] == H and mesh.shape["dp"] == 4
    shards = shards_whole_heads if whole_heads else shards_split_heads
    in_specs = (
        P(("dp", "tensor"), None),
        P(),
        P(),
        P(None, "tensor"),
        P("tensor", None),
        P(None, "tensor"),
        P("tensor", None),
        P("dp", None),
        P("dp", None),
    )
    out_specs = (P(("dp", "tensor"), None), P("dp", None, None, None, "tensor"))
    return jax.shard_map(shards, mesh=mesh, in_specs=in_specs, out_specs=out_specs, check_vma=False)
```

```python
import functools
import math

import jax
import jax.numpy as jnp
from jax import lax
from jax.experimental import pallas as pl
from jax.experimental.pallas import tpu as pltpu
from jax.sharding import PartitionSpec as P

H = 8
HD = 256
ROT = 64
PAGE = 16


epsilon = 1e-05
rotary_base = 10000.0
key_block = 256


def shortened(array):

    def short(part):
        return part.astype(jnp.bfloat16) if part.dtype == jnp.float32 else part

    return jax.tree.map(short, array)


def swapped(block, axis, apart):
    count = lax.axis_size(axis)
    route = []
    for low in range(count):
        high = low | 1 << apart
        if high != low and high < count:
            route += [(low, high), (high, low)]
    return lax.ppermute(block, axis, route)


def layer_norm(values, gain):
    floats = values.astype(jnp.float32)
    center = jnp.mean(floats, axis=-1, keepdims=True)
    shifted = floats - center
    spread = jnp.mean(shifted * shifted, axis=-1, keepdims=True)
    return (shifted * lax.rsqrt(spread + epsilon) * gain).astype(jnp.bfloat16)


def positions_of(stream):
    indices = jnp.arange(stream.shape[0], dtype=jnp.int32)
    boundary = jnp.concatenate([jnp.ones((1,), dtype=bool), stream[1:] != stream[:-1]])
    starting = lax.cummax(jnp.where(boundary, indices, jnp.zeros_like(indices)), axis=0)
    return (indices, starting)


def rotate_heads(vectors, offsets, rotary_dims):
    half_dims = rotary_dims // 2
    frequency = jnp.exp(
        jnp.arange(half_dims, dtype=jnp.float32) * (-2.0 * math.log(rotary_base) / rotary_dims)
    )
    angles = offsets.astype(jnp.float32)[:, None] * frequency[None, :]
    cosine = jnp.cos(angles)
    sine = jnp.sin(angles)
    floats = vectors.astype(jnp.float32)
    leading = floats[..., :half_dims]
    trailing = floats[..., half_dims:rotary_dims]
    rotated = jnp.concatenate(
        [
            leading * cosine - trailing * sine,
            trailing * cosine + leading * sine,
            floats[..., rotary_dims:],
        ],
        axis=-1,
    )
    return rotated.astype(jnp.bfloat16)


def shards_split_heads(
    hidden_states,
    attention_gain,
    feedforward_gain,
    heads_weight,
    output_weight,
    upward_weight,
    downward_weight,
    segments,
    page_targets,
):
    tensor_count = lax.axis_size("tensor")
    replica_count = lax.axis_size("dp")
    tensor_index = lax.axis_index("tensor")
    quarters = tensor_count // H
    quarter_width = HD // quarters
    quarter_index = tensor_index % quarters
    stream = segments[0]
    tokens_total = stream.shape[0]
    level_count = quarters.bit_length() - 1
    normed_attention = layer_norm(hidden_states, attention_gain)
    normed_feedforward = layer_norm(hidden_states, feedforward_gain)
    shard_rows = lax.all_gather(
        (normed_attention, normed_feedforward), "tensor", axis=0, tiled=True
    )
    joined_rows = jnp.dot(shard_rows[0], heads_weight, preferred_element_type=jnp.float32).astype(
        jnp.bfloat16
    )
    upward = jnp.dot(shard_rows[1], upward_weight, preferred_element_type=jnp.float32)
    hidden_rows = jax.nn.gelu(upward, approximate=False).astype(jnp.bfloat16)
    hidden = hidden_rows
    pieces = (
        joined_rows.reshape(tokens_total, 3, quarter_width)
        .transpose(1, 0, 2)
        .reshape(1, 3, tokens_total * quarter_width)
    )
    for bit_number in range(level_count):
        partner = swapped(shortened(pieces), "tensor", bit_number).astype(pieces.dtype)
        lower = tensor_index >> bit_number & 1 == 0
        pieces = jnp.where(
            lower, jnp.concatenate([pieces, partner], 0), jnp.concatenate([partner, pieces], 0)
        )
    whole_head = (
        pieces.reshape(quarters, 3, tokens_total, quarter_width)
        .transpose(1, 2, 0, 3)
        .reshape(3, tokens_total, HD)
    )
    indices, starting = positions_of(stream)
    offsets = indices - starting
    queries = rotate_heads(whole_head[0], offsets, ROT)
    keys = rotate_heads(whole_head[1], offsets, ROT)
    values = whole_head[2]
    block_rows = tokens_total // (2 * quarters)
    score_scale = HD ** (-0.5)

    def attend_block(block_number):
        first_row = block_number * block_rows
        block_queries = lax.dynamic_slice_in_dim(queries, first_row, block_rows, 0)
        query_segments = lax.dynamic_slice_in_dim(stream, first_row, block_rows, 0)
        query_indices = first_row + jnp.arange(block_rows, dtype=jnp.int32)
        lowest = lax.dynamic_index_in_dim(starting, first_row, 0, keepdims=False) // key_block
        highest = (first_row + block_rows + key_block - 1) // key_block

        def scores_of(key_number):
            key_first = key_number * key_block
            key_indices = key_first + jnp.arange(key_block, dtype=jnp.int32)
            scores = (
                jnp.dot(block_queries, keys.T, preferred_element_type=jnp.float32) * score_scale
            )
            allowed = (stream[None, :] == query_segments[:, None]) & (
                key_indices[None, :] <= query_indices[:, None]
            )
            return (scores, allowed)

        def find_peak(key_number, peak):
            scores, allowed = scores_of(key_number)
            return jnp.maximum(peak, jnp.max(jnp.where(allowed, scores, -jnp.inf), axis=1))

        peak = lax.fori_loop(
            lowest, highest, find_peak, jnp.full((block_rows,), -jnp.inf, jnp.float32)
        )

        def accumulate(key_number, state):
            weight_sum, mixed_sum = state
            scores, allowed = scores_of(key_number)
            weights = jnp.where(allowed, jnp.exp(scores - peak[:, None]), 0.0)
            mixed_next = mixed_sum + jnp.dot(
                weights.astype(jnp.bfloat16), values, preferred_element_type=jnp.float32
            )
            return (weight_sum + jnp.sum(weights, axis=1), mixed_next)

        start_state = (
            jnp.zeros((block_rows,), jnp.float32),
            jnp.zeros((block_rows, HD), jnp.float32),
        )
        weight_sum, mixed_sum = lax.fori_loop(lowest, highest, accumulate, start_state)
        return (mixed_sum / weight_sum[:, None]).astype(jnp.bfloat16)

    own_blocks = (2 * quarter_index, 2 * quarter_index + 1)
    own_rows = jnp.concatenate([attend_block(own_blocks[0]), attend_block(own_blocks[1])], 0)[None]
    for bit_number in range(level_count):
        partner = swapped(own_rows, "tensor", bit_number)
        lower = tensor_index >> bit_number & 1 == 0
        own_rows = jnp.where(
            lower, jnp.concatenate([own_rows, partner], 0), jnp.concatenate([partner, own_rows], 0)
        )
    attended = own_rows.reshape(tokens_total, HD)
    attended_quarter = lax.dynamic_slice_in_dim(
        attended, quarter_index * quarter_width, quarter_width, 1
    )
    hidden_rows = hidden
    summed = lax.psum_scatter(
        (
            jnp.dot(attended_quarter, output_weight, preferred_element_type=jnp.float32)
            + jnp.dot(hidden_rows, downward_weight, preferred_element_type=jnp.float32)
        ).astype(jnp.bfloat16),
        "tensor",
        scatter_dimension=0,
        tiled=True,
    ).astype(jnp.float32)
    layer_output = hidden_states.astype(jnp.float32) + summed
    key_quarter = lax.dynamic_slice_in_dim(keys, quarter_index * quarter_width, quarter_width, 1)
    value_quarter = joined_rows[:, 2 * quarter_width :]
    page_count = tokens_total // PAGE
    page_rows = jnp.concatenate([key_quarter, value_quarter], 1).reshape(
        page_count, PAGE * 2 * quarter_width
    )
    targets = page_targets[:, 0]
    page_numbers = jnp.arange(page_count, dtype=jnp.int32)
    earlier = jnp.sum(
        (
            (targets[None, :] == targets[:, None]) & (page_numbers[None, :] < page_numbers[:, None])
        ).astype(jnp.int32),
        axis=1,
    )
    capacity = 2 * page_count // replica_count
    slot_numbers = targets * capacity + earlier
    placing = (
        jnp.arange(replica_count * capacity, dtype=jnp.int32)[:, None] == slot_numbers[None, :]
    ).astype(jnp.bfloat16)
    outgoing = jnp.dot(placing, page_rows, preferred_element_type=jnp.float32).astype(jnp.bfloat16)
    outgoing = outgoing.reshape(replica_count, capacity, PAGE * 2 * quarter_width)
    incoming = lax.all_to_all(outgoing, "dp", split_axis=0, concat_axis=0, tiled=True)
    cache_pages = incoming.reshape(1, replica_count, capacity, PAGE, 2 * quarter_width)
    return (layer_output, cache_pages)


CORES = 2
MIB = 1 << 20


def in_hbm(array):
    return pltpu.with_memory_space_constraint(array, pltpu.HBM)


def exchanged(block, axis, mask):
    count = lax.axis_size(axis)
    return lax.ppermute(block, axis, [(member, member ^ mask) for member in range(count)])


def vmem_specs(count):
    return [pl.BlockSpec(memory_space=pltpu.VMEM)] * count


def prepare_kernel(count, segments_ref, *refs):
    sources, targets = refs[:count], refs[count : 2 * count]
    offsets_ref, cosine_ref, sine_down_ref, sine_up_ref, sems = refs[2 * count :]
    copies = []
    for number, (source, target) in enumerate(zip(sources, targets)):
        parts = 4 if source.shape[0] >= 256 else 1
        rows = source.shape[0] // parts
        for part in range(parts):
            place = pl.ds(part * rows, rows)
            copies.append(
                pltpu.make_async_copy(source.at[place], target.at[place], sems.at[number, part])
            )
    for copy in copies:
        copy.start()
    tokens = segments_ref.shape[1]
    shape = (tokens, tokens)
    rows = lax.broadcasted_iota(jnp.int32, shape, 0)
    columns = lax.broadcasted_iota(jnp.int32, shape, 1)
    across = jnp.broadcast_to(segments_ref[...], shape).astype(jnp.float32)
    down = jnp.sum(jnp.where(rows == columns, across, 0.0), axis=1, keepdims=True)
    earlier = (across == down) & (columns < rows)
    offsets = jnp.sum(jnp.where(earlier, 1.0, 0.0), axis=1, keepdims=True)
    offsets_ref[...] = jnp.broadcast_to(offsets, offsets_ref.shape)
    half = ROT // 2
    lane = lax.broadcasted_iota(jnp.int32, (tokens, 128), 1)
    step = (lane & (half - 1)).astype(jnp.float32)
    frequency = jnp.exp(step * (-2.0 * math.log(rotary_base) / ROT))
    angles = offsets * frequency
    sine = jnp.sin(angles)
    cosine_ref[...] = jnp.where(lane < ROT, jnp.cos(angles), 1.0)
    sine_down_ref[...] = jnp.where(lane < half, -sine, 0.0)
    sine_up_ref[...] = jnp.where((lane >= half) & (lane < ROT), sine, 0.0)
    for copy in copies:
        copy.wait()


def prepare(segments, staged):
    tokens = segments.shape[1]
    shapes = [pltpu.VMEM(array.shape, array.dtype) for array in staged]
    shapes += [pltpu.VMEM((tokens, 128), jnp.float32)] * 4
    count = len(staged)
    return pl.pallas_call(
        functools.partial(prepare_kernel, count),
        out_shape=shapes,
        in_specs=vmem_specs(1) + [pl.BlockSpec(memory_space=pltpu.HBM)] * count,
        out_specs=vmem_specs(len(shapes)),
        scratch_shapes=[pltpu.SemaphoreType.DMA((count, 4))],
        compiler_params=pltpu.CompilerParams(vmem_limit_bytes=8 * MIB),
        cost_estimate=pl.CostEstimate(
            flops=0, bytes_accessed=sum(array.nbytes for array in staged), transcendentals=0
        ),
        name="prepare",
    )(segments, *[in_hbm(array) for array in staged])


def layer_kernel(
    chips,
    *refs,
):
    blocks = refs[: CORES * chips]
    (
        attention_gain_ref,
        feedforward_gain_ref,
        heads_ref,
        output_ref,
        upward_ref,
        downward_ref,
        offsets_ref,
        cosine_ref,
        sine_down_ref,
        sine_up_ref,
        targets_ref,
        sibling_ref,
        own_ref,
        *pages_refs,
    ) = refs[CORES * chips : -8]
    attention_scr, feedforward_scr, joined_scr, hidden_scr, attended_scr = refs[-8:-3]
    named_ref, counts_ref, sem = refs[-3:]
    naming = pltpu.make_async_copy(targets_ref, named_ref, sem)
    naming.start()
    member = lax.axis_index("tensor")
    chip = member // CORES
    core = member % CORES
    group = lax.axis_index("dp")
    block_rows = blocks[0].shape[0]
    tokens = block_rows * CORES * chips
    piece = 16

    gain_a = attention_gain_ref[...]
    gain_f = feedforward_gain_ref[...]
    for mask in range(chips):
        for away in range(CORES):
            block_ref = blocks[mask * CORES + away]
            first = ((chip ^ mask) * CORES + (core ^ away)) * block_rows
            for part in range(block_rows // piece):
                floats = block_ref[part * piece : (part + 1) * piece, :].astype(jnp.float32)
                center = jnp.mean(floats, axis=-1, keepdims=True)
                shifted = floats - center
                spread = jnp.mean(shifted * shifted, axis=-1, keepdims=True)
                scaled = shifted * lax.rsqrt(spread + epsilon)
                place = pl.ds(pl.multiple_of(first + part * piece, piece), piece)
                attention_scr[place, :] = (scaled * gain_a).astype(jnp.bfloat16)
                feedforward_scr[place, :] = (scaled * gain_f).astype(jnp.bfloat16)

    normed = attention_scr[...]
    cosine = cosine_ref[...]
    sine_down = sine_down_ref[...]
    sine_up = sine_up_ref[...]
    for component in range(3):
        columns = slice(component * HD, (component + 1) * HD)
        joined = jnp.dot(
            normed, heads_ref[:, columns], preferred_element_type=jnp.float32
        ).astype(jnp.bfloat16)
        joined_scr[:, columns] = joined
        if component < 2:
            turning = joined[:, :128].astype(jnp.float32)
            turned = (
                turning * cosine
                + pltpu.roll(turning, 128 - ROT // 2, 1) * sine_down
                + pltpu.roll(turning, ROT // 2, 1) * sine_up
            )
            joined_scr[:, component * HD : component * HD + 128] = turned.astype(jnp.bfloat16)

    for page_ref in pages_refs:
        page_ref[...] = jnp.zeros(page_ref.shape, page_ref.dtype)
    capacity = pages_refs[0].shape[0]
    for target in range(len(pages_refs)):
        counts_ref[target] = 0
    naming.wait()
    for page in range(tokens // PAGE):
        target = named_ref[page]
        slot = counts_ref[target]
        counts_ref[target] = slot + 1
        slot = jnp.minimum(slot, capacity - 1)
        rows = joined_scr[page * PAGE : (page + 1) * PAGE, HD:]
        for mask, page_ref in enumerate(pages_refs):

            @pl.when(target == (group ^ mask))
            def _():
                page_ref[pl.ds(slot, 1)] = rows[None]

    shape = (tokens, tokens)
    row = lax.broadcasted_iota(jnp.int32, shape, 0)
    column = lax.broadcasted_iota(jnp.int32, shape, 1)
    reach = offsets_ref[:, :1].astype(jnp.int32)
    allowed = (column <= row) & (column >= row - reach)
    scores = lax.dot_general(
        joined_scr[:, :HD],
        joined_scr[:, HD : 2 * HD],
        (((1,), (1,)), ((), ())),
        preferred_element_type=jnp.float32,
    ) * (HD ** (-0.5))
    peak = jnp.max(jnp.where(allowed, scores, -jnp.inf), axis=1, keepdims=True)
    weights = jnp.where(allowed, jnp.exp(scores - peak), 0.0)
    weight_sum = jnp.sum(weights, axis=1, keepdims=True)
    mixed = jnp.dot(
        weights.astype(jnp.bfloat16), joined_scr[:, 2 * HD :], preferred_element_type=jnp.float32
    )
    attended_scr[...] = (mixed / weight_sum).astype(jnp.bfloat16)

    normed = feedforward_scr[...]
    chunk = 256
    for first in range(0, upward_ref.shape[1], chunk):
        columns = slice(first, first + chunk)
        upward = jnp.dot(normed, upward_ref[:, columns], preferred_element_type=jnp.float32)
        hidden = 0.5 * upward * (1.0 + lax.erf(upward * (0.5**0.5)))
        hidden_scr[:, columns] = hidden.astype(jnp.bfloat16)

    hidden = hidden_scr[...]
    attended = attended_scr[...]
    for first in range(0, downward_ref.shape[1], chunk):
        columns = slice(first, first + chunk)
        partial = jnp.dot(
            attended, output_ref[:, columns], preferred_element_type=jnp.float32
        ) + jnp.dot(hidden, downward_ref[:, columns], preferred_element_type=jnp.float32)
        partial = partial.reshape(chips, CORES, block_rows, chunk)
        even, odd = partial[:, 0], partial[:, 1]
        own = jnp.where(core == 0, even, odd)
        sibling = jnp.where(core == 0, odd, even)
        own_ref[:, :, columns] = own
        sibling_ref[:, :, columns] = sibling.astype(jnp.bfloat16)


def layer(blocks, gains, weights, tables, targets, replica_count):
    count = len(blocks)
    chips = count // CORES
    block_rows, width = blocks[0].shape
    tokens = block_rows * count
    capacity = 2 * (tokens // PAGE) // replica_count
    hidden_width = weights[2].shape[1]
    out_shape = [
        jax.ShapeDtypeStruct((chips, block_rows, width), jnp.bfloat16),
        jax.ShapeDtypeStruct((chips, block_rows, width), jnp.float32),
    ] + [jax.ShapeDtypeStruct((capacity, PAGE, 2 * HD), jnp.bfloat16)] * replica_count
    return pl.pallas_call(
        functools.partial(layer_kernel, chips),
        out_shape=out_shape,
        in_specs=vmem_specs(count + 2 + 4 + 4) + [pl.BlockSpec(memory_space=pltpu.HBM)],
        out_specs=vmem_specs(len(out_shape)),
        scratch_shapes=[
            pltpu.VMEM((tokens, width), jnp.bfloat16),
            pltpu.VMEM((tokens, width), jnp.bfloat16),
            pltpu.VMEM((tokens, 3 * HD), jnp.bfloat16),
            pltpu.VMEM((tokens, hidden_width), jnp.bfloat16),
            pltpu.VMEM((tokens, HD), jnp.bfloat16),
            pltpu.SMEM(targets.shape, jnp.int32),
            pltpu.SMEM((replica_count,), jnp.int32),
            pltpu.SemaphoreType.DMA(()),
        ],
        compiler_params=pltpu.CompilerParams(vmem_limit_bytes=32 * MIB),
        cost_estimate=pl.CostEstimate(
            flops=2 * tokens * width * (3 * HD + HD + 2 * hidden_width),
            bytes_accessed=16 * MIB,
            transcendentals=tokens * (hidden_width + tokens),
        ),
        name="layer",
    )(*blocks, *gains, *weights, *tables, in_hbm(targets))


def reduce_kernel(chips, own_ref, sibling_ref, hidden_ref, base_ref, *out_refs):
    chip = lax.axis_index("tensor") // CORES
    base_ref[...] = (
        hidden_ref[...].astype(jnp.float32)
        + own_ref[chip]
        + sibling_ref[chip].astype(jnp.float32)
    )
    for mask in range(1, chips):
        other = chip ^ mask
        out_refs[mask - 1][...] = (
            own_ref[other] + sibling_ref[other].astype(jnp.float32)
        ).astype(jnp.bfloat16)


def reduced(own, sibling, hidden_states):
    chips, block_rows, width = own.shape
    return pl.pallas_call(
        functools.partial(reduce_kernel, chips),
        out_shape=[jax.ShapeDtypeStruct((block_rows, width), jnp.float32)]
        + [jax.ShapeDtypeStruct((block_rows, width), jnp.bfloat16)] * (chips - 1),
        in_specs=vmem_specs(3),
        out_specs=vmem_specs(chips),
        compiler_params=pltpu.CompilerParams(vmem_limit_bytes=16 * MIB),
        name="reduced",
    )(own, sibling, hidden_states)


def finish_kernel(chips, base_ref, *refs):
    group = lax.axis_index("dp")
    parts, pages = refs[: chips - 1], refs[chips - 1 : -3]
    output_ref, cache_ref, sems = refs[-3:]
    copies = [
        pltpu.make_async_copy(page_ref, cache_ref.at[0, group ^ mask], sems.at[mask])
        for mask, page_ref in enumerate(pages)
    ]
    for copy in copies:
        copy.start()
    total = base_ref[...]
    for part_ref in parts:
        total = total + part_ref[...].astype(jnp.float32)
    output_ref[...] = total
    for copy in copies:
        copy.wait()


def finished(base, parts, pages):
    count = len(pages)
    return pl.pallas_call(
        functools.partial(finish_kernel, len(parts) + 1),
        out_shape=[
            jax.ShapeDtypeStruct(base.shape, base.dtype),
            jax.ShapeDtypeStruct((1, count) + pages[0].shape, pages[0].dtype),
        ],
        in_specs=vmem_specs(1 + len(parts)) + [pl.BlockSpec(memory_space=pl.ANY)] * count,
        out_specs=vmem_specs(1) + [pl.BlockSpec(memory_space=pltpu.HBM)],
        scratch_shapes=[pltpu.SemaphoreType.DMA((count,))],
        compiler_params=pltpu.CompilerParams(vmem_limit_bytes=8 * MIB),
        name="finished",
    )(base, *parts, *pages)


def shards_whole_heads(
    hidden_states,
    attention_gain,
    feedforward_gain,
    heads_weight,
    output_weight,
    upward_weight,
    downward_weight,
    segments,
    page_targets,
):
    chips = lax.axis_size("tensor") // CORES
    replica_count = lax.axis_size("dp")
    near = {mask: exchanged(hidden_states, "tensor", mask * CORES) for mask in (2, 3, 1)}
    beside = exchanged(hidden_states, "tensor", 1)
    (*staged,) = prepare(
        segments,
        (
            heads_weight,
            output_weight,
            upward_weight,
            downward_weight,
            attention_gain[None],
            feedforward_gain[None],
            hidden_states,
        ),
    )
    blocks = [staged[6], beside]
    for mask in range(1, chips):
        near[mask], staged[7] = lax.optimization_barrier((near[mask], staged[7]))
        blocks += [near[mask], exchanged(near[mask], "tensor", 1)]
    sibling, own, *pages = layer(
        blocks, staged[4:6], staged[:4], staged[7:], page_targets[:, 0], replica_count
    )
    received = exchanged(sibling, "tensor", 1)
    base, *outgoing = reduced(own, received, staged[6])
    outgoing, pages = lax.optimization_barrier((outgoing, pages))
    incoming = [
        exchanged(outgoing[mask - 1], "tensor", mask * CORES) for mask in (2, 3, 1)
    ]
    arriving = [pages[0]] + [
        exchanged(pages[mask], "dp", mask) for mask in range(1, replica_count)
    ]
    return tuple(finished(base, incoming, arriving))


def solution(mesh):
    whole_heads = mesh.shape["tensor"] == H and mesh.shape["dp"] == 4
    shards = shards_whole_heads if whole_heads else shards_split_heads
    in_specs = (
        P(("dp", "tensor"), None),
        P(),
        P(),
        P(None, "tensor"),
        P("tensor", None),
        P(None, "tensor"),
        P("tensor", None),
        P("dp", None),
        P("dp", None),
    )
    out_specs = (P(("dp", "tensor"), None), P("dp", None, None, None, "tensor"))
    return jax.shard_map(shards, mesh=mesh, in_specs=in_specs, out_specs=out_specs, check_vma=False)
```

```python
import functools
import math

import jax
import jax.numpy as jnp
from jax import lax
from jax.experimental import pallas as pl
from jax.experimental.pallas import tpu as pltpu
from jax.sharding import PartitionSpec as P

H = 8
HD = 256
ROT = 64
PAGE = 16


epsilon = 1e-05
rotary_base = 10000.0
key_block = 256


def shortened(array):

    def short(part):
        return part.astype(jnp.bfloat16) if part.dtype == jnp.float32 else part

    return jax.tree.map(short, array)


def swapped(block, axis, apart):
    count = lax.axis_size(axis)
    route = []
    for low in range(count):
        high = low | 1 << apart
        if high != low and high < count:
            route += [(low, high), (high, low)]
    return lax.ppermute(block, axis, route)


def layer_norm(values, gain):
    floats = values.astype(jnp.float32)
    center = jnp.mean(floats, axis=-1, keepdims=True)
    shifted = floats - center
    spread = jnp.mean(shifted * shifted, axis=-1, keepdims=True)
    return (shifted * lax.rsqrt(spread + epsilon) * gain).astype(jnp.bfloat16)


def positions_of(stream):
    indices = jnp.arange(stream.shape[0], dtype=jnp.int32)
    boundary = jnp.concatenate([jnp.ones((1,), dtype=bool), stream[1:] != stream[:-1]])
    starting = lax.cummax(jnp.where(boundary, indices, jnp.zeros_like(indices)), axis=0)
    return (indices, starting)


def rotate_heads(vectors, offsets, rotary_dims):
    half_dims = rotary_dims // 2
    frequency = jnp.exp(
        jnp.arange(half_dims, dtype=jnp.float32) * (-2.0 * math.log(rotary_base) / rotary_dims)
    )
    angles = offsets.astype(jnp.float32)[:, None] * frequency[None, :]
    cosine = jnp.cos(angles)
    sine = jnp.sin(angles)
    floats = vectors.astype(jnp.float32)
    leading = floats[..., :half_dims]
    trailing = floats[..., half_dims:rotary_dims]
    rotated = jnp.concatenate(
        [
            leading * cosine - trailing * sine,
            trailing * cosine + leading * sine,
            floats[..., rotary_dims:],
        ],
        axis=-1,
    )
    return rotated.astype(jnp.bfloat16)


def shards_split_heads(
    hidden_states,
    attention_gain,
    feedforward_gain,
    heads_weight,
    output_weight,
    upward_weight,
    downward_weight,
    segments,
    page_targets,
):
    tensor_count = lax.axis_size("tensor")
    replica_count = lax.axis_size("dp")
    tensor_index = lax.axis_index("tensor")
    quarters = tensor_count // H
    quarter_width = HD // quarters
    quarter_index = tensor_index % quarters
    stream = segments[0]
    tokens_total = stream.shape[0]
    level_count = quarters.bit_length() - 1
    normed_attention = layer_norm(hidden_states, attention_gain)
    normed_feedforward = layer_norm(hidden_states, feedforward_gain)
    shard_rows = lax.all_gather(
        (normed_attention, normed_feedforward), "tensor", axis=0, tiled=True
    )
    joined_rows = jnp.dot(shard_rows[0], heads_weight, preferred_element_type=jnp.float32).astype(
        jnp.bfloat16
    )
    upward = jnp.dot(shard_rows[1], upward_weight, preferred_element_type=jnp.float32)
    hidden_rows = jax.nn.gelu(upward, approximate=False).astype(jnp.bfloat16)
    hidden = hidden_rows
    pieces = (
        joined_rows.reshape(tokens_total, 3, quarter_width)
        .transpose(1, 0, 2)
        .reshape(1, 3, tokens_total * quarter_width)
    )
    for bit_number in range(level_count):
        partner = swapped(shortened(pieces), "tensor", bit_number).astype(pieces.dtype)
        lower = tensor_index >> bit_number & 1 == 0
        pieces = jnp.where(
            lower, jnp.concatenate([pieces, partner], 0), jnp.concatenate([partner, pieces], 0)
        )
    whole_head = (
        pieces.reshape(quarters, 3, tokens_total, quarter_width)
        .transpose(1, 2, 0, 3)
        .reshape(3, tokens_total, HD)
    )
    indices, starting = positions_of(stream)
    offsets = indices - starting
    queries = rotate_heads(whole_head[0], offsets, ROT)
    keys = rotate_heads(whole_head[1], offsets, ROT)
    values = whole_head[2]
    block_rows = tokens_total // (2 * quarters)
    score_scale = HD ** (-0.5)

    def attend_block(block_number):
        first_row = block_number * block_rows
        block_queries = lax.dynamic_slice_in_dim(queries, first_row, block_rows, 0)
        query_segments = lax.dynamic_slice_in_dim(stream, first_row, block_rows, 0)
        query_indices = first_row + jnp.arange(block_rows, dtype=jnp.int32)
        lowest = lax.dynamic_index_in_dim(starting, first_row, 0, keepdims=False) // key_block
        highest = (first_row + block_rows + key_block - 1) // key_block

        def scores_of(key_number):
            key_first = key_number * key_block
            key_indices = key_first + jnp.arange(key_block, dtype=jnp.int32)
            scores = (
                jnp.dot(block_queries, keys.T, preferred_element_type=jnp.float32) * score_scale
            )
            allowed = (stream[None, :] == query_segments[:, None]) & (
                key_indices[None, :] <= query_indices[:, None]
            )
            return (scores, allowed)

        def find_peak(key_number, peak):
            scores, allowed = scores_of(key_number)
            return jnp.maximum(peak, jnp.max(jnp.where(allowed, scores, -jnp.inf), axis=1))

        peak = lax.fori_loop(
            lowest, highest, find_peak, jnp.full((block_rows,), -jnp.inf, jnp.float32)
        )

        def accumulate(key_number, state):
            weight_sum, mixed_sum = state
            scores, allowed = scores_of(key_number)
            weights = jnp.where(allowed, jnp.exp(scores - peak[:, None]), 0.0)
            mixed_next = mixed_sum + jnp.dot(
                weights.astype(jnp.bfloat16), values, preferred_element_type=jnp.float32
            )
            return (weight_sum + jnp.sum(weights, axis=1), mixed_next)

        start_state = (
            jnp.zeros((block_rows,), jnp.float32),
            jnp.zeros((block_rows, HD), jnp.float32),
        )
        weight_sum, mixed_sum = lax.fori_loop(lowest, highest, accumulate, start_state)
        return (mixed_sum / weight_sum[:, None]).astype(jnp.bfloat16)

    own_blocks = (2 * quarter_index, 2 * quarter_index + 1)
    own_rows = jnp.concatenate([attend_block(own_blocks[0]), attend_block(own_blocks[1])], 0)[None]
    for bit_number in range(level_count):
        partner = swapped(own_rows, "tensor", bit_number)
        lower = tensor_index >> bit_number & 1 == 0
        own_rows = jnp.where(
            lower, jnp.concatenate([own_rows, partner], 0), jnp.concatenate([partner, own_rows], 0)
        )
    attended = own_rows.reshape(tokens_total, HD)
    attended_quarter = lax.dynamic_slice_in_dim(
        attended, quarter_index * quarter_width, quarter_width, 1
    )
    hidden_rows = hidden
    summed = lax.psum_scatter(
        (
            jnp.dot(attended_quarter, output_weight, preferred_element_type=jnp.float32)
            + jnp.dot(hidden_rows, downward_weight, preferred_element_type=jnp.float32)
        ).astype(jnp.bfloat16),
        "tensor",
        scatter_dimension=0,
        tiled=True,
    ).astype(jnp.float32)
    layer_output = hidden_states.astype(jnp.float32) + summed
    key_quarter = lax.dynamic_slice_in_dim(keys, quarter_index * quarter_width, quarter_width, 1)
    value_quarter = joined_rows[:, 2 * quarter_width :]
    page_count = tokens_total // PAGE
    page_rows = jnp.concatenate([key_quarter, value_quarter], 1).reshape(
        page_count, PAGE * 2 * quarter_width
    )
    targets = page_targets[:, 0]
    page_numbers = jnp.arange(page_count, dtype=jnp.int32)
    earlier = jnp.sum(
        (
            (targets[None, :] == targets[:, None]) & (page_numbers[None, :] < page_numbers[:, None])
        ).astype(jnp.int32),
        axis=1,
    )
    capacity = 2 * page_count // replica_count
    slot_numbers = targets * capacity + earlier
    placing = (
        jnp.arange(replica_count * capacity, dtype=jnp.int32)[:, None] == slot_numbers[None, :]
    ).astype(jnp.bfloat16)
    outgoing = jnp.dot(placing, page_rows, preferred_element_type=jnp.float32).astype(jnp.bfloat16)
    outgoing = outgoing.reshape(replica_count, capacity, PAGE * 2 * quarter_width)
    incoming = lax.all_to_all(outgoing, "dp", split_axis=0, concat_axis=0, tiled=True)
    cache_pages = incoming.reshape(1, replica_count, capacity, PAGE, 2 * quarter_width)
    return (layer_output, cache_pages)


CORES = 2
CHIPS = 4
MIB = 1 << 20


def in_hbm(array):
    return pltpu.with_memory_space_constraint(array, pltpu.HBM)


def exchanged(block, axis, mask):
    count = lax.axis_size(axis)
    return lax.ppermute(block, axis, [(member, member ^ mask) for member in range(count)])


def vmem_specs(count):
    return [pl.BlockSpec(memory_space=pltpu.VMEM)] * count


def parameters(mebibytes):
    return pltpu.CompilerParams(vmem_limit_bytes=mebibytes * MIB)


def whereabouts():
    member = lax.axis_index("tensor")
    return member // CORES, member % CORES


def position_of(kind, half, block_rows):
    chip, core = whereabouts()
    return ((chip ^ kind) * CORES + (core ^ half)) * block_rows


def positions_along(first, shape, axis, block_rows):
    chip, core = whereabouts()
    bits = block_rows.bit_length() - 1
    place = first + lax.broadcasted_iota(jnp.int32, shape, axis)
    kind = place >> (bits + 1)
    half = (place >> bits) & 1
    return ((((chip ^ kind) << 1) | (core ^ half)) << bits) | (place & (block_rows - 1))


def normalize(blocks, gain_refs, normed_refs):
    piece = 16
    gains = [gain_ref[...] for gain_ref in gain_refs]
    for number, block_ref in enumerate(blocks):
        block_rows = block_ref.shape[0]
        for part in range(0, block_rows, piece):
            floats = block_ref[part : part + piece, :].astype(jnp.float32)
            center = jnp.mean(floats, axis=-1, keepdims=True)
            shifted = floats - center
            spread = jnp.mean(shifted * shifted, axis=-1, keepdims=True)
            scaled = shifted * lax.rsqrt(spread + epsilon)
            first = number * block_rows + part
            for gain, normed_ref in zip(gains, normed_refs):
                normed_ref[first : first + piece, :] = (scaled * gain).astype(jnp.bfloat16)


def project(normed_ref, heads_ref, table_refs, places, joined_ref, first):
    rows = normed_ref.shape[0]
    block_rows = rows // len(places)
    for component in range(3):
        columns = slice(component * HD, (component + 1) * HD)
        joined = jnp.dot(
            normed_ref[...], heads_ref[:, columns], preferred_element_type=jnp.float32
        ).astype(jnp.bfloat16)
        joined_ref[first : first + rows, columns] = joined
        if component < 2:
            cosine, sine_down, sine_up = [
                jnp.concatenate(
                    [
                        table_ref[pl.ds(pl.multiple_of(place, block_rows), block_rows), :]
                        for place in places
                    ],
                    0,
                )
                for table_ref in table_refs
            ]
            turning = joined[:, :128].astype(jnp.float32)
            turned = (
                turning * cosine
                + pltpu.roll(turning, 128 - ROT // 2, 1) * sine_down
                + pltpu.roll(turning, ROT // 2, 1) * sine_up
            )
            joined_ref[first : first + rows, component * HD : component * HD + 128] = turned.astype(
                jnp.bfloat16
            )


def hide(normed_ref, upward_ref, hidden_ref):
    chunk = 256
    for first in range(0, upward_ref.shape[1], chunk):
        columns = slice(first, first + chunk)
        upward = jnp.dot(
            normed_ref[...], upward_ref[:, columns], preferred_element_type=jnp.float32
        )
        hidden = 0.5 * upward * (1.0 + lax.erf(upward * (0.5**0.5)))
        hidden_ref[:, columns] = hidden.astype(jnp.bfloat16)


def attend(joined_ref, offsets_ref, first, rows, block_rows):
    tokens = joined_ref.shape[0]
    starts = [
        position_of(place // (2 * block_rows), (place // block_rows) % 2, block_rows)
        for place in range(first, first + rows, block_rows)
    ]
    reach = jnp.concatenate(
        [
            offsets_ref[pl.ds(pl.multiple_of(start, block_rows), block_rows), :]
            for start in starts
        ],
        0,
    )[:, :1].astype(jnp.int32)
    row = positions_along(first, (rows, 1), 0, block_rows)
    column = positions_along(0, (1, tokens), 1, block_rows)
    allowed = (column <= row) & (column >= row - reach)
    scores = lax.dot_general(
        joined_ref[first : first + rows, :HD],
        joined_ref[:, HD : 2 * HD],
        (((1,), (1,)), ((), ())),
        preferred_element_type=jnp.float32,
    ) * (HD ** (-0.5))
    peak = jnp.max(jnp.where(allowed, scores, -jnp.inf), axis=1, keepdims=True)
    weights = jnp.where(allowed, jnp.exp(scores - peak), 0.0)
    weight_sum = jnp.sum(weights, axis=1, keepdims=True)
    mixed = jnp.dot(
        weights.astype(jnp.bfloat16), joined_ref[:, 2 * HD :], preferred_element_type=jnp.float32
    )
    return (mixed / weight_sum).astype(jnp.bfloat16)


def make_tables(segments_ref, offsets_ref, cosine_ref, sine_down_ref, sine_up_ref):
    tokens = segments_ref.shape[1]
    shape = (tokens, tokens)
    rows = lax.broadcasted_iota(jnp.int32, shape, 0)
    columns = lax.broadcasted_iota(jnp.int32, shape, 1)
    across = jnp.broadcast_to(segments_ref[...], shape).astype(jnp.float32)
    down = jnp.sum(jnp.where(rows == columns, across, 0.0), axis=1, keepdims=True)
    earlier = (across == down) & (columns < rows)
    offsets = jnp.sum(jnp.where(earlier, 1.0, 0.0), axis=1, keepdims=True)
    offsets_ref[...] = jnp.broadcast_to(offsets, offsets_ref.shape)
    half = ROT // 2
    lane = lax.broadcasted_iota(jnp.int32, (tokens, 128), 1)
    step = (lane & (half - 1)).astype(jnp.float32)
    frequency = jnp.exp(step * (-2.0 * math.log(rotary_base) / ROT))
    angles = offsets * frequency
    sine = jnp.sin(angles)
    cosine_ref[...] = jnp.where(lane < ROT, jnp.cos(angles), 1.0)
    sine_down_ref[...] = jnp.where(lane < half, -sine, 0.0)
    sine_up_ref[...] = jnp.where((lane >= half) & (lane < ROT), sine, 0.0)


def own_kernel(count, segments_ref, beside_ref, *refs):
    sources, targets = refs[:count], refs[count : 2 * count]
    offsets_ref, *table_refs, joined_ref, fed_ref = refs[2 * count : 2 * count + 6]
    attention_scr, feedforward_scr, hidden_scr, sems = refs[2 * count + 6 :]
    copies = []
    for number, (source, target) in enumerate(zip(sources, targets)):
        parts = 4 if source.shape[0] >= 256 else 1
        rows = source.shape[0] // parts
        places = [pl.ds(part * rows, rows) for part in range(parts)]
        copies.append(
            [
                pltpu.make_async_copy(source.at[place], target.at[place], sems.at[number, part])
                for part, place in enumerate(places)
            ]
        )
    for copy in sum(copies, []):
        copy.start()

    def wait_for(*numbers):
        for number in numbers:
            for copy in copies[number]:
                copy.wait()

    hidden_ref, *gain_refs, heads_ref, upward_ref, downward_ref, _ = targets
    block_rows = hidden_ref.shape[0]
    make_tables(segments_ref, offsets_ref, *table_refs)
    wait_for(0, 1, 2)
    normalize([hidden_ref, beside_ref], gain_refs, [attention_scr, feedforward_scr])
    wait_for(3)
    places = [position_of(0, half, block_rows) for half in range(CORES)]
    project(attention_scr, heads_ref, table_refs, places, joined_ref, 0)
    wait_for(4)
    hide(feedforward_scr, upward_ref, hidden_scr)
    wait_for(5)
    fed_ref[...] = jnp.dot(
        hidden_scr[...], downward_ref[...], preferred_element_type=jnp.float32
    )
    wait_for(6)


def own_rows(segments, beside, staged):
    tokens = segments.shape[1]
    block_rows, width = beside.shape
    rows = CORES * block_rows
    hidden_width = staged[4].shape[1]
    shapes = [pltpu.VMEM(array.shape, array.dtype) for array in staged]
    shapes += [pltpu.VMEM((tokens, 128), jnp.float32)] * 4
    shapes += [pltpu.VMEM((rows, 3 * HD), jnp.bfloat16), pltpu.VMEM((rows, width), jnp.float32)]
    count = len(staged)
    return pl.pallas_call(
        functools.partial(own_kernel, count),
        out_shape=shapes,
        in_specs=vmem_specs(2) + [pl.BlockSpec(memory_space=pltpu.HBM)] * count,
        out_specs=vmem_specs(len(shapes)),
        scratch_shapes=[
            pltpu.VMEM((rows, width), jnp.bfloat16),
            pltpu.VMEM((rows, width), jnp.bfloat16),
            pltpu.VMEM((rows, hidden_width), jnp.bfloat16),
            pltpu.SemaphoreType.DMA((count, 4)),
        ],
        compiler_params=parameters(12),
        cost_estimate=pl.CostEstimate(
            flops=2 * rows * width * (3 * HD + 2 * hidden_width),
            bytes_accessed=sum(array.nbytes for array in staged),
            transcendentals=rows * hidden_width,
        ),
        name="own_rows",
    )(segments, beside, *[in_hbm(array) for array in staged])


def middle_kernel(*refs):
    blocks, (gain_a, gain_f, heads_ref, upward_ref, downward_ref) = refs[:4], refs[4:9]
    table_refs = refs[9:12]
    joined_ref, fed_ref, attention_scr, feedforward_scr, hidden_scr = refs[12:]
    block_rows = blocks[0].shape[0]
    normalize(blocks, [gain_a, gain_f], [attention_scr, feedforward_scr])
    places = [position_of(kind, half, block_rows) for kind in (1, 2) for half in range(CORES)]
    project(attention_scr, heads_ref, table_refs, places, joined_ref, 0)
    hide(feedforward_scr, upward_ref, hidden_scr)
    chunk = 512
    for first in range(0, downward_ref.shape[1], chunk):
        columns = slice(first, first + chunk)
        fed_ref[:, columns] = jnp.dot(
            hidden_scr[...], downward_ref[:, columns], preferred_element_type=jnp.float32
        )


def middle_rows(blocks, gains, weights, tables):
    block_rows, width = blocks[0].shape
    rows = len(blocks) * block_rows
    hidden_width = weights[1].shape[1]
    return pl.pallas_call(
        middle_kernel,
        out_shape=[
            pltpu.VMEM((rows, 3 * HD), jnp.bfloat16),
            pltpu.VMEM((rows, width), jnp.float32),
        ],
        in_specs=vmem_specs(len(blocks) + 2 + 3 + 3),
        out_specs=vmem_specs(2),
        scratch_shapes=[
            pltpu.VMEM((rows, width), jnp.bfloat16),
            pltpu.VMEM((rows, width), jnp.bfloat16),
            pltpu.VMEM((rows, hidden_width), jnp.bfloat16),
        ],
        compiler_params=parameters(12),
        cost_estimate=pl.CostEstimate(
            flops=2 * rows * width * (3 * HD + 2 * hidden_width),
            bytes_accessed=MIB,
            transcendentals=rows * hidden_width,
        ),
        name="middle_rows",
    )(*blocks, *gains, *weights, *tables)


def last_kernel(*refs):
    blocks, (gain_a, gain_f, heads_ref, upward_ref, downward_ref, output_ref) = refs[:2], refs[2:8]
    offsets_ref, *table_refs = refs[8:12]
    joined_own_ref, joined_middle_ref = refs[12:14]
    joined_ref, sibling_ref, own_ref, attention_scr, feedforward_scr, hidden_scr = refs[14:]
    block_rows = blocks[0].shape[0]
    tokens = joined_ref.shape[0]
    first = tokens - CORES * block_rows
    normalize(blocks, [gain_a, gain_f], [attention_scr, feedforward_scr])
    own_count = joined_own_ref.shape[0]
    joined_ref[:own_count, :] = joined_own_ref[...]
    joined_ref[own_count:first, :] = joined_middle_ref[...]
    places = [position_of(CHIPS - 1, half, block_rows) for half in range(CORES)]
    project(attention_scr, heads_ref, table_refs, places, joined_ref, first)
    hide(feedforward_scr, upward_ref, hidden_scr)
    attended = attend(joined_ref, offsets_ref, first, CORES * block_rows, block_rows)
    chunk = 512
    for begin in range(0, downward_ref.shape[1], chunk):
        columns = slice(begin, begin + chunk)
        partial = jnp.dot(
            hidden_scr[...], downward_ref[:, columns], preferred_element_type=jnp.float32
        ) + jnp.dot(attended, output_ref[:, columns], preferred_element_type=jnp.float32)
        own_ref[:, columns] = partial[:block_rows]
        sibling_ref[:, columns] = partial[block_rows:].astype(jnp.bfloat16)


def last_rows(blocks, gains, weights, tables, joined_own, joined_middle):
    block_rows, width = blocks[0].shape
    rows = len(blocks) * block_rows
    hidden_width = weights[1].shape[1]
    tokens = joined_own.shape[0] + joined_middle.shape[0] + rows
    return pl.pallas_call(
        last_kernel,
        out_shape=[
            pltpu.VMEM((tokens, 3 * HD), jnp.bfloat16),
            pltpu.VMEM((block_rows, width), jnp.bfloat16),
            pltpu.VMEM((block_rows, width), jnp.float32),
        ],
        in_specs=vmem_specs(len(blocks) + 2 + 4 + 4 + 2),
        out_specs=vmem_specs(3),
        scratch_shapes=[
            pltpu.VMEM((rows, width), jnp.bfloat16),
            pltpu.VMEM((rows, width), jnp.bfloat16),
            pltpu.VMEM((rows, hidden_width), jnp.bfloat16),
        ],
        compiler_params=parameters(12),
        cost_estimate=pl.CostEstimate(
            flops=2 * rows * width * (3 * HD + HD + 2 * hidden_width),
            bytes_accessed=MIB,
            transcendentals=rows * hidden_width,
        ),
        name="last_rows",
    )(*blocks, *gains, *weights, *tables, joined_own, joined_middle)


def tail_kernel(block_rows, joined_ref, offsets_ref, output_ref, fed_own_ref, fed_middle_ref, *refs):
    targets_ref, *sibling_refs = refs[:4]
    own_refs = refs[4:7]
    pages_refs, (named_ref, counts_ref, slots_ref, sem) = refs[7:-4], refs[-4:]
    naming = pltpu.make_async_copy(targets_ref, named_ref, sem)
    naming.start()
    tokens = joined_ref.shape[0]
    kind_rows = CORES * block_rows
    rows = tokens - kind_rows
    attended = attend(joined_ref, offsets_ref, 0, rows, block_rows)
    chunk = 512
    for begin in range(0, output_ref.shape[1], chunk):
        columns = slice(begin, begin + chunk)
        product = jnp.dot(attended, output_ref[:, columns], preferred_element_type=jnp.float32)
        near = product[:kind_rows] + fed_own_ref[:, columns]
        middle = product[kind_rows:] + fed_middle_ref[:, columns]
        for kind, partial in enumerate((near, middle[:kind_rows], middle[kind_rows:])):
            own_refs[kind][:, columns] = partial[:block_rows]
            sibling_refs[kind][:, columns] = partial[block_rows:].astype(jnp.bfloat16)

    chip, core = whereabouts()
    group = lax.axis_index("dp")
    naming.wait()
    for target in range(len(pages_refs)):
        counts_ref[target] = 0
    for page in range(tokens // PAGE):
        target = named_ref[page]
        slot = counts_ref[target]
        counts_ref[target] = slot + 1
        slots_ref[page] = slot
    for page_ref in pages_refs:
        page_ref[...] = jnp.zeros(page_ref.shape, page_ref.dtype)
    capacity = pages_refs[0].shape[0]
    for place in range(0, tokens, PAGE):
        kind, half = place // kind_rows, (place // block_rows) % CORES
        start = ((chip ^ kind) * CORES + (core ^ half)) * block_rows + place % block_rows
        page = start // PAGE
        target = named_ref[page]
        slot = jnp.minimum(slots_ref[page], capacity - 1)
        for mask, page_ref in enumerate(pages_refs):

            @pl.when(target == (group ^ mask))
            def _():
                page_ref[pl.ds(slot, 1)] = joined_ref[place : place + PAGE, HD:][None]


def tail_rows(joined, offsets, output_weight, fed_own, fed_middle, targets, replica_count):
    tokens = joined.shape[0]
    width = fed_own.shape[1]
    block_rows = fed_own.shape[0] // CORES
    page_count = tokens // PAGE
    capacity = 2 * page_count // replica_count
    shapes = [
        pltpu.VMEM((block_rows, width), dtype) for dtype in [jnp.bfloat16] * 3 + [jnp.float32] * 3
    ] + [pltpu.VMEM((capacity, PAGE, 2 * HD), jnp.bfloat16)] * replica_count
    return pl.pallas_call(
        functools.partial(tail_kernel, block_rows),
        out_shape=shapes,
        in_specs=vmem_specs(5) + [pl.BlockSpec(memory_space=pltpu.HBM)],
        out_specs=vmem_specs(len(shapes)),
        scratch_shapes=[
            pltpu.SMEM(targets.shape, jnp.int32),
            pltpu.SMEM((replica_count,), jnp.int32),
            pltpu.SMEM((page_count,), jnp.int32),
            pltpu.SemaphoreType.DMA(()),
        ],
        compiler_params=parameters(12),
        cost_estimate=pl.CostEstimate(
            flops=2 * tokens * width * HD, bytes_accessed=MIB, transcendentals=tokens * tokens
        ),
        name="tail_rows",
    )(joined, offsets, output_weight, fed_own, fed_middle, in_hbm(targets))


def add_kernel(*refs):
    total = refs[0][...].astype(jnp.float32)
    for ref in refs[1:-1]:
        total = total + ref[...].astype(jnp.float32)
    refs[-1][...] = total.astype(refs[-1].dtype)


def added(name, *parts):
    return pl.pallas_call(
        add_kernel,
        out_shape=pltpu.VMEM(parts[0].shape, jnp.bfloat16),
        in_specs=vmem_specs(len(parts)),
        out_specs=pl.BlockSpec(memory_space=pltpu.VMEM),
        compiler_params=parameters(4),
        name=name,
    )(*parts)


def sums_kernel(passing_ref, *refs):
    twos, ones, zeros = refs[0:2], refs[2:4], refs[4:7]
    second_ref, first_ref, base_ref = refs[7:]

    def total(parts):
        return sum([part[...].astype(jnp.float32) for part in parts[1:]], parts[0][...])

    second_ref[...] = total((twos[1], twos[0], passing_ref)).astype(jnp.bfloat16)
    first_ref[...] = total((ones[1], ones[0])).astype(jnp.bfloat16)
    base_ref[...] = total((zeros[1], zeros[0], zeros[2]))


def remaining_sums(passing, twos, ones, zeros, hidden):
    return pl.pallas_call(
        sums_kernel,
        out_shape=[
            pltpu.VMEM(hidden.shape, jnp.bfloat16),
            pltpu.VMEM(hidden.shape, jnp.bfloat16),
            pltpu.VMEM(hidden.shape, jnp.float32),
        ],
        in_specs=vmem_specs(8),
        out_specs=vmem_specs(3),
        compiler_params=parameters(4),
        name="remaining_sums",
    )(passing, *twos, *ones, *zeros, hidden)


def finish_kernel(part_count, base_ref, *refs):
    group = lax.axis_index("dp")
    parts, pages = refs[:part_count], refs[part_count:-3]
    output_ref, cache_ref, sems = refs[-3:]
    copies = [
        pltpu.make_async_copy(page_ref, cache_ref.at[0, group ^ mask], sems.at[mask])
        for mask, page_ref in enumerate(pages)
    ]
    for copy in copies:
        copy.start()
    total = base_ref[...]
    for part_ref in parts:
        total = total + part_ref[...].astype(jnp.float32)
    output_ref[...] = total
    for copy in copies:
        copy.wait()


def finished(base, parts, pages):
    count = len(pages)
    return pl.pallas_call(
        functools.partial(finish_kernel, len(parts)),
        out_shape=[
            jax.ShapeDtypeStruct(base.shape, base.dtype),
            jax.ShapeDtypeStruct((1, count) + pages[0].shape, pages[0].dtype),
        ],
        in_specs=vmem_specs(1 + len(parts)) + [pl.BlockSpec(memory_space=pl.ANY)] * count,
        out_specs=vmem_specs(1) + [pl.BlockSpec(memory_space=pltpu.HBM)],
        scratch_shapes=[pltpu.SemaphoreType.DMA((count,))],
        compiler_params=parameters(4),
        name="finished",
    )(base, *parts, *pages)


def shards_whole_heads(
    hidden_states,
    attention_gain,
    feedforward_gain,
    heads_weight,
    output_weight,
    upward_weight,
    downward_weight,
    segments,
    page_targets,
):
    replica_count = lax.axis_size("dp")
    to_chip = [mask * CORES for mask in range(CHIPS)]
    second = exchanged(hidden_states, "tensor", to_chip[2])
    first = exchanged(hidden_states, "tensor", to_chip[1])
    beside = exchanged(hidden_states, "tensor", 1)
    staged = (
        hidden_states,
        attention_gain[None],
        feedforward_gain[None],
        heads_weight,
        upward_weight,
        downward_weight,
        output_weight,
    )
    hidden, *rest = own_rows(segments, beside, staged)
    gains, (heads, upward, downward, output), tables = rest[:2], rest[2:6], rest[6:10]
    joined_own, fed_own = rest[10:]

    second, first, joined_own = lax.optimization_barrier((second, first, joined_own))
    third = exchanged(second, "tensor", to_chip[1])
    second_beside = exchanged(second, "tensor", 1)
    first_beside = exchanged(first, "tensor", 1)
    third_beside = exchanged(third, "tensor", 1)
    joined_middle, fed_middle = middle_rows(
        (first, first_beside, second, second_beside), gains, (heads, upward, downward), tables[1:]
    )
    joined, sibling, own = last_rows(
        (third, third_beside),
        gains,
        (heads, upward, downward, output),
        tables,
        joined_own,
        joined_middle,
    )

    received = exchanged(sibling, "tensor", 1)
    parts = tail_rows(
        joined, tables[0], output, fed_own, fed_middle, page_targets[:, 0], replica_count
    )
    third_sum = added("third_added", own, received)
    siblings, owns, pages = parts[:3], parts[3:6], parts[6:]
    third_sum, siblings = lax.optimization_barrier((third_sum, siblings))
    passing = exchanged(third_sum, "tensor", to_chip[1])
    pairs = [(exchanged(siblings[kind], "tensor", 1), owns[kind]) for kind in (2, 1, 0)]
    second_sum, first_sum, base = remaining_sums(passing, *pairs, hidden)
    second_sum, first_sum, pages = lax.optimization_barrier((second_sum, first_sum, pages))
    from_second = exchanged(second_sum, "tensor", to_chip[2])
    from_first = exchanged(first_sum, "tensor", to_chip[1])
    arriving = [pages[0]] + [
        exchanged(pages[mask], "dp", mask) for mask in range(1, replica_count)
    ]
    return tuple(finished(base, (from_second, from_first), arriving))


def solution(mesh):
    whole_heads = mesh.shape["tensor"] == H and mesh.shape["dp"] == 4
    shards = shards_whole_heads if whole_heads else shards_split_heads
    in_specs = (
        P(("dp", "tensor"), None),
        P(),
        P(),
        P(None, "tensor"),
        P("tensor", None),
        P(None, "tensor"),
        P("tensor", None),
        P("dp", None),
        P("dp", None),
    )
    out_specs = (P(("dp", "tensor"), None), P("dp", None, None, None, "tensor"))
    return jax.shard_map(shards, mesh=mesh, in_specs=in_specs, out_specs=out_specs, check_vma=False)
```

```python
import functools
import math

import jax
import jax.numpy as jnp
from jax import lax
from jax.experimental import pallas as pl
from jax.experimental.pallas import tpu as pltpu
from jax.sharding import PartitionSpec as P

H = 8
HD = 256
ROT = 64
PAGE = 16


epsilon = 1e-05
rotary_base = 10000.0
key_block = 256


def shortened(array):

    def short(part):
        return part.astype(jnp.bfloat16) if part.dtype == jnp.float32 else part

    return jax.tree.map(short, array)


def swapped(block, axis, apart):
    count = lax.axis_size(axis)
    route = []
    for low in range(count):
        high = low | 1 << apart
        if high != low and high < count:
            route += [(low, high), (high, low)]
    return lax.ppermute(block, axis, route)


def layer_norm(values, gain):
    floats = values.astype(jnp.float32)
    center = jnp.mean(floats, axis=-1, keepdims=True)
    shifted = floats - center
    spread = jnp.mean(shifted * shifted, axis=-1, keepdims=True)
    return (shifted * lax.rsqrt(spread + epsilon) * gain).astype(jnp.bfloat16)


def positions_of(stream):
    indices = jnp.arange(stream.shape[0], dtype=jnp.int32)
    boundary = jnp.concatenate([jnp.ones((1,), dtype=bool), stream[1:] != stream[:-1]])
    starting = lax.cummax(jnp.where(boundary, indices, jnp.zeros_like(indices)), axis=0)
    return (indices, starting)


def rotate_heads(vectors, offsets, rotary_dims):
    half_dims = rotary_dims // 2
    frequency = jnp.exp(
        jnp.arange(half_dims, dtype=jnp.float32) * (-2.0 * math.log(rotary_base) / rotary_dims)
    )
    angles = offsets.astype(jnp.float32)[:, None] * frequency[None, :]
    cosine = jnp.cos(angles)
    sine = jnp.sin(angles)
    floats = vectors.astype(jnp.float32)
    leading = floats[..., :half_dims]
    trailing = floats[..., half_dims:rotary_dims]
    rotated = jnp.concatenate(
        [
            leading * cosine - trailing * sine,
            trailing * cosine + leading * sine,
            floats[..., rotary_dims:],
        ],
        axis=-1,
    )
    return rotated.astype(jnp.bfloat16)


def shards_split_heads(
    hidden_states,
    attention_gain,
    feedforward_gain,
    heads_weight,
    output_weight,
    upward_weight,
    downward_weight,
    segments,
    page_targets,
):
    tensor_count = lax.axis_size("tensor")
    replica_count = lax.axis_size("dp")
    tensor_index = lax.axis_index("tensor")
    quarters = tensor_count // H
    quarter_width = HD // quarters
    quarter_index = tensor_index % quarters
    stream = segments[0]
    tokens_total = stream.shape[0]
    level_count = quarters.bit_length() - 1
    normed_attention = layer_norm(hidden_states, attention_gain)
    normed_feedforward = layer_norm(hidden_states, feedforward_gain)
    shard_rows = lax.all_gather(
        (normed_attention, normed_feedforward), "tensor", axis=0, tiled=True
    )
    joined_rows = jnp.dot(shard_rows[0], heads_weight, preferred_element_type=jnp.float32).astype(
        jnp.bfloat16
    )
    upward = jnp.dot(shard_rows[1], upward_weight, preferred_element_type=jnp.float32)
    hidden_rows = jax.nn.gelu(upward, approximate=False).astype(jnp.bfloat16)
    hidden = hidden_rows
    pieces = (
        joined_rows.reshape(tokens_total, 3, quarter_width)
        .transpose(1, 0, 2)
        .reshape(1, 3, tokens_total * quarter_width)
    )
    for bit_number in range(level_count):
        partner = swapped(shortened(pieces), "tensor", bit_number).astype(pieces.dtype)
        lower = tensor_index >> bit_number & 1 == 0
        pieces = jnp.where(
            lower, jnp.concatenate([pieces, partner], 0), jnp.concatenate([partner, pieces], 0)
        )
    whole_head = (
        pieces.reshape(quarters, 3, tokens_total, quarter_width)
        .transpose(1, 2, 0, 3)
        .reshape(3, tokens_total, HD)
    )
    indices, starting = positions_of(stream)
    offsets = indices - starting
    queries = rotate_heads(whole_head[0], offsets, ROT)
    keys = rotate_heads(whole_head[1], offsets, ROT)
    values = whole_head[2]
    block_rows = tokens_total // (2 * quarters)
    score_scale = HD ** (-0.5)

    def attend_block(block_number):
        first_row = block_number * block_rows
        block_queries = lax.dynamic_slice_in_dim(queries, first_row, block_rows, 0)
        query_segments = lax.dynamic_slice_in_dim(stream, first_row, block_rows, 0)
        query_indices = first_row + jnp.arange(block_rows, dtype=jnp.int32)
        lowest = lax.dynamic_index_in_dim(starting, first_row, 0, keepdims=False) // key_block
        highest = (first_row + block_rows + key_block - 1) // key_block

        def scores_of(key_number):
            key_first = key_number * key_block
            key_indices = key_first + jnp.arange(key_block, dtype=jnp.int32)
            scores = (
                jnp.dot(block_queries, keys.T, preferred_element_type=jnp.float32) * score_scale
            )
            allowed = (stream[None, :] == query_segments[:, None]) & (
                key_indices[None, :] <= query_indices[:, None]
            )
            return (scores, allowed)

        def find_peak(key_number, peak):
            scores, allowed = scores_of(key_number)
            return jnp.maximum(peak, jnp.max(jnp.where(allowed, scores, -jnp.inf), axis=1))

        peak = lax.fori_loop(
            lowest, highest, find_peak, jnp.full((block_rows,), -jnp.inf, jnp.float32)
        )

        def accumulate(key_number, state):
            weight_sum, mixed_sum = state
            scores, allowed = scores_of(key_number)
            weights = jnp.where(allowed, jnp.exp(scores - peak[:, None]), 0.0)
            mixed_next = mixed_sum + jnp.dot(
                weights.astype(jnp.bfloat16), values, preferred_element_type=jnp.float32
            )
            return (weight_sum + jnp.sum(weights, axis=1), mixed_next)

        start_state = (
            jnp.zeros((block_rows,), jnp.float32),
            jnp.zeros((block_rows, HD), jnp.float32),
        )
        weight_sum, mixed_sum = lax.fori_loop(lowest, highest, accumulate, start_state)
        return (mixed_sum / weight_sum[:, None]).astype(jnp.bfloat16)

    own_blocks = (2 * quarter_index, 2 * quarter_index + 1)
    own_rows = jnp.concatenate([attend_block(own_blocks[0]), attend_block(own_blocks[1])], 0)[None]
    for bit_number in range(level_count):
        partner = swapped(own_rows, "tensor", bit_number)
        lower = tensor_index >> bit_number & 1 == 0
        own_rows = jnp.where(
            lower, jnp.concatenate([own_rows, partner], 0), jnp.concatenate([partner, own_rows], 0)
        )
    attended = own_rows.reshape(tokens_total, HD)
    attended_quarter = lax.dynamic_slice_in_dim(
        attended, quarter_index * quarter_width, quarter_width, 1
    )
    hidden_rows = hidden
    summed = lax.psum_scatter(
        (
            jnp.dot(attended_quarter, output_weight, preferred_element_type=jnp.float32)
            + jnp.dot(hidden_rows, downward_weight, preferred_element_type=jnp.float32)
        ).astype(jnp.bfloat16),
        "tensor",
        scatter_dimension=0,
        tiled=True,
    ).astype(jnp.float32)
    layer_output = hidden_states.astype(jnp.float32) + summed
    key_quarter = lax.dynamic_slice_in_dim(keys, quarter_index * quarter_width, quarter_width, 1)
    value_quarter = joined_rows[:, 2 * quarter_width :]
    page_count = tokens_total // PAGE
    page_rows = jnp.concatenate([key_quarter, value_quarter], 1).reshape(
        page_count, PAGE * 2 * quarter_width
    )
    targets = page_targets[:, 0]
    page_numbers = jnp.arange(page_count, dtype=jnp.int32)
    earlier = jnp.sum(
        (
            (targets[None, :] == targets[:, None]) & (page_numbers[None, :] < page_numbers[:, None])
        ).astype(jnp.int32),
        axis=1,
    )
    capacity = 2 * page_count // replica_count
    slot_numbers = targets * capacity + earlier
    placing = (
        jnp.arange(replica_count * capacity, dtype=jnp.int32)[:, None] == slot_numbers[None, :]
    ).astype(jnp.bfloat16)
    outgoing = jnp.dot(placing, page_rows, preferred_element_type=jnp.float32).astype(jnp.bfloat16)
    outgoing = outgoing.reshape(replica_count, capacity, PAGE * 2 * quarter_width)
    incoming = lax.all_to_all(outgoing, "dp", split_axis=0, concat_axis=0, tiled=True)
    cache_pages = incoming.reshape(1, replica_count, capacity, PAGE, 2 * quarter_width)
    return (layer_output, cache_pages)


CORES = 2
CHIPS = 4
MIB = 1 << 20


def in_hbm(array):
    return pltpu.with_memory_space_constraint(array, pltpu.HBM)


def exchanged(block, axis, mask):
    count = lax.axis_size(axis)
    return lax.ppermute(block, axis, [(member, member ^ mask) for member in range(count)])


def vmem_specs(count):
    return [pl.BlockSpec(memory_space=pltpu.VMEM)] * count


def parameters(mebibytes):
    return pltpu.CompilerParams(vmem_limit_bytes=mebibytes * MIB)


def whereabouts():
    member = lax.axis_index("tensor")
    return member // CORES, member % CORES


def position_of(kind, half, block_rows):
    chip, core = whereabouts()
    return ((chip ^ kind) * CORES + (core ^ half)) * block_rows


def positions_along(first, shape, axis, block_rows):
    chip, core = whereabouts()
    bits = block_rows.bit_length() - 1
    place = first + lax.broadcasted_iota(jnp.int32, shape, axis)
    kind = place >> (bits + 1)
    half = (place >> bits) & 1
    return ((((chip ^ kind) << 1) | (core ^ half)) << bits) | (place & (block_rows - 1))


def normalize(blocks, gain_refs, normed_refs):
    piece = 16
    gains = [gain_ref[...] for gain_ref in gain_refs]
    for number, block_ref in enumerate(blocks):
        block_rows = block_ref.shape[0]
        for part in range(0, block_rows, piece):
            floats = block_ref[part : part + piece, :].astype(jnp.float32)
            center = jnp.mean(floats, axis=-1, keepdims=True)
            shifted = floats - center
            spread = jnp.mean(shifted * shifted, axis=-1, keepdims=True)
            scaled = shifted * lax.rsqrt(spread + epsilon)
            first = number * block_rows + part
            for gain, normed_ref in zip(gains, normed_refs):
                normed_ref[first : first + piece, :] = (scaled * gain).astype(jnp.bfloat16)


def project(normed_ref, heads_ref, table_refs, places, joined_ref, first):
    rows = normed_ref.shape[0]
    block_rows = rows // len(places)
    for component in range(3):
        columns = slice(component * HD, (component + 1) * HD)
        joined = jnp.dot(
            normed_ref[...], heads_ref[:, columns], preferred_element_type=jnp.float32
        ).astype(jnp.bfloat16)
        joined_ref[first : first + rows, columns] = joined
        if component < 2:
            cosine, sine_down, sine_up = [
                jnp.concatenate(
                    [
                        table_ref[pl.ds(pl.multiple_of(place, block_rows), block_rows), :]
                        for place in places
                    ],
                    0,
                )
                for table_ref in table_refs
            ]
            turning = joined[:, :128].astype(jnp.float32)
            turned = (
                turning * cosine
                + pltpu.roll(turning, 128 - ROT // 2, 1) * sine_down
                + pltpu.roll(turning, ROT // 2, 1) * sine_up
            )
            joined_ref[first : first + rows, component * HD : component * HD + 128] = turned.astype(
                jnp.bfloat16
            )


def hide(normed_ref, upward_ref, hidden_ref, place):
    chunk = 256
    rows = slice(place, place + normed_ref.shape[0])
    for first in range(0, upward_ref.shape[1], chunk):
        columns = slice(first, first + chunk)
        upward = jnp.dot(
            normed_ref[...], upward_ref[:, columns], preferred_element_type=jnp.float32
        )
        hidden = 0.5 * upward * (1.0 + lax.erf(upward * (0.5**0.5)))
        hidden_ref[rows, columns] = hidden.astype(jnp.bfloat16)


def attend(joined_ref, offsets_ref, first, rows, block_rows):
    tokens = joined_ref.shape[0]
    starts = [
        position_of(place // (2 * block_rows), (place // block_rows) % 2, block_rows)
        for place in range(first, first + rows, block_rows)
    ]
    reach = jnp.concatenate(
        [
            offsets_ref[pl.ds(pl.multiple_of(start, block_rows), block_rows), :]
            for start in starts
        ],
        0,
    )[:, :1].astype(jnp.int32)
    row = positions_along(first, (rows, 1), 0, block_rows)
    column = positions_along(0, (1, tokens), 1, block_rows)
    allowed = (column <= row) & (column >= row - reach)
    scores = lax.dot_general(
        joined_ref[first : first + rows, :HD],
        joined_ref[:, HD : 2 * HD],
        (((1,), (1,)), ((), ())),
        preferred_element_type=jnp.float32,
    ) * (HD ** (-0.5))
    peak = jnp.max(jnp.where(allowed, scores, -jnp.inf), axis=1, keepdims=True)
    weights = jnp.where(allowed, jnp.exp(scores - peak), 0.0)
    weight_sum = jnp.sum(weights, axis=1, keepdims=True)
    mixed = jnp.dot(
        weights.astype(jnp.bfloat16), joined_ref[:, 2 * HD :], preferred_element_type=jnp.float32
    )
    return (mixed / weight_sum).astype(jnp.bfloat16)


def make_tables(segments_ref, offsets_ref, cosine_ref, sine_down_ref, sine_up_ref):
    tokens = segments_ref.shape[1]
    shape = (tokens, tokens)
    rows = lax.broadcasted_iota(jnp.int32, shape, 0)
    columns = lax.broadcasted_iota(jnp.int32, shape, 1)
    across = jnp.broadcast_to(segments_ref[...], shape).astype(jnp.float32)
    down = jnp.sum(jnp.where(rows == columns, across, 0.0), axis=1, keepdims=True)
    earlier = (across == down) & (columns < rows)
    offsets = jnp.sum(jnp.where(earlier, 1.0, 0.0), axis=1, keepdims=True)
    offsets_ref[...] = jnp.broadcast_to(offsets, offsets_ref.shape)
    half = ROT // 2
    lane = lax.broadcasted_iota(jnp.int32, (tokens, 128), 1)
    step = (lane & (half - 1)).astype(jnp.float32)
    frequency = jnp.exp(step * (-2.0 * math.log(rotary_base) / ROT))
    angles = offsets * frequency
    sine = jnp.sin(angles)
    cosine_ref[...] = jnp.where(lane < ROT, jnp.cos(angles), 1.0)
    sine_down_ref[...] = jnp.where(lane < half, -sine, 0.0)
    sine_up_ref[...] = jnp.where((lane >= half) & (lane < ROT), sine, 0.0)


def copies_in(sources, targets, sems):
    copies = []
    for number, (source, target) in enumerate(zip(sources, targets)):
        parts = 4 if source.shape[0] >= 256 else 1
        rows = source.shape[0] // parts
        places = [pl.ds(part * rows, rows) for part in range(parts)]
        copies.append(
            [
                pltpu.make_async_copy(source.at[place], target.at[place], sems.at[number, part])
                for part, place in enumerate(places)
            ]
        )
    for copy in sum(copies, []):
        copy.start()
    return copies


def wait_for(copies):
    for copy in copies:
        copy.wait()


def own_kernel(count, *refs):
    sources, targets = refs[:count], refs[count : 2 * count]
    offsets_ref, *table_refs, joined_ref, hidden_ref = refs[2 * count : 2 * count + 6]
    attention_scr, feedforward_scr, sems = refs[2 * count + 6 :]
    copies = copies_in(sources, targets, sems)
    segments_ref, states_ref, *gain_refs, heads_ref, upward_ref = targets
    block_rows = states_ref.shape[0]
    wait_for(copies[0])
    make_tables(segments_ref, offsets_ref, *table_refs)
    for number in (1, 2, 3):
        wait_for(copies[number])
    normalize([states_ref], gain_refs, [attention_scr, feedforward_scr])
    wait_for(copies[4])
    places = [position_of(0, 0, block_rows)]
    project(attention_scr, heads_ref, table_refs, places, joined_ref, 0)
    wait_for(copies[5])
    hide(feedforward_scr, upward_ref, hidden_ref, 0)


def own_rows(staged):
    tokens = staged[0].shape[1]
    rows, width = staged[1].shape
    hidden_width = staged[5].shape[1]
    shapes = [pltpu.VMEM(array.shape, array.dtype) for array in staged]
    shapes += [pltpu.VMEM((tokens, 128), jnp.float32)] * 4
    shapes += [
        pltpu.VMEM((rows, 3 * HD), jnp.bfloat16),
        pltpu.VMEM((rows, hidden_width), jnp.bfloat16),
    ]
    count = len(staged)
    return pl.pallas_call(
        functools.partial(own_kernel, count),
        out_shape=shapes,
        in_specs=[pl.BlockSpec(memory_space=pltpu.HBM)] * count,
        out_specs=vmem_specs(len(shapes)),
        scratch_shapes=[
            pltpu.VMEM((rows, width), jnp.bfloat16),
            pltpu.VMEM((rows, width), jnp.bfloat16),
            pltpu.SemaphoreType.DMA((count, 4)),
        ],
        compiler_params=parameters(12),
        cost_estimate=pl.CostEstimate(
            flops=2 * rows * width * (3 * HD + hidden_width),
            bytes_accessed=sum(array.nbytes for array in staged),
            transcendentals=rows * hidden_width,
        ),
        name="own_rows",
    )(*[in_hbm(array) for array in staged])


def middle_kernel(origins, *refs):
    count = len(origins)
    blocks, (gain_a, gain_f, heads_ref, upward_ref) = refs[:count], refs[count : count + 4]
    table_refs, source_ref = refs[count + 4 : count + 7], refs[count + 7]
    joined_ref, hidden_ref, target_ref = refs[count + 8 : count + 11]
    attention_scr, feedforward_scr, sems = refs[count + 11 :]
    (copies,) = copies_in([source_ref], [target_ref], sems)
    block_rows = blocks[0].shape[0]
    normalize(blocks, [gain_a, gain_f], [attention_scr, feedforward_scr])
    places = [position_of(kind, half, block_rows) for kind, half in origins]
    project(attention_scr, heads_ref, table_refs, places, joined_ref, 0)
    hide(feedforward_scr, upward_ref, hidden_ref, 0)
    wait_for(copies)


def middle_rows(name, origins, blocks, gains, weights, tables, staged):
    block_rows, width = blocks[0].shape
    rows = len(blocks) * block_rows
    hidden_width = weights[1].shape[1]
    return pl.pallas_call(
        functools.partial(middle_kernel, origins),
        out_shape=[
            pltpu.VMEM((rows, 3 * HD), jnp.bfloat16),
            pltpu.VMEM((rows, hidden_width), jnp.bfloat16),
            pltpu.VMEM(staged.shape, staged.dtype),
        ],
        in_specs=vmem_specs(len(blocks) + 2 + 2 + 3) + [pl.BlockSpec(memory_space=pltpu.HBM)],
        out_specs=vmem_specs(3),
        scratch_shapes=[
            pltpu.VMEM((rows, width), jnp.bfloat16),
            pltpu.VMEM((rows, width), jnp.bfloat16),
            pltpu.SemaphoreType.DMA((1, 4)),
        ],
        compiler_params=parameters(12),
        cost_estimate=pl.CostEstimate(
            flops=2 * rows * width * (3 * HD + hidden_width),
            bytes_accessed=staged.nbytes,
            transcendentals=rows * hidden_width,
        ),
        name=name,
    )(*blocks, *gains, *weights, *tables, in_hbm(staged))


def last_kernel(*refs):
    blocks, (gain_a, gain_f, heads_ref, upward_ref, downward_ref, output_ref) = refs[:2], refs[2:8]
    offsets_ref, *table_refs = refs[8:12]
    pieces = refs[12:15]
    joined_ref, sibling_ref, own_ref, attention_scr, feedforward_scr, hidden_scr = refs[15:]
    block_rows = blocks[0].shape[0]
    tokens = joined_ref.shape[0]
    first = tokens - CORES * block_rows
    normalize(blocks, [gain_a, gain_f], [attention_scr, feedforward_scr])
    for kind in range(CHIPS - 1):
        for half in range(CORES):
            place = (kind * CORES + half) * block_rows
            joined_ref[place : place + block_rows, :] = piece_of(pieces, kind, half, block_rows)
    places = [position_of(CHIPS - 1, half, block_rows) for half in range(CORES)]
    project(attention_scr, heads_ref, table_refs, places, joined_ref, first)
    hide(feedforward_scr, upward_ref, hidden_scr, 0)
    attended = attend(joined_ref, offsets_ref, first, CORES * block_rows, block_rows)
    partial_sums(attended, hidden_scr[...], output_ref, downward_ref, [own_ref], [sibling_ref])


def piece_of(pieces, kind, half, block_rows):
    piece = 2 if half else min(kind, 1)
    place = (kind if half else (0, 1, 0)[kind]) * block_rows
    return pieces[piece][place : place + block_rows, :]


def partial_sums(attended, hidden, output_ref, downward_ref, own_refs, sibling_refs):
    rows = attended.shape[0] // (2 * len(own_refs))
    chunk = 512
    for begin in range(0, downward_ref.shape[1], chunk):
        columns = slice(begin, begin + chunk)
        partial = jnp.dot(
            hidden, downward_ref[:, columns], preferred_element_type=jnp.float32
        ) + jnp.dot(attended, output_ref[:, columns], preferred_element_type=jnp.float32)
        for number, (own_ref, sibling_ref) in enumerate(zip(own_refs, sibling_refs)):
            first = 2 * number * rows
            middle = first + rows
            own_ref[:, columns] = partial[first:middle]
            sibling_ref[:, columns] = partial[middle : middle + rows].astype(jnp.bfloat16)


def last_rows(blocks, gains, weights, tables, pieces):
    block_rows, width = blocks[0].shape
    rows = len(blocks) * block_rows
    hidden_width = weights[1].shape[1]
    tokens = CHIPS * CORES * block_rows
    return pl.pallas_call(
        last_kernel,
        out_shape=[
            pltpu.VMEM((tokens, 3 * HD), jnp.bfloat16),
            pltpu.VMEM((block_rows, width), jnp.bfloat16),
            pltpu.VMEM((block_rows, width), jnp.float32),
        ],
        in_specs=vmem_specs(len(blocks) + 2 + 4 + 4 + 3),
        out_specs=vmem_specs(3),
        scratch_shapes=[
            pltpu.VMEM((rows, width), jnp.bfloat16),
            pltpu.VMEM((rows, width), jnp.bfloat16),
            pltpu.VMEM((rows, hidden_width), jnp.bfloat16),
        ],
        compiler_params=parameters(12),
        cost_estimate=pl.CostEstimate(
            flops=2 * rows * width * (3 * HD + HD + 2 * hidden_width),
            bytes_accessed=MIB,
            transcendentals=rows * hidden_width,
        ),
        name="last_rows",
    )(*blocks, *gains, *weights, *tables, *pieces)


def kind_kernel(kinds, joined_ref, offsets_ref, output_ref, downward_ref, *refs):
    pieces, refs = refs[:3], refs[3:]
    count = len(kinds)
    siblings, owns = refs[:count], refs[count : 2 * count]
    block_rows = owns[0].shape[0]
    rows = CORES * block_rows * count
    attended = attend(joined_ref, offsets_ref, kinds[0] * CORES * block_rows, rows, block_rows)
    hidden = jnp.concatenate(
        [piece_of(pieces, kind, half, block_rows) for kind in kinds for half in range(CORES)], 0
    )
    partial_sums(attended, hidden, output_ref, downward_ref, owns, siblings)


def kind_rows(name, kinds, joined, offsets, weights, pieces):
    block_rows = pieces[0].shape[0]
    output_weight, downward_weight = weights
    width = output_weight.shape[1]
    shape = (block_rows, width)
    count = len(kinds)
    tokens = joined.shape[0]
    return pl.pallas_call(
        functools.partial(kind_kernel, kinds),
        out_shape=[pltpu.VMEM(shape, jnp.bfloat16)] * count + [pltpu.VMEM(shape, jnp.float32)] * count,
        in_specs=vmem_specs(7),
        out_specs=vmem_specs(2 * count),
        compiler_params=parameters(12),
        cost_estimate=pl.CostEstimate(
            flops=4 * block_rows * count * width * (HD + downward_weight.shape[0]),
            bytes_accessed=MIB,
            transcendentals=2 * block_rows * count * tokens,
        ),
        name=name,
    )(joined, offsets, output_weight, downward_weight, *pieces)


def pages_kernel(block_rows, joined_ref, targets_ref, *refs):
    pages_refs, (named_ref, counts_ref, slots_ref, sem) = refs[:-4], refs[-4:]
    naming = pltpu.make_async_copy(targets_ref, named_ref, sem)
    naming.start()
    tokens = joined_ref.shape[0]
    for page_ref in pages_refs:
        page_ref[...] = jnp.zeros(page_ref.shape, page_ref.dtype)
    chip, core = whereabouts()
    group = lax.axis_index("dp")
    naming.wait()
    for target in range(len(pages_refs)):
        counts_ref[target] = 0
    for page in range(tokens // PAGE):
        target = named_ref[page]
        slot = counts_ref[target]
        counts_ref[target] = slot + 1
        slots_ref[page] = slot
    capacity = pages_refs[0].shape[0]
    for place in range(0, tokens, PAGE):
        kind, half = place // (CORES * block_rows), (place // block_rows) % CORES
        start = ((chip ^ kind) * CORES + (core ^ half)) * block_rows + place % block_rows
        page = start // PAGE
        target = named_ref[page]
        slot = jnp.minimum(slots_ref[page], capacity - 1)
        for mask, page_ref in enumerate(pages_refs):

            @pl.when(target == (group ^ mask))
            def _():
                page_ref[pl.ds(slot, 1)] = joined_ref[place : place + PAGE, HD:][None]


def cached_pages(joined, targets, replica_count):
    tokens = joined.shape[0]
    page_count = tokens // PAGE
    capacity = 2 * page_count // replica_count
    shapes = [pltpu.VMEM((capacity, PAGE, 2 * HD), jnp.bfloat16)] * replica_count
    return pl.pallas_call(
        functools.partial(pages_kernel, tokens // (CHIPS * CORES)),
        out_shape=shapes,
        in_specs=vmem_specs(1) + [pl.BlockSpec(memory_space=pltpu.HBM)],
        out_specs=vmem_specs(len(shapes)),
        scratch_shapes=[
            pltpu.SMEM(targets.shape, jnp.int32),
            pltpu.SMEM((replica_count,), jnp.int32),
            pltpu.SMEM((page_count,), jnp.int32),
            pltpu.SemaphoreType.DMA(()),
        ],
        compiler_params=parameters(8),
        cost_estimate=pl.CostEstimate(flops=0, bytes_accessed=MIB, transcendentals=0),
        name="cached_pages",
    )(joined, in_hbm(targets))


def add_kernel(*refs):
    total = refs[0][...].astype(jnp.float32)
    for ref in refs[1:-1]:
        total = total + ref[...].astype(jnp.float32)
    refs[-1][...] = total.astype(refs[-1].dtype)


def added(name, *parts):
    return pl.pallas_call(
        add_kernel,
        out_shape=pltpu.VMEM(parts[0].shape, jnp.bfloat16),
        in_specs=vmem_specs(len(parts)),
        out_specs=pl.BlockSpec(memory_space=pltpu.VMEM),
        compiler_params=parameters(4),
        name=name,
    )(*parts)


def near_kernel(*refs):
    ones, zeros, (first_ref, base_ref) = refs[:2], refs[2:5], refs[5:]
    first = ones[0][...] + ones[1][...].astype(jnp.float32)
    first_ref[...] = first.astype(jnp.bfloat16)
    base = zeros[0][...] + zeros[1][...].astype(jnp.float32)
    base_ref[...] = zeros[2][...].astype(jnp.float32) + base


def near_sums(ones, zeros):
    shape = ones[0].shape
    return pl.pallas_call(
        near_kernel,
        out_shape=[pltpu.VMEM(shape, jnp.bfloat16), pltpu.VMEM(shape, jnp.float32)],
        in_specs=vmem_specs(5),
        out_specs=vmem_specs(2),
        compiler_params=parameters(4),
        name="near_sums",
    )(*ones, *zeros)


def place_kernel(*refs):
    group = lax.axis_index("dp")
    pages, (cache_ref, sems) = refs[:-2], refs[-2:]
    copies = [
        pltpu.make_async_copy(page_ref, cache_ref.at[0, group ^ mask], sems.at[mask])
        for mask, page_ref in enumerate(pages)
    ]
    for copy in copies:
        copy.start()
    for copy in copies:
        copy.wait()


def placed(pages):
    count = len(pages)
    return pl.pallas_call(
        place_kernel,
        out_shape=jax.ShapeDtypeStruct((1, count) + pages[0].shape, pages[0].dtype),
        in_specs=[pl.BlockSpec(memory_space=pl.ANY)] * count,
        out_specs=pl.BlockSpec(memory_space=pltpu.HBM),
        scratch_shapes=[pltpu.SemaphoreType.DMA((count,))],
        compiler_params=parameters(4),
        name="placed",
    )(*pages)


def finish_kernel(base_ref, *refs):
    total = base_ref[...]
    for part_ref in refs[:-1]:
        total = total + part_ref[...].astype(jnp.float32)
    refs[-1][...] = total


def finished(base, parts):
    return pl.pallas_call(
        finish_kernel,
        out_shape=jax.ShapeDtypeStruct(base.shape, base.dtype),
        in_specs=vmem_specs(1 + len(parts)),
        out_specs=pl.BlockSpec(memory_space=pltpu.VMEM),
        compiler_params=parameters(4),
        name="finished",
    )(base, *parts)


def shards_whole_heads(
    hidden_states,
    attention_gain,
    feedforward_gain,
    heads_weight,
    output_weight,
    upward_weight,
    downward_weight,
    segments,
    page_targets,
):
    replica_count = lax.axis_size("dp")
    to_chip = [mask * CORES for mask in range(CHIPS)]
    second = exchanged(hidden_states, "tensor", to_chip[2])
    first = exchanged(hidden_states, "tensor", to_chip[1])
    beside = exchanged(hidden_states, "tensor", 1)
    staged = (
        segments,
        hidden_states,
        attention_gain[None],
        feedforward_gain[None],
        heads_weight,
        upward_weight,
    )
    staged = own_rows(staged)
    hidden, gains, (heads, upward), tables = staged[1], staged[2:4], staged[4:6], staged[6:10]
    own_joined, own_hidden = staged[10:]

    second, first, own_joined = lax.optimization_barrier((second, first, own_joined))
    third = exchanged(second, "tensor", to_chip[1])
    second_beside = exchanged(second, "tensor", 1)
    first_beside = exchanged(first, "tensor", 1)
    there_joined, there_hidden, downward = middle_rows(
        "there_rows",
        ((2, 0), (1, 0)),
        (second, first),
        gains,
        (heads, upward),
        tables[1:],
        downward_weight,
    )
    third, there_joined = lax.optimization_barrier((third, there_joined))
    third_beside = exchanged(third, "tensor", 1)
    beside_joined, beside_hidden, output = middle_rows(
        "beside_rows",
        ((0, 1), (1, 1), (2, 1)),
        (beside, first_beside, second_beside),
        gains,
        (heads, upward),
        tables[1:],
        output_weight,
    )
    joined, sibling, own = last_rows(
        (third, third_beside),
        gains,
        (heads, upward, downward, output),
        tables,
        (own_joined, there_joined, beside_joined),
    )

    pieces = (own_hidden, there_hidden, beside_hidden)
    received = exchanged(sibling, "tensor", 1)
    second_sibling, second_own = kind_rows(
        "second_rows", (2,), joined, tables[0], (output, downward), pieces
    )
    third_sum = added("third_added", own, received)
    third_sum, second_sibling, joined = lax.optimization_barrier(
        (third_sum, second_sibling, joined)
    )
    passing = exchanged(third_sum, "tensor", to_chip[1])
    second_received = exchanged(second_sibling, "tensor", 1)
    zero_sibling, first_sibling, zero_own, first_own = kind_rows(
        "near_rows", (0, 1), joined, tables[0], (output, downward), pieces
    )
    first_received = exchanged(first_sibling, "tensor", 1)
    zero_received = exchanged(zero_sibling, "tensor", 1)
    pages = cached_pages(joined, page_targets[:, 0], replica_count)
    arriving = [pages[0]] + [
        exchanged(pages[mask], "dp", mask) for mask in range(1, replica_count)
    ]
    second_sum = added("second_added", second_own, passing, second_received)
    from_second = exchanged(second_sum, "tensor", to_chip[2])
    first_sum, base = near_sums((first_own, first_received), (zero_own, zero_received, hidden))
    from_first = exchanged(first_sum, "tensor", to_chip[1])
    cache_pages = placed(arriving)
    base, cache_pages = lax.optimization_barrier((base, cache_pages))
    return (finished(base, (from_second, from_first)), cache_pages)


def solution(mesh):
    whole_heads = mesh.shape["tensor"] == H and mesh.shape["dp"] == 4
    shards = shards_whole_heads if whole_heads else shards_split_heads
    in_specs = (
        P(("dp", "tensor"), None),
        P(),
        P(),
        P(None, "tensor"),
        P("tensor", None),
        P(None, "tensor"),
        P("tensor", None),
        P("dp", None),
        P("dp", None),
    )
    out_specs = (P(("dp", "tensor"), None), P("dp", None, None, None, "tensor"))
    return jax.shard_map(shards, mesh=mesh, in_specs=in_specs, out_specs=out_specs, check_vma=False)
```

```python
import functools
import math

import jax
import jax.numpy as jnp
from jax import lax
from jax.experimental import pallas as pl
from jax.experimental.pallas import tpu as pltpu
from jax.sharding import PartitionSpec as P

H = 8
HD = 256
ROT = 64
PAGE = 16


epsilon = 1e-05
rotary_base = 10000.0
key_block = 256


def shortened(array):

    def short(part):
        return part.astype(jnp.bfloat16) if part.dtype == jnp.float32 else part

    return jax.tree.map(short, array)


def swapped(block, axis, apart):
    count = lax.axis_size(axis)
    route = []
    for low in range(count):
        high = low | 1 << apart
        if high != low and high < count:
            route += [(low, high), (high, low)]
    return lax.ppermute(block, axis, route)


def layer_norm(values, gain):
    floats = values.astype(jnp.float32)
    center = jnp.mean(floats, axis=-1, keepdims=True)
    shifted = floats - center
    spread = jnp.mean(shifted * shifted, axis=-1, keepdims=True)
    return (shifted * lax.rsqrt(spread + epsilon) * gain).astype(jnp.bfloat16)


def positions_of(stream):
    indices = jnp.arange(stream.shape[0], dtype=jnp.int32)
    boundary = jnp.concatenate([jnp.ones((1,), dtype=bool), stream[1:] != stream[:-1]])
    starting = lax.cummax(jnp.where(boundary, indices, jnp.zeros_like(indices)), axis=0)
    return (indices, starting)


def rotate_heads(vectors, offsets, rotary_dims):
    half_dims = rotary_dims // 2
    frequency = jnp.exp(
        jnp.arange(half_dims, dtype=jnp.float32) * (-2.0 * math.log(rotary_base) / rotary_dims)
    )
    angles = offsets.astype(jnp.float32)[:, None] * frequency[None, :]
    cosine = jnp.cos(angles)
    sine = jnp.sin(angles)
    floats = vectors.astype(jnp.float32)
    leading = floats[..., :half_dims]
    trailing = floats[..., half_dims:rotary_dims]
    rotated = jnp.concatenate(
        [
            leading * cosine - trailing * sine,
            trailing * cosine + leading * sine,
            floats[..., rotary_dims:],
        ],
        axis=-1,
    )
    return rotated.astype(jnp.bfloat16)


def shards_split_heads(
    hidden_states,
    attention_gain,
    feedforward_gain,
    heads_weight,
    output_weight,
    upward_weight,
    downward_weight,
    segments,
    page_targets,
):
    tensor_count = lax.axis_size("tensor")
    replica_count = lax.axis_size("dp")
    tensor_index = lax.axis_index("tensor")
    quarters = tensor_count // H
    quarter_width = HD // quarters
    quarter_index = tensor_index % quarters
    stream = segments[0]
    tokens_total = stream.shape[0]
    level_count = quarters.bit_length() - 1
    normed_attention = layer_norm(hidden_states, attention_gain)
    normed_feedforward = layer_norm(hidden_states, feedforward_gain)
    shard_rows = lax.all_gather(
        (normed_attention, normed_feedforward), "tensor", axis=0, tiled=True
    )
    joined_rows = jnp.dot(shard_rows[0], heads_weight, preferred_element_type=jnp.float32).astype(
        jnp.bfloat16
    )
    upward = jnp.dot(shard_rows[1], upward_weight, preferred_element_type=jnp.float32)
    hidden_rows = jax.nn.gelu(upward, approximate=False).astype(jnp.bfloat16)
    hidden = hidden_rows
    pieces = (
        joined_rows.reshape(tokens_total, 3, quarter_width)
        .transpose(1, 0, 2)
        .reshape(1, 3, tokens_total * quarter_width)
    )
    for bit_number in range(level_count):
        partner = swapped(shortened(pieces), "tensor", bit_number).astype(pieces.dtype)
        lower = tensor_index >> bit_number & 1 == 0
        pieces = jnp.where(
            lower, jnp.concatenate([pieces, partner], 0), jnp.concatenate([partner, pieces], 0)
        )
    whole_head = (
        pieces.reshape(quarters, 3, tokens_total, quarter_width)
        .transpose(1, 2, 0, 3)
        .reshape(3, tokens_total, HD)
    )
    indices, starting = positions_of(stream)
    offsets = indices - starting
    queries = rotate_heads(whole_head[0], offsets, ROT)
    keys = rotate_heads(whole_head[1], offsets, ROT)
    values = whole_head[2]
    block_rows = tokens_total // (2 * quarters)
    score_scale = HD ** (-0.5)

    def attend_block(block_number):
        first_row = block_number * block_rows
        block_queries = lax.dynamic_slice_in_dim(queries, first_row, block_rows, 0)
        query_segments = lax.dynamic_slice_in_dim(stream, first_row, block_rows, 0)
        query_indices = first_row + jnp.arange(block_rows, dtype=jnp.int32)
        lowest = lax.dynamic_index_in_dim(starting, first_row, 0, keepdims=False) // key_block
        highest = (first_row + block_rows + key_block - 1) // key_block

        def scores_of(key_number):
            key_first = key_number * key_block
            key_indices = key_first + jnp.arange(key_block, dtype=jnp.int32)
            scores = (
                jnp.dot(block_queries, keys.T, preferred_element_type=jnp.float32) * score_scale
            )
            allowed = (stream[None, :] == query_segments[:, None]) & (
                key_indices[None, :] <= query_indices[:, None]
            )
            return (scores, allowed)

        def find_peak(key_number, peak):
            scores, allowed = scores_of(key_number)
            return jnp.maximum(peak, jnp.max(jnp.where(allowed, scores, -jnp.inf), axis=1))

        peak = lax.fori_loop(
            lowest, highest, find_peak, jnp.full((block_rows,), -jnp.inf, jnp.float32)
        )

        def accumulate(key_number, state):
            weight_sum, mixed_sum = state
            scores, allowed = scores_of(key_number)
            weights = jnp.where(allowed, jnp.exp(scores - peak[:, None]), 0.0)
            mixed_next = mixed_sum + jnp.dot(
                weights.astype(jnp.bfloat16), values, preferred_element_type=jnp.float32
            )
            return (weight_sum + jnp.sum(weights, axis=1), mixed_next)

        start_state = (
            jnp.zeros((block_rows,), jnp.float32),
            jnp.zeros((block_rows, HD), jnp.float32),
        )
        weight_sum, mixed_sum = lax.fori_loop(lowest, highest, accumulate, start_state)
        return (mixed_sum / weight_sum[:, None]).astype(jnp.bfloat16)

    own_blocks = (2 * quarter_index, 2 * quarter_index + 1)
    own_rows = jnp.concatenate([attend_block(own_blocks[0]), attend_block(own_blocks[1])], 0)[None]
    for bit_number in range(level_count):
        partner = swapped(own_rows, "tensor", bit_number)
        lower = tensor_index >> bit_number & 1 == 0
        own_rows = jnp.where(
            lower, jnp.concatenate([own_rows, partner], 0), jnp.concatenate([partner, own_rows], 0)
        )
    attended = own_rows.reshape(tokens_total, HD)
    attended_quarter = lax.dynamic_slice_in_dim(
        attended, quarter_index * quarter_width, quarter_width, 1
    )
    hidden_rows = hidden
    summed = lax.psum_scatter(
        (
            jnp.dot(attended_quarter, output_weight, preferred_element_type=jnp.float32)
            + jnp.dot(hidden_rows, downward_weight, preferred_element_type=jnp.float32)
        ).astype(jnp.bfloat16),
        "tensor",
        scatter_dimension=0,
        tiled=True,
    ).astype(jnp.float32)
    layer_output = hidden_states.astype(jnp.float32) + summed
    key_quarter = lax.dynamic_slice_in_dim(keys, quarter_index * quarter_width, quarter_width, 1)
    value_quarter = joined_rows[:, 2 * quarter_width :]
    page_count = tokens_total // PAGE
    page_rows = jnp.concatenate([key_quarter, value_quarter], 1).reshape(
        page_count, PAGE * 2 * quarter_width
    )
    targets = page_targets[:, 0]
    page_numbers = jnp.arange(page_count, dtype=jnp.int32)
    earlier = jnp.sum(
        (
            (targets[None, :] == targets[:, None]) & (page_numbers[None, :] < page_numbers[:, None])
        ).astype(jnp.int32),
        axis=1,
    )
    capacity = 2 * page_count // replica_count
    slot_numbers = targets * capacity + earlier
    placing = (
        jnp.arange(replica_count * capacity, dtype=jnp.int32)[:, None] == slot_numbers[None, :]
    ).astype(jnp.bfloat16)
    outgoing = jnp.dot(placing, page_rows, preferred_element_type=jnp.float32).astype(jnp.bfloat16)
    outgoing = outgoing.reshape(replica_count, capacity, PAGE * 2 * quarter_width)
    incoming = lax.all_to_all(outgoing, "dp", split_axis=0, concat_axis=0, tiled=True)
    cache_pages = incoming.reshape(1, replica_count, capacity, PAGE, 2 * quarter_width)
    return (layer_output, cache_pages)


CORES = 2
CHIPS = 4
MIB = 1 << 20


def in_hbm(array):
    return pltpu.with_memory_space_constraint(array, pltpu.HBM)


def exchanged(block, axis, mask):
    count = lax.axis_size(axis)
    return lax.ppermute(block, axis, [(member, member ^ mask) for member in range(count)])


def vmem_specs(count):
    return [pl.BlockSpec(memory_space=pltpu.VMEM)] * count


def parameters(mebibytes):
    return pltpu.CompilerParams(vmem_limit_bytes=mebibytes * MIB)


def whereabouts():
    member = lax.axis_index("tensor")
    return member // CORES, member % CORES


def position_of(kind, half, block_rows):
    chip, core = whereabouts()
    return ((chip ^ kind) * CORES + (core ^ half)) * block_rows


def positions_along(first, shape, axis, block_rows):
    chip, core = whereabouts()
    bits = block_rows.bit_length() - 1
    place = first + lax.broadcasted_iota(jnp.int32, shape, axis)
    kind = place >> (bits + 1)
    half = (place >> bits) & 1
    return ((((chip ^ kind) << 1) | (core ^ half)) << bits) | (place & (block_rows - 1))


def normalize(blocks, gain_refs, normed_refs):
    piece = 16
    gains = [gain_ref[...] for gain_ref in gain_refs]
    for number, block_ref in enumerate(blocks):
        block_rows = block_ref.shape[0]
        for part in range(0, block_rows, piece):
            floats = block_ref[part : part + piece, :].astype(jnp.float32)
            center = jnp.mean(floats, axis=-1, keepdims=True)
            shifted = floats - center
            spread = jnp.mean(shifted * shifted, axis=-1, keepdims=True)
            scaled = shifted * lax.rsqrt(spread + epsilon)
            first = number * block_rows + part
            for gain, normed_ref in zip(gains, normed_refs):
                normed_ref[first : first + piece, :] = (scaled * gain).astype(jnp.bfloat16)


def project(normed_ref, heads_ref, table_refs, places, joined_ref, first):
    rows = normed_ref.shape[0]
    block_rows = rows // len(places)
    for component in range(3):
        columns = slice(component * HD, (component + 1) * HD)
        joined = jnp.dot(
            normed_ref[...], heads_ref[:, columns], preferred_element_type=jnp.float32
        ).astype(jnp.bfloat16)
        joined_ref[first : first + rows, columns] = joined
        if component < 2:
            cosine, sine_down, sine_up = [
                jnp.concatenate(
                    [
                        table_ref[pl.ds(pl.multiple_of(place, block_rows), block_rows), :]
                        for place in places
                    ],
                    0,
                )
                for table_ref in table_refs
            ]
            turning = joined[:, :128].astype(jnp.float32)
            turned = (
                turning * cosine
                + pltpu.roll(turning, 128 - ROT // 2, 1) * sine_down
                + pltpu.roll(turning, ROT // 2, 1) * sine_up
            )
            joined_ref[first : first + rows, component * HD : component * HD + 128] = turned.astype(
                jnp.bfloat16
            )


def hide(normed_ref, upward_ref, hidden_ref, place):
    chunk = 256
    rows = slice(place, place + normed_ref.shape[0])
    for first in range(0, upward_ref.shape[1], chunk):
        columns = slice(first, first + chunk)
        upward = jnp.dot(
            normed_ref[...], upward_ref[:, columns], preferred_element_type=jnp.float32
        )
        hidden = 0.5 * upward * (1.0 + lax.erf(upward * (0.5**0.5)))
        hidden_ref[rows, columns] = hidden.astype(jnp.bfloat16)


def attend(joined_ref, offsets_ref, first, rows, block_rows):
    tokens = joined_ref.shape[0]
    starts = [
        position_of(place // (2 * block_rows), (place // block_rows) % 2, block_rows)
        for place in range(first, first + rows, block_rows)
    ]
    reach = jnp.concatenate(
        [
            offsets_ref[pl.ds(pl.multiple_of(start, block_rows), block_rows), :]
            for start in starts
        ],
        0,
    )[:, :1].astype(jnp.int32)
    row = positions_along(first, (rows, 1), 0, block_rows)
    column = positions_along(0, (1, tokens), 1, block_rows)
    allowed = (column <= row) & (column >= row - reach)
    scores = lax.dot_general(
        joined_ref[first : first + rows, :HD],
        joined_ref[:, HD : 2 * HD],
        (((1,), (1,)), ((), ())),
        preferred_element_type=jnp.float32,
    ) * (HD ** (-0.5))
    peak = jnp.max(jnp.where(allowed, scores, -jnp.inf), axis=1, keepdims=True)
    weights = jnp.where(allowed, jnp.exp(scores - peak), 0.0)
    weight_sum = jnp.sum(weights, axis=1, keepdims=True)
    mixed = jnp.dot(
        weights.astype(jnp.bfloat16), joined_ref[:, 2 * HD :], preferred_element_type=jnp.float32
    )
    return (mixed / weight_sum).astype(jnp.bfloat16)


def make_tables(segments_ref, offsets_ref, cosine_ref, sine_down_ref, sine_up_ref):
    tokens = segments_ref.shape[1]
    shape = (tokens, tokens)
    rows = lax.broadcasted_iota(jnp.int32, shape, 0)
    columns = lax.broadcasted_iota(jnp.int32, shape, 1)
    across = jnp.broadcast_to(segments_ref[...], shape).astype(jnp.float32)
    down = jnp.sum(jnp.where(rows == columns, across, 0.0), axis=1, keepdims=True)
    earlier = (across == down) & (columns < rows)
    offsets = jnp.sum(jnp.where(earlier, 1.0, 0.0), axis=1, keepdims=True)
    offsets_ref[...] = jnp.broadcast_to(offsets, offsets_ref.shape)
    half = ROT // 2
    lane = lax.broadcasted_iota(jnp.int32, (tokens, 128), 1)
    step = (lane & (half - 1)).astype(jnp.float32)
    frequency = jnp.exp(step * (-2.0 * math.log(rotary_base) / ROT))
    angles = offsets * frequency
    sine = jnp.sin(angles)
    cosine_ref[...] = jnp.where(lane < ROT, jnp.cos(angles), 1.0)
    sine_down_ref[...] = jnp.where(lane < half, -sine, 0.0)
    sine_up_ref[...] = jnp.where((lane >= half) & (lane < ROT), sine, 0.0)


def make_destinations(targets_ref, destinations_ref, replica_count, block_rows):
    page_count = targets_ref.shape[1]
    tokens = destinations_ref.shape[1]
    capacity = 2 * page_count // replica_count
    square = (page_count, page_count)
    rows = lax.broadcasted_iota(jnp.int32, square, 0)
    columns = lax.broadcasted_iota(jnp.int32, square, 1)
    across = jnp.broadcast_to(targets_ref[...], square).astype(jnp.float32)
    down = jnp.sum(jnp.where(rows == columns, across, 0.0), axis=1, keepdims=True)
    earlier = jnp.where((across == down) & (columns < rows), 1.0, 0.0)
    slots = jnp.sum(earlier, axis=1, keepdims=True).astype(jnp.int32)
    slots = (down.astype(jnp.int32) ^ lax.axis_index("dp")) * capacity + slots
    positions = positions_along(0, (1, tokens), 1, block_rows)
    bits = PAGE.bit_length() - 1
    pages = lax.broadcasted_iota(jnp.int32, (page_count, tokens), 0)
    chosen = jnp.where(pages == positions >> bits, slots.astype(jnp.float32), 0.0)
    slot = jnp.sum(chosen, axis=0, keepdims=True).astype(jnp.int32)
    destinations_ref[...] = slot * PAGE + (positions & (PAGE - 1))


def copies_in(sources, targets, sems):
    copies = []
    for number, (source, target) in enumerate(zip(sources, targets)):
        parts = 4 if source.shape[0] >= 256 else 1
        rows = source.shape[0] // parts
        places = [pl.ds(part * rows, rows) for part in range(parts)]
        copies.append(
            [
                pltpu.make_async_copy(source.at[place], target.at[place], sems.at[number, part])
                for part, place in enumerate(places)
            ]
        )
    for copy in sum(copies, []):
        copy.start()
    return copies


def wait_for(copies):
    for copy in copies:
        copy.wait()


def own_kernel(count, replica_count, *refs):
    sources, targets = refs[:count], refs[count : 2 * count]
    offsets_ref, *table_refs, destinations_ref, joined_ref, hidden_ref = refs[2 * count : -3]
    attention_scr, feedforward_scr, sems = refs[-3:]
    copies = copies_in(sources, targets, sems)
    segments_ref, targets_ref, states_ref, *gain_refs, heads_ref, upward_ref, _ = targets
    block_rows = states_ref.shape[0]
    wait_for(copies[0])
    make_tables(segments_ref, offsets_ref, *table_refs)
    wait_for(copies[1])
    make_destinations(targets_ref, destinations_ref, replica_count, block_rows)
    for number in (2, 3, 4):
        wait_for(copies[number])
    normalize([states_ref], gain_refs, [attention_scr, feedforward_scr])
    wait_for(copies[5])
    places = [position_of(0, 0, block_rows)]
    project(attention_scr, heads_ref, table_refs, places, joined_ref, 0)
    wait_for(copies[6])
    hide(feedforward_scr, upward_ref, hidden_ref, 0)
    wait_for(copies[7])


def own_rows(staged, replica_count):
    tokens = staged[0].shape[1]
    rows, width = staged[2].shape
    hidden_width = staged[6].shape[1]
    shapes = [pltpu.VMEM(array.shape, array.dtype) for array in staged]
    shapes += [pltpu.VMEM((tokens, 128), jnp.float32)] * 4
    shapes += [
        pltpu.VMEM((1, tokens), jnp.int32),
        pltpu.VMEM((rows, 3 * HD), jnp.bfloat16),
        pltpu.VMEM((rows, hidden_width), jnp.bfloat16),
    ]
    count = len(staged)
    return pl.pallas_call(
        functools.partial(own_kernel, count, replica_count),
        out_shape=shapes,
        in_specs=[pl.BlockSpec(memory_space=pltpu.HBM)] * count,
        out_specs=vmem_specs(len(shapes)),
        scratch_shapes=[
            pltpu.VMEM((rows, width), jnp.bfloat16),
            pltpu.VMEM((rows, width), jnp.bfloat16),
            pltpu.SemaphoreType.DMA((count, 4)),
        ],
        compiler_params=parameters(12),
        cost_estimate=pl.CostEstimate(
            flops=2 * rows * width * (3 * HD + hidden_width),
            bytes_accessed=sum(array.nbytes for array in staged),
            transcendentals=rows * hidden_width,
        ),
        name="own_rows",
    )(*[in_hbm(array) for array in staged])


def middle_kernel(origins, *refs):
    count = len(origins)
    blocks, (gain_a, gain_f, heads_ref, upward_ref) = refs[:count], refs[count : count + 4]
    table_refs, refs = refs[count + 4 : count + 7], refs[count + 7 :]
    staged = (len(refs) - 5) // 2
    sources, (joined_ref, hidden_ref), refs = refs[:staged], refs[staged:][:2], refs[staged + 2 :]
    targets, (attention_scr, feedforward_scr, sems) = refs[:staged], refs[staged:]
    copies = copies_in(sources, targets, sems)
    block_rows = blocks[0].shape[0]
    normalize(blocks, [gain_a, gain_f], [attention_scr, feedforward_scr])
    places = [position_of(kind, half, block_rows) for kind, half in origins]
    project(attention_scr, heads_ref, table_refs, places, joined_ref, 0)
    hide(feedforward_scr, upward_ref, hidden_ref, 0)
    wait_for(sum(copies, []))


def middle_rows(name, origins, blocks, gains, weights, tables, *staged):
    block_rows, width = blocks[0].shape
    rows = len(blocks) * block_rows
    hidden_width = weights[1].shape[1]
    return pl.pallas_call(
        functools.partial(middle_kernel, origins),
        out_shape=[
            pltpu.VMEM((rows, 3 * HD), jnp.bfloat16),
            pltpu.VMEM((rows, hidden_width), jnp.bfloat16),
        ]
        + [pltpu.VMEM(array.shape, array.dtype) for array in staged],
        in_specs=vmem_specs(len(blocks) + 2 + 2 + 3)
        + [pl.BlockSpec(memory_space=pltpu.HBM)] * len(staged),
        out_specs=vmem_specs(2 + len(staged)),
        scratch_shapes=[
            pltpu.VMEM((rows, width), jnp.bfloat16),
            pltpu.VMEM((rows, width), jnp.bfloat16),
            pltpu.SemaphoreType.DMA((max(len(staged), 1), 4)),
        ],
        compiler_params=parameters(12),
        cost_estimate=pl.CostEstimate(
            flops=2 * rows * width * (3 * HD + hidden_width),
            bytes_accessed=MIB,
            transcendentals=rows * hidden_width,
        ),
        name=name,
    )(*blocks, *gains, *weights, *tables, *[in_hbm(array) for array in staged])


def last_kernel(*refs):
    blocks, (gain_a, gain_f, heads_ref, upward_ref, downward_ref, output_ref) = refs[:2], refs[2:8]
    offsets_ref, *table_refs = refs[8:12]
    pieces = refs[12:15]
    joined_ref, sibling_ref, own_ref, attention_scr, feedforward_scr, hidden_scr = refs[15:]
    block_rows = blocks[0].shape[0]
    tokens = joined_ref.shape[0]
    first = tokens - CORES * block_rows
    normalize(blocks, [gain_a, gain_f], [attention_scr, feedforward_scr])
    for kind in range(CHIPS - 1):
        for half in range(CORES):
            place = (kind * CORES + half) * block_rows
            joined_ref[place : place + block_rows, :] = piece_of(pieces, kind, half, block_rows)
    places = [position_of(CHIPS - 1, half, block_rows) for half in range(CORES)]
    project(attention_scr, heads_ref, table_refs, places, joined_ref, first)
    hide(feedforward_scr, upward_ref, hidden_scr, 0)
    attended = attend(joined_ref, offsets_ref, first, CORES * block_rows, block_rows)
    partial_sums(attended, hidden_scr[...], output_ref, downward_ref, [own_ref], [sibling_ref])


def piece_of(pieces, kind, half, block_rows):
    piece, place = (0, 2, 1)[kind], 0
    if half:
        piece, place = 2, (kind + 1) * block_rows
    return pieces[piece][place : place + block_rows, :]


def partial_sums(attended, hidden, output_ref, downward_ref, own_refs, sibling_refs):
    rows = attended.shape[0] // (2 * len(own_refs))
    chunk = 512
    for begin in range(0, downward_ref.shape[1], chunk):
        columns = slice(begin, begin + chunk)
        partial = jnp.dot(
            hidden, downward_ref[:, columns], preferred_element_type=jnp.float32
        ) + jnp.dot(attended, output_ref[:, columns], preferred_element_type=jnp.float32)
        for number, (own_ref, sibling_ref) in enumerate(zip(own_refs, sibling_refs)):
            first = 2 * number * rows
            middle = first + rows
            own_ref[:, columns] = partial[first:middle]
            sibling_ref[:, columns] = partial[middle : middle + rows].astype(jnp.bfloat16)


def last_rows(blocks, gains, weights, tables, pieces):
    block_rows, width = blocks[0].shape
    rows = len(blocks) * block_rows
    hidden_width = weights[1].shape[1]
    tokens = CHIPS * CORES * block_rows
    return pl.pallas_call(
        last_kernel,
        out_shape=[
            pltpu.VMEM((tokens, 3 * HD), jnp.bfloat16),
            pltpu.VMEM((block_rows, width), jnp.bfloat16),
            pltpu.VMEM((block_rows, width), jnp.float32),
        ],
        in_specs=vmem_specs(len(blocks) + 2 + 4 + 4 + 3),
        out_specs=vmem_specs(3),
        scratch_shapes=[
            pltpu.VMEM((rows, width), jnp.bfloat16),
            pltpu.VMEM((rows, width), jnp.bfloat16),
            pltpu.VMEM((rows, hidden_width), jnp.bfloat16),
        ],
        compiler_params=parameters(12),
        cost_estimate=pl.CostEstimate(
            flops=2 * rows * width * (3 * HD + HD + 2 * hidden_width),
            bytes_accessed=MIB,
            transcendentals=rows * hidden_width,
        ),
        name="last_rows",
    )(*blocks, *gains, *weights, *tables, *pieces)


def kind_kernel(kinds, joined_ref, offsets_ref, output_ref, downward_ref, *refs):
    pieces, refs = refs[:3], refs[3:]
    count = len(kinds)
    siblings, owns = refs[:count], refs[count : 2 * count]
    block_rows = owns[0].shape[0]
    rows = CORES * block_rows * count
    attended = attend(joined_ref, offsets_ref, kinds[0] * CORES * block_rows, rows, block_rows)
    hidden = jnp.concatenate(
        [piece_of(pieces, kind, half, block_rows) for kind in kinds for half in range(CORES)], 0
    )
    partial_sums(attended, hidden, output_ref, downward_ref, owns, siblings)


def kind_rows(name, kinds, joined, offsets, weights, pieces):
    block_rows = pieces[0].shape[0]
    output_weight, downward_weight = weights
    width = output_weight.shape[1]
    shape = (block_rows, width)
    count = len(kinds)
    tokens = joined.shape[0]
    return pl.pallas_call(
        functools.partial(kind_kernel, kinds),
        out_shape=[pltpu.VMEM(shape, jnp.bfloat16)] * count + [pltpu.VMEM(shape, jnp.float32)] * count,
        in_specs=vmem_specs(7),
        out_specs=vmem_specs(2 * count),
        compiler_params=parameters(12),
        cost_estimate=pl.CostEstimate(
            flops=4 * block_rows * count * width * (HD + downward_weight.shape[0]),
            bytes_accessed=MIB,
            transcendentals=2 * block_rows * count * tokens,
        ),
        name=name,
    )(joined, offsets, output_weight, downward_weight, *pieces)


def pages_kernel(joined_ref, destinations_ref, *page_refs):
    tokens = joined_ref.shape[0]
    slot_rows = page_refs[0].shape[0] * PAGE
    for number, page_ref in enumerate(page_refs):
        shape = (slot_rows, tokens)
        row = number * slot_rows + lax.broadcasted_iota(jnp.int32, shape, 0)
        placing = jnp.where(row == destinations_ref[...], 1.0, 0.0).astype(jnp.bfloat16)
        rows = jnp.dot(placing, joined_ref[:, HD:], preferred_element_type=jnp.float32)
        page_ref[...] = rows.astype(jnp.bfloat16).reshape(page_ref.shape)


def cached_pages(joined, destinations, replica_count):
    tokens = joined.shape[0]
    capacity = 2 * (tokens // PAGE) // replica_count
    shapes = [pltpu.VMEM((capacity, PAGE, 2 * HD), jnp.bfloat16)] * replica_count
    return pl.pallas_call(
        pages_kernel,
        out_shape=shapes,
        in_specs=vmem_specs(2),
        out_specs=vmem_specs(len(shapes)),
        compiler_params=parameters(8),
        cost_estimate=pl.CostEstimate(flops=0, bytes_accessed=MIB, transcendentals=0),
        name="cached_pages",
    )(joined, destinations)


def add_kernel(*refs):
    total = refs[0][...].astype(jnp.float32)
    for ref in refs[1:-1]:
        total = total + ref[...].astype(jnp.float32)
    refs[-1][...] = total.astype(refs[-1].dtype)


def added(name, *parts):
    return pl.pallas_call(
        add_kernel,
        out_shape=pltpu.VMEM(parts[0].shape, jnp.bfloat16),
        in_specs=vmem_specs(len(parts)),
        out_specs=pl.BlockSpec(memory_space=pltpu.VMEM),
        compiler_params=parameters(4),
        name=name,
    )(*parts)


def near_kernel(*refs):
    ones, zeros, (first_ref, base_ref) = refs[:2], refs[2:5], refs[5:]
    first = ones[0][...] + ones[1][...].astype(jnp.float32)
    first_ref[...] = first.astype(jnp.bfloat16)
    base = zeros[0][...] + zeros[1][...].astype(jnp.float32)
    base_ref[...] = zeros[2][...].astype(jnp.float32) + base


def near_sums(ones, zeros):
    shape = ones[0].shape
    return pl.pallas_call(
        near_kernel,
        out_shape=[pltpu.VMEM(shape, jnp.bfloat16), pltpu.VMEM(shape, jnp.float32)],
        in_specs=vmem_specs(5),
        out_specs=vmem_specs(2),
        compiler_params=parameters(4),
        name="near_sums",
    )(*ones, *zeros)


def place_kernel(*refs):
    group = lax.axis_index("dp")
    pages, (cache_ref, sems) = refs[:-2], refs[-2:]
    copies = [
        pltpu.make_async_copy(page_ref, cache_ref.at[0, group ^ mask], sems.at[mask])
        for mask, page_ref in enumerate(pages)
    ]
    for copy in copies:
        copy.start()
    for copy in copies:
        copy.wait()


def placed(pages):
    count = len(pages)
    return pl.pallas_call(
        place_kernel,
        out_shape=jax.ShapeDtypeStruct((1, count) + pages[0].shape, pages[0].dtype),
        in_specs=[pl.BlockSpec(memory_space=pl.ANY)] * count,
        out_specs=pl.BlockSpec(memory_space=pltpu.HBM),
        scratch_shapes=[pltpu.SemaphoreType.DMA((count,))],
        compiler_params=parameters(4),
        name="placed",
    )(*pages)


def finish_kernel(base_ref, *refs):
    total = base_ref[...]
    for part_ref in refs[:-1]:
        total = total + part_ref[...].astype(jnp.float32)
    refs[-1][...] = total


def finished(base, parts):
    return pl.pallas_call(
        finish_kernel,
        out_shape=jax.ShapeDtypeStruct(base.shape, base.dtype),
        in_specs=vmem_specs(1 + len(parts)),
        out_specs=pl.BlockSpec(memory_space=pltpu.VMEM),
        compiler_params=parameters(4),
        name="finished",
    )(base, *parts)


def shards_whole_heads(
    hidden_states,
    attention_gain,
    feedforward_gain,
    heads_weight,
    output_weight,
    upward_weight,
    downward_weight,
    segments,
    page_targets,
):
    replica_count = lax.axis_size("dp")
    to_chip = [mask * CORES for mask in range(CHIPS)]
    second = exchanged(hidden_states, "tensor", to_chip[2])
    first = exchanged(hidden_states, "tensor", to_chip[1])
    beside = exchanged(hidden_states, "tensor", 1)
    staged = (
        segments,
        page_targets.reshape(1, -1),
        hidden_states,
        attention_gain[None],
        feedforward_gain[None],
        heads_weight,
        upward_weight,
        downward_weight,
    )
    staged = own_rows(staged, replica_count)
    hidden, gains, weights, tables = staged[2], staged[3:5], staged[5:8], staged[8:12]
    heads, upward, downward = weights
    destinations, own_joined, own_hidden = staged[12:]

    second, own_joined = lax.optimization_barrier((second, own_joined))
    third = exchanged(second, "tensor", to_chip[1])
    second_beside = exchanged(second, "tensor", 1)
    first_beside = exchanged(first, "tensor", 1)
    there_joined, there_hidden = middle_rows(
        "there_rows", ((2, 0),), (second,), gains, (heads, upward), tables[1:]
    )
    third, there_joined = lax.optimization_barrier((third, there_joined))
    third_beside = exchanged(third, "tensor", 1)
    beside_joined, beside_hidden, output = middle_rows(
        "beside_rows",
        ((1, 0), (0, 1), (1, 1), (2, 1)),
        (first, beside, first_beside, second_beside),
        gains,
        (heads, upward),
        tables[1:],
        output_weight,
    )
    joined, sibling, own = last_rows(
        (third, third_beside),
        gains,
        (heads, upward, downward, output),
        tables,
        (own_joined, there_joined, beside_joined),
    )

    pieces = (own_hidden, there_hidden, beside_hidden)
    received = exchanged(sibling, "tensor", 1)
    second_sibling, second_own = kind_rows(
        "second_rows", (2,), joined, tables[0], (output, downward), pieces
    )
    third_sum = added("third_added", own, received)
    third_sum, second_sibling, joined = lax.optimization_barrier(
        (third_sum, second_sibling, joined)
    )
    passing = exchanged(third_sum, "tensor", to_chip[1])
    second_received = exchanged(second_sibling, "tensor", 1)
    zero_sibling, first_sibling, zero_own, first_own = kind_rows(
        "near_rows", (0, 1), joined, tables[0], (output, downward), pieces
    )
    first_received = exchanged(first_sibling, "tensor", 1)
    zero_received = exchanged(zero_sibling, "tensor", 1)
    pages = cached_pages(joined, destinations, replica_count)
    second_sum = added("second_added", second_own, passing, second_received)
    second_sum, first_received = lax.optimization_barrier((second_sum, first_received))
    from_second = exchanged(second_sum, "tensor", to_chip[2])
    first_sum, base = near_sums((first_own, first_received), (zero_own, zero_received, hidden))
    first_sum, pages = lax.optimization_barrier((first_sum, pages))
    from_first = exchanged(first_sum, "tensor", to_chip[1])
    arriving = [pages[0]] + [
        exchanged(pages[mask], "dp", mask) for mask in range(1, replica_count)
    ]
    from_second, from_first, arriving = lax.optimization_barrier(
        (from_second, from_first, arriving)
    )
    cache_pages = placed(arriving)
    base, cache_pages = lax.optimization_barrier((base, cache_pages))
    return (finished(base, (from_second, from_first)), cache_pages)


def solution(mesh):
    whole_heads = mesh.shape["tensor"] == H and mesh.shape["dp"] == 4
    shards = shards_whole_heads if whole_heads else shards_split_heads
    in_specs = (
        P(("dp", "tensor"), None),
        P(),
        P(),
        P(None, "tensor"),
        P("tensor", None),
        P(None, "tensor"),
        P("tensor", None),
        P("dp", None),
        P("dp", None),
    )
    out_specs = (P(("dp", "tensor"), None), P("dp", None, None, None, "tensor"))
    return jax.shard_map(shards, mesh=mesh, in_specs=in_specs, out_specs=out_specs, check_vma=False)
```

```python
import functools
import math

import jax
import jax.numpy as jnp
from jax import lax
from jax.experimental import pallas as pl
from jax.experimental.pallas import tpu as pltpu
from jax.sharding import PartitionSpec as P

H = 8
HD = 256
ROT = 64
PAGE = 16


epsilon = 1e-05
rotary_base = 10000.0
key_block = 256


def shortened(array):

    def short(part):
        return part.astype(jnp.bfloat16) if part.dtype == jnp.float32 else part

    return jax.tree.map(short, array)


def swapped(block, axis, apart):
    count = lax.axis_size(axis)
    route = []
    for low in range(count):
        high = low | 1 << apart
        if high != low and high < count:
            route += [(low, high), (high, low)]
    return lax.ppermute(block, axis, route)


def layer_norm(values, gain):
    floats = values.astype(jnp.float32)
    center = jnp.mean(floats, axis=-1, keepdims=True)
    shifted = floats - center
    spread = jnp.mean(shifted * shifted, axis=-1, keepdims=True)
    return (shifted * lax.rsqrt(spread + epsilon) * gain).astype(jnp.bfloat16)


def positions_of(stream):
    indices = jnp.arange(stream.shape[0], dtype=jnp.int32)
    boundary = jnp.concatenate([jnp.ones((1,), dtype=bool), stream[1:] != stream[:-1]])
    starting = lax.cummax(jnp.where(boundary, indices, jnp.zeros_like(indices)), axis=0)
    return (indices, starting)


def rotate_heads(vectors, offsets, rotary_dims):
    half_dims = rotary_dims // 2
    frequency = jnp.exp(
        jnp.arange(half_dims, dtype=jnp.float32) * (-2.0 * math.log(rotary_base) / rotary_dims)
    )
    angles = offsets.astype(jnp.float32)[:, None] * frequency[None, :]
    cosine = jnp.cos(angles)
    sine = jnp.sin(angles)
    floats = vectors.astype(jnp.float32)
    leading = floats[..., :half_dims]
    trailing = floats[..., half_dims:rotary_dims]
    rotated = jnp.concatenate(
        [
            leading * cosine - trailing * sine,
            trailing * cosine + leading * sine,
            floats[..., rotary_dims:],
        ],
        axis=-1,
    )
    return rotated.astype(jnp.bfloat16)


def shards_split_heads(
    hidden_states,
    attention_gain,
    feedforward_gain,
    heads_weight,
    output_weight,
    upward_weight,
    downward_weight,
    segments,
    page_targets,
):
    tensor_count = lax.axis_size("tensor")
    replica_count = lax.axis_size("dp")
    tensor_index = lax.axis_index("tensor")
    quarters = tensor_count // H
    quarter_width = HD // quarters
    quarter_index = tensor_index % quarters
    stream = segments[0]
    tokens_total = stream.shape[0]
    level_count = quarters.bit_length() - 1
    normed_attention = layer_norm(hidden_states, attention_gain)
    normed_feedforward = layer_norm(hidden_states, feedforward_gain)
    shard_rows = lax.all_gather(
        (normed_attention, normed_feedforward), "tensor", axis=0, tiled=True
    )
    joined_rows = jnp.dot(shard_rows[0], heads_weight, preferred_element_type=jnp.float32).astype(
        jnp.bfloat16
    )
    upward = jnp.dot(shard_rows[1], upward_weight, preferred_element_type=jnp.float32)
    hidden_rows = jax.nn.gelu(upward, approximate=False).astype(jnp.bfloat16)
    hidden = hidden_rows
    pieces = (
        joined_rows.reshape(tokens_total, 3, quarter_width)
        .transpose(1, 0, 2)
        .reshape(1, 3, tokens_total * quarter_width)
    )
    for bit_number in range(level_count):
        partner = swapped(shortened(pieces), "tensor", bit_number).astype(pieces.dtype)
        lower = tensor_index >> bit_number & 1 == 0
        pieces = jnp.where(
            lower, jnp.concatenate([pieces, partner], 0), jnp.concatenate([partner, pieces], 0)
        )
    whole_head = (
        pieces.reshape(quarters, 3, tokens_total, quarter_width)
        .transpose(1, 2, 0, 3)
        .reshape(3, tokens_total, HD)
    )
    indices, starting = positions_of(stream)
    offsets = indices - starting
    queries = rotate_heads(whole_head[0], offsets, ROT)
    keys = rotate_heads(whole_head[1], offsets, ROT)
    values = whole_head[2]
    block_rows = tokens_total // (2 * quarters)
    score_scale = HD ** (-0.5)

    def attend_block(block_number):
        first_row = block_number * block_rows
        block_queries = lax.dynamic_slice_in_dim(queries, first_row, block_rows, 0)
        query_segments = lax.dynamic_slice_in_dim(stream, first_row, block_rows, 0)
        query_indices = first_row + jnp.arange(block_rows, dtype=jnp.int32)
        lowest = lax.dynamic_index_in_dim(starting, first_row, 0, keepdims=False) // key_block
        highest = (first_row + block_rows + key_block - 1) // key_block

        def scores_of(key_number):
            key_first = key_number * key_block
            key_indices = key_first + jnp.arange(key_block, dtype=jnp.int32)
            scores = (
                jnp.dot(block_queries, keys.T, preferred_element_type=jnp.float32) * score_scale
            )
            allowed = (stream[None, :] == query_segments[:, None]) & (
                key_indices[None, :] <= query_indices[:, None]
            )
            return (scores, allowed)

        def find_peak(key_number, peak):
            scores, allowed = scores_of(key_number)
            return jnp.maximum(peak, jnp.max(jnp.where(allowed, scores, -jnp.inf), axis=1))

        peak = lax.fori_loop(
            lowest, highest, find_peak, jnp.full((block_rows,), -jnp.inf, jnp.float32)
        )

        def accumulate(key_number, state):
            weight_sum, mixed_sum = state
            scores, allowed = scores_of(key_number)
            weights = jnp.where(allowed, jnp.exp(scores - peak[:, None]), 0.0)
            mixed_next = mixed_sum + jnp.dot(
                weights.astype(jnp.bfloat16), values, preferred_element_type=jnp.float32
            )
            return (weight_sum + jnp.sum(weights, axis=1), mixed_next)

        start_state = (
            jnp.zeros((block_rows,), jnp.float32),
            jnp.zeros((block_rows, HD), jnp.float32),
        )
        weight_sum, mixed_sum = lax.fori_loop(lowest, highest, accumulate, start_state)
        return (mixed_sum / weight_sum[:, None]).astype(jnp.bfloat16)

    own_blocks = (2 * quarter_index, 2 * quarter_index + 1)
    own_rows = jnp.concatenate([attend_block(own_blocks[0]), attend_block(own_blocks[1])], 0)[None]
    for bit_number in range(level_count):
        partner = swapped(own_rows, "tensor", bit_number)
        lower = tensor_index >> bit_number & 1 == 0
        own_rows = jnp.where(
            lower, jnp.concatenate([own_rows, partner], 0), jnp.concatenate([partner, own_rows], 0)
        )
    attended = own_rows.reshape(tokens_total, HD)
    attended_quarter = lax.dynamic_slice_in_dim(
        attended, quarter_index * quarter_width, quarter_width, 1
    )
    hidden_rows = hidden
    summed = lax.psum_scatter(
        (
            jnp.dot(attended_quarter, output_weight, preferred_element_type=jnp.float32)
            + jnp.dot(hidden_rows, downward_weight, preferred_element_type=jnp.float32)
        ).astype(jnp.bfloat16),
        "tensor",
        scatter_dimension=0,
        tiled=True,
    ).astype(jnp.float32)
    layer_output = hidden_states.astype(jnp.float32) + summed
    key_quarter = lax.dynamic_slice_in_dim(keys, quarter_index * quarter_width, quarter_width, 1)
    value_quarter = joined_rows[:, 2 * quarter_width :]
    page_count = tokens_total // PAGE
    page_rows = jnp.concatenate([key_quarter, value_quarter], 1).reshape(
        page_count, PAGE * 2 * quarter_width
    )
    targets = page_targets[:, 0]
    page_numbers = jnp.arange(page_count, dtype=jnp.int32)
    earlier = jnp.sum(
        (
            (targets[None, :] == targets[:, None]) & (page_numbers[None, :] < page_numbers[:, None])
        ).astype(jnp.int32),
        axis=1,
    )
    capacity = 2 * page_count // replica_count
    slot_numbers = targets * capacity + earlier
    placing = (
        jnp.arange(replica_count * capacity, dtype=jnp.int32)[:, None] == slot_numbers[None, :]
    ).astype(jnp.bfloat16)
    outgoing = jnp.dot(placing, page_rows, preferred_element_type=jnp.float32).astype(jnp.bfloat16)
    outgoing = outgoing.reshape(replica_count, capacity, PAGE * 2 * quarter_width)
    incoming = lax.all_to_all(outgoing, "dp", split_axis=0, concat_axis=0, tiled=True)
    cache_pages = incoming.reshape(1, replica_count, capacity, PAGE, 2 * quarter_width)
    return (layer_output, cache_pages)


CORES = 2
CHIPS = 4
MIB = 1 << 20


def in_hbm(array):
    return pltpu.with_memory_space_constraint(array, pltpu.HBM)


def exchanged(block, axis, mask):
    count = lax.axis_size(axis)
    return lax.ppermute(block, axis, [(member, member ^ mask) for member in range(count)])


def vmem_specs(count):
    return [pl.BlockSpec(memory_space=pltpu.VMEM)] * count


def parameters(mebibytes):
    return pltpu.CompilerParams(vmem_limit_bytes=mebibytes * MIB)


def whereabouts():
    member = lax.axis_index("tensor")
    return member // CORES, member % CORES


def position_of(kind, half, block_rows):
    chip, core = whereabouts()
    return ((chip ^ kind) * CORES + (core ^ half)) * block_rows


def positions_along(first, shape, axis, block_rows):
    chip, core = whereabouts()
    bits = block_rows.bit_length() - 1
    place = first + lax.broadcasted_iota(jnp.int32, shape, axis)
    kind = place >> (bits + 1)
    half = (place >> bits) & 1
    return ((((chip ^ kind) << 1) | (core ^ half)) << bits) | (place & (block_rows - 1))


def normalize(blocks, gain_refs, normed_refs):
    piece = 16
    gains = [gain_ref[...] for gain_ref in gain_refs]
    for number, block_ref in enumerate(blocks):
        block_rows = block_ref.shape[0]
        for part in range(0, block_rows, piece):
            floats = block_ref[part : part + piece, :].astype(jnp.float32)
            center = jnp.mean(floats, axis=-1, keepdims=True)
            shifted = floats - center
            spread = jnp.mean(shifted * shifted, axis=-1, keepdims=True)
            scaled = shifted * lax.rsqrt(spread + epsilon)
            first = number * block_rows + part
            for gain, normed_ref in zip(gains, normed_refs):
                normed_ref[first : first + piece, :] = (scaled * gain).astype(jnp.bfloat16)


def project(normed_ref, heads_ref, table_refs, places, joined_ref, first):
    rows = normed_ref.shape[0]
    block_rows = rows // len(places)
    for component in range(3):
        columns = slice(component * HD, (component + 1) * HD)
        joined = jnp.dot(
            normed_ref[...], heads_ref[:, columns], preferred_element_type=jnp.float32
        ).astype(jnp.bfloat16)
        joined_ref[first : first + rows, columns] = joined
        if component < 2:
            cosine, sine_down, sine_up = [
                jnp.concatenate(
                    [
                        table_ref[pl.ds(pl.multiple_of(place, block_rows), block_rows), :]
                        for place in places
                    ],
                    0,
                )
                for table_ref in table_refs
            ]
            turning = joined[:, :128].astype(jnp.float32)
            turned = (
                turning * cosine
                + pltpu.roll(turning, 128 - ROT // 2, 1) * sine_down
                + pltpu.roll(turning, ROT // 2, 1) * sine_up
            )
            joined_ref[first : first + rows, component * HD : component * HD + 128] = turned.astype(
                jnp.bfloat16
            )


def hide(normed_ref, upward_ref, hidden_ref, place):
    chunk = 256
    rows = slice(place, place + normed_ref.shape[0])
    for first in range(0, upward_ref.shape[1], chunk):
        columns = slice(first, first + chunk)
        upward = jnp.dot(
            normed_ref[...], upward_ref[:, columns], preferred_element_type=jnp.float32
        )
        hidden = 0.5 * upward * (1.0 + lax.erf(upward * (0.5**0.5)))
        hidden_ref[rows, columns] = hidden.astype(jnp.bfloat16)


def attend(joined_ref, offsets_ref, first, rows, block_rows):
    tokens = joined_ref.shape[0]
    starts = [
        position_of(place // (2 * block_rows), (place // block_rows) % 2, block_rows)
        for place in range(first, first + rows, block_rows)
    ]
    reach = jnp.concatenate(
        [
            offsets_ref[pl.ds(pl.multiple_of(start, block_rows), block_rows), :]
            for start in starts
        ],
        0,
    )[:, :1].astype(jnp.int32)
    row = positions_along(first, (rows, 1), 0, block_rows)
    column = positions_along(0, (1, tokens), 1, block_rows)
    allowed = (column <= row) & (column >= row - reach)
    scores = lax.dot_general(
        joined_ref[first : first + rows, :HD],
        joined_ref[:, HD : 2 * HD],
        (((1,), (1,)), ((), ())),
        preferred_element_type=jnp.float32,
    ) * (HD ** (-0.5))
    peak = jnp.max(jnp.where(allowed, scores, -jnp.inf), axis=1, keepdims=True)
    weights = jnp.where(allowed, jnp.exp(scores - peak), 0.0)
    weight_sum = jnp.sum(weights, axis=1, keepdims=True)
    mixed = jnp.dot(
        weights.astype(jnp.bfloat16), joined_ref[:, 2 * HD :], preferred_element_type=jnp.float32
    )
    return (mixed / weight_sum).astype(jnp.bfloat16)


def make_tables(segments_ref, offsets_ref, cosine_ref, sine_down_ref, sine_up_ref):
    tokens = segments_ref.shape[1]
    shape = (tokens, tokens)
    rows = lax.broadcasted_iota(jnp.int32, shape, 0)
    columns = lax.broadcasted_iota(jnp.int32, shape, 1)
    across = jnp.broadcast_to(segments_ref[...], shape).astype(jnp.float32)
    down = jnp.sum(jnp.where(rows == columns, across, 0.0), axis=1, keepdims=True)
    earlier = (across == down) & (columns < rows)
    offsets = jnp.sum(jnp.where(earlier, 1.0, 0.0), axis=1, keepdims=True)
    offsets_ref[...] = jnp.broadcast_to(offsets, offsets_ref.shape)
    half = ROT // 2
    lane = lax.broadcasted_iota(jnp.int32, (tokens, 128), 1)
    step = (lane & (half - 1)).astype(jnp.float32)
    frequency = jnp.exp(step * (-2.0 * math.log(rotary_base) / ROT))
    angles = offsets * frequency
    sine = jnp.sin(angles)
    cosine_ref[...] = jnp.where(lane < ROT, jnp.cos(angles), 1.0)
    sine_down_ref[...] = jnp.where(lane < half, -sine, 0.0)
    sine_up_ref[...] = jnp.where((lane >= half) & (lane < ROT), sine, 0.0)


def make_destinations(targets_ref, destinations_ref, replica_count, block_rows):
    page_count = targets_ref.shape[1]
    tokens = destinations_ref.shape[1]
    capacity = 2 * page_count // replica_count
    square = (page_count, page_count)
    rows = lax.broadcasted_iota(jnp.int32, square, 0)
    columns = lax.broadcasted_iota(jnp.int32, square, 1)
    across = jnp.broadcast_to(targets_ref[...], square).astype(jnp.float32)
    down = jnp.sum(jnp.where(rows == columns, across, 0.0), axis=1, keepdims=True)
    earlier = jnp.where((across == down) & (columns < rows), 1.0, 0.0)
    slots = jnp.sum(earlier, axis=1, keepdims=True).astype(jnp.int32)
    slots = (down.astype(jnp.int32) ^ lax.axis_index("dp")) * capacity + slots
    positions = positions_along(0, (1, tokens), 1, block_rows)
    bits = PAGE.bit_length() - 1
    pages = lax.broadcasted_iota(jnp.int32, (page_count, tokens), 0)
    chosen = jnp.where(pages == positions >> bits, slots.astype(jnp.float32), 0.0)
    slot = jnp.sum(chosen, axis=0, keepdims=True).astype(jnp.int32)
    destinations_ref[...] = slot * PAGE + (positions & (PAGE - 1))


def copies_in(sources, targets, sems):
    copies = []
    for number, (source, target) in enumerate(zip(sources, targets)):
        parts = 4 if source.shape[0] >= 256 else 1
        rows = source.shape[0] // parts
        places = [pl.ds(part * rows, rows) for part in range(parts)]
        copies.append(
            [
                pltpu.make_async_copy(source.at[place], target.at[place], sems.at[number, part])
                for part, place in enumerate(places)
            ]
        )
    for copy in sum(copies, []):
        copy.start()
    return copies


def wait_for(copies):
    for copy in copies:
        copy.wait()


def own_kernel(count, replica_count, *refs):
    sources, targets = refs[:count], refs[count : 2 * count]
    offsets_ref, *table_refs, destinations_ref, joined_ref, hidden_ref = refs[2 * count : -3]
    attention_scr, feedforward_scr, sems = refs[-3:]
    copies = copies_in(sources, targets, sems)
    segments_ref, targets_ref, states_ref, *gain_refs, heads_ref, upward_ref, _ = targets
    block_rows = states_ref.shape[0]
    wait_for(copies[0])
    make_tables(segments_ref, offsets_ref, *table_refs)
    wait_for(copies[1])
    make_destinations(targets_ref, destinations_ref, replica_count, block_rows)
    for number in (2, 3, 4):
        wait_for(copies[number])
    normalize([states_ref], gain_refs, [attention_scr, feedforward_scr])
    wait_for(copies[5])
    places = [position_of(0, 0, block_rows)]
    project(attention_scr, heads_ref, table_refs, places, joined_ref, 0)
    wait_for(copies[6])
    hide(feedforward_scr, upward_ref, hidden_ref, 0)
    wait_for(copies[7])


def own_rows(staged, replica_count):
    tokens = staged[0].shape[1]
    rows, width = staged[2].shape
    hidden_width = staged[6].shape[1]
    shapes = [pltpu.VMEM(array.shape, array.dtype) for array in staged]
    shapes += [pltpu.VMEM((tokens, 128), jnp.float32)] * 4
    shapes += [
        pltpu.VMEM((1, tokens), jnp.int32),
        pltpu.VMEM((rows, 3 * HD), jnp.bfloat16),
        pltpu.VMEM((rows, hidden_width), jnp.bfloat16),
    ]
    count = len(staged)
    return pl.pallas_call(
        functools.partial(own_kernel, count, replica_count),
        out_shape=shapes,
        in_specs=[pl.BlockSpec(memory_space=pltpu.HBM)] * count,
        out_specs=vmem_specs(len(shapes)),
        scratch_shapes=[
            pltpu.VMEM((rows, width), jnp.bfloat16),
            pltpu.VMEM((rows, width), jnp.bfloat16),
            pltpu.SemaphoreType.DMA((count, 4)),
        ],
        compiler_params=parameters(12),
        cost_estimate=pl.CostEstimate(
            flops=2 * rows * width * (3 * HD + hidden_width),
            bytes_accessed=sum(array.nbytes for array in staged),
            transcendentals=rows * hidden_width,
        ),
        name="own_rows",
    )(*[in_hbm(array) for array in staged])


def middle_kernel(origins, *refs):
    count = len(origins)
    blocks, (gain_a, gain_f, heads_ref, upward_ref) = refs[:count], refs[count : count + 4]
    table_refs, refs = refs[count + 4 : count + 7], refs[count + 7 :]
    staged = (len(refs) - 5) // 2
    sources, (joined_ref, hidden_ref), refs = refs[:staged], refs[staged:][:2], refs[staged + 2 :]
    targets, (attention_scr, feedforward_scr, sems) = refs[:staged], refs[staged:]
    copies = copies_in(sources, targets, sems)
    block_rows = blocks[0].shape[0]
    normalize(blocks, [gain_a, gain_f], [attention_scr, feedforward_scr])
    places = [position_of(kind, half, block_rows) for kind, half in origins]
    project(attention_scr, heads_ref, table_refs, places, joined_ref, 0)
    hide(feedforward_scr, upward_ref, hidden_ref, 0)
    wait_for(sum(copies, []))


def middle_rows(name, origins, blocks, gains, weights, tables, *staged):
    block_rows, width = blocks[0].shape
    rows = len(blocks) * block_rows
    hidden_width = weights[1].shape[1]
    return pl.pallas_call(
        functools.partial(middle_kernel, origins),
        out_shape=[
            pltpu.VMEM((rows, 3 * HD), jnp.bfloat16),
            pltpu.VMEM((rows, hidden_width), jnp.bfloat16),
        ]
        + [pltpu.VMEM(array.shape, array.dtype) for array in staged],
        in_specs=vmem_specs(len(blocks) + 2 + 2 + 3)
        + [pl.BlockSpec(memory_space=pltpu.HBM)] * len(staged),
        out_specs=vmem_specs(2 + len(staged)),
        scratch_shapes=[
            pltpu.VMEM((rows, width), jnp.bfloat16),
            pltpu.VMEM((rows, width), jnp.bfloat16),
            pltpu.SemaphoreType.DMA((max(len(staged), 1), 4)),
        ],
        compiler_params=parameters(12),
        cost_estimate=pl.CostEstimate(
            flops=2 * rows * width * (3 * HD + hidden_width),
            bytes_accessed=MIB,
            transcendentals=rows * hidden_width,
        ),
        name=name,
    )(*blocks, *gains, *weights, *tables, *[in_hbm(array) for array in staged])


def last_kernel(*refs):
    blocks, (gain_a, gain_f, heads_ref, upward_ref, downward_ref, output_ref) = refs[:2], refs[2:8]
    offsets_ref, *table_refs = refs[8:12]
    pieces = refs[12:15]
    joined_ref, sibling_ref, own_ref, attention_scr, feedforward_scr, hidden_scr = refs[15:]
    block_rows = blocks[0].shape[0]
    tokens = joined_ref.shape[0]
    first = tokens - CORES * block_rows
    normalize(blocks, [gain_a, gain_f], [attention_scr, feedforward_scr])
    for kind in range(CHIPS - 1):
        for half in range(CORES):
            place = (kind * CORES + half) * block_rows
            joined_ref[place : place + block_rows, :] = piece_of(pieces, kind, half, block_rows)
    places = [position_of(CHIPS - 1, half, block_rows) for half in range(CORES)]
    project(attention_scr, heads_ref, table_refs, places, joined_ref, first)
    hide(feedforward_scr, upward_ref, hidden_scr, 0)
    attended = attend(joined_ref, offsets_ref, first, CORES * block_rows, block_rows)
    partial_sums(attended, hidden_scr[...], output_ref, downward_ref, [own_ref], [sibling_ref])


def piece_of(pieces, kind, half, block_rows):
    piece, place = (0, 2, 1)[kind], 0
    if half:
        piece, place = 2, (kind + 1) * block_rows
    return pieces[piece][place : place + block_rows, :]


def partial_sums(attended, hidden, output_ref, downward_ref, own_refs, sibling_refs):
    rows = attended.shape[0] // (2 * len(own_refs))
    chunk = 512
    for begin in range(0, downward_ref.shape[1], chunk):
        columns = slice(begin, begin + chunk)
        partial = jnp.dot(
            hidden, downward_ref[:, columns], preferred_element_type=jnp.float32
        ) + jnp.dot(attended, output_ref[:, columns], preferred_element_type=jnp.float32)
        for number, (own_ref, sibling_ref) in enumerate(zip(own_refs, sibling_refs)):
            first = 2 * number * rows
            middle = first + rows
            own_ref[:, columns] = partial[first:middle]
            sibling_ref[:, columns] = partial[middle : middle + rows].astype(jnp.bfloat16)


def last_rows(blocks, gains, weights, tables, pieces):
    block_rows, width = blocks[0].shape
    rows = len(blocks) * block_rows
    hidden_width = weights[1].shape[1]
    tokens = CHIPS * CORES * block_rows
    return pl.pallas_call(
        last_kernel,
        out_shape=[
            pltpu.VMEM((tokens, 3 * HD), jnp.bfloat16),
            pltpu.VMEM((block_rows, width), jnp.bfloat16),
            pltpu.VMEM((block_rows, width), jnp.float32),
        ],
        in_specs=vmem_specs(len(blocks) + 2 + 4 + 4 + 3),
        out_specs=vmem_specs(3),
        scratch_shapes=[
            pltpu.VMEM((rows, width), jnp.bfloat16),
            pltpu.VMEM((rows, width), jnp.bfloat16),
            pltpu.VMEM((rows, hidden_width), jnp.bfloat16),
        ],
        compiler_params=parameters(12),
        cost_estimate=pl.CostEstimate(
            flops=2 * rows * width * (3 * HD + HD + 2 * hidden_width),
            bytes_accessed=MIB,
            transcendentals=rows * hidden_width,
        ),
        name="last_rows",
    )(*blocks, *gains, *weights, *tables, *pieces)


def kind_kernel(kinds, joined_ref, offsets_ref, output_ref, downward_ref, *refs):
    pieces, refs = refs[:3], refs[3:]
    count = len(kinds)
    siblings, owns = refs[:count], refs[count : 2 * count]
    block_rows = owns[0].shape[0]
    rows = CORES * block_rows * count
    attended = attend(joined_ref, offsets_ref, kinds[0] * CORES * block_rows, rows, block_rows)
    hidden = jnp.concatenate(
        [piece_of(pieces, kind, half, block_rows) for kind in kinds for half in range(CORES)], 0
    )
    partial_sums(attended, hidden, output_ref, downward_ref, owns, siblings)


def kind_rows(name, kinds, joined, offsets, weights, pieces):
    block_rows = pieces[0].shape[0]
    output_weight, downward_weight = weights
    width = output_weight.shape[1]
    shape = (block_rows, width)
    count = len(kinds)
    tokens = joined.shape[0]
    return pl.pallas_call(
        functools.partial(kind_kernel, kinds),
        out_shape=[pltpu.VMEM(shape, jnp.bfloat16)] * count + [pltpu.VMEM(shape, jnp.float32)] * count,
        in_specs=vmem_specs(7),
        out_specs=vmem_specs(2 * count),
        compiler_params=parameters(12),
        cost_estimate=pl.CostEstimate(
            flops=4 * block_rows * count * width * (HD + downward_weight.shape[0]),
            bytes_accessed=MIB,
            transcendentals=2 * block_rows * count * tokens,
        ),
        name=name,
    )(joined, offsets, output_weight, downward_weight, *pieces)


def pages_kernel(joined_ref, destinations_ref, *page_refs):
    tokens = joined_ref.shape[0]
    slot_rows = page_refs[0].shape[0] * PAGE
    for number, page_ref in enumerate(page_refs):
        shape = (slot_rows, tokens)
        row = number * slot_rows + lax.broadcasted_iota(jnp.int32, shape, 0)
        placing = jnp.where(row == destinations_ref[...], 1.0, 0.0).astype(jnp.bfloat16)
        rows = jnp.dot(placing, joined_ref[:, HD:], preferred_element_type=jnp.float32)
        page_ref[...] = rows.astype(jnp.bfloat16).reshape(page_ref.shape)


def cached_pages(joined, destinations, replica_count):
    tokens = joined.shape[0]
    capacity = 2 * (tokens // PAGE) // replica_count
    shapes = [pltpu.VMEM((capacity, PAGE, 2 * HD), jnp.bfloat16)] * replica_count
    return pl.pallas_call(
        pages_kernel,
        out_shape=shapes,
        in_specs=vmem_specs(2),
        out_specs=vmem_specs(len(shapes)),
        compiler_params=parameters(8),
        cost_estimate=pl.CostEstimate(flops=0, bytes_accessed=MIB, transcendentals=0),
        name="cached_pages",
    )(joined, destinations)


def add_kernel(*refs):
    total = refs[0][...].astype(jnp.float32)
    for ref in refs[1:-1]:
        total = total + ref[...].astype(jnp.float32)
    refs[-1][...] = total.astype(refs[-1].dtype)


def added(name, *parts):
    return pl.pallas_call(
        add_kernel,
        out_shape=pltpu.VMEM(parts[0].shape, jnp.bfloat16),
        in_specs=vmem_specs(len(parts)),
        out_specs=pl.BlockSpec(memory_space=pltpu.VMEM),
        compiler_params=parameters(4),
        name=name,
    )(*parts)


def sums_kernel(passing_ref, *refs):
    zeros, ones, twos = refs[0:2], refs[2:4], refs[4:6]
    hidden_ref, second_ref, first_ref, base_ref = refs[6:]

    def total(pair, extra=None):
        received_ref, own_ref = pair
        value = own_ref[...] + received_ref[...].astype(jnp.float32)
        return value if extra is None else value + extra[...].astype(jnp.float32)

    second_ref[...] = total(twos, passing_ref).astype(jnp.bfloat16)
    first_ref[...] = total(ones).astype(jnp.bfloat16)
    base_ref[...] = total(zeros, hidden_ref)


def remaining_sums(passing, pairs, hidden):
    shape = hidden.shape
    return pl.pallas_call(
        sums_kernel,
        out_shape=[
            pltpu.VMEM(shape, jnp.bfloat16),
            pltpu.VMEM(shape, jnp.bfloat16),
            pltpu.VMEM(shape, jnp.float32),
        ],
        in_specs=vmem_specs(8),
        out_specs=vmem_specs(3),
        compiler_params=parameters(4),
        name="remaining_sums",
    )(passing, *[array for pair in pairs for array in pair], hidden)


def place_kernel(masks, *refs):
    group = lax.axis_index("dp")
    pages, (cache_ref, sems) = refs[:-2], refs[-2:]
    copies = [
        pltpu.make_async_copy(page_ref, cache_ref.at[0, group ^ mask], sems.at[number])
        for number, (mask, page_ref) in enumerate(zip(masks, pages))
    ]
    for copy in copies:
        copy.start()
    for copy in copies:
        copy.wait()


def placed(masks, pages, replica_count):
    count = len(pages)
    return pl.pallas_call(
        functools.partial(place_kernel, masks),
        out_shape=jax.ShapeDtypeStruct((1, replica_count) + pages[0].shape, pages[0].dtype),
        in_specs=[pl.BlockSpec(memory_space=pl.ANY)] * count,
        out_specs=pl.BlockSpec(memory_space=pltpu.HBM),
        scratch_shapes=[pltpu.SemaphoreType.DMA((count,))],
        compiler_params=parameters(4),
        name="placed",
    )(*pages)


def finish_kernel(mask, base_ref, *refs):
    *parts, page_ref, _, output_ref, cache_ref, sem = refs
    target = cache_ref.at[0, lax.axis_index("dp") ^ mask]
    copy = pltpu.make_async_copy(page_ref, target, sem)
    copy.start()
    total = base_ref[...]
    for part_ref in parts:
        total = total + part_ref[...].astype(jnp.float32)
    output_ref[...] = total
    copy.wait()


def finished(base, parts, mask, page, cache):
    count = len(parts)
    return pl.pallas_call(
        functools.partial(finish_kernel, mask),
        out_shape=[
            jax.ShapeDtypeStruct(base.shape, base.dtype),
            jax.ShapeDtypeStruct(cache.shape, cache.dtype),
        ],
        in_specs=vmem_specs(1 + count)
        + [pl.BlockSpec(memory_space=pl.ANY), pl.BlockSpec(memory_space=pltpu.HBM)],
        out_specs=vmem_specs(1) + [pl.BlockSpec(memory_space=pltpu.HBM)],
        scratch_shapes=[pltpu.SemaphoreType.DMA(())],
        input_output_aliases={count + 2: 1},
        compiler_params=parameters(4),
        name="finished",
    )(base, *parts, page, cache)


def shards_whole_heads(
    hidden_states,
    attention_gain,
    feedforward_gain,
    heads_weight,
    output_weight,
    upward_weight,
    downward_weight,
    segments,
    page_targets,
):
    replica_count = lax.axis_size("dp")
    to_chip = [mask * CORES for mask in range(CHIPS)]
    second = exchanged(hidden_states, "tensor", to_chip[2])
    first = exchanged(hidden_states, "tensor", to_chip[1])
    beside = exchanged(hidden_states, "tensor", 1)
    staged = (
        segments,
        page_targets.reshape(1, -1),
        hidden_states,
        attention_gain[None],
        feedforward_gain[None],
        heads_weight,
        upward_weight,
        downward_weight,
    )
    staged = own_rows(staged, replica_count)
    hidden, gains, weights, tables = staged[2], staged[3:5], staged[5:8], staged[8:12]
    heads, upward, downward = weights
    destinations, own_joined, own_hidden = staged[12:]

    second, own_joined = lax.optimization_barrier((second, own_joined))
    third = exchanged(second, "tensor", to_chip[1])
    second_beside = exchanged(second, "tensor", 1)
    first_beside = exchanged(first, "tensor", 1)
    there_joined, there_hidden = middle_rows(
        "there_rows", ((2, 0),), (second,), gains, (heads, upward), tables[1:]
    )
    third, there_joined = lax.optimization_barrier((third, there_joined))
    third_beside = exchanged(third, "tensor", 1)
    beside_joined, beside_hidden, output = middle_rows(
        "beside_rows",
        ((1, 0), (0, 1), (1, 1), (2, 1)),
        (first, beside, first_beside, second_beside),
        gains,
        (heads, upward),
        tables[1:],
        output_weight,
    )
    joined, sibling, own = last_rows(
        (third, third_beside),
        gains,
        (heads, upward, downward, output),
        tables,
        (own_joined, there_joined, beside_joined),
    )

    pieces = (own_hidden, there_hidden, beside_hidden)
    received = exchanged(sibling, "tensor", 1)
    partials = kind_rows("rest_rows", (0, 1, 2), joined, tables[0], (output, downward), pieces)
    siblings, owns = partials[: CHIPS - 1], partials[CHIPS - 1 :]
    third_sum = added("third_added", own, received)
    third_sum, siblings, joined = lax.optimization_barrier((third_sum, siblings, joined))
    passing = exchanged(third_sum, "tensor", to_chip[1])
    pairs = [(exchanged(sibling, "tensor", 1), own) for sibling, own in zip(siblings, owns)]
    pages = cached_pages(joined, destinations, replica_count)
    early, late = (3, 1), 2
    arriving = [exchanged(pages[mask], "dp", mask) for mask in early]
    second_sum, first_sum, base = remaining_sums(passing, pairs, hidden)
    from_second = exchanged(second_sum, "tensor", to_chip[2])
    from_first = exchanged(first_sum, "tensor", to_chip[1])
    base, late_page = lax.optimization_barrier((base, pages[late]))
    late_page = exchanged(late_page, "dp", late)
    cache_pages = placed((0,) + early, [pages[0]] + arriving, replica_count)
    return tuple(finished(base, (from_second, from_first), late, late_page, cache_pages))


def solution(mesh):
    whole_heads = mesh.shape["tensor"] == H and mesh.shape["dp"] == 4
    shards = shards_whole_heads if whole_heads else shards_split_heads
    in_specs = (
        P(("dp", "tensor"), None),
        P(),
        P(),
        P(None, "tensor"),
        P("tensor", None),
        P(None, "tensor"),
        P("tensor", None),
        P("dp", None),
        P("dp", None),
    )
    out_specs = (P(("dp", "tensor"), None), P("dp", None, None, None, "tensor"))
    return jax.shard_map(shards, mesh=mesh, in_specs=in_specs, out_specs=out_specs, check_vma=False)
```

```python
import functools
import math

import jax
import jax.numpy as jnp
from jax import lax
from jax.experimental import pallas as pl
from jax.experimental.pallas import tpu as pltpu
from jax.sharding import PartitionSpec as P

H = 8
HD = 256
ROT = 64
PAGE = 16


epsilon = 1e-05
rotary_base = 10000.0
key_block = 256


def shortened(array):

    def short(part):
        return part.astype(jnp.bfloat16) if part.dtype == jnp.float32 else part

    return jax.tree.map(short, array)


def swapped(block, axis, apart):
    count = lax.axis_size(axis)
    route = []
    for low in range(count):
        high = low | 1 << apart
        if high != low and high < count:
            route += [(low, high), (high, low)]
    return lax.ppermute(block, axis, route)


def layer_norm(values, gain):
    floats = values.astype(jnp.float32)
    center = jnp.mean(floats, axis=-1, keepdims=True)
    shifted = floats - center
    spread = jnp.mean(shifted * shifted, axis=-1, keepdims=True)
    return (shifted * lax.rsqrt(spread + epsilon) * gain).astype(jnp.bfloat16)


def positions_of(stream):
    indices = jnp.arange(stream.shape[0], dtype=jnp.int32)
    boundary = jnp.concatenate([jnp.ones((1,), dtype=bool), stream[1:] != stream[:-1]])
    starting = lax.cummax(jnp.where(boundary, indices, jnp.zeros_like(indices)), axis=0)
    return (indices, starting)


def rotate_heads(vectors, offsets, rotary_dims):
    half_dims = rotary_dims // 2
    frequency = jnp.exp(
        jnp.arange(half_dims, dtype=jnp.float32) * (-2.0 * math.log(rotary_base) / rotary_dims)
    )
    angles = offsets.astype(jnp.float32)[:, None] * frequency[None, :]
    cosine = jnp.cos(angles)
    sine = jnp.sin(angles)
    floats = vectors.astype(jnp.float32)
    leading = floats[..., :half_dims]
    trailing = floats[..., half_dims:rotary_dims]
    rotated = jnp.concatenate(
        [
            leading * cosine - trailing * sine,
            trailing * cosine + leading * sine,
            floats[..., rotary_dims:],
        ],
        axis=-1,
    )
    return rotated.astype(jnp.bfloat16)


def shards_split_heads(
    hidden_states,
    attention_gain,
    feedforward_gain,
    heads_weight,
    output_weight,
    upward_weight,
    downward_weight,
    segments,
    page_targets,
):
    tensor_count = lax.axis_size("tensor")
    replica_count = lax.axis_size("dp")
    tensor_index = lax.axis_index("tensor")
    quarters = tensor_count // H
    quarter_width = HD // quarters
    quarter_index = tensor_index % quarters
    stream = segments[0]
    tokens_total = stream.shape[0]
    level_count = quarters.bit_length() - 1
    normed_attention = layer_norm(hidden_states, attention_gain)
    normed_feedforward = layer_norm(hidden_states, feedforward_gain)
    shard_rows = lax.all_gather(
        (normed_attention, normed_feedforward), "tensor", axis=0, tiled=True
    )
    joined_rows = jnp.dot(shard_rows[0], heads_weight, preferred_element_type=jnp.float32).astype(
        jnp.bfloat16
    )
    upward = jnp.dot(shard_rows[1], upward_weight, preferred_element_type=jnp.float32)
    hidden_rows = jax.nn.gelu(upward, approximate=False).astype(jnp.bfloat16)
    hidden = hidden_rows
    pieces = (
        joined_rows.reshape(tokens_total, 3, quarter_width)
        .transpose(1, 0, 2)
        .reshape(1, 3, tokens_total * quarter_width)
    )
    for bit_number in range(level_count):
        partner = swapped(shortened(pieces), "tensor", bit_number).astype(pieces.dtype)
        lower = tensor_index >> bit_number & 1 == 0
        pieces = jnp.where(
            lower, jnp.concatenate([pieces, partner], 0), jnp.concatenate([partner, pieces], 0)
        )
    whole_head = (
        pieces.reshape(quarters, 3, tokens_total, quarter_width)
        .transpose(1, 2, 0, 3)
        .reshape(3, tokens_total, HD)
    )
    indices, starting = positions_of(stream)
    offsets = indices - starting
    queries = rotate_heads(whole_head[0], offsets, ROT)
    keys = rotate_heads(whole_head[1], offsets, ROT)
    values = whole_head[2]
    block_rows = tokens_total // (2 * quarters)
    score_scale = HD ** (-0.5)

    def attend_block(block_number):
        first_row = block_number * block_rows
        block_queries = lax.dynamic_slice_in_dim(queries, first_row, block_rows, 0)
        query_segments = lax.dynamic_slice_in_dim(stream, first_row, block_rows, 0)
        query_indices = first_row + jnp.arange(block_rows, dtype=jnp.int32)
        lowest = lax.dynamic_index_in_dim(starting, first_row, 0, keepdims=False) // key_block
        highest = (first_row + block_rows + key_block - 1) // key_block

        def scores_of(key_number):
            key_first = key_number * key_block
            key_indices = key_first + jnp.arange(key_block, dtype=jnp.int32)
            scores = (
                jnp.dot(block_queries, keys.T, preferred_element_type=jnp.float32) * score_scale
            )
            allowed = (stream[None, :] == query_segments[:, None]) & (
                key_indices[None, :] <= query_indices[:, None]
            )
            return (scores, allowed)

        def find_peak(key_number, peak):
            scores, allowed = scores_of(key_number)
            return jnp.maximum(peak, jnp.max(jnp.where(allowed, scores, -jnp.inf), axis=1))

        peak = lax.fori_loop(
            lowest, highest, find_peak, jnp.full((block_rows,), -jnp.inf, jnp.float32)
        )

        def accumulate(key_number, state):
            weight_sum, mixed_sum = state
            scores, allowed = scores_of(key_number)
            weights = jnp.where(allowed, jnp.exp(scores - peak[:, None]), 0.0)
            mixed_next = mixed_sum + jnp.dot(
                weights.astype(jnp.bfloat16), values, preferred_element_type=jnp.float32
            )
            return (weight_sum + jnp.sum(weights, axis=1), mixed_next)

        start_state = (
            jnp.zeros((block_rows,), jnp.float32),
            jnp.zeros((block_rows, HD), jnp.float32),
        )
        weight_sum, mixed_sum = lax.fori_loop(lowest, highest, accumulate, start_state)
        return (mixed_sum / weight_sum[:, None]).astype(jnp.bfloat16)

    own_blocks = (2 * quarter_index, 2 * quarter_index + 1)
    own_rows = jnp.concatenate([attend_block(own_blocks[0]), attend_block(own_blocks[1])], 0)[None]
    for bit_number in range(level_count):
        partner = swapped(own_rows, "tensor", bit_number)
        lower = tensor_index >> bit_number & 1 == 0
        own_rows = jnp.where(
            lower, jnp.concatenate([own_rows, partner], 0), jnp.concatenate([partner, own_rows], 0)
        )
    attended = own_rows.reshape(tokens_total, HD)
    attended_quarter = lax.dynamic_slice_in_dim(
        attended, quarter_index * quarter_width, quarter_width, 1
    )
    hidden_rows = hidden
    summed = lax.psum_scatter(
        (
            jnp.dot(attended_quarter, output_weight, preferred_element_type=jnp.float32)
            + jnp.dot(hidden_rows, downward_weight, preferred_element_type=jnp.float32)
        ).astype(jnp.bfloat16),
        "tensor",
        scatter_dimension=0,
        tiled=True,
    ).astype(jnp.float32)
    layer_output = hidden_states.astype(jnp.float32) + summed
    key_quarter = lax.dynamic_slice_in_dim(keys, quarter_index * quarter_width, quarter_width, 1)
    value_quarter = joined_rows[:, 2 * quarter_width :]
    page_count = tokens_total // PAGE
    page_rows = jnp.concatenate([key_quarter, value_quarter], 1).reshape(
        page_count, PAGE * 2 * quarter_width
    )
    targets = page_targets[:, 0]
    page_numbers = jnp.arange(page_count, dtype=jnp.int32)
    earlier = jnp.sum(
        (
            (targets[None, :] == targets[:, None]) & (page_numbers[None, :] < page_numbers[:, None])
        ).astype(jnp.int32),
        axis=1,
    )
    capacity = 2 * page_count // replica_count
    slot_numbers = targets * capacity + earlier
    placing = (
        jnp.arange(replica_count * capacity, dtype=jnp.int32)[:, None] == slot_numbers[None, :]
    ).astype(jnp.bfloat16)
    outgoing = jnp.dot(placing, page_rows, preferred_element_type=jnp.float32).astype(jnp.bfloat16)
    outgoing = outgoing.reshape(replica_count, capacity, PAGE * 2 * quarter_width)
    incoming = lax.all_to_all(outgoing, "dp", split_axis=0, concat_axis=0, tiled=True)
    cache_pages = incoming.reshape(1, replica_count, capacity, PAGE, 2 * quarter_width)
    return (layer_output, cache_pages)


CORES = 2
CHIPS = 4
MIB = 1 << 20


def in_hbm(array):
    return pltpu.with_memory_space_constraint(array, pltpu.HBM)


def exchanged(block, axis, mask):
    count = lax.axis_size(axis)
    return lax.ppermute(block, axis, [(member, member ^ mask) for member in range(count)])


def vmem_specs(count):
    return [pl.BlockSpec(memory_space=pltpu.VMEM)] * count


def parameters(mebibytes):
    return pltpu.CompilerParams(vmem_limit_bytes=mebibytes * MIB)


def whereabouts():
    member = lax.axis_index("tensor")
    return member // CORES, member % CORES


def position_of(kind, half, block_rows):
    chip, core = whereabouts()
    return ((chip ^ kind) * CORES + (core ^ half)) * block_rows


def positions_along(first, shape, axis, block_rows):
    chip, core = whereabouts()
    bits = block_rows.bit_length() - 1
    place = first + lax.broadcasted_iota(jnp.int32, shape, axis)
    kind = place >> (bits + 1)
    half = (place >> bits) & 1
    return ((((chip ^ kind) << 1) | (core ^ half)) << bits) | (place & (block_rows - 1))


def normalize(blocks, gain_refs, normed_refs):
    piece = 16
    gains = [gain_ref[...] for gain_ref in gain_refs]
    for number, block_ref in enumerate(blocks):
        block_rows = block_ref.shape[0]
        for part in range(0, block_rows, piece):
            floats = block_ref[part : part + piece, :].astype(jnp.float32)
            center = jnp.mean(floats, axis=-1, keepdims=True)
            shifted = floats - center
            spread = jnp.mean(shifted * shifted, axis=-1, keepdims=True)
            scaled = shifted * lax.rsqrt(spread + epsilon)
            first = number * block_rows + part
            for gain, normed_ref in zip(gains, normed_refs):
                normed_ref[first : first + piece, :] = (scaled * gain).astype(jnp.bfloat16)


def project(normed_ref, heads_ref, table_refs, places, joined_ref, first):
    rows = normed_ref.shape[0]
    block_rows = rows // len(places)
    for component in range(3):
        columns = slice(component * HD, (component + 1) * HD)
        joined = jnp.dot(
            normed_ref[...], heads_ref[:, columns], preferred_element_type=jnp.float32
        ).astype(jnp.bfloat16)
        joined_ref[first : first + rows, columns] = joined
        if component < 2:
            cosine, sine_down, sine_up = [
                jnp.concatenate(
                    [
                        table_ref[pl.ds(pl.multiple_of(place, block_rows), block_rows), :]
                        for place in places
                    ],
                    0,
                )
                for table_ref in table_refs
            ]
            turning = joined[:, :128].astype(jnp.float32)
            turned = (
                turning * cosine
                + pltpu.roll(turning, 128 - ROT // 2, 1) * sine_down
                + pltpu.roll(turning, ROT // 2, 1) * sine_up
            )
            joined_ref[first : first + rows, component * HD : component * HD + 128] = turned.astype(
                jnp.bfloat16
            )


def hide(normed_ref, upward_ref, hidden_ref, place):
    chunk = 256
    rows = slice(place, place + normed_ref.shape[0])
    for first in range(0, upward_ref.shape[1], chunk):
        columns = slice(first, first + chunk)
        upward = jnp.dot(
            normed_ref[...], upward_ref[:, columns], preferred_element_type=jnp.float32
        )
        hidden = 0.5 * upward * (1.0 + lax.erf(upward * (0.5**0.5)))
        hidden_ref[rows, columns] = hidden.astype(jnp.bfloat16)


def attend(joined_ref, offsets_ref, first, rows, block_rows):
    tokens = joined_ref.shape[0]
    starts = [
        position_of(place // (2 * block_rows), (place // block_rows) % 2, block_rows)
        for place in range(first, first + rows, block_rows)
    ]
    reach = jnp.concatenate(
        [
            offsets_ref[pl.ds(pl.multiple_of(start, block_rows), block_rows), :]
            for start in starts
        ],
        0,
    )[:, :1].astype(jnp.int32)
    row = positions_along(first, (rows, 1), 0, block_rows)
    column = positions_along(0, (1, tokens), 1, block_rows)
    allowed = (column <= row) & (column >= row - reach)
    scores = lax.dot_general(
        joined_ref[first : first + rows, :HD],
        joined_ref[:, HD : 2 * HD],
        (((1,), (1,)), ((), ())),
        preferred_element_type=jnp.float32,
    ) * (HD ** (-0.5))
    peak = jnp.max(jnp.where(allowed, scores, -jnp.inf), axis=1, keepdims=True)
    weights = jnp.where(allowed, jnp.exp(scores - peak), 0.0)
    weight_sum = jnp.sum(weights, axis=1, keepdims=True)
    mixed = jnp.dot(
        weights.astype(jnp.bfloat16), joined_ref[:, 2 * HD :], preferred_element_type=jnp.float32
    )
    return (mixed / weight_sum).astype(jnp.bfloat16)


def make_tables(segments_ref, offsets_ref, cosine_ref, sine_down_ref, sine_up_ref):
    tokens = segments_ref.shape[1]
    shape = (tokens, tokens)
    rows = lax.broadcasted_iota(jnp.int32, shape, 0)
    columns = lax.broadcasted_iota(jnp.int32, shape, 1)
    across = jnp.broadcast_to(segments_ref[...], shape).astype(jnp.float32)
    down = jnp.sum(jnp.where(rows == columns, across, 0.0), axis=1, keepdims=True)
    earlier = (across == down) & (columns < rows)
    offsets = jnp.sum(jnp.where(earlier, 1.0, 0.0), axis=1, keepdims=True)
    offsets_ref[...] = jnp.broadcast_to(offsets, offsets_ref.shape)
    half = ROT // 2
    lane = lax.broadcasted_iota(jnp.int32, (tokens, 128), 1)
    step = (lane & (half - 1)).astype(jnp.float32)
    frequency = jnp.exp(step * (-2.0 * math.log(rotary_base) / ROT))
    angles = offsets * frequency
    sine = jnp.sin(angles)
    cosine_ref[...] = jnp.where(lane < ROT, jnp.cos(angles), 1.0)
    sine_down_ref[...] = jnp.where(lane < half, -sine, 0.0)
    sine_up_ref[...] = jnp.where((lane >= half) & (lane < ROT), sine, 0.0)


def make_destinations(targets_ref, destinations_ref, replica_count, block_rows):
    page_count = targets_ref.shape[1]
    tokens = destinations_ref.shape[1]
    capacity = 2 * page_count // replica_count
    square = (page_count, page_count)
    rows = lax.broadcasted_iota(jnp.int32, square, 0)
    columns = lax.broadcasted_iota(jnp.int32, square, 1)
    across = jnp.broadcast_to(targets_ref[...], square).astype(jnp.float32)
    down = jnp.sum(jnp.where(rows == columns, across, 0.0), axis=1, keepdims=True)
    earlier = jnp.where((across == down) & (columns < rows), 1.0, 0.0)
    slots = jnp.sum(earlier, axis=1, keepdims=True).astype(jnp.int32)
    slots = (down.astype(jnp.int32) ^ lax.axis_index("dp")) * capacity + slots
    positions = positions_along(0, (1, tokens), 1, block_rows)
    bits = PAGE.bit_length() - 1
    pages = lax.broadcasted_iota(jnp.int32, (page_count, tokens), 0)
    chosen = jnp.where(pages == positions >> bits, slots.astype(jnp.float32), 0.0)
    slot = jnp.sum(chosen, axis=0, keepdims=True).astype(jnp.int32)
    destinations_ref[...] = slot * PAGE + (positions & (PAGE - 1))


def copies_in(sources, targets, sems):
    copies = []
    for number, (source, target) in enumerate(zip(sources, targets)):
        parts = 4 if source.shape[0] >= 256 else 1
        rows = source.shape[0] // parts
        places = [pl.ds(part * rows, rows) for part in range(parts)]
        copies.append(
            [
                pltpu.make_async_copy(source.at[place], target.at[place], sems.at[number, part])
                for part, place in enumerate(places)
            ]
        )
    for copy in sum(copies, []):
        copy.start()
    return copies


def wait_for(copies):
    for copy in copies:
        copy.wait()


def own_kernel(count, replica_count, *refs):
    sources, targets = refs[:count], refs[count : 2 * count]
    offsets_ref, *table_refs, destinations_ref, joined_ref, hidden_ref = refs[2 * count : -3]
    attention_scr, feedforward_scr, sems = refs[-3:]
    copies = copies_in(sources, targets, sems)
    segments_ref, targets_ref, states_ref, *gain_refs, heads_ref, upward_ref, _ = targets
    block_rows = states_ref.shape[0]
    wait_for(copies[0])
    make_tables(segments_ref, offsets_ref, *table_refs)
    wait_for(copies[1])
    make_destinations(targets_ref, destinations_ref, replica_count, block_rows)
    for number in (2, 3, 4):
        wait_for(copies[number])
    normalize([states_ref], gain_refs, [attention_scr, feedforward_scr])
    wait_for(copies[5])
    places = [position_of(0, 0, block_rows)]
    project(attention_scr, heads_ref, table_refs, places, joined_ref, 0)
    wait_for(copies[6])
    hide(feedforward_scr, upward_ref, hidden_ref, 0)
    wait_for(copies[7])


def own_rows(staged, replica_count):
    tokens = staged[0].shape[1]
    rows, width = staged[2].shape
    hidden_width = staged[6].shape[1]
    shapes = [pltpu.VMEM(array.shape, array.dtype) for array in staged]
    shapes += [pltpu.VMEM((tokens, 128), jnp.float32)] * 4
    shapes += [
        pltpu.VMEM((1, tokens), jnp.int32),
        pltpu.VMEM((rows, 3 * HD), jnp.bfloat16),
        pltpu.VMEM((rows, hidden_width), jnp.bfloat16),
    ]
    count = len(staged)
    return pl.pallas_call(
        functools.partial(own_kernel, count, replica_count),
        out_shape=shapes,
        in_specs=[pl.BlockSpec(memory_space=pltpu.HBM)] * count,
        out_specs=vmem_specs(len(shapes)),
        scratch_shapes=[
            pltpu.VMEM((rows, width), jnp.bfloat16),
            pltpu.VMEM((rows, width), jnp.bfloat16),
            pltpu.SemaphoreType.DMA((count, 4)),
        ],
        compiler_params=parameters(12),
        cost_estimate=pl.CostEstimate(
            flops=2 * rows * width * (3 * HD + hidden_width),
            bytes_accessed=sum(array.nbytes for array in staged),
            transcendentals=rows * hidden_width,
        ),
        name="own_rows",
    )(*[in_hbm(array) for array in staged])


def middle_kernel(origins, *refs):
    count = len(origins)
    blocks, (gain_a, gain_f, heads_ref, upward_ref) = refs[:count], refs[count : count + 4]
    table_refs, refs = refs[count + 4 : count + 7], refs[count + 7 :]
    staged = (len(refs) - 5) // 2
    sources, (joined_ref, hidden_ref), refs = refs[:staged], refs[staged:][:2], refs[staged + 2 :]
    targets, (attention_scr, feedforward_scr, sems) = refs[:staged], refs[staged:]
    copies = copies_in(sources, targets, sems)
    block_rows = blocks[0].shape[0]
    normalize(blocks, [gain_a, gain_f], [attention_scr, feedforward_scr])
    places = [position_of(kind, half, block_rows) for kind, half in origins]
    project(attention_scr, heads_ref, table_refs, places, joined_ref, 0)
    hide(feedforward_scr, upward_ref, hidden_ref, 0)
    wait_for(sum(copies, []))


def middle_rows(name, origins, blocks, gains, weights, tables, *staged):
    block_rows, width = blocks[0].shape
    rows = len(blocks) * block_rows
    hidden_width = weights[1].shape[1]
    return pl.pallas_call(
        functools.partial(middle_kernel, origins),
        out_shape=[
            pltpu.VMEM((rows, 3 * HD), jnp.bfloat16),
            pltpu.VMEM((rows, hidden_width), jnp.bfloat16),
        ]
        + [pltpu.VMEM(array.shape, array.dtype) for array in staged],
        in_specs=vmem_specs(len(blocks) + 2 + 2 + 3)
        + [pl.BlockSpec(memory_space=pltpu.HBM)] * len(staged),
        out_specs=vmem_specs(2 + len(staged)),
        scratch_shapes=[
            pltpu.VMEM((rows, width), jnp.bfloat16),
            pltpu.VMEM((rows, width), jnp.bfloat16),
            pltpu.SemaphoreType.DMA((max(len(staged), 1), 4)),
        ],
        compiler_params=parameters(12),
        cost_estimate=pl.CostEstimate(
            flops=2 * rows * width * (3 * HD + hidden_width),
            bytes_accessed=MIB,
            transcendentals=rows * hidden_width,
        ),
        name=name,
    )(*blocks, *gains, *weights, *tables, *[in_hbm(array) for array in staged])


def last_kernel(*refs):
    blocks, (gain_a, gain_f, heads_ref, upward_ref, downward_ref, output_ref) = refs[:2], refs[2:8]
    offsets_ref, *table_refs = refs[8:12]
    pieces = refs[12:15]
    joined_ref, sibling_ref, own_ref, attention_scr, feedforward_scr, hidden_scr = refs[15:]
    block_rows = blocks[0].shape[0]
    tokens = joined_ref.shape[0]
    first = tokens - CORES * block_rows
    normalize(blocks, [gain_a, gain_f], [attention_scr, feedforward_scr])
    for kind in range(CHIPS - 1):
        for half in range(CORES):
            place = (kind * CORES + half) * block_rows
            joined_ref[place : place + block_rows, :] = piece_of(pieces, kind, half, block_rows)
    places = [position_of(CHIPS - 1, half, block_rows) for half in range(CORES)]
    project(attention_scr, heads_ref, table_refs, places, joined_ref, first)
    hide(feedforward_scr, upward_ref, hidden_scr, 0)
    attended = attend(joined_ref, offsets_ref, first, CORES * block_rows, block_rows)
    partial_sums(attended, hidden_scr[...], output_ref, downward_ref, [own_ref], [sibling_ref])


def piece_of(pieces, kind, half, block_rows):
    piece, place = (0, 2, 1)[kind], 0
    if half:
        piece, place = 2, (kind + 1) * block_rows
    return pieces[piece][place : place + block_rows, :]


def partial_sums(attended, hidden, output_ref, downward_ref, own_refs, sibling_refs):
    rows = attended.shape[0] // (2 * len(own_refs))
    chunk = 512
    for begin in range(0, downward_ref.shape[1], chunk):
        columns = slice(begin, begin + chunk)
        partial = jnp.dot(
            hidden, downward_ref[:, columns], preferred_element_type=jnp.float32
        ) + jnp.dot(attended, output_ref[:, columns], preferred_element_type=jnp.float32)
        for number, (own_ref, sibling_ref) in enumerate(zip(own_refs, sibling_refs)):
            first = 2 * number * rows
            middle = first + rows
            own_ref[:, columns] = partial[first:middle]
            sibling_ref[:, columns] = partial[middle : middle + rows].astype(jnp.bfloat16)


def last_rows(blocks, gains, weights, tables, pieces):
    block_rows, width = blocks[0].shape
    rows = len(blocks) * block_rows
    hidden_width = weights[1].shape[1]
    tokens = CHIPS * CORES * block_rows
    return pl.pallas_call(
        last_kernel,
        out_shape=[
            pltpu.VMEM((tokens, 3 * HD), jnp.bfloat16),
            pltpu.VMEM((block_rows, width), jnp.bfloat16),
            pltpu.VMEM((block_rows, width), jnp.float32),
        ],
        in_specs=vmem_specs(len(blocks) + 2 + 4 + 4 + 3),
        out_specs=vmem_specs(3),
        scratch_shapes=[
            pltpu.VMEM((rows, width), jnp.bfloat16),
            pltpu.VMEM((rows, width), jnp.bfloat16),
            pltpu.VMEM((rows, hidden_width), jnp.bfloat16),
        ],
        compiler_params=parameters(12),
        cost_estimate=pl.CostEstimate(
            flops=2 * rows * width * (3 * HD + HD + 2 * hidden_width),
            bytes_accessed=MIB,
            transcendentals=rows * hidden_width,
        ),
        name="last_rows",
    )(*blocks, *gains, *weights, *tables, *pieces)


def kind_kernel(kinds, joined_ref, offsets_ref, output_ref, downward_ref, *refs):
    pieces, refs = refs[:3], refs[3:]
    count = len(kinds)
    siblings, owns = refs[:count], refs[count : 2 * count]
    block_rows = owns[0].shape[0]
    rows = CORES * block_rows * count
    attended = attend(joined_ref, offsets_ref, kinds[0] * CORES * block_rows, rows, block_rows)
    hidden = jnp.concatenate(
        [piece_of(pieces, kind, half, block_rows) for kind in kinds for half in range(CORES)], 0
    )
    partial_sums(attended, hidden, output_ref, downward_ref, owns, siblings)


def kind_rows(name, kinds, joined, offsets, weights, pieces):
    block_rows = pieces[0].shape[0]
    output_weight, downward_weight = weights
    width = output_weight.shape[1]
    shape = (block_rows, width)
    count = len(kinds)
    tokens = joined.shape[0]
    return pl.pallas_call(
        functools.partial(kind_kernel, kinds),
        out_shape=[pltpu.VMEM(shape, jnp.bfloat16)] * count + [pltpu.VMEM(shape, jnp.float32)] * count,
        in_specs=vmem_specs(7),
        out_specs=vmem_specs(2 * count),
        compiler_params=parameters(12),
        cost_estimate=pl.CostEstimate(
            flops=4 * block_rows * count * width * (HD + downward_weight.shape[0]),
            bytes_accessed=MIB,
            transcendentals=2 * block_rows * count * tokens,
        ),
        name=name,
    )(joined, offsets, output_weight, downward_weight, *pieces)


def pages_kernel(joined_ref, destinations_ref, *page_refs):
    tokens = joined_ref.shape[0]
    slot_rows = page_refs[0].shape[0] * PAGE
    for number, page_ref in enumerate(page_refs):
        shape = (slot_rows, tokens)
        row = number * slot_rows + lax.broadcasted_iota(jnp.int32, shape, 0)
        placing = jnp.where(row == destinations_ref[...], 1.0, 0.0).astype(jnp.bfloat16)
        rows = jnp.dot(placing, joined_ref[:, HD:], preferred_element_type=jnp.float32)
        page_ref[...] = rows.astype(jnp.bfloat16).reshape(page_ref.shape)


def cached_pages(joined, destinations, replica_count):
    tokens = joined.shape[0]
    capacity = 2 * (tokens // PAGE) // replica_count
    shapes = [pltpu.VMEM((capacity, PAGE, 2 * HD), jnp.bfloat16)] * replica_count
    return pl.pallas_call(
        pages_kernel,
        out_shape=shapes,
        in_specs=vmem_specs(2),
        out_specs=vmem_specs(len(shapes)),
        compiler_params=parameters(8),
        cost_estimate=pl.CostEstimate(flops=0, bytes_accessed=MIB, transcendentals=0),
        name="cached_pages",
    )(joined, destinations)


def add_kernel(*refs):
    total = refs[0][...].astype(jnp.float32)
    for ref in refs[1:-1]:
        total = total + ref[...].astype(jnp.float32)
    refs[-1][...] = total.astype(refs[-1].dtype)


def added(name, *parts):
    return pl.pallas_call(
        add_kernel,
        out_shape=pltpu.VMEM(parts[0].shape, jnp.bfloat16),
        in_specs=vmem_specs(len(parts)),
        out_specs=pl.BlockSpec(memory_space=pltpu.VMEM),
        compiler_params=parameters(4),
        name=name,
    )(*parts)


def sums_kernel(passing_ref, *refs):
    zeros, ones, twos = refs[0:2], refs[2:4], refs[4:6]
    hidden_ref, second_ref, first_ref, base_ref = refs[6:]

    def total(pair, extra=None):
        received_ref, own_ref = pair
        value = own_ref[...] + received_ref[...].astype(jnp.float32)
        return value if extra is None else value + extra[...].astype(jnp.float32)

    second_ref[...] = total(twos, passing_ref).astype(jnp.bfloat16)
    first_ref[...] = total(ones).astype(jnp.bfloat16)
    base_ref[...] = total(zeros, hidden_ref)


def remaining_sums(passing, pairs, hidden):
    shape = hidden.shape
    return pl.pallas_call(
        sums_kernel,
        out_shape=[
            pltpu.VMEM(shape, jnp.bfloat16),
            pltpu.VMEM(shape, jnp.bfloat16),
            pltpu.VMEM(shape, jnp.float32),
        ],
        in_specs=vmem_specs(8),
        out_specs=vmem_specs(3),
        compiler_params=parameters(4),
        name="remaining_sums",
    )(passing, *[array for pair in pairs for array in pair], hidden)


def place_kernel(masks, *refs):
    group = lax.axis_index("dp")
    pages, (cache_ref, sems) = refs[:-2], refs[-2:]
    copies = [
        pltpu.make_async_copy(page_ref, cache_ref.at[0, group ^ mask], sems.at[number])
        for number, (mask, page_ref) in enumerate(zip(masks, pages))
    ]
    for copy in copies:
        copy.start()
    for copy in copies:
        copy.wait()


def placed(masks, pages, replica_count):
    count = len(pages)
    return pl.pallas_call(
        functools.partial(place_kernel, masks),
        out_shape=jax.ShapeDtypeStruct((1, replica_count) + pages[0].shape, pages[0].dtype),
        in_specs=[pl.BlockSpec(memory_space=pl.ANY)] * count,
        out_specs=pl.BlockSpec(memory_space=pltpu.HBM),
        scratch_shapes=[pltpu.SemaphoreType.DMA((count,))],
        compiler_params=parameters(4),
        name="placed",
    )(*pages)


def finish_kernel(masks, base_ref, *refs):
    count = len(masks)
    *parts, _, output_ref, cache_ref, total_scr, sems = refs
    parts, pages = parts[:-count], parts[-count:]
    group = lax.axis_index("dp")
    copies = [
        pltpu.make_async_copy(page_ref, cache_ref.at[0, group ^ mask], sems.at[number])
        for number, (mask, page_ref) in enumerate(zip(masks, pages))
    ]
    for copy in copies:
        copy.start()
    total = base_ref[...]
    for part_ref in parts:
        total = total + part_ref[...].astype(jnp.float32)
    total_scr[...] = total
    copies.append(pltpu.make_async_copy(total_scr, output_ref, sems.at[count]))
    copies[-1].start()
    for copy in copies:
        copy.wait()


def finished(base, parts, masks, pages, cache):
    count = len(pages)
    return pl.pallas_call(
        functools.partial(finish_kernel, masks),
        out_shape=[
            jax.ShapeDtypeStruct(base.shape, base.dtype),
            jax.ShapeDtypeStruct(cache.shape, cache.dtype),
        ],
        in_specs=vmem_specs(1 + len(parts))
        + [pl.BlockSpec(memory_space=pl.ANY)] * count
        + [pl.BlockSpec(memory_space=pltpu.HBM)],
        out_specs=[pl.BlockSpec(memory_space=pltpu.HBM)] * 2,
        scratch_shapes=[
            pltpu.VMEM(base.shape, base.dtype),
            pltpu.SemaphoreType.DMA((count + 1,)),
        ],
        input_output_aliases={1 + len(parts) + count: 1},
        compiler_params=parameters(4),
        name="finished",
    )(base, *parts, *pages, cache)


def shards_whole_heads(
    hidden_states,
    attention_gain,
    feedforward_gain,
    heads_weight,
    output_weight,
    upward_weight,
    downward_weight,
    segments,
    page_targets,
):
    replica_count = lax.axis_size("dp")
    to_chip = [mask * CORES for mask in range(CHIPS)]
    second = exchanged(hidden_states, "tensor", to_chip[2])
    staged = (
        segments,
        page_targets.reshape(1, -1),
        hidden_states,
        attention_gain[None],
        feedforward_gain[None],
        heads_weight,
        upward_weight,
        downward_weight,
    )
    staged = own_rows(staged, replica_count)
    hidden, gains, weights, tables = staged[2], staged[3:5], staged[5:8], staged[8:12]
    heads, upward, downward = weights
    destinations, own_joined, own_hidden = staged[12:]

    first = exchanged(hidden, "tensor", to_chip[1])
    beside = exchanged(hidden, "tensor", 1)
    second, own_joined = lax.optimization_barrier((second, own_joined))
    third = exchanged(second, "tensor", to_chip[1])
    second_beside = exchanged(second, "tensor", 1)
    first_beside = exchanged(first, "tensor", 1)
    there_joined, there_hidden = middle_rows(
        "there_rows", ((2, 0),), (second,), gains, (heads, upward), tables[1:]
    )
    third, there_joined = lax.optimization_barrier((third, there_joined))
    third_beside = exchanged(third, "tensor", 1)
    beside_joined, beside_hidden, output = middle_rows(
        "beside_rows",
        ((1, 0), (0, 1), (1, 1), (2, 1)),
        (first, beside, first_beside, second_beside),
        gains,
        (heads, upward),
        tables[1:],
        output_weight,
    )
    joined, sibling, own = last_rows(
        (third, third_beside),
        gains,
        (heads, upward, downward, output),
        tables,
        (own_joined, there_joined, beside_joined),
    )

    pieces = (own_hidden, there_hidden, beside_hidden)
    received = exchanged(sibling, "tensor", 1)
    partials = kind_rows("rest_rows", (0, 1, 2), joined, tables[0], (output, downward), pieces)
    siblings, owns = partials[: CHIPS - 1], partials[CHIPS - 1 :]
    third_sum = added("third_added", own, received)
    third_sum, siblings, joined = lax.optimization_barrier((third_sum, siblings, joined))
    passing = exchanged(third_sum, "tensor", to_chip[1])
    pairs = [(exchanged(sibling, "tensor", 1), own) for sibling, own in zip(siblings, owns)]
    pages = cached_pages(joined, destinations, replica_count)
    early, late = (3,), (1, 2)
    arriving = [exchanged(pages[mask], "dp", mask) for mask in early]
    second_sum, first_sum, base = remaining_sums(passing, pairs, hidden)
    from_second = exchanged(second_sum, "tensor", to_chip[2])
    from_first = exchanged(first_sum, "tensor", to_chip[1])
    base, late_pages = lax.optimization_barrier((base, [pages[mask] for mask in late]))
    late_pages = [exchanged(page, "dp", mask) for mask, page in zip(late, late_pages)]
    cache_pages = placed((0,) + early, [pages[0]] + arriving, replica_count)
    return tuple(finished(base, (from_second, from_first), late, late_pages, cache_pages))


def solution(mesh):
    whole_heads = mesh.shape["tensor"] == H and mesh.shape["dp"] == 4
    shards = shards_whole_heads if whole_heads else shards_split_heads
    in_specs = (
        P(("dp", "tensor"), None),
        P(),
        P(),
        P(None, "tensor"),
        P("tensor", None),
        P(None, "tensor"),
        P("tensor", None),
        P("dp", None),
        P("dp", None),
    )
    out_specs = (P(("dp", "tensor"), None), P("dp", None, None, None, "tensor"))
    return jax.shard_map(shards, mesh=mesh, in_specs=in_specs, out_specs=out_specs, check_vma=False)
```

```python
import functools
import math

import jax
import jax.numpy as jnp
from jax import lax
from jax.experimental import pallas as pl
from jax.experimental.pallas import tpu as pltpu
from jax.sharding import PartitionSpec as P

H = 8
HD = 256
ROT = 64
PAGE = 16


epsilon = 1e-05
rotary_base = 10000.0
key_block = 256


def shortened(array):

    def short(part):
        return part.astype(jnp.bfloat16) if part.dtype == jnp.float32 else part

    return jax.tree.map(short, array)


def swapped(block, axis, apart):
    count = lax.axis_size(axis)
    route = []
    for low in range(count):
        high = low | 1 << apart
        if high != low and high < count:
            route += [(low, high), (high, low)]
    return lax.ppermute(block, axis, route)


def layer_norm(values, gain):
    floats = values.astype(jnp.float32)
    center = jnp.mean(floats, axis=-1, keepdims=True)
    shifted = floats - center
    spread = jnp.mean(shifted * shifted, axis=-1, keepdims=True)
    return (shifted * lax.rsqrt(spread + epsilon) * gain).astype(jnp.bfloat16)


def positions_of(stream):
    indices = jnp.arange(stream.shape[0], dtype=jnp.int32)
    boundary = jnp.concatenate([jnp.ones((1,), dtype=bool), stream[1:] != stream[:-1]])
    starting = lax.cummax(jnp.where(boundary, indices, jnp.zeros_like(indices)), axis=0)
    return (indices, starting)


def rotate_heads(vectors, offsets, rotary_dims):
    half_dims = rotary_dims // 2
    frequency = jnp.exp(
        jnp.arange(half_dims, dtype=jnp.float32) * (-2.0 * math.log(rotary_base) / rotary_dims)
    )
    angles = offsets.astype(jnp.float32)[:, None] * frequency[None, :]
    cosine = jnp.cos(angles)
    sine = jnp.sin(angles)
    floats = vectors.astype(jnp.float32)
    leading = floats[..., :half_dims]
    trailing = floats[..., half_dims:rotary_dims]
    rotated = jnp.concatenate(
        [
            leading * cosine - trailing * sine,
            trailing * cosine + leading * sine,
            floats[..., rotary_dims:],
        ],
        axis=-1,
    )
    return rotated.astype(jnp.bfloat16)


def shards_split_heads(
    hidden_states,
    attention_gain,
    feedforward_gain,
    heads_weight,
    output_weight,
    upward_weight,
    downward_weight,
    segments,
    page_targets,
):
    tensor_count = lax.axis_size("tensor")
    replica_count = lax.axis_size("dp")
    tensor_index = lax.axis_index("tensor")
    quarters = tensor_count // H
    quarter_width = HD // quarters
    quarter_index = tensor_index % quarters
    stream = segments[0]
    tokens_total = stream.shape[0]
    level_count = quarters.bit_length() - 1
    normed_attention = layer_norm(hidden_states, attention_gain)
    normed_feedforward = layer_norm(hidden_states, feedforward_gain)
    shard_rows = lax.all_gather(
        (normed_attention, normed_feedforward), "tensor", axis=0, tiled=True
    )
    joined_rows = jnp.dot(shard_rows[0], heads_weight, preferred_element_type=jnp.float32).astype(
        jnp.bfloat16
    )
    upward = jnp.dot(shard_rows[1], upward_weight, preferred_element_type=jnp.float32)
    hidden_rows = jax.nn.gelu(upward, approximate=False).astype(jnp.bfloat16)
    hidden = hidden_rows
    pieces = (
        joined_rows.reshape(tokens_total, 3, quarter_width)
        .transpose(1, 0, 2)
        .reshape(1, 3, tokens_total * quarter_width)
    )
    for bit_number in range(level_count):
        partner = swapped(shortened(pieces), "tensor", bit_number).astype(pieces.dtype)
        lower = tensor_index >> bit_number & 1 == 0
        pieces = jnp.where(
            lower, jnp.concatenate([pieces, partner], 0), jnp.concatenate([partner, pieces], 0)
        )
    whole_head = (
        pieces.reshape(quarters, 3, tokens_total, quarter_width)
        .transpose(1, 2, 0, 3)
        .reshape(3, tokens_total, HD)
    )
    indices, starting = positions_of(stream)
    offsets = indices - starting
    queries = rotate_heads(whole_head[0], offsets, ROT)
    keys = rotate_heads(whole_head[1], offsets, ROT)
    values = whole_head[2]
    block_rows = tokens_total // (2 * quarters)
    score_scale = HD ** (-0.5)

    def attend_block(block_number):
        first_row = block_number * block_rows
        block_queries = lax.dynamic_slice_in_dim(queries, first_row, block_rows, 0)
        query_segments = lax.dynamic_slice_in_dim(stream, first_row, block_rows, 0)
        query_indices = first_row + jnp.arange(block_rows, dtype=jnp.int32)
        lowest = lax.dynamic_index_in_dim(starting, first_row, 0, keepdims=False) // key_block
        highest = (first_row + block_rows + key_block - 1) // key_block

        def scores_of(key_number):
            key_first = key_number * key_block
            key_indices = key_first + jnp.arange(key_block, dtype=jnp.int32)
            scores = (
                jnp.dot(block_queries, keys.T, preferred_element_type=jnp.float32) * score_scale
            )
            allowed = (stream[None, :] == query_segments[:, None]) & (
                key_indices[None, :] <= query_indices[:, None]
            )
            return (scores, allowed)

        def find_peak(key_number, peak):
            scores, allowed = scores_of(key_number)
            return jnp.maximum(peak, jnp.max(jnp.where(allowed, scores, -jnp.inf), axis=1))

        peak = lax.fori_loop(
            lowest, highest, find_peak, jnp.full((block_rows,), -jnp.inf, jnp.float32)
        )

        def accumulate(key_number, state):
            weight_sum, mixed_sum = state
            scores, allowed = scores_of(key_number)
            weights = jnp.where(allowed, jnp.exp(scores - peak[:, None]), 0.0)
            mixed_next = mixed_sum + jnp.dot(
                weights.astype(jnp.bfloat16), values, preferred_element_type=jnp.float32
            )
            return (weight_sum + jnp.sum(weights, axis=1), mixed_next)

        start_state = (
            jnp.zeros((block_rows,), jnp.float32),
            jnp.zeros((block_rows, HD), jnp.float32),
        )
        weight_sum, mixed_sum = lax.fori_loop(lowest, highest, accumulate, start_state)
        return (mixed_sum / weight_sum[:, None]).astype(jnp.bfloat16)

    own_blocks = (2 * quarter_index, 2 * quarter_index + 1)
    own_rows = jnp.concatenate([attend_block(own_blocks[0]), attend_block(own_blocks[1])], 0)[None]
    for bit_number in range(level_count):
        partner = swapped(own_rows, "tensor", bit_number)
        lower = tensor_index >> bit_number & 1 == 0
        own_rows = jnp.where(
            lower, jnp.concatenate([own_rows, partner], 0), jnp.concatenate([partner, own_rows], 0)
        )
    attended = own_rows.reshape(tokens_total, HD)
    attended_quarter = lax.dynamic_slice_in_dim(
        attended, quarter_index * quarter_width, quarter_width, 1
    )
    hidden_rows = hidden
    summed = lax.psum_scatter(
        (
            jnp.dot(attended_quarter, output_weight, preferred_element_type=jnp.float32)
            + jnp.dot(hidden_rows, downward_weight, preferred_element_type=jnp.float32)
        ).astype(jnp.bfloat16),
        "tensor",
        scatter_dimension=0,
        tiled=True,
    ).astype(jnp.float32)
    layer_output = hidden_states.astype(jnp.float32) + summed
    key_quarter = lax.dynamic_slice_in_dim(keys, quarter_index * quarter_width, quarter_width, 1)
    value_quarter = joined_rows[:, 2 * quarter_width :]
    page_count = tokens_total // PAGE
    page_rows = jnp.concatenate([key_quarter, value_quarter], 1).reshape(
        page_count, PAGE * 2 * quarter_width
    )
    targets = page_targets[:, 0]
    page_numbers = jnp.arange(page_count, dtype=jnp.int32)
    earlier = jnp.sum(
        (
            (targets[None, :] == targets[:, None]) & (page_numbers[None, :] < page_numbers[:, None])
        ).astype(jnp.int32),
        axis=1,
    )
    capacity = 2 * page_count // replica_count
    slot_numbers = targets * capacity + earlier
    placing = (
        jnp.arange(replica_count * capacity, dtype=jnp.int32)[:, None] == slot_numbers[None, :]
    ).astype(jnp.bfloat16)
    outgoing = jnp.dot(placing, page_rows, preferred_element_type=jnp.float32).astype(jnp.bfloat16)
    outgoing = outgoing.reshape(replica_count, capacity, PAGE * 2 * quarter_width)
    incoming = lax.all_to_all(outgoing, "dp", split_axis=0, concat_axis=0, tiled=True)
    cache_pages = incoming.reshape(1, replica_count, capacity, PAGE, 2 * quarter_width)
    return (layer_output, cache_pages)


CORES = 2
CHIPS = 4
MIB = 1 << 20


def in_hbm(array):
    return pltpu.with_memory_space_constraint(array, pltpu.HBM)


def exchanged(block, axis, mask):
    count = lax.axis_size(axis)
    return lax.ppermute(block, axis, [(member, member ^ mask) for member in range(count)])


def vmem_specs(count):
    return [pl.BlockSpec(memory_space=pltpu.VMEM)] * count


def parameters(mebibytes):
    return pltpu.CompilerParams(vmem_limit_bytes=mebibytes * MIB)


def whereabouts():
    member = lax.axis_index("tensor")
    return member // CORES, member % CORES


def position_of(kind, half, block_rows):
    chip, core = whereabouts()
    return ((chip ^ kind) * CORES + (core ^ half)) * block_rows


def positions_along(first, shape, axis, block_rows):
    chip, core = whereabouts()
    bits = block_rows.bit_length() - 1
    place = first + lax.broadcasted_iota(jnp.int32, shape, axis)
    kind = place >> (bits + 1)
    half = (place >> bits) & 1
    return ((((chip ^ kind) << 1) | (core ^ half)) << bits) | (place & (block_rows - 1))


def normalize(blocks, gain_refs, normed_refs):
    piece = 16
    gains = [gain_ref[...] for gain_ref in gain_refs]
    for number, block_ref in enumerate(blocks):
        block_rows = block_ref.shape[0]
        for part in range(0, block_rows, piece):
            floats = block_ref[part : part + piece, :].astype(jnp.float32)
            center = jnp.mean(floats, axis=-1, keepdims=True)
            shifted = floats - center
            spread = jnp.mean(shifted * shifted, axis=-1, keepdims=True)
            scaled = shifted * lax.rsqrt(spread + epsilon)
            first = number * block_rows + part
            for gain, normed_ref in zip(gains, normed_refs):
                normed_ref[first : first + piece, :] = (scaled * gain).astype(jnp.bfloat16)


def project(normed_ref, heads_ref, table_refs, places, joined_ref, first):
    rows = normed_ref.shape[0]
    block_rows = rows // len(places)
    for component in range(3):
        columns = slice(component * HD, (component + 1) * HD)
        joined = jnp.dot(
            normed_ref[...], heads_ref[:, columns], preferred_element_type=jnp.float32
        ).astype(jnp.bfloat16)
        joined_ref[first : first + rows, columns] = joined
        if component < 2:
            cosine, sine_down, sine_up = [
                jnp.concatenate(
                    [
                        table_ref[pl.ds(pl.multiple_of(place, block_rows), block_rows), :]
                        for place in places
                    ],
                    0,
                )
                for table_ref in table_refs
            ]
            turning = joined[:, :128].astype(jnp.float32)
            turned = (
                turning * cosine
                + pltpu.roll(turning, 128 - ROT // 2, 1) * sine_down
                + pltpu.roll(turning, ROT // 2, 1) * sine_up
            )
            joined_ref[first : first + rows, component * HD : component * HD + 128] = turned.astype(
                jnp.bfloat16
            )


def hide(normed_ref, upward_ref, hidden_ref, place):
    chunk = 256
    rows = slice(place, place + normed_ref.shape[0])
    for first in range(0, upward_ref.shape[1], chunk):
        columns = slice(first, first + chunk)
        upward = jnp.dot(
            normed_ref[...], upward_ref[:, columns], preferred_element_type=jnp.float32
        )
        hidden = 0.5 * upward * (1.0 + lax.erf(upward * (0.5**0.5)))
        hidden_ref[rows, columns] = hidden.astype(jnp.bfloat16)


def attend(joined_ref, offsets_ref, first, rows, block_rows):
    tokens = joined_ref.shape[0]
    starts = [
        position_of(place // (2 * block_rows), (place // block_rows) % 2, block_rows)
        for place in range(first, first + rows, block_rows)
    ]
    reach = jnp.concatenate(
        [
            offsets_ref[pl.ds(pl.multiple_of(start, block_rows), block_rows), :]
            for start in starts
        ],
        0,
    )[:, :1].astype(jnp.int32)
    row = positions_along(first, (rows, 1), 0, block_rows)
    column = positions_along(0, (1, tokens), 1, block_rows)
    allowed = (column <= row) & (column >= row - reach)
    scores = lax.dot_general(
        joined_ref[first : first + rows, :HD],
        joined_ref[:, HD : 2 * HD],
        (((1,), (1,)), ((), ())),
        preferred_element_type=jnp.float32,
    ) * (HD ** (-0.5))
    peak = jnp.max(jnp.where(allowed, scores, -jnp.inf), axis=1, keepdims=True)
    weights = jnp.where(allowed, jnp.exp(scores - peak), 0.0)
    weight_sum = jnp.sum(weights, axis=1, keepdims=True)
    mixed = jnp.dot(
        weights.astype(jnp.bfloat16), joined_ref[:, 2 * HD :], preferred_element_type=jnp.float32
    )
    return (mixed / weight_sum).astype(jnp.bfloat16)


def make_tables(segments_ref, offsets_ref, cosine_ref, sine_down_ref, sine_up_ref):
    tokens = segments_ref.shape[1]
    shape = (tokens, tokens)
    rows = lax.broadcasted_iota(jnp.int32, shape, 0)
    columns = lax.broadcasted_iota(jnp.int32, shape, 1)
    across = jnp.broadcast_to(segments_ref[...], shape).astype(jnp.float32)
    down = jnp.sum(jnp.where(rows == columns, across, 0.0), axis=1, keepdims=True)
    earlier = (across == down) & (columns < rows)
    offsets = jnp.sum(jnp.where(earlier, 1.0, 0.0), axis=1, keepdims=True)
    offsets_ref[...] = jnp.broadcast_to(offsets, offsets_ref.shape)
    half = ROT // 2
    lane = lax.broadcasted_iota(jnp.int32, (tokens, 128), 1)
    step = (lane & (half - 1)).astype(jnp.float32)
    frequency = jnp.exp(step * (-2.0 * math.log(rotary_base) / ROT))
    angles = offsets * frequency
    sine = jnp.sin(angles)
    cosine_ref[...] = jnp.where(lane < ROT, jnp.cos(angles), 1.0)
    sine_down_ref[...] = jnp.where(lane < half, -sine, 0.0)
    sine_up_ref[...] = jnp.where((lane >= half) & (lane < ROT), sine, 0.0)


def make_destinations(targets_ref, destinations_ref, replica_count, block_rows):
    page_count = targets_ref.shape[1]
    tokens = destinations_ref.shape[1]
    capacity = 2 * page_count // replica_count
    square = (page_count, page_count)
    rows = lax.broadcasted_iota(jnp.int32, square, 0)
    columns = lax.broadcasted_iota(jnp.int32, square, 1)
    across = jnp.broadcast_to(targets_ref[...], square).astype(jnp.float32)
    down = jnp.sum(jnp.where(rows == columns, across, 0.0), axis=1, keepdims=True)
    earlier = jnp.where((across == down) & (columns < rows), 1.0, 0.0)
    slots = jnp.sum(earlier, axis=1, keepdims=True).astype(jnp.int32)
    slots = (down.astype(jnp.int32) ^ lax.axis_index("dp")) * capacity + slots
    positions = positions_along(0, (1, tokens), 1, block_rows)
    bits = PAGE.bit_length() - 1
    pages = lax.broadcasted_iota(jnp.int32, (page_count, tokens), 0)
    chosen = jnp.where(pages == positions >> bits, slots.astype(jnp.float32), 0.0)
    slot = jnp.sum(chosen, axis=0, keepdims=True).astype(jnp.int32)
    destinations_ref[...] = slot * PAGE + (positions & (PAGE - 1))


def copies_in(sources, targets, sems):
    copies = []
    for number, (source, target) in enumerate(zip(sources, targets)):
        parts = 4 if source.shape[0] >= 256 else 1
        rows = source.shape[0] // parts
        places = [pl.ds(part * rows, rows) for part in range(parts)]
        copies.append(
            [
                pltpu.make_async_copy(source.at[place], target.at[place], sems.at[number, part])
                for part, place in enumerate(places)
            ]
        )
    for copy in sum(copies, []):
        copy.start()
    return copies


def wait_for(copies):
    for copy in copies:
        copy.wait()


def own_kernel(count, replica_count, *refs):
    sources, targets = refs[:count], refs[count : 2 * count]
    offsets_ref, *table_refs, destinations_ref, joined_ref, hidden_ref = refs[2 * count : -3]
    attention_scr, feedforward_scr, sems = refs[-3:]
    copies = copies_in(sources, targets, sems)
    segments_ref, targets_ref, states_ref, *gain_refs, heads_ref, upward_ref, _ = targets
    block_rows = states_ref.shape[0]
    wait_for(copies[0])
    make_tables(segments_ref, offsets_ref, *table_refs)
    wait_for(copies[1])
    make_destinations(targets_ref, destinations_ref, replica_count, block_rows)
    for number in (2, 3, 4):
        wait_for(copies[number])
    normalize([states_ref], gain_refs, [attention_scr, feedforward_scr])
    wait_for(copies[5])
    places = [position_of(0, 0, block_rows)]
    project(attention_scr, heads_ref, table_refs, places, joined_ref, 0)
    wait_for(copies[6])
    hide(feedforward_scr, upward_ref, hidden_ref, 0)
    wait_for(copies[7])


def own_rows(staged, replica_count):
    tokens = staged[0].shape[1]
    rows, width = staged[2].shape
    hidden_width = staged[6].shape[1]
    shapes = [pltpu.VMEM(array.shape, array.dtype) for array in staged]
    shapes += [pltpu.VMEM((tokens, 128), jnp.float32)] * 4
    shapes += [
        pltpu.VMEM((1, tokens), jnp.int32),
        pltpu.VMEM((rows, 3 * HD), jnp.bfloat16),
        pltpu.VMEM((rows, hidden_width), jnp.bfloat16),
    ]
    count = len(staged)
    return pl.pallas_call(
        functools.partial(own_kernel, count, replica_count),
        out_shape=shapes,
        in_specs=[pl.BlockSpec(memory_space=pltpu.HBM)] * count,
        out_specs=vmem_specs(len(shapes)),
        scratch_shapes=[
            pltpu.VMEM((rows, width), jnp.bfloat16),
            pltpu.VMEM((rows, width), jnp.bfloat16),
            pltpu.SemaphoreType.DMA((count, 4)),
        ],
        compiler_params=parameters(12),
        cost_estimate=pl.CostEstimate(
            flops=2 * rows * width * (3 * HD + hidden_width),
            bytes_accessed=sum(array.nbytes for array in staged),
            transcendentals=rows * hidden_width,
        ),
        name="own_rows",
    )(*[in_hbm(array) for array in staged])


def middle_kernel(origins, *refs):
    count = len(origins)
    blocks, (gain_a, gain_f, heads_ref, upward_ref) = refs[:count], refs[count : count + 4]
    table_refs, refs = refs[count + 4 : count + 7], refs[count + 7 :]
    staged = (len(refs) - 5) // 2
    sources, (joined_ref, hidden_ref), refs = refs[:staged], refs[staged:][:2], refs[staged + 2 :]
    targets, (attention_scr, feedforward_scr, sems) = refs[:staged], refs[staged:]
    copies = copies_in(sources, targets, sems)
    block_rows = blocks[0].shape[0]
    normalize(blocks, [gain_a, gain_f], [attention_scr, feedforward_scr])
    places = [position_of(kind, half, block_rows) for kind, half in origins]
    project(attention_scr, heads_ref, table_refs, places, joined_ref, 0)
    hide(feedforward_scr, upward_ref, hidden_ref, 0)
    wait_for(sum(copies, []))


def middle_rows(name, origins, blocks, gains, weights, tables, *staged):
    block_rows, width = blocks[0].shape
    rows = len(blocks) * block_rows
    hidden_width = weights[1].shape[1]
    return pl.pallas_call(
        functools.partial(middle_kernel, origins),
        out_shape=[
            pltpu.VMEM((rows, 3 * HD), jnp.bfloat16),
            pltpu.VMEM((rows, hidden_width), jnp.bfloat16),
        ]
        + [pltpu.VMEM(array.shape, array.dtype) for array in staged],
        in_specs=vmem_specs(len(blocks) + 2 + 2 + 3)
        + [pl.BlockSpec(memory_space=pltpu.HBM)] * len(staged),
        out_specs=vmem_specs(2 + len(staged)),
        scratch_shapes=[
            pltpu.VMEM((rows, width), jnp.bfloat16),
            pltpu.VMEM((rows, width), jnp.bfloat16),
            pltpu.SemaphoreType.DMA((max(len(staged), 1), 4)),
        ],
        compiler_params=parameters(12),
        cost_estimate=pl.CostEstimate(
            flops=2 * rows * width * (3 * HD + hidden_width),
            bytes_accessed=MIB,
            transcendentals=rows * hidden_width,
        ),
        name=name,
    )(*blocks, *gains, *weights, *tables, *[in_hbm(array) for array in staged])


def last_kernel(*refs):
    blocks, (gain_a, gain_f, heads_ref, upward_ref, downward_ref, output_ref) = refs[:3], refs[3:9]
    offsets_ref, *table_refs = refs[9:13]
    own_joined_ref, middle_joined_ref = refs[13:15]
    joined_ref, fed_ref, sibling_ref, own_ref = refs[15:19]
    attention_scr, feedforward_scr, hidden_scr = refs[19:]
    block_rows = blocks[0].shape[0]
    tokens = joined_ref.shape[0]
    first = tokens - len(blocks) * block_rows
    normalize(blocks, [gain_a, gain_f], [attention_scr, feedforward_scr])
    joined_ref[:block_rows, :] = own_joined_ref[...]
    joined_ref[block_rows:first, :] = middle_joined_ref[...]
    origins = ((CHIPS - 2, 1), (CHIPS - 1, 0), (CHIPS - 1, 1))
    places = [position_of(kind, half, block_rows) for kind, half in origins]
    project(attention_scr, heads_ref, table_refs, places, joined_ref, first)
    hide(feedforward_scr, upward_ref, hidden_scr, 0)
    rows = CORES * block_rows
    attended = attend(joined_ref, offsets_ref, tokens - rows, rows, block_rows)
    chunk = 512
    for begin in range(0, downward_ref.shape[1], chunk):
        columns = slice(begin, begin + chunk)
        fed = jnp.dot(hidden_scr[...], downward_ref[:, columns], preferred_element_type=jnp.float32)
        fed_ref[:, columns] = fed[:block_rows]
        partial = fed[block_rows:] + jnp.dot(
            attended, output_ref[:, columns], preferred_element_type=jnp.float32
        )
        own_ref[:, columns] = partial[:block_rows]
        sibling_ref[:, columns] = partial[block_rows:].astype(jnp.bfloat16)


def last_rows(blocks, gains, weights, tables, own_joined, middle_joined):
    block_rows, width = blocks[0].shape
    rows = len(blocks) * block_rows
    hidden_width = weights[1].shape[1]
    tokens = CHIPS * CORES * block_rows
    return pl.pallas_call(
        last_kernel,
        out_shape=[
            pltpu.VMEM((tokens, 3 * HD), jnp.bfloat16),
            pltpu.VMEM((block_rows, width), jnp.float32),
            pltpu.VMEM((block_rows, width), jnp.bfloat16),
            pltpu.VMEM((block_rows, width), jnp.float32),
        ],
        in_specs=vmem_specs(len(blocks) + 2 + 4 + 4 + 2),
        out_specs=vmem_specs(4),
        scratch_shapes=[
            pltpu.VMEM((rows, width), jnp.bfloat16),
            pltpu.VMEM((rows, width), jnp.bfloat16),
            pltpu.VMEM((rows, hidden_width), jnp.bfloat16),
        ],
        compiler_params=parameters(12),
        cost_estimate=pl.CostEstimate(
            flops=2 * rows * width * (3 * HD + HD + 2 * hidden_width),
            bytes_accessed=MIB,
            transcendentals=rows * hidden_width,
        ),
        name="last_rows",
    )(*blocks, *gains, *weights, *tables, own_joined, middle_joined)


def fed_kernel(own_hidden_ref, middle_hidden_ref, downward_ref, fed_ref):
    hidden = jnp.concatenate([own_hidden_ref[...], middle_hidden_ref[...]], 0)
    chunk = 512
    for begin in range(0, downward_ref.shape[1], chunk):
        columns = slice(begin, begin + chunk)
        fed_ref[:, columns] = jnp.dot(
            hidden, downward_ref[:, columns], preferred_element_type=jnp.float32
        )


def fed_rows(own_hidden, middle_hidden, downward_weight):
    rows = own_hidden.shape[0] + middle_hidden.shape[0]
    depth, width = downward_weight.shape
    return pl.pallas_call(
        fed_kernel,
        out_shape=pltpu.VMEM((rows, width), jnp.float32),
        in_specs=vmem_specs(3),
        out_specs=pl.BlockSpec(memory_space=pltpu.VMEM),
        compiler_params=parameters(12),
        cost_estimate=pl.CostEstimate(
            flops=2 * rows * depth * width, bytes_accessed=MIB, transcendentals=0
        ),
        name="fed_rows",
    )(own_hidden, middle_hidden, downward_weight)


def rest_kernel(joined_ref, offsets_ref, output_ref, fed_ref, fed_beside_ref, *refs):
    count = len(refs) // 2
    siblings, owns = refs[:count], refs[count:]
    block_rows = owns[0].shape[0]
    rows = fed_ref.shape[0] + fed_beside_ref.shape[0]
    attended = attend(joined_ref, offsets_ref, 0, rows, block_rows)
    chunk = 512
    for begin in range(0, output_ref.shape[1], chunk):
        columns = slice(begin, begin + chunk)
        fed = jnp.concatenate([fed_ref[:, columns], fed_beside_ref[:, columns]], 0)
        partial = fed + jnp.dot(
            attended, output_ref[:, columns], preferred_element_type=jnp.float32
        )
        for number, (sibling_ref, own_ref) in enumerate(zip(siblings, owns)):
            first = CORES * number * block_rows
            middle = first + block_rows
            own_ref[:, columns] = partial[first:middle]
            sibling_ref[:, columns] = partial[middle : middle + block_rows].astype(jnp.bfloat16)


def rest_rows(joined, offsets, output_weight, fed, fed_beside):
    width = fed.shape[1]
    rows = fed.shape[0] + fed_beside.shape[0]
    count = CHIPS - 1
    shape = (rows // (CORES * count), width)
    shapes = [pltpu.VMEM(shape, dtype) for dtype in [jnp.bfloat16] * count + [jnp.float32] * count]
    return pl.pallas_call(
        rest_kernel,
        out_shape=shapes,
        in_specs=vmem_specs(5),
        out_specs=vmem_specs(2 * count),
        compiler_params=parameters(12),
        cost_estimate=pl.CostEstimate(
            flops=2 * rows * width * HD,
            bytes_accessed=MIB,
            transcendentals=rows * joined.shape[0],
        ),
        name="rest_rows",
    )(joined, offsets, output_weight, fed, fed_beside)


def pages_kernel(joined_ref, destinations_ref, *page_refs):
    tokens = joined_ref.shape[0]
    slot_rows = page_refs[0].shape[0] * PAGE
    for number, page_ref in enumerate(page_refs):
        shape = (slot_rows, tokens)
        row = number * slot_rows + lax.broadcasted_iota(jnp.int32, shape, 0)
        placing = jnp.where(row == destinations_ref[...], 1.0, 0.0).astype(jnp.bfloat16)
        rows = jnp.dot(placing, joined_ref[:, HD:], preferred_element_type=jnp.float32)
        page_ref[...] = rows.astype(jnp.bfloat16).reshape(page_ref.shape)


def cached_pages(joined, destinations, replica_count):
    tokens = joined.shape[0]
    capacity = 2 * (tokens // PAGE) // replica_count
    shapes = [pltpu.VMEM((capacity, PAGE, 2 * HD), jnp.bfloat16)] * replica_count
    return pl.pallas_call(
        pages_kernel,
        out_shape=shapes,
        in_specs=vmem_specs(2),
        out_specs=vmem_specs(len(shapes)),
        compiler_params=parameters(8),
        cost_estimate=pl.CostEstimate(flops=0, bytes_accessed=MIB, transcendentals=0),
        name="cached_pages",
    )(joined, destinations)


def add_kernel(*refs):
    total = refs[0][...].astype(jnp.float32)
    for ref in refs[1:-1]:
        total = total + ref[...].astype(jnp.float32)
    refs[-1][...] = total.astype(refs[-1].dtype)


def added(name, *parts):
    return pl.pallas_call(
        add_kernel,
        out_shape=pltpu.VMEM(parts[0].shape, jnp.bfloat16),
        in_specs=vmem_specs(len(parts)),
        out_specs=pl.BlockSpec(memory_space=pltpu.VMEM),
        compiler_params=parameters(4),
        name=name,
    )(*parts)


def sums_kernel(passing_ref, *refs):
    zeros, ones, twos = refs[0:2], refs[2:4], refs[4:6]
    hidden_ref, second_ref, first_ref, base_ref = refs[6:]

    def total(pair, extra=None):
        received_ref, own_ref = pair
        value = own_ref[...] + received_ref[...].astype(jnp.float32)
        return value if extra is None else value + extra[...].astype(jnp.float32)

    second_ref[...] = total(twos, passing_ref).astype(jnp.bfloat16)
    first_ref[...] = total(ones).astype(jnp.bfloat16)
    base_ref[...] = total(zeros, hidden_ref)


def remaining_sums(passing, pairs, hidden):
    shape = hidden.shape
    return pl.pallas_call(
        sums_kernel,
        out_shape=[
            pltpu.VMEM(shape, jnp.bfloat16),
            pltpu.VMEM(shape, jnp.bfloat16),
            pltpu.VMEM(shape, jnp.float32),
        ],
        in_specs=vmem_specs(8),
        out_specs=vmem_specs(3),
        compiler_params=parameters(4),
        name="remaining_sums",
    )(passing, *[array for pair in pairs for array in pair], hidden)


def place_kernel(masks, *refs):
    group = lax.axis_index("dp")
    pages, (cache_ref, sems) = refs[:-2], refs[-2:]
    copies = [
        pltpu.make_async_copy(page_ref, cache_ref.at[0, group ^ mask], sems.at[number])
        for number, (mask, page_ref) in enumerate(zip(masks, pages))
    ]
    for copy in copies:
        copy.start()
    for copy in copies:
        copy.wait()


def placed(masks, pages, replica_count):
    count = len(pages)
    return pl.pallas_call(
        functools.partial(place_kernel, masks),
        out_shape=jax.ShapeDtypeStruct((1, replica_count) + pages[0].shape, pages[0].dtype),
        in_specs=[pl.BlockSpec(memory_space=pl.ANY)] * count,
        out_specs=pl.BlockSpec(memory_space=pltpu.HBM),
        scratch_shapes=[pltpu.SemaphoreType.DMA((count,))],
        compiler_params=parameters(4),
        name="placed",
    )(*pages)


def finish_kernel(masks, base_ref, *refs):
    count = len(masks)
    *parts, _, output_ref, cache_ref, total_scr, sems = refs
    parts, pages = parts[:-count], parts[-count:]
    group = lax.axis_index("dp")
    copies = [
        pltpu.make_async_copy(page_ref, cache_ref.at[0, group ^ mask], sems.at[number])
        for number, (mask, page_ref) in enumerate(zip(masks, pages))
    ]
    for copy in copies:
        copy.start()
    total = base_ref[...]
    for part_ref in parts:
        total = total + part_ref[...].astype(jnp.float32)
    total_scr[...] = total
    copies.append(pltpu.make_async_copy(total_scr, output_ref, sems.at[count]))
    copies[-1].start()
    for copy in copies:
        copy.wait()


def finished(base, parts, masks, pages, cache):
    count = len(pages)
    return pl.pallas_call(
        functools.partial(finish_kernel, masks),
        out_shape=[
            jax.ShapeDtypeStruct(base.shape, base.dtype),
            jax.ShapeDtypeStruct(cache.shape, cache.dtype),
        ],
        in_specs=vmem_specs(1 + len(parts))
        + [pl.BlockSpec(memory_space=pl.ANY)] * count
        + [pl.BlockSpec(memory_space=pltpu.HBM)],
        out_specs=[pl.BlockSpec(memory_space=pltpu.HBM)] * 2,
        scratch_shapes=[
            pltpu.VMEM(base.shape, base.dtype),
            pltpu.SemaphoreType.DMA((count + 1,)),
        ],
        input_output_aliases={1 + len(parts) + count: 1},
        compiler_params=parameters(4),
        name="finished",
    )(base, *parts, *pages, cache)


def shards_whole_heads(
    hidden_states,
    attention_gain,
    feedforward_gain,
    heads_weight,
    output_weight,
    upward_weight,
    downward_weight,
    segments,
    page_targets,
):
    replica_count = lax.axis_size("dp")
    to_chip = [mask * CORES for mask in range(CHIPS)]
    second = exchanged(hidden_states, "tensor", to_chip[2])
    first = exchanged(hidden_states, "tensor", to_chip[1])
    beside = exchanged(hidden_states, "tensor", 1)
    staged = (
        segments,
        page_targets.reshape(1, -1),
        hidden_states,
        attention_gain[None],
        feedforward_gain[None],
        heads_weight,
        upward_weight,
        downward_weight,
    )
    staged = own_rows(staged, replica_count)
    hidden, gains, weights, tables = staged[2], staged[3:5], staged[5:8], staged[8:12]
    heads, upward, downward = weights
    destinations, own_joined, own_hidden = staged[12:]

    first, own_joined = lax.optimization_barrier((first, own_joined))
    first_beside = exchanged(first, "tensor", 1)
    second, first_beside, beside = lax.optimization_barrier((second, first_beside, beside))
    third = exchanged(second, "tensor", to_chip[1])
    middle_joined, middle_hidden, output = middle_rows(
        "middle_rows",
        ((0, 1), (1, 0), (1, 1), (2, 0)),
        (beside, first, first_beside, second),
        gains,
        (heads, upward),
        tables[1:],
        output_weight,
    )
    second, middle_joined = lax.optimization_barrier((second, middle_joined))
    second_beside = exchanged(second, "tensor", 1)
    third, second_beside, middle_joined, middle_hidden = lax.optimization_barrier(
        (third, second_beside, middle_joined, middle_hidden)
    )
    third_beside = exchanged(third, "tensor", 1)
    fed = fed_rows(own_hidden, middle_hidden, downward)
    third_beside, fed = lax.optimization_barrier((third_beside, fed))
    joined, fed_beside, sibling, own = last_rows(
        (second_beside, third, third_beside),
        gains,
        (heads, upward, downward, output),
        tables,
        own_joined,
        middle_joined,
    )

    received = exchanged(sibling, "tensor", 1)
    partials = rest_rows(joined, tables[0], output, fed, fed_beside)
    siblings, owns = partials[: CHIPS - 1], partials[CHIPS - 1 :]
    third_sum = added("third_added", own, received)
    third_sum, siblings, joined = lax.optimization_barrier((third_sum, siblings, joined))
    passing = exchanged(third_sum, "tensor", to_chip[1])
    pairs = [(exchanged(sibling, "tensor", 1), own) for sibling, own in zip(siblings, owns)]
    pages = cached_pages(joined, destinations, replica_count)
    early, late = (3,), (1, 2)
    arriving = [exchanged(pages[mask], "dp", mask) for mask in early]
    second_sum, first_sum, base = remaining_sums(passing, pairs, hidden)
    from_second = exchanged(second_sum, "tensor", to_chip[2])
    from_first = exchanged(first_sum, "tensor", to_chip[1])
    base, late_pages = lax.optimization_barrier((base, [pages[mask] for mask in late]))
    late_pages = [exchanged(page, "dp", mask) for mask, page in zip(late, late_pages)]
    cache_pages = placed((0,) + early, [pages[0]] + arriving, replica_count)
    return tuple(finished(base, (from_second, from_first), late, late_pages, cache_pages))


def solution(mesh):
    whole_heads = mesh.shape["tensor"] == H and mesh.shape["dp"] == 4
    shards = shards_whole_heads if whole_heads else shards_split_heads
    in_specs = (
        P(("dp", "tensor"), None),
        P(),
        P(),
        P(None, "tensor"),
        P("tensor", None),
        P(None, "tensor"),
        P("tensor", None),
        P("dp", None),
        P("dp", None),
    )
    out_specs = (P(("dp", "tensor"), None), P("dp", None, None, None, "tensor"))
    return jax.shard_map(shards, mesh=mesh, in_specs=in_specs, out_specs=out_specs, check_vma=False)
```

```python
import functools
import math

import jax
import jax.numpy as jnp
from jax import lax
from jax.experimental import pallas as pl
from jax.experimental.pallas import tpu as pltpu
from jax.sharding import PartitionSpec as P

H = 8
HD = 256
ROT = 64
PAGE = 16


epsilon = 1e-05
rotary_base = 10000.0
key_block = 256


def shortened(array):

    def short(part):
        return part.astype(jnp.bfloat16) if part.dtype == jnp.float32 else part

    return jax.tree.map(short, array)


def swapped(block, axis, apart):
    count = lax.axis_size(axis)
    route = []
    for low in range(count):
        high = low | 1 << apart
        if high != low and high < count:
            route += [(low, high), (high, low)]
    return lax.ppermute(block, axis, route)


def layer_norm(values, gain):
    floats = values.astype(jnp.float32)
    center = jnp.mean(floats, axis=-1, keepdims=True)
    shifted = floats - center
    spread = jnp.mean(shifted * shifted, axis=-1, keepdims=True)
    return (shifted * lax.rsqrt(spread + epsilon) * gain).astype(jnp.bfloat16)


def positions_of(stream):
    indices = jnp.arange(stream.shape[0], dtype=jnp.int32)
    boundary = jnp.concatenate([jnp.ones((1,), dtype=bool), stream[1:] != stream[:-1]])
    starting = lax.cummax(jnp.where(boundary, indices, jnp.zeros_like(indices)), axis=0)
    return (indices, starting)


def rotate_heads(vectors, offsets, rotary_dims):
    half_dims = rotary_dims // 2
    frequency = jnp.exp(
        jnp.arange(half_dims, dtype=jnp.float32) * (-2.0 * math.log(rotary_base) / rotary_dims)
    )
    angles = offsets.astype(jnp.float32)[:, None] * frequency[None, :]
    cosine = jnp.cos(angles)
    sine = jnp.sin(angles)
    floats = vectors.astype(jnp.float32)
    leading = floats[..., :half_dims]
    trailing = floats[..., half_dims:rotary_dims]
    rotated = jnp.concatenate(
        [
            leading * cosine - trailing * sine,
            trailing * cosine + leading * sine,
            floats[..., rotary_dims:],
        ],
        axis=-1,
    )
    return rotated.astype(jnp.bfloat16)


def shards_split_heads(
    hidden_states,
    attention_gain,
    feedforward_gain,
    heads_weight,
    output_weight,
    upward_weight,
    downward_weight,
    segments,
    page_targets,
):
    tensor_count = lax.axis_size("tensor")
    replica_count = lax.axis_size("dp")
    tensor_index = lax.axis_index("tensor")
    quarters = tensor_count // H
    quarter_width = HD // quarters
    quarter_index = tensor_index % quarters
    stream = segments[0]
    tokens_total = stream.shape[0]
    level_count = quarters.bit_length() - 1
    normed_attention = layer_norm(hidden_states, attention_gain)
    normed_feedforward = layer_norm(hidden_states, feedforward_gain)
    shard_rows = lax.all_gather(
        (normed_attention, normed_feedforward), "tensor", axis=0, tiled=True
    )
    joined_rows = jnp.dot(shard_rows[0], heads_weight, preferred_element_type=jnp.float32).astype(
        jnp.bfloat16
    )
    upward = jnp.dot(shard_rows[1], upward_weight, preferred_element_type=jnp.float32)
    hidden_rows = jax.nn.gelu(upward, approximate=False).astype(jnp.bfloat16)
    hidden = hidden_rows
    pieces = (
        joined_rows.reshape(tokens_total, 3, quarter_width)
        .transpose(1, 0, 2)
        .reshape(1, 3, tokens_total * quarter_width)
    )
    for bit_number in range(level_count):
        partner = swapped(shortened(pieces), "tensor", bit_number).astype(pieces.dtype)
        lower = tensor_index >> bit_number & 1 == 0
        pieces = jnp.where(
            lower, jnp.concatenate([pieces, partner], 0), jnp.concatenate([partner, pieces], 0)
        )
    whole_head = (
        pieces.reshape(quarters, 3, tokens_total, quarter_width)
        .transpose(1, 2, 0, 3)
        .reshape(3, tokens_total, HD)
    )
    indices, starting = positions_of(stream)
    offsets = indices - starting
    queries = rotate_heads(whole_head[0], offsets, ROT)
    keys = rotate_heads(whole_head[1], offsets, ROT)
    values = whole_head[2]
    block_rows = tokens_total // (2 * quarters)
    score_scale = HD ** (-0.5)

    def attend_block(block_number):
        first_row = block_number * block_rows
        block_queries = lax.dynamic_slice_in_dim(queries, first_row, block_rows, 0)
        query_segments = lax.dynamic_slice_in_dim(stream, first_row, block_rows, 0)
        query_indices = first_row + jnp.arange(block_rows, dtype=jnp.int32)
        lowest = lax.dynamic_index_in_dim(starting, first_row, 0, keepdims=False) // key_block
        highest = (first_row + block_rows + key_block - 1) // key_block

        def scores_of(key_number):
            key_first = key_number * key_block
            key_indices = key_first + jnp.arange(key_block, dtype=jnp.int32)
            scores = (
                jnp.dot(block_queries, keys.T, preferred_element_type=jnp.float32) * score_scale
            )
            allowed = (stream[None, :] == query_segments[:, None]) & (
                key_indices[None, :] <= query_indices[:, None]
            )
            return (scores, allowed)

        def find_peak(key_number, peak):
            scores, allowed = scores_of(key_number)
            return jnp.maximum(peak, jnp.max(jnp.where(allowed, scores, -jnp.inf), axis=1))

        peak = lax.fori_loop(
            lowest, highest, find_peak, jnp.full((block_rows,), -jnp.inf, jnp.float32)
        )

        def accumulate(key_number, state):
            weight_sum, mixed_sum = state
            scores, allowed = scores_of(key_number)
            weights = jnp.where(allowed, jnp.exp(scores - peak[:, None]), 0.0)
            mixed_next = mixed_sum + jnp.dot(
                weights.astype(jnp.bfloat16), values, preferred_element_type=jnp.float32
            )
            return (weight_sum + jnp.sum(weights, axis=1), mixed_next)

        start_state = (
            jnp.zeros((block_rows,), jnp.float32),
            jnp.zeros((block_rows, HD), jnp.float32),
        )
        weight_sum, mixed_sum = lax.fori_loop(lowest, highest, accumulate, start_state)
        return (mixed_sum / weight_sum[:, None]).astype(jnp.bfloat16)

    own_blocks = (2 * quarter_index, 2 * quarter_index + 1)
    own_rows = jnp.concatenate([attend_block(own_blocks[0]), attend_block(own_blocks[1])], 0)[None]
    for bit_number in range(level_count):
        partner = swapped(own_rows, "tensor", bit_number)
        lower = tensor_index >> bit_number & 1 == 0
        own_rows = jnp.where(
            lower, jnp.concatenate([own_rows, partner], 0), jnp.concatenate([partner, own_rows], 0)
        )
    attended = own_rows.reshape(tokens_total, HD)
    attended_quarter = lax.dynamic_slice_in_dim(
        attended, quarter_index * quarter_width, quarter_width, 1
    )
    hidden_rows = hidden
    summed = lax.psum_scatter(
        (
            jnp.dot(attended_quarter, output_weight, preferred_element_type=jnp.float32)
            + jnp.dot(hidden_rows, downward_weight, preferred_element_type=jnp.float32)
        ).astype(jnp.bfloat16),
        "tensor",
        scatter_dimension=0,
        tiled=True,
    ).astype(jnp.float32)
    layer_output = hidden_states.astype(jnp.float32) + summed
    key_quarter = lax.dynamic_slice_in_dim(keys, quarter_index * quarter_width, quarter_width, 1)
    value_quarter = joined_rows[:, 2 * quarter_width :]
    page_count = tokens_total // PAGE
    page_rows = jnp.concatenate([key_quarter, value_quarter], 1).reshape(
        page_count, PAGE * 2 * quarter_width
    )
    targets = page_targets[:, 0]
    page_numbers = jnp.arange(page_count, dtype=jnp.int32)
    earlier = jnp.sum(
        (
            (targets[None, :] == targets[:, None]) & (page_numbers[None, :] < page_numbers[:, None])
        ).astype(jnp.int32),
        axis=1,
    )
    capacity = 2 * page_count // replica_count
    slot_numbers = targets * capacity + earlier
    placing = (
        jnp.arange(replica_count * capacity, dtype=jnp.int32)[:, None] == slot_numbers[None, :]
    ).astype(jnp.bfloat16)
    outgoing = jnp.dot(placing, page_rows, preferred_element_type=jnp.float32).astype(jnp.bfloat16)
    outgoing = outgoing.reshape(replica_count, capacity, PAGE * 2 * quarter_width)
    incoming = lax.all_to_all(outgoing, "dp", split_axis=0, concat_axis=0, tiled=True)
    cache_pages = incoming.reshape(1, replica_count, capacity, PAGE, 2 * quarter_width)
    return (layer_output, cache_pages)


CORES = 2
CHIPS = 4
MIB = 1 << 20


def in_hbm(array):
    return pltpu.with_memory_space_constraint(array, pltpu.HBM)


def exchanged(block, axis, mask):
    count = lax.axis_size(axis)
    return lax.ppermute(block, axis, [(member, member ^ mask) for member in range(count)])


def exchanged_by(core, block, axis, mask):
    count = lax.axis_size(axis)
    members = [member for member in range(count) if member % CORES == core]
    return lax.ppermute(block, axis, [(member, member ^ mask) for member in members])


def vmem_specs(count):
    return [pl.BlockSpec(memory_space=pltpu.VMEM)] * count


def parameters(mebibytes):
    return pltpu.CompilerParams(vmem_limit_bytes=mebibytes * MIB)


def whereabouts():
    member = lax.axis_index("tensor")
    return member // CORES, member % CORES


def position_of(kind, half, block_rows):
    chip, core = whereabouts()
    return ((chip ^ kind) * CORES + (core ^ half)) * block_rows


def positions_along(first, shape, axis, block_rows):
    chip, core = whereabouts()
    bits = block_rows.bit_length() - 1
    place = first + lax.broadcasted_iota(jnp.int32, shape, axis)
    kind = place >> (bits + 1)
    half = (place >> bits) & 1
    return ((((chip ^ kind) << 1) | (core ^ half)) << bits) | (place & (block_rows - 1))


def normalize(blocks, gain_refs, normed_refs):
    piece = 16
    gains = [gain_ref[...] for gain_ref in gain_refs]
    for number, block_ref in enumerate(blocks):
        block_rows = block_ref.shape[0]
        for part in range(0, block_rows, piece):
            floats = block_ref[part : part + piece, :].astype(jnp.float32)
            center = jnp.mean(floats, axis=-1, keepdims=True)
            shifted = floats - center
            spread = jnp.mean(shifted * shifted, axis=-1, keepdims=True)
            scaled = shifted * lax.rsqrt(spread + epsilon)
            first = number * block_rows + part
            for gain, normed_ref in zip(gains, normed_refs):
                normed_ref[first : first + piece, :] = (scaled * gain).astype(jnp.bfloat16)


def project(normed_ref, heads_ref, table_refs, places, joined_ref, first):
    rows = normed_ref.shape[0]
    block_rows = rows // len(places)
    for component in range(3):
        columns = slice(component * HD, (component + 1) * HD)
        joined = jnp.dot(
            normed_ref[...], heads_ref[:, columns], preferred_element_type=jnp.float32
        ).astype(jnp.bfloat16)
        joined_ref[first : first + rows, columns] = joined
        if component < 2:
            cosine, sine_down, sine_up = [
                jnp.concatenate(
                    [
                        table_ref[pl.ds(pl.multiple_of(place, block_rows), block_rows), :]
                        for place in places
                    ],
                    0,
                )
                for table_ref in table_refs
            ]
            turning = joined[:, :128].astype(jnp.float32)
            turned = (
                turning * cosine
                + pltpu.roll(turning, 128 - ROT // 2, 1) * sine_down
                + pltpu.roll(turning, ROT // 2, 1) * sine_up
            )
            joined_ref[first : first + rows, component * HD : component * HD + 128] = turned.astype(
                jnp.bfloat16
            )


def hide(normed_ref, upward_ref, hidden_ref, place):
    chunk = 256
    rows = slice(place, place + normed_ref.shape[0])
    for first in range(0, upward_ref.shape[1], chunk):
        columns = slice(first, first + chunk)
        upward = jnp.dot(
            normed_ref[...], upward_ref[:, columns], preferred_element_type=jnp.float32
        )
        hidden = 0.5 * upward * (1.0 + lax.erf(upward * (0.5**0.5)))
        hidden_ref[rows, columns] = hidden.astype(jnp.bfloat16)


def attend(joined_ref, offsets_ref, first, rows, block_rows):
    tokens = joined_ref.shape[0]
    starts = [
        position_of(place // (2 * block_rows), (place // block_rows) % 2, block_rows)
        for place in range(first, first + rows, block_rows)
    ]
    reach = jnp.concatenate(
        [
            offsets_ref[pl.ds(pl.multiple_of(start, block_rows), block_rows), :]
            for start in starts
        ],
        0,
    )[:, :1].astype(jnp.int32)
    row = positions_along(first, (rows, 1), 0, block_rows)
    column = positions_along(0, (1, tokens), 1, block_rows)
    allowed = (column <= row) & (column >= row - reach)
    scores = lax.dot_general(
        joined_ref[first : first + rows, :HD],
        joined_ref[:, HD : 2 * HD],
        (((1,), (1,)), ((), ())),
        preferred_element_type=jnp.float32,
    ) * (HD ** (-0.5))
    peak = jnp.max(jnp.where(allowed, scores, -jnp.inf), axis=1, keepdims=True)
    weights = jnp.where(allowed, jnp.exp(scores - peak), 0.0)
    weight_sum = jnp.sum(weights, axis=1, keepdims=True)
    mixed = jnp.dot(
        weights.astype(jnp.bfloat16), joined_ref[:, 2 * HD :], preferred_element_type=jnp.float32
    )
    return (mixed / weight_sum).astype(jnp.bfloat16)


def make_tables(segments_ref, offsets_ref, cosine_ref, sine_down_ref, sine_up_ref):
    tokens = segments_ref.shape[1]
    shape = (tokens, tokens)
    rows = lax.broadcasted_iota(jnp.int32, shape, 0)
    columns = lax.broadcasted_iota(jnp.int32, shape, 1)
    across = jnp.broadcast_to(segments_ref[...], shape).astype(jnp.float32)
    down = jnp.sum(jnp.where(rows == columns, across, 0.0), axis=1, keepdims=True)
    earlier = (across == down) & (columns < rows)
    offsets = jnp.sum(jnp.where(earlier, 1.0, 0.0), axis=1, keepdims=True)
    offsets_ref[...] = jnp.broadcast_to(offsets, offsets_ref.shape)
    half = ROT // 2
    lane = lax.broadcasted_iota(jnp.int32, (tokens, 128), 1)
    step = (lane & (half - 1)).astype(jnp.float32)
    frequency = jnp.exp(step * (-2.0 * math.log(rotary_base) / ROT))
    angles = offsets * frequency
    sine = jnp.sin(angles)
    cosine_ref[...] = jnp.where(lane < ROT, jnp.cos(angles), 1.0)
    sine_down_ref[...] = jnp.where(lane < half, -sine, 0.0)
    sine_up_ref[...] = jnp.where((lane >= half) & (lane < ROT), sine, 0.0)


def make_destinations(targets_ref, destinations_ref, replica_count, block_rows):
    page_count = targets_ref.shape[1]
    tokens = destinations_ref.shape[1]
    capacity = 2 * page_count // replica_count
    square = (page_count, page_count)
    rows = lax.broadcasted_iota(jnp.int32, square, 0)
    columns = lax.broadcasted_iota(jnp.int32, square, 1)
    across = jnp.broadcast_to(targets_ref[...], square).astype(jnp.float32)
    down = jnp.sum(jnp.where(rows == columns, across, 0.0), axis=1, keepdims=True)
    earlier = jnp.where((across == down) & (columns < rows), 1.0, 0.0)
    slots = jnp.sum(earlier, axis=1, keepdims=True).astype(jnp.int32)
    slots = (down.astype(jnp.int32) ^ lax.axis_index("dp")) * capacity + slots
    positions = positions_along(0, (1, tokens), 1, block_rows)
    bits = PAGE.bit_length() - 1
    pages = lax.broadcasted_iota(jnp.int32, (page_count, tokens), 0)
    chosen = jnp.where(pages == positions >> bits, slots.astype(jnp.float32), 0.0)
    slot = jnp.sum(chosen, axis=0, keepdims=True).astype(jnp.int32)
    destinations_ref[...] = slot * PAGE + (positions & (PAGE - 1))


def copies_in(sources, targets, sems):
    copies = []
    for number, (source, target) in enumerate(zip(sources, targets)):
        parts = 4 if source.shape[0] >= 256 else 1
        rows = source.shape[0] // parts
        places = [pl.ds(part * rows, rows) for part in range(parts)]
        copies.append(
            [
                pltpu.make_async_copy(source.at[place], target.at[place], sems.at[number, part])
                for part, place in enumerate(places)
            ]
        )
    for copy in sum(copies, []):
        copy.start()
    return copies


def wait_for(copies):
    for copy in copies:
        copy.wait()


def own_kernel(count, replica_count, *refs):
    sources, targets = refs[:count], refs[count : 2 * count]
    offsets_ref, *table_refs, destinations_ref, joined_ref, feedforward_ref = refs[2 * count : -2]
    attention_scr, sems = refs[-2:]
    copies = copies_in(sources, targets, sems)
    segments_ref, targets_ref, states_ref, *gain_refs, heads_ref = targets
    block_rows = states_ref.shape[0]
    wait_for(copies[0])
    make_tables(segments_ref, offsets_ref, *table_refs)
    wait_for(copies[1])
    make_destinations(targets_ref, destinations_ref, replica_count, block_rows)
    for number in (2, 3, 4):
        wait_for(copies[number])
    normalize([states_ref], gain_refs, [attention_scr, feedforward_ref])
    wait_for(copies[5])
    places = [position_of(0, 0, block_rows)]
    project(attention_scr, heads_ref, table_refs, places, joined_ref, 0)


def own_rows(staged, replica_count):
    tokens = staged[0].shape[1]
    rows, width = staged[2].shape
    shapes = [pltpu.VMEM(array.shape, array.dtype) for array in staged]
    shapes += [pltpu.VMEM((tokens, 128), jnp.float32)] * 4
    shapes += [
        pltpu.VMEM((1, tokens), jnp.int32),
        pltpu.VMEM((rows, 3 * HD), jnp.bfloat16),
        pltpu.VMEM((rows, width), jnp.bfloat16),
    ]
    count = len(staged)
    return pl.pallas_call(
        functools.partial(own_kernel, count, replica_count),
        out_shape=shapes,
        in_specs=[pl.BlockSpec(memory_space=pltpu.HBM)] * count,
        out_specs=vmem_specs(len(shapes)),
        scratch_shapes=[
            pltpu.VMEM((rows, width), jnp.bfloat16),
            pltpu.SemaphoreType.DMA((count, 4)),
        ],
        compiler_params=parameters(12),
        cost_estimate=pl.CostEstimate(
            flops=2 * rows * width * 3 * HD,
            bytes_accessed=sum(array.nbytes for array in staged),
            transcendentals=0,
        ),
        name="own_rows",
    )(*[in_hbm(array) for array in staged])


def units_kernel(feedforward_ref, *refs):
    sources, targets, hidden_ref, sems = refs[:2], refs[2:4], refs[4], refs[5]
    copies = copies_in(sources, targets, sems)
    wait_for(copies[0])
    hide(feedforward_ref, targets[0], hidden_ref, 0)
    wait_for(copies[1])


def own_units(normed, upward_weight, downward_weight):
    rows = normed.shape[0]
    staged = (upward_weight, downward_weight)
    hidden_width = upward_weight.shape[1]
    return pl.pallas_call(
        units_kernel,
        out_shape=[pltpu.VMEM(array.shape, array.dtype) for array in staged]
        + [pltpu.VMEM((rows, hidden_width), jnp.bfloat16)],
        in_specs=vmem_specs(1) + [pl.BlockSpec(memory_space=pltpu.HBM)] * 2,
        out_specs=vmem_specs(3),
        scratch_shapes=[pltpu.SemaphoreType.DMA((2, 4))],
        compiler_params=parameters(12),
        cost_estimate=pl.CostEstimate(
            flops=0, bytes_accessed=MIB, transcendentals=rows * hidden_width
        ),
        name="own_units",
    )(normed, *[in_hbm(array) for array in staged])


def middle_kernel(origins, *refs):
    count = len(origins)
    blocks, refs = refs[: count + 1], refs[count + 1 :]
    gain_a, gain_f, heads_ref, upward_ref, *table_refs, source_ref = refs[:8]
    joined_ref, hidden_ref, second_ref, target_ref = refs[8:12]
    attention_scr, feedforward_scr, sems = refs[12:]
    copies = copies_in([source_ref], [target_ref], sems)
    block_rows = blocks[0].shape[0]
    second_ref[...] = blocks[-2][...] + blocks[-1][...]
    blocks = (*blocks[:-2], second_ref)
    normalize(blocks, [gain_a, gain_f], [attention_scr, feedforward_scr])
    places = [position_of(kind, half, block_rows) for kind, half in origins]
    project(attention_scr, heads_ref, table_refs, places, joined_ref, 0)
    hide(feedforward_scr, upward_ref, hidden_ref, 0)
    wait_for(sum(copies, []))


def middle_rows(origins, blocks, gains, weights, tables, staged):
    block_rows, width = blocks[0].shape
    rows = len(origins) * block_rows
    hidden_width = weights[1].shape[1]
    return pl.pallas_call(
        functools.partial(middle_kernel, origins),
        out_shape=[
            pltpu.VMEM((rows, 3 * HD), jnp.bfloat16),
            pltpu.VMEM((rows, hidden_width), jnp.bfloat16),
            pltpu.VMEM((block_rows, width), jnp.bfloat16),
            pltpu.VMEM(staged.shape, staged.dtype),
        ],
        in_specs=vmem_specs(len(blocks) + 2 + 2 + 3) + [pl.BlockSpec(memory_space=pltpu.HBM)],
        out_specs=vmem_specs(4),
        scratch_shapes=[
            pltpu.VMEM((rows, width), jnp.bfloat16),
            pltpu.VMEM((rows, width), jnp.bfloat16),
            pltpu.SemaphoreType.DMA((1, 4)),
        ],
        compiler_params=parameters(12),
        cost_estimate=pl.CostEstimate(
            flops=2 * rows * width * (3 * HD + hidden_width),
            bytes_accessed=MIB,
            transcendentals=rows * hidden_width,
        ),
        name="middle_rows",
    )(*blocks, *gains, *weights, *tables, in_hbm(staged))


def last_kernel(*refs):
    blocks, (gain_a, gain_f, heads_ref, upward_ref, downward_ref, output_ref) = refs[:3], refs[3:9]
    offsets_ref, *table_refs = refs[9:13]
    own_joined_ref, middle_joined_ref = refs[13:15]
    joined_ref, fed_ref, sibling_ref, own_ref = refs[15:19]
    attention_scr, feedforward_scr, hidden_scr = refs[19:]
    block_rows = blocks[0].shape[0]
    tokens = joined_ref.shape[0]
    first = tokens - len(blocks) * block_rows
    normalize(blocks, [gain_a, gain_f], [attention_scr, feedforward_scr])
    joined_ref[:block_rows, :] = own_joined_ref[...]
    joined_ref[block_rows:first, :] = middle_joined_ref[...]
    origins = ((CHIPS - 2, 1), (CHIPS - 1, 0), (CHIPS - 1, 1))
    places = [position_of(kind, half, block_rows) for kind, half in origins]
    project(attention_scr, heads_ref, table_refs, places, joined_ref, first)
    hide(feedforward_scr, upward_ref, hidden_scr, 0)
    rows = CORES * block_rows
    attended = attend(joined_ref, offsets_ref, tokens - rows, rows, block_rows)
    chunk = 512
    for begin in range(0, downward_ref.shape[1], chunk):
        columns = slice(begin, begin + chunk)
        fed = jnp.dot(hidden_scr[...], downward_ref[:, columns], preferred_element_type=jnp.float32)
        fed_ref[:, columns] = fed[:block_rows]
        partial = fed[block_rows:] + jnp.dot(
            attended, output_ref[:, columns], preferred_element_type=jnp.float32
        )
        own_ref[:, columns] = partial[:block_rows]
        sibling_ref[:, columns] = partial[block_rows:].astype(jnp.bfloat16)


def last_rows(blocks, gains, weights, tables, own_joined, middle_joined):
    block_rows, width = blocks[0].shape
    rows = len(blocks) * block_rows
    hidden_width = weights[1].shape[1]
    tokens = CHIPS * CORES * block_rows
    return pl.pallas_call(
        last_kernel,
        out_shape=[
            pltpu.VMEM((tokens, 3 * HD), jnp.bfloat16),
            pltpu.VMEM((block_rows, width), jnp.float32),
            pltpu.VMEM((block_rows, width), jnp.bfloat16),
            pltpu.VMEM((block_rows, width), jnp.float32),
        ],
        in_specs=vmem_specs(len(blocks) + 2 + 4 + 4 + 2),
        out_specs=vmem_specs(4),
        scratch_shapes=[
            pltpu.VMEM((rows, width), jnp.bfloat16),
            pltpu.VMEM((rows, width), jnp.bfloat16),
            pltpu.VMEM((rows, hidden_width), jnp.bfloat16),
        ],
        compiler_params=parameters(12),
        cost_estimate=pl.CostEstimate(
            flops=2 * rows * width * (3 * HD + HD + 2 * hidden_width),
            bytes_accessed=MIB,
            transcendentals=rows * hidden_width,
        ),
        name="last_rows",
    )(*blocks, *gains, *weights, *tables, own_joined, middle_joined)


def fed_kernel(own_hidden_ref, middle_hidden_ref, downward_ref, fed_ref):
    hidden = jnp.concatenate([own_hidden_ref[...], middle_hidden_ref[...]], 0)
    chunk = 512
    for begin in range(0, downward_ref.shape[1], chunk):
        columns = slice(begin, begin + chunk)
        fed_ref[:, columns] = jnp.dot(
            hidden, downward_ref[:, columns], preferred_element_type=jnp.float32
        )


def fed_rows(own_hidden, middle_hidden, downward_weight):
    rows = own_hidden.shape[0] + middle_hidden.shape[0]
    depth, width = downward_weight.shape
    return pl.pallas_call(
        fed_kernel,
        out_shape=pltpu.VMEM((rows, width), jnp.float32),
        in_specs=vmem_specs(3),
        out_specs=pl.BlockSpec(memory_space=pltpu.VMEM),
        compiler_params=parameters(12),
        cost_estimate=pl.CostEstimate(
            flops=2 * rows * depth * width, bytes_accessed=MIB, transcendentals=0
        ),
        name="fed_rows",
    )(own_hidden, middle_hidden, downward_weight)


def rest_kernel(joined_ref, offsets_ref, output_ref, fed_ref, fed_beside_ref, *refs):
    count = len(refs) // 2
    siblings, owns = refs[:count], refs[count:]
    block_rows = owns[0].shape[0]
    rows = fed_ref.shape[0] + fed_beside_ref.shape[0]
    attended = attend(joined_ref, offsets_ref, 0, rows, block_rows)
    chunk = 512
    for begin in range(0, output_ref.shape[1], chunk):
        columns = slice(begin, begin + chunk)
        fed = jnp.concatenate([fed_ref[:, columns], fed_beside_ref[:, columns]], 0)
        partial = fed + jnp.dot(
            attended, output_ref[:, columns], preferred_element_type=jnp.float32
        )
        for number, (sibling_ref, own_ref) in enumerate(zip(siblings, owns)):
            first = CORES * number * block_rows
            middle = first + block_rows
            own_ref[:, columns] = partial[first:middle]
            sibling_ref[:, columns] = partial[middle : middle + block_rows].astype(jnp.bfloat16)


def rest_rows(joined, offsets, output_weight, fed, fed_beside):
    width = fed.shape[1]
    rows = fed.shape[0] + fed_beside.shape[0]
    count = CHIPS - 1
    shape = (rows // (CORES * count), width)
    shapes = [pltpu.VMEM(shape, dtype) for dtype in [jnp.bfloat16] * count + [jnp.float32] * count]
    return pl.pallas_call(
        rest_kernel,
        out_shape=shapes,
        in_specs=vmem_specs(5),
        out_specs=vmem_specs(2 * count),
        compiler_params=parameters(12),
        cost_estimate=pl.CostEstimate(
            flops=2 * rows * width * HD,
            bytes_accessed=MIB,
            transcendentals=rows * joined.shape[0],
        ),
        name="rest_rows",
    )(joined, offsets, output_weight, fed, fed_beside)


def pages_kernel(joined_ref, destinations_ref, *page_refs):
    tokens = joined_ref.shape[0]
    slot_rows = page_refs[0].shape[0] * PAGE
    for number, page_ref in enumerate(page_refs):
        shape = (slot_rows, tokens)
        row = number * slot_rows + lax.broadcasted_iota(jnp.int32, shape, 0)
        placing = jnp.where(row == destinations_ref[...], 1.0, 0.0).astype(jnp.bfloat16)
        rows = jnp.dot(placing, joined_ref[:, HD:], preferred_element_type=jnp.float32)
        page_ref[...] = rows.astype(jnp.bfloat16).reshape(page_ref.shape)


def cached_pages(joined, destinations, replica_count):
    tokens = joined.shape[0]
    capacity = 2 * (tokens // PAGE) // replica_count
    shapes = [pltpu.VMEM((capacity, PAGE, 2 * HD), jnp.bfloat16)] * replica_count
    return pl.pallas_call(
        pages_kernel,
        out_shape=shapes,
        in_specs=vmem_specs(2),
        out_specs=vmem_specs(len(shapes)),
        compiler_params=parameters(8),
        cost_estimate=pl.CostEstimate(flops=0, bytes_accessed=MIB, transcendentals=0),
        name="cached_pages",
    )(joined, destinations)


def add_kernel(*refs):
    total = refs[0][...].astype(jnp.float32)
    for ref in refs[1:-1]:
        total = total + ref[...].astype(jnp.float32)
    refs[-1][...] = total.astype(refs[-1].dtype)


def added(name, *parts):
    return pl.pallas_call(
        add_kernel,
        out_shape=pltpu.VMEM(parts[0].shape, jnp.bfloat16),
        in_specs=vmem_specs(len(parts)),
        out_specs=pl.BlockSpec(memory_space=pltpu.VMEM),
        compiler_params=parameters(4),
        name=name,
    )(*parts)


def sums_kernel(passing_ref, *refs):
    zeros, ones, twos = refs[0:2], refs[2:4], refs[4:6]
    hidden_ref, second_ref, first_ref, base_ref = refs[6:]

    def total(pair, extra=None):
        received_ref, own_ref = pair
        value = own_ref[...] + received_ref[...].astype(jnp.float32)
        return value if extra is None else value + extra[...].astype(jnp.float32)

    second_ref[...] = total(twos, passing_ref).astype(jnp.bfloat16)
    first_ref[...] = total(ones).astype(jnp.bfloat16)
    base_ref[...] = total(zeros, hidden_ref)


def remaining_sums(passing, pairs, hidden):
    shape = hidden.shape
    return pl.pallas_call(
        sums_kernel,
        out_shape=[
            pltpu.VMEM(shape, jnp.bfloat16),
            pltpu.VMEM(shape, jnp.bfloat16),
            pltpu.VMEM(shape, jnp.float32),
        ],
        in_specs=vmem_specs(8),
        out_specs=vmem_specs(3),
        compiler_params=parameters(4),
        name="remaining_sums",
    )(passing, *[array for pair in pairs for array in pair], hidden)


def place_kernel(masks, *refs):
    group = lax.axis_index("dp")
    pages, (cache_ref, sems) = refs[:-2], refs[-2:]
    copies = [
        pltpu.make_async_copy(page_ref, cache_ref.at[0, group ^ mask], sems.at[number])
        for number, (mask, page_ref) in enumerate(zip(masks, pages))
    ]
    for copy in copies:
        copy.start()
    for copy in copies:
        copy.wait()


def placed(masks, pages, replica_count):
    count = len(pages)
    return pl.pallas_call(
        functools.partial(place_kernel, masks),
        out_shape=jax.ShapeDtypeStruct((1, replica_count) + pages[0].shape, pages[0].dtype),
        in_specs=[pl.BlockSpec(memory_space=pl.ANY)] * count,
        out_specs=pl.BlockSpec(memory_space=pltpu.HBM),
        scratch_shapes=[pltpu.SemaphoreType.DMA((count,))],
        compiler_params=parameters(4),
        name="placed",
    )(*pages)


def finish_kernel(masks, base_ref, *refs):
    count = len(masks)
    *parts, _, output_ref, cache_ref, total_scr, sems = refs
    parts, pages = parts[:-count], parts[-count:]
    group = lax.axis_index("dp")
    copies = [
        pltpu.make_async_copy(page_ref, cache_ref.at[0, group ^ mask], sems.at[number])
        for number, (mask, page_ref) in enumerate(zip(masks, pages))
    ]
    for copy in copies:
        copy.start()
    total = base_ref[...]
    for part_ref in parts:
        total = total + part_ref[...].astype(jnp.float32)
    total_scr[...] = total
    copies.append(pltpu.make_async_copy(total_scr, output_ref, sems.at[count]))
    copies[-1].start()
    for copy in copies:
        copy.wait()


def finished(base, parts, masks, pages, cache):
    count = len(pages)
    return pl.pallas_call(
        functools.partial(finish_kernel, masks),
        out_shape=[
            jax.ShapeDtypeStruct(base.shape, base.dtype),
            jax.ShapeDtypeStruct(cache.shape, cache.dtype),
        ],
        in_specs=vmem_specs(1 + len(parts))
        + [pl.BlockSpec(memory_space=pl.ANY)] * count
        + [pl.BlockSpec(memory_space=pltpu.HBM)],
        out_specs=[pl.BlockSpec(memory_space=pltpu.HBM)] * 2,
        scratch_shapes=[
            pltpu.VMEM(base.shape, base.dtype),
            pltpu.SemaphoreType.DMA((count + 1,)),
        ],
        input_output_aliases={1 + len(parts) + count: 1},
        compiler_params=parameters(4),
        name="finished",
    )(base, *parts, *pages, cache)


def shards_whole_heads(
    hidden_states,
    attention_gain,
    feedforward_gain,
    heads_weight,
    output_weight,
    upward_weight,
    downward_weight,
    segments,
    page_targets,
):
    replica_count = lax.axis_size("dp")
    to_chip = [mask * CORES for mask in range(CHIPS)]
    second_even = exchanged_by(0, hidden_states, "tensor", to_chip[2])
    first = exchanged(hidden_states, "tensor", to_chip[1])
    beside = exchanged(hidden_states, "tensor", 1)
    staged = (
        segments,
        page_targets.reshape(1, -1),
        hidden_states,
        attention_gain[None],
        feedforward_gain[None],
        heads_weight,
    )
    staged = own_rows(staged, replica_count)
    hidden, gains, heads, tables = staged[2], staged[3:5], staged[5], staged[6:10]
    destinations, own_joined, own_feedforward = staged[10:]
    second_odd = exchanged_by(1, hidden, "tensor", to_chip[2])
    upward, downward, own_hidden = own_units(own_feedforward, upward_weight, downward_weight)

    first, second_even, own_hidden = lax.optimization_barrier((first, second_even, own_hidden))
    third_even = exchanged_by(0, second_even, "tensor", to_chip[1])
    first_beside = exchanged(first, "tensor", 1)
    second_odd, first_beside, beside = lax.optimization_barrier(
        (second_odd, first_beside, beside)
    )
    third_odd = exchanged_by(1, second_odd, "tensor", to_chip[1])
    middle_joined, middle_hidden, second, output = middle_rows(
        ((0, 1), (1, 0), (1, 1), (2, 0)),
        (beside, first, first_beside, second_even, second_odd),
        gains,
        (heads, upward),
        tables[1:],
        output_weight,
    )
    second_beside = exchanged(second, "tensor", 1)
    third_even, third_odd, middle_joined, middle_hidden = lax.optimization_barrier(
        (third_even, third_odd, middle_joined, middle_hidden)
    )
    third = added("third_block", third_even, third_odd)
    third, second_beside = lax.optimization_barrier((third, second_beside))
    third_beside = exchanged(third, "tensor", 1)
    fed = fed_rows(own_hidden, middle_hidden, downward)
    third_beside, fed = lax.optimization_barrier((third_beside, fed))
    joined, fed_beside, sibling, own = last_rows(
        (second_beside, third, third_beside),
        gains,
        (heads, upward, downward, output),
        tables,
        own_joined,
        middle_joined,
    )

    received = exchanged(sibling, "tensor", 1)
    partials = rest_rows(joined, tables[0], output, fed, fed_beside)
    siblings, owns = partials[: CHIPS - 1], partials[CHIPS - 1 :]
    third_sum = added("third_added", own, received)
    third_sum, siblings, joined = lax.optimization_barrier((third_sum, siblings, joined))
    passing = exchanged(third_sum, "tensor", to_chip[1])
    pairs = [(exchanged(sibling, "tensor", 1), own) for sibling, own in zip(siblings, owns)]
    pages = cached_pages(joined, destinations, replica_count)
    early, late = (3,), (1, 2)
    arriving = [exchanged(pages[mask], "dp", mask) for mask in early]
    second_sum, first_sum, base = remaining_sums(passing, pairs, hidden)
    from_second = exchanged(second_sum, "tensor", to_chip[2])
    from_first = exchanged(first_sum, "tensor", to_chip[1])
    base, late_pages = lax.optimization_barrier((base, [pages[mask] for mask in late]))
    late_pages = [exchanged(page, "dp", mask) for mask, page in zip(late, late_pages)]
    cache_pages = placed((0,) + early, [pages[0]] + arriving, replica_count)
    return tuple(finished(base, (from_second, from_first), late, late_pages, cache_pages))


def solution(mesh):
    whole_heads = mesh.shape["tensor"] == H and mesh.shape["dp"] == 4
    shards = shards_whole_heads if whole_heads else shards_split_heads
    in_specs = (
        P(("dp", "tensor"), None),
        P(),
        P(),
        P(None, "tensor"),
        P("tensor", None),
        P(None, "tensor"),
        P("tensor", None),
        P("dp", None),
        P("dp", None),
    )
    out_specs = (P(("dp", "tensor"), None), P("dp", None, None, None, "tensor"))
    return jax.shard_map(shards, mesh=mesh, in_specs=in_specs, out_specs=out_specs, check_vma=False)
```

```python
import functools
import math

import jax
import jax.numpy as jnp
from jax import lax
from jax.experimental import pallas as pl
from jax.experimental.pallas import tpu as pltpu
from jax.sharding import PartitionSpec as P

H = 8
HD = 256
ROT = 64
PAGE = 16


epsilon = 1e-05
rotary_base = 10000.0
key_block = 256


def shortened(array):

    def short(part):
        return part.astype(jnp.bfloat16) if part.dtype == jnp.float32 else part

    return jax.tree.map(short, array)


def swapped(block, axis, apart):
    count = lax.axis_size(axis)
    route = []
    for low in range(count):
        high = low | 1 << apart
        if high != low and high < count:
            route += [(low, high), (high, low)]
    return lax.ppermute(block, axis, route)


def layer_norm(values, gain):
    floats = values.astype(jnp.float32)
    center = jnp.mean(floats, axis=-1, keepdims=True)
    shifted = floats - center
    spread = jnp.mean(shifted * shifted, axis=-1, keepdims=True)
    return (shifted * lax.rsqrt(spread + epsilon) * gain).astype(jnp.bfloat16)


def positions_of(stream):
    indices = jnp.arange(stream.shape[0], dtype=jnp.int32)
    boundary = jnp.concatenate([jnp.ones((1,), dtype=bool), stream[1:] != stream[:-1]])
    starting = lax.cummax(jnp.where(boundary, indices, jnp.zeros_like(indices)), axis=0)
    return (indices, starting)


def rotate_heads(vectors, offsets, rotary_dims):
    half_dims = rotary_dims // 2
    frequency = jnp.exp(
        jnp.arange(half_dims, dtype=jnp.float32) * (-2.0 * math.log(rotary_base) / rotary_dims)
    )
    angles = offsets.astype(jnp.float32)[:, None] * frequency[None, :]
    cosine = jnp.cos(angles)
    sine = jnp.sin(angles)
    floats = vectors.astype(jnp.float32)
    leading = floats[..., :half_dims]
    trailing = floats[..., half_dims:rotary_dims]
    rotated = jnp.concatenate(
        [
            leading * cosine - trailing * sine,
            trailing * cosine + leading * sine,
            floats[..., rotary_dims:],
        ],
        axis=-1,
    )
    return rotated.astype(jnp.bfloat16)


def shards_split_heads(
    hidden_states,
    attention_gain,
    feedforward_gain,
    heads_weight,
    output_weight,
    upward_weight,
    downward_weight,
    segments,
    page_targets,
):
    tensor_count = lax.axis_size("tensor")
    replica_count = lax.axis_size("dp")
    tensor_index = lax.axis_index("tensor")
    quarters = tensor_count // H
    quarter_width = HD // quarters
    quarter_index = tensor_index % quarters
    stream = segments[0]
    tokens_total = stream.shape[0]
    level_count = quarters.bit_length() - 1
    normed_attention = layer_norm(hidden_states, attention_gain)
    normed_feedforward = layer_norm(hidden_states, feedforward_gain)
    shard_rows = lax.all_gather(
        (normed_attention, normed_feedforward), "tensor", axis=0, tiled=True
    )
    joined_rows = jnp.dot(shard_rows[0], heads_weight, preferred_element_type=jnp.float32).astype(
        jnp.bfloat16
    )
    upward = jnp.dot(shard_rows[1], upward_weight, preferred_element_type=jnp.float32)
    hidden_rows = jax.nn.gelu(upward, approximate=False).astype(jnp.bfloat16)
    hidden = hidden_rows
    pieces = (
        joined_rows.reshape(tokens_total, 3, quarter_width)
        .transpose(1, 0, 2)
        .reshape(1, 3, tokens_total * quarter_width)
    )
    for bit_number in range(level_count):
        partner = swapped(shortened(pieces), "tensor", bit_number).astype(pieces.dtype)
        lower = tensor_index >> bit_number & 1 == 0
        pieces = jnp.where(
            lower, jnp.concatenate([pieces, partner], 0), jnp.concatenate([partner, pieces], 0)
        )
    whole_head = (
        pieces.reshape(quarters, 3, tokens_total, quarter_width)
        .transpose(1, 2, 0, 3)
        .reshape(3, tokens_total, HD)
    )
    indices, starting = positions_of(stream)
    offsets = indices - starting
    queries = rotate_heads(whole_head[0], offsets, ROT)
    keys = rotate_heads(whole_head[1], offsets, ROT)
    values = whole_head[2]
    block_rows = tokens_total // (2 * quarters)
    score_scale = HD ** (-0.5)

    def attend_block(block_number):
        first_row = block_number * block_rows
        block_queries = lax.dynamic_slice_in_dim(queries, first_row, block_rows, 0)
        query_segments = lax.dynamic_slice_in_dim(stream, first_row, block_rows, 0)
        query_indices = first_row + jnp.arange(block_rows, dtype=jnp.int32)
        lowest = lax.dynamic_index_in_dim(starting, first_row, 0, keepdims=False) // key_block
        highest = (first_row + block_rows + key_block - 1) // key_block

        def scores_of(key_number):
            key_first = key_number * key_block
            key_indices = key_first + jnp.arange(key_block, dtype=jnp.int32)
            scores = (
                jnp.dot(block_queries, keys.T, preferred_element_type=jnp.float32) * score_scale
            )
            allowed = (stream[None, :] == query_segments[:, None]) & (
                key_indices[None, :] <= query_indices[:, None]
            )
            return (scores, allowed)

        def find_peak(key_number, peak):
            scores, allowed = scores_of(key_number)
            return jnp.maximum(peak, jnp.max(jnp.where(allowed, scores, -jnp.inf), axis=1))

        peak = lax.fori_loop(
            lowest, highest, find_peak, jnp.full((block_rows,), -jnp.inf, jnp.float32)
        )

        def accumulate(key_number, state):
            weight_sum, mixed_sum = state
            scores, allowed = scores_of(key_number)
            weights = jnp.where(allowed, jnp.exp(scores - peak[:, None]), 0.0)
            mixed_next = mixed_sum + jnp.dot(
                weights.astype(jnp.bfloat16), values, preferred_element_type=jnp.float32
            )
            return (weight_sum + jnp.sum(weights, axis=1), mixed_next)

        start_state = (
            jnp.zeros((block_rows,), jnp.float32),
            jnp.zeros((block_rows, HD), jnp.float32),
        )
        weight_sum, mixed_sum = lax.fori_loop(lowest, highest, accumulate, start_state)
        return (mixed_sum / weight_sum[:, None]).astype(jnp.bfloat16)

    own_blocks = (2 * quarter_index, 2 * quarter_index + 1)
    own_rows = jnp.concatenate([attend_block(own_blocks[0]), attend_block(own_blocks[1])], 0)[None]
    for bit_number in range(level_count):
        partner = swapped(own_rows, "tensor", bit_number)
        lower = tensor_index >> bit_number & 1 == 0
        own_rows = jnp.where(
            lower, jnp.concatenate([own_rows, partner], 0), jnp.concatenate([partner, own_rows], 0)
        )
    attended = own_rows.reshape(tokens_total, HD)
    attended_quarter = lax.dynamic_slice_in_dim(
        attended, quarter_index * quarter_width, quarter_width, 1
    )
    hidden_rows = hidden
    summed = lax.psum_scatter(
        (
            jnp.dot(attended_quarter, output_weight, preferred_element_type=jnp.float32)
            + jnp.dot(hidden_rows, downward_weight, preferred_element_type=jnp.float32)
        ).astype(jnp.bfloat16),
        "tensor",
        scatter_dimension=0,
        tiled=True,
    ).astype(jnp.float32)
    layer_output = hidden_states.astype(jnp.float32) + summed
    key_quarter = lax.dynamic_slice_in_dim(keys, quarter_index * quarter_width, quarter_width, 1)
    value_quarter = joined_rows[:, 2 * quarter_width :]
    page_count = tokens_total // PAGE
    page_rows = jnp.concatenate([key_quarter, value_quarter], 1).reshape(
        page_count, PAGE * 2 * quarter_width
    )
    targets = page_targets[:, 0]
    page_numbers = jnp.arange(page_count, dtype=jnp.int32)
    earlier = jnp.sum(
        (
            (targets[None, :] == targets[:, None]) & (page_numbers[None, :] < page_numbers[:, None])
        ).astype(jnp.int32),
        axis=1,
    )
    capacity = 2 * page_count // replica_count
    slot_numbers = targets * capacity + earlier
    placing = (
        jnp.arange(replica_count * capacity, dtype=jnp.int32)[:, None] == slot_numbers[None, :]
    ).astype(jnp.bfloat16)
    outgoing = jnp.dot(placing, page_rows, preferred_element_type=jnp.float32).astype(jnp.bfloat16)
    outgoing = outgoing.reshape(replica_count, capacity, PAGE * 2 * quarter_width)
    incoming = lax.all_to_all(outgoing, "dp", split_axis=0, concat_axis=0, tiled=True)
    cache_pages = incoming.reshape(1, replica_count, capacity, PAGE, 2 * quarter_width)
    return (layer_output, cache_pages)


CORES = 2
CHIPS = 4
MIB = 1 << 20


def in_hbm(array):
    return pltpu.with_memory_space_constraint(array, pltpu.HBM)


def exchanged(block, axis, mask):
    count = lax.axis_size(axis)
    return lax.ppermute(block, axis, [(member, member ^ mask) for member in range(count)])


def vmem_specs(count):
    return [pl.BlockSpec(memory_space=pltpu.VMEM)] * count


def parameters(mebibytes):
    return pltpu.CompilerParams(vmem_limit_bytes=mebibytes * MIB)


def whereabouts():
    member = lax.axis_index("tensor")
    return member // CORES, member % CORES


def position_of(kind, half, block_rows):
    chip, core = whereabouts()
    return ((chip ^ kind) * CORES + (core ^ half)) * block_rows


def positions_along(first, shape, axis, block_rows):
    chip, core = whereabouts()
    bits = block_rows.bit_length() - 1
    place = first + lax.broadcasted_iota(jnp.int32, shape, axis)
    kind = place >> (bits + 1)
    half = (place >> bits) & 1
    return ((((chip ^ kind) << 1) | (core ^ half)) << bits) | (place & (block_rows - 1))


def normalize(blocks, gain_refs, normed_refs):
    piece = 16
    gains = [gain_ref[...] for gain_ref in gain_refs]
    for number, block_ref in enumerate(blocks):
        block_rows = block_ref.shape[0]
        for part in range(0, block_rows, piece):
            floats = block_ref[part : part + piece, :].astype(jnp.float32)
            center = jnp.mean(floats, axis=-1, keepdims=True)
            shifted = floats - center
            spread = jnp.mean(shifted * shifted, axis=-1, keepdims=True)
            scaled = shifted * lax.rsqrt(spread + epsilon)
            first = number * block_rows + part
            for gain, normed_ref in zip(gains, normed_refs):
                normed_ref[first : first + piece, :] = (scaled * gain).astype(jnp.bfloat16)


def project(normed_ref, heads_ref, table_refs, places, joined_ref, first):
    rows = normed_ref.shape[0]
    block_rows = rows // len(places)
    for component in range(3):
        columns = slice(component * HD, (component + 1) * HD)
        joined = jnp.dot(
            normed_ref[...], heads_ref[:, columns], preferred_element_type=jnp.float32
        ).astype(jnp.bfloat16)
        joined_ref[first : first + rows, columns] = joined
        if component < 2:
            cosine, sine_down, sine_up = [
                jnp.concatenate(
                    [
                        table_ref[pl.ds(pl.multiple_of(place, block_rows), block_rows), :]
                        for place in places
                    ],
                    0,
                )
                for table_ref in table_refs
            ]
            turning = joined[:, :128].astype(jnp.float32)
            turned = (
                turning * cosine
                + pltpu.roll(turning, 128 - ROT // 2, 1) * sine_down
                + pltpu.roll(turning, ROT // 2, 1) * sine_up
            )
            joined_ref[first : first + rows, component * HD : component * HD + 128] = turned.astype(
                jnp.bfloat16
            )


def hide(normed_ref, upward_ref, hidden_ref, place):
    chunk = 256
    rows = slice(place, place + normed_ref.shape[0])
    for first in range(0, upward_ref.shape[1], chunk):
        columns = slice(first, first + chunk)
        upward = jnp.dot(
            normed_ref[...], upward_ref[:, columns], preferred_element_type=jnp.float32
        )
        hidden = 0.5 * upward * (1.0 + lax.erf(upward * (0.5**0.5)))
        hidden_ref[rows, columns] = hidden.astype(jnp.bfloat16)


def attend(joined_ref, offsets_ref, first, rows, block_rows):
    tokens = joined_ref.shape[0]
    starts = [
        position_of(place // (2 * block_rows), (place // block_rows) % 2, block_rows)
        for place in range(first, first + rows, block_rows)
    ]
    reach = jnp.concatenate(
        [
            offsets_ref[pl.ds(pl.multiple_of(start, block_rows), block_rows), :]
            for start in starts
        ],
        0,
    )[:, :1].astype(jnp.int32)
    row = positions_along(first, (rows, 1), 0, block_rows)
    column = positions_along(0, (1, tokens), 1, block_rows)
    allowed = (column <= row) & (column >= row - reach)
    scores = lax.dot_general(
        joined_ref[first : first + rows, :HD],
        joined_ref[:, HD : 2 * HD],
        (((1,), (1,)), ((), ())),
        preferred_element_type=jnp.float32,
    ) * (HD ** (-0.5))
    peak = jnp.max(jnp.where(allowed, scores, -jnp.inf), axis=1, keepdims=True)
    weights = jnp.where(allowed, jnp.exp(scores - peak), 0.0)
    weight_sum = jnp.sum(weights, axis=1, keepdims=True)
    mixed = jnp.dot(
        weights.astype(jnp.bfloat16), joined_ref[:, 2 * HD :], preferred_element_type=jnp.float32
    )
    return (mixed / weight_sum).astype(jnp.bfloat16)


def make_tables(segments_ref, offsets_ref, cosine_ref, sine_down_ref, sine_up_ref):
    tokens = segments_ref.shape[1]
    shape = (tokens, tokens)
    rows = lax.broadcasted_iota(jnp.int32, shape, 0)
    columns = lax.broadcasted_iota(jnp.int32, shape, 1)
    across = jnp.broadcast_to(segments_ref[...], shape).astype(jnp.float32)
    down = jnp.sum(jnp.where(rows == columns, across, 0.0), axis=1, keepdims=True)
    earlier = (across == down) & (columns < rows)
    offsets = jnp.sum(jnp.where(earlier, 1.0, 0.0), axis=1, keepdims=True)
    offsets_ref[...] = jnp.broadcast_to(offsets, offsets_ref.shape)
    half = ROT // 2
    lane = lax.broadcasted_iota(jnp.int32, (tokens, 128), 1)
    step = (lane & (half - 1)).astype(jnp.float32)
    frequency = jnp.exp(step * (-2.0 * math.log(rotary_base) / ROT))
    angles = offsets * frequency
    sine = jnp.sin(angles)
    cosine_ref[...] = jnp.where(lane < ROT, jnp.cos(angles), 1.0)
    sine_down_ref[...] = jnp.where(lane < half, -sine, 0.0)
    sine_up_ref[...] = jnp.where((lane >= half) & (lane < ROT), sine, 0.0)


def make_destinations(targets_ref, destinations_ref, replica_count, block_rows):
    page_count = targets_ref.shape[1]
    tokens = destinations_ref.shape[1]
    capacity = 2 * page_count // replica_count
    square = (page_count, page_count)
    rows = lax.broadcasted_iota(jnp.int32, square, 0)
    columns = lax.broadcasted_iota(jnp.int32, square, 1)
    across = jnp.broadcast_to(targets_ref[...], square).astype(jnp.float32)
    down = jnp.sum(jnp.where(rows == columns, across, 0.0), axis=1, keepdims=True)
    earlier = jnp.where((across == down) & (columns < rows), 1.0, 0.0)
    slots = jnp.sum(earlier, axis=1, keepdims=True).astype(jnp.int32)
    slots = (down.astype(jnp.int32) ^ lax.axis_index("dp")) * capacity + slots
    positions = positions_along(0, (1, tokens), 1, block_rows)
    bits = PAGE.bit_length() - 1
    pages = lax.broadcasted_iota(jnp.int32, (page_count, tokens), 0)
    chosen = jnp.where(pages == positions >> bits, slots.astype(jnp.float32), 0.0)
    slot = jnp.sum(chosen, axis=0, keepdims=True).astype(jnp.int32)
    destinations_ref[...] = slot * PAGE + (positions & (PAGE - 1))


def copies_in(sources, targets, sems):
    copies = []
    for number, (source, target) in enumerate(zip(sources, targets)):
        parts = 4 if source.shape[0] >= 256 else 1
        rows = source.shape[0] // parts
        places = [pl.ds(part * rows, rows) for part in range(parts)]
        copies.append(
            [
                pltpu.make_async_copy(source.at[place], target.at[place], sems.at[number, part])
                for part, place in enumerate(places)
            ]
        )
    for copy in sum(copies, []):
        copy.start()
    return copies


def wait_for(copies):
    for copy in copies:
        copy.wait()


def own_kernel(count, replica_count, *refs):
    sources, targets = refs[:count], refs[count : 2 * count]
    offsets_ref, *table_refs, destinations_ref, joined_ref, hidden_ref = refs[2 * count : -3]
    attention_scr, feedforward_scr, sems = refs[-3:]
    copies = copies_in(sources, targets, sems)
    segments_ref, targets_ref, states_ref, *gain_refs, heads_ref, upward_ref = targets
    block_rows = states_ref.shape[0]
    wait_for(copies[0])
    make_tables(segments_ref, offsets_ref, *table_refs)
    wait_for(copies[1])
    make_destinations(targets_ref, destinations_ref, replica_count, block_rows)
    for number in (2, 3, 4):
        wait_for(copies[number])
    normalize([states_ref], gain_refs, [attention_scr, feedforward_scr])
    wait_for(copies[5])
    places = [position_of(0, 0, block_rows)]
    project(attention_scr, heads_ref, table_refs, places, joined_ref, 0)
    wait_for(copies[6])
    hide(feedforward_scr, upward_ref, hidden_ref, 0)


def own_rows(staged, replica_count):
    tokens = staged[0].shape[1]
    rows, width = staged[2].shape
    hidden_width = staged[6].shape[1]
    shapes = [pltpu.VMEM(array.shape, array.dtype) for array in staged]
    shapes += [pltpu.VMEM((tokens, 128), jnp.float32)] * 4
    shapes += [
        pltpu.VMEM((1, tokens), jnp.int32),
        pltpu.VMEM((rows, 3 * HD), jnp.bfloat16),
        pltpu.VMEM((rows, hidden_width), jnp.bfloat16),
    ]
    count = len(staged)
    return pl.pallas_call(
        functools.partial(own_kernel, count, replica_count),
        out_shape=shapes,
        in_specs=[pl.BlockSpec(memory_space=pltpu.HBM)] * count,
        out_specs=vmem_specs(len(shapes)),
        scratch_shapes=[
            pltpu.VMEM((rows, width), jnp.bfloat16),
            pltpu.VMEM((rows, width), jnp.bfloat16),
            pltpu.SemaphoreType.DMA((count, 4)),
        ],
        compiler_params=parameters(12),
        cost_estimate=pl.CostEstimate(
            flops=2 * rows * width * (3 * HD + hidden_width),
            bytes_accessed=sum(array.nbytes for array in staged),
            transcendentals=rows * hidden_width,
        ),
        name="own_rows",
    )(*[in_hbm(array) for array in staged])


def middle_kernel(origins, *refs):
    count = len(origins)
    blocks, (gain_a, gain_f, heads_ref, upward_ref) = refs[:count], refs[count : count + 4]
    table_refs, refs = refs[count + 4 : count + 7], refs[count + 7 :]
    staged = (len(refs) - 5) // 2
    sources, (joined_ref, hidden_ref), refs = refs[:staged], refs[staged:][:2], refs[staged + 2 :]
    targets, (attention_scr, feedforward_scr, sems) = refs[:staged], refs[staged:]
    copies = copies_in(sources, targets, sems)
    block_rows = blocks[0].shape[0]
    normalize(blocks, [gain_a, gain_f], [attention_scr, feedforward_scr])
    places = [position_of(kind, half, block_rows) for kind, half in origins]
    project(attention_scr, heads_ref, table_refs, places, joined_ref, 0)
    hide(feedforward_scr, upward_ref, hidden_ref, 0)
    wait_for(sum(copies, []))


def middle_rows(name, origins, blocks, gains, weights, tables, *staged):
    block_rows, width = blocks[0].shape
    rows = len(blocks) * block_rows
    hidden_width = weights[1].shape[1]
    return pl.pallas_call(
        functools.partial(middle_kernel, origins),
        out_shape=[
            pltpu.VMEM((rows, 3 * HD), jnp.bfloat16),
            pltpu.VMEM((rows, hidden_width), jnp.bfloat16),
        ]
        + [pltpu.VMEM(array.shape, array.dtype) for array in staged],
        in_specs=vmem_specs(len(blocks) + 2 + 2 + 3)
        + [pl.BlockSpec(memory_space=pltpu.HBM)] * len(staged),
        out_specs=vmem_specs(2 + len(staged)),
        scratch_shapes=[
            pltpu.VMEM((rows, width), jnp.bfloat16),
            pltpu.VMEM((rows, width), jnp.bfloat16),
            pltpu.SemaphoreType.DMA((max(len(staged), 1), 4)),
        ],
        compiler_params=parameters(12),
        cost_estimate=pl.CostEstimate(
            flops=2 * rows * width * (3 * HD + hidden_width),
            bytes_accessed=MIB,
            transcendentals=rows * hidden_width,
        ),
        name=name,
    )(*blocks, *gains, *weights, *tables, *[in_hbm(array) for array in staged])


def last_kernel(*refs):
    blocks, (gain_a, gain_f, heads_ref, upward_ref, downward_ref, output_ref) = refs[:3], refs[3:9]
    offsets_ref, *table_refs = refs[9:13]
    own_joined_ref, middle_joined_ref = refs[13:15]
    joined_ref, fed_ref, sibling_ref, own_ref = refs[15:19]
    attention_scr, feedforward_scr, hidden_scr = refs[19:]
    block_rows = blocks[0].shape[0]
    tokens = joined_ref.shape[0]
    first = tokens - len(blocks) * block_rows
    normalize(blocks, [gain_a, gain_f], [attention_scr, feedforward_scr])
    joined_ref[:block_rows, :] = own_joined_ref[...]
    joined_ref[block_rows:first, :] = middle_joined_ref[...]
    origins = ((CHIPS - 2, 1), (CHIPS - 1, 0), (CHIPS - 1, 1))
    places = [position_of(kind, half, block_rows) for kind, half in origins]
    project(attention_scr, heads_ref, table_refs, places, joined_ref, first)
    hide(feedforward_scr, upward_ref, hidden_scr, 0)
    rows = CORES * block_rows
    attended = attend(joined_ref, offsets_ref, tokens - rows, rows, block_rows)
    chunk = 512
    for begin in range(0, downward_ref.shape[1], chunk):
        columns = slice(begin, begin + chunk)
        fed = jnp.dot(hidden_scr[...], downward_ref[:, columns], preferred_element_type=jnp.float32)
        fed_ref[:, columns] = fed[:block_rows]
        partial = fed[block_rows:] + jnp.dot(
            attended, output_ref[:, columns], preferred_element_type=jnp.float32
        )
        own_ref[:, columns] = partial[:block_rows]
        sibling_ref[:, columns] = partial[block_rows:].astype(jnp.bfloat16)


def last_rows(blocks, gains, weights, tables, own_joined, middle_joined):
    block_rows, width = blocks[0].shape
    rows = len(blocks) * block_rows
    hidden_width = weights[1].shape[1]
    tokens = CHIPS * CORES * block_rows
    return pl.pallas_call(
        last_kernel,
        out_shape=[
            pltpu.VMEM((tokens, 3 * HD), jnp.bfloat16),
            pltpu.VMEM((block_rows, width), jnp.float32),
            pltpu.VMEM((block_rows, width), jnp.bfloat16),
            pltpu.VMEM((block_rows, width), jnp.float32),
        ],
        in_specs=vmem_specs(len(blocks) + 2 + 4 + 4 + 2),
        out_specs=vmem_specs(4),
        scratch_shapes=[
            pltpu.VMEM((rows, width), jnp.bfloat16),
            pltpu.VMEM((rows, width), jnp.bfloat16),
            pltpu.VMEM((rows, hidden_width), jnp.bfloat16),
        ],
        compiler_params=parameters(12),
        cost_estimate=pl.CostEstimate(
            flops=2 * rows * width * (3 * HD + HD + 2 * hidden_width),
            bytes_accessed=MIB,
            transcendentals=rows * hidden_width,
        ),
        name="last_rows",
    )(*blocks, *gains, *weights, *tables, own_joined, middle_joined)


def fed_kernel(own_hidden_ref, middle_hidden_ref, downward_ref, fed_ref):
    hidden = jnp.concatenate([own_hidden_ref[...], middle_hidden_ref[...]], 0)
    chunk = 512
    for begin in range(0, downward_ref.shape[1], chunk):
        columns = slice(begin, begin + chunk)
        fed_ref[:, columns] = jnp.dot(
            hidden, downward_ref[:, columns], preferred_element_type=jnp.float32
        )


def fed_rows(own_hidden, middle_hidden, downward_weight):
    rows = own_hidden.shape[0] + middle_hidden.shape[0]
    depth, width = downward_weight.shape
    return pl.pallas_call(
        fed_kernel,
        out_shape=pltpu.VMEM((rows, width), jnp.float32),
        in_specs=vmem_specs(3),
        out_specs=pl.BlockSpec(memory_space=pltpu.VMEM),
        compiler_params=parameters(12),
        cost_estimate=pl.CostEstimate(
            flops=2 * rows * depth * width, bytes_accessed=MIB, transcendentals=0
        ),
        name="fed_rows",
    )(own_hidden, middle_hidden, downward_weight)


def rest_kernel(joined_ref, offsets_ref, output_ref, fed_ref, fed_beside_ref, *refs):
    count = len(refs) // 2
    siblings, owns = refs[:count], refs[count:]
    block_rows = owns[0].shape[0]
    rows = fed_ref.shape[0] + fed_beside_ref.shape[0]
    attended = attend(joined_ref, offsets_ref, 0, rows, block_rows)
    chunk = 512
    for begin in range(0, output_ref.shape[1], chunk):
        columns = slice(begin, begin + chunk)
        fed = jnp.concatenate([fed_ref[:, columns], fed_beside_ref[:, columns]], 0)
        partial = fed + jnp.dot(
            attended, output_ref[:, columns], preferred_element_type=jnp.float32
        )
        for number, (sibling_ref, own_ref) in enumerate(zip(siblings, owns)):
            first = CORES * number * block_rows
            middle = first + block_rows
            own_ref[:, columns] = partial[first:middle]
            sibling_ref[:, columns] = partial[middle : middle + block_rows].astype(jnp.bfloat16)


def rest_rows(joined, offsets, output_weight, fed, fed_beside):
    width = fed.shape[1]
    rows = fed.shape[0] + fed_beside.shape[0]
    count = CHIPS - 1
    shape = (rows // (CORES * count), width)
    shapes = [pltpu.VMEM(shape, dtype) for dtype in [jnp.bfloat16] * count + [jnp.float32] * count]
    return pl.pallas_call(
        rest_kernel,
        out_shape=shapes,
        in_specs=vmem_specs(5),
        out_specs=vmem_specs(2 * count),
        compiler_params=parameters(12),
        cost_estimate=pl.CostEstimate(
            flops=2 * rows * width * HD,
            bytes_accessed=MIB,
            transcendentals=rows * joined.shape[0],
        ),
        name="rest_rows",
    )(joined, offsets, output_weight, fed, fed_beside)


def pages_kernel(joined_ref, destinations_ref, *page_refs):
    tokens = joined_ref.shape[0]
    slot_rows = page_refs[0].shape[0] * PAGE
    for number, page_ref in enumerate(page_refs):
        shape = (slot_rows, tokens)
        row = number * slot_rows + lax.broadcasted_iota(jnp.int32, shape, 0)
        placing = jnp.where(row == destinations_ref[...], 1.0, 0.0).astype(jnp.bfloat16)
        rows = jnp.dot(placing, joined_ref[:, HD:], preferred_element_type=jnp.float32)
        page_ref[...] = rows.astype(jnp.bfloat16).reshape(page_ref.shape)


def cached_pages(joined, destinations, replica_count):
    tokens = joined.shape[0]
    capacity = 2 * (tokens // PAGE) // replica_count
    shapes = [pltpu.VMEM((capacity, PAGE, 2 * HD), jnp.bfloat16)] * replica_count
    return pl.pallas_call(
        pages_kernel,
        out_shape=shapes,
        in_specs=vmem_specs(2),
        out_specs=vmem_specs(len(shapes)),
        compiler_params=parameters(8),
        cost_estimate=pl.CostEstimate(flops=0, bytes_accessed=MIB, transcendentals=0),
        name="cached_pages",
    )(joined, destinations)


def add_kernel(*refs):
    total = refs[0][...].astype(jnp.float32)
    for ref in refs[1:-1]:
        total = total + ref[...].astype(jnp.float32)
    refs[-1][...] = total.astype(refs[-1].dtype)


def added(name, *parts):
    return pl.pallas_call(
        add_kernel,
        out_shape=pltpu.VMEM(parts[0].shape, jnp.bfloat16),
        in_specs=vmem_specs(len(parts)),
        out_specs=pl.BlockSpec(memory_space=pltpu.VMEM),
        compiler_params=parameters(4),
        name=name,
    )(*parts)


def sums_kernel(passing_ref, *refs):
    zeros, ones, twos = refs[0:2], refs[2:4], refs[4:6]
    hidden_ref, second_ref, first_ref, base_ref = refs[6:]

    def total(pair, extra=None):
        received_ref, own_ref = pair
        value = own_ref[...] + received_ref[...].astype(jnp.float32)
        return value if extra is None else value + extra[...].astype(jnp.float32)

    second_ref[...] = total(twos, passing_ref).astype(jnp.bfloat16)
    first_ref[...] = total(ones).astype(jnp.bfloat16)
    base_ref[...] = total(zeros, hidden_ref)


def remaining_sums(passing, pairs, hidden):
    shape = hidden.shape
    return pl.pallas_call(
        sums_kernel,
        out_shape=[
            pltpu.VMEM(shape, jnp.bfloat16),
            pltpu.VMEM(shape, jnp.bfloat16),
            pltpu.VMEM(shape, jnp.float32),
        ],
        in_specs=vmem_specs(8),
        out_specs=vmem_specs(3),
        compiler_params=parameters(4),
        name="remaining_sums",
    )(passing, *[array for pair in pairs for array in pair], hidden)


def place_kernel(masks, *refs):
    group = lax.axis_index("dp")
    pages, (cache_ref, sems) = refs[:-2], refs[-2:]
    copies = [
        pltpu.make_async_copy(page_ref, cache_ref.at[0, group ^ mask], sems.at[number])
        for number, (mask, page_ref) in enumerate(zip(masks, pages))
    ]
    for copy in copies:
        copy.start()
    for copy in copies:
        copy.wait()


def placed(masks, pages, replica_count):
    count = len(pages)
    return pl.pallas_call(
        functools.partial(place_kernel, masks),
        out_shape=jax.ShapeDtypeStruct((1, replica_count) + pages[0].shape, pages[0].dtype),
        in_specs=[pl.BlockSpec(memory_space=pl.ANY)] * count,
        out_specs=pl.BlockSpec(memory_space=pltpu.HBM),
        scratch_shapes=[pltpu.SemaphoreType.DMA((count,))],
        compiler_params=parameters(4),
        name="placed",
    )(*pages)


def finish_kernel(masks, base_ref, *refs):
    count = len(masks)
    *parts, _, output_ref, cache_ref, total_scr, sems = refs
    parts, pages = parts[:-count], parts[-count:]
    group = lax.axis_index("dp")
    copies = [
        pltpu.make_async_copy(page_ref, cache_ref.at[0, group ^ mask], sems.at[number])
        for number, (mask, page_ref) in enumerate(zip(masks, pages))
    ]
    for copy in copies:
        copy.start()
    total = base_ref[...]
    for part_ref in parts:
        total = total + part_ref[...].astype(jnp.float32)
    total_scr[...] = total
    copies.append(pltpu.make_async_copy(total_scr, output_ref, sems.at[count]))
    copies[-1].start()
    for copy in copies:
        copy.wait()


def finished(base, parts, masks, pages, cache):
    count = len(pages)
    return pl.pallas_call(
        functools.partial(finish_kernel, masks),
        out_shape=[
            jax.ShapeDtypeStruct(base.shape, base.dtype),
            jax.ShapeDtypeStruct(cache.shape, cache.dtype),
        ],
        in_specs=vmem_specs(1 + len(parts))
        + [pl.BlockSpec(memory_space=pl.ANY)] * count
        + [pl.BlockSpec(memory_space=pltpu.HBM)],
        out_specs=[pl.BlockSpec(memory_space=pltpu.HBM)] * 2,
        scratch_shapes=[
            pltpu.VMEM(base.shape, base.dtype),
            pltpu.SemaphoreType.DMA((count + 1,)),
        ],
        input_output_aliases={1 + len(parts) + count: 1},
        compiler_params=parameters(4),
        name="finished",
    )(base, *parts, *pages, cache)


def shards_whole_heads(
    hidden_states,
    attention_gain,
    feedforward_gain,
    heads_weight,
    output_weight,
    upward_weight,
    downward_weight,
    segments,
    page_targets,
):
    replica_count = lax.axis_size("dp")
    to_chip = [mask * CORES for mask in range(CHIPS)]
    second = exchanged(hidden_states, "tensor", to_chip[2])
    first = exchanged(hidden_states, "tensor", to_chip[1])
    beside = exchanged(hidden_states, "tensor", 1)
    staged = (
        segments,
        page_targets.reshape(1, -1),
        hidden_states,
        attention_gain[None],
        feedforward_gain[None],
        heads_weight,
        upward_weight,
    )
    staged = own_rows(staged, replica_count)
    hidden, gains, (heads, upward), tables = staged[2], staged[3:5], staged[5:7], staged[7:11]
    destinations, own_joined, own_hidden = staged[11:]

    first, second, own_joined = lax.optimization_barrier((first, second, own_joined))
    first_beside = exchanged(first, "tensor", 1)
    third = exchanged(second, "tensor", to_chip[1])
    middle_joined, middle_hidden, downward, output = middle_rows(
        "middle_rows",
        ((0, 1), (1, 0), (1, 1), (2, 0)),
        (beside, first, first_beside, second),
        gains,
        (heads, upward),
        tables[1:],
        downward_weight,
        output_weight,
    )
    second, middle_joined = lax.optimization_barrier((second, middle_joined))
    second_beside = exchanged(second, "tensor", 1)
    third, second_beside, middle_joined, middle_hidden = lax.optimization_barrier(
        (third, second_beside, middle_joined, middle_hidden)
    )
    third_beside = exchanged(third, "tensor", 1)
    fed = fed_rows(own_hidden, middle_hidden, downward)
    third_beside, fed = lax.optimization_barrier((third_beside, fed))
    joined, fed_beside, sibling, own = last_rows(
        (second_beside, third, third_beside),
        gains,
        (heads, upward, downward, output),
        tables,
        own_joined,
        middle_joined,
    )

    received = exchanged(sibling, "tensor", 1)
    partials = rest_rows(joined, tables[0], output, fed, fed_beside)
    siblings, owns = partials[: CHIPS - 1], partials[CHIPS - 1 :]
    third_sum = added("third_added", own, received)
    third_sum, siblings, joined = lax.optimization_barrier((third_sum, siblings, joined))
    passing = exchanged(third_sum, "tensor", to_chip[1])
    pairs = [(exchanged(sibling, "tensor", 1), own) for sibling, own in zip(siblings, owns)]
    pages = cached_pages(joined, destinations, replica_count)
    early, late = (3,), (1, 2)
    arriving = [exchanged(pages[mask], "dp", mask) for mask in early]
    second_sum, first_sum, base = remaining_sums(passing, pairs, hidden)
    from_second = exchanged(second_sum, "tensor", to_chip[2])
    from_first = exchanged(first_sum, "tensor", to_chip[1])
    base, late_pages = lax.optimization_barrier((base, [pages[mask] for mask in late]))
    late_pages = [exchanged(page, "dp", mask) for mask, page in zip(late, late_pages)]
    cache_pages = placed((0,) + early, [pages[0]] + arriving, replica_count)
    return tuple(finished(base, (from_second, from_first), late, late_pages, cache_pages))


def solution(mesh):
    whole_heads = mesh.shape["tensor"] == H and mesh.shape["dp"] == 4
    shards = shards_whole_heads if whole_heads else shards_split_heads
    in_specs = (
        P(("dp", "tensor"), None),
        P(),
        P(),
        P(None, "tensor"),
        P("tensor", None),
        P(None, "tensor"),
        P("tensor", None),
        P("dp", None),
        P("dp", None),
    )
    out_specs = (P(("dp", "tensor"), None), P("dp", None, None, None, "tensor"))
    return jax.shard_map(shards, mesh=mesh, in_specs=in_specs, out_specs=out_specs, check_vma=False)
```

```python
import functools
import math

import jax
import jax.numpy as jnp
from jax import lax
from jax.experimental import pallas as pl
from jax.experimental.pallas import tpu as pltpu
from jax.sharding import PartitionSpec as P

H = 8
HD = 256
ROT = 64
PAGE = 16


epsilon = 1e-05
rotary_base = 10000.0
key_block = 256


def shortened(array):

    def short(part):
        return part.astype(jnp.bfloat16) if part.dtype == jnp.float32 else part

    return jax.tree.map(short, array)


def swapped(block, axis, apart):
    count = lax.axis_size(axis)
    route = []
    for low in range(count):
        high = low | 1 << apart
        if high != low and high < count:
            route += [(low, high), (high, low)]
    return lax.ppermute(block, axis, route)


def layer_norm(values, gain):
    floats = values.astype(jnp.float32)
    center = jnp.mean(floats, axis=-1, keepdims=True)
    shifted = floats - center
    spread = jnp.mean(shifted * shifted, axis=-1, keepdims=True)
    return (shifted * lax.rsqrt(spread + epsilon) * gain).astype(jnp.bfloat16)


def positions_of(stream):
    indices = jnp.arange(stream.shape[0], dtype=jnp.int32)
    boundary = jnp.concatenate([jnp.ones((1,), dtype=bool), stream[1:] != stream[:-1]])
    starting = lax.cummax(jnp.where(boundary, indices, jnp.zeros_like(indices)), axis=0)
    return (indices, starting)


def rotate_heads(vectors, offsets, rotary_dims):
    half_dims = rotary_dims // 2
    frequency = jnp.exp(
        jnp.arange(half_dims, dtype=jnp.float32) * (-2.0 * math.log(rotary_base) / rotary_dims)
    )
    angles = offsets.astype(jnp.float32)[:, None] * frequency[None, :]
    cosine = jnp.cos(angles)
    sine = jnp.sin(angles)
    floats = vectors.astype(jnp.float32)
    leading = floats[..., :half_dims]
    trailing = floats[..., half_dims:rotary_dims]
    rotated = jnp.concatenate(
        [
            leading * cosine - trailing * sine,
            trailing * cosine + leading * sine,
            floats[..., rotary_dims:],
        ],
        axis=-1,
    )
    return rotated.astype(jnp.bfloat16)


def shards_split_heads(
    hidden_states,
    attention_gain,
    feedforward_gain,
    heads_weight,
    output_weight,
    upward_weight,
    downward_weight,
    segments,
    page_targets,
):
    tensor_count = lax.axis_size("tensor")
    replica_count = lax.axis_size("dp")
    tensor_index = lax.axis_index("tensor")
    quarters = tensor_count // H
    quarter_width = HD // quarters
    quarter_index = tensor_index % quarters
    stream = segments[0]
    tokens_total = stream.shape[0]
    level_count = quarters.bit_length() - 1
    normed_attention = layer_norm(hidden_states, attention_gain)
    normed_feedforward = layer_norm(hidden_states, feedforward_gain)
    shard_rows = lax.all_gather(
        (normed_attention, normed_feedforward), "tensor", axis=0, tiled=True
    )
    joined_rows = jnp.dot(shard_rows[0], heads_weight, preferred_element_type=jnp.float32).astype(
        jnp.bfloat16
    )
    upward = jnp.dot(shard_rows[1], upward_weight, preferred_element_type=jnp.float32)
    hidden_rows = jax.nn.gelu(upward, approximate=False).astype(jnp.bfloat16)
    hidden = hidden_rows
    pieces = (
        joined_rows.reshape(tokens_total, 3, quarter_width)
        .transpose(1, 0, 2)
        .reshape(1, 3, tokens_total * quarter_width)
    )
    for bit_number in range(level_count):
        partner = swapped(shortened(pieces), "tensor", bit_number).astype(pieces.dtype)
        lower = tensor_index >> bit_number & 1 == 0
        pieces = jnp.where(
            lower, jnp.concatenate([pieces, partner], 0), jnp.concatenate([partner, pieces], 0)
        )
    whole_head = (
        pieces.reshape(quarters, 3, tokens_total, quarter_width)
        .transpose(1, 2, 0, 3)
        .reshape(3, tokens_total, HD)
    )
    indices, starting = positions_of(stream)
    offsets = indices - starting
    queries = rotate_heads(whole_head[0], offsets, ROT)
    keys = rotate_heads(whole_head[1], offsets, ROT)
    values = whole_head[2]
    block_rows = tokens_total // (2 * quarters)
    score_scale = HD ** (-0.5)

    def attend_block(block_number):
        first_row = block_number * block_rows
        block_queries = lax.dynamic_slice_in_dim(queries, first_row, block_rows, 0)
        query_segments = lax.dynamic_slice_in_dim(stream, first_row, block_rows, 0)
        query_indices = first_row + jnp.arange(block_rows, dtype=jnp.int32)
        lowest = lax.dynamic_index_in_dim(starting, first_row, 0, keepdims=False) // key_block
        highest = (first_row + block_rows + key_block - 1) // key_block

        def scores_of(key_number):
            key_first = key_number * key_block
            key_indices = key_first + jnp.arange(key_block, dtype=jnp.int32)
            scores = (
                jnp.dot(block_queries, keys.T, preferred_element_type=jnp.float32) * score_scale
            )
            allowed = (stream[None, :] == query_segments[:, None]) & (
                key_indices[None, :] <= query_indices[:, None]
            )
            return (scores, allowed)

        def find_peak(key_number, peak):
            scores, allowed = scores_of(key_number)
            return jnp.maximum(peak, jnp.max(jnp.where(allowed, scores, -jnp.inf), axis=1))

        peak = lax.fori_loop(
            lowest, highest, find_peak, jnp.full((block_rows,), -jnp.inf, jnp.float32)
        )

        def accumulate(key_number, state):
            weight_sum, mixed_sum = state
            scores, allowed = scores_of(key_number)
            weights = jnp.where(allowed, jnp.exp(scores - peak[:, None]), 0.0)
            mixed_next = mixed_sum + jnp.dot(
                weights.astype(jnp.bfloat16), values, preferred_element_type=jnp.float32
            )
            return (weight_sum + jnp.sum(weights, axis=1), mixed_next)

        start_state = (
            jnp.zeros((block_rows,), jnp.float32),
            jnp.zeros((block_rows, HD), jnp.float32),
        )
        weight_sum, mixed_sum = lax.fori_loop(lowest, highest, accumulate, start_state)
        return (mixed_sum / weight_sum[:, None]).astype(jnp.bfloat16)

    own_blocks = (2 * quarter_index, 2 * quarter_index + 1)
    own_rows = jnp.concatenate([attend_block(own_blocks[0]), attend_block(own_blocks[1])], 0)[None]
    for bit_number in range(level_count):
        partner = swapped(own_rows, "tensor", bit_number)
        lower = tensor_index >> bit_number & 1 == 0
        own_rows = jnp.where(
            lower, jnp.concatenate([own_rows, partner], 0), jnp.concatenate([partner, own_rows], 0)
        )
    attended = own_rows.reshape(tokens_total, HD)
    attended_quarter = lax.dynamic_slice_in_dim(
        attended, quarter_index * quarter_width, quarter_width, 1
    )
    hidden_rows = hidden
    summed = lax.psum_scatter(
        (
            jnp.dot(attended_quarter, output_weight, preferred_element_type=jnp.float32)
            + jnp.dot(hidden_rows, downward_weight, preferred_element_type=jnp.float32)
        ).astype(jnp.bfloat16),
        "tensor",
        scatter_dimension=0,
        tiled=True,
    ).astype(jnp.float32)
    layer_output = hidden_states.astype(jnp.float32) + summed
    key_quarter = lax.dynamic_slice_in_dim(keys, quarter_index * quarter_width, quarter_width, 1)
    value_quarter = joined_rows[:, 2 * quarter_width :]
    page_count = tokens_total // PAGE
    page_rows = jnp.concatenate([key_quarter, value_quarter], 1).reshape(
        page_count, PAGE * 2 * quarter_width
    )
    targets = page_targets[:, 0]
    page_numbers = jnp.arange(page_count, dtype=jnp.int32)
    earlier = jnp.sum(
        (
            (targets[None, :] == targets[:, None]) & (page_numbers[None, :] < page_numbers[:, None])
        ).astype(jnp.int32),
        axis=1,
    )
    capacity = 2 * page_count // replica_count
    slot_numbers = targets * capacity + earlier
    placing = (
        jnp.arange(replica_count * capacity, dtype=jnp.int32)[:, None] == slot_numbers[None, :]
    ).astype(jnp.bfloat16)
    outgoing = jnp.dot(placing, page_rows, preferred_element_type=jnp.float32).astype(jnp.bfloat16)
    outgoing = outgoing.reshape(replica_count, capacity, PAGE * 2 * quarter_width)
    incoming = lax.all_to_all(outgoing, "dp", split_axis=0, concat_axis=0, tiled=True)
    cache_pages = incoming.reshape(1, replica_count, capacity, PAGE, 2 * quarter_width)
    return (layer_output, cache_pages)


CORES = 2
CHIPS = 4
MIB = 1 << 20


def in_hbm(array):
    return pltpu.with_memory_space_constraint(array, pltpu.HBM)


def exchanged(block, axis, mask):
    count = lax.axis_size(axis)
    return lax.ppermute(block, axis, [(member, member ^ mask) for member in range(count)])


def vmem_specs(count):
    return [pl.BlockSpec(memory_space=pltpu.VMEM)] * count


def parameters(mebibytes):
    return pltpu.CompilerParams(vmem_limit_bytes=mebibytes * MIB)


def whereabouts():
    member = lax.axis_index("tensor")
    return member // CORES, member % CORES


def position_of(kind, half, block_rows):
    chip, core = whereabouts()
    return ((chip ^ kind) * CORES + (core ^ half)) * block_rows


def positions_along(first, shape, axis, block_rows):
    chip, core = whereabouts()
    bits = block_rows.bit_length() - 1
    place = first + lax.broadcasted_iota(jnp.int32, shape, axis)
    kind = place >> (bits + 1)
    half = (place >> bits) & 1
    return ((((chip ^ kind) << 1) | (core ^ half)) << bits) | (place & (block_rows - 1))


def normalize(blocks, gain_refs, normed_refs):
    piece = 16
    gains = [gain_ref[...] for gain_ref in gain_refs]
    for number, block_ref in enumerate(blocks):
        block_rows = block_ref.shape[0]
        for part in range(0, block_rows, piece):
            floats = block_ref[part : part + piece, :].astype(jnp.float32)
            center = jnp.mean(floats, axis=-1, keepdims=True)
            shifted = floats - center
            spread = jnp.mean(shifted * shifted, axis=-1, keepdims=True)
            scaled = shifted * lax.rsqrt(spread + epsilon)
            first = number * block_rows + part
            for gain, normed_ref in zip(gains, normed_refs):
                normed_ref[first : first + piece, :] = (scaled * gain).astype(jnp.bfloat16)


def project(normed_ref, heads_ref, table_refs, places, joined_ref, first):
    rows = normed_ref.shape[0]
    block_rows = rows // len(places)
    for component in range(3):
        columns = slice(component * HD, (component + 1) * HD)
        joined = jnp.dot(
            normed_ref[...], heads_ref[:, columns], preferred_element_type=jnp.float32
        ).astype(jnp.bfloat16)
        joined_ref[first : first + rows, columns] = joined
        if component < 2:
            cosine, sine_down, sine_up = [
                jnp.concatenate(
                    [
                        table_ref[pl.ds(pl.multiple_of(place, block_rows), block_rows), :]
                        for place in places
                    ],
                    0,
                )
                for table_ref in table_refs
            ]
            turning = joined[:, :128].astype(jnp.float32)
            turned = (
                turning * cosine
                + pltpu.roll(turning, 128 - ROT // 2, 1) * sine_down
                + pltpu.roll(turning, ROT // 2, 1) * sine_up
            )
            joined_ref[first : first + rows, component * HD : component * HD + 128] = turned.astype(
                jnp.bfloat16
            )


def hide(normed_ref, upward_ref, hidden_ref, place):
    chunk = 256
    rows = slice(place, place + normed_ref.shape[0])
    for first in range(0, upward_ref.shape[1], chunk):
        columns = slice(first, first + chunk)
        upward = jnp.dot(
            normed_ref[...], upward_ref[:, columns], preferred_element_type=jnp.float32
        )
        hidden = 0.5 * upward * (1.0 + lax.erf(upward * (0.5**0.5)))
        hidden_ref[rows, columns] = hidden.astype(jnp.bfloat16)


def attend(joined_ref, offsets_ref, first, rows, block_rows):
    tokens = joined_ref.shape[0]
    starts = [
        position_of(place // (2 * block_rows), (place // block_rows) % 2, block_rows)
        for place in range(first, first + rows, block_rows)
    ]
    reach = jnp.concatenate(
        [
            offsets_ref[pl.ds(pl.multiple_of(start, block_rows), block_rows), :]
            for start in starts
        ],
        0,
    )[:, :1].astype(jnp.int32)
    row = positions_along(first, (rows, 1), 0, block_rows)
    column = positions_along(0, (1, tokens), 1, block_rows)
    allowed = (column <= row) & (column >= row - reach)
    scores = lax.dot_general(
        joined_ref[first : first + rows, :HD],
        joined_ref[:, HD : 2 * HD],
        (((1,), (1,)), ((), ())),
        preferred_element_type=jnp.float32,
    ) * (HD ** (-0.5))
    peak = jnp.max(jnp.where(allowed, scores, -jnp.inf), axis=1, keepdims=True)
    weights = jnp.where(allowed, jnp.exp(scores - peak), 0.0)
    weight_sum = jnp.sum(weights, axis=1, keepdims=True)
    mixed = jnp.dot(
        weights.astype(jnp.bfloat16), joined_ref[:, 2 * HD :], preferred_element_type=jnp.float32
    )
    return (mixed / weight_sum).astype(jnp.bfloat16)


def make_tables(segments_ref, offsets_ref, cosine_ref, sine_down_ref, sine_up_ref):
    tokens = segments_ref.shape[1]
    shape = (tokens, tokens)
    rows = lax.broadcasted_iota(jnp.int32, shape, 0)
    columns = lax.broadcasted_iota(jnp.int32, shape, 1)
    across = jnp.broadcast_to(segments_ref[...], shape).astype(jnp.float32)
    down = jnp.sum(jnp.where(rows == columns, across, 0.0), axis=1, keepdims=True)
    earlier = (across == down) & (columns < rows)
    offsets = jnp.sum(jnp.where(earlier, 1.0, 0.0), axis=1, keepdims=True)
    offsets_ref[...] = jnp.broadcast_to(offsets, offsets_ref.shape)
    half = ROT // 2
    lane = lax.broadcasted_iota(jnp.int32, (tokens, 128), 1)
    step = (lane & (half - 1)).astype(jnp.float32)
    frequency = jnp.exp(step * (-2.0 * math.log(rotary_base) / ROT))
    angles = offsets * frequency
    sine = jnp.sin(angles)
    cosine_ref[...] = jnp.where(lane < ROT, jnp.cos(angles), 1.0)
    sine_down_ref[...] = jnp.where(lane < half, -sine, 0.0)
    sine_up_ref[...] = jnp.where((lane >= half) & (lane < ROT), sine, 0.0)


def make_destinations(targets_ref, destinations_ref, replica_count, block_rows):
    page_count = targets_ref.shape[1]
    tokens = destinations_ref.shape[1]
    capacity = 2 * page_count // replica_count
    square = (page_count, page_count)
    rows = lax.broadcasted_iota(jnp.int32, square, 0)
    columns = lax.broadcasted_iota(jnp.int32, square, 1)
    across = jnp.broadcast_to(targets_ref[...], square).astype(jnp.float32)
    down = jnp.sum(jnp.where(rows == columns, across, 0.0), axis=1, keepdims=True)
    earlier = jnp.where((across == down) & (columns < rows), 1.0, 0.0)
    slots = jnp.sum(earlier, axis=1, keepdims=True).astype(jnp.int32)
    slots = (down.astype(jnp.int32) ^ lax.axis_index("dp")) * capacity + slots
    positions = positions_along(0, (1, tokens), 1, block_rows)
    bits = PAGE.bit_length() - 1
    pages = lax.broadcasted_iota(jnp.int32, (page_count, tokens), 0)
    chosen = jnp.where(pages == positions >> bits, slots.astype(jnp.float32), 0.0)
    slot = jnp.sum(chosen, axis=0, keepdims=True).astype(jnp.int32)
    destinations_ref[...] = slot * PAGE + (positions & (PAGE - 1))


def copies_in(sources, targets, sems):
    copies = []
    for number, (source, target) in enumerate(zip(sources, targets)):
        parts = 4 if source.shape[0] >= 256 else 1
        rows = source.shape[0] // parts
        places = [pl.ds(part * rows, rows) for part in range(parts)]
        copies.append(
            [
                pltpu.make_async_copy(source.at[place], target.at[place], sems.at[number, part])
                for part, place in enumerate(places)
            ]
        )
    for copy in sum(copies, []):
        copy.start()
    return copies


def wait_for(copies):
    for copy in copies:
        copy.wait()


def own_kernel(count, replica_count, *refs):
    sources, targets = refs[:count], refs[count : 2 * count]
    offsets_ref, *table_refs, destinations_ref, joined_ref, hidden_ref = refs[2 * count : -3]
    attention_scr, feedforward_scr, sems = refs[-3:]
    copies = copies_in(sources, targets, sems)
    segments_ref, targets_ref, states_ref, *gain_refs, heads_ref, upward_ref, _ = targets
    block_rows = states_ref.shape[0]
    wait_for(copies[0])
    make_tables(segments_ref, offsets_ref, *table_refs)
    wait_for(copies[1])
    make_destinations(targets_ref, destinations_ref, replica_count, block_rows)
    for number in (2, 3, 4):
        wait_for(copies[number])
    normalize([states_ref], gain_refs, [attention_scr, feedforward_scr])
    wait_for(copies[5])
    places = [position_of(0, 0, block_rows)]
    project(attention_scr, heads_ref, table_refs, places, joined_ref, 0)
    wait_for(copies[6])
    hide(feedforward_scr, upward_ref, hidden_ref, 0)
    wait_for(copies[7])


def own_rows(staged, replica_count):
    tokens = staged[0].shape[1]
    rows, width = staged[2].shape
    hidden_width = staged[6].shape[1]
    shapes = [pltpu.VMEM(array.shape, array.dtype) for array in staged]
    shapes += [pltpu.VMEM((tokens, 128), jnp.float32)] * 4
    shapes += [
        pltpu.VMEM((1, tokens), jnp.int32),
        pltpu.VMEM((rows, 3 * HD), jnp.bfloat16),
        pltpu.VMEM((rows, hidden_width), jnp.bfloat16),
    ]
    count = len(staged)
    return pl.pallas_call(
        functools.partial(own_kernel, count, replica_count),
        out_shape=shapes,
        in_specs=[pl.BlockSpec(memory_space=pltpu.HBM)] * count,
        out_specs=vmem_specs(len(shapes)),
        scratch_shapes=[
            pltpu.VMEM((rows, width), jnp.bfloat16),
            pltpu.VMEM((rows, width), jnp.bfloat16),
            pltpu.SemaphoreType.DMA((count, 4)),
        ],
        compiler_params=parameters(12),
        cost_estimate=pl.CostEstimate(
            flops=2 * rows * width * (3 * HD + hidden_width),
            bytes_accessed=sum(array.nbytes for array in staged),
            transcendentals=rows * hidden_width,
        ),
        name="own_rows",
    )(*[in_hbm(array) for array in staged])


def middle_kernel(origins, *refs):
    count = len(origins)
    blocks, (gain_a, gain_f, heads_ref, upward_ref) = refs[:count], refs[count : count + 4]
    table_refs, refs = refs[count + 4 : count + 7], refs[count + 7 :]
    staged = (len(refs) - 5) // 2
    sources, (joined_ref, hidden_ref), refs = refs[:staged], refs[staged:][:2], refs[staged + 2 :]
    targets, (attention_scr, feedforward_scr, sems) = refs[:staged], refs[staged:]
    copies = copies_in(sources, targets, sems)
    block_rows = blocks[0].shape[0]
    normalize(blocks, [gain_a, gain_f], [attention_scr, feedforward_scr])
    places = [position_of(kind, half, block_rows) for kind, half in origins]
    project(attention_scr, heads_ref, table_refs, places, joined_ref, 0)
    hide(feedforward_scr, upward_ref, hidden_ref, 0)
    wait_for(sum(copies, []))


def middle_rows(name, origins, blocks, gains, weights, tables, *staged):
    block_rows, width = blocks[0].shape
    rows = len(blocks) * block_rows
    hidden_width = weights[1].shape[1]
    return pl.pallas_call(
        functools.partial(middle_kernel, origins),
        out_shape=[
            pltpu.VMEM((rows, 3 * HD), jnp.bfloat16),
            pltpu.VMEM((rows, hidden_width), jnp.bfloat16),
        ]
        + [pltpu.VMEM(array.shape, array.dtype) for array in staged],
        in_specs=vmem_specs(len(blocks) + 2 + 2 + 3)
        + [pl.BlockSpec(memory_space=pltpu.HBM)] * len(staged),
        out_specs=vmem_specs(2 + len(staged)),
        scratch_shapes=[
            pltpu.VMEM((rows, width), jnp.bfloat16),
            pltpu.VMEM((rows, width), jnp.bfloat16),
            pltpu.SemaphoreType.DMA((max(len(staged), 1), 4)),
        ],
        compiler_params=parameters(12),
        cost_estimate=pl.CostEstimate(
            flops=2 * rows * width * (3 * HD + hidden_width),
            bytes_accessed=MIB,
            transcendentals=rows * hidden_width,
        ),
        name=name,
    )(*blocks, *gains, *weights, *tables, *[in_hbm(array) for array in staged])


def last_kernel(*refs):
    blocks, (gain_a, gain_f, heads_ref, upward_ref, downward_ref, output_ref) = refs[:3], refs[3:9]
    offsets_ref, *table_refs = refs[9:13]
    own_joined_ref, middle_joined_ref = refs[13:15]
    joined_ref, fed_ref, sibling_ref, own_ref = refs[15:19]
    attention_scr, feedforward_scr, hidden_scr = refs[19:]
    block_rows = blocks[0].shape[0]
    tokens = joined_ref.shape[0]
    first = tokens - len(blocks) * block_rows
    normalize(blocks, [gain_a, gain_f], [attention_scr, feedforward_scr])
    joined_ref[:block_rows, :] = own_joined_ref[...]
    joined_ref[block_rows:first, :] = middle_joined_ref[...]
    origins = ((CHIPS - 2, 1), (CHIPS - 1, 0), (CHIPS - 1, 1))
    places = [position_of(kind, half, block_rows) for kind, half in origins]
    project(attention_scr, heads_ref, table_refs, places, joined_ref, first)
    rows = CORES * block_rows
    attended = attend(joined_ref, offsets_ref, tokens - rows, rows, block_rows)
    hide(feedforward_scr, upward_ref, hidden_scr, 0)
    chunk = 512
    for begin in range(0, downward_ref.shape[1], chunk):
        columns = slice(begin, begin + chunk)
        fed = jnp.dot(hidden_scr[...], downward_ref[:, columns], preferred_element_type=jnp.float32)
        fed_ref[:, columns] = fed[:block_rows]
        partial = fed[block_rows:] + jnp.dot(
            attended, output_ref[:, columns], preferred_element_type=jnp.float32
        )
        own_ref[:, columns] = partial[:block_rows]
        sibling_ref[:, columns] = partial[block_rows:].astype(jnp.bfloat16)


def last_rows(blocks, gains, weights, tables, own_joined, middle_joined):
    block_rows, width = blocks[0].shape
    rows = len(blocks) * block_rows
    hidden_width = weights[1].shape[1]
    tokens = CHIPS * CORES * block_rows
    return pl.pallas_call(
        last_kernel,
        out_shape=[
            pltpu.VMEM((tokens, 3 * HD), jnp.bfloat16),
            pltpu.VMEM((block_rows, width), jnp.float32),
            pltpu.VMEM((block_rows, width), jnp.bfloat16),
            pltpu.VMEM((block_rows, width), jnp.float32),
        ],
        in_specs=vmem_specs(len(blocks) + 2 + 4 + 4 + 2),
        out_specs=vmem_specs(4),
        scratch_shapes=[
            pltpu.VMEM((rows, width), jnp.bfloat16),
            pltpu.VMEM((rows, width), jnp.bfloat16),
            pltpu.VMEM((rows, hidden_width), jnp.bfloat16),
        ],
        compiler_params=parameters(12),
        cost_estimate=pl.CostEstimate(
            flops=2 * rows * width * (3 * HD + HD + 2 * hidden_width),
            bytes_accessed=MIB,
            transcendentals=rows * hidden_width,
        ),
        name="last_rows",
    )(*blocks, *gains, *weights, *tables, own_joined, middle_joined)


def fed_kernel(own_hidden_ref, middle_hidden_ref, downward_ref, fed_ref):
    hidden = jnp.concatenate([own_hidden_ref[...], middle_hidden_ref[...]], 0)
    chunk = 512
    for begin in range(0, downward_ref.shape[1], chunk):
        columns = slice(begin, begin + chunk)
        fed_ref[:, columns] = jnp.dot(
            hidden, downward_ref[:, columns], preferred_element_type=jnp.float32
        )


def fed_rows(own_hidden, middle_hidden, downward_weight):
    rows = own_hidden.shape[0] + middle_hidden.shape[0]
    depth, width = downward_weight.shape
    return pl.pallas_call(
        fed_kernel,
        out_shape=pltpu.VMEM((rows, width), jnp.float32),
        in_specs=vmem_specs(3),
        out_specs=pl.BlockSpec(memory_space=pltpu.VMEM),
        compiler_params=parameters(12),
        cost_estimate=pl.CostEstimate(
            flops=2 * rows * depth * width, bytes_accessed=MIB, transcendentals=0
        ),
        name="fed_rows",
    )(own_hidden, middle_hidden, downward_weight)


def rest_kernel(joined_ref, offsets_ref, output_ref, fed_ref, fed_beside_ref, *refs):
    count = len(refs) // 2
    siblings, owns = refs[:count], refs[count:]
    block_rows = owns[0].shape[0]
    rows = fed_ref.shape[0] + fed_beside_ref.shape[0]
    attended = attend(joined_ref, offsets_ref, 0, rows, block_rows)
    chunk = 512
    for begin in range(0, output_ref.shape[1], chunk):
        columns = slice(begin, begin + chunk)
        fed = jnp.concatenate([fed_ref[:, columns], fed_beside_ref[:, columns]], 0)
        partial = fed + jnp.dot(
            attended, output_ref[:, columns], preferred_element_type=jnp.float32
        )
        for number, (sibling_ref, own_ref) in enumerate(zip(siblings, owns)):
            first = CORES * number * block_rows
            middle = first + block_rows
            own_ref[:, columns] = partial[first:middle]
            sibling_ref[:, columns] = partial[middle : middle + block_rows].astype(jnp.bfloat16)


def rest_rows(joined, offsets, output_weight, fed, fed_beside):
    width = fed.shape[1]
    rows = fed.shape[0] + fed_beside.shape[0]
    count = CHIPS - 1
    shape = (rows // (CORES * count), width)
    shapes = [pltpu.VMEM(shape, dtype) for dtype in [jnp.bfloat16] * count + [jnp.float32] * count]
    return pl.pallas_call(
        rest_kernel,
        out_shape=shapes,
        in_specs=vmem_specs(5),
        out_specs=vmem_specs(2 * count),
        compiler_params=parameters(12),
        cost_estimate=pl.CostEstimate(
            flops=2 * rows * width * HD,
            bytes_accessed=MIB,
            transcendentals=rows * joined.shape[0],
        ),
        name="rest_rows",
    )(joined, offsets, output_weight, fed, fed_beside)


def pages_kernel(joined_ref, destinations_ref, *page_refs):
    tokens = joined_ref.shape[0]
    slot_rows = page_refs[0].shape[0] * PAGE
    for number, page_ref in enumerate(page_refs):
        shape = (slot_rows, tokens)
        row = number * slot_rows + lax.broadcasted_iota(jnp.int32, shape, 0)
        placing = jnp.where(row == destinations_ref[...], 1.0, 0.0).astype(jnp.bfloat16)
        rows = jnp.dot(placing, joined_ref[:, HD:], preferred_element_type=jnp.float32)
        page_ref[...] = rows.astype(jnp.bfloat16).reshape(page_ref.shape)


def cached_pages(joined, destinations, replica_count):
    tokens = joined.shape[0]
    capacity = 2 * (tokens // PAGE) // replica_count
    shapes = [pltpu.VMEM((capacity, PAGE, 2 * HD), jnp.bfloat16)] * replica_count
    return pl.pallas_call(
        pages_kernel,
        out_shape=shapes,
        in_specs=vmem_specs(2),
        out_specs=vmem_specs(len(shapes)),
        compiler_params=parameters(8),
        cost_estimate=pl.CostEstimate(flops=0, bytes_accessed=MIB, transcendentals=0),
        name="cached_pages",
    )(joined, destinations)


def add_kernel(*refs):
    total = refs[0][...].astype(jnp.float32)
    for ref in refs[1:-1]:
        total = total + ref[...].astype(jnp.float32)
    refs[-1][...] = total.astype(refs[-1].dtype)


def added(name, *parts):
    return pl.pallas_call(
        add_kernel,
        out_shape=pltpu.VMEM(parts[0].shape, jnp.bfloat16),
        in_specs=vmem_specs(len(parts)),
        out_specs=pl.BlockSpec(memory_space=pltpu.VMEM),
        compiler_params=parameters(4),
        name=name,
    )(*parts)


def sums_kernel(passing_ref, *refs):
    zeros, ones, twos = refs[0:2], refs[2:4], refs[4:6]
    hidden_ref, second_ref, first_ref, base_ref = refs[6:]

    def total(pair, extra=None):
        received_ref, own_ref = pair
        value = own_ref[...] + received_ref[...].astype(jnp.float32)
        return value if extra is None else value + extra[...].astype(jnp.float32)

    second_ref[...] = total(twos, passing_ref).astype(jnp.bfloat16)
    first_ref[...] = total(ones).astype(jnp.bfloat16)
    base_ref[...] = total(zeros, hidden_ref)


def remaining_sums(passing, pairs, hidden):
    shape = hidden.shape
    return pl.pallas_call(
        sums_kernel,
        out_shape=[
            pltpu.VMEM(shape, jnp.bfloat16),
            pltpu.VMEM(shape, jnp.bfloat16),
            pltpu.VMEM(shape, jnp.float32),
        ],
        in_specs=vmem_specs(8),
        out_specs=vmem_specs(3),
        compiler_params=parameters(4),
        name="remaining_sums",
    )(passing, *[array for pair in pairs for array in pair], hidden)


def place_kernel(masks, *refs):
    group = lax.axis_index("dp")
    pages, (cache_ref, sems) = refs[:-2], refs[-2:]
    copies = [
        pltpu.make_async_copy(page_ref, cache_ref.at[0, group ^ mask], sems.at[number])
        for number, (mask, page_ref) in enumerate(zip(masks, pages))
    ]
    for copy in copies:
        copy.start()
    for copy in copies:
        copy.wait()


def placed(masks, pages, replica_count):
    count = len(pages)
    return pl.pallas_call(
        functools.partial(place_kernel, masks),
        out_shape=jax.ShapeDtypeStruct((1, replica_count) + pages[0].shape, pages[0].dtype),
        in_specs=[pl.BlockSpec(memory_space=pl.ANY)] * count,
        out_specs=pl.BlockSpec(memory_space=pltpu.HBM),
        scratch_shapes=[pltpu.SemaphoreType.DMA((count,))],
        compiler_params=parameters(4),
        name="placed",
    )(*pages)


def finish_kernel(masks, base_ref, *refs):
    count = len(masks)
    *parts, _, output_ref, cache_ref, total_scr, sems = refs
    parts, pages = parts[:-count], parts[-count:]
    group = lax.axis_index("dp")
    copies = [
        pltpu.make_async_copy(page_ref, cache_ref.at[0, group ^ mask], sems.at[number])
        for number, (mask, page_ref) in enumerate(zip(masks, pages))
    ]
    for copy in copies:
        copy.start()
    total = base_ref[...]
    for part_ref in parts:
        total = total + part_ref[...].astype(jnp.float32)
    total_scr[...] = total
    copies.append(pltpu.make_async_copy(total_scr, output_ref, sems.at[count]))
    copies[-1].start()
    for copy in copies:
        copy.wait()


def finished(base, parts, masks, pages, cache):
    count = len(pages)
    return pl.pallas_call(
        functools.partial(finish_kernel, masks),
        out_shape=[
            jax.ShapeDtypeStruct(base.shape, base.dtype),
            jax.ShapeDtypeStruct(cache.shape, cache.dtype),
        ],
        in_specs=vmem_specs(1 + len(parts))
        + [pl.BlockSpec(memory_space=pl.ANY)] * count
        + [pl.BlockSpec(memory_space=pltpu.HBM)],
        out_specs=[pl.BlockSpec(memory_space=pltpu.HBM)] * 2,
        scratch_shapes=[
            pltpu.VMEM(base.shape, base.dtype),
            pltpu.SemaphoreType.DMA((count + 1,)),
        ],
        input_output_aliases={1 + len(parts) + count: 1},
        compiler_params=parameters(4),
        name="finished",
    )(base, *parts, *pages, cache)


def shards_whole_heads(
    hidden_states,
    attention_gain,
    feedforward_gain,
    heads_weight,
    output_weight,
    upward_weight,
    downward_weight,
    segments,
    page_targets,
):
    replica_count = lax.axis_size("dp")
    to_chip = [mask * CORES for mask in range(CHIPS)]
    second = exchanged(hidden_states, "tensor", to_chip[2])
    first = exchanged(hidden_states, "tensor", to_chip[1])
    beside = exchanged(hidden_states, "tensor", 1)
    staged = (
        segments,
        page_targets.reshape(1, -1),
        hidden_states,
        attention_gain[None],
        feedforward_gain[None],
        heads_weight,
        upward_weight,
        downward_weight,
    )
    staged = own_rows(staged, replica_count)
    hidden, gains, weights, tables = staged[2], staged[3:5], staged[5:8], staged[8:12]
    heads, upward, downward = weights
    destinations, own_joined, own_hidden = staged[12:]

    first, second, own_joined = lax.optimization_barrier((first, second, own_joined))
    first_beside = exchanged(first, "tensor", 1)
    third = exchanged(second, "tensor", to_chip[1])
    middle_joined, middle_hidden, output = middle_rows(
        "middle_rows",
        ((0, 1), (1, 0), (1, 1), (2, 0)),
        (beside, first, first_beside, second),
        gains,
        (heads, upward),
        tables[1:],
        output_weight,
    )
    second, middle_joined = lax.optimization_barrier((second, middle_joined))
    second_beside = exchanged(second, "tensor", 1)
    third, second_beside, middle_joined, middle_hidden = lax.optimization_barrier(
        (third, second_beside, middle_joined, middle_hidden)
    )
    third_beside = exchanged(third, "tensor", 1)
    fed = fed_rows(own_hidden, middle_hidden, downward)
    third_beside, fed = lax.optimization_barrier((third_beside, fed))
    joined, fed_beside, sibling, own = last_rows(
        (second_beside, third, third_beside),
        gains,
        (heads, upward, downward, output),
        tables,
        own_joined,
        middle_joined,
    )

    received = exchanged(sibling, "tensor", 1)
    partials = rest_rows(joined, tables[0], output, fed, fed_beside)
    siblings, owns = partials[: CHIPS - 1], partials[CHIPS - 1 :]
    third_sum = added("third_added", own, received)
    third_sum, siblings, joined = lax.optimization_barrier((third_sum, siblings, joined))
    passing = exchanged(third_sum, "tensor", to_chip[1])
    pairs = [(exchanged(sibling, "tensor", 1), own) for sibling, own in zip(siblings, owns)]
    pages = cached_pages(joined, destinations, replica_count)
    early, late = (3,), (1, 2)
    arriving = [exchanged(pages[mask], "dp", mask) for mask in early]
    second_sum, first_sum, base = remaining_sums(passing, pairs, hidden)
    from_second = exchanged(second_sum, "tensor", to_chip[2])
    from_first = exchanged(first_sum, "tensor", to_chip[1])
    base, late_pages = lax.optimization_barrier((base, [pages[mask] for mask in late]))
    late_pages = [exchanged(page, "dp", mask) for mask, page in zip(late, late_pages)]
    cache_pages = placed((0,) + early, [pages[0]] + arriving, replica_count)
    return tuple(finished(base, (from_second, from_first), late, late_pages, cache_pages))


def solution(mesh):
    whole_heads = mesh.shape["tensor"] == H and mesh.shape["dp"] == 4
    shards = shards_whole_heads if whole_heads else shards_split_heads
    in_specs = (
        P(("dp", "tensor"), None),
        P(),
        P(),
        P(None, "tensor"),
        P("tensor", None),
        P(None, "tensor"),
        P("tensor", None),
        P("dp", None),
        P("dp", None),
    )
    out_specs = (P(("dp", "tensor"), None), P("dp", None, None, None, "tensor"))
    return jax.shard_map(shards, mesh=mesh, in_specs=in_specs, out_specs=out_specs, check_vma=False)
```

```python
import functools
import math

import jax
import jax.numpy as jnp
from jax import lax
from jax.experimental import pallas as pl
from jax.experimental.pallas import tpu as pltpu
from jax.sharding import PartitionSpec as P

H = 8
HD = 256
ROT = 64
PAGE = 16


epsilon = 1e-05
rotary_base = 10000.0
key_block = 256


def shortened(array):

    def short(part):
        return part.astype(jnp.bfloat16) if part.dtype == jnp.float32 else part

    return jax.tree.map(short, array)


def swapped(block, axis, apart):
    count = lax.axis_size(axis)
    route = []
    for low in range(count):
        high = low | 1 << apart
        if high != low and high < count:
            route += [(low, high), (high, low)]
    return lax.ppermute(block, axis, route)


def layer_norm(values, gain):
    floats = values.astype(jnp.float32)
    center = jnp.mean(floats, axis=-1, keepdims=True)
    shifted = floats - center
    spread = jnp.mean(shifted * shifted, axis=-1, keepdims=True)
    return (shifted * lax.rsqrt(spread + epsilon) * gain).astype(jnp.bfloat16)


def positions_of(stream):
    indices = jnp.arange(stream.shape[0], dtype=jnp.int32)
    boundary = jnp.concatenate([jnp.ones((1,), dtype=bool), stream[1:] != stream[:-1]])
    starting = lax.cummax(jnp.where(boundary, indices, jnp.zeros_like(indices)), axis=0)
    return (indices, starting)


def rotate_heads(vectors, offsets, rotary_dims):
    half_dims = rotary_dims // 2
    frequency = jnp.exp(
        jnp.arange(half_dims, dtype=jnp.float32) * (-2.0 * math.log(rotary_base) / rotary_dims)
    )
    angles = offsets.astype(jnp.float32)[:, None] * frequency[None, :]
    cosine = jnp.cos(angles)
    sine = jnp.sin(angles)
    floats = vectors.astype(jnp.float32)
    leading = floats[..., :half_dims]
    trailing = floats[..., half_dims:rotary_dims]
    rotated = jnp.concatenate(
        [
            leading * cosine - trailing * sine,
            trailing * cosine + leading * sine,
            floats[..., rotary_dims:],
        ],
        axis=-1,
    )
    return rotated.astype(jnp.bfloat16)


def shards_split_heads(
    hidden_states,
    attention_gain,
    feedforward_gain,
    heads_weight,
    output_weight,
    upward_weight,
    downward_weight,
    segments,
    page_targets,
):
    tensor_count = lax.axis_size("tensor")
    replica_count = lax.axis_size("dp")
    tensor_index = lax.axis_index("tensor")
    quarters = tensor_count // H
    quarter_width = HD // quarters
    quarter_index = tensor_index % quarters
    stream = segments[0]
    tokens_total = stream.shape[0]
    level_count = quarters.bit_length() - 1
    normed_attention = layer_norm(hidden_states, attention_gain)
    normed_feedforward = layer_norm(hidden_states, feedforward_gain)
    shard_rows = lax.all_gather(
        (normed_attention, normed_feedforward), "tensor", axis=0, tiled=True
    )
    joined_rows = jnp.dot(shard_rows[0], heads_weight, preferred_element_type=jnp.float32).astype(
        jnp.bfloat16
    )
    upward = jnp.dot(shard_rows[1], upward_weight, preferred_element_type=jnp.float32)
    hidden_rows = jax.nn.gelu(upward, approximate=False).astype(jnp.bfloat16)
    hidden = hidden_rows
    pieces = (
        joined_rows.reshape(tokens_total, 3, quarter_width)
        .transpose(1, 0, 2)
        .reshape(1, 3, tokens_total * quarter_width)
    )
    for bit_number in range(level_count):
        partner = swapped(shortened(pieces), "tensor", bit_number).astype(pieces.dtype)
        lower = tensor_index >> bit_number & 1 == 0
        pieces = jnp.where(
            lower, jnp.concatenate([pieces, partner], 0), jnp.concatenate([partner, pieces], 0)
        )
    whole_head = (
        pieces.reshape(quarters, 3, tokens_total, quarter_width)
        .transpose(1, 2, 0, 3)
        .reshape(3, tokens_total, HD)
    )
    indices, starting = positions_of(stream)
    offsets = indices - starting
    queries = rotate_heads(whole_head[0], offsets, ROT)
    keys = rotate_heads(whole_head[1], offsets, ROT)
    values = whole_head[2]
    block_rows = tokens_total // (2 * quarters)
    score_scale = HD ** (-0.5)

    def attend_block(block_number):
        first_row = block_number * block_rows
        block_queries = lax.dynamic_slice_in_dim(queries, first_row, block_rows, 0)
        query_segments = lax.dynamic_slice_in_dim(stream, first_row, block_rows, 0)
        query_indices = first_row + jnp.arange(block_rows, dtype=jnp.int32)
        lowest = lax.dynamic_index_in_dim(starting, first_row, 0, keepdims=False) // key_block
        highest = (first_row + block_rows + key_block - 1) // key_block

        def scores_of(key_number):
            key_first = key_number * key_block
            key_indices = key_first + jnp.arange(key_block, dtype=jnp.int32)
            scores = (
                jnp.dot(block_queries, keys.T, preferred_element_type=jnp.float32) * score_scale
            )
            allowed = (stream[None, :] == query_segments[:, None]) & (
                key_indices[None, :] <= query_indices[:, None]
            )
            return (scores, allowed)

        def find_peak(key_number, peak):
            scores, allowed = scores_of(key_number)
            return jnp.maximum(peak, jnp.max(jnp.where(allowed, scores, -jnp.inf), axis=1))

        peak = lax.fori_loop(
            lowest, highest, find_peak, jnp.full((block_rows,), -jnp.inf, jnp.float32)
        )

        def accumulate(key_number, state):
            weight_sum, mixed_sum = state
            scores, allowed = scores_of(key_number)
            weights = jnp.where(allowed, jnp.exp(scores - peak[:, None]), 0.0)
            mixed_next = mixed_sum + jnp.dot(
                weights.astype(jnp.bfloat16), values, preferred_element_type=jnp.float32
            )
            return (weight_sum + jnp.sum(weights, axis=1), mixed_next)

        start_state = (
            jnp.zeros((block_rows,), jnp.float32),
            jnp.zeros((block_rows, HD), jnp.float32),
        )
        weight_sum, mixed_sum = lax.fori_loop(lowest, highest, accumulate, start_state)
        return (mixed_sum / weight_sum[:, None]).astype(jnp.bfloat16)

    own_blocks = (2 * quarter_index, 2 * quarter_index + 1)
    own_rows = jnp.concatenate([attend_block(own_blocks[0]), attend_block(own_blocks[1])], 0)[None]
    for bit_number in range(level_count):
        partner = swapped(own_rows, "tensor", bit_number)
        lower = tensor_index >> bit_number & 1 == 0
        own_rows = jnp.where(
            lower, jnp.concatenate([own_rows, partner], 0), jnp.concatenate([partner, own_rows], 0)
        )
    attended = own_rows.reshape(tokens_total, HD)
    attended_quarter = lax.dynamic_slice_in_dim(
        attended, quarter_index * quarter_width, quarter_width, 1
    )
    hidden_rows = hidden
    summed = lax.psum_scatter(
        (
            jnp.dot(attended_quarter, output_weight, preferred_element_type=jnp.float32)
            + jnp.dot(hidden_rows, downward_weight, preferred_element_type=jnp.float32)
        ).astype(jnp.bfloat16),
        "tensor",
        scatter_dimension=0,
        tiled=True,
    ).astype(jnp.float32)
    layer_output = hidden_states.astype(jnp.float32) + summed
    key_quarter = lax.dynamic_slice_in_dim(keys, quarter_index * quarter_width, quarter_width, 1)
    value_quarter = joined_rows[:, 2 * quarter_width :]
    page_count = tokens_total // PAGE
    page_rows = jnp.concatenate([key_quarter, value_quarter], 1).reshape(
        page_count, PAGE * 2 * quarter_width
    )
    targets = page_targets[:, 0]
    page_numbers = jnp.arange(page_count, dtype=jnp.int32)
    earlier = jnp.sum(
        (
            (targets[None, :] == targets[:, None]) & (page_numbers[None, :] < page_numbers[:, None])
        ).astype(jnp.int32),
        axis=1,
    )
    capacity = 2 * page_count // replica_count
    slot_numbers = targets * capacity + earlier
    placing = (
        jnp.arange(replica_count * capacity, dtype=jnp.int32)[:, None] == slot_numbers[None, :]
    ).astype(jnp.bfloat16)
    outgoing = jnp.dot(placing, page_rows, preferred_element_type=jnp.float32).astype(jnp.bfloat16)
    outgoing = outgoing.reshape(replica_count, capacity, PAGE * 2 * quarter_width)
    incoming = lax.all_to_all(outgoing, "dp", split_axis=0, concat_axis=0, tiled=True)
    cache_pages = incoming.reshape(1, replica_count, capacity, PAGE, 2 * quarter_width)
    return (layer_output, cache_pages)


CORES = 2
CHIPS = 4
MIB = 1 << 20


def in_hbm(array):
    return pltpu.with_memory_space_constraint(array, pltpu.HBM)


def exchanged(block, axis, mask):
    count = lax.axis_size(axis)
    return lax.ppermute(block, axis, [(member, member ^ mask) for member in range(count)])


def vmem_specs(count):
    return [pl.BlockSpec(memory_space=pltpu.VMEM)] * count


def parameters(mebibytes):
    return pltpu.CompilerParams(vmem_limit_bytes=mebibytes * MIB)


def whereabouts():
    member = lax.axis_index("tensor")
    return member // CORES, member % CORES


def position_of(kind, half, block_rows):
    chip, core = whereabouts()
    return ((chip ^ kind) * CORES + (core ^ half)) * block_rows


def positions_along(first, shape, axis, block_rows):
    chip, core = whereabouts()
    bits = block_rows.bit_length() - 1
    place = first + lax.broadcasted_iota(jnp.int32, shape, axis)
    kind = place >> (bits + 1)
    half = (place >> bits) & 1
    return ((((chip ^ kind) << 1) | (core ^ half)) << bits) | (place & (block_rows - 1))


def normalize(blocks, gain_refs, normed_refs, place=0):
    piece = 16
    gains = [gain_ref[...] for gain_ref in gain_refs]
    for number, block_ref in enumerate(blocks):
        block_rows = block_ref.shape[0]
        for part in range(0, block_rows, piece):
            floats = block_ref[part : part + piece, :].astype(jnp.float32)
            center = jnp.mean(floats, axis=-1, keepdims=True)
            shifted = floats - center
            spread = jnp.mean(shifted * shifted, axis=-1, keepdims=True)
            scaled = shifted * lax.rsqrt(spread + epsilon)
            first = place + number * block_rows + part
            for gain, normed_ref in zip(gains, normed_refs):
                normed_ref[first : first + piece, :] = (scaled * gain).astype(jnp.bfloat16)


def project(normed_ref, heads_ref, table_refs, places, joined_ref, first):
    rows = normed_ref.shape[0]
    block_rows = rows // len(places)
    own = slice(first, first + rows)
    cosine, sine_down, sine_up = [
        jnp.concatenate(
            [
                table_ref[pl.ds(pl.multiple_of(place, block_rows), block_rows), :]
                for place in places
            ],
            0,
        )
        for table_ref in table_refs
    ]
    joined_ref[own, :] = jnp.dot(
        normed_ref[...], heads_ref[...], preferred_element_type=jnp.float32
    ).astype(jnp.bfloat16)
    for begin in (0, HD):
        columns = slice(begin, begin + 128)
        turning = joined_ref[own, columns].astype(jnp.float32)
        turned = (
            turning * cosine
            + pltpu.roll(turning, 128 - ROT // 2, 1) * sine_down
            + pltpu.roll(turning, ROT // 2, 1) * sine_up
        )
        joined_ref[own, columns] = turned.astype(jnp.bfloat16)


def hide(normed_ref, upward_ref, hidden_ref, place, chunk=256):
    rows = slice(place, place + normed_ref.shape[0])
    for first in range(0, upward_ref.shape[1], chunk):
        columns = slice(first, first + chunk)
        upward = jnp.dot(
            normed_ref[...], upward_ref[:, columns], preferred_element_type=jnp.float32
        )
        hidden = 0.5 * upward * (1.0 + lax.erf(upward * (0.5**0.5)))
        hidden_ref[rows, columns] = hidden.astype(jnp.bfloat16)


def attend(joined_ref, offsets_ref, first, rows, block_rows):
    tokens = joined_ref.shape[0]
    starts = [
        position_of(place // (2 * block_rows), (place // block_rows) % 2, block_rows)
        for place in range(first, first + rows, block_rows)
    ]
    reach = jnp.concatenate(
        [
            offsets_ref[pl.ds(pl.multiple_of(start, block_rows), block_rows), :]
            for start in starts
        ],
        0,
    )[:, :1].astype(jnp.int32)
    row = positions_along(first, (rows, 1), 0, block_rows)
    column = positions_along(0, (1, tokens), 1, block_rows)
    allowed = (column <= row) & (column >= row - reach)
    scores = lax.dot_general(
        joined_ref[first : first + rows, :HD],
        joined_ref[:, HD : 2 * HD],
        (((1,), (1,)), ((), ())),
        preferred_element_type=jnp.float32,
    ) * (HD ** (-0.5))
    peak = jnp.max(jnp.where(allowed, scores, -jnp.inf), axis=1, keepdims=True)
    weights = jnp.where(allowed, jnp.exp(scores - peak), 0.0)
    weight_sum = jnp.sum(weights, axis=1, keepdims=True)
    mixed = jnp.dot(
        weights.astype(jnp.bfloat16), joined_ref[:, 2 * HD :], preferred_element_type=jnp.float32
    )
    return (mixed / weight_sum).astype(jnp.bfloat16)


def make_tables(segments_ref, offsets_ref, cosine_ref, sine_down_ref, sine_up_ref):
    tokens = segments_ref.shape[1]
    shape = (tokens, tokens)
    rows = lax.broadcasted_iota(jnp.int32, shape, 0)
    columns = lax.broadcasted_iota(jnp.int32, shape, 1)
    across = jnp.broadcast_to(segments_ref[...], shape).astype(jnp.float32)
    down = jnp.sum(jnp.where(rows == columns, across, 0.0), axis=1, keepdims=True)
    earlier = (across == down) & (columns < rows)
    offsets = jnp.sum(jnp.where(earlier, 1.0, 0.0), axis=1, keepdims=True)
    offsets_ref[...] = jnp.broadcast_to(offsets, offsets_ref.shape)
    half = ROT // 2
    lane = lax.broadcasted_iota(jnp.int32, (tokens, 128), 1)
    step = (lane & (half - 1)).astype(jnp.float32)
    frequency = jnp.exp(step * (-2.0 * math.log(rotary_base) / ROT))
    angles = offsets * frequency
    sine = jnp.sin(angles)
    cosine_ref[...] = jnp.where(lane < ROT, jnp.cos(angles), 1.0)
    sine_down_ref[...] = jnp.where(lane < half, -sine, 0.0)
    sine_up_ref[...] = jnp.where((lane >= half) & (lane < ROT), sine, 0.0)


def make_destinations(targets_ref, destinations_ref, replica_count, block_rows):
    page_count = targets_ref.shape[1]
    tokens = destinations_ref.shape[1]
    capacity = 2 * page_count // replica_count
    square = (page_count, page_count)
    rows = lax.broadcasted_iota(jnp.int32, square, 0)
    columns = lax.broadcasted_iota(jnp.int32, square, 1)
    across = jnp.broadcast_to(targets_ref[...], square).astype(jnp.float32)
    down = jnp.sum(jnp.where(rows == columns, across, 0.0), axis=1, keepdims=True)
    earlier = jnp.where((across == down) & (columns < rows), 1.0, 0.0)
    slots = jnp.sum(earlier, axis=1, keepdims=True).astype(jnp.int32)
    slots = (down.astype(jnp.int32) ^ lax.axis_index("dp")) * capacity + slots
    positions = positions_along(0, (1, tokens), 1, block_rows)
    bits = PAGE.bit_length() - 1
    pages = lax.broadcasted_iota(jnp.int32, (page_count, tokens), 0)
    chosen = jnp.where(pages == positions >> bits, slots.astype(jnp.float32), 0.0)
    slot = jnp.sum(chosen, axis=0, keepdims=True).astype(jnp.int32)
    destinations_ref[...] = slot * PAGE + (positions & (PAGE - 1))


def copies_in(sources, targets, sems):
    copies = []
    for number, (source, target) in enumerate(zip(sources, targets)):
        parts = 4 if source.shape[0] >= 256 else 1
        rows = source.shape[0] // parts
        places = [pl.ds(part * rows, rows) for part in range(parts)]
        copies.append(
            [
                pltpu.make_async_copy(source.at[place], target.at[place], sems.at[number, part])
                for part, place in enumerate(places)
            ]
        )
    for copy in sum(copies, []):
        copy.start()
    return copies


def wait_for(copies):
    for copy in copies:
        copy.wait()


def own_kernel(count, replica_count, *refs):
    sources, targets = refs[:count], refs[count : 2 * count]
    offsets_ref, *table_refs, destinations_ref, joined_ref, hidden_ref = refs[2 * count : -3]
    attention_scr, feedforward_scr, sems = refs[-3:]
    copies = copies_in(sources, targets, sems)
    segments_ref, targets_ref, states_ref, *gain_refs, heads_ref, upward_ref, _ = targets
    block_rows = states_ref.shape[0]
    wait_for(copies[0])
    make_tables(segments_ref, offsets_ref, *table_refs)
    wait_for(copies[1])
    make_destinations(targets_ref, destinations_ref, replica_count, block_rows)
    for number in (2, 3, 4):
        wait_for(copies[number])
    normalize([states_ref], gain_refs, [attention_scr, feedforward_scr])
    wait_for(copies[5])
    places = [position_of(0, 0, block_rows)]
    project(attention_scr, heads_ref, table_refs, places, joined_ref, 0)
    wait_for(copies[6])
    hide(feedforward_scr, upward_ref, hidden_ref, 0)
    wait_for(copies[7])


def own_rows(staged, replica_count):
    tokens = staged[0].shape[1]
    rows, width = staged[2].shape
    hidden_width = staged[6].shape[1]
    shapes = [pltpu.VMEM(array.shape, array.dtype) for array in staged]
    shapes += [pltpu.VMEM((tokens, 128), jnp.float32)] * 4
    shapes += [
        pltpu.VMEM((1, tokens), jnp.int32),
        pltpu.VMEM((rows, 3 * HD), jnp.bfloat16),
        pltpu.VMEM((rows, hidden_width), jnp.bfloat16),
    ]
    count = len(staged)
    return pl.pallas_call(
        functools.partial(own_kernel, count, replica_count),
        out_shape=shapes,
        in_specs=[pl.BlockSpec(memory_space=pltpu.HBM)] * count,
        out_specs=vmem_specs(len(shapes)),
        scratch_shapes=[
            pltpu.VMEM((rows, width), jnp.bfloat16),
            pltpu.VMEM((rows, width), jnp.bfloat16),
            pltpu.SemaphoreType.DMA((count, 4)),
        ],
        compiler_params=parameters(12),
        cost_estimate=pl.CostEstimate(
            flops=2 * rows * width * (3 * HD + hidden_width),
            bytes_accessed=sum(array.nbytes for array in staged),
            transcendentals=rows * hidden_width,
        ),
        name="own_rows",
    )(*[in_hbm(array) for array in staged])


def middle_kernel(origins, *refs):
    count = len(origins)
    blocks, (gain_a, gain_f, heads_ref, upward_ref) = refs[:count], refs[count : count + 4]
    table_refs, refs = refs[count + 4 : count + 7], refs[count + 7 :]
    staged = (len(refs) - 5) // 2
    sources, (joined_ref, hidden_ref), refs = refs[:staged], refs[staged:][:2], refs[staged + 2 :]
    targets, (attention_scr, feedforward_scr, sems) = refs[:staged], refs[staged:]
    copies = copies_in(sources, targets, sems)
    block_rows = blocks[0].shape[0]
    normalize(blocks, [gain_a, gain_f], [attention_scr, feedforward_scr])
    places = [position_of(kind, half, block_rows) for kind, half in origins]
    project(attention_scr, heads_ref, table_refs, places, joined_ref, 0)
    hide(feedforward_scr, upward_ref, hidden_ref, 0)
    wait_for(sum(copies, []))


def middle_rows(name, origins, blocks, gains, weights, tables, *staged):
    block_rows, width = blocks[0].shape
    rows = len(blocks) * block_rows
    hidden_width = weights[1].shape[1]
    return pl.pallas_call(
        functools.partial(middle_kernel, origins),
        out_shape=[
            pltpu.VMEM((rows, 3 * HD), jnp.bfloat16),
            pltpu.VMEM((rows, hidden_width), jnp.bfloat16),
        ]
        + [pltpu.VMEM(array.shape, array.dtype) for array in staged],
        in_specs=vmem_specs(len(blocks) + 2 + 2 + 3)
        + [pl.BlockSpec(memory_space=pltpu.HBM)] * len(staged),
        out_specs=vmem_specs(2 + len(staged)),
        scratch_shapes=[
            pltpu.VMEM((rows, width), jnp.bfloat16),
            pltpu.VMEM((rows, width), jnp.bfloat16),
            pltpu.SemaphoreType.DMA((max(len(staged), 1), 4)),
        ],
        compiler_params=parameters(12),
        cost_estimate=pl.CostEstimate(
            flops=2 * rows * width * (3 * HD + hidden_width),
            bytes_accessed=MIB,
            transcendentals=rows * hidden_width,
        ),
        name=name,
    )(*blocks, *gains, *weights, *tables, *[in_hbm(array) for array in staged])


def last_kernel(*refs):
    block_ref, *normed_refs = refs[:3]
    gain_a, gain_f, heads_ref, upward_ref, downward_ref, output_ref = refs[3:9]
    offsets_ref, *table_refs = refs[9:13]
    own_joined_ref, middle_joined_ref = refs[13:15]
    joined_ref, fed_ref, sibling_ref, own_ref = refs[15:19]
    attention_scr, feedforward_scr, hidden_scr = refs[19:]
    block_rows = block_ref.shape[0]
    tokens = joined_ref.shape[0]
    first = tokens - attention_scr.shape[0]
    count = normed_refs[0].shape[0]
    normalize([block_ref], [gain_a, gain_f], [attention_scr, feedforward_scr], count)
    for normed_ref, normed_scr in zip(normed_refs, (attention_scr, feedforward_scr)):
        normed_scr[:count, :] = normed_ref[...]
    joined_ref[:block_rows, :] = own_joined_ref[...]
    joined_ref[block_rows:first, :] = middle_joined_ref[...]
    origins = ((CHIPS - 2, 1), (CHIPS - 1, 0), (CHIPS - 1, 1))
    places = [position_of(kind, half, block_rows) for kind, half in origins]
    project(attention_scr, heads_ref, table_refs, places, joined_ref, first)
    rows = CORES * block_rows
    hide(feedforward_scr, upward_ref, hidden_scr, 0, 512)
    attended = attend(joined_ref, offsets_ref, tokens - rows, rows, block_rows)
    chunk = 1024
    for begin in range(0, downward_ref.shape[1], chunk):
        columns = slice(begin, begin + chunk)
        fed = jnp.dot(hidden_scr[...], downward_ref[:, columns], preferred_element_type=jnp.float32)
        fed_ref[:, columns] = fed[:block_rows]
        partial = fed[block_rows:] + jnp.dot(
            attended, output_ref[:, columns], preferred_element_type=jnp.float32
        )
        own_ref[:, columns] = partial[:block_rows]
        sibling_ref[:, columns] = partial[block_rows:].astype(jnp.bfloat16)


def last_rows(block, normed, gains, weights, tables, own_joined, middle_joined):
    block_rows, width = block.shape
    rows = normed[0].shape[0] + block_rows
    hidden_width = weights[1].shape[1]
    tokens = CHIPS * CORES * block_rows
    return pl.pallas_call(
        last_kernel,
        out_shape=[
            pltpu.VMEM((tokens, 3 * HD), jnp.bfloat16),
            pltpu.VMEM((block_rows, width), jnp.float32),
            pltpu.VMEM((block_rows, width), jnp.bfloat16),
            pltpu.VMEM((block_rows, width), jnp.float32),
        ],
        in_specs=vmem_specs(1 + 2 + 2 + 4 + 4 + 2),
        out_specs=vmem_specs(4),
        scratch_shapes=[
            pltpu.VMEM((rows, width), jnp.bfloat16),
            pltpu.VMEM((rows, width), jnp.bfloat16),
            pltpu.VMEM((rows, hidden_width), jnp.bfloat16),
        ],
        compiler_params=parameters(12),
        cost_estimate=pl.CostEstimate(
            flops=2 * rows * width * (3 * HD + HD + 2 * hidden_width),
            bytes_accessed=MIB,
            transcendentals=rows * hidden_width,
        ),
        name="last_rows",
    )(block, *normed, *gains, *weights, *tables, own_joined, middle_joined)


def fed_kernel(own_hidden_ref, middle_hidden_ref, downward_ref, *refs):
    blocks, gain_refs, (fed_ref, *normed_refs) = refs[:2], refs[2:4], refs[4:]
    normalize(blocks, gain_refs, normed_refs)
    hidden = jnp.concatenate([own_hidden_ref[...], middle_hidden_ref[...]], 0)
    chunk = 512
    for begin in range(0, downward_ref.shape[1], chunk):
        columns = slice(begin, begin + chunk)
        fed_ref[:, columns] = jnp.dot(
            hidden, downward_ref[:, columns], preferred_element_type=jnp.float32
        )


def fed_rows(own_hidden, middle_hidden, downward_weight, blocks, gains):
    rows = own_hidden.shape[0] + middle_hidden.shape[0]
    depth, width = downward_weight.shape
    normed = pltpu.VMEM((len(blocks) * blocks[0].shape[0], width), jnp.bfloat16)
    return pl.pallas_call(
        fed_kernel,
        out_shape=[pltpu.VMEM((rows, width), jnp.float32), normed, normed],
        in_specs=vmem_specs(7),
        out_specs=vmem_specs(3),
        compiler_params=parameters(12),
        cost_estimate=pl.CostEstimate(
            flops=2 * rows * depth * width, bytes_accessed=MIB, transcendentals=0
        ),
        name="fed_rows",
    )(own_hidden, middle_hidden, downward_weight, *blocks, *gains)


def rest_kernel(joined_ref, offsets_ref, output_ref, fed_ref, fed_beside_ref, *refs):
    count = len(refs) // 2
    siblings, owns = refs[:count], refs[count:]
    block_rows = owns[0].shape[0]
    rows = fed_ref.shape[0] + fed_beside_ref.shape[0]
    attended = attend(joined_ref, offsets_ref, 0, rows, block_rows)
    chunk = 512
    for begin in range(0, output_ref.shape[1], chunk):
        columns = slice(begin, begin + chunk)
        fed = jnp.concatenate([fed_ref[:, columns], fed_beside_ref[:, columns]], 0)
        partial = fed + jnp.dot(
            attended, output_ref[:, columns], preferred_element_type=jnp.float32
        )
        for number, (sibling_ref, own_ref) in enumerate(zip(siblings, owns)):
            first = CORES * number * block_rows
            middle = first + block_rows
            own_ref[:, columns] = partial[first:middle]
            sibling_ref[:, columns] = partial[middle : middle + block_rows].astype(jnp.bfloat16)


def rest_rows(joined, offsets, output_weight, fed, fed_beside):
    width = fed.shape[1]
    rows = fed.shape[0] + fed_beside.shape[0]
    count = CHIPS - 1
    shape = (rows // (CORES * count), width)
    shapes = [pltpu.VMEM(shape, dtype) for dtype in [jnp.bfloat16] * count + [jnp.float32] * count]
    return pl.pallas_call(
        rest_kernel,
        out_shape=shapes,
        in_specs=vmem_specs(5),
        out_specs=vmem_specs(2 * count),
        compiler_params=parameters(12),
        cost_estimate=pl.CostEstimate(
            flops=2 * rows * width * HD,
            bytes_accessed=MIB,
            transcendentals=rows * joined.shape[0],
        ),
        name="rest_rows",
    )(joined, offsets, output_weight, fed, fed_beside)


def pages_kernel(joined_ref, destinations_ref, *page_refs):
    tokens = joined_ref.shape[0]
    slot_rows = page_refs[0].shape[0] * PAGE
    for number, page_ref in enumerate(page_refs):
        shape = (slot_rows, tokens)
        row = number * slot_rows + lax.broadcasted_iota(jnp.int32, shape, 0)
        placing = jnp.where(row == destinations_ref[...], 1.0, 0.0).astype(jnp.bfloat16)
        rows = jnp.dot(placing, joined_ref[:, HD:], preferred_element_type=jnp.float32)
        page_ref[...] = rows.astype(jnp.bfloat16).reshape(page_ref.shape)


def cached_pages(joined, destinations, replica_count):
    tokens = joined.shape[0]
    capacity = 2 * (tokens // PAGE) // replica_count
    shapes = [pltpu.VMEM((capacity, PAGE, 2 * HD), jnp.bfloat16)] * replica_count
    return pl.pallas_call(
        pages_kernel,
        out_shape=shapes,
        in_specs=vmem_specs(2),
        out_specs=vmem_specs(len(shapes)),
        compiler_params=parameters(8),
        cost_estimate=pl.CostEstimate(flops=0, bytes_accessed=MIB, transcendentals=0),
        name="cached_pages",
    )(joined, destinations)


def add_kernel(*refs):
    total = refs[0][...].astype(jnp.float32)
    for ref in refs[1:-1]:
        total = total + ref[...].astype(jnp.float32)
    refs[-1][...] = total.astype(refs[-1].dtype)


def added(name, *parts):
    return pl.pallas_call(
        add_kernel,
        out_shape=pltpu.VMEM(parts[0].shape, jnp.bfloat16),
        in_specs=vmem_specs(len(parts)),
        out_specs=pl.BlockSpec(memory_space=pltpu.VMEM),
        compiler_params=parameters(4),
        name=name,
    )(*parts)


def sums_kernel(passing_ref, *refs):
    zeros, ones, twos = refs[0:2], refs[2:4], refs[4:6]
    hidden_ref, second_ref, first_ref, base_ref = refs[6:]

    def total(pair, extra=None):
        received_ref, own_ref = pair
        value = own_ref[...] + received_ref[...].astype(jnp.float32)
        return value if extra is None else value + extra[...].astype(jnp.float32)

    second_ref[...] = total(twos, passing_ref).astype(jnp.bfloat16)
    first_ref[...] = total(ones).astype(jnp.bfloat16)
    base_ref[...] = total(zeros, hidden_ref)


def remaining_sums(passing, pairs, hidden):
    shape = hidden.shape
    return pl.pallas_call(
        sums_kernel,
        out_shape=[
            pltpu.VMEM(shape, jnp.bfloat16),
            pltpu.VMEM(shape, jnp.bfloat16),
            pltpu.VMEM(shape, jnp.float32),
        ],
        in_specs=vmem_specs(8),
        out_specs=vmem_specs(3),
        compiler_params=parameters(4),
        name="remaining_sums",
    )(passing, *[array for pair in pairs for array in pair], hidden)


def place_kernel(masks, *refs):
    group = lax.axis_index("dp")
    pages, (cache_ref, sems) = refs[:-2], refs[-2:]
    copies = [
        pltpu.make_async_copy(page_ref, cache_ref.at[0, group ^ mask], sems.at[number])
        for number, (mask, page_ref) in enumerate(zip(masks, pages))
    ]
    for copy in copies:
        copy.start()
    for copy in copies:
        copy.wait()


def placed(masks, pages, replica_count):
    count = len(pages)
    return pl.pallas_call(
        functools.partial(place_kernel, masks),
        out_shape=jax.ShapeDtypeStruct((1, replica_count) + pages[0].shape, pages[0].dtype),
        in_specs=[pl.BlockSpec(memory_space=pl.ANY)] * count,
        out_specs=pl.BlockSpec(memory_space=pltpu.HBM),
        scratch_shapes=[pltpu.SemaphoreType.DMA((count,))],
        compiler_params=parameters(4),
        name="placed",
    )(*pages)


def finish_kernel(masks, base_ref, *refs):
    count = len(masks)
    *parts, _, output_ref, cache_ref, total_scr, sems = refs
    parts, pages = parts[:-count], parts[-count:]
    group = lax.axis_index("dp")
    copies = [
        pltpu.make_async_copy(page_ref, cache_ref.at[0, group ^ mask], sems.at[number])
        for number, (mask, page_ref) in enumerate(zip(masks, pages))
    ]
    for copy in copies:
        copy.start()
    total = base_ref[...]
    for part_ref in parts:
        total = total + part_ref[...].astype(jnp.float32)
    total_scr[...] = total
    copies.append(pltpu.make_async_copy(total_scr, output_ref, sems.at[count]))
    copies[-1].start()
    for copy in copies:
        copy.wait()


def finished(base, parts, masks, pages, cache):
    count = len(pages)
    return pl.pallas_call(
        functools.partial(finish_kernel, masks),
        out_shape=[
            jax.ShapeDtypeStruct(base.shape, base.dtype),
            jax.ShapeDtypeStruct(cache.shape, cache.dtype),
        ],
        in_specs=vmem_specs(1 + len(parts))
        + [pl.BlockSpec(memory_space=pl.ANY)] * count
        + [pl.BlockSpec(memory_space=pltpu.HBM)],
        out_specs=[pl.BlockSpec(memory_space=pltpu.HBM)] * 2,
        scratch_shapes=[
            pltpu.VMEM(base.shape, base.dtype),
            pltpu.SemaphoreType.DMA((count + 1,)),
        ],
        input_output_aliases={1 + len(parts) + count: 1},
        compiler_params=parameters(4),
        name="finished",
    )(base, *parts, *pages, cache)


def shards_whole_heads(
    hidden_states,
    attention_gain,
    feedforward_gain,
    heads_weight,
    output_weight,
    upward_weight,
    downward_weight,
    segments,
    page_targets,
):
    replica_count = lax.axis_size("dp")
    to_chip = [mask * CORES for mask in range(CHIPS)]
    second = exchanged(hidden_states, "tensor", to_chip[2])
    first = exchanged(hidden_states, "tensor", to_chip[1])
    beside = exchanged(hidden_states, "tensor", 1)
    staged = (
        segments,
        page_targets.reshape(1, -1),
        hidden_states,
        attention_gain[None],
        feedforward_gain[None],
        heads_weight,
        upward_weight,
        downward_weight,
    )
    staged = own_rows(staged, replica_count)
    hidden, gains, weights, tables = staged[2], staged[3:5], staged[5:8], staged[8:12]
    heads, upward, downward = weights
    destinations, own_joined, own_hidden = staged[12:]

    first, second, own_joined = lax.optimization_barrier((first, second, own_joined))
    first_beside = exchanged(first, "tensor", 1)
    third = exchanged(second, "tensor", to_chip[1])
    middle_joined, middle_hidden, output = middle_rows(
        "middle_rows",
        ((0, 1), (1, 0), (1, 1), (2, 0)),
        (beside, first, first_beside, second),
        gains,
        (heads, upward),
        tables[1:],
        output_weight,
    )
    second, middle_joined = lax.optimization_barrier((second, middle_joined))
    second_beside = exchanged(second, "tensor", 1)
    third, second_beside, middle_joined, middle_hidden = lax.optimization_barrier(
        (third, second_beside, middle_joined, middle_hidden)
    )
    third_beside = exchanged(third, "tensor", 1)
    fed, *normed = fed_rows(own_hidden, middle_hidden, downward, (second_beside, third), gains)
    joined, fed_beside, sibling, own = last_rows(
        third_beside,
        normed,
        gains,
        (heads, upward, downward, output),
        tables,
        own_joined,
        middle_joined,
    )

    received = exchanged(sibling, "tensor", 1)
    partials = rest_rows(joined, tables[0], output, fed, fed_beside)
    siblings, owns = partials[: CHIPS - 1], partials[CHIPS - 1 :]
    third_sum = added("third_added", own, received)
    third_sum, siblings, joined = lax.optimization_barrier((third_sum, siblings, joined))
    passing = exchanged(third_sum, "tensor", to_chip[1])
    pairs = [(exchanged(sibling, "tensor", 1), own) for sibling, own in zip(siblings, owns)]
    pages = cached_pages(joined, destinations, replica_count)
    early, late = (3,), (1, 2)
    arriving = [exchanged(pages[mask], "dp", mask) for mask in early]
    second_sum, first_sum, base = remaining_sums(passing, pairs, hidden)
    from_second = exchanged(second_sum, "tensor", to_chip[2])
    from_first = exchanged(first_sum, "tensor", to_chip[1])
    base, late_pages = lax.optimization_barrier((base, [pages[mask] for mask in late]))
    late_pages = [exchanged(page, "dp", mask) for mask, page in zip(late, late_pages)]
    cache_pages = placed((0,) + early, [pages[0]] + arriving, replica_count)
    return tuple(finished(base, (from_second, from_first), late, late_pages, cache_pages))


def solution(mesh):
    whole_heads = mesh.shape["tensor"] == H and mesh.shape["dp"] == 4
    shards = shards_whole_heads if whole_heads else shards_split_heads
    in_specs = (
        P(("dp", "tensor"), None),
        P(),
        P(),
        P(None, "tensor"),
        P("tensor", None),
        P(None, "tensor"),
        P("tensor", None),
        P("dp", None),
        P("dp", None),
    )
    out_specs = (P(("dp", "tensor"), None), P("dp", None, None, None, "tensor"))
    return jax.shard_map(shards, mesh=mesh, in_specs=in_specs, out_specs=out_specs, check_vma=False)
```

```python
import functools
import math

import jax
import jax.numpy as jnp
from jax import lax
from jax.experimental import pallas as pl
from jax.experimental.pallas import tpu as pltpu
from jax.sharding import PartitionSpec as P

H = 8
HD = 256
ROT = 64
PAGE = 16


epsilon = 1e-05
rotary_base = 10000.0
key_block = 256


def shortened(array):

    def short(part):
        return part.astype(jnp.bfloat16) if part.dtype == jnp.float32 else part

    return jax.tree.map(short, array)


def swapped(block, axis, apart):
    count = lax.axis_size(axis)
    route = []
    for low in range(count):
        high = low | 1 << apart
        if high != low and high < count:
            route += [(low, high), (high, low)]
    return lax.ppermute(block, axis, route)


def layer_norm(values, gain):
    floats = values.astype(jnp.float32)
    center = jnp.mean(floats, axis=-1, keepdims=True)
    shifted = floats - center
    spread = jnp.mean(shifted * shifted, axis=-1, keepdims=True)
    return (shifted * lax.rsqrt(spread + epsilon) * gain).astype(jnp.bfloat16)


def positions_of(stream):
    indices = jnp.arange(stream.shape[0], dtype=jnp.int32)
    boundary = jnp.concatenate([jnp.ones((1,), dtype=bool), stream[1:] != stream[:-1]])
    starting = lax.cummax(jnp.where(boundary, indices, jnp.zeros_like(indices)), axis=0)
    return (indices, starting)


def rotate_heads(vectors, offsets, rotary_dims):
    half_dims = rotary_dims // 2
    frequency = jnp.exp(
        jnp.arange(half_dims, dtype=jnp.float32) * (-2.0 * math.log(rotary_base) / rotary_dims)
    )
    angles = offsets.astype(jnp.float32)[:, None] * frequency[None, :]
    cosine = jnp.cos(angles)
    sine = jnp.sin(angles)
    floats = vectors.astype(jnp.float32)
    leading = floats[..., :half_dims]
    trailing = floats[..., half_dims:rotary_dims]
    rotated = jnp.concatenate(
        [
            leading * cosine - trailing * sine,
            trailing * cosine + leading * sine,
            floats[..., rotary_dims:],
        ],
        axis=-1,
    )
    return rotated.astype(jnp.bfloat16)


def shards_split_heads(
    hidden_states,
    attention_gain,
    feedforward_gain,
    heads_weight,
    output_weight,
    upward_weight,
    downward_weight,
    segments,
    page_targets,
):
    tensor_count = lax.axis_size("tensor")
    replica_count = lax.axis_size("dp")
    tensor_index = lax.axis_index("tensor")
    quarters = tensor_count // H
    quarter_width = HD // quarters
    quarter_index = tensor_index % quarters
    stream = segments[0]
    tokens_total = stream.shape[0]
    level_count = quarters.bit_length() - 1
    normed_attention = layer_norm(hidden_states, attention_gain)
    normed_feedforward = layer_norm(hidden_states, feedforward_gain)
    shard_rows = lax.all_gather(
        (normed_attention, normed_feedforward), "tensor", axis=0, tiled=True
    )
    joined_rows = jnp.dot(shard_rows[0], heads_weight, preferred_element_type=jnp.float32).astype(
        jnp.bfloat16
    )
    upward = jnp.dot(shard_rows[1], upward_weight, preferred_element_type=jnp.float32)
    hidden_rows = jax.nn.gelu(upward, approximate=False).astype(jnp.bfloat16)
    hidden = hidden_rows
    pieces = (
        joined_rows.reshape(tokens_total, 3, quarter_width)
        .transpose(1, 0, 2)
        .reshape(1, 3, tokens_total * quarter_width)
    )
    for bit_number in range(level_count):
        partner = swapped(shortened(pieces), "tensor", bit_number).astype(pieces.dtype)
        lower = tensor_index >> bit_number & 1 == 0
        pieces = jnp.where(
            lower, jnp.concatenate([pieces, partner], 0), jnp.concatenate([partner, pieces], 0)
        )
    whole_head = (
        pieces.reshape(quarters, 3, tokens_total, quarter_width)
        .transpose(1, 2, 0, 3)
        .reshape(3, tokens_total, HD)
    )
    indices, starting = positions_of(stream)
    offsets = indices - starting
    queries = rotate_heads(whole_head[0], offsets, ROT)
    keys = rotate_heads(whole_head[1], offsets, ROT)
    values = whole_head[2]
    block_rows = tokens_total // (2 * quarters)
    score_scale = HD ** (-0.5)

    def attend_block(block_number):
        first_row = block_number * block_rows
        block_queries = lax.dynamic_slice_in_dim(queries, first_row, block_rows, 0)
        query_segments = lax.dynamic_slice_in_dim(stream, first_row, block_rows, 0)
        query_indices = first_row + jnp.arange(block_rows, dtype=jnp.int32)
        lowest = lax.dynamic_index_in_dim(starting, first_row, 0, keepdims=False) // key_block
        highest = (first_row + block_rows + key_block - 1) // key_block

        def scores_of(key_number):
            key_first = key_number * key_block
            key_indices = key_first + jnp.arange(key_block, dtype=jnp.int32)
            scores = (
                jnp.dot(block_queries, keys.T, preferred_element_type=jnp.float32) * score_scale
            )
            allowed = (stream[None, :] == query_segments[:, None]) & (
                key_indices[None, :] <= query_indices[:, None]
            )
            return (scores, allowed)

        def find_peak(key_number, peak):
            scores, allowed = scores_of(key_number)
            return jnp.maximum(peak, jnp.max(jnp.where(allowed, scores, -jnp.inf), axis=1))

        peak = lax.fori_loop(
            lowest, highest, find_peak, jnp.full((block_rows,), -jnp.inf, jnp.float32)
        )

        def accumulate(key_number, state):
            weight_sum, mixed_sum = state
            scores, allowed = scores_of(key_number)
            weights = jnp.where(allowed, jnp.exp(scores - peak[:, None]), 0.0)
            mixed_next = mixed_sum + jnp.dot(
                weights.astype(jnp.bfloat16), values, preferred_element_type=jnp.float32
            )
            return (weight_sum + jnp.sum(weights, axis=1), mixed_next)

        start_state = (
            jnp.zeros((block_rows,), jnp.float32),
            jnp.zeros((block_rows, HD), jnp.float32),
        )
        weight_sum, mixed_sum = lax.fori_loop(lowest, highest, accumulate, start_state)
        return (mixed_sum / weight_sum[:, None]).astype(jnp.bfloat16)

    own_blocks = (2 * quarter_index, 2 * quarter_index + 1)
    own_rows = jnp.concatenate([attend_block(own_blocks[0]), attend_block(own_blocks[1])], 0)[None]
    for bit_number in range(level_count):
        partner = swapped(own_rows, "tensor", bit_number)
        lower = tensor_index >> bit_number & 1 == 0
        own_rows = jnp.where(
            lower, jnp.concatenate([own_rows, partner], 0), jnp.concatenate([partner, own_rows], 0)
        )
    attended = own_rows.reshape(tokens_total, HD)
    attended_quarter = lax.dynamic_slice_in_dim(
        attended, quarter_index * quarter_width, quarter_width, 1
    )
    hidden_rows = hidden
    summed = lax.psum_scatter(
        (
            jnp.dot(attended_quarter, output_weight, preferred_element_type=jnp.float32)
            + jnp.dot(hidden_rows, downward_weight, preferred_element_type=jnp.float32)
        ).astype(jnp.bfloat16),
        "tensor",
        scatter_dimension=0,
        tiled=True,
    ).astype(jnp.float32)
    layer_output = hidden_states.astype(jnp.float32) + summed
    key_quarter = lax.dynamic_slice_in_dim(keys, quarter_index * quarter_width, quarter_width, 1)
    value_quarter = joined_rows[:, 2 * quarter_width :]
    page_count = tokens_total // PAGE
    page_rows = jnp.concatenate([key_quarter, value_quarter], 1).reshape(
        page_count, PAGE * 2 * quarter_width
    )
    targets = page_targets[:, 0]
    page_numbers = jnp.arange(page_count, dtype=jnp.int32)
    earlier = jnp.sum(
        (
            (targets[None, :] == targets[:, None]) & (page_numbers[None, :] < page_numbers[:, None])
        ).astype(jnp.int32),
        axis=1,
    )
    capacity = 2 * page_count // replica_count
    slot_numbers = targets * capacity + earlier
    placing = (
        jnp.arange(replica_count * capacity, dtype=jnp.int32)[:, None] == slot_numbers[None, :]
    ).astype(jnp.bfloat16)
    outgoing = jnp.dot(placing, page_rows, preferred_element_type=jnp.float32).astype(jnp.bfloat16)
    outgoing = outgoing.reshape(replica_count, capacity, PAGE * 2 * quarter_width)
    incoming = lax.all_to_all(outgoing, "dp", split_axis=0, concat_axis=0, tiled=True)
    cache_pages = incoming.reshape(1, replica_count, capacity, PAGE, 2 * quarter_width)
    return (layer_output, cache_pages)


CORES = 2
CHIPS = 4
MIB = 1 << 20


def in_hbm(array):
    return pltpu.with_memory_space_constraint(array, pltpu.HBM)


def exchanged(block, axis, mask):
    count = lax.axis_size(axis)
    return lax.ppermute(block, axis, [(member, member ^ mask) for member in range(count)])


def vmem_specs(count):
    return [pl.BlockSpec(memory_space=pltpu.VMEM)] * count


def parameters(mebibytes):
    return pltpu.CompilerParams(vmem_limit_bytes=mebibytes * MIB)


def whereabouts():
    member = lax.axis_index("tensor")
    return member // CORES, member % CORES


def position_of(kind, half, block_rows):
    chip, core = whereabouts()
    return ((chip ^ kind) * CORES + (core ^ half)) * block_rows


def positions_along(first, shape, axis, block_rows):
    chip, core = whereabouts()
    bits = block_rows.bit_length() - 1
    place = first + lax.broadcasted_iota(jnp.int32, shape, axis)
    kind = place >> (bits + 1)
    half = (place >> bits) & 1
    return ((((chip ^ kind) << 1) | (core ^ half)) << bits) | (place & (block_rows - 1))


def normalize(blocks, gain_refs, normed_refs, place=0):
    piece = 16
    gains = [gain_ref[...] for gain_ref in gain_refs]
    for number, block_ref in enumerate(blocks):
        block_rows = block_ref.shape[0]
        for part in range(0, block_rows, piece):
            floats = block_ref[part : part + piece, :].astype(jnp.float32)
            center = jnp.mean(floats, axis=-1, keepdims=True)
            shifted = floats - center
            spread = jnp.mean(shifted * shifted, axis=-1, keepdims=True)
            scaled = shifted * lax.rsqrt(spread + epsilon)
            first = place + number * block_rows + part
            for gain, normed_ref in zip(gains, normed_refs):
                normed_ref[first : first + piece, :] = (scaled * gain).astype(jnp.bfloat16)


def project(normed_ref, heads_ref, table_refs, places, joined_ref, first):
    rows = normed_ref.shape[0]
    block_rows = rows // len(places)
    own = slice(first, first + rows)
    cosine, sine_down, sine_up = [
        jnp.concatenate(
            [
                table_ref[pl.ds(pl.multiple_of(place, block_rows), block_rows), :]
                for place in places
            ],
            0,
        )
        for table_ref in table_refs
    ]
    joined_ref[own, :] = jnp.dot(
        normed_ref[...], heads_ref[...], preferred_element_type=jnp.float32
    ).astype(jnp.bfloat16)
    for begin in (0, HD):
        columns = slice(begin, begin + 128)
        turning = joined_ref[own, columns].astype(jnp.float32)
        turned = (
            turning * cosine
            + pltpu.roll(turning, 128 - ROT // 2, 1) * sine_down
            + pltpu.roll(turning, ROT // 2, 1) * sine_up
        )
        joined_ref[own, columns] = turned.astype(jnp.bfloat16)


def hide(normed_ref, upward_ref, hidden_ref, place, chunk=256):
    rows = slice(place, place + normed_ref.shape[0])
    for first in range(0, upward_ref.shape[1], chunk):
        columns = slice(first, first + chunk)
        upward = jnp.dot(
            normed_ref[...], upward_ref[:, columns], preferred_element_type=jnp.float32
        )
        hidden = 0.5 * upward * (1.0 + lax.erf(upward * (0.5**0.5)))
        hidden_ref[rows, columns] = hidden.astype(jnp.bfloat16)


def attend(joined_ref, offsets_ref, first, rows, block_rows):
    tokens = joined_ref.shape[0]
    starts = [
        position_of(place // (2 * block_rows), (place // block_rows) % 2, block_rows)
        for place in range(first, first + rows, block_rows)
    ]
    reach = jnp.concatenate(
        [
            offsets_ref[pl.ds(pl.multiple_of(start, block_rows), block_rows), :]
            for start in starts
        ],
        0,
    )[:, :1].astype(jnp.int32)
    row = positions_along(first, (rows, 1), 0, block_rows)
    column = positions_along(0, (1, tokens), 1, block_rows)
    allowed = (column <= row) & (column >= row - reach)
    scores = lax.dot_general(
        joined_ref[first : first + rows, :HD],
        joined_ref[:, HD : 2 * HD],
        (((1,), (1,)), ((), ())),
        preferred_element_type=jnp.float32,
    ) * (HD ** (-0.5))
    peak = jnp.max(jnp.where(allowed, scores, -jnp.inf), axis=1, keepdims=True)
    weights = jnp.where(allowed, jnp.exp(scores - peak), 0.0)
    weight_sum = jnp.sum(weights, axis=1, keepdims=True)
    mixed = jnp.dot(
        weights.astype(jnp.bfloat16), joined_ref[:, 2 * HD :], preferred_element_type=jnp.float32
    )
    return (mixed / weight_sum).astype(jnp.bfloat16)


def make_tables(segments_ref, offsets_ref, cosine_ref, sine_down_ref, sine_up_ref):
    tokens = segments_ref.shape[1]
    shape = (tokens, tokens)
    rows = lax.broadcasted_iota(jnp.int32, shape, 0)
    columns = lax.broadcasted_iota(jnp.int32, shape, 1)
    across = jnp.broadcast_to(segments_ref[...], shape).astype(jnp.float32)
    down = jnp.sum(jnp.where(rows == columns, across, 0.0), axis=1, keepdims=True)
    earlier = (across == down) & (columns < rows)
    offsets = jnp.sum(jnp.where(earlier, 1.0, 0.0), axis=1, keepdims=True)
    offsets_ref[...] = jnp.broadcast_to(offsets, offsets_ref.shape)
    half = ROT // 2
    lane = lax.broadcasted_iota(jnp.int32, (tokens, 128), 1)
    step = (lane & (half - 1)).astype(jnp.float32)
    frequency = jnp.exp(step * (-2.0 * math.log(rotary_base) / ROT))
    angles = offsets * frequency
    sine = jnp.sin(angles)
    cosine_ref[...] = jnp.where(lane < ROT, jnp.cos(angles), 1.0)
    sine_down_ref[...] = jnp.where(lane < half, -sine, 0.0)
    sine_up_ref[...] = jnp.where((lane >= half) & (lane < ROT), sine, 0.0)


def make_destinations(targets_ref, destinations_ref, replica_count, block_rows):
    page_count = targets_ref.shape[1]
    tokens = destinations_ref.shape[1]
    capacity = 2 * page_count // replica_count
    square = (page_count, page_count)
    rows = lax.broadcasted_iota(jnp.int32, square, 0)
    columns = lax.broadcasted_iota(jnp.int32, square, 1)
    across = jnp.broadcast_to(targets_ref[...], square).astype(jnp.float32)
    down = jnp.sum(jnp.where(rows == columns, across, 0.0), axis=1, keepdims=True)
    earlier = jnp.where((across == down) & (columns < rows), 1.0, 0.0)
    slots = jnp.sum(earlier, axis=1, keepdims=True).astype(jnp.int32)
    slots = (down.astype(jnp.int32) ^ lax.axis_index("dp")) * capacity + slots
    positions = positions_along(0, (1, tokens), 1, block_rows)
    bits = PAGE.bit_length() - 1
    pages = lax.broadcasted_iota(jnp.int32, (page_count, tokens), 0)
    chosen = jnp.where(pages == positions >> bits, slots.astype(jnp.float32), 0.0)
    slot = jnp.sum(chosen, axis=0, keepdims=True).astype(jnp.int32)
    destinations_ref[...] = slot * PAGE + (positions & (PAGE - 1))


def copies_in(sources, targets, sems):
    copies = []
    for number, (source, target) in enumerate(zip(sources, targets)):
        parts = 4 if source.shape[0] >= 256 else 1
        rows = source.shape[0] // parts
        places = [pl.ds(part * rows, rows) for part in range(parts)]
        copies.append(
            [
                pltpu.make_async_copy(source.at[place], target.at[place], sems.at[number, part])
                for part, place in enumerate(places)
            ]
        )
    for copy in sum(copies, []):
        copy.start()
    return copies


def wait_for(copies):
    for copy in copies:
        copy.wait()


def own_kernel(count, replica_count, *refs):
    sources, targets = refs[:count], refs[count : 2 * count]
    offsets_ref, *table_refs, destinations_ref, joined_ref, hidden_ref = refs[2 * count : -3]
    attention_scr, feedforward_scr, sems = refs[-3:]
    copies = copies_in(sources, targets, sems)
    segments_ref, targets_ref, states_ref, *gain_refs, heads_ref, upward_ref, _ = targets
    block_rows = states_ref.shape[0]
    wait_for(copies[0])
    make_tables(segments_ref, offsets_ref, *table_refs)
    wait_for(copies[1])
    make_destinations(targets_ref, destinations_ref, replica_count, block_rows)
    for number in (2, 3, 4):
        wait_for(copies[number])
    normalize([states_ref], gain_refs, [attention_scr, feedforward_scr])
    wait_for(copies[5])
    places = [position_of(0, 0, block_rows)]
    project(attention_scr, heads_ref, table_refs, places, joined_ref, 0)
    wait_for(copies[6])
    hide(feedforward_scr, upward_ref, hidden_ref, 0)
    wait_for(copies[7])


def own_rows(staged, replica_count):
    tokens = staged[0].shape[1]
    rows, width = staged[2].shape
    hidden_width = staged[6].shape[1]
    shapes = [pltpu.VMEM(array.shape, array.dtype) for array in staged]
    shapes += [pltpu.VMEM((tokens, 128), jnp.float32)] * 4
    shapes += [
        pltpu.VMEM((1, tokens), jnp.int32),
        pltpu.VMEM((rows, 3 * HD), jnp.bfloat16),
        pltpu.VMEM((rows, hidden_width), jnp.bfloat16),
    ]
    count = len(staged)
    return pl.pallas_call(
        functools.partial(own_kernel, count, replica_count),
        out_shape=shapes,
        in_specs=[pl.BlockSpec(memory_space=pltpu.HBM)] * count,
        out_specs=vmem_specs(len(shapes)),
        scratch_shapes=[
            pltpu.VMEM((rows, width), jnp.bfloat16),
            pltpu.VMEM((rows, width), jnp.bfloat16),
            pltpu.SemaphoreType.DMA((count, 4)),
        ],
        compiler_params=parameters(12),
        cost_estimate=pl.CostEstimate(
            flops=2 * rows * width * (3 * HD + hidden_width),
            bytes_accessed=sum(array.nbytes for array in staged),
            transcendentals=rows * hidden_width,
        ),
        name="own_rows",
    )(*[in_hbm(array) for array in staged])


def middle_kernel(origins, *refs):
    count = len(origins)
    blocks, (gain_a, gain_f, heads_ref, upward_ref) = refs[:count], refs[count : count + 4]
    table_refs, refs = refs[count + 4 : count + 7], refs[count + 7 :]
    staged = (len(refs) - 5) // 2
    sources, (joined_ref, hidden_ref), refs = refs[:staged], refs[staged:][:2], refs[staged + 2 :]
    targets, (attention_scr, feedforward_scr, sems) = refs[:staged], refs[staged:]
    copies = copies_in(sources, targets, sems)
    block_rows = blocks[0].shape[0]
    normalize(blocks, [gain_a, gain_f], [attention_scr, feedforward_scr])
    places = [position_of(kind, half, block_rows) for kind, half in origins]
    project(attention_scr, heads_ref, table_refs, places, joined_ref, 0)
    hide(feedforward_scr, upward_ref, hidden_ref, 0)
    wait_for(sum(copies, []))


def middle_rows(name, origins, blocks, gains, weights, tables, *staged):
    block_rows, width = blocks[0].shape
    rows = len(blocks) * block_rows
    hidden_width = weights[1].shape[1]
    return pl.pallas_call(
        functools.partial(middle_kernel, origins),
        out_shape=[
            pltpu.VMEM((rows, 3 * HD), jnp.bfloat16),
            pltpu.VMEM((rows, hidden_width), jnp.bfloat16),
        ]
        + [pltpu.VMEM(array.shape, array.dtype) for array in staged],
        in_specs=vmem_specs(len(blocks) + 2 + 2 + 3)
        + [pl.BlockSpec(memory_space=pltpu.HBM)] * len(staged),
        out_specs=vmem_specs(2 + len(staged)),
        scratch_shapes=[
            pltpu.VMEM((rows, width), jnp.bfloat16),
            pltpu.VMEM((rows, width), jnp.bfloat16),
            pltpu.SemaphoreType.DMA((max(len(staged), 1), 4)),
        ],
        compiler_params=parameters(12),
        cost_estimate=pl.CostEstimate(
            flops=2 * rows * width * (3 * HD + hidden_width),
            bytes_accessed=MIB,
            transcendentals=rows * hidden_width,
        ),
        name=name,
    )(*blocks, *gains, *weights, *tables, *[in_hbm(array) for array in staged])


def last_kernel(*refs):
    block_ref, *normed_refs = refs[:3]
    gain_a, gain_f, heads_ref, upward_ref, downward_ref, output_ref = refs[3:9]
    offsets_ref, *table_refs = refs[9:13]
    own_joined_ref, middle_joined_ref = refs[13:15]
    joined_ref, fed_ref, sibling_ref, own_ref = refs[15:19]
    attention_scr, feedforward_scr, hidden_scr = refs[19:]
    block_rows = block_ref.shape[0]
    tokens = joined_ref.shape[0]
    first = tokens - attention_scr.shape[0]
    count = normed_refs[0].shape[0]
    normalize([block_ref], [gain_a, gain_f], [attention_scr, feedforward_scr], count)
    for normed_ref, normed_scr in zip(normed_refs, (attention_scr, feedforward_scr)):
        normed_scr[:count, :] = normed_ref[...]
    joined_ref[:block_rows, :] = own_joined_ref[...]
    joined_ref[block_rows:first, :] = middle_joined_ref[...]
    origins = ((CHIPS - 2, 1), (CHIPS - 1, 0), (CHIPS - 1, 1))
    places = [position_of(kind, half, block_rows) for kind, half in origins]
    project(attention_scr, heads_ref, table_refs, places, joined_ref, first)
    rows = CORES * block_rows
    hide(feedforward_scr, upward_ref, hidden_scr, 0, 512)
    attended = attend(joined_ref, offsets_ref, tokens - rows, rows, block_rows)
    chunk = 1024
    for begin in range(0, downward_ref.shape[1], chunk):
        columns = slice(begin, begin + chunk)
        fed = jnp.dot(hidden_scr[...], downward_ref[:, columns], preferred_element_type=jnp.float32)
        fed_ref[:, columns] = fed[:block_rows]
        partial = fed[block_rows:] + jnp.dot(
            attended, output_ref[:, columns], preferred_element_type=jnp.float32
        )
        own_ref[:, columns] = partial[:block_rows]
        sibling_ref[:, columns] = partial[block_rows:].astype(jnp.bfloat16)


def last_rows(block, normed, gains, weights, tables, own_joined, middle_joined):
    block_rows, width = block.shape
    rows = normed[0].shape[0] + block_rows
    hidden_width = weights[1].shape[1]
    tokens = CHIPS * CORES * block_rows
    return pl.pallas_call(
        last_kernel,
        out_shape=[
            pltpu.VMEM((tokens, 3 * HD), jnp.bfloat16),
            pltpu.VMEM((block_rows, width), jnp.float32),
            pltpu.VMEM((block_rows, width), jnp.bfloat16),
            pltpu.VMEM((block_rows, width), jnp.float32),
        ],
        in_specs=vmem_specs(1 + 2 + 2 + 4 + 4 + 2),
        out_specs=vmem_specs(4),
        scratch_shapes=[
            pltpu.VMEM((rows, width), jnp.bfloat16),
            pltpu.VMEM((rows, width), jnp.bfloat16),
            pltpu.VMEM((rows, hidden_width), jnp.bfloat16),
        ],
        compiler_params=parameters(12),
        cost_estimate=pl.CostEstimate(
            flops=2 * rows * width * (3 * HD + HD + 2 * hidden_width),
            bytes_accessed=MIB,
            transcendentals=rows * hidden_width,
        ),
        name="last_rows",
    )(block, *normed, *gains, *weights, *tables, own_joined, middle_joined)


def fed_kernel(own_hidden_ref, middle_hidden_ref, downward_ref, *refs):
    blocks, gain_refs, (fed_ref, *normed_refs) = refs[:2], refs[2:4], refs[4:]
    normalize(blocks, gain_refs, normed_refs)
    hidden = jnp.concatenate([own_hidden_ref[...], middle_hidden_ref[...]], 0)
    chunk = 512
    for begin in range(0, downward_ref.shape[1], chunk):
        columns = slice(begin, begin + chunk)
        fed_ref[:, columns] = jnp.dot(
            hidden, downward_ref[:, columns], preferred_element_type=jnp.float32
        )


def fed_rows(own_hidden, middle_hidden, downward_weight, blocks, gains):
    rows = own_hidden.shape[0] + middle_hidden.shape[0]
    depth, width = downward_weight.shape
    normed = pltpu.VMEM((len(blocks) * blocks[0].shape[0], width), jnp.bfloat16)
    return pl.pallas_call(
        fed_kernel,
        out_shape=[pltpu.VMEM((rows, width), jnp.float32), normed, normed],
        in_specs=vmem_specs(7),
        out_specs=vmem_specs(3),
        compiler_params=parameters(12),
        cost_estimate=pl.CostEstimate(
            flops=2 * rows * depth * width, bytes_accessed=MIB, transcendentals=0
        ),
        name="fed_rows",
    )(own_hidden, middle_hidden, downward_weight, *blocks, *gains)


def rest_kernel(joined_ref, offsets_ref, output_ref, fed_ref, fed_beside_ref, *refs):
    count = len(refs) // 2
    siblings, owns = refs[:count], refs[count:]
    block_rows = owns[0].shape[0]
    rows = fed_ref.shape[0] + fed_beside_ref.shape[0]
    attended = attend(joined_ref, offsets_ref, 0, rows, block_rows)
    chunk = 512
    for begin in range(0, output_ref.shape[1], chunk):
        columns = slice(begin, begin + chunk)
        fed = jnp.concatenate([fed_ref[:, columns], fed_beside_ref[:, columns]], 0)
        partial = fed + jnp.dot(
            attended, output_ref[:, columns], preferred_element_type=jnp.float32
        )
        for number, (sibling_ref, own_ref) in enumerate(zip(siblings, owns)):
            first = CORES * number * block_rows
            middle = first + block_rows
            own_ref[:, columns] = partial[first:middle]
            sibling_ref[:, columns] = partial[middle : middle + block_rows].astype(jnp.bfloat16)


def rest_rows(joined, offsets, output_weight, fed, fed_beside):
    width = fed.shape[1]
    rows = fed.shape[0] + fed_beside.shape[0]
    count = CHIPS - 1
    shape = (rows // (CORES * count), width)
    shapes = [pltpu.VMEM(shape, dtype) for dtype in [jnp.bfloat16] * count + [jnp.float32] * count]
    return pl.pallas_call(
        rest_kernel,
        out_shape=shapes,
        in_specs=vmem_specs(5),
        out_specs=vmem_specs(2 * count),
        compiler_params=parameters(12),
        cost_estimate=pl.CostEstimate(
            flops=2 * rows * width * HD,
            bytes_accessed=MIB,
            transcendentals=rows * joined.shape[0],
        ),
        name="rest_rows",
    )(joined, offsets, output_weight, fed, fed_beside)


def pages_kernel(joined_ref, destinations_ref, *page_refs):
    tokens = joined_ref.shape[0]
    slot_rows = page_refs[0].shape[0] * PAGE
    for number, page_ref in enumerate(page_refs):
        shape = (slot_rows, tokens)
        row = number * slot_rows + lax.broadcasted_iota(jnp.int32, shape, 0)
        placing = jnp.where(row == destinations_ref[...], 1.0, 0.0).astype(jnp.bfloat16)
        rows = jnp.dot(placing, joined_ref[:, HD:], preferred_element_type=jnp.float32)
        page_ref[...] = rows.astype(jnp.bfloat16).reshape(page_ref.shape)


def cached_pages(joined, destinations, replica_count):
    tokens = joined.shape[0]
    capacity = 2 * (tokens // PAGE) // replica_count
    shapes = [pltpu.VMEM((capacity, PAGE, 2 * HD), jnp.bfloat16)] * replica_count
    return pl.pallas_call(
        pages_kernel,
        out_shape=shapes,
        in_specs=vmem_specs(2),
        out_specs=vmem_specs(len(shapes)),
        compiler_params=parameters(8),
        cost_estimate=pl.CostEstimate(flops=0, bytes_accessed=MIB, transcendentals=0),
        name="cached_pages",
    )(joined, destinations)


def add_kernel(*refs):
    total = refs[0][...].astype(jnp.float32)
    for ref in refs[1:-1]:
        total = total + ref[...].astype(jnp.float32)
    refs[-1][...] = total.astype(refs[-1].dtype)


def added(name, *parts):
    return pl.pallas_call(
        add_kernel,
        out_shape=pltpu.VMEM(parts[0].shape, jnp.bfloat16),
        in_specs=vmem_specs(len(parts)),
        out_specs=pl.BlockSpec(memory_space=pltpu.VMEM),
        compiler_params=parameters(4),
        name=name,
    )(*parts)


def near_kernel(*refs):
    zeros, ones, hidden_ref, first_ref, base_ref = refs[0:2], refs[2:4], *refs[4:]

    def total(pair):
        received_ref, own_ref = pair
        return own_ref[...] + received_ref[...].astype(jnp.float32)

    first_ref[...] = total(ones).astype(jnp.bfloat16)
    base_ref[...] = total(zeros) + hidden_ref[...].astype(jnp.float32)


def near_sums(pairs, hidden):
    shape = hidden.shape
    return pl.pallas_call(
        near_kernel,
        out_shape=[pltpu.VMEM(shape, jnp.bfloat16), pltpu.VMEM(shape, jnp.float32)],
        in_specs=vmem_specs(5),
        out_specs=vmem_specs(2),
        compiler_params=parameters(4),
        name="near_sums",
    )(*[array for pair in pairs for array in pair], hidden)


def place_kernel(masks, *refs):
    group = lax.axis_index("dp")
    count = len(masks)
    pages, (part_ref, base_ref) = refs[:count], refs[count : count + 2]
    cache_ref, total_ref, sems = refs[count + 2 :]
    copies = [
        pltpu.make_async_copy(page_ref, cache_ref.at[0, group ^ mask], sems.at[number])
        for number, (mask, page_ref) in enumerate(zip(masks, pages))
    ]
    for copy in copies:
        copy.start()
    total_ref[...] = base_ref[...] + part_ref[...].astype(jnp.float32)
    for copy in copies:
        copy.wait()


def placed(masks, pages, part, base, replica_count):
    count = len(pages)
    return pl.pallas_call(
        functools.partial(place_kernel, masks),
        out_shape=[
            jax.ShapeDtypeStruct((1, replica_count) + pages[0].shape, pages[0].dtype),
            pltpu.VMEM(base.shape, base.dtype),
        ],
        in_specs=[pl.BlockSpec(memory_space=pl.ANY)] * count + vmem_specs(2),
        out_specs=[pl.BlockSpec(memory_space=pltpu.HBM)] + vmem_specs(1),
        scratch_shapes=[pltpu.SemaphoreType.DMA((count,))],
        compiler_params=parameters(4),
        name="placed",
    )(*pages, part, base)


def finish_kernel(masks, base_ref, *refs):
    count = len(masks)
    *parts, _, output_ref, cache_ref, total_scr, sems = refs
    parts, pages = parts[:-count], parts[-count:]
    group = lax.axis_index("dp")
    copies = [
        pltpu.make_async_copy(page_ref, cache_ref.at[0, group ^ mask], sems.at[number])
        for number, (mask, page_ref) in enumerate(zip(masks, pages))
    ]
    for copy in copies:
        copy.start()
    total = base_ref[...]
    for part_ref in parts:
        total = total + part_ref[...].astype(jnp.float32)
    total_scr[...] = total
    copies.append(pltpu.make_async_copy(total_scr, output_ref, sems.at[count]))
    copies[-1].start()
    for copy in copies:
        copy.wait()


def finished(base, parts, masks, pages, cache):
    count = len(pages)
    return pl.pallas_call(
        functools.partial(finish_kernel, masks),
        out_shape=[
            jax.ShapeDtypeStruct(base.shape, base.dtype),
            jax.ShapeDtypeStruct(cache.shape, cache.dtype),
        ],
        in_specs=vmem_specs(1 + len(parts))
        + [pl.BlockSpec(memory_space=pl.ANY)] * count
        + [pl.BlockSpec(memory_space=pltpu.HBM)],
        out_specs=[pl.BlockSpec(memory_space=pltpu.HBM)] * 2,
        scratch_shapes=[
            pltpu.VMEM(base.shape, base.dtype),
            pltpu.SemaphoreType.DMA((count + 1,)),
        ],
        input_output_aliases={1 + len(parts) + count: 1},
        compiler_params=parameters(4),
        name="finished",
    )(base, *parts, *pages, cache)


def shards_whole_heads(
    hidden_states,
    attention_gain,
    feedforward_gain,
    heads_weight,
    output_weight,
    upward_weight,
    downward_weight,
    segments,
    page_targets,
):
    replica_count = lax.axis_size("dp")
    to_chip = [mask * CORES for mask in range(CHIPS)]
    second = exchanged(hidden_states, "tensor", to_chip[2])
    first = exchanged(hidden_states, "tensor", to_chip[1])
    beside = exchanged(hidden_states, "tensor", 1)
    staged = (
        segments,
        page_targets.reshape(1, -1),
        hidden_states,
        attention_gain[None],
        feedforward_gain[None],
        heads_weight,
        upward_weight,
        downward_weight,
    )
    staged = own_rows(staged, replica_count)
    hidden, gains, weights, tables = staged[2], staged[3:5], staged[5:8], staged[8:12]
    heads, upward, downward = weights
    destinations, own_joined, own_hidden = staged[12:]

    first, second, own_joined = lax.optimization_barrier((first, second, own_joined))
    first_beside = exchanged(first, "tensor", 1)
    third = exchanged(second, "tensor", to_chip[1])
    middle_joined, middle_hidden, output = middle_rows(
        "middle_rows",
        ((0, 1), (1, 0), (1, 1), (2, 0)),
        (beside, first, first_beside, second),
        gains,
        (heads, upward),
        tables[1:],
        output_weight,
    )
    second, middle_joined = lax.optimization_barrier((second, middle_joined))
    second_beside = exchanged(second, "tensor", 1)
    third, second_beside, middle_joined, middle_hidden = lax.optimization_barrier(
        (third, second_beside, middle_joined, middle_hidden)
    )
    third_beside = exchanged(third, "tensor", 1)
    fed, *normed = fed_rows(own_hidden, middle_hidden, downward, (second_beside, third), gains)
    joined, fed_beside, sibling, own = last_rows(
        third_beside,
        normed,
        gains,
        (heads, upward, downward, output),
        tables,
        own_joined,
        middle_joined,
    )

    received = exchanged(sibling, "tensor", 1)
    partials = rest_rows(joined, tables[0], output, fed, fed_beside)
    siblings, owns = list(partials[: CHIPS - 1]), partials[CHIPS - 1 :]
    third_sum = added("third_added", own, received)
    third_sum, siblings[2], joined = lax.optimization_barrier((third_sum, siblings[2], joined))
    passing = exchanged(third_sum, "tensor", to_chip[1])
    pairs = [(exchanged(sibling, "tensor", 1), own) for sibling, own in zip(siblings, owns)]
    pages = cached_pages(joined, destinations, replica_count)
    early, late = (3,), (1, 2)
    arriving = [exchanged(pages[mask], "dp", mask) for mask in early]
    first_sum, base = near_sums(pairs[:2], hidden)
    from_first = exchanged(first_sum, "tensor", to_chip[1])
    second_received, second_own = pairs[2]
    second_sum = added("second_added", second_own, passing, second_received)
    second_sum, late_pages = lax.optimization_barrier(
        (second_sum, [pages[mask] for mask in late])
    )
    from_second = exchanged(second_sum, "tensor", to_chip[2])
    late_pages = [exchanged(page, "dp", mask) for mask, page in zip(late, late_pages)]
    cache_pages, base = placed((0,) + early, [pages[0]] + arriving, from_first, base, replica_count)
    return tuple(finished(base, (from_second,), late, late_pages, cache_pages))


def solution(mesh):
    whole_heads = mesh.shape["tensor"] == H and mesh.shape["dp"] == 4
    shards = shards_whole_heads if whole_heads else shards_split_heads
    in_specs = (
        P(("dp", "tensor"), None),
        P(),
        P(),
        P(None, "tensor"),
        P("tensor", None),
        P(None, "tensor"),
        P("tensor", None),
        P("dp", None),
        P("dp", None),
    )
    out_specs = (P(("dp", "tensor"), None), P("dp", None, None, None, "tensor"))
    return jax.shard_map(shards, mesh=mesh, in_specs=in_specs, out_specs=out_specs, check_vma=False)
```

```python
import functools
import math

import jax
import jax.numpy as jnp
from jax import lax
from jax.experimental import pallas as pl
from jax.experimental.pallas import tpu as pltpu
from jax.sharding import PartitionSpec as P

H = 8
HD = 256
ROT = 64
PAGE = 16


epsilon = 1e-05
rotary_base = 10000.0
key_block = 256


def shortened(array):

    def short(part):
        return part.astype(jnp.bfloat16) if part.dtype == jnp.float32 else part

    return jax.tree.map(short, array)


def swapped(block, axis, apart):
    count = lax.axis_size(axis)
    route = []
    for low in range(count):
        high = low | 1 << apart
        if high != low and high < count:
            route += [(low, high), (high, low)]
    return lax.ppermute(block, axis, route)


def layer_norm(values, gain):
    floats = values.astype(jnp.float32)
    center = jnp.mean(floats, axis=-1, keepdims=True)
    shifted = floats - center
    spread = jnp.mean(shifted * shifted, axis=-1, keepdims=True)
    return (shifted * lax.rsqrt(spread + epsilon) * gain).astype(jnp.bfloat16)


def positions_of(stream):
    indices = jnp.arange(stream.shape[0], dtype=jnp.int32)
    boundary = jnp.concatenate([jnp.ones((1,), dtype=bool), stream[1:] != stream[:-1]])
    starting = lax.cummax(jnp.where(boundary, indices, jnp.zeros_like(indices)), axis=0)
    return (indices, starting)


def rotate_heads(vectors, offsets, rotary_dims):
    half_dims = rotary_dims // 2
    frequency = jnp.exp(
        jnp.arange(half_dims, dtype=jnp.float32) * (-2.0 * math.log(rotary_base) / rotary_dims)
    )
    angles = offsets.astype(jnp.float32)[:, None] * frequency[None, :]
    cosine = jnp.cos(angles)
    sine = jnp.sin(angles)
    floats = vectors.astype(jnp.float32)
    leading = floats[..., :half_dims]
    trailing = floats[..., half_dims:rotary_dims]
    rotated = jnp.concatenate(
        [
            leading * cosine - trailing * sine,
            trailing * cosine + leading * sine,
            floats[..., rotary_dims:],
        ],
        axis=-1,
    )
    return rotated.astype(jnp.bfloat16)


def shards_split_heads(
    hidden_states,
    attention_gain,
    feedforward_gain,
    heads_weight,
    output_weight,
    upward_weight,
    downward_weight,
    segments,
    page_targets,
):
    tensor_count = lax.axis_size("tensor")
    replica_count = lax.axis_size("dp")
    tensor_index = lax.axis_index("tensor")
    quarters = tensor_count // H
    quarter_width = HD // quarters
    quarter_index = tensor_index % quarters
    stream = segments[0]
    tokens_total = stream.shape[0]
    level_count = quarters.bit_length() - 1
    normed_attention = layer_norm(hidden_states, attention_gain)
    normed_feedforward = layer_norm(hidden_states, feedforward_gain)
    shard_rows = lax.all_gather(
        (normed_attention, normed_feedforward), "tensor", axis=0, tiled=True
    )
    joined_rows = jnp.dot(shard_rows[0], heads_weight, preferred_element_type=jnp.float32).astype(
        jnp.bfloat16
    )
    upward = jnp.dot(shard_rows[1], upward_weight, preferred_element_type=jnp.float32)
    hidden_rows = jax.nn.gelu(upward, approximate=False).astype(jnp.bfloat16)
    hidden = hidden_rows
    pieces = (
        joined_rows.reshape(tokens_total, 3, quarter_width)
        .transpose(1, 0, 2)
        .reshape(1, 3, tokens_total * quarter_width)
    )
    for bit_number in range(level_count):
        partner = swapped(shortened(pieces), "tensor", bit_number).astype(pieces.dtype)
        lower = tensor_index >> bit_number & 1 == 0
        pieces = jnp.where(
            lower, jnp.concatenate([pieces, partner], 0), jnp.concatenate([partner, pieces], 0)
        )
    whole_head = (
        pieces.reshape(quarters, 3, tokens_total, quarter_width)
        .transpose(1, 2, 0, 3)
        .reshape(3, tokens_total, HD)
    )
    indices, starting = positions_of(stream)
    offsets = indices - starting
    queries = rotate_heads(whole_head[0], offsets, ROT)
    keys = rotate_heads(whole_head[1], offsets, ROT)
    values = whole_head[2]
    block_rows = tokens_total // (2 * quarters)
    score_scale = HD ** (-0.5)

    def attend_block(block_number):
        first_row = block_number * block_rows
        block_queries = lax.dynamic_slice_in_dim(queries, first_row, block_rows, 0)
        query_segments = lax.dynamic_slice_in_dim(stream, first_row, block_rows, 0)
        query_indices = first_row + jnp.arange(block_rows, dtype=jnp.int32)
        lowest = lax.dynamic_index_in_dim(starting, first_row, 0, keepdims=False) // key_block
        highest = (first_row + block_rows + key_block - 1) // key_block

        def scores_of(key_number):
            key_first = key_number * key_block
            key_indices = key_first + jnp.arange(key_block, dtype=jnp.int32)
            scores = (
                jnp.dot(block_queries, keys.T, preferred_element_type=jnp.float32) * score_scale
            )
            allowed = (stream[None, :] == query_segments[:, None]) & (
                key_indices[None, :] <= query_indices[:, None]
            )
            return (scores, allowed)

        def find_peak(key_number, peak):
            scores, allowed = scores_of(key_number)
            return jnp.maximum(peak, jnp.max(jnp.where(allowed, scores, -jnp.inf), axis=1))

        peak = lax.fori_loop(
            lowest, highest, find_peak, jnp.full((block_rows,), -jnp.inf, jnp.float32)
        )

        def accumulate(key_number, state):
            weight_sum, mixed_sum = state
            scores, allowed = scores_of(key_number)
            weights = jnp.where(allowed, jnp.exp(scores - peak[:, None]), 0.0)
            mixed_next = mixed_sum + jnp.dot(
                weights.astype(jnp.bfloat16), values, preferred_element_type=jnp.float32
            )
            return (weight_sum + jnp.sum(weights, axis=1), mixed_next)

        start_state = (
            jnp.zeros((block_rows,), jnp.float32),
            jnp.zeros((block_rows, HD), jnp.float32),
        )
        weight_sum, mixed_sum = lax.fori_loop(lowest, highest, accumulate, start_state)
        return (mixed_sum / weight_sum[:, None]).astype(jnp.bfloat16)

    own_blocks = (2 * quarter_index, 2 * quarter_index + 1)
    own_rows = jnp.concatenate([attend_block(own_blocks[0]), attend_block(own_blocks[1])], 0)[None]
    for bit_number in range(level_count):
        partner = swapped(own_rows, "tensor", bit_number)
        lower = tensor_index >> bit_number & 1 == 0
        own_rows = jnp.where(
            lower, jnp.concatenate([own_rows, partner], 0), jnp.concatenate([partner, own_rows], 0)
        )
    attended = own_rows.reshape(tokens_total, HD)
    attended_quarter = lax.dynamic_slice_in_dim(
        attended, quarter_index * quarter_width, quarter_width, 1
    )
    hidden_rows = hidden
    summed = lax.psum_scatter(
        (
            jnp.dot(attended_quarter, output_weight, preferred_element_type=jnp.float32)
            + jnp.dot(hidden_rows, downward_weight, preferred_element_type=jnp.float32)
        ).astype(jnp.bfloat16),
        "tensor",
        scatter_dimension=0,
        tiled=True,
    ).astype(jnp.float32)
    layer_output = hidden_states.astype(jnp.float32) + summed
    key_quarter = lax.dynamic_slice_in_dim(keys, quarter_index * quarter_width, quarter_width, 1)
    value_quarter = joined_rows[:, 2 * quarter_width :]
    page_count = tokens_total // PAGE
    page_rows = jnp.concatenate([key_quarter, value_quarter], 1).reshape(
        page_count, PAGE * 2 * quarter_width
    )
    targets = page_targets[:, 0]
    page_numbers = jnp.arange(page_count, dtype=jnp.int32)
    earlier = jnp.sum(
        (
            (targets[None, :] == targets[:, None]) & (page_numbers[None, :] < page_numbers[:, None])
        ).astype(jnp.int32),
        axis=1,
    )
    capacity = 2 * page_count // replica_count
    slot_numbers = targets * capacity + earlier
    placing = (
        jnp.arange(replica_count * capacity, dtype=jnp.int32)[:, None] == slot_numbers[None, :]
    ).astype(jnp.bfloat16)
    outgoing = jnp.dot(placing, page_rows, preferred_element_type=jnp.float32).astype(jnp.bfloat16)
    outgoing = outgoing.reshape(replica_count, capacity, PAGE * 2 * quarter_width)
    incoming = lax.all_to_all(outgoing, "dp", split_axis=0, concat_axis=0, tiled=True)
    cache_pages = incoming.reshape(1, replica_count, capacity, PAGE, 2 * quarter_width)
    return (layer_output, cache_pages)


CORES = 2
CHIPS = 4
MIB = 1 << 20


def in_hbm(array):
    return pltpu.with_memory_space_constraint(array, pltpu.HBM)


def exchanged(block, axis, mask):
    count = lax.axis_size(axis)
    return lax.ppermute(block, axis, [(member, member ^ mask) for member in range(count)])


def vmem_specs(count):
    return [pl.BlockSpec(memory_space=pltpu.VMEM)] * count


def parameters(mebibytes):
    return pltpu.CompilerParams(vmem_limit_bytes=mebibytes * MIB)


def whereabouts():
    member = lax.axis_index("tensor")
    return member // CORES, member % CORES


def position_of(kind, half, block_rows):
    chip, core = whereabouts()
    return ((chip ^ kind) * CORES + (core ^ half)) * block_rows


def positions_along(first, shape, axis, block_rows):
    chip, core = whereabouts()
    bits = block_rows.bit_length() - 1
    place = first + lax.broadcasted_iota(jnp.int32, shape, axis)
    kind = place >> (bits + 1)
    half = (place >> bits) & 1
    return ((((chip ^ kind) << 1) | (core ^ half)) << bits) | (place & (block_rows - 1))


def normalize(blocks, gain_refs, normed_refs, place=0):
    piece = 16
    gains = [gain_ref[...] for gain_ref in gain_refs]
    for number, block_ref in enumerate(blocks):
        block_rows = block_ref.shape[0]
        for part in range(0, block_rows, piece):
            floats = block_ref[part : part + piece, :].astype(jnp.float32)
            center = jnp.mean(floats, axis=-1, keepdims=True)
            shifted = floats - center
            spread = jnp.mean(shifted * shifted, axis=-1, keepdims=True)
            scaled = shifted * lax.rsqrt(spread + epsilon)
            first = place + number * block_rows + part
            for gain, normed_ref in zip(gains, normed_refs):
                normed_ref[first : first + piece, :] = (scaled * gain).astype(jnp.bfloat16)


def project(normed_ref, heads_ref, table_refs, places, joined_ref, first):
    rows = normed_ref.shape[0]
    block_rows = rows // len(places)
    own = slice(first, first + rows)
    cosine, sine_down, sine_up = [
        jnp.concatenate(
            [
                table_ref[pl.ds(pl.multiple_of(place, block_rows), block_rows), :]
                for place in places
            ],
            0,
        )
        for table_ref in table_refs
    ]
    joined_ref[own, :] = jnp.dot(
        normed_ref[...], heads_ref[...], preferred_element_type=jnp.float32
    ).astype(jnp.bfloat16)
    for begin in (0, HD):
        columns = slice(begin, begin + 128)
        turning = joined_ref[own, columns].astype(jnp.float32)
        turned = (
            turning * cosine
            + pltpu.roll(turning, 128 - ROT // 2, 1) * sine_down
            + pltpu.roll(turning, ROT // 2, 1) * sine_up
        )
        joined_ref[own, columns] = turned.astype(jnp.bfloat16)


def hide(normed_ref, upward_ref, hidden_ref, place, chunk=256):
    rows = slice(place, place + normed_ref.shape[0])
    for first in range(0, upward_ref.shape[1], chunk):
        columns = slice(first, first + chunk)
        upward = jnp.dot(
            normed_ref[...], upward_ref[:, columns], preferred_element_type=jnp.float32
        )
        hidden = 0.5 * upward * (1.0 + lax.erf(upward * (0.5**0.5)))
        hidden_ref[rows, columns] = hidden.astype(jnp.bfloat16)


def attend(joined_ref, offsets_ref, first, rows, block_rows):
    tokens = joined_ref.shape[0]
    starts = [
        position_of(place // (2 * block_rows), (place // block_rows) % 2, block_rows)
        for place in range(first, first + rows, block_rows)
    ]
    reach = jnp.concatenate(
        [
            offsets_ref[pl.ds(pl.multiple_of(start, block_rows), block_rows), :]
            for start in starts
        ],
        0,
    )[:, :1].astype(jnp.int32)
    row = positions_along(first, (rows, 1), 0, block_rows)
    column = positions_along(0, (1, tokens), 1, block_rows)
    allowed = (column <= row) & (column >= row - reach)
    scores = lax.dot_general(
        joined_ref[first : first + rows, :HD],
        joined_ref[:, HD : 2 * HD],
        (((1,), (1,)), ((), ())),
        preferred_element_type=jnp.float32,
    ) * (HD ** (-0.5))
    peak = jnp.max(jnp.where(allowed, scores, -jnp.inf), axis=1, keepdims=True)
    weights = jnp.where(allowed, jnp.exp(scores - peak), 0.0)
    weight_sum = jnp.sum(weights, axis=1, keepdims=True)
    mixed = jnp.dot(
        weights.astype(jnp.bfloat16), joined_ref[:, 2 * HD :], preferred_element_type=jnp.float32
    )
    return (mixed / weight_sum).astype(jnp.bfloat16)


def make_tables(segments_ref, offsets_ref, cosine_ref, sine_down_ref, sine_up_ref):
    tokens = segments_ref.shape[1]
    shape = (tokens, tokens)
    rows = lax.broadcasted_iota(jnp.int32, shape, 0)
    columns = lax.broadcasted_iota(jnp.int32, shape, 1)
    across = jnp.broadcast_to(segments_ref[...], shape).astype(jnp.float32)
    down = jnp.sum(jnp.where(rows == columns, across, 0.0), axis=1, keepdims=True)
    earlier = (across == down) & (columns < rows)
    offsets = jnp.sum(jnp.where(earlier, 1.0, 0.0), axis=1, keepdims=True)
    offsets_ref[...] = jnp.broadcast_to(offsets, offsets_ref.shape)
    half = ROT // 2
    lane = lax.broadcasted_iota(jnp.int32, (tokens, 128), 1)
    step = (lane & (half - 1)).astype(jnp.float32)
    frequency = jnp.exp(step * (-2.0 * math.log(rotary_base) / ROT))
    angles = offsets * frequency
    sine = jnp.sin(angles)
    cosine_ref[...] = jnp.where(lane < ROT, jnp.cos(angles), 1.0)
    sine_down_ref[...] = jnp.where(lane < half, -sine, 0.0)
    sine_up_ref[...] = jnp.where((lane >= half) & (lane < ROT), sine, 0.0)


def make_destinations(targets_ref, destinations_ref, replica_count, block_rows):
    page_count = targets_ref.shape[1]
    tokens = destinations_ref.shape[1]
    capacity = 2 * page_count // replica_count
    square = (page_count, page_count)
    rows = lax.broadcasted_iota(jnp.int32, square, 0)
    columns = lax.broadcasted_iota(jnp.int32, square, 1)
    across = jnp.broadcast_to(targets_ref[...], square).astype(jnp.float32)
    down = jnp.sum(jnp.where(rows == columns, across, 0.0), axis=1, keepdims=True)
    earlier = jnp.where((across == down) & (columns < rows), 1.0, 0.0)
    slots = jnp.sum(earlier, axis=1, keepdims=True).astype(jnp.int32)
    slots = (down.astype(jnp.int32) ^ lax.axis_index("dp")) * capacity + slots
    positions = positions_along(0, (1, tokens), 1, block_rows)
    bits = PAGE.bit_length() - 1
    pages = lax.broadcasted_iota(jnp.int32, (page_count, tokens), 0)
    chosen = jnp.where(pages == positions >> bits, slots.astype(jnp.float32), 0.0)
    slot = jnp.sum(chosen, axis=0, keepdims=True).astype(jnp.int32)
    destinations_ref[...] = slot * PAGE + (positions & (PAGE - 1))


def copies_in(sources, targets, sems):
    copies = []
    for number, (source, target) in enumerate(zip(sources, targets)):
        parts = 4 if source.shape[0] >= 256 else 1
        rows = source.shape[0] // parts
        places = [pl.ds(part * rows, rows) for part in range(parts)]
        copies.append(
            [
                pltpu.make_async_copy(source.at[place], target.at[place], sems.at[number, part])
                for part, place in enumerate(places)
            ]
        )
    for copy in sum(copies, []):
        copy.start()
    return copies


def wait_for(copies):
    for copy in copies:
        copy.wait()


def own_kernel(count, replica_count, *refs):
    sources, targets = refs[:count], refs[count : 2 * count]
    offsets_ref, *table_refs, destinations_ref, joined_ref, hidden_ref = refs[2 * count : -3]
    attention_scr, feedforward_scr, sems = refs[-3:]
    copies = copies_in(sources, targets, sems)
    segments_ref, targets_ref, states_ref, *gain_refs, heads_ref, upward_ref, _ = targets
    block_rows = states_ref.shape[0]
    wait_for(copies[0])
    make_tables(segments_ref, offsets_ref, *table_refs)
    wait_for(copies[1])
    make_destinations(targets_ref, destinations_ref, replica_count, block_rows)
    for number in (2, 3, 4):
        wait_for(copies[number])
    normalize([states_ref], gain_refs, [attention_scr, feedforward_scr])
    wait_for(copies[5])
    places = [position_of(0, 0, block_rows)]
    project(attention_scr, heads_ref, table_refs, places, joined_ref, 0)
    wait_for(copies[6])
    hide(feedforward_scr, upward_ref, hidden_ref, 0)
    wait_for(copies[7])


def own_rows(staged, replica_count):
    tokens = staged[0].shape[1]
    rows, width = staged[2].shape
    hidden_width = staged[6].shape[1]
    shapes = [pltpu.VMEM(array.shape, array.dtype) for array in staged]
    shapes += [pltpu.VMEM((tokens, 128), jnp.float32)] * 4
    shapes += [
        pltpu.VMEM((1, tokens), jnp.int32),
        pltpu.VMEM((rows, 3 * HD), jnp.bfloat16),
        pltpu.VMEM((rows, hidden_width), jnp.bfloat16),
    ]
    count = len(staged)
    return pl.pallas_call(
        functools.partial(own_kernel, count, replica_count),
        out_shape=shapes,
        in_specs=[pl.BlockSpec(memory_space=pltpu.HBM)] * count,
        out_specs=vmem_specs(len(shapes)),
        scratch_shapes=[
            pltpu.VMEM((rows, width), jnp.bfloat16),
            pltpu.VMEM((rows, width), jnp.bfloat16),
            pltpu.SemaphoreType.DMA((count, 4)),
        ],
        compiler_params=parameters(12),
        cost_estimate=pl.CostEstimate(
            flops=2 * rows * width * (3 * HD + hidden_width),
            bytes_accessed=sum(array.nbytes for array in staged),
            transcendentals=rows * hidden_width,
        ),
        name="own_rows",
    )(*[in_hbm(array) for array in staged])


def middle_kernel(origins, *refs):
    count = len(origins)
    blocks, (gain_a, gain_f, heads_ref, upward_ref) = refs[:count], refs[count : count + 4]
    table_refs, refs = refs[count + 4 : count + 7], refs[count + 7 :]
    staged = (len(refs) - 5) // 2
    sources, (joined_ref, hidden_ref), refs = refs[:staged], refs[staged:][:2], refs[staged + 2 :]
    targets, (attention_scr, feedforward_scr, sems) = refs[:staged], refs[staged:]
    copies = copies_in(sources, targets, sems)
    block_rows = blocks[0].shape[0]
    normalize(blocks, [gain_a, gain_f], [attention_scr, feedforward_scr])
    places = [position_of(kind, half, block_rows) for kind, half in origins]
    project(attention_scr, heads_ref, table_refs, places, joined_ref, 0)
    hide(feedforward_scr, upward_ref, hidden_ref, 0)
    wait_for(sum(copies, []))


def middle_rows(name, origins, blocks, gains, weights, tables, *staged):
    block_rows, width = blocks[0].shape
    rows = len(blocks) * block_rows
    hidden_width = weights[1].shape[1]
    return pl.pallas_call(
        functools.partial(middle_kernel, origins),
        out_shape=[
            pltpu.VMEM((rows, 3 * HD), jnp.bfloat16),
            pltpu.VMEM((rows, hidden_width), jnp.bfloat16),
        ]
        + [pltpu.VMEM(array.shape, array.dtype) for array in staged],
        in_specs=vmem_specs(len(blocks) + 2 + 2 + 3)
        + [pl.BlockSpec(memory_space=pltpu.HBM)] * len(staged),
        out_specs=vmem_specs(2 + len(staged)),
        scratch_shapes=[
            pltpu.VMEM((rows, width), jnp.bfloat16),
            pltpu.VMEM((rows, width), jnp.bfloat16),
            pltpu.SemaphoreType.DMA((max(len(staged), 1), 4)),
        ],
        compiler_params=parameters(12),
        cost_estimate=pl.CostEstimate(
            flops=2 * rows * width * (3 * HD + hidden_width),
            bytes_accessed=MIB,
            transcendentals=rows * hidden_width,
        ),
        name=name,
    )(*blocks, *gains, *weights, *tables, *[in_hbm(array) for array in staged])


def last_kernel(*refs):
    block_ref, *normed_refs = refs[:3]
    gain_a, gain_f, heads_ref, upward_ref, downward_ref, output_ref = refs[3:9]
    offsets_ref, *table_refs = refs[9:13]
    own_joined_ref, middle_joined_ref = refs[13:15]
    joined_ref, fed_ref, sibling_ref, own_ref = refs[15:19]
    attention_scr, feedforward_scr, hidden_scr = refs[19:]
    block_rows = block_ref.shape[0]
    tokens = joined_ref.shape[0]
    first = tokens - attention_scr.shape[0]
    count = normed_refs[0].shape[0]
    normalize([block_ref], [gain_a, gain_f], [attention_scr, feedforward_scr], count)
    for normed_ref, normed_scr in zip(normed_refs, (attention_scr, feedforward_scr)):
        normed_scr[:count, :] = normed_ref[...]
    joined_ref[:block_rows, :] = own_joined_ref[...]
    joined_ref[block_rows:first, :] = middle_joined_ref[...]
    origins = ((CHIPS - 2, 1), (CHIPS - 1, 0), (CHIPS - 1, 1))
    places = [position_of(kind, half, block_rows) for kind, half in origins]
    project(attention_scr, heads_ref, table_refs, places, joined_ref, first)
    rows = CORES * block_rows
    hide(feedforward_scr, upward_ref, hidden_scr, 0, 512)
    attended = attend(joined_ref, offsets_ref, tokens - rows, rows, block_rows)
    chunk = 1024
    for begin in range(0, downward_ref.shape[1], chunk):
        columns = slice(begin, begin + chunk)
        fed = jnp.dot(hidden_scr[...], downward_ref[:, columns], preferred_element_type=jnp.float32)
        fed_ref[:, columns] = fed[:block_rows]
        partial = fed[block_rows:] + jnp.dot(
            attended, output_ref[:, columns], preferred_element_type=jnp.float32
        )
        own_ref[:, columns] = partial[:block_rows]
        sibling_ref[:, columns] = partial[block_rows:].astype(jnp.bfloat16)


def last_rows(block, normed, gains, weights, tables, own_joined, middle_joined):
    block_rows, width = block.shape
    rows = normed[0].shape[0] + block_rows
    hidden_width = weights[1].shape[1]
    tokens = CHIPS * CORES * block_rows
    return pl.pallas_call(
        last_kernel,
        out_shape=[
            pltpu.VMEM((tokens, 3 * HD), jnp.bfloat16),
            pltpu.VMEM((block_rows, width), jnp.float32),
            pltpu.VMEM((block_rows, width), jnp.bfloat16),
            pltpu.VMEM((block_rows, width), jnp.float32),
        ],
        in_specs=vmem_specs(1 + 2 + 2 + 4 + 4 + 2),
        out_specs=vmem_specs(4),
        scratch_shapes=[
            pltpu.VMEM((rows, width), jnp.bfloat16),
            pltpu.VMEM((rows, width), jnp.bfloat16),
            pltpu.VMEM((rows, hidden_width), jnp.bfloat16),
        ],
        compiler_params=parameters(12),
        cost_estimate=pl.CostEstimate(
            flops=2 * rows * width * (3 * HD + HD + 2 * hidden_width),
            bytes_accessed=MIB,
            transcendentals=rows * hidden_width,
        ),
        name="last_rows",
    )(block, *normed, *gains, *weights, *tables, own_joined, middle_joined)


def fed_kernel(own_hidden_ref, middle_hidden_ref, downward_ref, *refs):
    blocks, gain_refs, (fed_ref, *normed_refs) = refs[:2], refs[2:4], refs[4:]
    normalize(blocks, gain_refs, normed_refs)
    hidden = jnp.concatenate([own_hidden_ref[...], middle_hidden_ref[...]], 0)
    chunk = 512
    for begin in range(0, downward_ref.shape[1], chunk):
        columns = slice(begin, begin + chunk)
        fed_ref[:, columns] = jnp.dot(
            hidden, downward_ref[:, columns], preferred_element_type=jnp.float32
        )


def fed_rows(own_hidden, middle_hidden, downward_weight, blocks, gains):
    rows = own_hidden.shape[0] + middle_hidden.shape[0]
    depth, width = downward_weight.shape
    normed = pltpu.VMEM((len(blocks) * blocks[0].shape[0], width), jnp.bfloat16)
    return pl.pallas_call(
        fed_kernel,
        out_shape=[pltpu.VMEM((rows, width), jnp.float32), normed, normed],
        in_specs=vmem_specs(7),
        out_specs=vmem_specs(3),
        compiler_params=parameters(12),
        cost_estimate=pl.CostEstimate(
            flops=2 * rows * depth * width, bytes_accessed=MIB, transcendentals=0
        ),
        name="fed_rows",
    )(own_hidden, middle_hidden, downward_weight, *blocks, *gains)


def rest_kernel(joined_ref, offsets_ref, output_ref, fed_ref, fed_beside_ref, *refs):
    near_ref, far_ref, *owns = refs
    block_rows = far_ref.shape[0]
    rows = fed_ref.shape[0] + fed_beside_ref.shape[0]
    attended = attend(joined_ref, offsets_ref, 0, rows, block_rows)
    chunk = 512
    for begin in range(0, output_ref.shape[1], chunk):
        columns = slice(begin, begin + chunk)
        fed = jnp.concatenate([fed_ref[:, columns], fed_beside_ref[:, columns]], 0)
        partial = fed + jnp.dot(
            attended, output_ref[:, columns], preferred_element_type=jnp.float32
        )
        for number, own_ref in enumerate(owns):
            first = CORES * number * block_rows
            middle = first + block_rows
            own_ref[:, columns] = partial[first:middle]
            sibling = partial[middle : middle + block_rows].astype(jnp.bfloat16)
            if number < near_ref.shape[0]:
                near_ref[number, :, columns] = sibling
            else:
                far_ref[:, columns] = sibling


def rest_rows(joined, offsets, output_weight, fed, fed_beside):
    width = fed.shape[1]
    rows = fed.shape[0] + fed_beside.shape[0]
    count = CHIPS - 1
    shape = (rows // (CORES * count), width)
    shapes = [pltpu.VMEM((count - 1, *shape), jnp.bfloat16), pltpu.VMEM(shape, jnp.bfloat16)]
    shapes += [pltpu.VMEM(shape, jnp.float32)] * count
    return pl.pallas_call(
        rest_kernel,
        out_shape=shapes,
        in_specs=vmem_specs(5),
        out_specs=vmem_specs(2 + count),
        compiler_params=parameters(12),
        cost_estimate=pl.CostEstimate(
            flops=2 * rows * width * HD,
            bytes_accessed=MIB,
            transcendentals=rows * joined.shape[0],
        ),
        name="rest_rows",
    )(joined, offsets, output_weight, fed, fed_beside)


def pages_kernel(joined_ref, destinations_ref, *page_refs):
    tokens = joined_ref.shape[0]
    slot_rows = page_refs[0].shape[0] * PAGE
    for number, page_ref in enumerate(page_refs):
        shape = (slot_rows, tokens)
        row = number * slot_rows + lax.broadcasted_iota(jnp.int32, shape, 0)
        placing = jnp.where(row == destinations_ref[...], 1.0, 0.0).astype(jnp.bfloat16)
        rows = jnp.dot(placing, joined_ref[:, HD:], preferred_element_type=jnp.float32)
        page_ref[...] = rows.astype(jnp.bfloat16).reshape(page_ref.shape)


def cached_pages(joined, destinations, replica_count):
    tokens = joined.shape[0]
    capacity = 2 * (tokens // PAGE) // replica_count
    shapes = [pltpu.VMEM((capacity, PAGE, 2 * HD), jnp.bfloat16)] * replica_count
    return pl.pallas_call(
        pages_kernel,
        out_shape=shapes,
        in_specs=vmem_specs(2),
        out_specs=vmem_specs(len(shapes)),
        compiler_params=parameters(8),
        cost_estimate=pl.CostEstimate(flops=0, bytes_accessed=MIB, transcendentals=0),
        name="cached_pages",
    )(joined, destinations)


def add_kernel(*refs):
    total = refs[0][...].astype(jnp.float32)
    for ref in refs[1:-1]:
        total = total + ref[...].astype(jnp.float32)
    refs[-1][...] = total.astype(refs[-1].dtype)


def added(name, *parts):
    return pl.pallas_call(
        add_kernel,
        out_shape=pltpu.VMEM(parts[0].shape, jnp.bfloat16),
        in_specs=vmem_specs(len(parts)),
        out_specs=pl.BlockSpec(memory_space=pltpu.VMEM),
        compiler_params=parameters(4),
        name=name,
    )(*parts)


def near_kernel(received_ref, zero_ref, one_ref, hidden_ref, first_ref, base_ref):
    first_ref[...] = (one_ref[...] + received_ref[1].astype(jnp.float32)).astype(jnp.bfloat16)
    zero = zero_ref[...] + received_ref[0].astype(jnp.float32)
    base_ref[...] = zero + hidden_ref[...].astype(jnp.float32)


def near_sums(received, owns, hidden):
    shape = hidden.shape
    return pl.pallas_call(
        near_kernel,
        out_shape=[pltpu.VMEM(shape, jnp.bfloat16), pltpu.VMEM(shape, jnp.float32)],
        in_specs=vmem_specs(4),
        out_specs=vmem_specs(2),
        compiler_params=parameters(4),
        name="near_sums",
    )(received, *owns, hidden)


def place_kernel(masks, *refs):
    group = lax.axis_index("dp")
    count = len(masks)
    pages, (part_ref, base_ref) = refs[:count], refs[count : count + 2]
    cache_ref, total_ref, sems = refs[count + 2 :]
    copies = [
        pltpu.make_async_copy(page_ref, cache_ref.at[0, group ^ mask], sems.at[number])
        for number, (mask, page_ref) in enumerate(zip(masks, pages))
    ]
    for copy in copies:
        copy.start()
    total_ref[...] = base_ref[...] + part_ref[...].astype(jnp.float32)
    for copy in copies:
        copy.wait()


def placed(masks, pages, part, base, replica_count):
    count = len(pages)
    return pl.pallas_call(
        functools.partial(place_kernel, masks),
        out_shape=[
            jax.ShapeDtypeStruct((1, replica_count) + pages[0].shape, pages[0].dtype),
            pltpu.VMEM(base.shape, base.dtype),
        ],
        in_specs=[pl.BlockSpec(memory_space=pl.ANY)] * count + vmem_specs(2),
        out_specs=[pl.BlockSpec(memory_space=pltpu.HBM)] + vmem_specs(1),
        scratch_shapes=[pltpu.SemaphoreType.DMA((count,))],
        compiler_params=parameters(4),
        name="placed",
    )(*pages, part, base)


def finish_kernel(masks, base_ref, *refs):
    count = len(masks)
    *parts, _, output_ref, cache_ref, total_scr, sems = refs
    parts, pages = parts[:-count], parts[-count:]
    group = lax.axis_index("dp")
    copies = [
        pltpu.make_async_copy(page_ref, cache_ref.at[0, group ^ mask], sems.at[number])
        for number, (mask, page_ref) in enumerate(zip(masks, pages))
    ]
    for copy in copies:
        copy.start()
    rows = 8
    for first in range(0, base_ref.shape[0], 2 * rows):
        both = slice(first, first + 2 * rows)
        total = base_ref[both, :]
        for part_ref in parts:
            total = total + part_ref[both, :].astype(jnp.float32)
        total_scr[both, :] = total
        for place in (first, first + rows):
            piece = pl.ds(place, rows)
            sem = sems.at[count + place // rows]
            copies.append(pltpu.make_async_copy(total_scr.at[piece], output_ref.at[piece], sem))
            copies[-1].start()
    for copy in copies:
        copy.wait()


def finished(base, parts, masks, pages, cache):
    count = len(pages)
    return pl.pallas_call(
        functools.partial(finish_kernel, masks),
        out_shape=[
            jax.ShapeDtypeStruct(base.shape, base.dtype),
            jax.ShapeDtypeStruct(cache.shape, cache.dtype),
        ],
        in_specs=vmem_specs(1 + len(parts))
        + [pl.BlockSpec(memory_space=pl.ANY)] * count
        + [pl.BlockSpec(memory_space=pltpu.HBM)],
        out_specs=[pl.BlockSpec(memory_space=pltpu.HBM)] * 2,
        scratch_shapes=[
            pltpu.VMEM(base.shape, base.dtype),
            pltpu.SemaphoreType.DMA((count + base.shape[0] // 8,)),
        ],
        input_output_aliases={1 + len(parts) + count: 1},
        compiler_params=parameters(4),
        name="finished",
    )(base, *parts, *pages, cache)


def shards_whole_heads(
    hidden_states,
    attention_gain,
    feedforward_gain,
    heads_weight,
    output_weight,
    upward_weight,
    downward_weight,
    segments,
    page_targets,
):
    replica_count = lax.axis_size("dp")
    to_chip = [mask * CORES for mask in range(CHIPS)]
    second = exchanged(hidden_states, "tensor", to_chip[2])
    first = exchanged(hidden_states, "tensor", to_chip[1])
    beside = exchanged(hidden_states, "tensor", 1)
    staged = (
        segments,
        page_targets.reshape(1, -1),
        hidden_states,
        attention_gain[None],
        feedforward_gain[None],
        heads_weight,
        upward_weight,
        downward_weight,
    )
    staged = own_rows(staged, replica_count)
    hidden, gains, weights, tables = staged[2], staged[3:5], staged[5:8], staged[8:12]
    heads, upward, downward = weights
    destinations, own_joined, own_hidden = staged[12:]

    first, second, own_joined = lax.optimization_barrier((first, second, own_joined))
    first_beside = exchanged(first, "tensor", 1)
    third = exchanged(second, "tensor", to_chip[1])
    middle_joined, middle_hidden, output = middle_rows(
        "middle_rows",
        ((0, 1), (1, 0), (1, 1), (2, 0)),
        (beside, first, first_beside, second),
        gains,
        (heads, upward),
        tables[1:],
        output_weight,
    )
    second, middle_joined = lax.optimization_barrier((second, middle_joined))
    second_beside = exchanged(second, "tensor", 1)
    third, second_beside, middle_joined, middle_hidden = lax.optimization_barrier(
        (third, second_beside, middle_joined, middle_hidden)
    )
    third_beside = exchanged(third, "tensor", 1)
    fed, *normed = fed_rows(own_hidden, middle_hidden, downward, (second_beside, third), gains)
    joined, fed_beside, sibling, own = last_rows(
        third_beside,
        normed,
        gains,
        (heads, upward, downward, output),
        tables,
        own_joined,
        middle_joined,
    )

    received = exchanged(sibling, "tensor", 1)
    partials = rest_rows(joined, tables[0], output, fed, fed_beside)
    near_sibling, far_sibling, *owns = partials
    near_received = exchanged(near_sibling, "tensor", 1)
    third_sum = added("third_added", own, received)
    third_sum, far_sibling, joined = lax.optimization_barrier((third_sum, far_sibling, joined))
    passing = exchanged(third_sum, "tensor", to_chip[1])
    far_received = exchanged(far_sibling, "tensor", 1)
    pages = cached_pages(joined, destinations, replica_count)
    early, late = (3,), (1, 2)
    arriving = [exchanged(pages[mask], "dp", mask) for mask in early]
    first_sum, base = near_sums(near_received, owns[:2], hidden)
    from_first = exchanged(first_sum, "tensor", to_chip[1])
    second_sum = added("second_added", owns[2], passing, far_received)
    second_sum, late_pages = lax.optimization_barrier(
        (second_sum, [pages[mask] for mask in late])
    )
    from_second = exchanged(second_sum, "tensor", to_chip[2])
    late_pages = [exchanged(page, "dp", mask) for mask, page in zip(late, late_pages)]
    cache_pages, base = placed((0,) + early, [pages[0]] + arriving, from_first, base, replica_count)
    return tuple(finished(base, (from_second,), late, late_pages, cache_pages))


def solution(mesh):
    whole_heads = mesh.shape["tensor"] == H and mesh.shape["dp"] == 4
    shards = shards_whole_heads if whole_heads else shards_split_heads
    in_specs = (
        P(("dp", "tensor"), None),
        P(),
        P(),
        P(None, "tensor"),
        P("tensor", None),
        P(None, "tensor"),
        P("tensor", None),
        P("dp", None),
        P("dp", None),
    )
    out_specs = (P(("dp", "tensor"), None), P("dp", None, None, None, "tensor"))
    return jax.shard_map(shards, mesh=mesh, in_specs=in_specs, out_specs=out_specs, check_vma=False)
```

```python
import functools
import math

import jax
import jax.numpy as jnp
from jax import lax
from jax.experimental import pallas as pl
from jax.experimental.pallas import tpu as pltpu
from jax.sharding import PartitionSpec as P

H = 8
HD = 256
ROT = 64
PAGE = 16


epsilon = 1e-05
rotary_base = 10000.0
key_block = 256


def shortened(array):

    def short(part):
        return part.astype(jnp.bfloat16) if part.dtype == jnp.float32 else part

    return jax.tree.map(short, array)


def swapped(block, axis, apart):
    count = lax.axis_size(axis)
    route = []
    for low in range(count):
        high = low | 1 << apart
        if high != low and high < count:
            route += [(low, high), (high, low)]
    return lax.ppermute(block, axis, route)


def layer_norm(values, gain):
    floats = values.astype(jnp.float32)
    center = jnp.mean(floats, axis=-1, keepdims=True)
    shifted = floats - center
    spread = jnp.mean(shifted * shifted, axis=-1, keepdims=True)
    return (shifted * lax.rsqrt(spread + epsilon) * gain).astype(jnp.bfloat16)


def positions_of(stream):
    indices = jnp.arange(stream.shape[0], dtype=jnp.int32)
    boundary = jnp.concatenate([jnp.ones((1,), dtype=bool), stream[1:] != stream[:-1]])
    starting = lax.cummax(jnp.where(boundary, indices, jnp.zeros_like(indices)), axis=0)
    return (indices, starting)


def rotate_heads(vectors, offsets, rotary_dims):
    half_dims = rotary_dims // 2
    frequency = jnp.exp(
        jnp.arange(half_dims, dtype=jnp.float32) * (-2.0 * math.log(rotary_base) / rotary_dims)
    )
    angles = offsets.astype(jnp.float32)[:, None] * frequency[None, :]
    cosine = jnp.cos(angles)
    sine = jnp.sin(angles)
    floats = vectors.astype(jnp.float32)
    leading = floats[..., :half_dims]
    trailing = floats[..., half_dims:rotary_dims]
    rotated = jnp.concatenate(
        [
            leading * cosine - trailing * sine,
            trailing * cosine + leading * sine,
            floats[..., rotary_dims:],
        ],
        axis=-1,
    )
    return rotated.astype(jnp.bfloat16)


def shards_split_heads(
    hidden_states,
    attention_gain,
    feedforward_gain,
    heads_weight,
    output_weight,
    upward_weight,
    downward_weight,
    segments,
    page_targets,
):
    tensor_count = lax.axis_size("tensor")
    replica_count = lax.axis_size("dp")
    tensor_index = lax.axis_index("tensor")
    quarters = tensor_count // H
    quarter_width = HD // quarters
    quarter_index = tensor_index % quarters
    stream = segments[0]
    tokens_total = stream.shape[0]
    level_count = quarters.bit_length() - 1
    normed_attention = layer_norm(hidden_states, attention_gain)
    normed_feedforward = layer_norm(hidden_states, feedforward_gain)
    shard_rows = lax.all_gather(
        (normed_attention, normed_feedforward), "tensor", axis=0, tiled=True
    )
    joined_rows = jnp.dot(shard_rows[0], heads_weight, preferred_element_type=jnp.float32).astype(
        jnp.bfloat16
    )
    upward = jnp.dot(shard_rows[1], upward_weight, preferred_element_type=jnp.float32)
    hidden_rows = jax.nn.gelu(upward, approximate=False).astype(jnp.bfloat16)
    hidden = hidden_rows
    pieces = (
        joined_rows.reshape(tokens_total, 3, quarter_width)
        .transpose(1, 0, 2)
        .reshape(1, 3, tokens_total * quarter_width)
    )
    for bit_number in range(level_count):
        partner = swapped(shortened(pieces), "tensor", bit_number).astype(pieces.dtype)
        lower = tensor_index >> bit_number & 1 == 0
        pieces = jnp.where(
            lower, jnp.concatenate([pieces, partner], 0), jnp.concatenate([partner, pieces], 0)
        )
    whole_head = (
        pieces.reshape(quarters, 3, tokens_total, quarter_width)
        .transpose(1, 2, 0, 3)
        .reshape(3, tokens_total, HD)
    )
    indices, starting = positions_of(stream)
    offsets = indices - starting
    queries = rotate_heads(whole_head[0], offsets, ROT)
    keys = rotate_heads(whole_head[1], offsets, ROT)
    values = whole_head[2]
    block_rows = tokens_total // (2 * quarters)
    score_scale = HD ** (-0.5)

    def attend_block(block_number):
        first_row = block_number * block_rows
        block_queries = lax.dynamic_slice_in_dim(queries, first_row, block_rows, 0)
        query_segments = lax.dynamic_slice_in_dim(stream, first_row, block_rows, 0)
        query_indices = first_row + jnp.arange(block_rows, dtype=jnp.int32)
        lowest = lax.dynamic_index_in_dim(starting, first_row, 0, keepdims=False) // key_block
        highest = (first_row + block_rows + key_block - 1) // key_block

        def scores_of(key_number):
            key_first = key_number * key_block
            key_indices = key_first + jnp.arange(key_block, dtype=jnp.int32)
            scores = (
                jnp.dot(block_queries, keys.T, preferred_element_type=jnp.float32) * score_scale
            )
            allowed = (stream[None, :] == query_segments[:, None]) & (
                key_indices[None, :] <= query_indices[:, None]
            )
            return (scores, allowed)

        def find_peak(key_number, peak):
            scores, allowed = scores_of(key_number)
            return jnp.maximum(peak, jnp.max(jnp.where(allowed, scores, -jnp.inf), axis=1))

        peak = lax.fori_loop(
            lowest, highest, find_peak, jnp.full((block_rows,), -jnp.inf, jnp.float32)
        )

        def accumulate(key_number, state):
            weight_sum, mixed_sum = state
            scores, allowed = scores_of(key_number)
            weights = jnp.where(allowed, jnp.exp(scores - peak[:, None]), 0.0)
            mixed_next = mixed_sum + jnp.dot(
                weights.astype(jnp.bfloat16), values, preferred_element_type=jnp.float32
            )
            return (weight_sum + jnp.sum(weights, axis=1), mixed_next)

        start_state = (
            jnp.zeros((block_rows,), jnp.float32),
            jnp.zeros((block_rows, HD), jnp.float32),
        )
        weight_sum, mixed_sum = lax.fori_loop(lowest, highest, accumulate, start_state)
        return (mixed_sum / weight_sum[:, None]).astype(jnp.bfloat16)

    own_blocks = (2 * quarter_index, 2 * quarter_index + 1)
    own_rows = jnp.concatenate([attend_block(own_blocks[0]), attend_block(own_blocks[1])], 0)[None]
    for bit_number in range(level_count):
        partner = swapped(own_rows, "tensor", bit_number)
        lower = tensor_index >> bit_number & 1 == 0
        own_rows = jnp.where(
            lower, jnp.concatenate([own_rows, partner], 0), jnp.concatenate([partner, own_rows], 0)
        )
    attended = own_rows.reshape(tokens_total, HD)
    attended_quarter = lax.dynamic_slice_in_dim(
        attended, quarter_index * quarter_width, quarter_width, 1
    )
    hidden_rows = hidden
    summed = lax.psum_scatter(
        (
            jnp.dot(attended_quarter, output_weight, preferred_element_type=jnp.float32)
            + jnp.dot(hidden_rows, downward_weight, preferred_element_type=jnp.float32)
        ).astype(jnp.bfloat16),
        "tensor",
        scatter_dimension=0,
        tiled=True,
    ).astype(jnp.float32)
    layer_output = hidden_states.astype(jnp.float32) + summed
    key_quarter = lax.dynamic_slice_in_dim(keys, quarter_index * quarter_width, quarter_width, 1)
    value_quarter = joined_rows[:, 2 * quarter_width :]
    page_count = tokens_total // PAGE
    page_rows = jnp.concatenate([key_quarter, value_quarter], 1).reshape(
        page_count, PAGE * 2 * quarter_width
    )
    targets = page_targets[:, 0]
    page_numbers = jnp.arange(page_count, dtype=jnp.int32)
    earlier = jnp.sum(
        (
            (targets[None, :] == targets[:, None]) & (page_numbers[None, :] < page_numbers[:, None])
        ).astype(jnp.int32),
        axis=1,
    )
    capacity = 2 * page_count // replica_count
    slot_numbers = targets * capacity + earlier
    placing = (
        jnp.arange(replica_count * capacity, dtype=jnp.int32)[:, None] == slot_numbers[None, :]
    ).astype(jnp.bfloat16)
    outgoing = jnp.dot(placing, page_rows, preferred_element_type=jnp.float32).astype(jnp.bfloat16)
    outgoing = outgoing.reshape(replica_count, capacity, PAGE * 2 * quarter_width)
    incoming = lax.all_to_all(outgoing, "dp", split_axis=0, concat_axis=0, tiled=True)
    cache_pages = incoming.reshape(1, replica_count, capacity, PAGE, 2 * quarter_width)
    return (layer_output, cache_pages)


CORES = 2
CHIPS = 4
MIB = 1 << 20


def in_hbm(array):
    return pltpu.with_memory_space_constraint(array, pltpu.HBM)


def exchanged(block, axis, mask):
    count = lax.axis_size(axis)
    return lax.ppermute(block, axis, [(member, member ^ mask) for member in range(count)])


def vmem_specs(count):
    return [pl.BlockSpec(memory_space=pltpu.VMEM)] * count


def parameters(mebibytes):
    return pltpu.CompilerParams(vmem_limit_bytes=mebibytes * MIB)


def whereabouts():
    member = lax.axis_index("tensor")
    return member // CORES, member % CORES


def position_of(kind, half, block_rows):
    chip, core = whereabouts()
    return ((chip ^ kind) * CORES + (core ^ half)) * block_rows


def positions_along(first, shape, axis, block_rows):
    chip, core = whereabouts()
    bits = block_rows.bit_length() - 1
    place = first + lax.broadcasted_iota(jnp.int32, shape, axis)
    kind = place >> (bits + 1)
    half = (place >> bits) & 1
    return ((((chip ^ kind) << 1) | (core ^ half)) << bits) | (place & (block_rows - 1))


def normalize(blocks, gain_refs, normed_refs, place=0):
    piece = 16
    gains = [gain_ref[...] for gain_ref in gain_refs]
    for number, block_ref in enumerate(blocks):
        block_rows = block_ref.shape[0]
        for part in range(0, block_rows, piece):
            floats = block_ref[part : part + piece, :].astype(jnp.float32)
            center = jnp.mean(floats, axis=-1, keepdims=True)
            shifted = floats - center
            spread = jnp.mean(shifted * shifted, axis=-1, keepdims=True)
            scaled = shifted * lax.rsqrt(spread + epsilon)
            first = place + number * block_rows + part
            for gain, normed_ref in zip(gains, normed_refs):
                normed_ref[first : first + piece, :] = (scaled * gain).astype(jnp.bfloat16)


def project(normed_ref, heads_ref, table_refs, places, joined_ref, first):
    rows = normed_ref.shape[0]
    block_rows = rows // len(places)
    own = slice(first, first + rows)
    cosine, sine_down, sine_up = [
        jnp.concatenate(
            [
                table_ref[pl.ds(pl.multiple_of(place, block_rows), block_rows), :]
                for place in places
            ],
            0,
        )
        for table_ref in table_refs
    ]
    joined_ref[own, :] = jnp.dot(
        normed_ref[...], heads_ref[...], preferred_element_type=jnp.float32
    ).astype(jnp.bfloat16)
    for begin in (0, HD):
        columns = slice(begin, begin + 128)
        turning = joined_ref[own, columns].astype(jnp.float32)
        turned = (
            turning * cosine
            + pltpu.roll(turning, 128 - ROT // 2, 1) * sine_down
            + pltpu.roll(turning, ROT // 2, 1) * sine_up
        )
        joined_ref[own, columns] = turned.astype(jnp.bfloat16)


def hide(normed_ref, upward_ref, hidden_ref, place, chunk=256):
    rows = slice(place, place + normed_ref.shape[0])
    for first in range(0, upward_ref.shape[1], chunk):
        columns = slice(first, first + chunk)
        upward = jnp.dot(
            normed_ref[...], upward_ref[:, columns], preferred_element_type=jnp.float32
        )
        hidden = 0.5 * upward * (1.0 + lax.erf(upward * (0.5**0.5)))
        hidden_ref[rows, columns] = hidden.astype(jnp.bfloat16)


def attend(joined_ref, offsets_ref, first, rows, block_rows):
    tokens = joined_ref.shape[0]
    starts = [
        position_of(place // (2 * block_rows), (place // block_rows) % 2, block_rows)
        for place in range(first, first + rows, block_rows)
    ]
    reach = jnp.concatenate(
        [
            offsets_ref[pl.ds(pl.multiple_of(start, block_rows), block_rows), :]
            for start in starts
        ],
        0,
    )[:, :1].astype(jnp.int32)
    row = positions_along(first, (rows, 1), 0, block_rows)
    column = positions_along(0, (1, tokens), 1, block_rows)
    allowed = (column <= row) & (column >= row - reach)
    scores = lax.dot_general(
        joined_ref[first : first + rows, :HD],
        joined_ref[:, HD : 2 * HD],
        (((1,), (1,)), ((), ())),
        preferred_element_type=jnp.float32,
    ) * (HD ** (-0.5))
    peak = jnp.max(jnp.where(allowed, scores, -jnp.inf), axis=1, keepdims=True)
    weights = jnp.where(allowed, jnp.exp(scores - peak), 0.0)
    weight_sum = jnp.sum(weights, axis=1, keepdims=True)
    mixed = jnp.dot(
        weights.astype(jnp.bfloat16), joined_ref[:, 2 * HD :], preferred_element_type=jnp.float32
    )
    return (mixed / weight_sum).astype(jnp.bfloat16)


def make_tables(segments_ref, offsets_ref, cosine_ref, sine_down_ref, sine_up_ref):
    tokens = segments_ref.shape[1]
    shape = (tokens, tokens)
    rows = lax.broadcasted_iota(jnp.int32, shape, 0)
    columns = lax.broadcasted_iota(jnp.int32, shape, 1)
    across = jnp.broadcast_to(segments_ref[...], shape).astype(jnp.float32)
    down = jnp.sum(jnp.where(rows == columns, across, 0.0), axis=1, keepdims=True)
    earlier = (across == down) & (columns < rows)
    offsets = jnp.sum(jnp.where(earlier, 1.0, 0.0), axis=1, keepdims=True)
    offsets_ref[...] = jnp.broadcast_to(offsets, offsets_ref.shape)
    half = ROT // 2
    lane = lax.broadcasted_iota(jnp.int32, (tokens, 128), 1)
    step = (lane & (half - 1)).astype(jnp.float32)
    frequency = jnp.exp(step * (-2.0 * math.log(rotary_base) / ROT))
    angles = offsets * frequency
    sine = jnp.sin(angles)
    cosine_ref[...] = jnp.where(lane < ROT, jnp.cos(angles), 1.0)
    sine_down_ref[...] = jnp.where(lane < half, -sine, 0.0)
    sine_up_ref[...] = jnp.where((lane >= half) & (lane < ROT), sine, 0.0)


def make_destinations(targets_ref, destinations_ref, replica_count, block_rows):
    page_count = targets_ref.shape[1]
    tokens = destinations_ref.shape[1]
    capacity = 2 * page_count // replica_count
    square = (page_count, page_count)
    rows = lax.broadcasted_iota(jnp.int32, square, 0)
    columns = lax.broadcasted_iota(jnp.int32, square, 1)
    across = jnp.broadcast_to(targets_ref[...], square).astype(jnp.float32)
    down = jnp.sum(jnp.where(rows == columns, across, 0.0), axis=1, keepdims=True)
    earlier = jnp.where((across == down) & (columns < rows), 1.0, 0.0)
    slots = jnp.sum(earlier, axis=1, keepdims=True).astype(jnp.int32)
    slots = (down.astype(jnp.int32) ^ lax.axis_index("dp")) * capacity + slots
    positions = positions_along(0, (1, tokens), 1, block_rows)
    bits = PAGE.bit_length() - 1
    pages = lax.broadcasted_iota(jnp.int32, (page_count, tokens), 0)
    chosen = jnp.where(pages == positions >> bits, slots.astype(jnp.float32), 0.0)
    slot = jnp.sum(chosen, axis=0, keepdims=True).astype(jnp.int32)
    destinations_ref[...] = slot * PAGE + (positions & (PAGE - 1))


def copies_in(sources, targets, sems, at_once=None):
    copies = []
    for number, (source, target) in enumerate(zip(sources, targets)):
        parts = 4 if source.shape[0] >= 256 else 1
        rows = source.shape[0] // parts
        places = [pl.ds(part * rows, rows) for part in range(parts)]
        copies.append(
            [
                pltpu.make_async_copy(source.at[place], target.at[place], sems.at[number, part])
                for part, place in enumerate(places)
            ]
        )
    for copy in sum(copies[:at_once], []):
        copy.start()
    return copies


def wait_for(copies):
    for copy in copies:
        copy.wait()


def own_kernel(count, replica_count, *refs):
    sources, targets = refs[:count], refs[count : 2 * count]
    offsets_ref, *table_refs, destinations_ref, joined_ref, hidden_ref = refs[2 * count : -3]
    attention_scr, feedforward_scr, sems = refs[-3:]
    copies = copies_in(sources, targets, sems, 7)
    segments_ref, targets_ref, states_ref, *gain_refs, heads_ref, upward_ref, _ = targets
    block_rows = states_ref.shape[0]
    wait_for(copies[0])
    make_tables(segments_ref, offsets_ref, *table_refs)
    wait_for(copies[1])
    make_destinations(targets_ref, destinations_ref, replica_count, block_rows)
    for number in (2, 3, 4):
        wait_for(copies[number])
    normalize([states_ref], gain_refs, [attention_scr, feedforward_scr])
    wait_for(copies[5])
    for copy in copies[7]:
        copy.start()
    places = [position_of(0, 0, block_rows)]
    project(attention_scr, heads_ref, table_refs, places, joined_ref, 0)
    wait_for(copies[6])
    hide(feedforward_scr, upward_ref, hidden_ref, 0)
    wait_for(copies[7])


def own_rows(staged, replica_count):
    tokens = staged[0].shape[1]
    rows, width = staged[2].shape
    hidden_width = staged[6].shape[1]
    shapes = [pltpu.VMEM(array.shape, array.dtype) for array in staged]
    shapes += [pltpu.VMEM((tokens, 128), jnp.float32)] * 4
    shapes += [
        pltpu.VMEM((1, tokens), jnp.int32),
        pltpu.VMEM((rows, 3 * HD), jnp.bfloat16),
        pltpu.VMEM((rows, hidden_width), jnp.bfloat16),
    ]
    count = len(staged)
    return pl.pallas_call(
        functools.partial(own_kernel, count, replica_count),
        out_shape=shapes,
        in_specs=[pl.BlockSpec(memory_space=pltpu.HBM)] * count,
        out_specs=vmem_specs(len(shapes)),
        scratch_shapes=[
            pltpu.VMEM((rows, width), jnp.bfloat16),
            pltpu.VMEM((rows, width), jnp.bfloat16),
            pltpu.SemaphoreType.DMA((count, 4)),
        ],
        compiler_params=parameters(12),
        cost_estimate=pl.CostEstimate(
            flops=2 * rows * width * (3 * HD + hidden_width),
            bytes_accessed=sum(array.nbytes for array in staged),
            transcendentals=rows * hidden_width,
        ),
        name="own_rows",
    )(*[in_hbm(array) for array in staged])


def middle_kernel(origins, *refs):
    count = len(origins)
    blocks, (gain_a, gain_f, heads_ref, upward_ref) = refs[:count], refs[count : count + 4]
    table_refs, refs = refs[count + 4 : count + 7], refs[count + 7 :]
    staged = (len(refs) - 5) // 2
    sources, (joined_ref, hidden_ref), refs = refs[:staged], refs[staged:][:2], refs[staged + 2 :]
    targets, (attention_scr, feedforward_scr, sems) = refs[:staged], refs[staged:]
    copies = copies_in(sources, targets, sems)
    block_rows = blocks[0].shape[0]
    normalize(blocks, [gain_a, gain_f], [attention_scr, feedforward_scr])
    places = [position_of(kind, half, block_rows) for kind, half in origins]
    project(attention_scr, heads_ref, table_refs, places, joined_ref, 0)
    hide(feedforward_scr, upward_ref, hidden_ref, 0)
    wait_for(sum(copies, []))


def middle_rows(name, origins, blocks, gains, weights, tables, *staged):
    block_rows, width = blocks[0].shape
    rows = len(blocks) * block_rows
    hidden_width = weights[1].shape[1]
    return pl.pallas_call(
        functools.partial(middle_kernel, origins),
        out_shape=[
            pltpu.VMEM((rows, 3 * HD), jnp.bfloat16),
            pltpu.VMEM((rows, hidden_width), jnp.bfloat16),
        ]
        + [pltpu.VMEM(array.shape, array.dtype) for array in staged],
        in_specs=vmem_specs(len(blocks) + 2 + 2 + 3)
        + [pl.BlockSpec(memory_space=pltpu.HBM)] * len(staged),
        out_specs=vmem_specs(2 + len(staged)),
        scratch_shapes=[
            pltpu.VMEM((rows, width), jnp.bfloat16),
            pltpu.VMEM((rows, width), jnp.bfloat16),
            pltpu.SemaphoreType.DMA((max(len(staged), 1), 4)),
        ],
        compiler_params=parameters(12),
        cost_estimate=pl.CostEstimate(
            flops=2 * rows * width * (3 * HD + hidden_width),
            bytes_accessed=MIB,
            transcendentals=rows * hidden_width,
        ),
        name=name,
    )(*blocks, *gains, *weights, *tables, *[in_hbm(array) for array in staged])


def last_kernel(*refs):
    block_ref, *normed_refs = refs[:3]
    gain_a, gain_f, heads_ref, upward_ref, downward_ref, output_ref = refs[3:9]
    offsets_ref, *table_refs = refs[9:13]
    own_joined_ref, middle_joined_ref = refs[13:15]
    joined_ref, fed_ref, sibling_ref, own_ref = refs[15:19]
    attention_scr, feedforward_scr, hidden_scr = refs[19:]
    block_rows = block_ref.shape[0]
    tokens = joined_ref.shape[0]
    first = tokens - attention_scr.shape[0]
    count = normed_refs[0].shape[0]
    normalize([block_ref], [gain_a, gain_f], [attention_scr, feedforward_scr], count)
    for normed_ref, normed_scr in zip(normed_refs, (attention_scr, feedforward_scr)):
        normed_scr[:count, :] = normed_ref[...]
    joined_ref[:block_rows, :] = own_joined_ref[...]
    joined_ref[block_rows:first, :] = middle_joined_ref[...]
    origins = ((CHIPS - 2, 1), (CHIPS - 1, 0), (CHIPS - 1, 1))
    places = [position_of(kind, half, block_rows) for kind, half in origins]
    project(attention_scr, heads_ref, table_refs, places, joined_ref, first)
    rows = CORES * block_rows
    hide(feedforward_scr, upward_ref, hidden_scr, 0, 512)
    attended = attend(joined_ref, offsets_ref, tokens - rows, rows, block_rows)
    chunk = 1024
    for begin in range(0, downward_ref.shape[1], chunk):
        columns = slice(begin, begin + chunk)
        fed = jnp.dot(hidden_scr[...], downward_ref[:, columns], preferred_element_type=jnp.float32)
        fed_ref[:, columns] = fed[:block_rows]
        partial = fed[block_rows:] + jnp.dot(
            attended, output_ref[:, columns], preferred_element_type=jnp.float32
        )
        own_ref[:, columns] = partial[:block_rows]
        sibling_ref[:, columns] = partial[block_rows:].astype(jnp.bfloat16)


def last_rows(block, normed, gains, weights, tables, own_joined, middle_joined):
    block_rows, width = block.shape
    rows = normed[0].shape[0] + block_rows
    hidden_width = weights[1].shape[1]
    tokens = CHIPS * CORES * block_rows
    return pl.pallas_call(
        last_kernel,
        out_shape=[
            pltpu.VMEM((tokens, 3 * HD), jnp.bfloat16),
            pltpu.VMEM((block_rows, width), jnp.float32),
            pltpu.VMEM((block_rows, width), jnp.bfloat16),
            pltpu.VMEM((block_rows, width), jnp.float32),
        ],
        in_specs=vmem_specs(1 + 2 + 2 + 4 + 4 + 2),
        out_specs=vmem_specs(4),
        scratch_shapes=[
            pltpu.VMEM((rows, width), jnp.bfloat16),
            pltpu.VMEM((rows, width), jnp.bfloat16),
            pltpu.VMEM((rows, hidden_width), jnp.bfloat16),
        ],
        compiler_params=parameters(12),
        cost_estimate=pl.CostEstimate(
            flops=2 * rows * width * (3 * HD + HD + 2 * hidden_width),
            bytes_accessed=MIB,
            transcendentals=rows * hidden_width,
        ),
        name="last_rows",
    )(block, *normed, *gains, *weights, *tables, own_joined, middle_joined)


def fed_kernel(own_hidden_ref, middle_hidden_ref, downward_ref, *refs):
    blocks, gain_refs, (fed_ref, *normed_refs) = refs[:2], refs[2:4], refs[4:]
    normalize(blocks, gain_refs, normed_refs)
    hidden = jnp.concatenate([own_hidden_ref[...], middle_hidden_ref[...]], 0)
    chunk = 512
    for begin in range(0, downward_ref.shape[1], chunk):
        columns = slice(begin, begin + chunk)
        fed_ref[:, columns] = jnp.dot(
            hidden, downward_ref[:, columns], preferred_element_type=jnp.float32
        )


def fed_rows(own_hidden, middle_hidden, downward_weight, blocks, gains):
    rows = own_hidden.shape[0] + middle_hidden.shape[0]
    depth, width = downward_weight.shape
    normed = pltpu.VMEM((len(blocks) * blocks[0].shape[0], width), jnp.bfloat16)
    return pl.pallas_call(
        fed_kernel,
        out_shape=[pltpu.VMEM((rows, width), jnp.float32), normed, normed],
        in_specs=vmem_specs(7),
        out_specs=vmem_specs(3),
        compiler_params=parameters(12),
        cost_estimate=pl.CostEstimate(
            flops=2 * rows * depth * width, bytes_accessed=MIB, transcendentals=0
        ),
        name="fed_rows",
    )(own_hidden, middle_hidden, downward_weight, *blocks, *gains)


def rest_kernel(joined_ref, offsets_ref, output_ref, fed_ref, fed_beside_ref, *refs):
    near_ref, far_ref, *owns = refs
    block_rows = far_ref.shape[0]
    rows = fed_ref.shape[0] + fed_beside_ref.shape[0]
    attended = attend(joined_ref, offsets_ref, 0, rows, block_rows)
    chunk = 512
    for begin in range(0, output_ref.shape[1], chunk):
        columns = slice(begin, begin + chunk)
        fed = jnp.concatenate([fed_ref[:, columns], fed_beside_ref[:, columns]], 0)
        partial = fed + jnp.dot(
            attended, output_ref[:, columns], preferred_element_type=jnp.float32
        )
        for number, own_ref in enumerate(owns):
            first = CORES * number * block_rows
            middle = first + block_rows
            own_ref[:, columns] = partial[first:middle]
            sibling = partial[middle : middle + block_rows].astype(jnp.bfloat16)
            if number < near_ref.shape[0]:
                near_ref[number, :, columns] = sibling
            else:
                far_ref[:, columns] = sibling


def rest_rows(joined, offsets, output_weight, fed, fed_beside):
    width = fed.shape[1]
    rows = fed.shape[0] + fed_beside.shape[0]
    count = CHIPS - 1
    shape = (rows // (CORES * count), width)
    shapes = [pltpu.VMEM((count - 1, *shape), jnp.bfloat16), pltpu.VMEM(shape, jnp.bfloat16)]
    shapes += [pltpu.VMEM(shape, jnp.float32)] * count
    return pl.pallas_call(
        rest_kernel,
        out_shape=shapes,
        in_specs=vmem_specs(5),
        out_specs=vmem_specs(2 + count),
        compiler_params=parameters(12),
        cost_estimate=pl.CostEstimate(
            flops=2 * rows * width * HD,
            bytes_accessed=MIB,
            transcendentals=rows * joined.shape[0],
        ),
        name="rest_rows",
    )(joined, offsets, output_weight, fed, fed_beside)


def pages_kernel(joined_ref, destinations_ref, *page_refs):
    tokens = joined_ref.shape[0]
    slot_rows = page_refs[0].shape[0] * PAGE
    for number, page_ref in enumerate(page_refs):
        shape = (slot_rows, tokens)
        row = number * slot_rows + lax.broadcasted_iota(jnp.int32, shape, 0)
        placing = jnp.where(row == destinations_ref[...], 1.0, 0.0).astype(jnp.bfloat16)
        rows = jnp.dot(placing, joined_ref[:, HD:], preferred_element_type=jnp.float32)
        page_ref[...] = rows.astype(jnp.bfloat16).reshape(page_ref.shape)


def cached_pages(joined, destinations, replica_count):
    tokens = joined.shape[0]
    capacity = 2 * (tokens // PAGE) // replica_count
    shapes = [pltpu.VMEM((capacity, PAGE, 2 * HD), jnp.bfloat16)] * replica_count
    return pl.pallas_call(
        pages_kernel,
        out_shape=shapes,
        in_specs=vmem_specs(2),
        out_specs=vmem_specs(len(shapes)),
        compiler_params=parameters(8),
        cost_estimate=pl.CostEstimate(flops=0, bytes_accessed=MIB, transcendentals=0),
        name="cached_pages",
    )(joined, destinations)


def add_kernel(*refs):
    total = refs[0][...].astype(jnp.float32)
    for ref in refs[1:-1]:
        total = total + ref[...].astype(jnp.float32)
    refs[-1][...] = total.astype(refs[-1].dtype)


def added(name, *parts):
    return pl.pallas_call(
        add_kernel,
        out_shape=pltpu.VMEM(parts[0].shape, jnp.bfloat16),
        in_specs=vmem_specs(len(parts)),
        out_specs=pl.BlockSpec(memory_space=pltpu.VMEM),
        compiler_params=parameters(4),
        name=name,
    )(*parts)


def near_kernel(received_ref, zero_ref, one_ref, hidden_ref, first_ref, base_ref):
    first_ref[...] = (one_ref[...] + received_ref[1].astype(jnp.float32)).astype(jnp.bfloat16)
    zero = zero_ref[...] + received_ref[0].astype(jnp.float32)
    base_ref[...] = zero + hidden_ref[...].astype(jnp.float32)


def near_sums(received, owns, hidden):
    shape = hidden.shape
    return pl.pallas_call(
        near_kernel,
        out_shape=[pltpu.VMEM(shape, jnp.bfloat16), pltpu.VMEM(shape, jnp.float32)],
        in_specs=vmem_specs(4),
        out_specs=vmem_specs(2),
        compiler_params=parameters(4),
        name="near_sums",
    )(received, *owns, hidden)


def place_kernel(masks, *refs):
    group = lax.axis_index("dp")
    count = len(masks)
    pages, (part_ref, base_ref) = refs[:count], refs[count : count + 2]
    cache_ref, total_ref, sems = refs[count + 2 :]
    copies = [
        pltpu.make_async_copy(page_ref, cache_ref.at[0, group ^ mask], sems.at[number])
        for number, (mask, page_ref) in enumerate(zip(masks, pages))
    ]
    for copy in copies:
        copy.start()
    total_ref[...] = base_ref[...] + part_ref[...].astype(jnp.float32)
    for copy in copies:
        copy.wait()


def placed(masks, pages, part, base, replica_count):
    count = len(pages)
    return pl.pallas_call(
        functools.partial(place_kernel, masks),
        out_shape=[
            jax.ShapeDtypeStruct((1, replica_count) + pages[0].shape, pages[0].dtype),
            pltpu.VMEM(base.shape, base.dtype),
        ],
        in_specs=[pl.BlockSpec(memory_space=pl.ANY)] * count + vmem_specs(2),
        out_specs=[pl.BlockSpec(memory_space=pltpu.HBM)] + vmem_specs(1),
        scratch_shapes=[pltpu.SemaphoreType.DMA((count,))],
        compiler_params=parameters(4),
        name="placed",
    )(*pages, part, base)


def finish_kernel(masks, base_ref, *refs):
    count = len(masks)
    *parts, _, output_ref, cache_ref, total_scr, sems = refs
    parts, pages = parts[:-count], parts[-count:]
    group = lax.axis_index("dp")
    copies = [
        pltpu.make_async_copy(page_ref, cache_ref.at[0, group ^ mask], sems.at[number])
        for number, (mask, page_ref) in enumerate(zip(masks, pages))
    ]
    for copy in copies:
        copy.start()
    total = base_ref[...]
    for part_ref in parts:
        total = total + part_ref[...].astype(jnp.float32)
    total_scr[...] = total
    copies.append(pltpu.make_async_copy(total_scr, output_ref, sems.at[count]))
    copies[-1].start()
    for copy in copies:
        copy.wait()


def finished(base, parts, masks, pages, cache):
    count = len(pages)
    return pl.pallas_call(
        functools.partial(finish_kernel, masks),
        out_shape=[
            jax.ShapeDtypeStruct(base.shape, base.dtype),
            jax.ShapeDtypeStruct(cache.shape, cache.dtype),
        ],
        in_specs=vmem_specs(1 + len(parts))
        + [pl.BlockSpec(memory_space=pl.ANY)] * count
        + [pl.BlockSpec(memory_space=pltpu.HBM)],
        out_specs=[pl.BlockSpec(memory_space=pltpu.HBM)] * 2,
        scratch_shapes=[
            pltpu.VMEM(base.shape, base.dtype),
            pltpu.SemaphoreType.DMA((count + 1,)),
        ],
        input_output_aliases={1 + len(parts) + count: 1},
        compiler_params=parameters(4),
        name="finished",
    )(base, *parts, *pages, cache)


def shards_whole_heads(
    hidden_states,
    attention_gain,
    feedforward_gain,
    heads_weight,
    output_weight,
    upward_weight,
    downward_weight,
    segments,
    page_targets,
):
    replica_count = lax.axis_size("dp")
    to_chip = [mask * CORES for mask in range(CHIPS)]
    second = exchanged(hidden_states, "tensor", to_chip[2])
    first = exchanged(hidden_states, "tensor", to_chip[1])
    beside = exchanged(hidden_states, "tensor", 1)
    staged = (
        segments,
        page_targets.reshape(1, -1),
        hidden_states,
        attention_gain[None],
        feedforward_gain[None],
        heads_weight,
        upward_weight,
        downward_weight,
    )
    staged = own_rows(staged, replica_count)
    hidden, gains, weights, tables = staged[2], staged[3:5], staged[5:8], staged[8:12]
    heads, upward, downward = weights
    destinations, own_joined, own_hidden = staged[12:]

    first, second, own_joined = lax.optimization_barrier((first, second, own_joined))
    first_beside = exchanged(first, "tensor", 1)
    third = exchanged(second, "tensor", to_chip[1])
    middle_joined, middle_hidden, output = middle_rows(
        "middle_rows",
        ((0, 1), (1, 0), (1, 1), (2, 0)),
        (beside, first, first_beside, second),
        gains,
        (heads, upward),
        tables[1:],
        output_weight,
    )
    second, middle_joined = lax.optimization_barrier((second, middle_joined))
    second_beside = exchanged(second, "tensor", 1)
    third, second_beside, middle_joined, middle_hidden = lax.optimization_barrier(
        (third, second_beside, middle_joined, middle_hidden)
    )
    third_beside = exchanged(third, "tensor", 1)
    fed, *normed = fed_rows(own_hidden, middle_hidden, downward, (second_beside, third), gains)
    joined, fed_beside, sibling, own = last_rows(
        third_beside,
        normed,
        gains,
        (heads, upward, downward, output),
        tables,
        own_joined,
        middle_joined,
    )

    received = exchanged(sibling, "tensor", 1)
    partials = rest_rows(joined, tables[0], output, fed, fed_beside)
    near_sibling, far_sibling, *owns = partials
    near_received = exchanged(near_sibling, "tensor", 1)
    third_sum = added("third_added", own, received)
    third_sum, far_sibling, joined = lax.optimization_barrier((third_sum, far_sibling, joined))
    passing = exchanged(third_sum, "tensor", to_chip[1])
    far_received = exchanged(far_sibling, "tensor", 1)
    pages = cached_pages(joined, destinations, replica_count)
    early, late = (3,), (1, 2)
    arriving = [exchanged(pages[mask], "dp", mask) for mask in early]
    first_sum, base = near_sums(near_received, owns[:2], hidden)
    from_first = exchanged(first_sum, "tensor", to_chip[1])
    second_sum = added("second_added", owns[2], passing, far_received)
    second_sum, late_pages = lax.optimization_barrier(
        (second_sum, [pages[mask] for mask in late])
    )
    from_second = exchanged(second_sum, "tensor", to_chip[2])
    late_pages = [exchanged(page, "dp", mask) for mask, page in zip(late, late_pages)]
    cache_pages, base = placed((0,) + early, [pages[0]] + arriving, from_first, base, replica_count)
    return tuple(finished(base, (from_second,), late, late_pages, cache_pages))


def solution(mesh):
    whole_heads = mesh.shape["tensor"] == H and mesh.shape["dp"] == 4
    shards = shards_whole_heads if whole_heads else shards_split_heads
    in_specs = (
        P(("dp", "tensor"), None),
        P(),
        P(),
        P(None, "tensor"),
        P("tensor", None),
        P(None, "tensor"),
        P("tensor", None),
        P("dp", None),
        P("dp", None),
    )
    out_specs = (P(("dp", "tensor"), None), P("dp", None, None, None, "tensor"))
    return jax.shard_map(shards, mesh=mesh, in_specs=in_specs, out_specs=out_specs, check_vma=False)
```

```python
import functools
import math

import jax
import jax.numpy as jnp
from jax import lax
from jax.experimental import pallas as pl
from jax.experimental.pallas import tpu as pltpu
from jax.sharding import PartitionSpec as P

H = 8
HD = 256
ROT = 64
PAGE = 16


epsilon = 1e-05
rotary_base = 10000.0
key_block = 256


def shortened(array):

    def short(part):
        return part.astype(jnp.bfloat16) if part.dtype == jnp.float32 else part

    return jax.tree.map(short, array)


def swapped(block, axis, apart):
    count = lax.axis_size(axis)
    route = []
    for low in range(count):
        high = low | 1 << apart
        if high != low and high < count:
            route += [(low, high), (high, low)]
    return lax.ppermute(block, axis, route)


def layer_norm(values, gain):
    floats = values.astype(jnp.float32)
    center = jnp.mean(floats, axis=-1, keepdims=True)
    shifted = floats - center
    spread = jnp.mean(shifted * shifted, axis=-1, keepdims=True)
    return (shifted * lax.rsqrt(spread + epsilon) * gain).astype(jnp.bfloat16)


def positions_of(stream):
    indices = jnp.arange(stream.shape[0], dtype=jnp.int32)
    boundary = jnp.concatenate([jnp.ones((1,), dtype=bool), stream[1:] != stream[:-1]])
    starting = lax.cummax(jnp.where(boundary, indices, jnp.zeros_like(indices)), axis=0)
    return (indices, starting)


def rotate_heads(vectors, offsets, rotary_dims):
    half_dims = rotary_dims // 2
    frequency = jnp.exp(
        jnp.arange(half_dims, dtype=jnp.float32) * (-2.0 * math.log(rotary_base) / rotary_dims)
    )
    angles = offsets.astype(jnp.float32)[:, None] * frequency[None, :]
    cosine = jnp.cos(angles)
    sine = jnp.sin(angles)
    floats = vectors.astype(jnp.float32)
    leading = floats[..., :half_dims]
    trailing = floats[..., half_dims:rotary_dims]
    rotated = jnp.concatenate(
        [
            leading * cosine - trailing * sine,
            trailing * cosine + leading * sine,
            floats[..., rotary_dims:],
        ],
        axis=-1,
    )
    return rotated.astype(jnp.bfloat16)


def shards_split_heads(
    hidden_states,
    attention_gain,
    feedforward_gain,
    heads_weight,
    output_weight,
    upward_weight,
    downward_weight,
    segments,
    page_targets,
):
    tensor_count = lax.axis_size("tensor")
    replica_count = lax.axis_size("dp")
    tensor_index = lax.axis_index("tensor")
    quarters = tensor_count // H
    quarter_width = HD // quarters
    quarter_index = tensor_index % quarters
    stream = segments[0]
    tokens_total = stream.shape[0]
    level_count = quarters.bit_length() - 1
    normed_attention = layer_norm(hidden_states, attention_gain)
    normed_feedforward = layer_norm(hidden_states, feedforward_gain)
    shard_rows = lax.all_gather(
        (normed_attention, normed_feedforward), "tensor", axis=0, tiled=True
    )
    joined_rows = jnp.dot(shard_rows[0], heads_weight, preferred_element_type=jnp.float32).astype(
        jnp.bfloat16
    )
    upward = jnp.dot(shard_rows[1], upward_weight, preferred_element_type=jnp.float32)
    hidden_rows = jax.nn.gelu(upward, approximate=False).astype(jnp.bfloat16)
    hidden = hidden_rows
    pieces = (
        joined_rows.reshape(tokens_total, 3, quarter_width)
        .transpose(1, 0, 2)
        .reshape(1, 3, tokens_total * quarter_width)
    )
    for bit_number in range(level_count):
        partner = swapped(shortened(pieces), "tensor", bit_number).astype(pieces.dtype)
        lower = tensor_index >> bit_number & 1 == 0
        pieces = jnp.where(
            lower, jnp.concatenate([pieces, partner], 0), jnp.concatenate([partner, pieces], 0)
        )
    whole_head = (
        pieces.reshape(quarters, 3, tokens_total, quarter_width)
        .transpose(1, 2, 0, 3)
        .reshape(3, tokens_total, HD)
    )
    indices, starting = positions_of(stream)
    offsets = indices - starting
    queries = rotate_heads(whole_head[0], offsets, ROT)
    keys = rotate_heads(whole_head[1], offsets, ROT)
    values = whole_head[2]
    block_rows = tokens_total // (2 * quarters)
    score_scale = HD ** (-0.5)

    def attend_block(block_number):
        first_row = block_number * block_rows
        block_queries = lax.dynamic_slice_in_dim(queries, first_row, block_rows, 0)
        query_segments = lax.dynamic_slice_in_dim(stream, first_row, block_rows, 0)
        query_indices = first_row + jnp.arange(block_rows, dtype=jnp.int32)
        lowest = lax.dynamic_index_in_dim(starting, first_row, 0, keepdims=False) // key_block
        highest = (first_row + block_rows + key_block - 1) // key_block

        def scores_of(key_number):
            key_first = key_number * key_block
            key_indices = key_first + jnp.arange(key_block, dtype=jnp.int32)
            scores = (
                jnp.dot(block_queries, keys.T, preferred_element_type=jnp.float32) * score_scale
            )
            allowed = (stream[None, :] == query_segments[:, None]) & (
                key_indices[None, :] <= query_indices[:, None]
            )
            return (scores, allowed)

        def find_peak(key_number, peak):
            scores, allowed = scores_of(key_number)
            return jnp.maximum(peak, jnp.max(jnp.where(allowed, scores, -jnp.inf), axis=1))

        peak = lax.fori_loop(
            lowest, highest, find_peak, jnp.full((block_rows,), -jnp.inf, jnp.float32)
        )

        def accumulate(key_number, state):
            weight_sum, mixed_sum = state
            scores, allowed = scores_of(key_number)
            weights = jnp.where(allowed, jnp.exp(scores - peak[:, None]), 0.0)
            mixed_next = mixed_sum + jnp.dot(
                weights.astype(jnp.bfloat16), values, preferred_element_type=jnp.float32
            )
            return (weight_sum + jnp.sum(weights, axis=1), mixed_next)

        start_state = (
            jnp.zeros((block_rows,), jnp.float32),
            jnp.zeros((block_rows, HD), jnp.float32),
        )
        weight_sum, mixed_sum = lax.fori_loop(lowest, highest, accumulate, start_state)
        return (mixed_sum / weight_sum[:, None]).astype(jnp.bfloat16)

    own_blocks = (2 * quarter_index, 2 * quarter_index + 1)
    own_rows = jnp.concatenate([attend_block(own_blocks[0]), attend_block(own_blocks[1])], 0)[None]
    for bit_number in range(level_count):
        partner = swapped(own_rows, "tensor", bit_number)
        lower = tensor_index >> bit_number & 1 == 0
        own_rows = jnp.where(
            lower, jnp.concatenate([own_rows, partner], 0), jnp.concatenate([partner, own_rows], 0)
        )
    attended = own_rows.reshape(tokens_total, HD)
    attended_quarter = lax.dynamic_slice_in_dim(
        attended, quarter_index * quarter_width, quarter_width, 1
    )
    hidden_rows = hidden
    summed = lax.psum_scatter(
        (
            jnp.dot(attended_quarter, output_weight, preferred_element_type=jnp.float32)
            + jnp.dot(hidden_rows, downward_weight, preferred_element_type=jnp.float32)
        ).astype(jnp.bfloat16),
        "tensor",
        scatter_dimension=0,
        tiled=True,
    ).astype(jnp.float32)
    layer_output = hidden_states.astype(jnp.float32) + summed
    key_quarter = lax.dynamic_slice_in_dim(keys, quarter_index * quarter_width, quarter_width, 1)
    value_quarter = joined_rows[:, 2 * quarter_width :]
    page_count = tokens_total // PAGE
    page_rows = jnp.concatenate([key_quarter, value_quarter], 1).reshape(
        page_count, PAGE * 2 * quarter_width
    )
    targets = page_targets[:, 0]
    page_numbers = jnp.arange(page_count, dtype=jnp.int32)
    earlier = jnp.sum(
        (
            (targets[None, :] == targets[:, None]) & (page_numbers[None, :] < page_numbers[:, None])
        ).astype(jnp.int32),
        axis=1,
    )
    capacity = 2 * page_count // replica_count
    slot_numbers = targets * capacity + earlier
    placing = (
        jnp.arange(replica_count * capacity, dtype=jnp.int32)[:, None] == slot_numbers[None, :]
    ).astype(jnp.bfloat16)
    outgoing = jnp.dot(placing, page_rows, preferred_element_type=jnp.float32).astype(jnp.bfloat16)
    outgoing = outgoing.reshape(replica_count, capacity, PAGE * 2 * quarter_width)
    incoming = lax.all_to_all(outgoing, "dp", split_axis=0, concat_axis=0, tiled=True)
    cache_pages = incoming.reshape(1, replica_count, capacity, PAGE, 2 * quarter_width)
    return (layer_output, cache_pages)


CORES = 2
CHIPS = 4
MIB = 1 << 20


def in_hbm(array):
    return pltpu.with_memory_space_constraint(array, pltpu.HBM)


def exchanged(block, axis, mask):
    count = lax.axis_size(axis)
    return lax.ppermute(block, axis, [(member, member ^ mask) for member in range(count)])


def vmem_specs(count):
    return [pl.BlockSpec(memory_space=pltpu.VMEM)] * count


def parameters(mebibytes):
    return pltpu.CompilerParams(vmem_limit_bytes=mebibytes * MIB)


def whereabouts():
    member = lax.axis_index("tensor")
    return member // CORES, member % CORES


def position_of(kind, half, block_rows):
    chip, core = whereabouts()
    return ((chip ^ kind) * CORES + (core ^ half)) * block_rows


def positions_along(first, shape, axis, block_rows):
    chip, core = whereabouts()
    bits = block_rows.bit_length() - 1
    place = first + lax.broadcasted_iota(jnp.int32, shape, axis)
    kind = place >> (bits + 1)
    half = (place >> bits) & 1
    return ((((chip ^ kind) << 1) | (core ^ half)) << bits) | (place & (block_rows - 1))


def normalize(blocks, gain_refs, normed_refs, place=0):
    piece = 16
    gains = [gain_ref[...] for gain_ref in gain_refs]
    for number, block_ref in enumerate(blocks):
        block_rows = block_ref.shape[0]
        for part in range(0, block_rows, piece):
            floats = block_ref[part : part + piece, :].astype(jnp.float32)
            center = jnp.mean(floats, axis=-1, keepdims=True)
            shifted = floats - center
            spread = jnp.mean(shifted * shifted, axis=-1, keepdims=True)
            scaled = shifted * lax.rsqrt(spread + epsilon)
            first = place + number * block_rows + part
            for gain, normed_ref in zip(gains, normed_refs):
                normed_ref[first : first + piece, :] = (scaled * gain).astype(jnp.bfloat16)


def project(normed_ref, heads_ref, table_refs, places, joined_ref, first):
    rows = normed_ref.shape[0]
    block_rows = rows // len(places)
    own = slice(first, first + rows)
    cosine, sine_down, sine_up = [
        jnp.concatenate(
            [
                table_ref[pl.ds(pl.multiple_of(place, block_rows), block_rows), :]
                for place in places
            ],
            0,
        )
        for table_ref in table_refs
    ]
    joined_ref[own, :] = jnp.dot(
        normed_ref[...], heads_ref[...], preferred_element_type=jnp.float32
    ).astype(jnp.bfloat16)
    for begin in (0, HD):
        columns = slice(begin, begin + 128)
        turning = joined_ref[own, columns].astype(jnp.float32)
        turned = (
            turning * cosine
            + pltpu.roll(turning, 128 - ROT // 2, 1) * sine_down
            + pltpu.roll(turning, ROT // 2, 1) * sine_up
        )
        joined_ref[own, columns] = turned.astype(jnp.bfloat16)


def hide(normed_ref, upward_ref, hidden_ref, place, chunk=256):
    rows = slice(place, place + normed_ref.shape[0])
    for first in range(0, upward_ref.shape[1], chunk):
        columns = slice(first, first + chunk)
        upward = jnp.dot(
            normed_ref[...], upward_ref[:, columns], preferred_element_type=jnp.float32
        )
        hidden = 0.5 * upward * (1.0 + lax.erf(upward * (0.5**0.5)))
        hidden_ref[rows, columns] = hidden.astype(jnp.bfloat16)


def attend(joined_ref, offsets_ref, first, rows, block_rows):
    tokens = joined_ref.shape[0]
    starts = [
        position_of(place // (2 * block_rows), (place // block_rows) % 2, block_rows)
        for place in range(first, first + rows, block_rows)
    ]
    reach = jnp.concatenate(
        [
            offsets_ref[pl.ds(pl.multiple_of(start, block_rows), block_rows), :]
            for start in starts
        ],
        0,
    )[:, :1].astype(jnp.int32)
    row = positions_along(first, (rows, 1), 0, block_rows)
    column = positions_along(0, (1, tokens), 1, block_rows)
    allowed = (column <= row) & (column >= row - reach)
    scores = lax.dot_general(
        joined_ref[first : first + rows, :HD],
        joined_ref[:, HD : 2 * HD],
        (((1,), (1,)), ((), ())),
        preferred_element_type=jnp.float32,
    ) * (HD ** (-0.5))
    peak = jnp.max(jnp.where(allowed, scores, -jnp.inf), axis=1, keepdims=True)
    weights = jnp.where(allowed, jnp.exp(scores - peak), 0.0)
    weight_sum = jnp.sum(weights, axis=1, keepdims=True)
    mixed = jnp.dot(
        weights.astype(jnp.bfloat16), joined_ref[:, 2 * HD :], preferred_element_type=jnp.float32
    )
    return (mixed / weight_sum).astype(jnp.bfloat16)


def make_tables(segments_ref, offsets_ref, cosine_ref, sine_down_ref, sine_up_ref):
    tokens = segments_ref.shape[1]
    shape = (tokens, tokens)
    rows = lax.broadcasted_iota(jnp.int32, shape, 0)
    columns = lax.broadcasted_iota(jnp.int32, shape, 1)
    across = jnp.broadcast_to(segments_ref[...], shape).astype(jnp.float32)
    down = jnp.sum(jnp.where(rows == columns, across, 0.0), axis=1, keepdims=True)
    earlier = (across == down) & (columns < rows)
    offsets = jnp.sum(jnp.where(earlier, 1.0, 0.0), axis=1, keepdims=True)
    offsets_ref[...] = jnp.broadcast_to(offsets, offsets_ref.shape)
    half = ROT // 2
    lane = lax.broadcasted_iota(jnp.int32, (tokens, 128), 1)
    step = (lane & (half - 1)).astype(jnp.float32)
    frequency = jnp.exp(step * (-2.0 * math.log(rotary_base) / ROT))
    angles = offsets * frequency
    sine = jnp.sin(angles)
    cosine_ref[...] = jnp.where(lane < ROT, jnp.cos(angles), 1.0)
    sine_down_ref[...] = jnp.where(lane < half, -sine, 0.0)
    sine_up_ref[...] = jnp.where((lane >= half) & (lane < ROT), sine, 0.0)


def make_destinations(targets_ref, destinations_ref, replica_count, block_rows):
    page_count = targets_ref.shape[1]
    tokens = destinations_ref.shape[1]
    capacity = 2 * page_count // replica_count
    square = (page_count, page_count)
    rows = lax.broadcasted_iota(jnp.int32, square, 0)
    columns = lax.broadcasted_iota(jnp.int32, square, 1)
    across = jnp.broadcast_to(targets_ref[...], square).astype(jnp.float32)
    down = jnp.sum(jnp.where(rows == columns, across, 0.0), axis=1, keepdims=True)
    earlier = jnp.where((across == down) & (columns < rows), 1.0, 0.0)
    slots = jnp.sum(earlier, axis=1, keepdims=True).astype(jnp.int32)
    slots = (down.astype(jnp.int32) ^ lax.axis_index("dp")) * capacity + slots
    positions = positions_along(0, (1, tokens), 1, block_rows)
    bits = PAGE.bit_length() - 1
    pages = lax.broadcasted_iota(jnp.int32, (page_count, tokens), 0)
    chosen = jnp.where(pages == positions >> bits, slots.astype(jnp.float32), 0.0)
    slot = jnp.sum(chosen, axis=0, keepdims=True).astype(jnp.int32)
    destinations_ref[...] = slot * PAGE + (positions & (PAGE - 1))


def copies_in(sources, targets, sems):
    copies = []
    for number, (source, target) in enumerate(zip(sources, targets)):
        parts = 4 if source.shape[0] >= 256 else 1
        rows = source.shape[0] // parts
        places = [pl.ds(part * rows, rows) for part in range(parts)]
        copies.append(
            [
                pltpu.make_async_copy(source.at[place], target.at[place], sems.at[number, part])
                for part, place in enumerate(places)
            ]
        )
    for copy in sum(copies, []):
        copy.start()
    return copies


def wait_for(copies):
    for copy in copies:
        copy.wait()


def own_kernel(count, replica_count, *refs):
    sources, targets = refs[:count], refs[count : 2 * count]
    offsets_ref, *table_refs, destinations_ref, joined_ref, hidden_ref = refs[2 * count : -3]
    attention_scr, feedforward_scr, sems = refs[-3:]
    copies = copies_in(sources, targets, sems)
    segments_ref, targets_ref, states_ref, *gain_refs, heads_ref, upward_ref, _ = targets
    block_rows = states_ref.shape[0]
    wait_for(copies[0])
    make_tables(segments_ref, offsets_ref, *table_refs)
    wait_for(copies[1])
    make_destinations(targets_ref, destinations_ref, replica_count, block_rows)
    for number in (2, 3, 4):
        wait_for(copies[number])
    normalize([states_ref], gain_refs, [attention_scr, feedforward_scr])
    wait_for(copies[5])
    places = [position_of(0, 0, block_rows)]
    project(attention_scr, heads_ref, table_refs, places, joined_ref, 0)
    wait_for(copies[6])
    hide(feedforward_scr, upward_ref, hidden_ref, 0)
    wait_for(copies[7])


def own_rows(staged, replica_count):
    tokens = staged[0].shape[1]
    rows, width = staged[2].shape
    hidden_width = staged[6].shape[1]
    shapes = [pltpu.VMEM(array.shape, array.dtype) for array in staged]
    shapes += [pltpu.VMEM((tokens, 128), jnp.float32)] * 4
    shapes += [
        pltpu.VMEM((1, tokens), jnp.int32),
        pltpu.VMEM((rows, 3 * HD), jnp.bfloat16),
        pltpu.VMEM((rows, hidden_width), jnp.bfloat16),
    ]
    count = len(staged)
    return pl.pallas_call(
        functools.partial(own_kernel, count, replica_count),
        out_shape=shapes,
        in_specs=[pl.BlockSpec(memory_space=pltpu.HBM)] * count,
        out_specs=vmem_specs(len(shapes)),
        scratch_shapes=[
            pltpu.VMEM((rows, width), jnp.bfloat16),
            pltpu.VMEM((rows, width), jnp.bfloat16),
            pltpu.SemaphoreType.DMA((count, 4)),
        ],
        compiler_params=parameters(12),
        cost_estimate=pl.CostEstimate(
            flops=2 * rows * width * (3 * HD + hidden_width),
            bytes_accessed=sum(array.nbytes for array in staged),
            transcendentals=rows * hidden_width,
        ),
        name="own_rows",
    )(*[in_hbm(array) for array in staged])


def middle_kernel(origins, *refs):
    count = len(origins)
    blocks, (gain_a, gain_f, heads_ref, upward_ref) = refs[:count], refs[count : count + 4]
    table_refs, refs = refs[count + 4 : count + 7], refs[count + 7 :]
    staged = (len(refs) - 5) // 2
    sources, (joined_ref, hidden_ref), refs = refs[:staged], refs[staged:][:2], refs[staged + 2 :]
    targets, (attention_scr, feedforward_scr, sems) = refs[:staged], refs[staged:]
    copies = copies_in(sources, targets, sems)
    block_rows = blocks[0].shape[0]
    normalize(blocks, [gain_a, gain_f], [attention_scr, feedforward_scr])
    places = [position_of(kind, half, block_rows) for kind, half in origins]
    project(attention_scr, heads_ref, table_refs, places, joined_ref, 0)
    hide(feedforward_scr, upward_ref, hidden_ref, 0)
    wait_for(sum(copies, []))


def middle_rows(name, origins, blocks, gains, weights, tables, *staged):
    block_rows, width = blocks[0].shape
    rows = len(blocks) * block_rows
    hidden_width = weights[1].shape[1]
    return pl.pallas_call(
        functools.partial(middle_kernel, origins),
        out_shape=[
            pltpu.VMEM((rows, 3 * HD), jnp.bfloat16),
            pltpu.VMEM((rows, hidden_width), jnp.bfloat16),
        ]
        + [pltpu.VMEM(array.shape, array.dtype) for array in staged],
        in_specs=vmem_specs(len(blocks) + 2 + 2 + 3)
        + [pl.BlockSpec(memory_space=pltpu.HBM)] * len(staged),
        out_specs=vmem_specs(2 + len(staged)),
        scratch_shapes=[
            pltpu.VMEM((rows, width), jnp.bfloat16),
            pltpu.VMEM((rows, width), jnp.bfloat16),
            pltpu.SemaphoreType.DMA((max(len(staged), 1), 4)),
        ],
        compiler_params=parameters(12),
        cost_estimate=pl.CostEstimate(
            flops=2 * rows * width * (3 * HD + hidden_width),
            bytes_accessed=MIB,
            transcendentals=rows * hidden_width,
        ),
        name=name,
    )(*blocks, *gains, *weights, *tables, *[in_hbm(array) for array in staged])


def last_kernel(*refs):
    block_ref, *normed_refs = refs[:3]
    gain_a, gain_f, heads_ref, upward_ref, downward_ref, output_ref = refs[3:9]
    offsets_ref, *table_refs = refs[9:13]
    own_joined_ref, middle_joined_ref = refs[13:15]
    joined_ref, fed_ref, sibling_ref, own_ref = refs[15:19]
    attention_scr, feedforward_scr, hidden_scr = refs[19:]
    block_rows = block_ref.shape[0]
    tokens = joined_ref.shape[0]
    first = tokens - attention_scr.shape[0]
    count = normed_refs[0].shape[0]
    normalize([block_ref], [gain_a, gain_f], [attention_scr, feedforward_scr], count)
    for normed_ref, normed_scr in zip(normed_refs, (attention_scr, feedforward_scr)):
        normed_scr[:count, :] = normed_ref[...]
    joined_ref[:block_rows, :] = own_joined_ref[...]
    joined_ref[block_rows:first, :] = middle_joined_ref[...]
    origins = ((CHIPS - 2, 1), (CHIPS - 1, 0), (CHIPS - 1, 1))
    places = [position_of(kind, half, block_rows) for kind, half in origins]
    project(attention_scr, heads_ref, table_refs, places, joined_ref, first)
    rows = CORES * block_rows
    hide(feedforward_scr, upward_ref, hidden_scr, 0, 512)
    attended = attend(joined_ref, offsets_ref, tokens - rows, rows, block_rows)
    chunk = 1024
    for begin in range(0, downward_ref.shape[1], chunk):
        columns = slice(begin, begin + chunk)
        fed = jnp.dot(hidden_scr[...], downward_ref[:, columns], preferred_element_type=jnp.float32)
        fed_ref[:, columns] = fed[:block_rows]
        partial = fed[block_rows:] + jnp.dot(
            attended, output_ref[:, columns], preferred_element_type=jnp.float32
        )
        own_ref[:, columns] = partial[:block_rows]
        sibling_ref[:, columns] = partial[block_rows:].astype(jnp.bfloat16)


def last_rows(block, normed, gains, weights, tables, own_joined, middle_joined):
    block_rows, width = block.shape
    rows = normed[0].shape[0] + block_rows
    hidden_width = weights[1].shape[1]
    tokens = CHIPS * CORES * block_rows
    return pl.pallas_call(
        last_kernel,
        out_shape=[
            pltpu.VMEM((tokens, 3 * HD), jnp.bfloat16),
            pltpu.VMEM((block_rows, width), jnp.float32),
            pltpu.VMEM((block_rows, width), jnp.bfloat16),
            pltpu.VMEM((block_rows, width), jnp.float32),
        ],
        in_specs=vmem_specs(1 + 2 + 2 + 4 + 4 + 2),
        out_specs=vmem_specs(4),
        scratch_shapes=[
            pltpu.VMEM((rows, width), jnp.bfloat16),
            pltpu.VMEM((rows, width), jnp.bfloat16),
            pltpu.VMEM((rows, hidden_width), jnp.bfloat16),
        ],
        compiler_params=parameters(12),
        cost_estimate=pl.CostEstimate(
            flops=2 * rows * width * (3 * HD + HD + 2 * hidden_width),
            bytes_accessed=MIB,
            transcendentals=rows * hidden_width,
        ),
        name="last_rows",
    )(block, *normed, *gains, *weights, *tables, own_joined, middle_joined)


def fed_kernel(own_hidden_ref, middle_hidden_ref, downward_ref, *refs):
    blocks, gain_refs, (fed_ref, *normed_refs) = refs[:2], refs[2:4], refs[4:]
    normalize(blocks, gain_refs, normed_refs)
    hidden = jnp.concatenate([own_hidden_ref[...], middle_hidden_ref[...]], 0)
    chunk = 512
    for begin in range(0, downward_ref.shape[1], chunk):
        columns = slice(begin, begin + chunk)
        fed_ref[:, columns] = jnp.dot(
            hidden, downward_ref[:, columns], preferred_element_type=jnp.float32
        )


def fed_rows(own_hidden, middle_hidden, downward_weight, blocks, gains):
    rows = own_hidden.shape[0] + middle_hidden.shape[0]
    depth, width = downward_weight.shape
    normed = pltpu.VMEM((len(blocks) * blocks[0].shape[0], width), jnp.bfloat16)
    return pl.pallas_call(
        fed_kernel,
        out_shape=[pltpu.VMEM((rows, width), jnp.float32), normed, normed],
        in_specs=vmem_specs(7),
        out_specs=vmem_specs(3),
        compiler_params=parameters(12),
        cost_estimate=pl.CostEstimate(
            flops=2 * rows * depth * width, bytes_accessed=MIB, transcendentals=0
        ),
        name="fed_rows",
    )(own_hidden, middle_hidden, downward_weight, *blocks, *gains)


def rest_kernel(joined_ref, offsets_ref, output_ref, fed_ref, fed_beside_ref, *refs):
    near_ref, far_ref, *owns = refs
    block_rows = far_ref.shape[0]
    rows = fed_ref.shape[0] + fed_beside_ref.shape[0]
    attended = attend(joined_ref, offsets_ref, 0, rows, block_rows)
    chunk = 512
    for begin in range(0, output_ref.shape[1], chunk):
        columns = slice(begin, begin + chunk)
        fed = jnp.concatenate([fed_ref[:, columns], fed_beside_ref[:, columns]], 0)
        partial = fed + jnp.dot(
            attended, output_ref[:, columns], preferred_element_type=jnp.float32
        )
        for number, own_ref in enumerate(owns):
            first = CORES * number * block_rows
            middle = first + block_rows
            own_ref[:, columns] = partial[first:middle]
            sibling = partial[middle : middle + block_rows].astype(jnp.bfloat16)
            if number < near_ref.shape[0]:
                near_ref[number, :, columns] = sibling
            else:
                far_ref[:, columns] = sibling


def rest_rows(joined, offsets, output_weight, fed, fed_beside):
    width = fed.shape[1]
    rows = fed.shape[0] + fed_beside.shape[0]
    count = CHIPS - 1
    shape = (rows // (CORES * count), width)
    shapes = [pltpu.VMEM((count - 1, *shape), jnp.bfloat16), pltpu.VMEM(shape, jnp.bfloat16)]
    shapes += [pltpu.VMEM(shape, jnp.float32)] * count
    return pl.pallas_call(
        rest_kernel,
        out_shape=shapes,
        in_specs=vmem_specs(5),
        out_specs=vmem_specs(2 + count),
        compiler_params=parameters(12),
        cost_estimate=pl.CostEstimate(
            flops=2 * rows * width * HD,
            bytes_accessed=MIB,
            transcendentals=rows * joined.shape[0],
        ),
        name="rest_rows",
    )(joined, offsets, output_weight, fed, fed_beside)


def pages_kernel(joined_ref, destinations_ref, *page_refs):
    tokens = joined_ref.shape[0]
    slot_rows = page_refs[0].shape[0] * PAGE
    for number, page_ref in enumerate(page_refs):
        shape = (slot_rows, tokens)
        row = number * slot_rows + lax.broadcasted_iota(jnp.int32, shape, 0)
        placing = jnp.where(row == destinations_ref[...], 1.0, 0.0).astype(jnp.bfloat16)
        rows = jnp.dot(placing, joined_ref[:, HD:], preferred_element_type=jnp.float32)
        page_ref[...] = rows.astype(jnp.bfloat16).reshape(page_ref.shape)


def cached_pages(joined, destinations, replica_count):
    tokens = joined.shape[0]
    capacity = 2 * (tokens // PAGE) // replica_count
    shapes = [pltpu.VMEM((capacity, PAGE, 2 * HD), jnp.bfloat16)] * replica_count
    return pl.pallas_call(
        pages_kernel,
        out_shape=shapes,
        in_specs=vmem_specs(2),
        out_specs=vmem_specs(len(shapes)),
        compiler_params=parameters(8),
        cost_estimate=pl.CostEstimate(flops=0, bytes_accessed=MIB, transcendentals=0),
        name="cached_pages",
    )(joined, destinations)


def add_kernel(*refs):
    total = refs[0][...].astype(jnp.float32)
    for ref in refs[1:-1]:
        total = total + ref[...].astype(jnp.float32)
    refs[-1][...] = total.astype(refs[-1].dtype)


def added(name, *parts):
    return pl.pallas_call(
        add_kernel,
        out_shape=pltpu.VMEM(parts[0].shape, jnp.bfloat16),
        in_specs=vmem_specs(len(parts)),
        out_specs=pl.BlockSpec(memory_space=pltpu.VMEM),
        compiler_params=parameters(4),
        name=name,
    )(*parts)


def near_kernel(received_ref, zero_ref, one_ref, hidden_ref, first_ref, base_ref):
    first_ref[...] = (one_ref[...] + received_ref[1].astype(jnp.float32)).astype(jnp.bfloat16)
    zero = zero_ref[...] + received_ref[0].astype(jnp.float32)
    base_ref[...] = zero + hidden_ref[...].astype(jnp.float32)


def near_sums(received, owns, hidden):
    shape = hidden.shape
    return pl.pallas_call(
        near_kernel,
        out_shape=[pltpu.VMEM(shape, jnp.bfloat16), pltpu.VMEM(shape, jnp.float32)],
        in_specs=vmem_specs(4),
        out_specs=vmem_specs(2),
        compiler_params=parameters(4),
        name="near_sums",
    )(received, *owns, hidden)


def place_kernel(masks, *refs):
    group = lax.axis_index("dp")
    count = len(masks)
    pages, (part_ref, base_ref) = refs[:count], refs[count : count + 2]
    cache_ref, total_ref, sems = refs[count + 2 :]
    copies = [
        pltpu.make_async_copy(page_ref, cache_ref.at[0, group ^ mask], sems.at[number])
        for number, (mask, page_ref) in enumerate(zip(masks, pages))
    ]
    for copy in copies:
        copy.start()
    total_ref[...] = base_ref[...] + part_ref[...].astype(jnp.float32)
    for copy in copies:
        copy.wait()


def placed(masks, pages, part, base, replica_count):
    count = len(pages)
    return pl.pallas_call(
        functools.partial(place_kernel, masks),
        out_shape=[
            jax.ShapeDtypeStruct((1, replica_count) + pages[0].shape, pages[0].dtype),
            pltpu.VMEM(base.shape, base.dtype),
        ],
        in_specs=[pl.BlockSpec(memory_space=pl.ANY)] * count + vmem_specs(2),
        out_specs=[pl.BlockSpec(memory_space=pltpu.HBM)] + vmem_specs(1),
        scratch_shapes=[pltpu.SemaphoreType.DMA((count,))],
        compiler_params=parameters(4),
        name="placed",
    )(*pages, part, base)


def finish_kernel(masks, base_ref, *refs):
    count = len(masks)
    *parts, _, output_ref, cache_ref, total_scr, sems = refs
    parts, pages = parts[:-count], parts[-count:]
    group = lax.axis_index("dp")
    copies = [
        pltpu.make_async_copy(page_ref, cache_ref.at[0, group ^ mask], sems.at[number])
        for number, (mask, page_ref) in enumerate(zip(masks, pages))
    ]
    for copy in copies:
        copy.start()
    total = base_ref[...]
    for part_ref in parts:
        total = total + part_ref[...].astype(jnp.float32)
    total_scr[...] = total
    copies.append(pltpu.make_async_copy(total_scr, output_ref, sems.at[count]))
    copies[-1].start()
    for copy in copies:
        copy.wait()


def finished(base, parts, masks, pages, cache):
    count = len(pages)
    return pl.pallas_call(
        functools.partial(finish_kernel, masks),
        out_shape=[
            jax.ShapeDtypeStruct(base.shape, base.dtype),
            jax.ShapeDtypeStruct(cache.shape, cache.dtype),
        ],
        in_specs=vmem_specs(1 + len(parts))
        + [pl.BlockSpec(memory_space=pl.ANY)] * count
        + [pl.BlockSpec(memory_space=pltpu.HBM)],
        out_specs=[pl.BlockSpec(memory_space=pltpu.HBM)] * 2,
        scratch_shapes=[
            pltpu.VMEM(base.shape, base.dtype),
            pltpu.SemaphoreType.DMA((count + 1,)),
        ],
        input_output_aliases={1 + len(parts) + count: 1},
        compiler_params=parameters(4),
        name="finished",
    )(base, *parts, *pages, cache)


def shards_whole_heads(
    hidden_states,
    attention_gain,
    feedforward_gain,
    heads_weight,
    output_weight,
    upward_weight,
    downward_weight,
    segments,
    page_targets,
):
    replica_count = lax.axis_size("dp")
    to_chip = [mask * CORES for mask in range(CHIPS)]
    second = exchanged(hidden_states, "tensor", to_chip[2])
    first = exchanged(hidden_states, "tensor", to_chip[1])
    beside = exchanged(hidden_states, "tensor", 1)
    staged = (
        segments,
        page_targets.reshape(1, -1),
        hidden_states,
        attention_gain[None],
        feedforward_gain[None],
        heads_weight,
        upward_weight,
        downward_weight,
    )
    staged = own_rows(staged, replica_count)
    hidden, gains, weights, tables = staged[2], staged[3:5], staged[5:8], staged[8:12]
    heads, upward, downward = weights
    destinations, own_joined, own_hidden = staged[12:]

    first, second, own_joined = lax.optimization_barrier((first, second, own_joined))
    first_beside = exchanged(first, "tensor", 1)
    third = exchanged(second, "tensor", to_chip[1])
    middle_joined, middle_hidden, output = middle_rows(
        "middle_rows",
        ((0, 1), (1, 0), (1, 1), (2, 0)),
        (beside, first, first_beside, second),
        gains,
        (heads, upward),
        tables[1:],
        output_weight,
    )
    second, middle_joined = lax.optimization_barrier((second, middle_joined))
    second_beside = exchanged(second, "tensor", 1)
    third, second_beside, middle_joined, middle_hidden = lax.optimization_barrier(
        (third, second_beside, middle_joined, middle_hidden)
    )
    third_beside = exchanged(third, "tensor", 1)
    fed, *normed = fed_rows(own_hidden, middle_hidden, downward, (second_beside, third), gains)
    joined, fed_beside, sibling, own = last_rows(
        third_beside,
        normed,
        gains,
        (heads, upward, downward, output),
        tables,
        own_joined,
        middle_joined,
    )

    received = exchanged(sibling, "tensor", 1)
    partials = rest_rows(joined, tables[0], output, fed, fed_beside)
    near_sibling, far_sibling, *owns = partials
    near_received = exchanged(near_sibling, "tensor", 1)
    third_sum = added("third_added", own, received)
    third_sum, far_sibling, joined = lax.optimization_barrier((third_sum, far_sibling, joined))
    passing = exchanged(third_sum, "tensor", to_chip[1])
    far_received = exchanged(far_sibling, "tensor", 1)
    pages = cached_pages(joined, destinations, replica_count)
    early, late = (3,), (2, 1)
    arriving = [exchanged(pages[mask], "dp", mask) for mask in early]
    first_sum, base = near_sums(near_received, owns[:2], hidden)
    from_first = exchanged(first_sum, "tensor", to_chip[1])
    second_sum = added("second_added", owns[2], passing, far_received)
    second_sum, late_pages = lax.optimization_barrier(
        (second_sum, [pages[mask] for mask in late])
    )
    from_second = exchanged(second_sum, "tensor", to_chip[2])
    late_pages = [exchanged(page, "dp", mask) for mask, page in zip(late, late_pages)]
    cache_pages, base = placed((0,) + early, [pages[0]] + arriving, from_first, base, replica_count)
    return tuple(finished(base, (from_second,), late, late_pages, cache_pages))


def solution(mesh):
    whole_heads = mesh.shape["tensor"] == H and mesh.shape["dp"] == 4
    shards = shards_whole_heads if whole_heads else shards_split_heads
    in_specs = (
        P(("dp", "tensor"), None),
        P(),
        P(),
        P(None, "tensor"),
        P("tensor", None),
        P(None, "tensor"),
        P("tensor", None),
        P("dp", None),
        P("dp", None),
    )
    out_specs = (P(("dp", "tensor"), None), P("dp", None, None, None, "tensor"))
    return jax.shard_map(shards, mesh=mesh, in_specs=in_specs, out_specs=out_specs, check_vma=False)
```

```python
import functools
import math

import jax
import jax.numpy as jnp
from jax import lax
from jax.experimental import pallas as pl
from jax.experimental.pallas import tpu as pltpu
from jax.sharding import PartitionSpec as P

H = 8
HD = 256
ROT = 64
PAGE = 16


epsilon = 1e-05
rotary_base = 10000.0
key_block = 256


def shortened(array):

    def short(part):
        return part.astype(jnp.bfloat16) if part.dtype == jnp.float32 else part

    return jax.tree.map(short, array)


def swapped(block, axis, apart):
    count = lax.axis_size(axis)
    route = []
    for low in range(count):
        high = low | 1 << apart
        if high != low and high < count:
            route += [(low, high), (high, low)]
    return lax.ppermute(block, axis, route)


def layer_norm(values, gain):
    floats = values.astype(jnp.float32)
    center = jnp.mean(floats, axis=-1, keepdims=True)
    shifted = floats - center
    spread = jnp.mean(shifted * shifted, axis=-1, keepdims=True)
    return (shifted * lax.rsqrt(spread + epsilon) * gain).astype(jnp.bfloat16)


def positions_of(stream):
    indices = jnp.arange(stream.shape[0], dtype=jnp.int32)
    boundary = jnp.concatenate([jnp.ones((1,), dtype=bool), stream[1:] != stream[:-1]])
    starting = lax.cummax(jnp.where(boundary, indices, jnp.zeros_like(indices)), axis=0)
    return (indices, starting)


def rotate_heads(vectors, offsets, rotary_dims):
    half_dims = rotary_dims // 2
    frequency = jnp.exp(
        jnp.arange(half_dims, dtype=jnp.float32) * (-2.0 * math.log(rotary_base) / rotary_dims)
    )
    angles = offsets.astype(jnp.float32)[:, None] * frequency[None, :]
    cosine = jnp.cos(angles)
    sine = jnp.sin(angles)
    floats = vectors.astype(jnp.float32)
    leading = floats[..., :half_dims]
    trailing = floats[..., half_dims:rotary_dims]
    rotated = jnp.concatenate(
        [
            leading * cosine - trailing * sine,
            trailing * cosine + leading * sine,
            floats[..., rotary_dims:],
        ],
        axis=-1,
    )
    return rotated.astype(jnp.bfloat16)


def shards_split_heads(
    hidden_states,
    attention_gain,
    feedforward_gain,
    heads_weight,
    output_weight,
    upward_weight,
    downward_weight,
    segments,
    page_targets,
):
    tensor_count = lax.axis_size("tensor")
    replica_count = lax.axis_size("dp")
    tensor_index = lax.axis_index("tensor")
    quarters = tensor_count // H
    quarter_width = HD // quarters
    quarter_index = tensor_index % quarters
    stream = segments[0]
    tokens_total = stream.shape[0]
    level_count = quarters.bit_length() - 1
    normed_attention = layer_norm(hidden_states, attention_gain)
    normed_feedforward = layer_norm(hidden_states, feedforward_gain)
    shard_rows = lax.all_gather(
        (normed_attention, normed_feedforward), "tensor", axis=0, tiled=True
    )
    joined_rows = jnp.dot(shard_rows[0], heads_weight, preferred_element_type=jnp.float32).astype(
        jnp.bfloat16
    )
    upward = jnp.dot(shard_rows[1], upward_weight, preferred_element_type=jnp.float32)
    hidden_rows = jax.nn.gelu(upward, approximate=False).astype(jnp.bfloat16)
    hidden = hidden_rows
    pieces = (
        joined_rows.reshape(tokens_total, 3, quarter_width)
        .transpose(1, 0, 2)
        .reshape(1, 3, tokens_total * quarter_width)
    )
    for bit_number in range(level_count):
        partner = swapped(shortened(pieces), "tensor", bit_number).astype(pieces.dtype)
        lower = tensor_index >> bit_number & 1 == 0
        pieces = jnp.where(
            lower, jnp.concatenate([pieces, partner], 0), jnp.concatenate([partner, pieces], 0)
        )
    whole_head = (
        pieces.reshape(quarters, 3, tokens_total, quarter_width)
        .transpose(1, 2, 0, 3)
        .reshape(3, tokens_total, HD)
    )
    indices, starting = positions_of(stream)
    offsets = indices - starting
    queries = rotate_heads(whole_head[0], offsets, ROT)
    keys = rotate_heads(whole_head[1], offsets, ROT)
    values = whole_head[2]
    block_rows = tokens_total // (2 * quarters)
    score_scale = HD ** (-0.5)

    def attend_block(block_number):
        first_row = block_number * block_rows
        block_queries = lax.dynamic_slice_in_dim(queries, first_row, block_rows, 0)
        query_segments = lax.dynamic_slice_in_dim(stream, first_row, block_rows, 0)
        query_indices = first_row + jnp.arange(block_rows, dtype=jnp.int32)
        lowest = lax.dynamic_index_in_dim(starting, first_row, 0, keepdims=False) // key_block
        highest = (first_row + block_rows + key_block - 1) // key_block

        def scores_of(key_number):
            key_first = key_number * key_block
            key_indices = key_first + jnp.arange(key_block, dtype=jnp.int32)
            scores = (
                jnp.dot(block_queries, keys.T, preferred_element_type=jnp.float32) * score_scale
            )
            allowed = (stream[None, :] == query_segments[:, None]) & (
                key_indices[None, :] <= query_indices[:, None]
            )
            return (scores, allowed)

        def find_peak(key_number, peak):
            scores, allowed = scores_of(key_number)
            return jnp.maximum(peak, jnp.max(jnp.where(allowed, scores, -jnp.inf), axis=1))

        peak = lax.fori_loop(
            lowest, highest, find_peak, jnp.full((block_rows,), -jnp.inf, jnp.float32)
        )

        def accumulate(key_number, state):
            weight_sum, mixed_sum = state
            scores, allowed = scores_of(key_number)
            weights = jnp.where(allowed, jnp.exp(scores - peak[:, None]), 0.0)
            mixed_next = mixed_sum + jnp.dot(
                weights.astype(jnp.bfloat16), values, preferred_element_type=jnp.float32
            )
            return (weight_sum + jnp.sum(weights, axis=1), mixed_next)

        start_state = (
            jnp.zeros((block_rows,), jnp.float32),
            jnp.zeros((block_rows, HD), jnp.float32),
        )
        weight_sum, mixed_sum = lax.fori_loop(lowest, highest, accumulate, start_state)
        return (mixed_sum / weight_sum[:, None]).astype(jnp.bfloat16)

    own_blocks = (2 * quarter_index, 2 * quarter_index + 1)
    own_rows = jnp.concatenate([attend_block(own_blocks[0]), attend_block(own_blocks[1])], 0)[None]
    for bit_number in range(level_count):
        partner = swapped(own_rows, "tensor", bit_number)
        lower = tensor_index >> bit_number & 1 == 0
        own_rows = jnp.where(
            lower, jnp.concatenate([own_rows, partner], 0), jnp.concatenate([partner, own_rows], 0)
        )
    attended = own_rows.reshape(tokens_total, HD)
    attended_quarter = lax.dynamic_slice_in_dim(
        attended, quarter_index * quarter_width, quarter_width, 1
    )
    hidden_rows = hidden
    summed = lax.psum_scatter(
        (
            jnp.dot(attended_quarter, output_weight, preferred_element_type=jnp.float32)
            + jnp.dot(hidden_rows, downward_weight, preferred_element_type=jnp.float32)
        ).astype(jnp.bfloat16),
        "tensor",
        scatter_dimension=0,
        tiled=True,
    ).astype(jnp.float32)
    layer_output = hidden_states.astype(jnp.float32) + summed
    key_quarter = lax.dynamic_slice_in_dim(keys, quarter_index * quarter_width, quarter_width, 1)
    value_quarter = joined_rows[:, 2 * quarter_width :]
    page_count = tokens_total // PAGE
    page_rows = jnp.concatenate([key_quarter, value_quarter], 1).reshape(
        page_count, PAGE * 2 * quarter_width
    )
    targets = page_targets[:, 0]
    page_numbers = jnp.arange(page_count, dtype=jnp.int32)
    earlier = jnp.sum(
        (
            (targets[None, :] == targets[:, None]) & (page_numbers[None, :] < page_numbers[:, None])
        ).astype(jnp.int32),
        axis=1,
    )
    capacity = 2 * page_count // replica_count
    slot_numbers = targets * capacity + earlier
    placing = (
        jnp.arange(replica_count * capacity, dtype=jnp.int32)[:, None] == slot_numbers[None, :]
    ).astype(jnp.bfloat16)
    outgoing = jnp.dot(placing, page_rows, preferred_element_type=jnp.float32).astype(jnp.bfloat16)
    outgoing = outgoing.reshape(replica_count, capacity, PAGE * 2 * quarter_width)
    incoming = lax.all_to_all(outgoing, "dp", split_axis=0, concat_axis=0, tiled=True)
    cache_pages = incoming.reshape(1, replica_count, capacity, PAGE, 2 * quarter_width)
    return (layer_output, cache_pages)


CORES = 2
CHIPS = 4
MIB = 1 << 20


def in_hbm(array):
    return pltpu.with_memory_space_constraint(array, pltpu.HBM)


def exchanged(block, axis, mask):
    count = lax.axis_size(axis)
    return lax.ppermute(block, axis, [(member, member ^ mask) for member in range(count)])


def vmem_specs(count):
    return [pl.BlockSpec(memory_space=pltpu.VMEM)] * count


def parameters(mebibytes):
    return pltpu.CompilerParams(vmem_limit_bytes=mebibytes * MIB)


def whereabouts():
    member = lax.axis_index("tensor")
    return member // CORES, member % CORES


def kind_at(stand):
    return stand ^ (stand >> 1)


def position_of(kind, half, block_rows):
    chip, core = whereabouts()
    return ((chip ^ kind) * CORES + (core ^ half)) * block_rows


def positions_along(first, shape, axis, block_rows):
    chip, core = whereabouts()
    bits = block_rows.bit_length() - 1
    place = first + lax.broadcasted_iota(jnp.int32, shape, axis)
    kind = kind_at(place >> (bits + 1))
    half = (place >> bits) & 1
    return ((((chip ^ kind) << 1) | (core ^ half)) << bits) | (place & (block_rows - 1))


def normalize(blocks, gain_refs, normed_refs, place=0):
    piece = 16
    gains = [gain_ref[...] for gain_ref in gain_refs]
    for number, block_ref in enumerate(blocks):
        block_rows = block_ref.shape[0]
        for part in range(0, block_rows, piece):
            floats = block_ref[part : part + piece, :].astype(jnp.float32)
            center = jnp.mean(floats, axis=-1, keepdims=True)
            shifted = floats - center
            spread = jnp.mean(shifted * shifted, axis=-1, keepdims=True)
            scaled = shifted * lax.rsqrt(spread + epsilon)
            first = place + number * block_rows + part
            for gain, normed_ref in zip(gains, normed_refs):
                normed_ref[first : first + piece, :] = (scaled * gain).astype(jnp.bfloat16)


def project(normed_ref, heads_ref, table_refs, places, joined_ref, first):
    rows = normed_ref.shape[0]
    block_rows = rows // len(places)
    own = slice(first, first + rows)
    cosine, sine_down, sine_up = [
        jnp.concatenate(
            [
                table_ref[pl.ds(pl.multiple_of(place, block_rows), block_rows), :]
                for place in places
            ],
            0,
        )
        for table_ref in table_refs
    ]
    joined_ref[own, :] = jnp.dot(
        normed_ref[...], heads_ref[...], preferred_element_type=jnp.float32
    ).astype(jnp.bfloat16)
    for begin in (0, HD):
        columns = slice(begin, begin + 128)
        turning = joined_ref[own, columns].astype(jnp.float32)
        turned = (
            turning * cosine
            + pltpu.roll(turning, 128 - ROT // 2, 1) * sine_down
            + pltpu.roll(turning, ROT // 2, 1) * sine_up
        )
        joined_ref[own, columns] = turned.astype(jnp.bfloat16)


def hide(normed_ref, upward_ref, hidden_ref, place, chunk=256):
    rows = slice(place, place + normed_ref.shape[0])
    for first in range(0, upward_ref.shape[1], chunk):
        columns = slice(first, first + chunk)
        upward = jnp.dot(
            normed_ref[...], upward_ref[:, columns], preferred_element_type=jnp.float32
        )
        hidden = 0.5 * upward * (1.0 + lax.erf(upward * (0.5**0.5)))
        hidden_ref[rows, columns] = hidden.astype(jnp.bfloat16)


def attend(joined_ref, offsets_ref, first, rows, block_rows):
    tokens = joined_ref.shape[0]
    starts = [
        position_of(kind_at(place // (2 * block_rows)), (place // block_rows) % 2, block_rows)
        for place in range(first, first + rows, block_rows)
    ]
    reach = jnp.concatenate(
        [
            offsets_ref[pl.ds(pl.multiple_of(start, block_rows), block_rows), :]
            for start in starts
        ],
        0,
    )[:, :1].astype(jnp.int32)
    row = positions_along(first, (rows, 1), 0, block_rows)
    column = positions_along(0, (1, tokens), 1, block_rows)
    allowed = (column <= row) & (column >= row - reach)
    scores = lax.dot_general(
        joined_ref[first : first + rows, :HD],
        joined_ref[:, HD : 2 * HD],
        (((1,), (1,)), ((), ())),
        preferred_element_type=jnp.float32,
    ) * (HD ** (-0.5))
    peak = jnp.max(jnp.where(allowed, scores, -jnp.inf), axis=1, keepdims=True)
    weights = jnp.where(allowed, jnp.exp(scores - peak), 0.0)
    weight_sum = jnp.sum(weights, axis=1, keepdims=True)
    mixed = jnp.dot(
        weights.astype(jnp.bfloat16), joined_ref[:, 2 * HD :], preferred_element_type=jnp.float32
    )
    return (mixed / weight_sum).astype(jnp.bfloat16)


def make_tables(segments_ref, offsets_ref, cosine_ref, sine_down_ref, sine_up_ref):
    tokens = segments_ref.shape[1]
    shape = (tokens, tokens)
    rows = lax.broadcasted_iota(jnp.int32, shape, 0)
    columns = lax.broadcasted_iota(jnp.int32, shape, 1)
    across = jnp.broadcast_to(segments_ref[...], shape).astype(jnp.float32)
    down = jnp.sum(jnp.where(rows == columns, across, 0.0), axis=1, keepdims=True)
    earlier = (across == down) & (columns < rows)
    offsets = jnp.sum(jnp.where(earlier, 1.0, 0.0), axis=1, keepdims=True)
    offsets_ref[...] = jnp.broadcast_to(offsets, offsets_ref.shape)
    half = ROT // 2
    lane = lax.broadcasted_iota(jnp.int32, (tokens, 128), 1)
    step = (lane & (half - 1)).astype(jnp.float32)
    frequency = jnp.exp(step * (-2.0 * math.log(rotary_base) / ROT))
    angles = offsets * frequency
    sine = jnp.sin(angles)
    cosine_ref[...] = jnp.where(lane < ROT, jnp.cos(angles), 1.0)
    sine_down_ref[...] = jnp.where(lane < half, -sine, 0.0)
    sine_up_ref[...] = jnp.where((lane >= half) & (lane < ROT), sine, 0.0)


def make_destinations(targets_ref, destinations_ref, replica_count, block_rows):
    page_count = targets_ref.shape[1]
    tokens = destinations_ref.shape[1]
    capacity = 2 * page_count // replica_count
    square = (page_count, page_count)
    rows = lax.broadcasted_iota(jnp.int32, square, 0)
    columns = lax.broadcasted_iota(jnp.int32, square, 1)
    across = jnp.broadcast_to(targets_ref[...], square).astype(jnp.float32)
    down = jnp.sum(jnp.where(rows == columns, across, 0.0), axis=1, keepdims=True)
    earlier = jnp.where((across == down) & (columns < rows), 1.0, 0.0)
    slots = jnp.sum(earlier, axis=1, keepdims=True).astype(jnp.int32)
    slots = (down.astype(jnp.int32) ^ lax.axis_index("dp")) * capacity + slots
    positions = positions_along(0, (1, tokens), 1, block_rows)
    bits = PAGE.bit_length() - 1
    pages = lax.broadcasted_iota(jnp.int32, (page_count, tokens), 0)
    chosen = jnp.where(pages == positions >> bits, slots.astype(jnp.float32), 0.0)
    slot = jnp.sum(chosen, axis=0, keepdims=True).astype(jnp.int32)
    destinations_ref[...] = slot * PAGE + (positions & (PAGE - 1))


def copies_in(sources, targets, sems):
    copies = []
    for number, (source, target) in enumerate(zip(sources, targets)):
        parts = 4 if source.shape[0] >= 256 else 1
        rows = source.shape[0] // parts
        places = [pl.ds(part * rows, rows) for part in range(parts)]
        copies.append(
            [
                pltpu.make_async_copy(source.at[place], target.at[place], sems.at[number, part])
                for part, place in enumerate(places)
            ]
        )
    for copy in sum(copies, []):
        copy.start()
    return copies


def wait_for(copies):
    for copy in copies:
        copy.wait()


def own_kernel(count, replica_count, *refs):
    sources, targets = refs[:count], refs[count : 2 * count]
    offsets_ref, *table_refs, destinations_ref, joined_ref, hidden_ref = refs[2 * count : -3]
    attention_scr, feedforward_scr, sems = refs[-3:]
    copies = copies_in(sources, targets, sems)
    segments_ref, targets_ref, states_ref, *gain_refs, heads_ref, upward_ref, _ = targets
    block_rows = states_ref.shape[0]
    wait_for(copies[0])
    make_tables(segments_ref, offsets_ref, *table_refs)
    wait_for(copies[1])
    make_destinations(targets_ref, destinations_ref, replica_count, block_rows)
    for number in (2, 3, 4):
        wait_for(copies[number])
    normalize([states_ref], gain_refs, [attention_scr, feedforward_scr])
    wait_for(copies[5])
    places = [position_of(0, 0, block_rows)]
    project(attention_scr, heads_ref, table_refs, places, joined_ref, 0)
    wait_for(copies[6])
    hide(feedforward_scr, upward_ref, hidden_ref, 0)
    wait_for(copies[7])


def own_rows(staged, replica_count):
    tokens = staged[0].shape[1]
    rows, width = staged[2].shape
    hidden_width = staged[6].shape[1]
    shapes = [pltpu.VMEM(array.shape, array.dtype) for array in staged]
    shapes += [pltpu.VMEM((tokens, 128), jnp.float32)] * 4
    shapes += [
        pltpu.VMEM((1, tokens), jnp.int32),
        pltpu.VMEM((rows, 3 * HD), jnp.bfloat16),
        pltpu.VMEM((rows, hidden_width), jnp.bfloat16),
    ]
    count = len(staged)
    return pl.pallas_call(
        functools.partial(own_kernel, count, replica_count),
        out_shape=shapes,
        in_specs=[pl.BlockSpec(memory_space=pltpu.HBM)] * count,
        out_specs=vmem_specs(len(shapes)),
        scratch_shapes=[
            pltpu.VMEM((rows, width), jnp.bfloat16),
            pltpu.VMEM((rows, width), jnp.bfloat16),
            pltpu.SemaphoreType.DMA((count, 4)),
        ],
        compiler_params=parameters(12),
        cost_estimate=pl.CostEstimate(
            flops=2 * rows * width * (3 * HD + hidden_width),
            bytes_accessed=sum(array.nbytes for array in staged),
            transcendentals=rows * hidden_width,
        ),
        name="own_rows",
    )(*[in_hbm(array) for array in staged])


def middle_kernel(origins, *refs):
    count = len(origins)
    blocks, (gain_a, gain_f, heads_ref, upward_ref) = refs[:count], refs[count : count + 4]
    table_refs, refs = refs[count + 4 : count + 7], refs[count + 7 :]
    staged = (len(refs) - 5) // 2
    sources, (joined_ref, hidden_ref), refs = refs[:staged], refs[staged:][:2], refs[staged + 2 :]
    targets, (attention_scr, feedforward_scr, sems) = refs[:staged], refs[staged:]
    copies = copies_in(sources, targets, sems)
    block_rows = blocks[0].shape[0]
    normalize(blocks, [gain_a, gain_f], [attention_scr, feedforward_scr])
    places = [position_of(kind, half, block_rows) for kind, half in origins]
    project(attention_scr, heads_ref, table_refs, places, joined_ref, 0)
    hide(feedforward_scr, upward_ref, hidden_ref, 0)
    wait_for(sum(copies, []))


def middle_rows(name, origins, blocks, gains, weights, tables, *staged):
    block_rows, width = blocks[0].shape
    rows = len(blocks) * block_rows
    hidden_width = weights[1].shape[1]
    return pl.pallas_call(
        functools.partial(middle_kernel, origins),
        out_shape=[
            pltpu.VMEM((rows, 3 * HD), jnp.bfloat16),
            pltpu.VMEM((rows, hidden_width), jnp.bfloat16),
        ]
        + [pltpu.VMEM(array.shape, array.dtype) for array in staged],
        in_specs=vmem_specs(len(blocks) + 2 + 2 + 3)
        + [pl.BlockSpec(memory_space=pltpu.HBM)] * len(staged),
        out_specs=vmem_specs(2 + len(staged)),
        scratch_shapes=[
            pltpu.VMEM((rows, width), jnp.bfloat16),
            pltpu.VMEM((rows, width), jnp.bfloat16),
            pltpu.SemaphoreType.DMA((max(len(staged), 1), 4)),
        ],
        compiler_params=parameters(12),
        cost_estimate=pl.CostEstimate(
            flops=2 * rows * width * (3 * HD + hidden_width),
            bytes_accessed=MIB,
            transcendentals=rows * hidden_width,
        ),
        name=name,
    )(*blocks, *gains, *weights, *tables, *[in_hbm(array) for array in staged])


def last_kernel(*refs):
    block_ref, *normed_refs = refs[:3]
    gain_a, gain_f, heads_ref, upward_ref, downward_ref, output_ref = refs[3:9]
    offsets_ref, *table_refs = refs[9:13]
    own_joined_ref, middle_joined_ref, early_ref = refs[13:16]
    joined_ref, fed_ref, sibling_ref, own_ref = refs[16:20]
    attention_scr, feedforward_scr, hidden_scr = refs[20:]
    block_rows = block_ref.shape[0]
    tokens = joined_ref.shape[0]
    first = tokens - attention_scr.shape[0]
    count = normed_refs[0].shape[0]
    normalize([block_ref], [gain_a, gain_f], [attention_scr, feedforward_scr], count)
    for normed_ref, normed_scr in zip(normed_refs, (attention_scr, feedforward_scr)):
        normed_scr[:count, :] = normed_ref[...]
    joined_ref[:block_rows, :] = own_joined_ref[...]
    joined_ref[block_rows:first, :] = middle_joined_ref[...]
    origins = ((3, 1), (2, 0), (2, 1))
    places = [position_of(kind, half, block_rows) for kind, half in origins]
    project(attention_scr, heads_ref, table_refs, places, joined_ref, first)
    rows = CORES * block_rows
    hide(feedforward_scr, upward_ref, hidden_scr, 0, 512)
    attended = attend(joined_ref, offsets_ref, first - block_rows, rows, block_rows)
    chunk = 1024
    for begin in range(0, downward_ref.shape[1], chunk):
        columns = slice(begin, begin + chunk)
        fed = jnp.dot(hidden_scr[...], downward_ref[:, columns], preferred_element_type=jnp.float32)
        fed_ref[:, columns] = fed[block_rows:]
        product = jnp.dot(attended, output_ref[:, columns], preferred_element_type=jnp.float32)
        own_ref[:, columns] = early_ref[first - block_rows :, columns] + product[:block_rows]
        sibling = fed[:block_rows] + product[block_rows:]
        sibling_ref[:, columns] = sibling.astype(jnp.bfloat16)


def last_rows(block, normed, gains, weights, tables, own_joined, middle_joined, early):
    block_rows, width = block.shape
    rows = normed[0].shape[0] + block_rows
    hidden_width = weights[1].shape[1]
    tokens = CHIPS * CORES * block_rows
    return pl.pallas_call(
        last_kernel,
        out_shape=[
            pltpu.VMEM((tokens, 3 * HD), jnp.bfloat16),
            pltpu.VMEM((CORES * block_rows, width), jnp.float32),
            pltpu.VMEM((block_rows, width), jnp.bfloat16),
            pltpu.VMEM((block_rows, width), jnp.float32),
        ],
        in_specs=vmem_specs(1 + 2 + 2 + 4 + 4 + 3),
        out_specs=vmem_specs(4),
        scratch_shapes=[
            pltpu.VMEM((rows, width), jnp.bfloat16),
            pltpu.VMEM((rows, width), jnp.bfloat16),
            pltpu.VMEM((rows, hidden_width), jnp.bfloat16),
        ],
        compiler_params=parameters(12),
        cost_estimate=pl.CostEstimate(
            flops=2 * rows * width * (3 * HD + HD + 2 * hidden_width),
            bytes_accessed=MIB,
            transcendentals=rows * hidden_width,
        ),
        name="last_rows",
    )(block, *normed, *gains, *weights, *tables, own_joined, middle_joined, early)


def fed_kernel(own_hidden_ref, middle_hidden_ref, downward_ref, *refs):
    blocks, gain_refs, (fed_ref, *normed_refs) = refs[:2], refs[2:4], refs[4:]
    normalize(blocks, gain_refs, normed_refs)
    hidden = jnp.concatenate([own_hidden_ref[...], middle_hidden_ref[...]], 0)
    chunk = 512
    for begin in range(0, downward_ref.shape[1], chunk):
        columns = slice(begin, begin + chunk)
        fed_ref[:, columns] = jnp.dot(
            hidden, downward_ref[:, columns], preferred_element_type=jnp.float32
        )


def fed_rows(own_hidden, middle_hidden, downward_weight, blocks, gains):
    rows = own_hidden.shape[0] + middle_hidden.shape[0]
    depth, width = downward_weight.shape
    normed = pltpu.VMEM((len(blocks) * blocks[0].shape[0], width), jnp.bfloat16)
    return pl.pallas_call(
        fed_kernel,
        out_shape=[pltpu.VMEM((rows, width), jnp.float32), normed, normed],
        in_specs=vmem_specs(7),
        out_specs=vmem_specs(3),
        compiler_params=parameters(12),
        cost_estimate=pl.CostEstimate(
            flops=2 * rows * depth * width, bytes_accessed=MIB, transcendentals=0
        ),
        name="fed_rows",
    )(own_hidden, middle_hidden, downward_weight, *blocks, *gains)


def rest_kernel(joined_ref, offsets_ref, output_ref, early_ref, late_ref, *refs):
    near_ref, far_ref, *owns = refs
    block_rows = far_ref.shape[0]
    late = CORES * block_rows
    early = late * near_ref.shape[0]
    tokens = joined_ref.shape[0]
    attended = jnp.concatenate(
        [
            attend(joined_ref, offsets_ref, 0, early, block_rows),
            attend(joined_ref, offsets_ref, tokens - late, late, block_rows),
        ],
        0,
    )
    chunk = 512
    for begin in range(0, output_ref.shape[1], chunk):
        columns = slice(begin, begin + chunk)
        fed = jnp.concatenate([early_ref[:early, columns], late_ref[:, columns]], 0)
        partial = fed + jnp.dot(
            attended, output_ref[:, columns], preferred_element_type=jnp.float32
        )
        for number, own_ref in enumerate(owns):
            first = CORES * number * block_rows
            middle = first + block_rows
            own_ref[:, columns] = partial[first:middle]
            sibling = partial[middle : middle + block_rows].astype(jnp.bfloat16)
            if number < near_ref.shape[0]:
                near_ref[number, :, columns] = sibling
            else:
                far_ref[:, columns] = sibling


def rest_rows(joined, offsets, output_weight, early, late):
    width = early.shape[1]
    count = CHIPS - 1
    rows = late.shape[0] * count
    shape = (rows // (CORES * count), width)
    shapes = [pltpu.VMEM((count - 1, *shape), jnp.bfloat16), pltpu.VMEM(shape, jnp.bfloat16)]
    shapes += [pltpu.VMEM(shape, jnp.float32)] * count
    return pl.pallas_call(
        rest_kernel,
        out_shape=shapes,
        in_specs=vmem_specs(5),
        out_specs=vmem_specs(2 + count),
        compiler_params=parameters(12),
        cost_estimate=pl.CostEstimate(
            flops=2 * rows * width * HD,
            bytes_accessed=MIB,
            transcendentals=rows * joined.shape[0],
        ),
        name="rest_rows",
    )(joined, offsets, output_weight, early, late)


def pages_kernel(joined_ref, destinations_ref, *page_refs):
    tokens = joined_ref.shape[0]
    slot_rows = page_refs[0].shape[0] * PAGE
    for number, page_ref in enumerate(page_refs):
        shape = (slot_rows, tokens)
        row = number * slot_rows + lax.broadcasted_iota(jnp.int32, shape, 0)
        placing = jnp.where(row == destinations_ref[...], 1.0, 0.0).astype(jnp.bfloat16)
        rows = jnp.dot(placing, joined_ref[:, HD:], preferred_element_type=jnp.float32)
        page_ref[...] = rows.astype(jnp.bfloat16).reshape(page_ref.shape)


def cached_pages(joined, destinations, replica_count):
    tokens = joined.shape[0]
    capacity = 2 * (tokens // PAGE) // replica_count
    shapes = [pltpu.VMEM((capacity, PAGE, 2 * HD), jnp.bfloat16)] * replica_count
    return pl.pallas_call(
        pages_kernel,
        out_shape=shapes,
        in_specs=vmem_specs(2),
        out_specs=vmem_specs(len(shapes)),
        compiler_params=parameters(8),
        cost_estimate=pl.CostEstimate(flops=0, bytes_accessed=MIB, transcendentals=0),
        name="cached_pages",
    )(joined, destinations)


def add_kernel(*refs):
    total = refs[0][...].astype(jnp.float32)
    for ref in refs[1:-1]:
        total = total + ref[...].astype(jnp.float32)
    refs[-1][...] = total.astype(refs[-1].dtype)


def added(name, *parts):
    return pl.pallas_call(
        add_kernel,
        out_shape=pltpu.VMEM(parts[0].shape, jnp.bfloat16),
        in_specs=vmem_specs(len(parts)),
        out_specs=pl.BlockSpec(memory_space=pltpu.VMEM),
        compiler_params=parameters(4),
        name=name,
    )(*parts)


def near_kernel(received_ref, zero_ref, one_ref, hidden_ref, first_ref, base_ref):
    first_ref[...] = (one_ref[...] + received_ref[1].astype(jnp.float32)).astype(jnp.bfloat16)
    zero = zero_ref[...] + received_ref[0].astype(jnp.float32)
    base_ref[...] = zero + hidden_ref[...].astype(jnp.float32)


def near_sums(received, owns, hidden):
    shape = hidden.shape
    return pl.pallas_call(
        near_kernel,
        out_shape=[pltpu.VMEM(shape, jnp.bfloat16), pltpu.VMEM(shape, jnp.float32)],
        in_specs=vmem_specs(4),
        out_specs=vmem_specs(2),
        compiler_params=parameters(4),
        name="near_sums",
    )(received, *owns, hidden)


def place_kernel(masks, *refs):
    group = lax.axis_index("dp")
    count = len(masks)
    pages, (part_ref, base_ref) = refs[:count], refs[count : count + 2]
    cache_ref, total_ref, sems = refs[count + 2 :]
    copies = [
        pltpu.make_async_copy(page_ref, cache_ref.at[0, group ^ mask], sems.at[number])
        for number, (mask, page_ref) in enumerate(zip(masks, pages))
    ]
    for copy in copies:
        copy.start()
    total_ref[...] = base_ref[...] + part_ref[...].astype(jnp.float32)
    for copy in copies:
        copy.wait()


def placed(masks, pages, part, base, replica_count):
    count = len(pages)
    return pl.pallas_call(
        functools.partial(place_kernel, masks),
        out_shape=[
            jax.ShapeDtypeStruct((1, replica_count) + pages[0].shape, pages[0].dtype),
            pltpu.VMEM(base.shape, base.dtype),
        ],
        in_specs=[pl.BlockSpec(memory_space=pl.ANY)] * count + vmem_specs(2),
        out_specs=[pl.BlockSpec(memory_space=pltpu.HBM)] + vmem_specs(1),
        scratch_shapes=[pltpu.SemaphoreType.DMA((count,))],
        compiler_params=parameters(4),
        name="placed",
    )(*pages, part, base)


def finish_kernel(masks, base_ref, *refs):
    count = len(masks)
    *parts, _, output_ref, cache_ref, total_scr, sems = refs
    parts, pages = parts[:-count], parts[-count:]
    group = lax.axis_index("dp")
    copies = [
        pltpu.make_async_copy(page_ref, cache_ref.at[0, group ^ mask], sems.at[number])
        for number, (mask, page_ref) in enumerate(zip(masks, pages))
    ]
    for copy in copies:
        copy.start()
    total = base_ref[...]
    for part_ref in parts:
        total = total + part_ref[...].astype(jnp.float32)
    total_scr[...] = total
    copies.append(pltpu.make_async_copy(total_scr, output_ref, sems.at[count]))
    copies[-1].start()
    for copy in copies:
        copy.wait()


def finished(base, parts, masks, pages, cache):
    count = len(pages)
    return pl.pallas_call(
        functools.partial(finish_kernel, masks),
        out_shape=[
            jax.ShapeDtypeStruct(base.shape, base.dtype),
            jax.ShapeDtypeStruct(cache.shape, cache.dtype),
        ],
        in_specs=vmem_specs(1 + len(parts))
        + [pl.BlockSpec(memory_space=pl.ANY)] * count
        + [pl.BlockSpec(memory_space=pltpu.HBM)],
        out_specs=[pl.BlockSpec(memory_space=pltpu.HBM)] * 2,
        scratch_shapes=[
            pltpu.VMEM(base.shape, base.dtype),
            pltpu.SemaphoreType.DMA((count + 1,)),
        ],
        input_output_aliases={1 + len(parts) + count: 1},
        compiler_params=parameters(4),
        name="finished",
    )(base, *parts, *pages, cache)


def shards_whole_heads(
    hidden_states,
    attention_gain,
    feedforward_gain,
    heads_weight,
    output_weight,
    upward_weight,
    downward_weight,
    segments,
    page_targets,
):
    replica_count = lax.axis_size("dp")
    to_chip = [mask * CORES for mask in range(CHIPS)]
    third = exchanged(hidden_states, "tensor", to_chip[3])
    first = exchanged(hidden_states, "tensor", to_chip[1])
    beside = exchanged(hidden_states, "tensor", 1)
    staged = (
        segments,
        page_targets.reshape(1, -1),
        hidden_states,
        attention_gain[None],
        feedforward_gain[None],
        heads_weight,
        upward_weight,
        downward_weight,
    )
    staged = own_rows(staged, replica_count)
    hidden, gains, weights, tables = staged[2], staged[3:5], staged[5:8], staged[8:12]
    heads, upward, downward = weights
    destinations, own_joined, own_hidden = staged[12:]

    first, third, own_joined = lax.optimization_barrier((first, third, own_joined))
    first_beside = exchanged(first, "tensor", 1)
    second = exchanged(third, "tensor", to_chip[1])
    middle_joined, middle_hidden, output = middle_rows(
        "middle_rows",
        ((0, 1), (1, 0), (1, 1), (3, 0)),
        (beside, first, first_beside, third),
        gains,
        (heads, upward),
        tables[1:],
        output_weight,
    )
    third, middle_joined = lax.optimization_barrier((third, middle_joined))
    third_beside = exchanged(third, "tensor", 1)
    second, third_beside, middle_joined, middle_hidden = lax.optimization_barrier(
        (second, third_beside, middle_joined, middle_hidden)
    )
    second_beside = exchanged(second, "tensor", 1)
    fed, *normed = fed_rows(own_hidden, middle_hidden, downward, (third_beside, second), gains)
    joined, fed_late, sibling, own = last_rows(
        second_beside,
        normed,
        gains,
        (heads, upward, downward, output),
        tables,
        own_joined,
        middle_joined,
        fed,
    )

    received = exchanged(sibling, "tensor", 1)
    partials = rest_rows(joined, tables[0], output, fed, fed_late)
    near_sibling, far_sibling, *owns = partials
    near_received = exchanged(near_sibling, "tensor", 1)
    third_sum = added("third_added", own, received)
    third_sum, far_sibling, joined = lax.optimization_barrier((third_sum, far_sibling, joined))
    passing = exchanged(third_sum, "tensor", to_chip[1])
    far_received = exchanged(far_sibling, "tensor", 1)
    pages = cached_pages(joined, destinations, replica_count)
    early, late = (3,), (2, 1)
    arriving = [exchanged(pages[mask], "dp", mask) for mask in early]
    first_sum, base = near_sums(near_received, owns[:2], hidden)
    from_first = exchanged(first_sum, "tensor", to_chip[1])
    second_sum = added("second_added", owns[2], passing, far_received)
    second_sum, late_pages = lax.optimization_barrier(
        (second_sum, [pages[mask] for mask in late])
    )
    from_second = exchanged(second_sum, "tensor", to_chip[2])
    late_pages = [exchanged(page, "dp", mask) for mask, page in zip(late, late_pages)]
    cache_pages, base = placed((0,) + early, [pages[0]] + arriving, from_first, base, replica_count)
    return tuple(finished(base, (from_second,), late, late_pages, cache_pages))


def solution(mesh):
    whole_heads = mesh.shape["tensor"] == H and mesh.shape["dp"] == 4
    shards = shards_whole_heads if whole_heads else shards_split_heads
    in_specs = (
        P(("dp", "tensor"), None),
        P(),
        P(),
        P(None, "tensor"),
        P("tensor", None),
        P(None, "tensor"),
        P("tensor", None),
        P("dp", None),
        P("dp", None),
    )
    out_specs = (P(("dp", "tensor"), None), P("dp", None, None, None, "tensor"))
    return jax.shard_map(shards, mesh=mesh, in_specs=in_specs, out_specs=out_specs, check_vma=False)
```

```python
import functools
import math

import jax
import jax.numpy as jnp
from jax import lax
from jax.experimental import pallas as pl
from jax.experimental.pallas import tpu as pltpu
from jax.sharding import PartitionSpec as P

H = 8
HD = 256
ROT = 64
PAGE = 16


epsilon = 1e-05
rotary_base = 10000.0
key_block = 256


def shortened(array):

    def short(part):
        return part.astype(jnp.bfloat16) if part.dtype == jnp.float32 else part

    return jax.tree.map(short, array)


def swapped(block, axis, apart):
    count = lax.axis_size(axis)
    route = []
    for low in range(count):
        high = low | 1 << apart
        if high != low and high < count:
            route += [(low, high), (high, low)]
    return lax.ppermute(block, axis, route)


def layer_norm(values, gain):
    floats = values.astype(jnp.float32)
    center = jnp.mean(floats, axis=-1, keepdims=True)
    shifted = floats - center
    spread = jnp.mean(shifted * shifted, axis=-1, keepdims=True)
    return (shifted * lax.rsqrt(spread + epsilon) * gain).astype(jnp.bfloat16)


def positions_of(stream):
    indices = jnp.arange(stream.shape[0], dtype=jnp.int32)
    boundary = jnp.concatenate([jnp.ones((1,), dtype=bool), stream[1:] != stream[:-1]])
    starting = lax.cummax(jnp.where(boundary, indices, jnp.zeros_like(indices)), axis=0)
    return (indices, starting)


def rotate_heads(vectors, offsets, rotary_dims):
    half_dims = rotary_dims // 2
    frequency = jnp.exp(
        jnp.arange(half_dims, dtype=jnp.float32) * (-2.0 * math.log(rotary_base) / rotary_dims)
    )
    angles = offsets.astype(jnp.float32)[:, None] * frequency[None, :]
    cosine = jnp.cos(angles)
    sine = jnp.sin(angles)
    floats = vectors.astype(jnp.float32)
    leading = floats[..., :half_dims]
    trailing = floats[..., half_dims:rotary_dims]
    rotated = jnp.concatenate(
        [
            leading * cosine - trailing * sine,
            trailing * cosine + leading * sine,
            floats[..., rotary_dims:],
        ],
        axis=-1,
    )
    return rotated.astype(jnp.bfloat16)


def shards_split_heads(
    hidden_states,
    attention_gain,
    feedforward_gain,
    heads_weight,
    output_weight,
    upward_weight,
    downward_weight,
    segments,
    page_targets,
):
    tensor_count = lax.axis_size("tensor")
    replica_count = lax.axis_size("dp")
    tensor_index = lax.axis_index("tensor")
    quarters = tensor_count // H
    quarter_width = HD // quarters
    quarter_index = tensor_index % quarters
    stream = segments[0]
    tokens_total = stream.shape[0]
    level_count = quarters.bit_length() - 1
    normed_attention = layer_norm(hidden_states, attention_gain)
    normed_feedforward = layer_norm(hidden_states, feedforward_gain)
    shard_rows = lax.all_gather(
        (normed_attention, normed_feedforward), "tensor", axis=0, tiled=True
    )
    joined_rows = jnp.dot(shard_rows[0], heads_weight, preferred_element_type=jnp.float32).astype(
        jnp.bfloat16
    )
    upward = jnp.dot(shard_rows[1], upward_weight, preferred_element_type=jnp.float32)
    hidden_rows = jax.nn.gelu(upward, approximate=False).astype(jnp.bfloat16)
    hidden = hidden_rows
    pieces = (
        joined_rows.reshape(tokens_total, 3, quarter_width)
        .transpose(1, 0, 2)
        .reshape(1, 3, tokens_total * quarter_width)
    )
    for bit_number in range(level_count):
        partner = swapped(shortened(pieces), "tensor", bit_number).astype(pieces.dtype)
        lower = tensor_index >> bit_number & 1 == 0
        pieces = jnp.where(
            lower, jnp.concatenate([pieces, partner], 0), jnp.concatenate([partner, pieces], 0)
        )
    whole_head = (
        pieces.reshape(quarters, 3, tokens_total, quarter_width)
        .transpose(1, 2, 0, 3)
        .reshape(3, tokens_total, HD)
    )
    indices, starting = positions_of(stream)
    offsets = indices - starting
    queries = rotate_heads(whole_head[0], offsets, ROT)
    keys = rotate_heads(whole_head[1], offsets, ROT)
    values = whole_head[2]
    block_rows = tokens_total // (2 * quarters)
    score_scale = HD ** (-0.5)

    def attend_block(block_number):
        first_row = block_number * block_rows
        block_queries = lax.dynamic_slice_in_dim(queries, first_row, block_rows, 0)
        query_segments = lax.dynamic_slice_in_dim(stream, first_row, block_rows, 0)
        query_indices = first_row + jnp.arange(block_rows, dtype=jnp.int32)
        lowest = lax.dynamic_index_in_dim(starting, first_row, 0, keepdims=False) // key_block
        highest = (first_row + block_rows + key_block - 1) // key_block

        def scores_of(key_number):
            key_first = key_number * key_block
            key_indices = key_first + jnp.arange(key_block, dtype=jnp.int32)
            scores = (
                jnp.dot(block_queries, keys.T, preferred_element_type=jnp.float32) * score_scale
            )
            allowed = (stream[None, :] == query_segments[:, None]) & (
                key_indices[None, :] <= query_indices[:, None]
            )
            return (scores, allowed)

        def find_peak(key_number, peak):
            scores, allowed = scores_of(key_number)
            return jnp.maximum(peak, jnp.max(jnp.where(allowed, scores, -jnp.inf), axis=1))

        peak = lax.fori_loop(
            lowest, highest, find_peak, jnp.full((block_rows,), -jnp.inf, jnp.float32)
        )

        def accumulate(key_number, state):
            weight_sum, mixed_sum = state
            scores, allowed = scores_of(key_number)
            weights = jnp.where(allowed, jnp.exp(scores - peak[:, None]), 0.0)
            mixed_next = mixed_sum + jnp.dot(
                weights.astype(jnp.bfloat16), values, preferred_element_type=jnp.float32
            )
            return (weight_sum + jnp.sum(weights, axis=1), mixed_next)

        start_state = (
            jnp.zeros((block_rows,), jnp.float32),
            jnp.zeros((block_rows, HD), jnp.float32),
        )
        weight_sum, mixed_sum = lax.fori_loop(lowest, highest, accumulate, start_state)
        return (mixed_sum / weight_sum[:, None]).astype(jnp.bfloat16)

    own_blocks = (2 * quarter_index, 2 * quarter_index + 1)
    own_rows = jnp.concatenate([attend_block(own_blocks[0]), attend_block(own_blocks[1])], 0)[None]
    for bit_number in range(level_count):
        partner = swapped(own_rows, "tensor", bit_number)
        lower = tensor_index >> bit_number & 1 == 0
        own_rows = jnp.where(
            lower, jnp.concatenate([own_rows, partner], 0), jnp.concatenate([partner, own_rows], 0)
        )
    attended = own_rows.reshape(tokens_total, HD)
    attended_quarter = lax.dynamic_slice_in_dim(
        attended, quarter_index * quarter_width, quarter_width, 1
    )
    hidden_rows = hidden
    summed = lax.psum_scatter(
        (
            jnp.dot(attended_quarter, output_weight, preferred_element_type=jnp.float32)
            + jnp.dot(hidden_rows, downward_weight, preferred_element_type=jnp.float32)
        ).astype(jnp.bfloat16),
        "tensor",
        scatter_dimension=0,
        tiled=True,
    ).astype(jnp.float32)
    layer_output = hidden_states.astype(jnp.float32) + summed
    key_quarter = lax.dynamic_slice_in_dim(keys, quarter_index * quarter_width, quarter_width, 1)
    value_quarter = joined_rows[:, 2 * quarter_width :]
    page_count = tokens_total // PAGE
    page_rows = jnp.concatenate([key_quarter, value_quarter], 1).reshape(
        page_count, PAGE * 2 * quarter_width
    )
    targets = page_targets[:, 0]
    page_numbers = jnp.arange(page_count, dtype=jnp.int32)
    earlier = jnp.sum(
        (
            (targets[None, :] == targets[:, None]) & (page_numbers[None, :] < page_numbers[:, None])
        ).astype(jnp.int32),
        axis=1,
    )
    capacity = 2 * page_count // replica_count
    slot_numbers = targets * capacity + earlier
    placing = (
        jnp.arange(replica_count * capacity, dtype=jnp.int32)[:, None] == slot_numbers[None, :]
    ).astype(jnp.bfloat16)
    outgoing = jnp.dot(placing, page_rows, preferred_element_type=jnp.float32).astype(jnp.bfloat16)
    outgoing = outgoing.reshape(replica_count, capacity, PAGE * 2 * quarter_width)
    incoming = lax.all_to_all(outgoing, "dp", split_axis=0, concat_axis=0, tiled=True)
    cache_pages = incoming.reshape(1, replica_count, capacity, PAGE, 2 * quarter_width)
    return (layer_output, cache_pages)


CORES = 2
CHIPS = 4
MIB = 1 << 20


def in_hbm(array):
    return pltpu.with_memory_space_constraint(array, pltpu.HBM)


def exchanged(block, axis, mask):
    count = lax.axis_size(axis)
    return lax.ppermute(block, axis, [(member, member ^ mask) for member in range(count)])


def vmem_specs(count):
    return [pl.BlockSpec(memory_space=pltpu.VMEM)] * count


def parameters(mebibytes):
    return pltpu.CompilerParams(vmem_limit_bytes=mebibytes * MIB)


def whereabouts():
    member = lax.axis_index("tensor")
    return member // CORES, member % CORES


ORDER = (0, 3, 1, 2)


def position_of(kind, half, block_rows):
    chip, core = whereabouts()
    return ((chip ^ kind) * CORES + (core ^ half)) * block_rows


def positions_along(first, shape, axis, block_rows):
    chip, core = whereabouts()
    bits = block_rows.bit_length() - 1
    place = first + lax.broadcasted_iota(jnp.int32, shape, axis)
    stand = place >> (bits + 1)
    kind = jnp.where(stand == 1, ORDER[1], jnp.maximum(stand - 1, 0))
    half = (place >> bits) & 1
    return ((((chip ^ kind) << 1) | (core ^ half)) << bits) | (place & (block_rows - 1))


def normalize(blocks, gain_refs, normed_refs, place=0):
    piece = 16
    gains = [gain_ref[...] for gain_ref in gain_refs]
    for number, block_ref in enumerate(blocks):
        block_rows = block_ref.shape[0]
        for part in range(0, block_rows, piece):
            floats = block_ref[part : part + piece, :].astype(jnp.float32)
            center = jnp.mean(floats, axis=-1, keepdims=True)
            shifted = floats - center
            spread = jnp.mean(shifted * shifted, axis=-1, keepdims=True)
            scaled = shifted * lax.rsqrt(spread + epsilon)
            first = place + number * block_rows + part
            for gain, normed_ref in zip(gains, normed_refs):
                normed_ref[first : first + piece, :] = (scaled * gain).astype(jnp.bfloat16)


def project(normed_ref, heads_ref, table_refs, places, joined_ref, first):
    rows = normed_ref.shape[0]
    block_rows = rows // len(places)
    own = slice(first, first + rows)
    cosine, sine_down, sine_up = [
        jnp.concatenate(
            [
                table_ref[pl.ds(pl.multiple_of(place, block_rows), block_rows), :]
                for place in places
            ],
            0,
        )
        for table_ref in table_refs
    ]
    joined_ref[own, :] = jnp.dot(
        normed_ref[...], heads_ref[...], preferred_element_type=jnp.float32
    ).astype(jnp.bfloat16)
    for begin in (0, HD):
        columns = slice(begin, begin + 128)
        turning = joined_ref[own, columns].astype(jnp.float32)
        turned = (
            turning * cosine
            + pltpu.roll(turning, 128 - ROT // 2, 1) * sine_down
            + pltpu.roll(turning, ROT // 2, 1) * sine_up
        )
        joined_ref[own, columns] = turned.astype(jnp.bfloat16)


def hide(normed_ref, upward_ref, hidden_ref, place, chunk=256):
    rows = slice(place, place + normed_ref.shape[0])
    for first in range(0, upward_ref.shape[1], chunk):
        columns = slice(first, first + chunk)
        upward = jnp.dot(
            normed_ref[...], upward_ref[:, columns], preferred_element_type=jnp.float32
        )
        hidden = 0.5 * upward * (1.0 + lax.erf(upward * (0.5**0.5)))
        hidden_ref[rows, columns] = hidden.astype(jnp.bfloat16)


def attend(joined_ref, offsets_ref, first, rows, block_rows):
    tokens = joined_ref.shape[0]
    starts = [
        position_of(ORDER[place // (2 * block_rows)], (place // block_rows) % 2, block_rows)
        for place in range(first, first + rows, block_rows)
    ]
    reach = jnp.concatenate(
        [
            offsets_ref[pl.ds(pl.multiple_of(start, block_rows), block_rows), :]
            for start in starts
        ],
        0,
    )[:, :1].astype(jnp.int32)
    row = positions_along(first, (rows, 1), 0, block_rows)
    column = positions_along(0, (1, tokens), 1, block_rows)
    allowed = (column <= row) & (column >= row - reach)
    scores = lax.dot_general(
        joined_ref[first : first + rows, :HD],
        joined_ref[:, HD : 2 * HD],
        (((1,), (1,)), ((), ())),
        preferred_element_type=jnp.float32,
    ) * (HD ** (-0.5))
    peak = jnp.max(jnp.where(allowed, scores, -jnp.inf), axis=1, keepdims=True)
    weights = jnp.where(allowed, jnp.exp(scores - peak), 0.0)
    weight_sum = jnp.sum(weights, axis=1, keepdims=True)
    mixed = jnp.dot(
        weights.astype(jnp.bfloat16), joined_ref[:, 2 * HD :], preferred_element_type=jnp.float32
    )
    return (mixed / weight_sum).astype(jnp.bfloat16)


def make_tables(segments_ref, offsets_ref, cosine_ref, sine_down_ref, sine_up_ref):
    tokens = segments_ref.shape[1]
    shape = (tokens, tokens)
    rows = lax.broadcasted_iota(jnp.int32, shape, 0)
    columns = lax.broadcasted_iota(jnp.int32, shape, 1)
    across = jnp.broadcast_to(segments_ref[...], shape).astype(jnp.float32)
    down = jnp.sum(jnp.where(rows == columns, across, 0.0), axis=1, keepdims=True)
    earlier = (across == down) & (columns < rows)
    offsets = jnp.sum(jnp.where(earlier, 1.0, 0.0), axis=1, keepdims=True)
    offsets_ref[...] = jnp.broadcast_to(offsets, offsets_ref.shape)
    half = ROT // 2
    lane = lax.broadcasted_iota(jnp.int32, (tokens, 128), 1)
    step = (lane & (half - 1)).astype(jnp.float32)
    frequency = jnp.exp(step * (-2.0 * math.log(rotary_base) / ROT))
    angles = offsets * frequency
    sine = jnp.sin(angles)
    cosine_ref[...] = jnp.where(lane < ROT, jnp.cos(angles), 1.0)
    sine_down_ref[...] = jnp.where(lane < half, -sine, 0.0)
    sine_up_ref[...] = jnp.where((lane >= half) & (lane < ROT), sine, 0.0)


def make_destinations(targets_ref, destinations_ref, replica_count, block_rows):
    page_count = targets_ref.shape[1]
    tokens = destinations_ref.shape[1]
    capacity = 2 * page_count // replica_count
    square = (page_count, page_count)
    rows = lax.broadcasted_iota(jnp.int32, square, 0)
    columns = lax.broadcasted_iota(jnp.int32, square, 1)
    across = jnp.broadcast_to(targets_ref[...], square).astype(jnp.float32)
    down = jnp.sum(jnp.where(rows == columns, across, 0.0), axis=1, keepdims=True)
    earlier = jnp.where((across == down) & (columns < rows), 1.0, 0.0)
    slots = jnp.sum(earlier, axis=1, keepdims=True).astype(jnp.int32)
    slots = (down.astype(jnp.int32) ^ lax.axis_index("dp")) * capacity + slots
    positions = positions_along(0, (1, tokens), 1, block_rows)
    bits = PAGE.bit_length() - 1
    pages = lax.broadcasted_iota(jnp.int32, (page_count, tokens), 0)
    chosen = jnp.where(pages == positions >> bits, slots.astype(jnp.float32), 0.0)
    slot = jnp.sum(chosen, axis=0, keepdims=True).astype(jnp.int32)
    destinations_ref[...] = slot * PAGE + (positions & (PAGE - 1))


def copies_in(sources, targets, sems):
    copies = []
    for number, (source, target) in enumerate(zip(sources, targets)):
        parts = 4 if source.shape[0] >= 256 else 1
        rows = source.shape[0] // parts
        places = [pl.ds(part * rows, rows) for part in range(parts)]
        copies.append(
            [
                pltpu.make_async_copy(source.at[place], target.at[place], sems.at[number, part])
                for part, place in enumerate(places)
            ]
        )
    for copy in sum(copies, []):
        copy.start()
    return copies


def wait_for(copies):
    for copy in copies:
        copy.wait()


def own_kernel(count, replica_count, *refs):
    sources, targets = refs[:count], refs[count : 2 * count]
    offsets_ref, *table_refs, destinations_ref, joined_ref, hidden_ref = refs[2 * count : -3]
    attention_scr, feedforward_scr, sems = refs[-3:]
    copies = copies_in(sources, targets, sems)
    segments_ref, targets_ref, states_ref, *gain_refs, heads_ref, upward_ref, _ = targets
    block_rows = states_ref.shape[0]
    wait_for(copies[0])
    make_tables(segments_ref, offsets_ref, *table_refs)
    wait_for(copies[1])
    make_destinations(targets_ref, destinations_ref, replica_count, block_rows)
    for number in (2, 3, 4):
        wait_for(copies[number])
    normalize([states_ref], gain_refs, [attention_scr, feedforward_scr])
    wait_for(copies[5])
    places = [position_of(0, 0, block_rows)]
    project(attention_scr, heads_ref, table_refs, places, joined_ref, 0)
    wait_for(copies[6])
    hide(feedforward_scr, upward_ref, hidden_ref, 0)
    wait_for(copies[7])


def own_rows(staged, replica_count):
    tokens = staged[0].shape[1]
    rows, width = staged[2].shape
    hidden_width = staged[6].shape[1]
    shapes = [pltpu.VMEM(array.shape, array.dtype) for array in staged]
    shapes += [pltpu.VMEM((tokens, 128), jnp.float32)] * 4
    shapes += [
        pltpu.VMEM((1, tokens), jnp.int32),
        pltpu.VMEM((rows, 3 * HD), jnp.bfloat16),
        pltpu.VMEM((rows, hidden_width), jnp.bfloat16),
    ]
    count = len(staged)
    return pl.pallas_call(
        functools.partial(own_kernel, count, replica_count),
        out_shape=shapes,
        in_specs=[pl.BlockSpec(memory_space=pltpu.HBM)] * count,
        out_specs=vmem_specs(len(shapes)),
        scratch_shapes=[
            pltpu.VMEM((rows, width), jnp.bfloat16),
            pltpu.VMEM((rows, width), jnp.bfloat16),
            pltpu.SemaphoreType.DMA((count, 4)),
        ],
        compiler_params=parameters(12),
        cost_estimate=pl.CostEstimate(
            flops=2 * rows * width * (3 * HD + hidden_width),
            bytes_accessed=sum(array.nbytes for array in staged),
            transcendentals=rows * hidden_width,
        ),
        name="own_rows",
    )(*[in_hbm(array) for array in staged])


def middle_kernel(origins, *refs):
    count = len(origins)
    blocks, (gain_a, gain_f, heads_ref, upward_ref) = refs[:count], refs[count : count + 4]
    table_refs, refs = refs[count + 4 : count + 7], refs[count + 7 :]
    staged = (len(refs) - 5) // 2
    sources, (joined_ref, hidden_ref), refs = refs[:staged], refs[staged:][:2], refs[staged + 2 :]
    targets, (attention_scr, feedforward_scr, sems) = refs[:staged], refs[staged:]
    copies = copies_in(sources, targets, sems)
    block_rows = blocks[0].shape[0]
    normalize(blocks, [gain_a, gain_f], [attention_scr, feedforward_scr])
    places = [position_of(kind, half, block_rows) for kind, half in origins]
    project(attention_scr, heads_ref, table_refs, places, joined_ref, 0)
    hide(feedforward_scr, upward_ref, hidden_ref, 0)
    wait_for(sum(copies, []))


def middle_rows(name, origins, blocks, gains, weights, tables, *staged):
    block_rows, width = blocks[0].shape
    rows = len(blocks) * block_rows
    hidden_width = weights[1].shape[1]
    return pl.pallas_call(
        functools.partial(middle_kernel, origins),
        out_shape=[
            pltpu.VMEM((rows, 3 * HD), jnp.bfloat16),
            pltpu.VMEM((rows, hidden_width), jnp.bfloat16),
        ]
        + [pltpu.VMEM(array.shape, array.dtype) for array in staged],
        in_specs=vmem_specs(len(blocks) + 2 + 2 + 3)
        + [pl.BlockSpec(memory_space=pltpu.HBM)] * len(staged),
        out_specs=vmem_specs(2 + len(staged)),
        scratch_shapes=[
            pltpu.VMEM((rows, width), jnp.bfloat16),
            pltpu.VMEM((rows, width), jnp.bfloat16),
            pltpu.SemaphoreType.DMA((max(len(staged), 1), 4)),
        ],
        compiler_params=parameters(12),
        cost_estimate=pl.CostEstimate(
            flops=2 * rows * width * (3 * HD + hidden_width),
            bytes_accessed=MIB,
            transcendentals=rows * hidden_width,
        ),
        name=name,
    )(*blocks, *gains, *weights, *tables, *[in_hbm(array) for array in staged])


def last_kernel(*refs):
    block_ref, *normed_refs = refs[:3]
    gain_a, gain_f, heads_ref, upward_ref, downward_ref, output_ref = refs[3:9]
    offsets_ref, *table_refs = refs[9:13]
    own_joined_ref, middle_joined_ref, early_ref = refs[13:16]
    joined_ref, fed_ref, sibling_ref, own_ref = refs[16:20]
    attention_scr, feedforward_scr, hidden_scr = refs[20:]
    block_rows = block_ref.shape[0]
    tokens = joined_ref.shape[0]
    first = tokens - attention_scr.shape[0]
    count = normed_refs[0].shape[0]
    normalize([block_ref], [gain_a, gain_f], [attention_scr, feedforward_scr], count)
    for normed_ref, normed_scr in zip(normed_refs, (attention_scr, feedforward_scr)):
        normed_scr[:count, :] = normed_ref[...]
    joined_ref[:block_rows, :] = own_joined_ref[...]
    joined_ref[block_rows:first, :] = middle_joined_ref[...]
    origins = ((3, 1), (1, 0), (1, 1), (2, 0), (2, 1))
    places = [position_of(kind, half, block_rows) for kind, half in origins]
    project(attention_scr, heads_ref, table_refs, places, joined_ref, first)
    rows = CORES * block_rows
    hide(feedforward_scr, upward_ref, hidden_scr, 0, 512)
    attended = attend(joined_ref, offsets_ref, first - block_rows, rows, block_rows)
    chunk = 1024
    for begin in range(0, downward_ref.shape[1], chunk):
        columns = slice(begin, begin + chunk)
        fed = jnp.dot(hidden_scr[...], downward_ref[:, columns], preferred_element_type=jnp.float32)
        fed_ref[:, columns] = fed[block_rows:]
        product = jnp.dot(attended, output_ref[:, columns], preferred_element_type=jnp.float32)
        own_ref[:, columns] = early_ref[first - block_rows :, columns] + product[:block_rows]
        sibling = fed[:block_rows] + product[block_rows:]
        sibling_ref[:, columns] = sibling.astype(jnp.bfloat16)


def last_rows(block, normed, gains, weights, tables, own_joined, middle_joined, early):
    block_rows, width = block.shape
    rows = normed[0].shape[0] + block_rows
    hidden_width = weights[1].shape[1]
    tokens = CHIPS * CORES * block_rows
    return pl.pallas_call(
        last_kernel,
        out_shape=[
            pltpu.VMEM((tokens, 3 * HD), jnp.bfloat16),
            pltpu.VMEM((rows - block_rows, width), jnp.float32),
            pltpu.VMEM((block_rows, width), jnp.bfloat16),
            pltpu.VMEM((block_rows, width), jnp.float32),
        ],
        in_specs=vmem_specs(1 + 2 + 2 + 4 + 4 + 3),
        out_specs=vmem_specs(4),
        scratch_shapes=[
            pltpu.VMEM((rows, width), jnp.bfloat16),
            pltpu.VMEM((rows, width), jnp.bfloat16),
            pltpu.VMEM((rows, hidden_width), jnp.bfloat16),
        ],
        compiler_params=parameters(12),
        cost_estimate=pl.CostEstimate(
            flops=2 * rows * width * (3 * HD + HD + 2 * hidden_width),
            bytes_accessed=MIB,
            transcendentals=rows * hidden_width,
        ),
        name="last_rows",
    )(block, *normed, *gains, *weights, *tables, own_joined, middle_joined, early)


def fed_kernel(own_hidden_ref, middle_hidden_ref, downward_ref, *refs):
    blocks, gain_refs, (fed_ref, *normed_refs) = refs[:-5], refs[-5:-3], refs[-3:]
    normalize(blocks, gain_refs, normed_refs)
    hidden = jnp.concatenate([own_hidden_ref[...], middle_hidden_ref[...]], 0)
    chunk = 512
    for begin in range(0, downward_ref.shape[1], chunk):
        columns = slice(begin, begin + chunk)
        fed_ref[:, columns] = jnp.dot(
            hidden, downward_ref[:, columns], preferred_element_type=jnp.float32
        )


def fed_rows(own_hidden, middle_hidden, downward_weight, blocks, gains):
    rows = own_hidden.shape[0] + middle_hidden.shape[0]
    depth, width = downward_weight.shape
    normed = pltpu.VMEM((len(blocks) * blocks[0].shape[0], width), jnp.bfloat16)
    return pl.pallas_call(
        fed_kernel,
        out_shape=[pltpu.VMEM((rows, width), jnp.float32), normed, normed],
        in_specs=vmem_specs(5 + len(blocks)),
        out_specs=vmem_specs(3),
        compiler_params=parameters(12),
        cost_estimate=pl.CostEstimate(
            flops=2 * rows * depth * width, bytes_accessed=MIB, transcendentals=0
        ),
        name="fed_rows",
    )(own_hidden, middle_hidden, downward_weight, *blocks, *gains)


def rest_kernel(joined_ref, offsets_ref, output_ref, early_ref, late_ref, *refs):
    near_ref, far_ref, *owns = refs
    block_rows = far_ref.shape[0]
    tokens = joined_ref.shape[0]
    early = CORES * block_rows
    attended = attend(joined_ref, offsets_ref, 0, tokens, block_rows)
    attended = jnp.concatenate([attended[:early], attended[2 * early :]], 0)
    chunk = 512
    for begin in range(0, output_ref.shape[1], chunk):
        columns = slice(begin, begin + chunk)
        fed = jnp.concatenate([early_ref[:early, columns], late_ref[:, columns]], 0)
        partial = fed + jnp.dot(
            attended, output_ref[:, columns], preferred_element_type=jnp.float32
        )
        for number, own_ref in enumerate(owns):
            first = CORES * number * block_rows
            middle = first + block_rows
            own_ref[:, columns] = partial[first:middle]
            sibling = partial[middle : middle + block_rows].astype(jnp.bfloat16)
            if number < near_ref.shape[0]:
                near_ref[number, :, columns] = sibling
            else:
                far_ref[:, columns] = sibling


def rest_rows(joined, offsets, output_weight, early, late):
    width = early.shape[1]
    count = CHIPS - 1
    rows = late.shape[0] * count // (count - 1)
    shape = (rows // (CORES * count), width)
    shapes = [pltpu.VMEM((count - 1, *shape), jnp.bfloat16), pltpu.VMEM(shape, jnp.bfloat16)]
    shapes += [pltpu.VMEM(shape, jnp.float32)] * count
    return pl.pallas_call(
        rest_kernel,
        out_shape=shapes,
        in_specs=vmem_specs(5),
        out_specs=vmem_specs(2 + count),
        compiler_params=parameters(12),
        cost_estimate=pl.CostEstimate(
            flops=2 * rows * width * HD,
            bytes_accessed=MIB,
            transcendentals=rows * joined.shape[0],
        ),
        name="rest_rows",
    )(joined, offsets, output_weight, early, late)


def pages_kernel(joined_ref, destinations_ref, *page_refs):
    tokens = joined_ref.shape[0]
    slot_rows = page_refs[0].shape[0] * PAGE
    for number, page_ref in enumerate(page_refs):
        shape = (slot_rows, tokens)
        row = number * slot_rows + lax.broadcasted_iota(jnp.int32, shape, 0)
        placing = jnp.where(row == destinations_ref[...], 1.0, 0.0).astype(jnp.bfloat16)
        rows = jnp.dot(placing, joined_ref[:, HD:], preferred_element_type=jnp.float32)
        page_ref[...] = rows.astype(jnp.bfloat16).reshape(page_ref.shape)


def cached_pages(joined, destinations, replica_count):
    tokens = joined.shape[0]
    capacity = 2 * (tokens // PAGE) // replica_count
    shapes = [pltpu.VMEM((capacity, PAGE, 2 * HD), jnp.bfloat16)] * replica_count
    return pl.pallas_call(
        pages_kernel,
        out_shape=shapes,
        in_specs=vmem_specs(2),
        out_specs=vmem_specs(len(shapes)),
        compiler_params=parameters(8),
        cost_estimate=pl.CostEstimate(flops=0, bytes_accessed=MIB, transcendentals=0),
        name="cached_pages",
    )(joined, destinations)


def add_kernel(*refs):
    total = refs[0][...].astype(jnp.float32)
    for ref in refs[1:-1]:
        total = total + ref[...].astype(jnp.float32)
    refs[-1][...] = total.astype(refs[-1].dtype)


def added(name, *parts):
    return pl.pallas_call(
        add_kernel,
        out_shape=pltpu.VMEM(parts[0].shape, jnp.bfloat16),
        in_specs=vmem_specs(len(parts)),
        out_specs=pl.BlockSpec(memory_space=pltpu.VMEM),
        compiler_params=parameters(4),
        name=name,
    )(*parts)


def near_kernel(received_ref, zero_ref, one_ref, hidden_ref, first_ref, base_ref):
    first_ref[...] = (one_ref[...] + received_ref[1].astype(jnp.float32)).astype(jnp.bfloat16)
    zero = zero_ref[...] + received_ref[0].astype(jnp.float32)
    base_ref[...] = zero + hidden_ref[...].astype(jnp.float32)


def near_sums(received, owns, hidden):
    shape = hidden.shape
    return pl.pallas_call(
        near_kernel,
        out_shape=[pltpu.VMEM(shape, jnp.bfloat16), pltpu.VMEM(shape, jnp.float32)],
        in_specs=vmem_specs(4),
        out_specs=vmem_specs(2),
        compiler_params=parameters(4),
        name="near_sums",
    )(received, *owns, hidden)


def place_kernel(masks, *refs):
    group = lax.axis_index("dp")
    count = len(masks)
    pages, (part_ref, base_ref) = refs[:count], refs[count : count + 2]
    cache_ref, total_ref, sems = refs[count + 2 :]
    copies = [
        pltpu.make_async_copy(page_ref, cache_ref.at[0, group ^ mask], sems.at[number])
        for number, (mask, page_ref) in enumerate(zip(masks, pages))
    ]
    for copy in copies:
        copy.start()
    total_ref[...] = base_ref[...] + part_ref[...].astype(jnp.float32)
    for copy in copies:
        copy.wait()


def placed(masks, pages, part, base, replica_count):
    count = len(pages)
    return pl.pallas_call(
        functools.partial(place_kernel, masks),
        out_shape=[
            jax.ShapeDtypeStruct((1, replica_count) + pages[0].shape, pages[0].dtype),
            pltpu.VMEM(base.shape, base.dtype),
        ],
        in_specs=[pl.BlockSpec(memory_space=pl.ANY)] * count + vmem_specs(2),
        out_specs=[pl.BlockSpec(memory_space=pltpu.HBM)] + vmem_specs(1),
        scratch_shapes=[pltpu.SemaphoreType.DMA((count,))],
        compiler_params=parameters(4),
        name="placed",
    )(*pages, part, base)


def finish_kernel(masks, base_ref, *refs):
    count = len(masks)
    *parts, _, output_ref, cache_ref, total_scr, sems = refs
    parts, pages = parts[:-count], parts[-count:]
    group = lax.axis_index("dp")
    copies = [
        pltpu.make_async_copy(page_ref, cache_ref.at[0, group ^ mask], sems.at[number])
        for number, (mask, page_ref) in enumerate(zip(masks, pages))
    ]
    for copy in copies:
        copy.start()
    total = base_ref[...]
    for part_ref in parts:
        total = total + part_ref[...].astype(jnp.float32)
    total_scr[...] = total
    copies.append(pltpu.make_async_copy(total_scr, output_ref, sems.at[count]))
    copies[-1].start()
    for copy in copies:
        copy.wait()


def finished(base, parts, masks, pages, cache):
    count = len(pages)
    return pl.pallas_call(
        functools.partial(finish_kernel, masks),
        out_shape=[
            jax.ShapeDtypeStruct(base.shape, base.dtype),
            jax.ShapeDtypeStruct(cache.shape, cache.dtype),
        ],
        in_specs=vmem_specs(1 + len(parts))
        + [pl.BlockSpec(memory_space=pl.ANY)] * count
        + [pl.BlockSpec(memory_space=pltpu.HBM)],
        out_specs=[pl.BlockSpec(memory_space=pltpu.HBM)] * 2,
        scratch_shapes=[
            pltpu.VMEM(base.shape, base.dtype),
            pltpu.SemaphoreType.DMA((count + 1,)),
        ],
        input_output_aliases={1 + len(parts) + count: 1},
        compiler_params=parameters(4),
        name="finished",
    )(base, *parts, *pages, cache)


def shards_whole_heads(
    hidden_states,
    attention_gain,
    feedforward_gain,
    heads_weight,
    output_weight,
    upward_weight,
    downward_weight,
    segments,
    page_targets,
):
    replica_count = lax.axis_size("dp")
    to_chip = [mask * CORES for mask in range(CHIPS)]
    third = exchanged(hidden_states, "tensor", to_chip[3])
    first = exchanged(hidden_states, "tensor", to_chip[1])
    beside = exchanged(hidden_states, "tensor", 1)
    staged = (
        segments,
        page_targets.reshape(1, -1),
        hidden_states,
        attention_gain[None],
        feedforward_gain[None],
        heads_weight,
        upward_weight,
        downward_weight,
    )
    staged = own_rows(staged, replica_count)
    hidden, gains, weights, tables = staged[2], staged[3:5], staged[5:8], staged[8:12]
    heads, upward, downward = weights
    destinations, own_joined, own_hidden = staged[12:]

    third, own_joined = lax.optimization_barrier((third, own_joined))
    second = exchanged(third, "tensor", to_chip[1])
    middle_joined, middle_hidden, output = middle_rows(
        "middle_rows",
        ((0, 1), (3, 0)),
        (beside, third),
        gains,
        (heads, upward),
        tables[1:],
        output_weight,
    )
    third, first, middle_joined = lax.optimization_barrier((third, first, middle_joined))
    first_beside = exchanged(first, "tensor", 1)
    third_beside = exchanged(third, "tensor", 1)
    second, first_beside, third_beside, middle_joined, middle_hidden = lax.optimization_barrier(
        (second, first_beside, third_beside, middle_joined, middle_hidden)
    )
    second_beside = exchanged(second, "tensor", 1)
    fed, *normed = fed_rows(
        own_hidden, middle_hidden, downward, (third_beside, first, first_beside, second), gains
    )
    joined, fed_late, sibling, own = last_rows(
        second_beside,
        normed,
        gains,
        (heads, upward, downward, output),
        tables,
        own_joined,
        middle_joined,
        fed,
    )

    received = exchanged(sibling, "tensor", 1)
    partials = rest_rows(joined, tables[0], output, fed, fed_late)
    near_sibling, far_sibling, *owns = partials
    near_received = exchanged(near_sibling, "tensor", 1)
    third_sum = added("third_added", own, received)
    third_sum, far_sibling, joined = lax.optimization_barrier((third_sum, far_sibling, joined))
    passing = exchanged(third_sum, "tensor", to_chip[1])
    far_received = exchanged(far_sibling, "tensor", 1)
    pages = cached_pages(joined, destinations, replica_count)
    early, late = (3,), (2, 1)
    arriving = [exchanged(pages[mask], "dp", mask) for mask in early]
    first_sum, base = near_sums(near_received, owns[:2], hidden)
    from_first = exchanged(first_sum, "tensor", to_chip[1])
    second_sum = added("second_added", owns[2], passing, far_received)
    second_sum, late_pages = lax.optimization_barrier(
        (second_sum, [pages[mask] for mask in late])
    )
    from_second = exchanged(second_sum, "tensor", to_chip[2])
    late_pages = [exchanged(page, "dp", mask) for mask, page in zip(late, late_pages)]
    cache_pages, base = placed((0,) + early, [pages[0]] + arriving, from_first, base, replica_count)
    return tuple(finished(base, (from_second,), late, late_pages, cache_pages))


def solution(mesh):
    whole_heads = mesh.shape["tensor"] == H and mesh.shape["dp"] == 4
    shards = shards_whole_heads if whole_heads else shards_split_heads
    in_specs = (
        P(("dp", "tensor"), None),
        P(),
        P(),
        P(None, "tensor"),
        P("tensor", None),
        P(None, "tensor"),
        P("tensor", None),
        P("dp", None),
        P("dp", None),
    )
    out_specs = (P(("dp", "tensor"), None), P("dp", None, None, None, "tensor"))
    return jax.shard_map(shards, mesh=mesh, in_specs=in_specs, out_specs=out_specs, check_vma=False)
```

```python
import functools
import math

import jax
import jax.numpy as jnp
from jax import lax
from jax.experimental import pallas as pl
from jax.experimental.pallas import tpu as pltpu
from jax.sharding import PartitionSpec as P

H = 8
HD = 256
ROT = 64
PAGE = 16


epsilon = 1e-05
rotary_base = 10000.0
key_block = 256


def shortened(array):

    def short(part):
        return part.astype(jnp.bfloat16) if part.dtype == jnp.float32 else part

    return jax.tree.map(short, array)


def swapped(block, axis, apart):
    count = lax.axis_size(axis)
    route = []
    for low in range(count):
        high = low | 1 << apart
        if high != low and high < count:
            route += [(low, high), (high, low)]
    return lax.ppermute(block, axis, route)


def layer_norm(values, gain):
    floats = values.astype(jnp.float32)
    center = jnp.mean(floats, axis=-1, keepdims=True)
    shifted = floats - center
    spread = jnp.mean(shifted * shifted, axis=-1, keepdims=True)
    return (shifted * lax.rsqrt(spread + epsilon) * gain).astype(jnp.bfloat16)


def positions_of(stream):
    indices = jnp.arange(stream.shape[0], dtype=jnp.int32)
    boundary = jnp.concatenate([jnp.ones((1,), dtype=bool), stream[1:] != stream[:-1]])
    starting = lax.cummax(jnp.where(boundary, indices, jnp.zeros_like(indices)), axis=0)
    return (indices, starting)


def rotate_heads(vectors, offsets, rotary_dims):
    half_dims = rotary_dims // 2
    frequency = jnp.exp(
        jnp.arange(half_dims, dtype=jnp.float32) * (-2.0 * math.log(rotary_base) / rotary_dims)
    )
    angles = offsets.astype(jnp.float32)[:, None] * frequency[None, :]
    cosine = jnp.cos(angles)
    sine = jnp.sin(angles)
    floats = vectors.astype(jnp.float32)
    leading = floats[..., :half_dims]
    trailing = floats[..., half_dims:rotary_dims]
    rotated = jnp.concatenate(
        [
            leading * cosine - trailing * sine,
            trailing * cosine + leading * sine,
            floats[..., rotary_dims:],
        ],
        axis=-1,
    )
    return rotated.astype(jnp.bfloat16)


def shards_split_heads(
    hidden_states,
    attention_gain,
    feedforward_gain,
    heads_weight,
    output_weight,
    upward_weight,
    downward_weight,
    segments,
    page_targets,
):
    tensor_count = lax.axis_size("tensor")
    replica_count = lax.axis_size("dp")
    tensor_index = lax.axis_index("tensor")
    quarters = tensor_count // H
    quarter_width = HD // quarters
    quarter_index = tensor_index % quarters
    stream = segments[0]
    tokens_total = stream.shape[0]
    level_count = quarters.bit_length() - 1
    normed_attention = layer_norm(hidden_states, attention_gain)
    normed_feedforward = layer_norm(hidden_states, feedforward_gain)
    shard_rows = lax.all_gather(
        (normed_attention, normed_feedforward), "tensor", axis=0, tiled=True
    )
    joined_rows = jnp.dot(shard_rows[0], heads_weight, preferred_element_type=jnp.float32).astype(
        jnp.bfloat16
    )
    upward = jnp.dot(shard_rows[1], upward_weight, preferred_element_type=jnp.float32)
    hidden_rows = jax.nn.gelu(upward, approximate=False).astype(jnp.bfloat16)
    hidden = hidden_rows
    pieces = (
        joined_rows.reshape(tokens_total, 3, quarter_width)
        .transpose(1, 0, 2)
        .reshape(1, 3, tokens_total * quarter_width)
    )
    for bit_number in range(level_count):
        partner = swapped(shortened(pieces), "tensor", bit_number).astype(pieces.dtype)
        lower = tensor_index >> bit_number & 1 == 0
        pieces = jnp.where(
            lower, jnp.concatenate([pieces, partner], 0), jnp.concatenate([partner, pieces], 0)
        )
    whole_head = (
        pieces.reshape(quarters, 3, tokens_total, quarter_width)
        .transpose(1, 2, 0, 3)
        .reshape(3, tokens_total, HD)
    )
    indices, starting = positions_of(stream)
    offsets = indices - starting
    queries = rotate_heads(whole_head[0], offsets, ROT)
    keys = rotate_heads(whole_head[1], offsets, ROT)
    values = whole_head[2]
    block_rows = tokens_total // (2 * quarters)
    score_scale = HD ** (-0.5)

    def attend_block(block_number):
        first_row = block_number * block_rows
        block_queries = lax.dynamic_slice_in_dim(queries, first_row, block_rows, 0)
        query_segments = lax.dynamic_slice_in_dim(stream, first_row, block_rows, 0)
        query_indices = first_row + jnp.arange(block_rows, dtype=jnp.int32)
        lowest = lax.dynamic_index_in_dim(starting, first_row, 0, keepdims=False) // key_block
        highest = (first_row + block_rows + key_block - 1) // key_block

        def scores_of(key_number):
            key_first = key_number * key_block
            key_indices = key_first + jnp.arange(key_block, dtype=jnp.int32)
            scores = (
                jnp.dot(block_queries, keys.T, preferred_element_type=jnp.float32) * score_scale
            )
            allowed = (stream[None, :] == query_segments[:, None]) & (
                key_indices[None, :] <= query_indices[:, None]
            )
            return (scores, allowed)

        def find_peak(key_number, peak):
            scores, allowed = scores_of(key_number)
            return jnp.maximum(peak, jnp.max(jnp.where(allowed, scores, -jnp.inf), axis=1))

        peak = lax.fori_loop(
            lowest, highest, find_peak, jnp.full((block_rows,), -jnp.inf, jnp.float32)
        )

        def accumulate(key_number, state):
            weight_sum, mixed_sum = state
            scores, allowed = scores_of(key_number)
            weights = jnp.where(allowed, jnp.exp(scores - peak[:, None]), 0.0)
            mixed_next = mixed_sum + jnp.dot(
                weights.astype(jnp.bfloat16), values, preferred_element_type=jnp.float32
            )
            return (weight_sum + jnp.sum(weights, axis=1), mixed_next)

        start_state = (
            jnp.zeros((block_rows,), jnp.float32),
            jnp.zeros((block_rows, HD), jnp.float32),
        )
        weight_sum, mixed_sum = lax.fori_loop(lowest, highest, accumulate, start_state)
        return (mixed_sum / weight_sum[:, None]).astype(jnp.bfloat16)

    own_blocks = (2 * quarter_index, 2 * quarter_index + 1)
    own_rows = jnp.concatenate([attend_block(own_blocks[0]), attend_block(own_blocks[1])], 0)[None]
    for bit_number in range(level_count):
        partner = swapped(own_rows, "tensor", bit_number)
        lower = tensor_index >> bit_number & 1 == 0
        own_rows = jnp.where(
            lower, jnp.concatenate([own_rows, partner], 0), jnp.concatenate([partner, own_rows], 0)
        )
    attended = own_rows.reshape(tokens_total, HD)
    attended_quarter = lax.dynamic_slice_in_dim(
        attended, quarter_index * quarter_width, quarter_width, 1
    )
    hidden_rows = hidden
    summed = lax.psum_scatter(
        (
            jnp.dot(attended_quarter, output_weight, preferred_element_type=jnp.float32)
            + jnp.dot(hidden_rows, downward_weight, preferred_element_type=jnp.float32)
        ).astype(jnp.bfloat16),
        "tensor",
        scatter_dimension=0,
        tiled=True,
    ).astype(jnp.float32)
    layer_output = hidden_states.astype(jnp.float32) + summed
    key_quarter = lax.dynamic_slice_in_dim(keys, quarter_index * quarter_width, quarter_width, 1)
    value_quarter = joined_rows[:, 2 * quarter_width :]
    page_count = tokens_total // PAGE
    page_rows = jnp.concatenate([key_quarter, value_quarter], 1).reshape(
        page_count, PAGE * 2 * quarter_width
    )
    targets = page_targets[:, 0]
    page_numbers = jnp.arange(page_count, dtype=jnp.int32)
    earlier = jnp.sum(
        (
            (targets[None, :] == targets[:, None]) & (page_numbers[None, :] < page_numbers[:, None])
        ).astype(jnp.int32),
        axis=1,
    )
    capacity = 2 * page_count // replica_count
    slot_numbers = targets * capacity + earlier
    placing = (
        jnp.arange(replica_count * capacity, dtype=jnp.int32)[:, None] == slot_numbers[None, :]
    ).astype(jnp.bfloat16)
    outgoing = jnp.dot(placing, page_rows, preferred_element_type=jnp.float32).astype(jnp.bfloat16)
    outgoing = outgoing.reshape(replica_count, capacity, PAGE * 2 * quarter_width)
    incoming = lax.all_to_all(outgoing, "dp", split_axis=0, concat_axis=0, tiled=True)
    cache_pages = incoming.reshape(1, replica_count, capacity, PAGE, 2 * quarter_width)
    return (layer_output, cache_pages)


CORES = 2
CHIPS = 4
MIB = 1 << 20


def in_hbm(array):
    return pltpu.with_memory_space_constraint(array, pltpu.HBM)


def exchanged(block, axis, mask):
    count = lax.axis_size(axis)
    return lax.ppermute(block, axis, [(member, member ^ mask) for member in range(count)])


def vmem_specs(count):
    return [pl.BlockSpec(memory_space=pltpu.VMEM)] * count


def parameters(mebibytes):
    return pltpu.CompilerParams(vmem_limit_bytes=mebibytes * MIB)


def whereabouts():
    member = lax.axis_index("tensor")
    return member // CORES, member % CORES


ORDER = (0, 3, 1, 2)


def position_of(kind, half, block_rows):
    chip, core = whereabouts()
    return ((chip ^ kind) * CORES + (core ^ half)) * block_rows


def positions_along(first, shape, axis, block_rows):
    chip, core = whereabouts()
    bits = block_rows.bit_length() - 1
    place = first + lax.broadcasted_iota(jnp.int32, shape, axis)
    stand = place >> (bits + 1)
    kind = jnp.where(stand == 1, ORDER[1], jnp.maximum(stand - 1, 0))
    half = (place >> bits) & 1
    return ((((chip ^ kind) << 1) | (core ^ half)) << bits) | (place & (block_rows - 1))


def normalize(blocks, gain_refs, normed_refs, place=0):
    piece = 16
    gains = [gain_ref[...] for gain_ref in gain_refs]
    for number, block_ref in enumerate(blocks):
        block_rows = block_ref.shape[0]
        for part in range(0, block_rows, piece):
            floats = block_ref[part : part + piece, :].astype(jnp.float32)
            center = jnp.mean(floats, axis=-1, keepdims=True)
            shifted = floats - center
            spread = jnp.mean(shifted * shifted, axis=-1, keepdims=True)
            scaled = shifted * lax.rsqrt(spread + epsilon)
            first = place + number * block_rows + part
            for gain, normed_ref in zip(gains, normed_refs):
                normed_ref[first : first + piece, :] = (scaled * gain).astype(jnp.bfloat16)


def project(normed_ref, heads_ref, table_refs, places, joined_ref, first):
    rows = normed_ref.shape[0]
    block_rows = rows // len(places)
    own = slice(first, first + rows)
    cosine, sine_down, sine_up = [
        jnp.concatenate(
            [
                table_ref[pl.ds(pl.multiple_of(place, block_rows), block_rows), :]
                for place in places
            ],
            0,
        )
        for table_ref in table_refs
    ]
    for begin in range(0, heads_ref.shape[1], HD):
        columns = slice(begin, begin + HD)
        joined_ref[own, columns] = jnp.dot(
            normed_ref[...], heads_ref[:, columns], preferred_element_type=jnp.float32
        ).astype(jnp.bfloat16)
    for begin in (0, HD):
        columns = slice(begin, begin + 128)
        turning = joined_ref[own, columns].astype(jnp.float32)
        turned = (
            turning * cosine
            + pltpu.roll(turning, 128 - ROT // 2, 1) * sine_down
            + pltpu.roll(turning, ROT // 2, 1) * sine_up
        )
        joined_ref[own, columns] = turned.astype(jnp.bfloat16)


def hide(normed_ref, upward_ref, hidden_ref, place, chunk=256):
    rows = slice(place, place + normed_ref.shape[0])
    for first in range(0, upward_ref.shape[1], chunk):
        columns = slice(first, first + chunk)
        upward = jnp.dot(
            normed_ref[...], upward_ref[:, columns], preferred_element_type=jnp.float32
        )
        hidden = 0.5 * upward * (1.0 + lax.erf(upward * (0.5**0.5)))
        hidden_ref[rows, columns] = hidden.astype(jnp.bfloat16)


def attend(joined_ref, offsets_ref, first, rows, block_rows):
    tokens = joined_ref.shape[0]
    starts = [
        position_of(ORDER[place // (2 * block_rows)], (place // block_rows) % 2, block_rows)
        for place in range(first, first + rows, block_rows)
    ]
    reach = jnp.concatenate(
        [
            offsets_ref[pl.ds(pl.multiple_of(start, block_rows), block_rows), :]
            for start in starts
        ],
        0,
    )[:, :1].astype(jnp.int32)
    row = positions_along(first, (rows, 1), 0, block_rows)
    column = positions_along(0, (1, tokens), 1, block_rows)
    allowed = (column <= row) & (column >= row - reach)
    scores = lax.dot_general(
        joined_ref[first : first + rows, :HD],
        joined_ref[:, HD : 2 * HD],
        (((1,), (1,)), ((), ())),
        preferred_element_type=jnp.float32,
    ) * (HD ** (-0.5))
    peak = jnp.max(jnp.where(allowed, scores, -jnp.inf), axis=1, keepdims=True)
    weights = jnp.where(allowed, jnp.exp(scores - peak), 0.0)
    weight_sum = jnp.sum(weights, axis=1, keepdims=True)
    mixed = jnp.dot(
        weights.astype(jnp.bfloat16), joined_ref[:, 2 * HD :], preferred_element_type=jnp.float32
    )
    return (mixed / weight_sum).astype(jnp.bfloat16)


def make_tables(segments_ref, offsets_ref, cosine_ref, sine_down_ref, sine_up_ref):
    tokens = segments_ref.shape[1]
    shape = (tokens, tokens)
    rows = lax.broadcasted_iota(jnp.int32, shape, 0)
    columns = lax.broadcasted_iota(jnp.int32, shape, 1)
    across = jnp.broadcast_to(segments_ref[...], shape).astype(jnp.float32)
    down = jnp.sum(jnp.where(rows == columns, across, 0.0), axis=1, keepdims=True)
    earlier = (across == down) & (columns < rows)
    offsets = jnp.sum(jnp.where(earlier, 1.0, 0.0), axis=1, keepdims=True)
    offsets_ref[...] = jnp.broadcast_to(offsets, offsets_ref.shape)
    half = ROT // 2
    lane = lax.broadcasted_iota(jnp.int32, (tokens, 128), 1)
    step = (lane & (half - 1)).astype(jnp.float32)
    frequency = jnp.exp(step * (-2.0 * math.log(rotary_base) / ROT))
    angles = offsets * frequency
    sine = jnp.sin(angles)
    cosine_ref[...] = jnp.where(lane < ROT, jnp.cos(angles), 1.0)
    sine_down_ref[...] = jnp.where(lane < half, -sine, 0.0)
    sine_up_ref[...] = jnp.where((lane >= half) & (lane < ROT), sine, 0.0)


def make_destinations(targets_ref, destinations_ref, replica_count, block_rows):
    page_count = targets_ref.shape[1]
    tokens = destinations_ref.shape[1]
    capacity = 2 * page_count // replica_count
    square = (page_count, page_count)
    rows = lax.broadcasted_iota(jnp.int32, square, 0)
    columns = lax.broadcasted_iota(jnp.int32, square, 1)
    across = jnp.broadcast_to(targets_ref[...], square).astype(jnp.float32)
    down = jnp.sum(jnp.where(rows == columns, across, 0.0), axis=1, keepdims=True)
    earlier = jnp.where((across == down) & (columns < rows), 1.0, 0.0)
    slots = jnp.sum(earlier, axis=1, keepdims=True).astype(jnp.int32)
    slots = (down.astype(jnp.int32) ^ lax.axis_index("dp")) * capacity + slots
    positions = positions_along(0, (1, tokens), 1, block_rows)
    bits = PAGE.bit_length() - 1
    pages = lax.broadcasted_iota(jnp.int32, (page_count, tokens), 0)
    chosen = jnp.where(pages == positions >> bits, slots.astype(jnp.float32), 0.0)
    slot = jnp.sum(chosen, axis=0, keepdims=True).astype(jnp.int32)
    destinations_ref[...] = slot * PAGE + (positions & (PAGE - 1))


def copies_in(sources, targets, sems):
    copies = []
    for number, (source, target) in enumerate(zip(sources, targets)):
        parts = 4 if source.shape[0] >= 256 else 1
        rows = source.shape[0] // parts
        places = [pl.ds(part * rows, rows) for part in range(parts)]
        copies.append(
            [
                pltpu.make_async_copy(source.at[place], target.at[place], sems.at[number, part])
                for part, place in enumerate(places)
            ]
        )
    for copy in sum(copies, []):
        copy.start()
    return copies


def wait_for(copies):
    for copy in copies:
        copy.wait()


def own_kernel(count, replica_count, *refs):
    sources, targets = refs[:count], refs[count : 2 * count]
    offsets_ref, *table_refs, destinations_ref, joined_ref, hidden_ref = refs[2 * count : -3]
    attention_scr, feedforward_scr, sems = refs[-3:]
    copies = copies_in(sources, targets, sems)
    segments_ref, targets_ref, states_ref, *gain_refs, heads_ref, upward_ref, _ = targets
    block_rows = states_ref.shape[0]
    wait_for(copies[0])
    make_tables(segments_ref, offsets_ref, *table_refs)
    wait_for(copies[1])
    make_destinations(targets_ref, destinations_ref, replica_count, block_rows)
    for number in (2, 3, 4):
        wait_for(copies[number])
    normalize([states_ref], gain_refs, [attention_scr, feedforward_scr])
    wait_for(copies[5])
    places = [position_of(0, 0, block_rows)]
    project(attention_scr, heads_ref, table_refs, places, joined_ref, 0)
    wait_for(copies[6])
    hide(feedforward_scr, upward_ref, hidden_ref, 0)
    wait_for(copies[7])


def own_rows(staged, replica_count):
    tokens = staged[0].shape[1]
    rows, width = staged[2].shape
    hidden_width = staged[6].shape[1]
    shapes = [pltpu.VMEM(array.shape, array.dtype) for array in staged]
    shapes += [pltpu.VMEM((tokens, 128), jnp.float32)] * 4
    shapes += [
        pltpu.VMEM((1, tokens), jnp.int32),
        pltpu.VMEM((rows, 3 * HD), jnp.bfloat16),
        pltpu.VMEM((rows, hidden_width), jnp.bfloat16),
    ]
    count = len(staged)
    return pl.pallas_call(
        functools.partial(own_kernel, count, replica_count),
        out_shape=shapes,
        in_specs=[pl.BlockSpec(memory_space=pltpu.HBM)] * count,
        out_specs=vmem_specs(len(shapes)),
        scratch_shapes=[
            pltpu.VMEM((rows, width), jnp.bfloat16),
            pltpu.VMEM((rows, width), jnp.bfloat16),
            pltpu.SemaphoreType.DMA((count, 4)),
        ],
        compiler_params=parameters(12),
        cost_estimate=pl.CostEstimate(
            flops=2 * rows * width * (3 * HD + hidden_width),
            bytes_accessed=sum(array.nbytes for array in staged),
            transcendentals=rows * hidden_width,
        ),
        name="own_rows",
    )(*[in_hbm(array) for array in staged])


def middle_kernel(origins, *refs):
    count = len(origins)
    blocks, (gain_a, gain_f, heads_ref, upward_ref) = refs[:count], refs[count : count + 4]
    table_refs, refs = refs[count + 4 : count + 7], refs[count + 7 :]
    staged = (len(refs) - 5) // 2
    sources, (joined_ref, hidden_ref), refs = refs[:staged], refs[staged:][:2], refs[staged + 2 :]
    targets, (attention_scr, feedforward_scr, sems) = refs[:staged], refs[staged:]
    copies = copies_in(sources, targets, sems)
    block_rows = blocks[0].shape[0]
    normalize(blocks, [gain_a, gain_f], [attention_scr, feedforward_scr])
    places = [position_of(kind, half, block_rows) for kind, half in origins]
    project(attention_scr, heads_ref, table_refs, places, joined_ref, 0)
    hide(feedforward_scr, upward_ref, hidden_ref, 0)
    wait_for(sum(copies, []))


def middle_rows(name, origins, blocks, gains, weights, tables, *staged):
    block_rows, width = blocks[0].shape
    rows = len(blocks) * block_rows
    hidden_width = weights[1].shape[1]
    return pl.pallas_call(
        functools.partial(middle_kernel, origins),
        out_shape=[
            pltpu.VMEM((rows, 3 * HD), jnp.bfloat16),
            pltpu.VMEM((rows, hidden_width), jnp.bfloat16),
        ]
        + [pltpu.VMEM(array.shape, array.dtype) for array in staged],
        in_specs=vmem_specs(len(blocks) + 2 + 2 + 3)
        + [pl.BlockSpec(memory_space=pltpu.HBM)] * len(staged),
        out_specs=vmem_specs(2 + len(staged)),
        scratch_shapes=[
            pltpu.VMEM((rows, width), jnp.bfloat16),
            pltpu.VMEM((rows, width), jnp.bfloat16),
            pltpu.SemaphoreType.DMA((max(len(staged), 1), 4)),
        ],
        compiler_params=parameters(12),
        cost_estimate=pl.CostEstimate(
            flops=2 * rows * width * (3 * HD + hidden_width),
            bytes_accessed=MIB,
            transcendentals=rows * hidden_width,
        ),
        name=name,
    )(*blocks, *gains, *weights, *tables, *[in_hbm(array) for array in staged])


def last_kernel(*refs):
    block_ref, *normed_refs = refs[:3]
    gain_a, gain_f, heads_ref, upward_ref, downward_ref, output_ref = refs[3:9]
    offsets_ref, *table_refs = refs[9:13]
    own_joined_ref, middle_joined_ref, early_ref = refs[13:16]
    joined_ref, fed_ref, sibling_ref, own_ref = refs[16:20]
    attention_scr, feedforward_scr, hidden_scr = refs[20:]
    block_rows = block_ref.shape[0]
    tokens = joined_ref.shape[0]
    first = tokens - attention_scr.shape[0]
    count = normed_refs[0].shape[0]
    normalize([block_ref], [gain_a, gain_f], [attention_scr, feedforward_scr], count)
    for normed_ref, normed_scr in zip(normed_refs, (attention_scr, feedforward_scr)):
        normed_scr[:count, :] = normed_ref[...]
    joined_ref[:block_rows, :] = own_joined_ref[...]
    joined_ref[block_rows:first, :] = middle_joined_ref[...]
    origins = ((3, 1), (1, 0), (1, 1), (2, 0), (2, 1))
    places = [position_of(kind, half, block_rows) for kind, half in origins]
    project(attention_scr, heads_ref, table_refs, places, joined_ref, first)
    rows = CORES * block_rows
    hide(feedforward_scr, upward_ref, hidden_scr, 0)
    attended = attend(joined_ref, offsets_ref, first - block_rows, rows, block_rows)
    chunk = 512
    for begin in range(0, downward_ref.shape[1], chunk):
        columns = slice(begin, begin + chunk)
        fed = jnp.dot(hidden_scr[...], downward_ref[:, columns], preferred_element_type=jnp.float32)
        fed_ref[:, columns] = fed[block_rows:]
        product = jnp.dot(attended, output_ref[:, columns], preferred_element_type=jnp.float32)
        own_ref[:, columns] = early_ref[first - block_rows :, columns] + product[:block_rows]
        sibling = fed[:block_rows] + product[block_rows:]
        sibling_ref[:, columns] = sibling.astype(jnp.bfloat16)


def last_rows(block, normed, gains, weights, tables, own_joined, middle_joined, early):
    block_rows, width = block.shape
    rows = normed[0].shape[0] + block_rows
    hidden_width = weights[1].shape[1]
    tokens = CHIPS * CORES * block_rows
    return pl.pallas_call(
        last_kernel,
        out_shape=[
            pltpu.VMEM((tokens, 3 * HD), jnp.bfloat16),
            pltpu.VMEM((rows - block_rows, width), jnp.float32),
            pltpu.VMEM((block_rows, width), jnp.bfloat16),
            pltpu.VMEM((block_rows, width), jnp.float32),
        ],
        in_specs=vmem_specs(1 + 2 + 2 + 4 + 4 + 3),
        out_specs=vmem_specs(4),
        scratch_shapes=[
            pltpu.VMEM((rows, width), jnp.bfloat16),
            pltpu.VMEM((rows, width), jnp.bfloat16),
            pltpu.VMEM((rows, hidden_width), jnp.bfloat16),
        ],
        compiler_params=parameters(12),
        cost_estimate=pl.CostEstimate(
            flops=2 * rows * width * (3 * HD + HD + 2 * hidden_width),
            bytes_accessed=MIB,
            transcendentals=rows * hidden_width,
        ),
        name="last_rows",
    )(block, *normed, *gains, *weights, *tables, own_joined, middle_joined, early)


def fed_kernel(own_hidden_ref, middle_hidden_ref, downward_ref, *refs):
    blocks, gain_refs, (fed_ref, *normed_refs) = refs[:-5], refs[-5:-3], refs[-3:]
    normalize(blocks, gain_refs, normed_refs)
    hidden = jnp.concatenate([own_hidden_ref[...], middle_hidden_ref[...]], 0)
    chunk = 512
    for begin in range(0, downward_ref.shape[1], chunk):
        columns = slice(begin, begin + chunk)
        fed_ref[:, columns] = jnp.dot(
            hidden, downward_ref[:, columns], preferred_element_type=jnp.float32
        )


def fed_rows(own_hidden, middle_hidden, downward_weight, blocks, gains):
    rows = own_hidden.shape[0] + middle_hidden.shape[0]
    depth, width = downward_weight.shape
    normed = pltpu.VMEM((len(blocks) * blocks[0].shape[0], width), jnp.bfloat16)
    return pl.pallas_call(
        fed_kernel,
        out_shape=[pltpu.VMEM((rows, width), jnp.float32), normed, normed],
        in_specs=vmem_specs(5 + len(blocks)),
        out_specs=vmem_specs(3),
        compiler_params=parameters(12),
        cost_estimate=pl.CostEstimate(
            flops=2 * rows * depth * width, bytes_accessed=MIB, transcendentals=0
        ),
        name="fed_rows",
    )(own_hidden, middle_hidden, downward_weight, *blocks, *gains)


def rest_kernel(joined_ref, offsets_ref, output_ref, early_ref, late_ref, *refs):
    near_ref, far_ref, *owns = refs
    block_rows = far_ref.shape[0]
    tokens = joined_ref.shape[0]
    early = CORES * block_rows
    attended = attend(joined_ref, offsets_ref, 0, tokens, block_rows)
    attended = jnp.concatenate([attended[:early], attended[2 * early :]], 0)
    chunk = 512
    for begin in range(0, output_ref.shape[1], chunk):
        columns = slice(begin, begin + chunk)
        fed = jnp.concatenate([early_ref[:early, columns], late_ref[:, columns]], 0)
        partial = fed + jnp.dot(
            attended, output_ref[:, columns], preferred_element_type=jnp.float32
        )
        for number, own_ref in enumerate(owns):
            first = CORES * number * block_rows
            middle = first + block_rows
            own_ref[:, columns] = partial[first:middle]
            sibling = partial[middle : middle + block_rows].astype(jnp.bfloat16)
            if number < near_ref.shape[0]:
                near_ref[number, :, columns] = sibling
            else:
                far_ref[:, columns] = sibling


def rest_rows(joined, offsets, output_weight, early, late):
    width = early.shape[1]
    count = CHIPS - 1
    rows = late.shape[0] * count // (count - 1)
    shape = (rows // (CORES * count), width)
    shapes = [pltpu.VMEM((count - 1, *shape), jnp.bfloat16), pltpu.VMEM(shape, jnp.bfloat16)]
    shapes += [pltpu.VMEM(shape, jnp.float32)] * count
    return pl.pallas_call(
        rest_kernel,
        out_shape=shapes,
        in_specs=vmem_specs(5),
        out_specs=vmem_specs(2 + count),
        compiler_params=parameters(12),
        cost_estimate=pl.CostEstimate(
            flops=2 * rows * width * HD,
            bytes_accessed=MIB,
            transcendentals=rows * joined.shape[0],
        ),
        name="rest_rows",
    )(joined, offsets, output_weight, early, late)


def pages_kernel(joined_ref, destinations_ref, *page_refs):
    tokens = joined_ref.shape[0]
    slot_rows = page_refs[0].shape[0] * PAGE
    for number, page_ref in enumerate(page_refs):
        shape = (slot_rows, tokens)
        row = number * slot_rows + lax.broadcasted_iota(jnp.int32, shape, 0)
        placing = jnp.where(row == destinations_ref[...], 1.0, 0.0).astype(jnp.bfloat16)
        rows = jnp.dot(placing, joined_ref[:, HD:], preferred_element_type=jnp.float32)
        page_ref[...] = rows.astype(jnp.bfloat16).reshape(page_ref.shape)


def cached_pages(joined, destinations, replica_count):
    tokens = joined.shape[0]
    capacity = 2 * (tokens // PAGE) // replica_count
    shapes = [pltpu.VMEM((capacity, PAGE, 2 * HD), jnp.bfloat16)] * replica_count
    return pl.pallas_call(
        pages_kernel,
        out_shape=shapes,
        in_specs=vmem_specs(2),
        out_specs=vmem_specs(len(shapes)),
        compiler_params=parameters(8),
        cost_estimate=pl.CostEstimate(flops=0, bytes_accessed=MIB, transcendentals=0),
        name="cached_pages",
    )(joined, destinations)


def add_kernel(*refs):
    total = refs[0][...].astype(jnp.float32)
    for ref in refs[1:-1]:
        total = total + ref[...].astype(jnp.float32)
    refs[-1][...] = total.astype(refs[-1].dtype)


def added(name, *parts):
    return pl.pallas_call(
        add_kernel,
        out_shape=pltpu.VMEM(parts[0].shape, jnp.bfloat16),
        in_specs=vmem_specs(len(parts)),
        out_specs=pl.BlockSpec(memory_space=pltpu.VMEM),
        compiler_params=parameters(4),
        name=name,
    )(*parts)


def near_kernel(received_ref, zero_ref, one_ref, hidden_ref, first_ref, base_ref):
    first_ref[...] = (one_ref[...] + received_ref[1].astype(jnp.float32)).astype(jnp.bfloat16)
    zero = zero_ref[...] + received_ref[0].astype(jnp.float32)
    base_ref[...] = zero + hidden_ref[...].astype(jnp.float32)


def near_sums(received, owns, hidden):
    shape = hidden.shape
    return pl.pallas_call(
        near_kernel,
        out_shape=[pltpu.VMEM(shape, jnp.bfloat16), pltpu.VMEM(shape, jnp.float32)],
        in_specs=vmem_specs(4),
        out_specs=vmem_specs(2),
        compiler_params=parameters(4),
        name="near_sums",
    )(received, *owns, hidden)


def place_kernel(masks, *refs):
    group = lax.axis_index("dp")
    count = len(masks)
    pages, (part_ref, base_ref) = refs[:count], refs[count : count + 2]
    cache_ref, total_ref, sems = refs[count + 2 :]
    copies = [
        pltpu.make_async_copy(page_ref, cache_ref.at[0, group ^ mask], sems.at[number])
        for number, (mask, page_ref) in enumerate(zip(masks, pages))
    ]
    for copy in copies:
        copy.start()
    total_ref[...] = base_ref[...] + part_ref[...].astype(jnp.float32)
    for copy in copies:
        copy.wait()


def placed(masks, pages, part, base, replica_count):
    count = len(pages)
    return pl.pallas_call(
        functools.partial(place_kernel, masks),
        out_shape=[
            jax.ShapeDtypeStruct((1, replica_count) + pages[0].shape, pages[0].dtype),
            pltpu.VMEM(base.shape, base.dtype),
        ],
        in_specs=[pl.BlockSpec(memory_space=pl.ANY)] * count + vmem_specs(2),
        out_specs=[pl.BlockSpec(memory_space=pltpu.HBM)] + vmem_specs(1),
        scratch_shapes=[pltpu.SemaphoreType.DMA((count,))],
        compiler_params=parameters(4),
        name="placed",
    )(*pages, part, base)


def finish_kernel(masks, base_ref, *refs):
    count = len(masks)
    *parts, _, output_ref, cache_ref, total_scr, sems = refs
    parts, pages = parts[:-count], parts[-count:]
    group = lax.axis_index("dp")
    copies = [
        pltpu.make_async_copy(page_ref, cache_ref.at[0, group ^ mask], sems.at[number])
        for number, (mask, page_ref) in enumerate(zip(masks, pages))
    ]
    for copy in copies:
        copy.start()
    total = base_ref[...]
    for part_ref in parts:
        total = total + part_ref[...].astype(jnp.float32)
    total_scr[...] = total
    copies.append(pltpu.make_async_copy(total_scr, output_ref, sems.at[count]))
    copies[-1].start()
    for copy in copies:
        copy.wait()


def finished(base, parts, masks, pages, cache):
    count = len(pages)
    return pl.pallas_call(
        functools.partial(finish_kernel, masks),
        out_shape=[
            jax.ShapeDtypeStruct(base.shape, base.dtype),
            jax.ShapeDtypeStruct(cache.shape, cache.dtype),
        ],
        in_specs=vmem_specs(1 + len(parts))
        + [pl.BlockSpec(memory_space=pl.ANY)] * count
        + [pl.BlockSpec(memory_space=pltpu.HBM)],
        out_specs=[pl.BlockSpec(memory_space=pltpu.HBM)] * 2,
        scratch_shapes=[
            pltpu.VMEM(base.shape, base.dtype),
            pltpu.SemaphoreType.DMA((count + 1,)),
        ],
        input_output_aliases={1 + len(parts) + count: 1},
        compiler_params=parameters(4),
        name="finished",
    )(base, *parts, *pages, cache)


def shards_whole_heads(
    hidden_states,
    attention_gain,
    feedforward_gain,
    heads_weight,
    output_weight,
    upward_weight,
    downward_weight,
    segments,
    page_targets,
):
    replica_count = lax.axis_size("dp")
    to_chip = [mask * CORES for mask in range(CHIPS)]
    third = exchanged(hidden_states, "tensor", to_chip[3])
    first = exchanged(hidden_states, "tensor", to_chip[1])
    beside = exchanged(hidden_states, "tensor", 1)
    staged = (
        segments,
        page_targets.reshape(1, -1),
        hidden_states,
        attention_gain[None],
        feedforward_gain[None],
        heads_weight,
        upward_weight,
        downward_weight,
    )
    staged = own_rows(staged, replica_count)
    hidden, gains, weights, tables = staged[2], staged[3:5], staged[5:8], staged[8:12]
    heads, upward, downward = weights
    destinations, own_joined, own_hidden = staged[12:]

    third, own_joined = lax.optimization_barrier((third, own_joined))
    second = exchanged(third, "tensor", to_chip[1])
    middle_joined, middle_hidden, output = middle_rows(
        "middle_rows",
        ((0, 1), (3, 0)),
        (beside, third),
        gains,
        (heads, upward),
        tables[1:],
        output_weight,
    )
    third, first, middle_joined = lax.optimization_barrier((third, first, middle_joined))
    first_beside = exchanged(first, "tensor", 1)
    third_beside = exchanged(third, "tensor", 1)
    second, first_beside, third_beside, middle_joined, middle_hidden = lax.optimization_barrier(
        (second, first_beside, third_beside, middle_joined, middle_hidden)
    )
    second_beside = exchanged(second, "tensor", 1)
    fed, *normed = fed_rows(
        own_hidden, middle_hidden, downward, (third_beside, first, first_beside, second), gains
    )
    joined, fed_late, sibling, own = last_rows(
        second_beside,
        normed,
        gains,
        (heads, upward, downward, output),
        tables,
        own_joined,
        middle_joined,
        fed,
    )

    received = exchanged(sibling, "tensor", 1)
    partials = rest_rows(joined, tables[0], output, fed, fed_late)
    near_sibling, far_sibling, *owns = partials
    near_received = exchanged(near_sibling, "tensor", 1)
    third_sum = added("third_added", own, received)
    third_sum, far_sibling, joined = lax.optimization_barrier((third_sum, far_sibling, joined))
    passing = exchanged(third_sum, "tensor", to_chip[1])
    pages = cached_pages(joined, destinations, replica_count)
    far_sibling, pages = lax.optimization_barrier((far_sibling, pages))
    far_received = exchanged(far_sibling, "tensor", 1)
    early, late = (3,), (2, 1)
    arriving = [exchanged(pages[mask], "dp", mask) for mask in early]
    first_sum, base = near_sums(near_received, owns[:2], hidden)
    from_first = exchanged(first_sum, "tensor", to_chip[1])
    second_sum = added("second_added", owns[2], passing, far_received)
    second_sum, late_pages = lax.optimization_barrier(
        (second_sum, [pages[mask] for mask in late])
    )
    from_second = exchanged(second_sum, "tensor", to_chip[2])
    late_pages = [exchanged(page, "dp", mask) for mask, page in zip(late, late_pages)]
    cache_pages, base = placed((0,) + early, [pages[0]] + arriving, from_first, base, replica_count)
    return tuple(finished(base, (from_second,), late, late_pages, cache_pages))


def solution(mesh):
    whole_heads = mesh.shape["tensor"] == H and mesh.shape["dp"] == 4
    shards = shards_whole_heads if whole_heads else shards_split_heads
    in_specs = (
        P(("dp", "tensor"), None),
        P(),
        P(),
        P(None, "tensor"),
        P("tensor", None),
        P(None, "tensor"),
        P("tensor", None),
        P("dp", None),
        P("dp", None),
    )
    out_specs = (P(("dp", "tensor"), None), P("dp", None, None, None, "tensor"))
    return jax.shard_map(shards, mesh=mesh, in_specs=in_specs, out_specs=out_specs, check_vma=False)
```

```python
import functools
import math

import jax
import jax.numpy as jnp
from jax import lax
from jax.experimental import pallas as pl
from jax.experimental.pallas import tpu as pltpu
from jax.sharding import PartitionSpec as P

H = 8
HD = 256
ROT = 64
PAGE = 16


epsilon = 1e-05
rotary_base = 10000.0
key_block = 256


def shortened(array):

    def short(part):
        return part.astype(jnp.bfloat16) if part.dtype == jnp.float32 else part

    return jax.tree.map(short, array)


def swapped(block, axis, apart):
    count = lax.axis_size(axis)
    route = []
    for low in range(count):
        high = low | 1 << apart
        if high != low and high < count:
            route += [(low, high), (high, low)]
    return lax.ppermute(block, axis, route)


def layer_norm(values, gain):
    floats = values.astype(jnp.float32)
    center = jnp.mean(floats, axis=-1, keepdims=True)
    shifted = floats - center
    spread = jnp.mean(shifted * shifted, axis=-1, keepdims=True)
    return (shifted * lax.rsqrt(spread + epsilon) * gain).astype(jnp.bfloat16)


def positions_of(stream):
    indices = jnp.arange(stream.shape[0], dtype=jnp.int32)
    boundary = jnp.concatenate([jnp.ones((1,), dtype=bool), stream[1:] != stream[:-1]])
    starting = lax.cummax(jnp.where(boundary, indices, jnp.zeros_like(indices)), axis=0)
    return (indices, starting)


def rotate_heads(vectors, offsets, rotary_dims):
    half_dims = rotary_dims // 2
    frequency = jnp.exp(
        jnp.arange(half_dims, dtype=jnp.float32) * (-2.0 * math.log(rotary_base) / rotary_dims)
    )
    angles = offsets.astype(jnp.float32)[:, None] * frequency[None, :]
    cosine = jnp.cos(angles)
    sine = jnp.sin(angles)
    floats = vectors.astype(jnp.float32)
    leading = floats[..., :half_dims]
    trailing = floats[..., half_dims:rotary_dims]
    rotated = jnp.concatenate(
        [
            leading * cosine - trailing * sine,
            trailing * cosine + leading * sine,
            floats[..., rotary_dims:],
        ],
        axis=-1,
    )
    return rotated.astype(jnp.bfloat16)


def shards_split_heads(
    hidden_states,
    attention_gain,
    feedforward_gain,
    heads_weight,
    output_weight,
    upward_weight,
    downward_weight,
    segments,
    page_targets,
):
    tensor_count = lax.axis_size("tensor")
    replica_count = lax.axis_size("dp")
    tensor_index = lax.axis_index("tensor")
    quarters = tensor_count // H
    quarter_width = HD // quarters
    quarter_index = tensor_index % quarters
    stream = segments[0]
    tokens_total = stream.shape[0]
    level_count = quarters.bit_length() - 1
    normed_attention = layer_norm(hidden_states, attention_gain)
    normed_feedforward = layer_norm(hidden_states, feedforward_gain)
    shard_rows = lax.all_gather(
        (normed_attention, normed_feedforward), "tensor", axis=0, tiled=True
    )
    joined_rows = jnp.dot(shard_rows[0], heads_weight, preferred_element_type=jnp.float32).astype(
        jnp.bfloat16
    )
    upward = jnp.dot(shard_rows[1], upward_weight, preferred_element_type=jnp.float32)
    hidden_rows = jax.nn.gelu(upward, approximate=False).astype(jnp.bfloat16)
    hidden = hidden_rows
    pieces = (
        joined_rows.reshape(tokens_total, 3, quarter_width)
        .transpose(1, 0, 2)
        .reshape(1, 3, tokens_total * quarter_width)
    )
    for bit_number in range(level_count):
        partner = swapped(shortened(pieces), "tensor", bit_number).astype(pieces.dtype)
        lower = tensor_index >> bit_number & 1 == 0
        pieces = jnp.where(
            lower, jnp.concatenate([pieces, partner], 0), jnp.concatenate([partner, pieces], 0)
        )
    whole_head = (
        pieces.reshape(quarters, 3, tokens_total, quarter_width)
        .transpose(1, 2, 0, 3)
        .reshape(3, tokens_total, HD)
    )
    indices, starting = positions_of(stream)
    offsets = indices - starting
    queries = rotate_heads(whole_head[0], offsets, ROT)
    keys = rotate_heads(whole_head[1], offsets, ROT)
    values = whole_head[2]
    block_rows = tokens_total // (2 * quarters)
    score_scale = HD ** (-0.5)

    def attend_block(block_number):
        first_row = block_number * block_rows
        block_queries = lax.dynamic_slice_in_dim(queries, first_row, block_rows, 0)
        query_segments = lax.dynamic_slice_in_dim(stream, first_row, block_rows, 0)
        query_indices = first_row + jnp.arange(block_rows, dtype=jnp.int32)
        lowest = lax.dynamic_index_in_dim(starting, first_row, 0, keepdims=False) // key_block
        highest = (first_row + block_rows + key_block - 1) // key_block

        def scores_of(key_number):
            key_first = key_number * key_block
            key_indices = key_first + jnp.arange(key_block, dtype=jnp.int32)
            scores = (
                jnp.dot(block_queries, keys.T, preferred_element_type=jnp.float32) * score_scale
            )
            allowed = (stream[None, :] == query_segments[:, None]) & (
                key_indices[None, :] <= query_indices[:, None]
            )
            return (scores, allowed)

        def find_peak(key_number, peak):
            scores, allowed = scores_of(key_number)
            return jnp.maximum(peak, jnp.max(jnp.where(allowed, scores, -jnp.inf), axis=1))

        peak = lax.fori_loop(
            lowest, highest, find_peak, jnp.full((block_rows,), -jnp.inf, jnp.float32)
        )

        def accumulate(key_number, state):
            weight_sum, mixed_sum = state
            scores, allowed = scores_of(key_number)
            weights = jnp.where(allowed, jnp.exp(scores - peak[:, None]), 0.0)
            mixed_next = mixed_sum + jnp.dot(
                weights.astype(jnp.bfloat16), values, preferred_element_type=jnp.float32
            )
            return (weight_sum + jnp.sum(weights, axis=1), mixed_next)

        start_state = (
            jnp.zeros((block_rows,), jnp.float32),
            jnp.zeros((block_rows, HD), jnp.float32),
        )
        weight_sum, mixed_sum = lax.fori_loop(lowest, highest, accumulate, start_state)
        return (mixed_sum / weight_sum[:, None]).astype(jnp.bfloat16)

    own_blocks = (2 * quarter_index, 2 * quarter_index + 1)
    own_rows = jnp.concatenate([attend_block(own_blocks[0]), attend_block(own_blocks[1])], 0)[None]
    for bit_number in range(level_count):
        partner = swapped(own_rows, "tensor", bit_number)
        lower = tensor_index >> bit_number & 1 == 0
        own_rows = jnp.where(
            lower, jnp.concatenate([own_rows, partner], 0), jnp.concatenate([partner, own_rows], 0)
        )
    attended = own_rows.reshape(tokens_total, HD)
    attended_quarter = lax.dynamic_slice_in_dim(
        attended, quarter_index * quarter_width, quarter_width, 1
    )
    hidden_rows = hidden
    summed = lax.psum_scatter(
        (
            jnp.dot(attended_quarter, output_weight, preferred_element_type=jnp.float32)
            + jnp.dot(hidden_rows, downward_weight, preferred_element_type=jnp.float32)
        ).astype(jnp.bfloat16),
        "tensor",
        scatter_dimension=0,
        tiled=True,
    ).astype(jnp.float32)
    layer_output = hidden_states.astype(jnp.float32) + summed
    key_quarter = lax.dynamic_slice_in_dim(keys, quarter_index * quarter_width, quarter_width, 1)
    value_quarter = joined_rows[:, 2 * quarter_width :]
    page_count = tokens_total // PAGE
    page_rows = jnp.concatenate([key_quarter, value_quarter], 1).reshape(
        page_count, PAGE * 2 * quarter_width
    )
    targets = page_targets[:, 0]
    page_numbers = jnp.arange(page_count, dtype=jnp.int32)
    earlier = jnp.sum(
        (
            (targets[None, :] == targets[:, None]) & (page_numbers[None, :] < page_numbers[:, None])
        ).astype(jnp.int32),
        axis=1,
    )
    capacity = 2 * page_count // replica_count
    slot_numbers = targets * capacity + earlier
    placing = (
        jnp.arange(replica_count * capacity, dtype=jnp.int32)[:, None] == slot_numbers[None, :]
    ).astype(jnp.bfloat16)
    outgoing = jnp.dot(placing, page_rows, preferred_element_type=jnp.float32).astype(jnp.bfloat16)
    outgoing = outgoing.reshape(replica_count, capacity, PAGE * 2 * quarter_width)
    incoming = lax.all_to_all(outgoing, "dp", split_axis=0, concat_axis=0, tiled=True)
    cache_pages = incoming.reshape(1, replica_count, capacity, PAGE, 2 * quarter_width)
    return (layer_output, cache_pages)


CORES = 2
CHIPS = 4
MIB = 1 << 20


def in_hbm(array):
    return pltpu.with_memory_space_constraint(array, pltpu.HBM)


def exchanged(block, axis, mask):
    count = lax.axis_size(axis)
    return lax.ppermute(block, axis, [(member, member ^ mask) for member in range(count)])


def vmem_specs(count):
    return [pl.BlockSpec(memory_space=pltpu.VMEM)] * count


def parameters(mebibytes):
    return pltpu.CompilerParams(vmem_limit_bytes=mebibytes * MIB)


def whereabouts():
    member = lax.axis_index("tensor")
    return member // CORES, member % CORES


ORDER = (0, 3, 1, 2)


def position_of(kind, half, block_rows):
    chip, core = whereabouts()
    return ((chip ^ kind) * CORES + (core ^ half)) * block_rows


def positions_along(first, shape, axis, block_rows):
    chip, core = whereabouts()
    bits = block_rows.bit_length() - 1
    place = first + lax.broadcasted_iota(jnp.int32, shape, axis)
    stand = place >> (bits + 1)
    kind = jnp.where(stand == 1, ORDER[1], jnp.maximum(stand - 1, 0))
    half = (place >> bits) & 1
    return ((((chip ^ kind) << 1) | (core ^ half)) << bits) | (place & (block_rows - 1))


def normalize(blocks, gain_refs, normed_refs, place=0):
    piece = 16
    gains = [gain_ref[...] for gain_ref in gain_refs]
    for number, block_ref in enumerate(blocks):
        block_rows = block_ref.shape[0]
        for part in range(0, block_rows, piece):
            floats = block_ref[part : part + piece, :].astype(jnp.float32)
            center = jnp.mean(floats, axis=-1, keepdims=True)
            shifted = floats - center
            spread = jnp.mean(shifted * shifted, axis=-1, keepdims=True)
            scaled = shifted * lax.rsqrt(spread + epsilon)
            first = place + number * block_rows + part
            for gain, normed_ref in zip(gains, normed_refs):
                normed_ref[first : first + piece, :] = (scaled * gain).astype(jnp.bfloat16)


def project(normed_ref, heads_ref, table_refs, places, joined_ref, first):
    rows = normed_ref.shape[0]
    block_rows = rows // len(places)
    own = slice(first, first + rows)
    cosine, sine_down, sine_up = [
        jnp.concatenate(
            [
                table_ref[pl.ds(pl.multiple_of(place, block_rows), block_rows), :]
                for place in places
            ],
            0,
        )
        for table_ref in table_refs
    ]
    for begin in range(0, heads_ref.shape[1], HD):
        columns = slice(begin, begin + HD)
        joined_ref[own, columns] = jnp.dot(
            normed_ref[...], heads_ref[:, columns], preferred_element_type=jnp.float32
        ).astype(jnp.bfloat16)
    for begin in (0, HD):
        columns = slice(begin, begin + 128)
        turning = joined_ref[own, columns].astype(jnp.float32)
        turned = (
            turning * cosine
            + pltpu.roll(turning, 128 - ROT // 2, 1) * sine_down
            + pltpu.roll(turning, ROT // 2, 1) * sine_up
        )
        joined_ref[own, columns] = turned.astype(jnp.bfloat16)


def hide(normed_ref, upward_ref, hidden_ref, place, chunk=256):
    rows = slice(place, place + normed_ref.shape[0])
    for first in range(0, upward_ref.shape[1], chunk):
        columns = slice(first, first + chunk)
        upward = jnp.dot(
            normed_ref[...], upward_ref[:, columns], preferred_element_type=jnp.float32
        )
        hidden = 0.5 * upward * (1.0 + lax.erf(upward * (0.5**0.5)))
        hidden_ref[rows, columns] = hidden.astype(jnp.bfloat16)


def attend(joined_ref, offsets_ref, first, rows, block_rows):
    tokens = joined_ref.shape[0]
    starts = [
        position_of(ORDER[place // (2 * block_rows)], (place // block_rows) % 2, block_rows)
        for place in range(first, first + rows, block_rows)
    ]
    reach = jnp.concatenate(
        [
            offsets_ref[pl.ds(pl.multiple_of(start, block_rows), block_rows), :]
            for start in starts
        ],
        0,
    )[:, :1].astype(jnp.int32)
    row = positions_along(first, (rows, 1), 0, block_rows)
    column = positions_along(0, (1, tokens), 1, block_rows)
    allowed = (column <= row) & (column >= row - reach)
    scores = lax.dot_general(
        joined_ref[first : first + rows, :HD],
        joined_ref[:, HD : 2 * HD],
        (((1,), (1,)), ((), ())),
        preferred_element_type=jnp.float32,
    ) * (HD ** (-0.5))
    peak = jnp.max(jnp.where(allowed, scores, -jnp.inf), axis=1, keepdims=True)
    weights = jnp.where(allowed, jnp.exp(scores - peak), 0.0)
    weight_sum = jnp.sum(weights, axis=1, keepdims=True)
    mixed = jnp.dot(
        weights.astype(jnp.bfloat16), joined_ref[:, 2 * HD :], preferred_element_type=jnp.float32
    )
    return (mixed / weight_sum).astype(jnp.bfloat16)


def make_tables(segments_ref, offsets_ref, cosine_ref, sine_down_ref, sine_up_ref):
    tokens = segments_ref.shape[1]
    shape = (tokens, tokens)
    rows = lax.broadcasted_iota(jnp.int32, shape, 0)
    columns = lax.broadcasted_iota(jnp.int32, shape, 1)
    across = jnp.broadcast_to(segments_ref[...], shape).astype(jnp.float32)
    down = jnp.sum(jnp.where(rows == columns, across, 0.0), axis=1, keepdims=True)
    earlier = (across == down) & (columns < rows)
    offsets = jnp.sum(jnp.where(earlier, 1.0, 0.0), axis=1, keepdims=True)
    offsets_ref[...] = jnp.broadcast_to(offsets, offsets_ref.shape)
    half = ROT // 2
    lane = lax.broadcasted_iota(jnp.int32, (tokens, 128), 1)
    step = (lane & (half - 1)).astype(jnp.float32)
    frequency = jnp.exp(step * (-2.0 * math.log(rotary_base) / ROT))
    angles = offsets * frequency
    sine = jnp.sin(angles)
    cosine_ref[...] = jnp.where(lane < ROT, jnp.cos(angles), 1.0)
    sine_down_ref[...] = jnp.where(lane < half, -sine, 0.0)
    sine_up_ref[...] = jnp.where((lane >= half) & (lane < ROT), sine, 0.0)


def make_destinations(targets_ref, destinations_ref, replica_count, block_rows):
    page_count = targets_ref.shape[1]
    tokens = destinations_ref.shape[1]
    capacity = 2 * page_count // replica_count
    square = (page_count, page_count)
    rows = lax.broadcasted_iota(jnp.int32, square, 0)
    columns = lax.broadcasted_iota(jnp.int32, square, 1)
    across = jnp.broadcast_to(targets_ref[...], square).astype(jnp.float32)
    down = jnp.sum(jnp.where(rows == columns, across, 0.0), axis=1, keepdims=True)
    earlier = jnp.where((across == down) & (columns < rows), 1.0, 0.0)
    slots = jnp.sum(earlier, axis=1, keepdims=True).astype(jnp.int32)
    slots = (down.astype(jnp.int32) ^ lax.axis_index("dp")) * capacity + slots
    positions = positions_along(0, (1, tokens), 1, block_rows)
    bits = PAGE.bit_length() - 1
    pages = lax.broadcasted_iota(jnp.int32, (page_count, tokens), 0)
    chosen = jnp.where(pages == positions >> bits, slots.astype(jnp.float32), 0.0)
    slot = jnp.sum(chosen, axis=0, keepdims=True).astype(jnp.int32)
    destinations_ref[...] = slot * PAGE + (positions & (PAGE - 1))


def copies_in(sources, targets, sems):
    copies = []
    for number, (source, target) in enumerate(zip(sources, targets)):
        parts = 4 if source.shape[0] >= 256 else 1
        rows = source.shape[0] // parts
        places = [pl.ds(part * rows, rows) for part in range(parts)]
        copies.append(
            [
                pltpu.make_async_copy(source.at[place], target.at[place], sems.at[number, part])
                for part, place in enumerate(places)
            ]
        )
    for copy in sum(copies, []):
        copy.start()
    return copies


def wait_for(copies):
    for copy in copies:
        copy.wait()


def own_kernel(count, replica_count, *refs):
    sources, targets = refs[:count], refs[count : 2 * count]
    offsets_ref, *table_refs, destinations_ref, joined_ref, hidden_ref = refs[2 * count : -3]
    attention_scr, feedforward_scr, sems = refs[-3:]
    copies = copies_in(sources, targets, sems)
    segments_ref, targets_ref, states_ref, *gain_refs, heads_ref, upward_ref, _ = targets
    block_rows = states_ref.shape[0]
    wait_for(copies[0])
    make_tables(segments_ref, offsets_ref, *table_refs)
    wait_for(copies[1])
    make_destinations(targets_ref, destinations_ref, replica_count, block_rows)
    for number in (2, 3, 4):
        wait_for(copies[number])
    normalize([states_ref], gain_refs, [attention_scr, feedforward_scr])
    wait_for(copies[5])
    places = [position_of(0, 0, block_rows)]
    project(attention_scr, heads_ref, table_refs, places, joined_ref, 0)
    wait_for(copies[6])
    hide(feedforward_scr, upward_ref, hidden_ref, 0)
    wait_for(copies[7])


def own_rows(staged, replica_count):
    tokens = staged[0].shape[1]
    rows, width = staged[2].shape
    hidden_width = staged[6].shape[1]
    shapes = [pltpu.VMEM(array.shape, array.dtype) for array in staged]
    shapes += [pltpu.VMEM((tokens, 128), jnp.float32)] * 4
    shapes += [
        pltpu.VMEM((1, tokens), jnp.int32),
        pltpu.VMEM((rows, 3 * HD), jnp.bfloat16),
        pltpu.VMEM((rows, hidden_width), jnp.bfloat16),
    ]
    count = len(staged)
    return pl.pallas_call(
        functools.partial(own_kernel, count, replica_count),
        out_shape=shapes,
        in_specs=[pl.BlockSpec(memory_space=pltpu.HBM)] * count,
        out_specs=vmem_specs(len(shapes)),
        scratch_shapes=[
            pltpu.VMEM((rows, width), jnp.bfloat16),
            pltpu.VMEM((rows, width), jnp.bfloat16),
            pltpu.SemaphoreType.DMA((count, 4)),
        ],
        compiler_params=parameters(12),
        cost_estimate=pl.CostEstimate(
            flops=2 * rows * width * (3 * HD + hidden_width),
            bytes_accessed=sum(array.nbytes for array in staged),
            transcendentals=rows * hidden_width,
        ),
        name="own_rows",
    )(*[in_hbm(array) for array in staged])


def middle_kernel(origins, *refs):
    count = len(origins)
    blocks, (gain_a, gain_f, heads_ref, upward_ref) = refs[:count], refs[count : count + 4]
    table_refs, refs = refs[count + 4 : count + 7], refs[count + 7 :]
    staged = (len(refs) - 5) // 2
    sources, (joined_ref, hidden_ref), refs = refs[:staged], refs[staged:][:2], refs[staged + 2 :]
    targets, (attention_scr, feedforward_scr, sems) = refs[:staged], refs[staged:]
    copies = copies_in(sources, targets, sems)
    block_rows = blocks[0].shape[0]
    normalize(blocks, [gain_a, gain_f], [attention_scr, feedforward_scr])
    places = [position_of(kind, half, block_rows) for kind, half in origins]
    project(attention_scr, heads_ref, table_refs, places, joined_ref, 0)
    hide(feedforward_scr, upward_ref, hidden_ref, 0)
    wait_for(sum(copies, []))


def middle_rows(name, origins, blocks, gains, weights, tables, *staged):
    block_rows, width = blocks[0].shape
    rows = len(blocks) * block_rows
    hidden_width = weights[1].shape[1]
    return pl.pallas_call(
        functools.partial(middle_kernel, origins),
        out_shape=[
            pltpu.VMEM((rows, 3 * HD), jnp.bfloat16),
            pltpu.VMEM((rows, hidden_width), jnp.bfloat16),
        ]
        + [pltpu.VMEM(array.shape, array.dtype) for array in staged],
        in_specs=vmem_specs(len(blocks) + 2 + 2 + 3)
        + [pl.BlockSpec(memory_space=pltpu.HBM)] * len(staged),
        out_specs=vmem_specs(2 + len(staged)),
        scratch_shapes=[
            pltpu.VMEM((rows, width), jnp.bfloat16),
            pltpu.VMEM((rows, width), jnp.bfloat16),
            pltpu.SemaphoreType.DMA((max(len(staged), 1), 4)),
        ],
        compiler_params=parameters(12),
        cost_estimate=pl.CostEstimate(
            flops=2 * rows * width * (3 * HD + hidden_width),
            bytes_accessed=MIB,
            transcendentals=rows * hidden_width,
        ),
        name=name,
    )(*blocks, *gains, *weights, *tables, *[in_hbm(array) for array in staged])


def last_kernel(*refs):
    block_ref, *normed_refs = refs[:3]
    gain_a, gain_f, heads_ref, upward_ref, downward_ref, output_ref = refs[3:9]
    offsets_ref, *table_refs = refs[9:13]
    own_joined_ref, middle_joined_ref, early_ref = refs[13:16]
    joined_ref, fed_ref, sibling_ref, own_ref = refs[16:20]
    attention_scr, feedforward_scr, hidden_scr = refs[20:]
    block_rows = block_ref.shape[0]
    tokens = joined_ref.shape[0]
    first = tokens - attention_scr.shape[0]
    count = normed_refs[0].shape[0]
    normalize([block_ref], [gain_a, gain_f], [attention_scr, feedforward_scr], count)
    for normed_ref, normed_scr in zip(normed_refs, (attention_scr, feedforward_scr)):
        normed_scr[:count, :] = normed_ref[...]
    early = 3 * block_rows
    middle = early + block_rows
    joined_ref[:block_rows, :] = own_joined_ref[...]
    joined_ref[block_rows:early, :] = middle_joined_ref[: 2 * block_rows, :]
    origins = ((3, 1), (1, 1), (2, 0), (2, 1))
    places = [position_of(kind, half, block_rows) for kind, half in origins]
    project(attention_scr, heads_ref, table_refs, places, joined_ref, first)
    joined_ref[early:middle, :] = joined_ref[first : first + block_rows, :]
    joined_ref[middle : middle + block_rows, :] = middle_joined_ref[2 * block_rows :, :]
    rows = CORES * block_rows
    hide(feedforward_scr, upward_ref, hidden_scr, 0)
    attended = attend(joined_ref, offsets_ref, early - block_rows, rows, block_rows)
    chunk = 512
    for begin in range(0, downward_ref.shape[1], chunk):
        columns = slice(begin, begin + chunk)
        fed = jnp.dot(hidden_scr[...], downward_ref[:, columns], preferred_element_type=jnp.float32)
        fed_ref[:, columns] = fed[block_rows:]
        product = jnp.dot(attended, output_ref[:, columns], preferred_element_type=jnp.float32)
        own_ref[:, columns] = early_ref[early - block_rows : early, columns] + product[:block_rows]
        sibling = fed[:block_rows] + product[block_rows:]
        sibling_ref[:, columns] = sibling.astype(jnp.bfloat16)


def last_rows(block, normed, gains, weights, tables, own_joined, middle_joined, early):
    block_rows, width = block.shape
    rows = normed[0].shape[0] + block_rows
    hidden_width = weights[1].shape[1]
    tokens = CHIPS * CORES * block_rows
    return pl.pallas_call(
        last_kernel,
        out_shape=[
            pltpu.VMEM((tokens, 3 * HD), jnp.bfloat16),
            pltpu.VMEM((rows - block_rows, width), jnp.float32),
            pltpu.VMEM((block_rows, width), jnp.bfloat16),
            pltpu.VMEM((block_rows, width), jnp.float32),
        ],
        in_specs=vmem_specs(1 + 2 + 2 + 4 + 4 + 3),
        out_specs=vmem_specs(4),
        scratch_shapes=[
            pltpu.VMEM((rows, width), jnp.bfloat16),
            pltpu.VMEM((rows, width), jnp.bfloat16),
            pltpu.VMEM((rows, hidden_width), jnp.bfloat16),
        ],
        compiler_params=parameters(12),
        cost_estimate=pl.CostEstimate(
            flops=2 * rows * width * (3 * HD + HD + 2 * hidden_width),
            bytes_accessed=MIB,
            transcendentals=rows * hidden_width,
        ),
        name="last_rows",
    )(block, *normed, *gains, *weights, *tables, own_joined, middle_joined, early)


def fed_kernel(own_hidden_ref, middle_hidden_ref, downward_ref, *refs):
    blocks, gain_refs, (fed_ref, *normed_refs) = refs[:-5], refs[-5:-3], refs[-3:]
    normalize(blocks, gain_refs, normed_refs)
    hidden = jnp.concatenate([own_hidden_ref[...], middle_hidden_ref[...]], 0)
    chunk = 512
    for begin in range(0, downward_ref.shape[1], chunk):
        columns = slice(begin, begin + chunk)
        fed_ref[:, columns] = jnp.dot(
            hidden, downward_ref[:, columns], preferred_element_type=jnp.float32
        )


def fed_rows(own_hidden, middle_hidden, downward_weight, blocks, gains):
    rows = own_hidden.shape[0] + middle_hidden.shape[0]
    depth, width = downward_weight.shape
    normed = pltpu.VMEM((len(blocks) * blocks[0].shape[0], width), jnp.bfloat16)
    return pl.pallas_call(
        fed_kernel,
        out_shape=[pltpu.VMEM((rows, width), jnp.float32), normed, normed],
        in_specs=vmem_specs(5 + len(blocks)),
        out_specs=vmem_specs(3),
        compiler_params=parameters(12),
        cost_estimate=pl.CostEstimate(
            flops=2 * rows * depth * width, bytes_accessed=MIB, transcendentals=0
        ),
        name="fed_rows",
    )(own_hidden, middle_hidden, downward_weight, *blocks, *gains)


def rest_kernel(joined_ref, offsets_ref, output_ref, early_ref, late_ref, *refs):
    near_ref, far_ref, *owns = refs
    block_rows = far_ref.shape[0]
    tokens = joined_ref.shape[0]
    early = CORES * block_rows
    attended = attend(joined_ref, offsets_ref, 0, tokens, block_rows)
    attended = jnp.concatenate([attended[:early], attended[2 * early :]], 0)
    chunk = 512
    for begin in range(0, output_ref.shape[1], chunk):
        columns = slice(begin, begin + chunk)
        fed = jnp.concatenate(
            [
                early_ref[:early, columns],
                early_ref[early + block_rows :, columns],
                late_ref[:, columns],
            ],
            0,
        )
        partial = fed + jnp.dot(
            attended, output_ref[:, columns], preferred_element_type=jnp.float32
        )
        for number, own_ref in enumerate(owns):
            first = CORES * number * block_rows
            middle = first + block_rows
            own_ref[:, columns] = partial[first:middle]
            sibling = partial[middle : middle + block_rows].astype(jnp.bfloat16)
            if number < near_ref.shape[0]:
                near_ref[number, :, columns] = sibling
            else:
                far_ref[:, columns] = sibling


def rest_rows(joined, offsets, output_weight, early, late):
    width = early.shape[1]
    count = CHIPS - 1
    shape = (joined.shape[0] // (CORES * CHIPS), width)
    rows = CORES * count * shape[0]
    shapes = [pltpu.VMEM((count - 1, *shape), jnp.bfloat16), pltpu.VMEM(shape, jnp.bfloat16)]
    shapes += [pltpu.VMEM(shape, jnp.float32)] * count
    return pl.pallas_call(
        rest_kernel,
        out_shape=shapes,
        in_specs=vmem_specs(5),
        out_specs=vmem_specs(2 + count),
        compiler_params=parameters(12),
        cost_estimate=pl.CostEstimate(
            flops=2 * rows * width * HD,
            bytes_accessed=MIB,
            transcendentals=rows * joined.shape[0],
        ),
        name="rest_rows",
    )(joined, offsets, output_weight, early, late)


def pages_kernel(joined_ref, destinations_ref, *page_refs):
    tokens = joined_ref.shape[0]
    slot_rows = page_refs[0].shape[0] * PAGE
    for number, page_ref in enumerate(page_refs):
        shape = (slot_rows, tokens)
        row = number * slot_rows + lax.broadcasted_iota(jnp.int32, shape, 0)
        placing = jnp.where(row == destinations_ref[...], 1.0, 0.0).astype(jnp.bfloat16)
        rows = jnp.dot(placing, joined_ref[:, HD:], preferred_element_type=jnp.float32)
        page_ref[...] = rows.astype(jnp.bfloat16).reshape(page_ref.shape)


def cached_pages(joined, destinations, replica_count):
    tokens = joined.shape[0]
    capacity = 2 * (tokens // PAGE) // replica_count
    shapes = [pltpu.VMEM((capacity, PAGE, 2 * HD), jnp.bfloat16)] * replica_count
    return pl.pallas_call(
        pages_kernel,
        out_shape=shapes,
        in_specs=vmem_specs(2),
        out_specs=vmem_specs(len(shapes)),
        compiler_params=parameters(8),
        cost_estimate=pl.CostEstimate(flops=0, bytes_accessed=MIB, transcendentals=0),
        name="cached_pages",
    )(joined, destinations)


def add_kernel(*refs):
    total = refs[0][...].astype(jnp.float32)
    for ref in refs[1:-1]:
        total = total + ref[...].astype(jnp.float32)
    refs[-1][...] = total.astype(refs[-1].dtype)


def added(name, *parts):
    return pl.pallas_call(
        add_kernel,
        out_shape=pltpu.VMEM(parts[0].shape, jnp.bfloat16),
        in_specs=vmem_specs(len(parts)),
        out_specs=pl.BlockSpec(memory_space=pltpu.VMEM),
        compiler_params=parameters(4),
        name=name,
    )(*parts)


def near_kernel(received_ref, zero_ref, one_ref, hidden_ref, first_ref, base_ref):
    first_ref[...] = (one_ref[...] + received_ref[1].astype(jnp.float32)).astype(jnp.bfloat16)
    zero = zero_ref[...] + received_ref[0].astype(jnp.float32)
    base_ref[...] = zero + hidden_ref[...].astype(jnp.float32)


def near_sums(received, owns, hidden):
    shape = hidden.shape
    return pl.pallas_call(
        near_kernel,
        out_shape=[pltpu.VMEM(shape, jnp.bfloat16), pltpu.VMEM(shape, jnp.float32)],
        in_specs=vmem_specs(4),
        out_specs=vmem_specs(2),
        compiler_params=parameters(4),
        name="near_sums",
    )(received, *owns, hidden)


def place_kernel(masks, *refs):
    group = lax.axis_index("dp")
    count = len(masks)
    pages, (part_ref, base_ref) = refs[:count], refs[count : count + 2]
    cache_ref, total_ref, sems = refs[count + 2 :]
    copies = [
        pltpu.make_async_copy(page_ref, cache_ref.at[0, group ^ mask], sems.at[number])
        for number, (mask, page_ref) in enumerate(zip(masks, pages))
    ]
    for copy in copies:
        copy.start()
    total_ref[...] = base_ref[...] + part_ref[...].astype(jnp.float32)
    for copy in copies:
        copy.wait()


def placed(masks, pages, part, base, replica_count):
    count = len(pages)
    return pl.pallas_call(
        functools.partial(place_kernel, masks),
        out_shape=[
            jax.ShapeDtypeStruct((1, replica_count) + pages[0].shape, pages[0].dtype),
            pltpu.VMEM(base.shape, base.dtype),
        ],
        in_specs=[pl.BlockSpec(memory_space=pl.ANY)] * count + vmem_specs(2),
        out_specs=[pl.BlockSpec(memory_space=pltpu.HBM)] + vmem_specs(1),
        scratch_shapes=[pltpu.SemaphoreType.DMA((count,))],
        compiler_params=parameters(4),
        name="placed",
    )(*pages, part, base)


def finish_kernel(masks, base_ref, *refs):
    count = len(masks)
    *parts, _, output_ref, cache_ref, total_scr, sems = refs
    parts, pages = parts[:-count], parts[-count:]
    group = lax.axis_index("dp")
    copies = [
        pltpu.make_async_copy(page_ref, cache_ref.at[0, group ^ mask], sems.at[number])
        for number, (mask, page_ref) in enumerate(zip(masks, pages))
    ]
    for copy in copies:
        copy.start()
    total = base_ref[...]
    for part_ref in parts:
        total = total + part_ref[...].astype(jnp.float32)
    total_scr[...] = total
    copies.append(pltpu.make_async_copy(total_scr, output_ref, sems.at[count]))
    copies[-1].start()
    for copy in copies:
        copy.wait()


def finished(base, parts, masks, pages, cache):
    count = len(pages)
    return pl.pallas_call(
        functools.partial(finish_kernel, masks),
        out_shape=[
            jax.ShapeDtypeStruct(base.shape, base.dtype),
            jax.ShapeDtypeStruct(cache.shape, cache.dtype),
        ],
        in_specs=vmem_specs(1 + len(parts))
        + [pl.BlockSpec(memory_space=pl.ANY)] * count
        + [pl.BlockSpec(memory_space=pltpu.HBM)],
        out_specs=[pl.BlockSpec(memory_space=pltpu.HBM)] * 2,
        scratch_shapes=[
            pltpu.VMEM(base.shape, base.dtype),
            pltpu.SemaphoreType.DMA((count + 1,)),
        ],
        input_output_aliases={1 + len(parts) + count: 1},
        compiler_params=parameters(4),
        name="finished",
    )(base, *parts, *pages, cache)


def shards_whole_heads(
    hidden_states,
    attention_gain,
    feedforward_gain,
    heads_weight,
    output_weight,
    upward_weight,
    downward_weight,
    segments,
    page_targets,
):
    replica_count = lax.axis_size("dp")
    to_chip = [mask * CORES for mask in range(CHIPS)]
    third = exchanged(hidden_states, "tensor", to_chip[3])
    first = exchanged(hidden_states, "tensor", to_chip[1])
    beside = exchanged(hidden_states, "tensor", 1)
    staged = (
        segments,
        page_targets.reshape(1, -1),
        hidden_states,
        attention_gain[None],
        feedforward_gain[None],
        heads_weight,
        upward_weight,
        downward_weight,
    )
    staged = own_rows(staged, replica_count)
    hidden, gains, weights, tables = staged[2], staged[3:5], staged[5:8], staged[8:12]
    heads, upward, downward = weights
    destinations, own_joined, own_hidden = staged[12:]

    third, own_joined = lax.optimization_barrier((third, own_joined))
    second = exchanged(third, "tensor", to_chip[1])
    middle_joined, middle_hidden, output = middle_rows(
        "middle_rows",
        ((0, 1), (3, 0), (1, 0)),
        (beside, third, first),
        gains,
        (heads, upward),
        tables[1:],
        output_weight,
    )
    third, first, middle_joined = lax.optimization_barrier((third, first, middle_joined))
    first_beside = exchanged(first, "tensor", 1)
    third_beside = exchanged(third, "tensor", 1)
    second, first_beside, third_beside, middle_joined, middle_hidden = lax.optimization_barrier(
        (second, first_beside, third_beside, middle_joined, middle_hidden)
    )
    second_beside = exchanged(second, "tensor", 1)
    fed, *normed = fed_rows(
        own_hidden, middle_hidden, downward, (third_beside, first_beside, second), gains
    )
    joined, fed_late, sibling, own = last_rows(
        second_beside,
        normed,
        gains,
        (heads, upward, downward, output),
        tables,
        own_joined,
        middle_joined,
        fed,
    )

    received = exchanged(sibling, "tensor", 1)
    partials = rest_rows(joined, tables[0], output, fed, fed_late)
    near_sibling, far_sibling, *owns = partials
    near_received = exchanged(near_sibling, "tensor", 1)
    third_sum = added("third_added", own, received)
    third_sum, far_sibling, joined = lax.optimization_barrier((third_sum, far_sibling, joined))
    passing = exchanged(third_sum, "tensor", to_chip[1])
    pages = cached_pages(joined, destinations, replica_count)
    far_sibling, pages = lax.optimization_barrier((far_sibling, pages))
    far_received = exchanged(far_sibling, "tensor", 1)
    early, late = (3,), (2, 1)
    arriving = [exchanged(pages[mask], "dp", mask) for mask in early]
    first_sum, base = near_sums(near_received, owns[:2], hidden)
    from_first = exchanged(first_sum, "tensor", to_chip[1])
    second_sum = added("second_added", owns[2], passing, far_received)
    second_sum, late_pages = lax.optimization_barrier(
        (second_sum, [pages[mask] for mask in late])
    )
    from_second = exchanged(second_sum, "tensor", to_chip[2])
    late_pages = [exchanged(page, "dp", mask) for mask, page in zip(late, late_pages)]
    cache_pages, base = placed((0,) + early, [pages[0]] + arriving, from_first, base, replica_count)
    return tuple(finished(base, (from_second,), late, late_pages, cache_pages))


def solution(mesh):
    whole_heads = mesh.shape["tensor"] == H and mesh.shape["dp"] == 4
    shards = shards_whole_heads if whole_heads else shards_split_heads
    in_specs = (
        P(("dp", "tensor"), None),
        P(),
        P(),
        P(None, "tensor"),
        P("tensor", None),
        P(None, "tensor"),
        P("tensor", None),
        P("dp", None),
        P("dp", None),
    )
    out_specs = (P(("dp", "tensor"), None), P("dp", None, None, None, "tensor"))
    return jax.shard_map(shards, mesh=mesh, in_specs=in_specs, out_specs=out_specs, check_vma=False)
```

```python
import functools
import math

import jax
import jax.numpy as jnp
from jax import lax
from jax.experimental import pallas as pl
from jax.experimental.pallas import tpu as pltpu
from jax.sharding import PartitionSpec as P

H = 8
HD = 256
ROT = 64
PAGE = 16


epsilon = 1e-05
rotary_base = 10000.0
key_block = 256


def shortened(array):

    def short(part):
        return part.astype(jnp.bfloat16) if part.dtype == jnp.float32 else part

    return jax.tree.map(short, array)


def swapped(block, axis, apart):
    count = lax.axis_size(axis)
    route = []
    for low in range(count):
        high = low | 1 << apart
        if high != low and high < count:
            route += [(low, high), (high, low)]
    return lax.ppermute(block, axis, route)


def layer_norm(values, gain):
    floats = values.astype(jnp.float32)
    center = jnp.mean(floats, axis=-1, keepdims=True)
    shifted = floats - center
    spread = jnp.mean(shifted * shifted, axis=-1, keepdims=True)
    return (shifted * lax.rsqrt(spread + epsilon) * gain).astype(jnp.bfloat16)


def positions_of(stream):
    indices = jnp.arange(stream.shape[0], dtype=jnp.int32)
    boundary = jnp.concatenate([jnp.ones((1,), dtype=bool), stream[1:] != stream[:-1]])
    starting = lax.cummax(jnp.where(boundary, indices, jnp.zeros_like(indices)), axis=0)
    return (indices, starting)


def rotate_heads(vectors, offsets, rotary_dims):
    half_dims = rotary_dims // 2
    frequency = jnp.exp(
        jnp.arange(half_dims, dtype=jnp.float32) * (-2.0 * math.log(rotary_base) / rotary_dims)
    )
    angles = offsets.astype(jnp.float32)[:, None] * frequency[None, :]
    cosine = jnp.cos(angles)
    sine = jnp.sin(angles)
    floats = vectors.astype(jnp.float32)
    leading = floats[..., :half_dims]
    trailing = floats[..., half_dims:rotary_dims]
    rotated = jnp.concatenate(
        [
            leading * cosine - trailing * sine,
            trailing * cosine + leading * sine,
            floats[..., rotary_dims:],
        ],
        axis=-1,
    )
    return rotated.astype(jnp.bfloat16)


def shards_split_heads(
    hidden_states,
    attention_gain,
    feedforward_gain,
    heads_weight,
    output_weight,
    upward_weight,
    downward_weight,
    segments,
    page_targets,
):
    tensor_count = lax.axis_size("tensor")
    replica_count = lax.axis_size("dp")
    tensor_index = lax.axis_index("tensor")
    quarters = tensor_count // H
    quarter_width = HD // quarters
    quarter_index = tensor_index % quarters
    stream = segments[0]
    tokens_total = stream.shape[0]
    level_count = quarters.bit_length() - 1
    normed_attention = layer_norm(hidden_states, attention_gain)
    normed_feedforward = layer_norm(hidden_states, feedforward_gain)
    shard_rows = lax.all_gather(
        (normed_attention, normed_feedforward), "tensor", axis=0, tiled=True
    )
    joined_rows = jnp.dot(shard_rows[0], heads_weight, preferred_element_type=jnp.float32).astype(
        jnp.bfloat16
    )
    upward = jnp.dot(shard_rows[1], upward_weight, preferred_element_type=jnp.float32)
    hidden_rows = jax.nn.gelu(upward, approximate=False).astype(jnp.bfloat16)
    hidden = hidden_rows
    pieces = (
        joined_rows.reshape(tokens_total, 3, quarter_width)
        .transpose(1, 0, 2)
        .reshape(1, 3, tokens_total * quarter_width)
    )
    for bit_number in range(level_count):
        partner = swapped(shortened(pieces), "tensor", bit_number).astype(pieces.dtype)
        lower = tensor_index >> bit_number & 1 == 0
        pieces = jnp.where(
            lower, jnp.concatenate([pieces, partner], 0), jnp.concatenate([partner, pieces], 0)
        )
    whole_head = (
        pieces.reshape(quarters, 3, tokens_total, quarter_width)
        .transpose(1, 2, 0, 3)
        .reshape(3, tokens_total, HD)
    )
    indices, starting = positions_of(stream)
    offsets = indices - starting
    queries = rotate_heads(whole_head[0], offsets, ROT)
    keys = rotate_heads(whole_head[1], offsets, ROT)
    values = whole_head[2]
    block_rows = tokens_total // (2 * quarters)
    score_scale = HD ** (-0.5)

    def attend_block(block_number):
        first_row = block_number * block_rows
        block_queries = lax.dynamic_slice_in_dim(queries, first_row, block_rows, 0)
        query_segments = lax.dynamic_slice_in_dim(stream, first_row, block_rows, 0)
        query_indices = first_row + jnp.arange(block_rows, dtype=jnp.int32)
        lowest = lax.dynamic_index_in_dim(starting, first_row, 0, keepdims=False) // key_block
        highest = (first_row + block_rows + key_block - 1) // key_block

        def scores_of(key_number):
            key_first = key_number * key_block
            key_indices = key_first + jnp.arange(key_block, dtype=jnp.int32)
            scores = (
                jnp.dot(block_queries, keys.T, preferred_element_type=jnp.float32) * score_scale
            )
            allowed = (stream[None, :] == query_segments[:, None]) & (
                key_indices[None, :] <= query_indices[:, None]
            )
            return (scores, allowed)

        def find_peak(key_number, peak):
            scores, allowed = scores_of(key_number)
            return jnp.maximum(peak, jnp.max(jnp.where(allowed, scores, -jnp.inf), axis=1))

        peak = lax.fori_loop(
            lowest, highest, find_peak, jnp.full((block_rows,), -jnp.inf, jnp.float32)
        )

        def accumulate(key_number, state):
            weight_sum, mixed_sum = state
            scores, allowed = scores_of(key_number)
            weights = jnp.where(allowed, jnp.exp(scores - peak[:, None]), 0.0)
            mixed_next = mixed_sum + jnp.dot(
                weights.astype(jnp.bfloat16), values, preferred_element_type=jnp.float32
            )
            return (weight_sum + jnp.sum(weights, axis=1), mixed_next)

        start_state = (
            jnp.zeros((block_rows,), jnp.float32),
            jnp.zeros((block_rows, HD), jnp.float32),
        )
        weight_sum, mixed_sum = lax.fori_loop(lowest, highest, accumulate, start_state)
        return (mixed_sum / weight_sum[:, None]).astype(jnp.bfloat16)

    own_blocks = (2 * quarter_index, 2 * quarter_index + 1)
    own_rows = jnp.concatenate([attend_block(own_blocks[0]), attend_block(own_blocks[1])], 0)[None]
    for bit_number in range(level_count):
        partner = swapped(own_rows, "tensor", bit_number)
        lower = tensor_index >> bit_number & 1 == 0
        own_rows = jnp.where(
            lower, jnp.concatenate([own_rows, partner], 0), jnp.concatenate([partner, own_rows], 0)
        )
    attended = own_rows.reshape(tokens_total, HD)
    attended_quarter = lax.dynamic_slice_in_dim(
        attended, quarter_index * quarter_width, quarter_width, 1
    )
    hidden_rows = hidden
    summed = lax.psum_scatter(
        (
            jnp.dot(attended_quarter, output_weight, preferred_element_type=jnp.float32)
            + jnp.dot(hidden_rows, downward_weight, preferred_element_type=jnp.float32)
        ).astype(jnp.bfloat16),
        "tensor",
        scatter_dimension=0,
        tiled=True,
    ).astype(jnp.float32)
    layer_output = hidden_states.astype(jnp.float32) + summed
    key_quarter = lax.dynamic_slice_in_dim(keys, quarter_index * quarter_width, quarter_width, 1)
    value_quarter = joined_rows[:, 2 * quarter_width :]
    page_count = tokens_total // PAGE
    page_rows = jnp.concatenate([key_quarter, value_quarter], 1).reshape(
        page_count, PAGE * 2 * quarter_width
    )
    targets = page_targets[:, 0]
    page_numbers = jnp.arange(page_count, dtype=jnp.int32)
    earlier = jnp.sum(
        (
            (targets[None, :] == targets[:, None]) & (page_numbers[None, :] < page_numbers[:, None])
        ).astype(jnp.int32),
        axis=1,
    )
    capacity = 2 * page_count // replica_count
    slot_numbers = targets * capacity + earlier
    placing = (
        jnp.arange(replica_count * capacity, dtype=jnp.int32)[:, None] == slot_numbers[None, :]
    ).astype(jnp.bfloat16)
    outgoing = jnp.dot(placing, page_rows, preferred_element_type=jnp.float32).astype(jnp.bfloat16)
    outgoing = outgoing.reshape(replica_count, capacity, PAGE * 2 * quarter_width)
    incoming = lax.all_to_all(outgoing, "dp", split_axis=0, concat_axis=0, tiled=True)
    cache_pages = incoming.reshape(1, replica_count, capacity, PAGE, 2 * quarter_width)
    return (layer_output, cache_pages)


CORES = 2
CHIPS = 4
MIB = 1 << 20


def in_hbm(array):
    return pltpu.with_memory_space_constraint(array, pltpu.HBM)


def exchanged(block, axis, mask):
    count = lax.axis_size(axis)
    return lax.ppermute(block, axis, [(member, member ^ mask) for member in range(count)])


def vmem_specs(count):
    return [pl.BlockSpec(memory_space=pltpu.VMEM)] * count


def parameters(mebibytes):
    return pltpu.CompilerParams(vmem_limit_bytes=mebibytes * MIB)


def whereabouts():
    member = lax.axis_index("tensor")
    return member // CORES, member % CORES


ORDER = (0, 3, 1, 2)


def position_of(kind, half, block_rows):
    chip, core = whereabouts()
    return ((chip ^ kind) * CORES + (core ^ half)) * block_rows


def positions_along(first, shape, axis, block_rows):
    chip, core = whereabouts()
    bits = block_rows.bit_length() - 1
    place = first + lax.broadcasted_iota(jnp.int32, shape, axis)
    stand = place >> (bits + 1)
    kind = jnp.where(stand == 1, ORDER[1], jnp.maximum(stand - 1, 0))
    half = (place >> bits) & 1
    return ((((chip ^ kind) << 1) | (core ^ half)) << bits) | (place & (block_rows - 1))


def normalize(blocks, gain_refs, normed_refs, place=0):
    piece = 16
    gains = [gain_ref[...] for gain_ref in gain_refs]
    for number, block_ref in enumerate(blocks):
        block_rows = block_ref.shape[0]
        for part in range(0, block_rows, piece):
            floats = block_ref[part : part + piece, :].astype(jnp.float32)
            center = jnp.mean(floats, axis=-1, keepdims=True)
            shifted = floats - center
            spread = jnp.mean(shifted * shifted, axis=-1, keepdims=True)
            scaled = shifted * lax.rsqrt(spread + epsilon)
            first = place + number * block_rows + part
            for gain, normed_ref in zip(gains, normed_refs):
                normed_ref[first : first + piece, :] = (scaled * gain).astype(jnp.bfloat16)


def project(normed_ref, heads_ref, table_refs, places, joined_ref, first):
    rows = normed_ref.shape[0]
    block_rows = rows // len(places)
    own = slice(first, first + rows)
    cosine, sine_down, sine_up = [
        jnp.concatenate(
            [
                table_ref[pl.ds(pl.multiple_of(place, block_rows), block_rows), :]
                for place in places
            ],
            0,
        )
        for table_ref in table_refs
    ]
    for begin in range(0, heads_ref.shape[1], HD):
        columns = slice(begin, begin + HD)
        joined_ref[own, columns] = jnp.dot(
            normed_ref[...], heads_ref[:, columns], preferred_element_type=jnp.float32
        ).astype(jnp.bfloat16)
    for begin in (0, HD):
        columns = slice(begin, begin + 128)
        turning = joined_ref[own, columns].astype(jnp.float32)
        turned = (
            turning * cosine
            + pltpu.roll(turning, 128 - ROT // 2, 1) * sine_down
            + pltpu.roll(turning, ROT // 2, 1) * sine_up
        )
        joined_ref[own, columns] = turned.astype(jnp.bfloat16)


def hide(normed_ref, upward_ref, hidden_ref, place, chunk=256):
    rows = slice(place, place + normed_ref.shape[0])
    for first in range(0, upward_ref.shape[1], chunk):
        columns = slice(first, first + chunk)
        upward = jnp.dot(
            normed_ref[...], upward_ref[:, columns], preferred_element_type=jnp.float32
        )
        hidden = 0.5 * upward * (1.0 + lax.erf(upward * (0.5**0.5)))
        hidden_ref[rows, columns] = hidden.astype(jnp.bfloat16)


def attend(joined_ref, offsets_ref, first, rows, block_rows):
    tokens = joined_ref.shape[0]
    starts = [
        position_of(ORDER[place // (2 * block_rows)], (place // block_rows) % 2, block_rows)
        for place in range(first, first + rows, block_rows)
    ]
    reach = jnp.concatenate(
        [
            offsets_ref[pl.ds(pl.multiple_of(start, block_rows), block_rows), :]
            for start in starts
        ],
        0,
    )[:, :1].astype(jnp.int32)
    row = positions_along(first, (rows, 1), 0, block_rows)
    column = positions_along(0, (1, tokens), 1, block_rows)
    allowed = (column <= row) & (column >= row - reach)
    scores = lax.dot_general(
        joined_ref[first : first + rows, :HD],
        joined_ref[:, HD : 2 * HD],
        (((1,), (1,)), ((), ())),
        preferred_element_type=jnp.float32,
    ) * (HD ** (-0.5))
    peak = jnp.max(jnp.where(allowed, scores, -jnp.inf), axis=1, keepdims=True)
    weights = jnp.where(allowed, jnp.exp(scores - peak), 0.0)
    weight_sum = jnp.sum(weights, axis=1, keepdims=True)
    mixed = jnp.dot(
        weights.astype(jnp.bfloat16), joined_ref[:, 2 * HD :], preferred_element_type=jnp.float32
    )
    return (mixed / weight_sum).astype(jnp.bfloat16)


def make_tables(segments_ref, offsets_ref, cosine_ref, sine_down_ref, sine_up_ref):
    tokens = segments_ref.shape[1]
    shape = (tokens, tokens)
    rows = lax.broadcasted_iota(jnp.int32, shape, 0)
    columns = lax.broadcasted_iota(jnp.int32, shape, 1)
    across = jnp.broadcast_to(segments_ref[...], shape).astype(jnp.float32)
    down = jnp.sum(jnp.where(rows == columns, across, 0.0), axis=1, keepdims=True)
    earlier = (across == down) & (columns < rows)
    offsets = jnp.sum(jnp.where(earlier, 1.0, 0.0), axis=1, keepdims=True)
    offsets_ref[...] = jnp.broadcast_to(offsets, offsets_ref.shape)
    half = ROT // 2
    lane = lax.broadcasted_iota(jnp.int32, (tokens, 128), 1)
    step = (lane & (half - 1)).astype(jnp.float32)
    frequency = jnp.exp(step * (-2.0 * math.log(rotary_base) / ROT))
    angles = offsets * frequency
    sine = jnp.sin(angles)
    cosine_ref[...] = jnp.where(lane < ROT, jnp.cos(angles), 1.0)
    sine_down_ref[...] = jnp.where(lane < half, -sine, 0.0)
    sine_up_ref[...] = jnp.where((lane >= half) & (lane < ROT), sine, 0.0)


def make_destinations(targets_ref, destinations_ref, replica_count, block_rows):
    page_count = targets_ref.shape[1]
    tokens = destinations_ref.shape[1]
    capacity = 2 * page_count // replica_count
    square = (page_count, page_count)
    rows = lax.broadcasted_iota(jnp.int32, square, 0)
    columns = lax.broadcasted_iota(jnp.int32, square, 1)
    across = jnp.broadcast_to(targets_ref[...], square).astype(jnp.float32)
    down = jnp.sum(jnp.where(rows == columns, across, 0.0), axis=1, keepdims=True)
    earlier = jnp.where((across == down) & (columns < rows), 1.0, 0.0)
    slots = jnp.sum(earlier, axis=1, keepdims=True).astype(jnp.int32)
    slots = (down.astype(jnp.int32) ^ lax.axis_index("dp")) * capacity + slots
    positions = positions_along(0, (1, tokens), 1, block_rows)
    bits = PAGE.bit_length() - 1
    pages = lax.broadcasted_iota(jnp.int32, (page_count, tokens), 0)
    chosen = jnp.where(pages == positions >> bits, slots.astype(jnp.float32), 0.0)
    slot = jnp.sum(chosen, axis=0, keepdims=True).astype(jnp.int32)
    destinations_ref[...] = slot * PAGE + (positions & (PAGE - 1))


def copies_in(sources, targets, sems, tails=False):
    copies = []
    for number, (source, target) in enumerate(zip(sources, targets)):
        parts = 4 if target.shape[0] >= 256 else 1
        rows = target.shape[0] // parts
        skipped = source.shape[0] - target.shape[0] if tails else 0
        copies.append(
            [
                pltpu.make_async_copy(
                    source.at[pl.ds(skipped + part * rows, rows)],
                    target.at[pl.ds(part * rows, rows)],
                    sems.at[number, part],
                )
                for part in range(parts)
            ]
        )
    for copy in sum(copies, []):
        copy.start()
    return copies


def wait_for(copies):
    for copy in copies:
        copy.wait()


def own_kernel(count, replica_count, *refs):
    sources, targets = refs[:count], refs[count : 2 * count]
    offsets_ref, *table_refs, destinations_ref, joined_ref, hidden_ref = refs[2 * count : -3]
    attention_scr, feedforward_scr, sems = refs[-3:]
    copies = copies_in(sources, targets, sems)
    segments_ref, targets_ref, states_ref, *gain_refs, heads_ref, upward_ref, _ = targets
    block_rows = states_ref.shape[0]
    wait_for(copies[0])
    make_tables(segments_ref, offsets_ref, *table_refs)
    wait_for(copies[1])
    make_destinations(targets_ref, destinations_ref, replica_count, block_rows)
    for number in (2, 3, 4):
        wait_for(copies[number])
    normalize([states_ref], gain_refs, [attention_scr, feedforward_scr])
    wait_for(copies[5])
    places = [position_of(0, 0, block_rows)]
    project(attention_scr, heads_ref, table_refs, places, joined_ref, 0)
    wait_for(copies[6])
    hide(feedforward_scr, upward_ref, hidden_ref, 0)
    wait_for(copies[7])


def own_rows(staged, replica_count):
    tokens = staged[0].shape[1]
    rows, width = staged[2].shape
    hidden_width = staged[6].shape[1]
    shapes = [pltpu.VMEM(array.shape, array.dtype) for array in staged[:-1]]
    depth = staged[-1].shape[0] // 2
    shapes += [pltpu.VMEM((depth, width), staged[-1].dtype)]
    shapes += [pltpu.VMEM((tokens, 128), jnp.float32)] * 4
    shapes += [
        pltpu.VMEM((1, tokens), jnp.int32),
        pltpu.VMEM((rows, 3 * HD), jnp.bfloat16),
        pltpu.VMEM((rows, hidden_width), jnp.bfloat16),
    ]
    count = len(staged)
    return pl.pallas_call(
        functools.partial(own_kernel, count, replica_count),
        out_shape=shapes,
        in_specs=[pl.BlockSpec(memory_space=pltpu.HBM)] * count,
        out_specs=vmem_specs(len(shapes)),
        scratch_shapes=[
            pltpu.VMEM((rows, width), jnp.bfloat16),
            pltpu.VMEM((rows, width), jnp.bfloat16),
            pltpu.SemaphoreType.DMA((count, 4)),
        ],
        compiler_params=parameters(12),
        cost_estimate=pl.CostEstimate(
            flops=2 * rows * width * (3 * HD + hidden_width),
            bytes_accessed=sum(array.nbytes for array in staged),
            transcendentals=rows * hidden_width,
        ),
        name="own_rows",
    )(*[in_hbm(array) for array in staged])


def middle_kernel(origins, *refs):
    count = len(origins)
    blocks, (gain_a, gain_f, heads_ref, upward_ref) = refs[:count], refs[count : count + 4]
    table_refs, refs = refs[count + 4 : count + 7], refs[count + 7 :]
    staged = (len(refs) - 5) // 2
    sources, (joined_ref, hidden_ref), refs = refs[:staged], refs[staged:][:2], refs[staged + 2 :]
    targets, (attention_scr, feedforward_scr, sems) = refs[:staged], refs[staged:]
    copies = copies_in(sources, targets, sems, True)
    block_rows = blocks[0].shape[0]
    normalize(blocks, [gain_a, gain_f], [attention_scr, feedforward_scr])
    places = [position_of(kind, half, block_rows) for kind, half in origins]
    project(attention_scr, heads_ref, table_refs, places, joined_ref, 0)
    hide(feedforward_scr, upward_ref, hidden_ref, 0)
    wait_for(sum(copies, []))


def middle_rows(name, origins, blocks, gains, weights, tables, *staged):
    block_rows, width = blocks[0].shape
    rows = len(blocks) * block_rows
    hidden_width = weights[1].shape[1]
    return pl.pallas_call(
        functools.partial(middle_kernel, origins),
        out_shape=[
            pltpu.VMEM((rows, 3 * HD), jnp.bfloat16),
            pltpu.VMEM((rows, hidden_width), jnp.bfloat16),
        ]
        + [pltpu.VMEM((count, array.shape[1]), array.dtype) for count, array in staged],
        in_specs=vmem_specs(len(blocks) + 2 + 2 + 3)
        + [pl.BlockSpec(memory_space=pltpu.HBM)] * len(staged),
        out_specs=vmem_specs(2 + len(staged)),
        scratch_shapes=[
            pltpu.VMEM((rows, width), jnp.bfloat16),
            pltpu.VMEM((rows, width), jnp.bfloat16),
            pltpu.SemaphoreType.DMA((max(len(staged), 1), 4)),
        ],
        compiler_params=parameters(12),
        cost_estimate=pl.CostEstimate(
            flops=2 * rows * width * (3 * HD + hidden_width),
            bytes_accessed=MIB,
            transcendentals=rows * hidden_width,
        ),
        name=name,
    )(*blocks, *gains, *weights, *tables, *[in_hbm(array) for _, array in staged])


def last_kernel(*refs):
    block_ref, *normed_refs = refs[:3]
    gain_a, gain_f, heads_ref, upward_ref, *downward_refs, output_ref = refs[3:10]
    offsets_ref, *table_refs = refs[10:14]
    own_joined_ref, middle_joined_ref, early_ref = refs[14:17]
    joined_ref, fed_ref, sibling_ref, own_ref = refs[17:21]
    attention_scr, feedforward_scr, hidden_scr = refs[21:]
    block_rows = block_ref.shape[0]
    tokens = joined_ref.shape[0]
    first = tokens - attention_scr.shape[0]
    count = normed_refs[0].shape[0]
    normalize([block_ref], [gain_a, gain_f], [attention_scr, feedforward_scr], count)
    for normed_ref, normed_scr in zip(normed_refs, (attention_scr, feedforward_scr)):
        normed_scr[:count, :] = normed_ref[...]
    early = 3 * block_rows
    middle = early + block_rows
    joined_ref[:block_rows, :] = own_joined_ref[...]
    joined_ref[block_rows:early, :] = middle_joined_ref[: 2 * block_rows, :]
    origins = ((3, 1), (1, 1), (2, 0), (2, 1))
    places = [position_of(kind, half, block_rows) for kind, half in origins]
    project(attention_scr, heads_ref, table_refs, places, joined_ref, first)
    joined_ref[early:middle, :] = joined_ref[first : first + block_rows, :]
    joined_ref[middle : middle + block_rows, :] = middle_joined_ref[2 * block_rows :, :]
    rows = CORES * block_rows
    hide(feedforward_scr, upward_ref, hidden_scr, 0)
    attended = attend(joined_ref, offsets_ref, early - block_rows, rows, block_rows)
    chunk = 512
    for begin in range(0, output_ref.shape[1], chunk):
        columns = slice(begin, begin + chunk)
        fed = down(hidden_scr[...], downward_refs, columns)
        fed_ref[:, columns] = fed[block_rows:]
        product = jnp.dot(attended, output_ref[:, columns], preferred_element_type=jnp.float32)
        own_ref[:, columns] = early_ref[early - block_rows : early, columns] + product[:block_rows]
        sibling = fed[:block_rows] + product[block_rows:]
        sibling_ref[:, columns] = sibling.astype(jnp.bfloat16)


def last_rows(block, normed, gains, weights, tables, own_joined, middle_joined, early):
    block_rows, width = block.shape
    rows = normed[0].shape[0] + block_rows
    hidden_width = weights[1].shape[1]
    tokens = CHIPS * CORES * block_rows
    return pl.pallas_call(
        last_kernel,
        out_shape=[
            pltpu.VMEM((tokens, 3 * HD), jnp.bfloat16),
            pltpu.VMEM((rows - block_rows, width), jnp.float32),
            pltpu.VMEM((block_rows, width), jnp.bfloat16),
            pltpu.VMEM((block_rows, width), jnp.float32),
        ],
        in_specs=vmem_specs(1 + 2 + 2 + 5 + 4 + 3),
        out_specs=vmem_specs(4),
        scratch_shapes=[
            pltpu.VMEM((rows, width), jnp.bfloat16),
            pltpu.VMEM((rows, width), jnp.bfloat16),
            pltpu.VMEM((rows, hidden_width), jnp.bfloat16),
        ],
        compiler_params=parameters(12),
        cost_estimate=pl.CostEstimate(
            flops=2 * rows * width * (3 * HD + HD + 2 * hidden_width),
            bytes_accessed=MIB,
            transcendentals=rows * hidden_width,
        ),
        name="last_rows",
    )(block, *normed, *gains, *weights, *tables, own_joined, middle_joined, early)


def down(hidden, downward_refs, columns):
    depth = downward_refs[0].shape[0]
    upper, lower = [
        jnp.dot(
            hidden[:, number * depth : (number + 1) * depth],
            downward_ref[:, columns],
            preferred_element_type=jnp.float32,
        )
        for number, downward_ref in enumerate(downward_refs)
    ]
    return upper + lower


def fed_kernel(own_hidden_ref, middle_hidden_ref, upper_ref, lower_ref, *refs):
    blocks, gain_refs, (fed_ref, *normed_refs) = refs[:-5], refs[-5:-3], refs[-3:]
    normalize(blocks, gain_refs, normed_refs)
    hidden = jnp.concatenate([own_hidden_ref[...], middle_hidden_ref[...]], 0)
    chunk = 512
    for begin in range(0, upper_ref.shape[1], chunk):
        columns = slice(begin, begin + chunk)
        fed_ref[:, columns] = down(hidden, (upper_ref, lower_ref), columns)


def fed_rows(own_hidden, middle_hidden, downward_weights, blocks, gains):
    rows = own_hidden.shape[0] + middle_hidden.shape[0]
    depth, width = own_hidden.shape[1], downward_weights[0].shape[1]
    normed = pltpu.VMEM((len(blocks) * blocks[0].shape[0], width), jnp.bfloat16)
    return pl.pallas_call(
        fed_kernel,
        out_shape=[pltpu.VMEM((rows, width), jnp.float32), normed, normed],
        in_specs=vmem_specs(6 + len(blocks)),
        out_specs=vmem_specs(3),
        compiler_params=parameters(12),
        cost_estimate=pl.CostEstimate(
            flops=2 * rows * depth * width, bytes_accessed=MIB, transcendentals=0
        ),
        name="fed_rows",
    )(own_hidden, middle_hidden, *downward_weights, *blocks, *gains)


def rest_kernel(joined_ref, offsets_ref, output_ref, early_ref, late_ref, *refs):
    near_ref, far_ref, *owns = refs
    block_rows = far_ref.shape[0]
    tokens = joined_ref.shape[0]
    early = CORES * block_rows
    attended = attend(joined_ref, offsets_ref, 0, tokens, block_rows)
    attended = jnp.concatenate([attended[:early], attended[2 * early :]], 0)
    chunk = 512
    for begin in range(0, output_ref.shape[1], chunk):
        columns = slice(begin, begin + chunk)
        fed = jnp.concatenate(
            [
                early_ref[:early, columns],
                early_ref[early + block_rows :, columns],
                late_ref[:, columns],
            ],
            0,
        )
        partial = fed + jnp.dot(
            attended, output_ref[:, columns], preferred_element_type=jnp.float32
        )
        for number, own_ref in enumerate(owns):
            first = CORES * number * block_rows
            middle = first + block_rows
            own_ref[:, columns] = partial[first:middle]
            sibling = partial[middle : middle + block_rows].astype(jnp.bfloat16)
            if number < near_ref.shape[0]:
                near_ref[number, :, columns] = sibling
            else:
                far_ref[:, columns] = sibling


def rest_rows(joined, offsets, output_weight, early, late):
    width = early.shape[1]
    count = CHIPS - 1
    shape = (joined.shape[0] // (CORES * CHIPS), width)
    rows = CORES * count * shape[0]
    shapes = [pltpu.VMEM((count - 1, *shape), jnp.bfloat16), pltpu.VMEM(shape, jnp.bfloat16)]
    shapes += [pltpu.VMEM(shape, jnp.float32)] * count
    return pl.pallas_call(
        rest_kernel,
        out_shape=shapes,
        in_specs=vmem_specs(5),
        out_specs=vmem_specs(2 + count),
        compiler_params=parameters(12),
        cost_estimate=pl.CostEstimate(
            flops=2 * rows * width * HD,
            bytes_accessed=MIB,
            transcendentals=rows * joined.shape[0],
        ),
        name="rest_rows",
    )(joined, offsets, output_weight, early, late)


def pages_kernel(joined_ref, destinations_ref, *page_refs):
    tokens = joined_ref.shape[0]
    slot_rows = page_refs[0].shape[0] * PAGE
    for number, page_ref in enumerate(page_refs):
        shape = (slot_rows, tokens)
        row = number * slot_rows + lax.broadcasted_iota(jnp.int32, shape, 0)
        placing = jnp.where(row == destinations_ref[...], 1.0, 0.0).astype(jnp.bfloat16)
        rows = jnp.dot(placing, joined_ref[:, HD:], preferred_element_type=jnp.float32)
        page_ref[...] = rows.astype(jnp.bfloat16).reshape(page_ref.shape)


def cached_pages(joined, destinations, replica_count):
    tokens = joined.shape[0]
    capacity = 2 * (tokens // PAGE) // replica_count
    shapes = [pltpu.VMEM((capacity, PAGE, 2 * HD), jnp.bfloat16)] * replica_count
    return pl.pallas_call(
        pages_kernel,
        out_shape=shapes,
        in_specs=vmem_specs(2),
        out_specs=vmem_specs(len(shapes)),
        compiler_params=parameters(8),
        cost_estimate=pl.CostEstimate(flops=0, bytes_accessed=MIB, transcendentals=0),
        name="cached_pages",
    )(joined, destinations)


def add_kernel(*refs):
    total = refs[0][...].astype(jnp.float32)
    for ref in refs[1:-1]:
        total = total + ref[...].astype(jnp.float32)
    refs[-1][...] = total.astype(refs[-1].dtype)


def added(name, *parts):
    return pl.pallas_call(
        add_kernel,
        out_shape=pltpu.VMEM(parts[0].shape, jnp.bfloat16),
        in_specs=vmem_specs(len(parts)),
        out_specs=pl.BlockSpec(memory_space=pltpu.VMEM),
        compiler_params=parameters(4),
        name=name,
    )(*parts)


def near_kernel(received_ref, zero_ref, one_ref, hidden_ref, first_ref, base_ref):
    first_ref[...] = (one_ref[...] + received_ref[1].astype(jnp.float32)).astype(jnp.bfloat16)
    zero = zero_ref[...] + received_ref[0].astype(jnp.float32)
    base_ref[...] = zero + hidden_ref[...].astype(jnp.float32)


def near_sums(received, owns, hidden):
    shape = hidden.shape
    return pl.pallas_call(
        near_kernel,
        out_shape=[pltpu.VMEM(shape, jnp.bfloat16), pltpu.VMEM(shape, jnp.float32)],
        in_specs=vmem_specs(4),
        out_specs=vmem_specs(2),
        compiler_params=parameters(4),
        name="near_sums",
    )(received, *owns, hidden)


def place_kernel(masks, *refs):
    group = lax.axis_index("dp")
    count = len(masks)
    pages, (part_ref, base_ref) = refs[:count], refs[count : count + 2]
    cache_ref, total_ref, sems = refs[count + 2 :]
    copies = [
        pltpu.make_async_copy(page_ref, cache_ref.at[0, group ^ mask], sems.at[number])
        for number, (mask, page_ref) in enumerate(zip(masks, pages))
    ]
    for copy in copies:
        copy.start()
    total_ref[...] = base_ref[...] + part_ref[...].astype(jnp.float32)
    for copy in copies:
        copy.wait()


def placed(masks, pages, part, base, replica_count):
    count = len(pages)
    return pl.pallas_call(
        functools.partial(place_kernel, masks),
        out_shape=[
            jax.ShapeDtypeStruct((1, replica_count) + pages[0].shape, pages[0].dtype),
            pltpu.VMEM(base.shape, base.dtype),
        ],
        in_specs=[pl.BlockSpec(memory_space=pl.ANY)] * count + vmem_specs(2),
        out_specs=[pl.BlockSpec(memory_space=pltpu.HBM)] + vmem_specs(1),
        scratch_shapes=[pltpu.SemaphoreType.DMA((count,))],
        compiler_params=parameters(4),
        name="placed",
    )(*pages, part, base)


def finish_kernel(masks, base_ref, *refs):
    count = len(masks)
    *parts, _, output_ref, cache_ref, total_scr, sems = refs
    parts, pages = parts[:-count], parts[-count:]
    group = lax.axis_index("dp")
    copies = [
        pltpu.make_async_copy(page_ref, cache_ref.at[0, group ^ mask], sems.at[number])
        for number, (mask, page_ref) in enumerate(zip(masks, pages))
    ]
    for copy in copies:
        copy.start()
    total = base_ref[...]
    for part_ref in parts:
        total = total + part_ref[...].astype(jnp.float32)
    total_scr[...] = total
    copies.append(pltpu.make_async_copy(total_scr, output_ref, sems.at[count]))
    copies[-1].start()
    for copy in copies:
        copy.wait()


def finished(base, parts, masks, pages, cache):
    count = len(pages)
    return pl.pallas_call(
        functools.partial(finish_kernel, masks),
        out_shape=[
            jax.ShapeDtypeStruct(base.shape, base.dtype),
            jax.ShapeDtypeStruct(cache.shape, cache.dtype),
        ],
        in_specs=vmem_specs(1 + len(parts))
        + [pl.BlockSpec(memory_space=pl.ANY)] * count
        + [pl.BlockSpec(memory_space=pltpu.HBM)],
        out_specs=[pl.BlockSpec(memory_space=pltpu.HBM)] * 2,
        scratch_shapes=[
            pltpu.VMEM(base.shape, base.dtype),
            pltpu.SemaphoreType.DMA((count + 1,)),
        ],
        input_output_aliases={1 + len(parts) + count: 1},
        compiler_params=parameters(4),
        name="finished",
    )(base, *parts, *pages, cache)


def shards_whole_heads(
    hidden_states,
    attention_gain,
    feedforward_gain,
    heads_weight,
    output_weight,
    upward_weight,
    downward_weight,
    segments,
    page_targets,
):
    replica_count = lax.axis_size("dp")
    to_chip = [mask * CORES for mask in range(CHIPS)]
    third = exchanged(hidden_states, "tensor", to_chip[3])
    first = exchanged(hidden_states, "tensor", to_chip[1])
    beside = exchanged(hidden_states, "tensor", 1)
    staged = (
        segments,
        page_targets.reshape(1, -1),
        hidden_states,
        attention_gain[None],
        feedforward_gain[None],
        heads_weight,
        upward_weight,
        downward_weight,
    )
    staged = own_rows(staged, replica_count)
    hidden, gains, weights, tables = staged[2], staged[3:5], staged[5:8], staged[8:12]
    heads, upward, downward = weights
    destinations, own_joined, own_hidden = staged[12:]

    third, own_joined = lax.optimization_barrier((third, own_joined))
    second = exchanged(third, "tensor", to_chip[1])
    middle_joined, middle_hidden, lower, output = middle_rows(
        "middle_rows",
        ((0, 1), (3, 0), (1, 0)),
        (beside, third, first),
        gains,
        (heads, upward),
        tables[1:],
        (downward_weight.shape[0] // 2, downward_weight),
        (output_weight.shape[0], output_weight),
    )
    third, first, middle_joined = lax.optimization_barrier((third, first, middle_joined))
    first_beside = exchanged(first, "tensor", 1)
    third_beside = exchanged(third, "tensor", 1)
    second, first_beside, third_beside, middle_joined, middle_hidden = lax.optimization_barrier(
        (second, first_beside, third_beside, middle_joined, middle_hidden)
    )
    second_beside = exchanged(second, "tensor", 1)
    fed, *normed = fed_rows(
        own_hidden, middle_hidden, (downward, lower), (third_beside, first_beside, second), gains
    )
    joined, fed_late, sibling, own = last_rows(
        second_beside,
        normed,
        gains,
        (heads, upward, downward, lower, output),
        tables,
        own_joined,
        middle_joined,
        fed,
    )

    received = exchanged(sibling, "tensor", 1)
    partials = rest_rows(joined, tables[0], output, fed, fed_late)
    near_sibling, far_sibling, *owns = partials
    near_received = exchanged(near_sibling, "tensor", 1)
    third_sum = added("third_added", own, received)
    third_sum, far_sibling, joined = lax.optimization_barrier((third_sum, far_sibling, joined))
    passing = exchanged(third_sum, "tensor", to_chip[1])
    pages = cached_pages(joined, destinations, replica_count)
    far_sibling, pages = lax.optimization_barrier((far_sibling, pages))
    far_received = exchanged(far_sibling, "tensor", 1)
    early, late = (3,), (2, 1)
    arriving = [exchanged(pages[mask], "dp", mask) for mask in early]
    first_sum, base = near_sums(near_received, owns[:2], hidden)
    from_first = exchanged(first_sum, "tensor", to_chip[1])
    second_sum = added("second_added", owns[2], passing, far_received)
    second_sum, late_pages = lax.optimization_barrier(
        (second_sum, [pages[mask] for mask in late])
    )
    from_second = exchanged(second_sum, "tensor", to_chip[2])
    late_pages = [exchanged(page, "dp", mask) for mask, page in zip(late, late_pages)]
    cache_pages, base = placed((0,) + early, [pages[0]] + arriving, from_first, base, replica_count)
    return tuple(finished(base, (from_second,), late, late_pages, cache_pages))


def solution(mesh):
    whole_heads = mesh.shape["tensor"] == H and mesh.shape["dp"] == 4
    shards = shards_whole_heads if whole_heads else shards_split_heads
    in_specs = (
        P(("dp", "tensor"), None),
        P(),
        P(),
        P(None, "tensor"),
        P("tensor", None),
        P(None, "tensor"),
        P("tensor", None),
        P("dp", None),
        P("dp", None),
    )
    out_specs = (P(("dp", "tensor"), None), P("dp", None, None, None, "tensor"))
    return jax.shard_map(shards, mesh=mesh, in_specs=in_specs, out_specs=out_specs, check_vma=False)
```

```python
import functools
import math

import jax
import jax.numpy as jnp
from jax import lax
from jax.experimental import pallas as pl
from jax.experimental.pallas import tpu as pltpu
from jax.sharding import PartitionSpec as P

H = 8
HD = 256
ROT = 64
PAGE = 16


epsilon = 1e-05
rotary_base = 10000.0
key_block = 256


def shortened(array):

    def short(part):
        return part.astype(jnp.bfloat16) if part.dtype == jnp.float32 else part

    return jax.tree.map(short, array)


def swapped(block, axis, apart):
    count = lax.axis_size(axis)
    route = []
    for low in range(count):
        high = low | 1 << apart
        if high != low and high < count:
            route += [(low, high), (high, low)]
    return lax.ppermute(block, axis, route)


def layer_norm(values, gain):
    floats = values.astype(jnp.float32)
    center = jnp.mean(floats, axis=-1, keepdims=True)
    shifted = floats - center
    spread = jnp.mean(shifted * shifted, axis=-1, keepdims=True)
    return (shifted * lax.rsqrt(spread + epsilon) * gain).astype(jnp.bfloat16)


def positions_of(stream):
    indices = jnp.arange(stream.shape[0], dtype=jnp.int32)
    boundary = jnp.concatenate([jnp.ones((1,), dtype=bool), stream[1:] != stream[:-1]])
    starting = lax.cummax(jnp.where(boundary, indices, jnp.zeros_like(indices)), axis=0)
    return (indices, starting)


def rotate_heads(vectors, offsets, rotary_dims):
    half_dims = rotary_dims // 2
    frequency = jnp.exp(
        jnp.arange(half_dims, dtype=jnp.float32) * (-2.0 * math.log(rotary_base) / rotary_dims)
    )
    angles = offsets.astype(jnp.float32)[:, None] * frequency[None, :]
    cosine = jnp.cos(angles)
    sine = jnp.sin(angles)
    floats = vectors.astype(jnp.float32)
    leading = floats[..., :half_dims]
    trailing = floats[..., half_dims:rotary_dims]
    rotated = jnp.concatenate(
        [
            leading * cosine - trailing * sine,
            trailing * cosine + leading * sine,
            floats[..., rotary_dims:],
        ],
        axis=-1,
    )
    return rotated.astype(jnp.bfloat16)


def shards_split_heads(
    hidden_states,
    attention_gain,
    feedforward_gain,
    heads_weight,
    output_weight,
    upward_weight,
    downward_weight,
    segments,
    page_targets,
):
    tensor_count = lax.axis_size("tensor")
    replica_count = lax.axis_size("dp")
    tensor_index = lax.axis_index("tensor")
    quarters = tensor_count // H
    quarter_width = HD // quarters
    quarter_index = tensor_index % quarters
    stream = segments[0]
    tokens_total = stream.shape[0]
    level_count = quarters.bit_length() - 1
    normed_attention = layer_norm(hidden_states, attention_gain)
    normed_feedforward = layer_norm(hidden_states, feedforward_gain)
    shard_rows = lax.all_gather(
        (normed_attention, normed_feedforward), "tensor", axis=0, tiled=True
    )
    joined_rows = jnp.dot(shard_rows[0], heads_weight, preferred_element_type=jnp.float32).astype(
        jnp.bfloat16
    )
    upward = jnp.dot(shard_rows[1], upward_weight, preferred_element_type=jnp.float32)
    hidden_rows = jax.nn.gelu(upward, approximate=False).astype(jnp.bfloat16)
    hidden = hidden_rows
    pieces = (
        joined_rows.reshape(tokens_total, 3, quarter_width)
        .transpose(1, 0, 2)
        .reshape(1, 3, tokens_total * quarter_width)
    )
    for bit_number in range(level_count):
        partner = swapped(shortened(pieces), "tensor", bit_number).astype(pieces.dtype)
        lower = tensor_index >> bit_number & 1 == 0
        pieces = jnp.where(
            lower, jnp.concatenate([pieces, partner], 0), jnp.concatenate([partner, pieces], 0)
        )
    whole_head = (
        pieces.reshape(quarters, 3, tokens_total, quarter_width)
        .transpose(1, 2, 0, 3)
        .reshape(3, tokens_total, HD)
    )
    indices, starting = positions_of(stream)
    offsets = indices - starting
    queries = rotate_heads(whole_head[0], offsets, ROT)
    keys = rotate_heads(whole_head[1], offsets, ROT)
    values = whole_head[2]
    block_rows = tokens_total // (2 * quarters)
    score_scale = HD ** (-0.5)

    def attend_block(block_number):
        first_row = block_number * block_rows
        block_queries = lax.dynamic_slice_in_dim(queries, first_row, block_rows, 0)
        query_segments = lax.dynamic_slice_in_dim(stream, first_row, block_rows, 0)
        query_indices = first_row + jnp.arange(block_rows, dtype=jnp.int32)
        lowest = lax.dynamic_index_in_dim(starting, first_row, 0, keepdims=False) // key_block
        highest = (first_row + block_rows + key_block - 1) // key_block

        def scores_of(key_number):
            key_first = key_number * key_block
            key_indices = key_first + jnp.arange(key_block, dtype=jnp.int32)
            scores = (
                jnp.dot(block_queries, keys.T, preferred_element_type=jnp.float32) * score_scale
            )
            allowed = (stream[None, :] == query_segments[:, None]) & (
                key_indices[None, :] <= query_indices[:, None]
            )
            return (scores, allowed)

        def find_peak(key_number, peak):
            scores, allowed = scores_of(key_number)
            return jnp.maximum(peak, jnp.max(jnp.where(allowed, scores, -jnp.inf), axis=1))

        peak = lax.fori_loop(
            lowest, highest, find_peak, jnp.full((block_rows,), -jnp.inf, jnp.float32)
        )

        def accumulate(key_number, state):
            weight_sum, mixed_sum = state
            scores, allowed = scores_of(key_number)
            weights = jnp.where(allowed, jnp.exp(scores - peak[:, None]), 0.0)
            mixed_next = mixed_sum + jnp.dot(
                weights.astype(jnp.bfloat16), values, preferred_element_type=jnp.float32
            )
            return (weight_sum + jnp.sum(weights, axis=1), mixed_next)

        start_state = (
            jnp.zeros((block_rows,), jnp.float32),
            jnp.zeros((block_rows, HD), jnp.float32),
        )
        weight_sum, mixed_sum = lax.fori_loop(lowest, highest, accumulate, start_state)
        return (mixed_sum / weight_sum[:, None]).astype(jnp.bfloat16)

    own_blocks = (2 * quarter_index, 2 * quarter_index + 1)
    own_rows = jnp.concatenate([attend_block(own_blocks[0]), attend_block(own_blocks[1])], 0)[None]
    for bit_number in range(level_count):
        partner = swapped(own_rows, "tensor", bit_number)
        lower = tensor_index >> bit_number & 1 == 0
        own_rows = jnp.where(
            lower, jnp.concatenate([own_rows, partner], 0), jnp.concatenate([partner, own_rows], 0)
        )
    attended = own_rows.reshape(tokens_total, HD)
    attended_quarter = lax.dynamic_slice_in_dim(
        attended, quarter_index * quarter_width, quarter_width, 1
    )
    hidden_rows = hidden
    summed = lax.psum_scatter(
        (
            jnp.dot(attended_quarter, output_weight, preferred_element_type=jnp.float32)
            + jnp.dot(hidden_rows, downward_weight, preferred_element_type=jnp.float32)
        ).astype(jnp.bfloat16),
        "tensor",
        scatter_dimension=0,
        tiled=True,
    ).astype(jnp.float32)
    layer_output = hidden_states.astype(jnp.float32) + summed
    key_quarter = lax.dynamic_slice_in_dim(keys, quarter_index * quarter_width, quarter_width, 1)
    value_quarter = joined_rows[:, 2 * quarter_width :]
    page_count = tokens_total // PAGE
    page_rows = jnp.concatenate([key_quarter, value_quarter], 1).reshape(
        page_count, PAGE * 2 * quarter_width
    )
    targets = page_targets[:, 0]
    page_numbers = jnp.arange(page_count, dtype=jnp.int32)
    earlier = jnp.sum(
        (
            (targets[None, :] == targets[:, None]) & (page_numbers[None, :] < page_numbers[:, None])
        ).astype(jnp.int32),
        axis=1,
    )
    capacity = 2 * page_count // replica_count
    slot_numbers = targets * capacity + earlier
    placing = (
        jnp.arange(replica_count * capacity, dtype=jnp.int32)[:, None] == slot_numbers[None, :]
    ).astype(jnp.bfloat16)
    outgoing = jnp.dot(placing, page_rows, preferred_element_type=jnp.float32).astype(jnp.bfloat16)
    outgoing = outgoing.reshape(replica_count, capacity, PAGE * 2 * quarter_width)
    incoming = lax.all_to_all(outgoing, "dp", split_axis=0, concat_axis=0, tiled=True)
    cache_pages = incoming.reshape(1, replica_count, capacity, PAGE, 2 * quarter_width)
    return (layer_output, cache_pages)


CORES = 2
CHIPS = 4
MIB = 1 << 20


def in_hbm(array):
    return pltpu.with_memory_space_constraint(array, pltpu.HBM)


def exchanged(block, axis, mask):
    count = lax.axis_size(axis)
    return lax.ppermute(block, axis, [(member, member ^ mask) for member in range(count)])


def vmem_specs(count):
    return [pl.BlockSpec(memory_space=pltpu.VMEM)] * count


def parameters(mebibytes):
    return pltpu.CompilerParams(vmem_limit_bytes=mebibytes * MIB)


def whereabouts():
    member = lax.axis_index("tensor")
    return member // CORES, member % CORES


ORDER = (0, 3, 1, 2)


def position_of(kind, half, block_rows):
    chip, core = whereabouts()
    return ((chip ^ kind) * CORES + (core ^ half)) * block_rows


def positions_along(first, shape, axis, block_rows):
    chip, core = whereabouts()
    bits = block_rows.bit_length() - 1
    place = first + lax.broadcasted_iota(jnp.int32, shape, axis)
    stand = place >> (bits + 1)
    kind = jnp.where(stand == 1, ORDER[1], jnp.maximum(stand - 1, 0))
    half = (place >> bits) & 1
    return ((((chip ^ kind) << 1) | (core ^ half)) << bits) | (place & (block_rows - 1))


def normalize(blocks, gain_refs, normed_refs, place=0):
    piece = 16
    gains = [gain_ref[...] for gain_ref in gain_refs]
    for number, block_ref in enumerate(blocks):
        block_rows = block_ref.shape[0]
        for part in range(0, block_rows, piece):
            floats = block_ref[part : part + piece, :].astype(jnp.float32)
            center = jnp.mean(floats, axis=-1, keepdims=True)
            shifted = floats - center
            spread = jnp.mean(shifted * shifted, axis=-1, keepdims=True)
            scaled = shifted * lax.rsqrt(spread + epsilon)
            first = place + number * block_rows + part
            for gain, normed_ref in zip(gains, normed_refs):
                normed_ref[first : first + piece, :] = (scaled * gain).astype(jnp.bfloat16)


def project(normed_ref, heads_ref, table_refs, places, joined_ref, first):
    block_rows = normed_ref.shape[0] // (4 if len(places) == 3 else len(places))
    rows = block_rows * len(places)
    own = slice(first, first + rows)
    cosine, sine_down, sine_up = [
        jnp.concatenate(
            [
                table_ref[pl.ds(pl.multiple_of(place, block_rows), block_rows), :]
                for place in places
            ],
            0,
        )
        for table_ref in table_refs
    ]
    for begin in range(0, heads_ref.shape[1], HD):
        columns = slice(begin, begin + HD)
        joined = jnp.dot(
            normed_ref[...], heads_ref[:, columns], preferred_element_type=jnp.float32
        )
        joined_ref[own, columns] = joined[:rows].astype(jnp.bfloat16)
    for begin in (0, HD):
        columns = slice(begin, begin + 128)
        turning = joined_ref[own, columns].astype(jnp.float32)
        turned = (
            turning * cosine
            + pltpu.roll(turning, 128 - ROT // 2, 1) * sine_down
            + pltpu.roll(turning, ROT // 2, 1) * sine_up
        )
        joined_ref[own, columns] = turned.astype(jnp.bfloat16)


def hide(normed_ref, upward_ref, hidden_ref, place, chunk=256):
    count = min(normed_ref.shape[0], hidden_ref.shape[0] - place)
    rows = slice(place, place + count)
    for first in range(0, upward_ref.shape[1], chunk):
        columns = slice(first, first + chunk)
        upward = jnp.dot(
            normed_ref[...], upward_ref[:, columns], preferred_element_type=jnp.float32
        )
        hidden = 0.5 * upward * (1.0 + lax.erf(upward * (0.5**0.5)))
        hidden_ref[rows, columns] = hidden[:count].astype(jnp.bfloat16)


def attend(joined_ref, offsets_ref, first, rows, block_rows):
    tokens = joined_ref.shape[0]
    starts = [
        position_of(ORDER[place // (2 * block_rows)], (place // block_rows) % 2, block_rows)
        for place in range(first, first + rows, block_rows)
    ]
    reach = jnp.concatenate(
        [
            offsets_ref[pl.ds(pl.multiple_of(start, block_rows), block_rows), :]
            for start in starts
        ],
        0,
    )[:, :1].astype(jnp.int32)
    row = positions_along(first, (rows, 1), 0, block_rows)
    column = positions_along(0, (1, tokens), 1, block_rows)
    allowed = (column <= row) & (column >= row - reach)
    scores = lax.dot_general(
        joined_ref[first : first + rows, :HD],
        joined_ref[:, HD : 2 * HD],
        (((1,), (1,)), ((), ())),
        preferred_element_type=jnp.float32,
    ) * (HD ** (-0.5))
    peak = jnp.max(jnp.where(allowed, scores, -jnp.inf), axis=1, keepdims=True)
    weights = jnp.where(allowed, jnp.exp(scores - peak), 0.0)
    weight_sum = jnp.sum(weights, axis=1, keepdims=True)
    mixed = jnp.dot(
        weights.astype(jnp.bfloat16), joined_ref[:, 2 * HD :], preferred_element_type=jnp.float32
    )
    return (mixed / weight_sum).astype(jnp.bfloat16)


def make_tables(segments_ref, offsets_ref, cosine_ref, sine_down_ref, sine_up_ref):
    tokens = segments_ref.shape[1]
    shape = (tokens, tokens)
    rows = lax.broadcasted_iota(jnp.int32, shape, 0)
    columns = lax.broadcasted_iota(jnp.int32, shape, 1)
    across = jnp.broadcast_to(segments_ref[...], shape).astype(jnp.float32)
    down = jnp.sum(jnp.where(rows == columns, across, 0.0), axis=1, keepdims=True)
    earlier = (across == down) & (columns < rows)
    offsets = jnp.sum(jnp.where(earlier, 1.0, 0.0), axis=1, keepdims=True)
    offsets_ref[...] = jnp.broadcast_to(offsets, offsets_ref.shape)
    half = ROT // 2
    lane = lax.broadcasted_iota(jnp.int32, (tokens, 128), 1)
    step = (lane & (half - 1)).astype(jnp.float32)
    frequency = jnp.exp(step * (-2.0 * math.log(rotary_base) / ROT))
    angles = offsets * frequency
    sine = jnp.sin(angles)
    cosine_ref[...] = jnp.where(lane < ROT, jnp.cos(angles), 1.0)
    sine_down_ref[...] = jnp.where(lane < half, -sine, 0.0)
    sine_up_ref[...] = jnp.where((lane >= half) & (lane < ROT), sine, 0.0)


def make_destinations(targets_ref, destinations_ref, replica_count, block_rows):
    page_count = targets_ref.shape[1]
    tokens = destinations_ref.shape[1]
    capacity = 2 * page_count // replica_count
    square = (page_count, page_count)
    rows = lax.broadcasted_iota(jnp.int32, square, 0)
    columns = lax.broadcasted_iota(jnp.int32, square, 1)
    across = jnp.broadcast_to(targets_ref[...], square).astype(jnp.float32)
    down = jnp.sum(jnp.where(rows == columns, across, 0.0), axis=1, keepdims=True)
    earlier = jnp.where((across == down) & (columns < rows), 1.0, 0.0)
    slots = jnp.sum(earlier, axis=1, keepdims=True).astype(jnp.int32)
    slots = (down.astype(jnp.int32) ^ lax.axis_index("dp")) * capacity + slots
    positions = positions_along(0, (1, tokens), 1, block_rows)
    bits = PAGE.bit_length() - 1
    pages = lax.broadcasted_iota(jnp.int32, (page_count, tokens), 0)
    chosen = jnp.where(pages == positions >> bits, slots.astype(jnp.float32), 0.0)
    slot = jnp.sum(chosen, axis=0, keepdims=True).astype(jnp.int32)
    destinations_ref[...] = slot * PAGE + (positions & (PAGE - 1))


def copies_in(sources, targets, sems):
    copies = []
    for number, (source, target) in enumerate(zip(sources, targets)):
        parts = 4 if source.shape[0] >= 256 else 1
        rows = source.shape[0] // parts
        places = [pl.ds(part * rows, rows) for part in range(parts)]
        copies.append(
            [
                pltpu.make_async_copy(source.at[place], target.at[place], sems.at[number, part])
                for part, place in enumerate(places)
            ]
        )
    for copy in sum(copies, []):
        copy.start()
    return copies


def wait_for(copies):
    for copy in copies:
        copy.wait()


def own_kernel(count, replica_count, *refs):
    sources, targets = refs[:count], refs[count : 2 * count]
    offsets_ref, *table_refs, destinations_ref, joined_ref, hidden_ref = refs[2 * count : -3]
    attention_scr, feedforward_scr, sems = refs[-3:]
    copies = copies_in(sources, targets, sems)
    segments_ref, targets_ref, states_ref, *gain_refs, heads_ref, upward_ref, _ = targets
    block_rows = states_ref.shape[0]
    wait_for(copies[0])
    make_tables(segments_ref, offsets_ref, *table_refs)
    wait_for(copies[1])
    make_destinations(targets_ref, destinations_ref, replica_count, block_rows)
    for number in (2, 3, 4):
        wait_for(copies[number])
    normalize([states_ref], gain_refs, [attention_scr, feedforward_scr])
    wait_for(copies[5])
    places = [position_of(0, 0, block_rows)]
    project(attention_scr, heads_ref, table_refs, places, joined_ref, 0)
    wait_for(copies[6])
    hide(feedforward_scr, upward_ref, hidden_ref, 0)
    wait_for(copies[7])


def own_rows(staged, replica_count):
    tokens = staged[0].shape[1]
    rows, width = staged[2].shape
    hidden_width = staged[6].shape[1]
    shapes = [pltpu.VMEM(array.shape, array.dtype) for array in staged]
    shapes += [pltpu.VMEM((tokens, 128), jnp.float32)] * 4
    shapes += [
        pltpu.VMEM((1, tokens), jnp.int32),
        pltpu.VMEM((rows, 3 * HD), jnp.bfloat16),
        pltpu.VMEM((rows, hidden_width), jnp.bfloat16),
    ]
    count = len(staged)
    return pl.pallas_call(
        functools.partial(own_kernel, count, replica_count),
        out_shape=shapes,
        in_specs=[pl.BlockSpec(memory_space=pltpu.HBM)] * count,
        out_specs=vmem_specs(len(shapes)),
        scratch_shapes=[
            pltpu.VMEM((rows, width), jnp.bfloat16),
            pltpu.VMEM((rows, width), jnp.bfloat16),
            pltpu.SemaphoreType.DMA((count, 4)),
        ],
        compiler_params=parameters(12),
        cost_estimate=pl.CostEstimate(
            flops=2 * rows * width * (3 * HD + hidden_width),
            bytes_accessed=sum(array.nbytes for array in staged),
            transcendentals=rows * hidden_width,
        ),
        name="own_rows",
    )(*[in_hbm(array) for array in staged])


def middle_kernel(origins, *refs):
    count = len(origins)
    blocks, (gain_a, gain_f, heads_ref, upward_ref) = refs[:count], refs[count : count + 4]
    table_refs, refs = refs[count + 4 : count + 7], refs[count + 7 :]
    staged = (len(refs) - 5) // 2
    sources, (joined_ref, hidden_ref), refs = refs[:staged], refs[staged:][:2], refs[staged + 2 :]
    targets, (attention_scr, feedforward_scr, sems) = refs[:staged], refs[staged:]
    copies = copies_in(sources, targets, sems)
    block_rows = blocks[0].shape[0]
    normalize(blocks, [gain_a, gain_f], [attention_scr, feedforward_scr])
    for normed_scr in (attention_scr, feedforward_scr):
        normed_scr[count * block_rows :, :] = jnp.zeros((block_rows, normed_scr.shape[1]), jnp.bfloat16)
    places = [position_of(kind, half, block_rows) for kind, half in origins]
    project(attention_scr, heads_ref, table_refs, places, joined_ref, 0)
    hide(feedforward_scr, upward_ref, hidden_ref, 0)
    wait_for(sum(copies, []))


def middle_rows(name, origins, blocks, gains, weights, tables, *staged):
    block_rows, width = blocks[0].shape
    rows = len(blocks) * block_rows
    hidden_width = weights[1].shape[1]
    return pl.pallas_call(
        functools.partial(middle_kernel, origins),
        out_shape=[
            pltpu.VMEM((rows, 3 * HD), jnp.bfloat16),
            pltpu.VMEM((rows, hidden_width), jnp.bfloat16),
        ]
        + [pltpu.VMEM(array.shape, array.dtype) for array in staged],
        in_specs=vmem_specs(len(blocks) + 2 + 2 + 3)
        + [pl.BlockSpec(memory_space=pltpu.HBM)] * len(staged),
        out_specs=vmem_specs(2 + len(staged)),
        scratch_shapes=[
            pltpu.VMEM((rows + block_rows, width), jnp.bfloat16),
            pltpu.VMEM((rows + block_rows, width), jnp.bfloat16),
            pltpu.SemaphoreType.DMA((max(len(staged), 1), 4)),
        ],
        compiler_params=parameters(12),
        cost_estimate=pl.CostEstimate(
            flops=2 * rows * width * (3 * HD + hidden_width),
            bytes_accessed=MIB,
            transcendentals=rows * hidden_width,
        ),
        name=name,
    )(*blocks, *gains, *weights, *tables, *[in_hbm(array) for array in staged])


def last_kernel(*refs):
    block_ref, *normed_refs = refs[:3]
    gain_a, gain_f, heads_ref, upward_ref, downward_ref, output_ref = refs[3:9]
    offsets_ref, *table_refs = refs[9:13]
    own_joined_ref, middle_joined_ref, early_ref = refs[13:16]
    joined_ref, fed_ref, sibling_ref, own_ref = refs[16:20]
    attention_scr, feedforward_scr, hidden_scr = refs[20:]
    block_rows = block_ref.shape[0]
    tokens = joined_ref.shape[0]
    first = tokens - attention_scr.shape[0]
    count = normed_refs[0].shape[0]
    normalize([block_ref], [gain_a, gain_f], [attention_scr, feedforward_scr], count)
    for normed_ref, normed_scr in zip(normed_refs, (attention_scr, feedforward_scr)):
        normed_scr[:count, :] = normed_ref[...]
    early = 3 * block_rows
    middle = early + block_rows
    joined_ref[:block_rows, :] = own_joined_ref[...]
    joined_ref[block_rows:early, :] = middle_joined_ref[: 2 * block_rows, :]
    origins = ((3, 1), (1, 1), (2, 0), (2, 1))
    places = [position_of(kind, half, block_rows) for kind, half in origins]
    project(attention_scr, heads_ref, table_refs, places, joined_ref, first)
    joined_ref[early:middle, :] = joined_ref[first : first + block_rows, :]
    joined_ref[middle : middle + block_rows, :] = middle_joined_ref[2 * block_rows :, :]
    rows = CORES * block_rows
    hide(feedforward_scr, upward_ref, hidden_scr, 0)
    attended = attend(joined_ref, offsets_ref, early - block_rows, rows, block_rows)
    chunk = 512
    for begin in range(0, downward_ref.shape[1], chunk):
        columns = slice(begin, begin + chunk)
        fed = jnp.dot(hidden_scr[...], downward_ref[:, columns], preferred_element_type=jnp.float32)
        fed_ref[:, columns] = fed[block_rows:]
        product = jnp.dot(attended, output_ref[:, columns], preferred_element_type=jnp.float32)
        own_ref[:, columns] = early_ref[early - block_rows : early, columns] + product[:block_rows]
        sibling = fed[:block_rows] + product[block_rows:]
        sibling_ref[:, columns] = sibling.astype(jnp.bfloat16)


def last_rows(block, normed, gains, weights, tables, own_joined, middle_joined, early):
    block_rows, width = block.shape
    rows = normed[0].shape[0] + block_rows
    hidden_width = weights[1].shape[1]
    tokens = CHIPS * CORES * block_rows
    return pl.pallas_call(
        last_kernel,
        out_shape=[
            pltpu.VMEM((tokens, 3 * HD), jnp.bfloat16),
            pltpu.VMEM((rows - block_rows, width), jnp.float32),
            pltpu.VMEM((block_rows, width), jnp.bfloat16),
            pltpu.VMEM((block_rows, width), jnp.float32),
        ],
        in_specs=vmem_specs(1 + 2 + 2 + 4 + 4 + 3),
        out_specs=vmem_specs(4),
        scratch_shapes=[
            pltpu.VMEM((rows, width), jnp.bfloat16),
            pltpu.VMEM((rows, width), jnp.bfloat16),
            pltpu.VMEM((rows, hidden_width), jnp.bfloat16),
        ],
        compiler_params=parameters(12),
        cost_estimate=pl.CostEstimate(
            flops=2 * rows * width * (3 * HD + HD + 2 * hidden_width),
            bytes_accessed=MIB,
            transcendentals=rows * hidden_width,
        ),
        name="last_rows",
    )(block, *normed, *gains, *weights, *tables, own_joined, middle_joined, early)


def fed_kernel(own_hidden_ref, middle_hidden_ref, downward_ref, *refs):
    blocks, gain_refs, (fed_ref, *normed_refs) = refs[:-5], refs[-5:-3], refs[-3:]
    normalize(blocks, gain_refs, normed_refs)
    hidden = jnp.concatenate([own_hidden_ref[...], middle_hidden_ref[...]], 0)
    chunk = 512
    for begin in range(0, downward_ref.shape[1], chunk):
        columns = slice(begin, begin + chunk)
        fed_ref[:, columns] = jnp.dot(
            hidden, downward_ref[:, columns], preferred_element_type=jnp.float32
        )


def fed_rows(own_hidden, middle_hidden, downward_weight, blocks, gains):
    rows = own_hidden.shape[0] + middle_hidden.shape[0]
    depth, width = downward_weight.shape
    normed = pltpu.VMEM((len(blocks) * blocks[0].shape[0], width), jnp.bfloat16)
    return pl.pallas_call(
        fed_kernel,
        out_shape=[pltpu.VMEM((rows, width), jnp.float32), normed, normed],
        in_specs=vmem_specs(5 + len(blocks)),
        out_specs=vmem_specs(3),
        compiler_params=parameters(12),
        cost_estimate=pl.CostEstimate(
            flops=2 * rows * depth * width, bytes_accessed=MIB, transcendentals=0
        ),
        name="fed_rows",
    )(own_hidden, middle_hidden, downward_weight, *blocks, *gains)


def rest_kernel(joined_ref, offsets_ref, output_ref, early_ref, late_ref, *refs):
    near_ref, far_ref, *owns = refs
    block_rows = far_ref.shape[0]
    tokens = joined_ref.shape[0]
    early = CORES * block_rows
    attended = attend(joined_ref, offsets_ref, 0, tokens, block_rows)
    attended = jnp.concatenate([attended[:early], attended[2 * early :]], 0)
    chunk = 512
    for begin in range(0, output_ref.shape[1], chunk):
        columns = slice(begin, begin + chunk)
        fed = jnp.concatenate(
            [
                early_ref[:early, columns],
                early_ref[early + block_rows :, columns],
                late_ref[:, columns],
            ],
            0,
        )
        partial = fed + jnp.dot(
            attended, output_ref[:, columns], preferred_element_type=jnp.float32
        )
        for number, own_ref in enumerate(owns):
            first = CORES * number * block_rows
            middle = first + block_rows
            own_ref[:, columns] = partial[first:middle]
            sibling = partial[middle : middle + block_rows].astype(jnp.bfloat16)
            if number < near_ref.shape[0]:
                near_ref[number, :, columns] = sibling
            else:
                far_ref[:, columns] = sibling


def rest_rows(joined, offsets, output_weight, early, late):
    width = early.shape[1]
    count = CHIPS - 1
    shape = (joined.shape[0] // (CORES * CHIPS), width)
    rows = CORES * count * shape[0]
    shapes = [pltpu.VMEM((count - 1, *shape), jnp.bfloat16), pltpu.VMEM(shape, jnp.bfloat16)]
    shapes += [pltpu.VMEM(shape, jnp.float32)] * count
    return pl.pallas_call(
        rest_kernel,
        out_shape=shapes,
        in_specs=vmem_specs(5),
        out_specs=vmem_specs(2 + count),
        compiler_params=parameters(12),
        cost_estimate=pl.CostEstimate(
            flops=2 * rows * width * HD,
            bytes_accessed=MIB,
            transcendentals=rows * joined.shape[0],
        ),
        name="rest_rows",
    )(joined, offsets, output_weight, early, late)


def pages_kernel(joined_ref, destinations_ref, *page_refs):
    tokens = joined_ref.shape[0]
    slot_rows = page_refs[0].shape[0] * PAGE
    for number, page_ref in enumerate(page_refs):
        shape = (slot_rows, tokens)
        row = number * slot_rows + lax.broadcasted_iota(jnp.int32, shape, 0)
        placing = jnp.where(row == destinations_ref[...], 1.0, 0.0).astype(jnp.bfloat16)
        rows = jnp.dot(placing, joined_ref[:, HD:], preferred_element_type=jnp.float32)
        page_ref[...] = rows.astype(jnp.bfloat16).reshape(page_ref.shape)


def cached_pages(joined, destinations, replica_count):
    tokens = joined.shape[0]
    capacity = 2 * (tokens // PAGE) // replica_count
    shapes = [pltpu.VMEM((capacity, PAGE, 2 * HD), jnp.bfloat16)] * replica_count
    return pl.pallas_call(
        pages_kernel,
        out_shape=shapes,
        in_specs=vmem_specs(2),
        out_specs=vmem_specs(len(shapes)),
        compiler_params=parameters(8),
        cost_estimate=pl.CostEstimate(flops=0, bytes_accessed=MIB, transcendentals=0),
        name="cached_pages",
    )(joined, destinations)


def add_kernel(*refs):
    total = refs[0][...].astype(jnp.float32)
    for ref in refs[1:-1]:
        total = total + ref[...].astype(jnp.float32)
    refs[-1][...] = total.astype(refs[-1].dtype)


def added(name, *parts):
    return pl.pallas_call(
        add_kernel,
        out_shape=pltpu.VMEM(parts[0].shape, jnp.bfloat16),
        in_specs=vmem_specs(len(parts)),
        out_specs=pl.BlockSpec(memory_space=pltpu.VMEM),
        compiler_params=parameters(4),
        name=name,
    )(*parts)


def near_kernel(received_ref, zero_ref, one_ref, hidden_ref, first_ref, base_ref):
    first_ref[...] = (one_ref[...] + received_ref[1].astype(jnp.float32)).astype(jnp.bfloat16)
    zero = zero_ref[...] + received_ref[0].astype(jnp.float32)
    base_ref[...] = zero + hidden_ref[...].astype(jnp.float32)


def near_sums(received, owns, hidden):
    shape = hidden.shape
    return pl.pallas_call(
        near_kernel,
        out_shape=[pltpu.VMEM(shape, jnp.bfloat16), pltpu.VMEM(shape, jnp.float32)],
        in_specs=vmem_specs(4),
        out_specs=vmem_specs(2),
        compiler_params=parameters(4),
        name="near_sums",
    )(received, *owns, hidden)


def place_kernel(masks, *refs):
    group = lax.axis_index("dp")
    count = len(masks)
    pages, (part_ref, base_ref) = refs[:count], refs[count : count + 2]
    cache_ref, total_ref, sems = refs[count + 2 :]
    copies = [
        pltpu.make_async_copy(page_ref, cache_ref.at[0, group ^ mask], sems.at[number])
        for number, (mask, page_ref) in enumerate(zip(masks, pages))
    ]
    for copy in copies:
        copy.start()
    total_ref[...] = base_ref[...] + part_ref[...].astype(jnp.float32)
    for copy in copies:
        copy.wait()


def placed(masks, pages, part, base, replica_count):
    count = len(pages)
    return pl.pallas_call(
        functools.partial(place_kernel, masks),
        out_shape=[
            jax.ShapeDtypeStruct((1, replica_count) + pages[0].shape, pages[0].dtype),
            pltpu.VMEM(base.shape, base.dtype),
        ],
        in_specs=[pl.BlockSpec(memory_space=pl.ANY)] * count + vmem_specs(2),
        out_specs=[pl.BlockSpec(memory_space=pltpu.HBM)] + vmem_specs(1),
        scratch_shapes=[pltpu.SemaphoreType.DMA((count,))],
        compiler_params=parameters(4),
        name="placed",
    )(*pages, part, base)


def finish_kernel(masks, base_ref, *refs):
    count = len(masks)
    *parts, _, output_ref, cache_ref, total_scr, sems = refs
    parts, pages = parts[:-count], parts[-count:]
    group = lax.axis_index("dp")
    copies = [
        pltpu.make_async_copy(page_ref, cache_ref.at[0, group ^ mask], sems.at[number])
        for number, (mask, page_ref) in enumerate(zip(masks, pages))
    ]
    for copy in copies:
        copy.start()
    total = base_ref[...]
    for part_ref in parts:
        total = total + part_ref[...].astype(jnp.float32)
    total_scr[...] = total
    copies.append(pltpu.make_async_copy(total_scr, output_ref, sems.at[count]))
    copies[-1].start()
    for copy in copies:
        copy.wait()


def finished(base, parts, masks, pages, cache):
    count = len(pages)
    return pl.pallas_call(
        functools.partial(finish_kernel, masks),
        out_shape=[
            jax.ShapeDtypeStruct(base.shape, base.dtype),
            jax.ShapeDtypeStruct(cache.shape, cache.dtype),
        ],
        in_specs=vmem_specs(1 + len(parts))
        + [pl.BlockSpec(memory_space=pl.ANY)] * count
        + [pl.BlockSpec(memory_space=pltpu.HBM)],
        out_specs=[pl.BlockSpec(memory_space=pltpu.HBM)] * 2,
        scratch_shapes=[
            pltpu.VMEM(base.shape, base.dtype),
            pltpu.SemaphoreType.DMA((count + 1,)),
        ],
        input_output_aliases={1 + len(parts) + count: 1},
        compiler_params=parameters(4),
        name="finished",
    )(base, *parts, *pages, cache)


def shards_whole_heads(
    hidden_states,
    attention_gain,
    feedforward_gain,
    heads_weight,
    output_weight,
    upward_weight,
    downward_weight,
    segments,
    page_targets,
):
    replica_count = lax.axis_size("dp")
    to_chip = [mask * CORES for mask in range(CHIPS)]
    third = exchanged(hidden_states, "tensor", to_chip[3])
    first = exchanged(hidden_states, "tensor", to_chip[1])
    beside = exchanged(hidden_states, "tensor", 1)
    staged = (
        segments,
        page_targets.reshape(1, -1),
        hidden_states,
        attention_gain[None],
        feedforward_gain[None],
        heads_weight,
        upward_weight,
        downward_weight,
    )
    staged = own_rows(staged, replica_count)
    hidden, gains, weights, tables = staged[2], staged[3:5], staged[5:8], staged[8:12]
    heads, upward, downward = weights
    destinations, own_joined, own_hidden = staged[12:]

    third, own_joined = lax.optimization_barrier((third, own_joined))
    second = exchanged(third, "tensor", to_chip[1])
    middle_joined, middle_hidden, output = middle_rows(
        "middle_rows",
        ((0, 1), (3, 0), (1, 0)),
        (beside, third, first),
        gains,
        (heads, upward),
        tables[1:],
        output_weight,
    )
    third, first, middle_joined = lax.optimization_barrier((third, first, middle_joined))
    first_beside = exchanged(first, "tensor", 1)
    third_beside = exchanged(third, "tensor", 1)
    second, first_beside, third_beside, middle_joined, middle_hidden = lax.optimization_barrier(
        (second, first_beside, third_beside, middle_joined, middle_hidden)
    )
    second_beside = exchanged(second, "tensor", 1)
    fed, *normed = fed_rows(
        own_hidden, middle_hidden, downward, (third_beside, first_beside, second), gains
    )
    joined, fed_late, sibling, own = last_rows(
        second_beside,
        normed,
        gains,
        (heads, upward, downward, output),
        tables,
        own_joined,
        middle_joined,
        fed,
    )

    received = exchanged(sibling, "tensor", 1)
    partials = rest_rows(joined, tables[0], output, fed, fed_late)
    near_sibling, far_sibling, *owns = partials
    near_received = exchanged(near_sibling, "tensor", 1)
    third_sum = added("third_added", own, received)
    third_sum, far_sibling, joined = lax.optimization_barrier((third_sum, far_sibling, joined))
    passing = exchanged(third_sum, "tensor", to_chip[1])
    pages = cached_pages(joined, destinations, replica_count)
    far_sibling, pages = lax.optimization_barrier((far_sibling, pages))
    far_received = exchanged(far_sibling, "tensor", 1)
    early, late = (3,), (2, 1)
    arriving = [exchanged(pages[mask], "dp", mask) for mask in early]
    first_sum, base = near_sums(near_received, owns[:2], hidden)
    from_first = exchanged(first_sum, "tensor", to_chip[1])
    second_sum = added("second_added", owns[2], passing, far_received)
    second_sum, late_pages = lax.optimization_barrier(
        (second_sum, [pages[mask] for mask in late])
    )
    from_second = exchanged(second_sum, "tensor", to_chip[2])
    late_pages = [exchanged(page, "dp", mask) for mask, page in zip(late, late_pages)]
    cache_pages, base = placed((0,) + early, [pages[0]] + arriving, from_first, base, replica_count)
    return tuple(finished(base, (from_second,), late, late_pages, cache_pages))


def solution(mesh):
    whole_heads = mesh.shape["tensor"] == H and mesh.shape["dp"] == 4
    shards = shards_whole_heads if whole_heads else shards_split_heads
    in_specs = (
        P(("dp", "tensor"), None),
        P(),
        P(),
        P(None, "tensor"),
        P("tensor", None),
        P(None, "tensor"),
        P("tensor", None),
        P("dp", None),
        P("dp", None),
    )
    out_specs = (P(("dp", "tensor"), None), P("dp", None, None, None, "tensor"))
    return jax.shard_map(shards, mesh=mesh, in_specs=in_specs, out_specs=out_specs, check_vma=False)
```

```python
import functools
import math

import jax
import jax.numpy as jnp
from jax import lax
from jax.experimental import pallas as pl
from jax.experimental.pallas import tpu as pltpu
from jax.sharding import PartitionSpec as P

H = 8
HD = 256
ROT = 64
PAGE = 16


epsilon = 1e-05
rotary_base = 10000.0
key_block = 256


def shortened(array):

    def short(part):
        return part.astype(jnp.bfloat16) if part.dtype == jnp.float32 else part

    return jax.tree.map(short, array)


def swapped(block, axis, apart):
    count = lax.axis_size(axis)
    route = []
    for low in range(count):
        high = low | 1 << apart
        if high != low and high < count:
            route += [(low, high), (high, low)]
    return lax.ppermute(block, axis, route)


def layer_norm(values, gain):
    floats = values.astype(jnp.float32)
    center = jnp.mean(floats, axis=-1, keepdims=True)
    shifted = floats - center
    spread = jnp.mean(shifted * shifted, axis=-1, keepdims=True)
    return (shifted * lax.rsqrt(spread + epsilon) * gain).astype(jnp.bfloat16)


def positions_of(stream):
    indices = jnp.arange(stream.shape[0], dtype=jnp.int32)
    boundary = jnp.concatenate([jnp.ones((1,), dtype=bool), stream[1:] != stream[:-1]])
    starting = lax.cummax(jnp.where(boundary, indices, jnp.zeros_like(indices)), axis=0)
    return (indices, starting)


def rotate_heads(vectors, offsets, rotary_dims):
    half_dims = rotary_dims // 2
    frequency = jnp.exp(
        jnp.arange(half_dims, dtype=jnp.float32) * (-2.0 * math.log(rotary_base) / rotary_dims)
    )
    angles = offsets.astype(jnp.float32)[:, None] * frequency[None, :]
    cosine = jnp.cos(angles)
    sine = jnp.sin(angles)
    floats = vectors.astype(jnp.float32)
    leading = floats[..., :half_dims]
    trailing = floats[..., half_dims:rotary_dims]
    rotated = jnp.concatenate(
        [
            leading * cosine - trailing * sine,
            trailing * cosine + leading * sine,
            floats[..., rotary_dims:],
        ],
        axis=-1,
    )
    return rotated.astype(jnp.bfloat16)


def shards_split_heads(
    hidden_states,
    attention_gain,
    feedforward_gain,
    heads_weight,
    output_weight,
    upward_weight,
    downward_weight,
    segments,
    page_targets,
):
    tensor_count = lax.axis_size("tensor")
    replica_count = lax.axis_size("dp")
    tensor_index = lax.axis_index("tensor")
    quarters = tensor_count // H
    quarter_width = HD // quarters
    quarter_index = tensor_index % quarters
    stream = segments[0]
    tokens_total = stream.shape[0]
    level_count = quarters.bit_length() - 1
    normed_attention = layer_norm(hidden_states, attention_gain)
    normed_feedforward = layer_norm(hidden_states, feedforward_gain)
    shard_rows = lax.all_gather(
        (normed_attention, normed_feedforward), "tensor", axis=0, tiled=True
    )
    joined_rows = jnp.dot(shard_rows[0], heads_weight, preferred_element_type=jnp.float32).astype(
        jnp.bfloat16
    )
    upward = jnp.dot(shard_rows[1], upward_weight, preferred_element_type=jnp.float32)
    hidden_rows = jax.nn.gelu(upward, approximate=False).astype(jnp.bfloat16)
    hidden = hidden_rows
    pieces = (
        joined_rows.reshape(tokens_total, 3, quarter_width)
        .transpose(1, 0, 2)
        .reshape(1, 3, tokens_total * quarter_width)
    )
    for bit_number in range(level_count):
        partner = swapped(shortened(pieces), "tensor", bit_number).astype(pieces.dtype)
        lower = tensor_index >> bit_number & 1 == 0
        pieces = jnp.where(
            lower, jnp.concatenate([pieces, partner], 0), jnp.concatenate([partner, pieces], 0)
        )
    whole_head = (
        pieces.reshape(quarters, 3, tokens_total, quarter_width)
        .transpose(1, 2, 0, 3)
        .reshape(3, tokens_total, HD)
    )
    indices, starting = positions_of(stream)
    offsets = indices - starting
    queries = rotate_heads(whole_head[0], offsets, ROT)
    keys = rotate_heads(whole_head[1], offsets, ROT)
    values = whole_head[2]
    block_rows = tokens_total // (2 * quarters)
    score_scale = HD ** (-0.5)

    def attend_block(block_number):
        first_row = block_number * block_rows
        block_queries = lax.dynamic_slice_in_dim(queries, first_row, block_rows, 0)
        query_segments = lax.dynamic_slice_in_dim(stream, first_row, block_rows, 0)
        query_indices = first_row + jnp.arange(block_rows, dtype=jnp.int32)
        lowest = lax.dynamic_index_in_dim(starting, first_row, 0, keepdims=False) // key_block
        highest = (first_row + block_rows + key_block - 1) // key_block

        def scores_of(key_number):
            key_first = key_number * key_block
            key_indices = key_first + jnp.arange(key_block, dtype=jnp.int32)
            scores = (
                jnp.dot(block_queries, keys.T, preferred_element_type=jnp.float32) * score_scale
            )
            allowed = (stream[None, :] == query_segments[:, None]) & (
                key_indices[None, :] <= query_indices[:, None]
            )
            return (scores, allowed)

        def find_peak(key_number, peak):
            scores, allowed = scores_of(key_number)
            return jnp.maximum(peak, jnp.max(jnp.where(allowed, scores, -jnp.inf), axis=1))

        peak = lax.fori_loop(
            lowest, highest, find_peak, jnp.full((block_rows,), -jnp.inf, jnp.float32)
        )

        def accumulate(key_number, state):
            weight_sum, mixed_sum = state
            scores, allowed = scores_of(key_number)
            weights = jnp.where(allowed, jnp.exp(scores - peak[:, None]), 0.0)
            mixed_next = mixed_sum + jnp.dot(
                weights.astype(jnp.bfloat16), values, preferred_element_type=jnp.float32
            )
            return (weight_sum + jnp.sum(weights, axis=1), mixed_next)

        start_state = (
            jnp.zeros((block_rows,), jnp.float32),
            jnp.zeros((block_rows, HD), jnp.float32),
        )
        weight_sum, mixed_sum = lax.fori_loop(lowest, highest, accumulate, start_state)
        return (mixed_sum / weight_sum[:, None]).astype(jnp.bfloat16)

    own_blocks = (2 * quarter_index, 2 * quarter_index + 1)
    own_rows = jnp.concatenate([attend_block(own_blocks[0]), attend_block(own_blocks[1])], 0)[None]
    for bit_number in range(level_count):
        partner = swapped(own_rows, "tensor", bit_number)
        lower = tensor_index >> bit_number & 1 == 0
        own_rows = jnp.where(
            lower, jnp.concatenate([own_rows, partner], 0), jnp.concatenate([partner, own_rows], 0)
        )
    attended = own_rows.reshape(tokens_total, HD)
    attended_quarter = lax.dynamic_slice_in_dim(
        attended, quarter_index * quarter_width, quarter_width, 1
    )
    hidden_rows = hidden
    summed = lax.psum_scatter(
        (
            jnp.dot(attended_quarter, output_weight, preferred_element_type=jnp.float32)
            + jnp.dot(hidden_rows, downward_weight, preferred_element_type=jnp.float32)
        ).astype(jnp.bfloat16),
        "tensor",
        scatter_dimension=0,
        tiled=True,
    ).astype(jnp.float32)
    layer_output = hidden_states.astype(jnp.float32) + summed
    key_quarter = lax.dynamic_slice_in_dim(keys, quarter_index * quarter_width, quarter_width, 1)
    value_quarter = joined_rows[:, 2 * quarter_width :]
    page_count = tokens_total // PAGE
    page_rows = jnp.concatenate([key_quarter, value_quarter], 1).reshape(
        page_count, PAGE * 2 * quarter_width
    )
    targets = page_targets[:, 0]
    page_numbers = jnp.arange(page_count, dtype=jnp.int32)
    earlier = jnp.sum(
        (
            (targets[None, :] == targets[:, None]) & (page_numbers[None, :] < page_numbers[:, None])
        ).astype(jnp.int32),
        axis=1,
    )
    capacity = 2 * page_count // replica_count
    slot_numbers = targets * capacity + earlier
    placing = (
        jnp.arange(replica_count * capacity, dtype=jnp.int32)[:, None] == slot_numbers[None, :]
    ).astype(jnp.bfloat16)
    outgoing = jnp.dot(placing, page_rows, preferred_element_type=jnp.float32).astype(jnp.bfloat16)
    outgoing = outgoing.reshape(replica_count, capacity, PAGE * 2 * quarter_width)
    incoming = lax.all_to_all(outgoing, "dp", split_axis=0, concat_axis=0, tiled=True)
    cache_pages = incoming.reshape(1, replica_count, capacity, PAGE, 2 * quarter_width)
    return (layer_output, cache_pages)


CORES = 2
CHIPS = 4
MIB = 1 << 20


def in_hbm(array):
    return pltpu.with_memory_space_constraint(array, pltpu.HBM)


def exchanged(block, axis, mask):
    count = lax.axis_size(axis)
    return lax.ppermute(block, axis, [(member, member ^ mask) for member in range(count)])


def vmem_specs(count):
    return [pl.BlockSpec(memory_space=pltpu.VMEM)] * count


def parameters(mebibytes):
    return pltpu.CompilerParams(vmem_limit_bytes=mebibytes * MIB)


def whereabouts():
    member = lax.axis_index("tensor")
    return member // CORES, member % CORES


ORDER = (0, 3, 1, 2)


def position_of(kind, half, block_rows):
    chip, core = whereabouts()
    return ((chip ^ kind) * CORES + (core ^ half)) * block_rows


def positions_along(first, shape, axis, block_rows):
    chip, core = whereabouts()
    bits = block_rows.bit_length() - 1
    place = first + lax.broadcasted_iota(jnp.int32, shape, axis)
    stand = place >> (bits + 1)
    kind = jnp.where(stand == 1, ORDER[1], jnp.maximum(stand - 1, 0))
    half = (place >> bits) & 1
    return ((((chip ^ kind) << 1) | (core ^ half)) << bits) | (place & (block_rows - 1))


def normalize(blocks, gain_refs, normed_refs, place=0):
    piece = 16
    gains = [gain_ref[...] for gain_ref in gain_refs]
    for number, block_ref in enumerate(blocks):
        block_rows = block_ref.shape[0]
        for part in range(0, block_rows, piece):
            floats = block_ref[part : part + piece, :].astype(jnp.float32)
            center = jnp.mean(floats, axis=-1, keepdims=True)
            shifted = floats - center
            spread = jnp.mean(shifted * shifted, axis=-1, keepdims=True)
            scaled = shifted * lax.rsqrt(spread + epsilon)
            first = place + number * block_rows + part
            for gain, normed_ref in zip(gains, normed_refs):
                normed_ref[first : first + piece, :] = (scaled * gain).astype(jnp.bfloat16)


def project(normed_ref, heads_ref, table_refs, places, joined_ref, first):
    block_rows = normed_ref.shape[0] // (4 if len(places) == 3 else len(places))
    rows = block_rows * len(places)
    own = slice(first, first + rows)
    cosine, sine_down, sine_up = [
        jnp.concatenate(
            [
                table_ref[pl.ds(pl.multiple_of(place, block_rows), block_rows), :]
                for place in places
            ],
            0,
        )
        for table_ref in table_refs
    ]
    for begin in range(0, heads_ref.shape[1], HD):
        columns = slice(begin, begin + HD)
        joined = jnp.dot(
            normed_ref[...], heads_ref[:, columns], preferred_element_type=jnp.float32
        )
        joined_ref[own, columns] = joined[:rows].astype(jnp.bfloat16)
    for begin in (0, HD):
        columns = slice(begin, begin + 128)
        turning = joined_ref[own, columns].astype(jnp.float32)
        turned = (
            turning * cosine
            + pltpu.roll(turning, 128 - ROT // 2, 1) * sine_down
            + pltpu.roll(turning, ROT // 2, 1) * sine_up
        )
        joined_ref[own, columns] = turned.astype(jnp.bfloat16)


def hide(normed_ref, upward_ref, hidden_ref, place, chunk=256):
    count = min(normed_ref.shape[0], hidden_ref.shape[0] - place)
    rows = slice(place, place + count)
    for first in range(0, upward_ref.shape[1], chunk):
        columns = slice(first, first + chunk)
        upward = jnp.dot(
            normed_ref[...], upward_ref[:, columns], preferred_element_type=jnp.float32
        )
        hidden = 0.5 * upward * (1.0 + lax.erf(upward * (0.5**0.5)))
        hidden_ref[rows, columns] = hidden[:count].astype(jnp.bfloat16)


def attend(joined_ref, offsets_ref, first, rows, block_rows):
    tokens = joined_ref.shape[0]
    starts = [
        position_of(ORDER[place // (2 * block_rows)], (place // block_rows) % 2, block_rows)
        for place in range(first, first + rows, block_rows)
    ]
    reach = jnp.concatenate(
        [
            offsets_ref[pl.ds(pl.multiple_of(start, block_rows), block_rows), :]
            for start in starts
        ],
        0,
    )[:, :1].astype(jnp.int32)
    row = positions_along(first, (rows, 1), 0, block_rows)
    column = positions_along(0, (1, tokens), 1, block_rows)
    allowed = (column <= row) & (column >= row - reach)
    scores = lax.dot_general(
        joined_ref[first : first + rows, :HD],
        joined_ref[:, HD : 2 * HD],
        (((1,), (1,)), ((), ())),
        preferred_element_type=jnp.float32,
    ) * (HD ** (-0.5))
    peak = jnp.max(jnp.where(allowed, scores, -jnp.inf), axis=1, keepdims=True)
    weights = jnp.where(allowed, jnp.exp(scores - peak), 0.0)
    weight_sum = jnp.sum(weights, axis=1, keepdims=True)
    mixed = jnp.dot(
        weights.astype(jnp.bfloat16), joined_ref[:, 2 * HD :], preferred_element_type=jnp.float32
    )
    return (mixed / weight_sum).astype(jnp.bfloat16)


def make_tables(segments_ref, offsets_ref, cosine_ref, sine_down_ref, sine_up_ref):
    tokens = segments_ref.shape[1]
    shape = (tokens, tokens)
    rows = lax.broadcasted_iota(jnp.int32, shape, 0)
    columns = lax.broadcasted_iota(jnp.int32, shape, 1)
    across = jnp.broadcast_to(segments_ref[...], shape).astype(jnp.float32)
    down = jnp.sum(jnp.where(rows == columns, across, 0.0), axis=1, keepdims=True)
    earlier = (across == down) & (columns < rows)
    offsets = jnp.sum(jnp.where(earlier, 1.0, 0.0), axis=1, keepdims=True)
    offsets_ref[...] = jnp.broadcast_to(offsets, offsets_ref.shape)
    half = ROT // 2
    lane = lax.broadcasted_iota(jnp.int32, (tokens, 128), 1)
    step = (lane & (half - 1)).astype(jnp.float32)
    frequency = jnp.exp(step * (-2.0 * math.log(rotary_base) / ROT))
    angles = offsets * frequency
    sine = jnp.sin(angles)
    cosine_ref[...] = jnp.where(lane < ROT, jnp.cos(angles), 1.0)
    sine_down_ref[...] = jnp.where(lane < half, -sine, 0.0)
    sine_up_ref[...] = jnp.where((lane >= half) & (lane < ROT), sine, 0.0)


def make_destinations(targets_ref, destinations_ref, replica_count, block_rows):
    page_count = targets_ref.shape[1]
    tokens = destinations_ref.shape[1]
    capacity = 2 * page_count // replica_count
    square = (page_count, page_count)
    rows = lax.broadcasted_iota(jnp.int32, square, 0)
    columns = lax.broadcasted_iota(jnp.int32, square, 1)
    across = jnp.broadcast_to(targets_ref[...], square).astype(jnp.float32)
    down = jnp.sum(jnp.where(rows == columns, across, 0.0), axis=1, keepdims=True)
    earlier = jnp.where((across == down) & (columns < rows), 1.0, 0.0)
    slots = jnp.sum(earlier, axis=1, keepdims=True).astype(jnp.int32)
    slots = (down.astype(jnp.int32) ^ lax.axis_index("dp")) * capacity + slots
    positions = positions_along(0, (1, tokens), 1, block_rows)
    bits = PAGE.bit_length() - 1
    pages = lax.broadcasted_iota(jnp.int32, (page_count, tokens), 0)
    chosen = jnp.where(pages == positions >> bits, slots.astype(jnp.float32), 0.0)
    slot = jnp.sum(chosen, axis=0, keepdims=True).astype(jnp.int32)
    destinations_ref[...] = slot * PAGE + (positions & (PAGE - 1))


def copies_in(sources, targets, sems):
    copies = []
    for number, (source, target) in enumerate(zip(sources, targets)):
        parts = 4 if source.shape[0] >= 256 else 1
        rows = source.shape[0] // parts
        places = [pl.ds(part * rows, rows) for part in range(parts)]
        copies.append(
            [
                pltpu.make_async_copy(source.at[place], target.at[place], sems.at[number, part])
                for part, place in enumerate(places)
            ]
        )
    for copy in sum(copies, []):
        copy.start()
    return copies


def wait_for(copies):
    for copy in copies:
        copy.wait()


def own_kernel(count, replica_count, *refs):
    sources, targets = refs[:count], refs[count : 2 * count]
    offsets_ref, *table_refs, destinations_ref, joined_ref, hidden_ref = refs[2 * count : -3]
    attention_scr, feedforward_scr, sems = refs[-3:]
    copies = copies_in(sources, targets, sems)
    segments_ref, targets_ref, states_ref, *gain_refs, heads_ref, upward_ref, _ = targets
    block_rows = states_ref.shape[0]
    wait_for(copies[0])
    make_tables(segments_ref, offsets_ref, *table_refs)
    wait_for(copies[1])
    make_destinations(targets_ref, destinations_ref, replica_count, block_rows)
    for number in (2, 3, 4):
        wait_for(copies[number])
    normalize([states_ref], gain_refs, [attention_scr, feedforward_scr])
    wait_for(copies[5])
    places = [position_of(0, 0, block_rows)]
    project(attention_scr, heads_ref, table_refs, places, joined_ref, 0)
    wait_for(copies[6])
    hide(feedforward_scr, upward_ref, hidden_ref, 0)
    wait_for(copies[7])


def own_rows(staged, replica_count):
    tokens = staged[0].shape[1]
    rows, width = staged[2].shape
    hidden_width = staged[6].shape[1]
    shapes = [pltpu.VMEM(array.shape, array.dtype) for array in staged]
    shapes += [pltpu.VMEM((tokens, 128), jnp.float32)] * 4
    shapes += [
        pltpu.VMEM((1, tokens), jnp.int32),
        pltpu.VMEM((rows, 3 * HD), jnp.bfloat16),
        pltpu.VMEM((rows, hidden_width), jnp.bfloat16),
    ]
    count = len(staged)
    return pl.pallas_call(
        functools.partial(own_kernel, count, replica_count),
        out_shape=shapes,
        in_specs=[pl.BlockSpec(memory_space=pltpu.HBM)] * count,
        out_specs=vmem_specs(len(shapes)),
        scratch_shapes=[
            pltpu.VMEM((rows, width), jnp.bfloat16),
            pltpu.VMEM((rows, width), jnp.bfloat16),
            pltpu.SemaphoreType.DMA((count, 4)),
        ],
        compiler_params=parameters(12),
        cost_estimate=pl.CostEstimate(
            flops=2 * rows * width * (3 * HD + hidden_width),
            bytes_accessed=sum(array.nbytes for array in staged),
            transcendentals=rows * hidden_width,
        ),
        name="own_rows",
    )(*[in_hbm(array) for array in staged])


def middle_kernel(origins, *refs):
    count = len(origins)
    blocks, (gain_a, gain_f, heads_ref, upward_ref) = refs[:count], refs[count : count + 4]
    table_refs, refs = refs[count + 4 : count + 7], refs[count + 7 :]
    staged = (len(refs) - 5) // 2
    sources, (joined_ref, hidden_ref), refs = refs[:staged], refs[staged:][:2], refs[staged + 2 :]
    targets, (attention_scr, feedforward_scr, sems) = refs[:staged], refs[staged:]
    copies = copies_in(sources, targets, sems)
    block_rows = blocks[0].shape[0]
    normalize(blocks, [gain_a, gain_f], [attention_scr, feedforward_scr])
    for normed_scr in (attention_scr, feedforward_scr):
        normed_scr[count * block_rows :, :] = jnp.zeros((block_rows, normed_scr.shape[1]), jnp.bfloat16)
    places = [position_of(kind, half, block_rows) for kind, half in origins]
    project(attention_scr, heads_ref, table_refs, places, joined_ref, 0)
    hide(feedforward_scr, upward_ref, hidden_ref, 0)
    wait_for(sum(copies, []))


def middle_rows(name, origins, blocks, gains, weights, tables, *staged):
    block_rows, width = blocks[0].shape
    rows = len(blocks) * block_rows
    hidden_width = weights[1].shape[1]
    return pl.pallas_call(
        functools.partial(middle_kernel, origins),
        out_shape=[
            pltpu.VMEM((rows, 3 * HD), jnp.bfloat16),
            pltpu.VMEM((rows, hidden_width), jnp.bfloat16),
        ]
        + [pltpu.VMEM(array.shape, array.dtype) for array in staged],
        in_specs=vmem_specs(len(blocks) + 2 + 2 + 3)
        + [pl.BlockSpec(memory_space=pltpu.HBM)] * len(staged),
        out_specs=vmem_specs(2 + len(staged)),
        scratch_shapes=[
            pltpu.VMEM((rows + block_rows, width), jnp.bfloat16),
            pltpu.VMEM((rows + block_rows, width), jnp.bfloat16),
            pltpu.SemaphoreType.DMA((max(len(staged), 1), 4)),
        ],
        compiler_params=parameters(12),
        cost_estimate=pl.CostEstimate(
            flops=2 * rows * width * (3 * HD + hidden_width),
            bytes_accessed=MIB,
            transcendentals=rows * hidden_width,
        ),
        name=name,
    )(*blocks, *gains, *weights, *tables, *[in_hbm(array) for array in staged])


def last_kernel(*refs):
    block_ref, *normed_refs = refs[:3]
    gain_a, gain_f, heads_ref, upward_ref, downward_ref, output_ref = refs[3:9]
    offsets_ref, *table_refs = refs[9:13]
    own_joined_ref, middle_joined_ref, early_ref = refs[13:16]
    joined_ref, fed_ref, sibling_ref, own_ref = refs[16:20]
    attention_scr, feedforward_scr, hidden_scr = refs[20:]
    block_rows = block_ref.shape[0]
    tokens = joined_ref.shape[0]
    first = tokens - attention_scr.shape[0]
    count = normed_refs[0].shape[0]
    normalize([block_ref], [gain_a, gain_f], [attention_scr, feedforward_scr], count)
    for normed_ref, normed_scr in zip(normed_refs, (attention_scr, feedforward_scr)):
        normed_scr[:count, :] = normed_ref[...]
    early = 3 * block_rows
    middle = early + block_rows
    joined_ref[:block_rows, :] = own_joined_ref[...]
    joined_ref[block_rows:early, :] = middle_joined_ref[: 2 * block_rows, :]
    origins = ((3, 1), (1, 1), (2, 0), (2, 1))
    places = [position_of(kind, half, block_rows) for kind, half in origins]
    project(attention_scr, heads_ref, table_refs, places, joined_ref, first)
    joined_ref[early:middle, :] = joined_ref[first : first + block_rows, :]
    joined_ref[middle : middle + block_rows, :] = middle_joined_ref[2 * block_rows :, :]
    rows = CORES * block_rows
    hide(feedforward_scr, upward_ref, hidden_scr, 0)
    attended = attend(joined_ref, offsets_ref, early - block_rows, rows, block_rows)
    chunk = 256
    for begin in range(0, downward_ref.shape[1], chunk):
        columns = slice(begin, begin + chunk)
        fed = jnp.dot(hidden_scr[...], downward_ref[:, columns], preferred_element_type=jnp.float32)
        fed_ref[:, columns] = fed[block_rows:]
        product = jnp.dot(attended, output_ref[:, columns], preferred_element_type=jnp.float32)
        own_ref[:, columns] = early_ref[early - block_rows : early, columns] + product[:block_rows]
        sibling = fed[:block_rows] + product[block_rows:]
        sibling_ref[:, columns] = sibling.astype(jnp.bfloat16)


def last_rows(block, normed, gains, weights, tables, own_joined, middle_joined, early):
    block_rows, width = block.shape
    rows = normed[0].shape[0] + block_rows
    hidden_width = weights[1].shape[1]
    tokens = CHIPS * CORES * block_rows
    return pl.pallas_call(
        last_kernel,
        out_shape=[
            pltpu.VMEM((tokens, 3 * HD), jnp.bfloat16),
            pltpu.VMEM((rows - block_rows, width), jnp.float32),
            pltpu.VMEM((block_rows, width), jnp.bfloat16),
            pltpu.VMEM((block_rows, width), jnp.float32),
        ],
        in_specs=vmem_specs(1 + 2 + 2 + 4 + 4 + 3),
        out_specs=vmem_specs(4),
        scratch_shapes=[
            pltpu.VMEM((rows, width), jnp.bfloat16),
            pltpu.VMEM((rows, width), jnp.bfloat16),
            pltpu.VMEM((rows, hidden_width), jnp.bfloat16),
        ],
        compiler_params=parameters(12),
        cost_estimate=pl.CostEstimate(
            flops=2 * rows * width * (3 * HD + HD + 2 * hidden_width),
            bytes_accessed=MIB,
            transcendentals=rows * hidden_width,
        ),
        name="last_rows",
    )(block, *normed, *gains, *weights, *tables, own_joined, middle_joined, early)


def fed_kernel(own_hidden_ref, middle_hidden_ref, downward_ref, *refs):
    blocks, gain_refs, (fed_ref, *normed_refs) = refs[:-5], refs[-5:-3], refs[-3:]
    normalize(blocks, gain_refs, normed_refs)
    hidden = jnp.concatenate([own_hidden_ref[...], middle_hidden_ref[...]], 0)
    chunk = 256
    for begin in range(0, downward_ref.shape[1], chunk):
        columns = slice(begin, begin + chunk)
        fed_ref[:, columns] = jnp.dot(
            hidden, downward_ref[:, columns], preferred_element_type=jnp.float32
        )


def fed_rows(own_hidden, middle_hidden, downward_weight, blocks, gains):
    rows = own_hidden.shape[0] + middle_hidden.shape[0]
    depth, width = downward_weight.shape
    normed = pltpu.VMEM((len(blocks) * blocks[0].shape[0], width), jnp.bfloat16)
    return pl.pallas_call(
        fed_kernel,
        out_shape=[pltpu.VMEM((rows, width), jnp.float32), normed, normed],
        in_specs=vmem_specs(5 + len(blocks)),
        out_specs=vmem_specs(3),
        compiler_params=parameters(12),
        cost_estimate=pl.CostEstimate(
            flops=2 * rows * depth * width, bytes_accessed=MIB, transcendentals=0
        ),
        name="fed_rows",
    )(own_hidden, middle_hidden, downward_weight, *blocks, *gains)


def rest_kernel(joined_ref, offsets_ref, output_ref, early_ref, late_ref, *refs):
    near_ref, far_ref, *owns = refs
    block_rows = far_ref.shape[0]
    tokens = joined_ref.shape[0]
    early = CORES * block_rows
    attended = attend(joined_ref, offsets_ref, 0, tokens, block_rows)
    attended = jnp.concatenate([attended[:early], attended[2 * early :]], 0)
    chunk = 512
    for begin in range(0, output_ref.shape[1], chunk):
        columns = slice(begin, begin + chunk)
        fed = jnp.concatenate(
            [
                early_ref[:early, columns],
                early_ref[early + block_rows :, columns],
                late_ref[:, columns],
            ],
            0,
        )
        partial = fed + jnp.dot(
            attended, output_ref[:, columns], preferred_element_type=jnp.float32
        )
        for number, own_ref in enumerate(owns):
            first = CORES * number * block_rows
            middle = first + block_rows
            own_ref[:, columns] = partial[first:middle]
            sibling = partial[middle : middle + block_rows].astype(jnp.bfloat16)
            if number < near_ref.shape[0]:
                near_ref[number, :, columns] = sibling
            else:
                far_ref[:, columns] = sibling


def rest_rows(joined, offsets, output_weight, early, late):
    width = early.shape[1]
    count = CHIPS - 1
    shape = (joined.shape[0] // (CORES * CHIPS), width)
    rows = CORES * count * shape[0]
    shapes = [pltpu.VMEM((count - 1, *shape), jnp.bfloat16), pltpu.VMEM(shape, jnp.bfloat16)]
    shapes += [pltpu.VMEM(shape, jnp.float32)] * count
    return pl.pallas_call(
        rest_kernel,
        out_shape=shapes,
        in_specs=vmem_specs(5),
        out_specs=vmem_specs(2 + count),
        compiler_params=parameters(12),
        cost_estimate=pl.CostEstimate(
            flops=2 * rows * width * HD,
            bytes_accessed=MIB,
            transcendentals=rows * joined.shape[0],
        ),
        name="rest_rows",
    )(joined, offsets, output_weight, early, late)


def pages_kernel(joined_ref, destinations_ref, *page_refs):
    tokens = joined_ref.shape[0]
    slot_rows = page_refs[0].shape[0] * PAGE
    for number, page_ref in enumerate(page_refs):
        shape = (slot_rows, tokens)
        row = number * slot_rows + lax.broadcasted_iota(jnp.int32, shape, 0)
        placing = jnp.where(row == destinations_ref[...], 1.0, 0.0).astype(jnp.bfloat16)
        rows = jnp.dot(placing, joined_ref[:, HD:], preferred_element_type=jnp.float32)
        page_ref[...] = rows.astype(jnp.bfloat16).reshape(page_ref.shape)


def cached_pages(joined, destinations, replica_count):
    tokens = joined.shape[0]
    capacity = 2 * (tokens // PAGE) // replica_count
    shapes = [pltpu.VMEM((capacity, PAGE, 2 * HD), jnp.bfloat16)] * replica_count
    return pl.pallas_call(
        pages_kernel,
        out_shape=shapes,
        in_specs=vmem_specs(2),
        out_specs=vmem_specs(len(shapes)),
        compiler_params=parameters(8),
        cost_estimate=pl.CostEstimate(flops=0, bytes_accessed=MIB, transcendentals=0),
        name="cached_pages",
    )(joined, destinations)


def add_kernel(*refs):
    total = refs[0][...].astype(jnp.float32)
    for ref in refs[1:-1]:
        total = total + ref[...].astype(jnp.float32)
    refs[-1][...] = total.astype(refs[-1].dtype)


def added(name, *parts):
    return pl.pallas_call(
        add_kernel,
        out_shape=pltpu.VMEM(parts[0].shape, jnp.bfloat16),
        in_specs=vmem_specs(len(parts)),
        out_specs=pl.BlockSpec(memory_space=pltpu.VMEM),
        compiler_params=parameters(4),
        name=name,
    )(*parts)


def near_kernel(received_ref, zero_ref, one_ref, hidden_ref, first_ref, base_ref):
    first_ref[...] = (one_ref[...] + received_ref[1].astype(jnp.float32)).astype(jnp.bfloat16)
    zero = zero_ref[...] + received_ref[0].astype(jnp.float32)
    base_ref[...] = zero + hidden_ref[...].astype(jnp.float32)


def near_sums(received, owns, hidden):
    shape = hidden.shape
    return pl.pallas_call(
        near_kernel,
        out_shape=[pltpu.VMEM(shape, jnp.bfloat16), pltpu.VMEM(shape, jnp.float32)],
        in_specs=vmem_specs(4),
        out_specs=vmem_specs(2),
        compiler_params=parameters(4),
        name="near_sums",
    )(received, *owns, hidden)


def place_kernel(masks, *refs):
    group = lax.axis_index("dp")
    count = len(masks)
    pages, (part_ref, base_ref) = refs[:count], refs[count : count + 2]
    cache_ref, total_ref, sems = refs[count + 2 :]
    copies = [
        pltpu.make_async_copy(page_ref, cache_ref.at[0, group ^ mask], sems.at[number])
        for number, (mask, page_ref) in enumerate(zip(masks, pages))
    ]
    for copy in copies:
        copy.start()
    total_ref[...] = base_ref[...] + part_ref[...].astype(jnp.float32)
    for copy in copies:
        copy.wait()


def placed(masks, pages, part, base, replica_count):
    count = len(pages)
    return pl.pallas_call(
        functools.partial(place_kernel, masks),
        out_shape=[
            jax.ShapeDtypeStruct((1, replica_count) + pages[0].shape, pages[0].dtype),
            pltpu.VMEM(base.shape, base.dtype),
        ],
        in_specs=[pl.BlockSpec(memory_space=pl.ANY)] * count + vmem_specs(2),
        out_specs=[pl.BlockSpec(memory_space=pltpu.HBM)] + vmem_specs(1),
        scratch_shapes=[pltpu.SemaphoreType.DMA((count,))],
        compiler_params=parameters(4),
        name="placed",
    )(*pages, part, base)


def finish_kernel(masks, base_ref, *refs):
    count = len(masks)
    *parts, _, output_ref, cache_ref, total_scr, sems = refs
    parts, pages = parts[:-count], parts[-count:]
    group = lax.axis_index("dp")
    copies = [
        pltpu.make_async_copy(page_ref, cache_ref.at[0, group ^ mask], sems.at[number])
        for number, (mask, page_ref) in enumerate(zip(masks, pages))
    ]
    for copy in copies:
        copy.start()
    total = base_ref[...]
    for part_ref in parts:
        total = total + part_ref[...].astype(jnp.float32)
    total_scr[...] = total
    copies.append(pltpu.make_async_copy(total_scr, output_ref, sems.at[count]))
    copies[-1].start()
    for copy in copies:
        copy.wait()


def finished(base, parts, masks, pages, cache):
    count = len(pages)
    return pl.pallas_call(
        functools.partial(finish_kernel, masks),
        out_shape=[
            jax.ShapeDtypeStruct(base.shape, base.dtype),
            jax.ShapeDtypeStruct(cache.shape, cache.dtype),
        ],
        in_specs=vmem_specs(1 + len(parts))
        + [pl.BlockSpec(memory_space=pl.ANY)] * count
        + [pl.BlockSpec(memory_space=pltpu.HBM)],
        out_specs=[pl.BlockSpec(memory_space=pltpu.HBM)] * 2,
        scratch_shapes=[
            pltpu.VMEM(base.shape, base.dtype),
            pltpu.SemaphoreType.DMA((count + 1,)),
        ],
        input_output_aliases={1 + len(parts) + count: 1},
        compiler_params=parameters(4),
        name="finished",
    )(base, *parts, *pages, cache)


def shards_whole_heads(
    hidden_states,
    attention_gain,
    feedforward_gain,
    heads_weight,
    output_weight,
    upward_weight,
    downward_weight,
    segments,
    page_targets,
):
    replica_count = lax.axis_size("dp")
    to_chip = [mask * CORES for mask in range(CHIPS)]
    third = exchanged(hidden_states, "tensor", to_chip[3])
    first = exchanged(hidden_states, "tensor", to_chip[1])
    beside = exchanged(hidden_states, "tensor", 1)
    staged = (
        segments,
        page_targets.reshape(1, -1),
        hidden_states,
        attention_gain[None],
        feedforward_gain[None],
        heads_weight,
        upward_weight,
        downward_weight,
    )
    staged = own_rows(staged, replica_count)
    hidden, gains, weights, tables = staged[2], staged[3:5], staged[5:8], staged[8:12]
    heads, upward, downward = weights
    destinations, own_joined, own_hidden = staged[12:]

    third, own_joined = lax.optimization_barrier((third, own_joined))
    second = exchanged(third, "tensor", to_chip[1])
    middle_joined, middle_hidden, output = middle_rows(
        "middle_rows",
        ((0, 1), (3, 0), (1, 0)),
        (beside, third, first),
        gains,
        (heads, upward),
        tables[1:],
        output_weight,
    )
    third, first, middle_joined = lax.optimization_barrier((third, first, middle_joined))
    first_beside = exchanged(first, "tensor", 1)
    third_beside = exchanged(third, "tensor", 1)
    second, first_beside, third_beside, middle_joined, middle_hidden = lax.optimization_barrier(
        (second, first_beside, third_beside, middle_joined, middle_hidden)
    )
    second_beside = exchanged(second, "tensor", 1)
    fed, *normed = fed_rows(
        own_hidden, middle_hidden, downward, (third_beside, first_beside, second), gains
    )
    joined, fed_late, sibling, own = last_rows(
        second_beside,
        normed,
        gains,
        (heads, upward, downward, output),
        tables,
        own_joined,
        middle_joined,
        fed,
    )

    received = exchanged(sibling, "tensor", 1)
    partials = rest_rows(joined, tables[0], output, fed, fed_late)
    near_sibling, far_sibling, *owns = partials
    near_received = exchanged(near_sibling, "tensor", 1)
    third_sum = added("third_added", own, received)
    third_sum, far_sibling, joined = lax.optimization_barrier((third_sum, far_sibling, joined))
    passing = exchanged(third_sum, "tensor", to_chip[1])
    pages = cached_pages(joined, destinations, replica_count)
    far_sibling, pages = lax.optimization_barrier((far_sibling, pages))
    far_received = exchanged(far_sibling, "tensor", 1)
    early, late = (3,), (2, 1)
    arriving = [exchanged(pages[mask], "dp", mask) for mask in early]
    first_sum, base = near_sums(near_received, owns[:2], hidden)
    from_first = exchanged(first_sum, "tensor", to_chip[1])
    second_sum = added("second_added", owns[2], passing, far_received)
    second_sum, late_pages = lax.optimization_barrier(
        (second_sum, [pages[mask] for mask in late])
    )
    from_second = exchanged(second_sum, "tensor", to_chip[2])
    late_pages = [exchanged(page, "dp", mask) for mask, page in zip(late, late_pages)]
    cache_pages, base = placed((0,) + early, [pages[0]] + arriving, from_first, base, replica_count)
    return tuple(finished(base, (from_second,), late, late_pages, cache_pages))


def solution(mesh):
    whole_heads = mesh.shape["tensor"] == H and mesh.shape["dp"] == 4
    shards = shards_whole_heads if whole_heads else shards_split_heads
    in_specs = (
        P(("dp", "tensor"), None),
        P(),
        P(),
        P(None, "tensor"),
        P("tensor", None),
        P(None, "tensor"),
        P("tensor", None),
        P("dp", None),
        P("dp", None),
    )
    out_specs = (P(("dp", "tensor"), None), P("dp", None, None, None, "tensor"))
    return jax.shard_map(shards, mesh=mesh, in_specs=in_specs, out_specs=out_specs, check_vma=False)
```

```python
import functools
import math

import jax
import jax.numpy as jnp
from jax import lax
from jax.experimental import pallas as pl
from jax.experimental.pallas import tpu as pltpu
from jax.sharding import PartitionSpec as P

H = 8
HD = 256
ROT = 64
PAGE = 16


epsilon = 1e-05
rotary_base = 10000.0
key_block = 256


def shortened(array):

    def short(part):
        return part.astype(jnp.bfloat16) if part.dtype == jnp.float32 else part

    return jax.tree.map(short, array)


def swapped(block, axis, apart):
    count = lax.axis_size(axis)
    route = []
    for low in range(count):
        high = low | 1 << apart
        if high != low and high < count:
            route += [(low, high), (high, low)]
    return lax.ppermute(block, axis, route)


def layer_norm(values, gain):
    floats = values.astype(jnp.float32)
    center = jnp.mean(floats, axis=-1, keepdims=True)
    shifted = floats - center
    spread = jnp.mean(shifted * shifted, axis=-1, keepdims=True)
    return (shifted * lax.rsqrt(spread + epsilon) * gain).astype(jnp.bfloat16)


def positions_of(stream):
    indices = jnp.arange(stream.shape[0], dtype=jnp.int32)
    boundary = jnp.concatenate([jnp.ones((1,), dtype=bool), stream[1:] != stream[:-1]])
    starting = lax.cummax(jnp.where(boundary, indices, jnp.zeros_like(indices)), axis=0)
    return (indices, starting)


def rotate_heads(vectors, offsets, rotary_dims):
    half_dims = rotary_dims // 2
    frequency = jnp.exp(
        jnp.arange(half_dims, dtype=jnp.float32) * (-2.0 * math.log(rotary_base) / rotary_dims)
    )
    angles = offsets.astype(jnp.float32)[:, None] * frequency[None, :]
    cosine = jnp.cos(angles)
    sine = jnp.sin(angles)
    floats = vectors.astype(jnp.float32)
    leading = floats[..., :half_dims]
    trailing = floats[..., half_dims:rotary_dims]
    rotated = jnp.concatenate(
        [
            leading * cosine - trailing * sine,
            trailing * cosine + leading * sine,
            floats[..., rotary_dims:],
        ],
        axis=-1,
    )
    return rotated.astype(jnp.bfloat16)


def shards_split_heads(
    hidden_states,
    attention_gain,
    feedforward_gain,
    heads_weight,
    output_weight,
    upward_weight,
    downward_weight,
    segments,
    page_targets,
):
    tensor_count = lax.axis_size("tensor")
    replica_count = lax.axis_size("dp")
    tensor_index = lax.axis_index("tensor")
    quarters = tensor_count // H
    quarter_width = HD // quarters
    quarter_index = tensor_index % quarters
    stream = segments[0]
    tokens_total = stream.shape[0]
    level_count = quarters.bit_length() - 1
    normed_attention = layer_norm(hidden_states, attention_gain)
    normed_feedforward = layer_norm(hidden_states, feedforward_gain)
    shard_rows = lax.all_gather(
        (normed_attention, normed_feedforward), "tensor", axis=0, tiled=True
    )
    joined_rows = jnp.dot(shard_rows[0], heads_weight, preferred_element_type=jnp.float32).astype(
        jnp.bfloat16
    )
    upward = jnp.dot(shard_rows[1], upward_weight, preferred_element_type=jnp.float32)
    hidden_rows = jax.nn.gelu(upward, approximate=False).astype(jnp.bfloat16)
    hidden = hidden_rows
    pieces = (
        joined_rows.reshape(tokens_total, 3, quarter_width)
        .transpose(1, 0, 2)
        .reshape(1, 3, tokens_total * quarter_width)
    )
    for bit_number in range(level_count):
        partner = swapped(shortened(pieces), "tensor", bit_number).astype(pieces.dtype)
        lower = tensor_index >> bit_number & 1 == 0
        pieces = jnp.where(
            lower, jnp.concatenate([pieces, partner], 0), jnp.concatenate([partner, pieces], 0)
        )
    whole_head = (
        pieces.reshape(quarters, 3, tokens_total, quarter_width)
        .transpose(1, 2, 0, 3)
        .reshape(3, tokens_total, HD)
    )
    indices, starting = positions_of(stream)
    offsets = indices - starting
    queries = rotate_heads(whole_head[0], offsets, ROT)
    keys = rotate_heads(whole_head[1], offsets, ROT)
    values = whole_head[2]
    block_rows = tokens_total // (2 * quarters)
    score_scale = HD ** (-0.5)

    def attend_block(block_number):
        first_row = block_number * block_rows
        block_queries = lax.dynamic_slice_in_dim(queries, first_row, block_rows, 0)
        query_segments = lax.dynamic_slice_in_dim(stream, first_row, block_rows, 0)
        query_indices = first_row + jnp.arange(block_rows, dtype=jnp.int32)
        lowest = lax.dynamic_index_in_dim(starting, first_row, 0, keepdims=False) // key_block
        highest = (first_row + block_rows + key_block - 1) // key_block

        def scores_of(key_number):
            key_first = key_number * key_block
            key_indices = key_first + jnp.arange(key_block, dtype=jnp.int32)
            scores = (
                jnp.dot(block_queries, keys.T, preferred_element_type=jnp.float32) * score_scale
            )
            allowed = (stream[None, :] == query_segments[:, None]) & (
                key_indices[None, :] <= query_indices[:, None]
            )
            return (scores, allowed)

        def find_peak(key_number, peak):
            scores, allowed = scores_of(key_number)
            return jnp.maximum(peak, jnp.max(jnp.where(allowed, scores, -jnp.inf), axis=1))

        peak = lax.fori_loop(
            lowest, highest, find_peak, jnp.full((block_rows,), -jnp.inf, jnp.float32)
        )

        def accumulate(key_number, state):
            weight_sum, mixed_sum = state
            scores, allowed = scores_of(key_number)
            weights = jnp.where(allowed, jnp.exp(scores - peak[:, None]), 0.0)
            mixed_next = mixed_sum + jnp.dot(
                weights.astype(jnp.bfloat16), values, preferred_element_type=jnp.float32
            )
            return (weight_sum + jnp.sum(weights, axis=1), mixed_next)

        start_state = (
            jnp.zeros((block_rows,), jnp.float32),
            jnp.zeros((block_rows, HD), jnp.float32),
        )
        weight_sum, mixed_sum = lax.fori_loop(lowest, highest, accumulate, start_state)
        return (mixed_sum / weight_sum[:, None]).astype(jnp.bfloat16)

    own_blocks = (2 * quarter_index, 2 * quarter_index + 1)
    own_rows = jnp.concatenate([attend_block(own_blocks[0]), attend_block(own_blocks[1])], 0)[None]
    for bit_number in range(level_count):
        partner = swapped(own_rows, "tensor", bit_number)
        lower = tensor_index >> bit_number & 1 == 0
        own_rows = jnp.where(
            lower, jnp.concatenate([own_rows, partner], 0), jnp.concatenate([partner, own_rows], 0)
        )
    attended = own_rows.reshape(tokens_total, HD)
    attended_quarter = lax.dynamic_slice_in_dim(
        attended, quarter_index * quarter_width, quarter_width, 1
    )
    hidden_rows = hidden
    summed = lax.psum_scatter(
        (
            jnp.dot(attended_quarter, output_weight, preferred_element_type=jnp.float32)
            + jnp.dot(hidden_rows, downward_weight, preferred_element_type=jnp.float32)
        ).astype(jnp.bfloat16),
        "tensor",
        scatter_dimension=0,
        tiled=True,
    ).astype(jnp.float32)
    layer_output = hidden_states.astype(jnp.float32) + summed
    key_quarter = lax.dynamic_slice_in_dim(keys, quarter_index * quarter_width, quarter_width, 1)
    value_quarter = joined_rows[:, 2 * quarter_width :]
    page_count = tokens_total // PAGE
    page_rows = jnp.concatenate([key_quarter, value_quarter], 1).reshape(
        page_count, PAGE * 2 * quarter_width
    )
    targets = page_targets[:, 0]
    page_numbers = jnp.arange(page_count, dtype=jnp.int32)
    earlier = jnp.sum(
        (
            (targets[None, :] == targets[:, None]) & (page_numbers[None, :] < page_numbers[:, None])
        ).astype(jnp.int32),
        axis=1,
    )
    capacity = 2 * page_count // replica_count
    slot_numbers = targets * capacity + earlier
    placing = (
        jnp.arange(replica_count * capacity, dtype=jnp.int32)[:, None] == slot_numbers[None, :]
    ).astype(jnp.bfloat16)
    outgoing = jnp.dot(placing, page_rows, preferred_element_type=jnp.float32).astype(jnp.bfloat16)
    outgoing = outgoing.reshape(replica_count, capacity, PAGE * 2 * quarter_width)
    incoming = lax.all_to_all(outgoing, "dp", split_axis=0, concat_axis=0, tiled=True)
    cache_pages = incoming.reshape(1, replica_count, capacity, PAGE, 2 * quarter_width)
    return (layer_output, cache_pages)


CORES = 2
CHIPS = 4
MIB = 1 << 20


def in_hbm(array):
    return pltpu.with_memory_space_constraint(array, pltpu.HBM)


def exchanged(block, axis, mask):
    count = lax.axis_size(axis)
    return lax.ppermute(block, axis, [(member, member ^ mask) for member in range(count)])


def vmem_specs(count):
    return [pl.BlockSpec(memory_space=pltpu.VMEM)] * count


def parameters(mebibytes):
    return pltpu.CompilerParams(vmem_limit_bytes=mebibytes * MIB)


def whereabouts():
    member = lax.axis_index("tensor")
    return member // CORES, member % CORES


ORDER = (0, 3, 1, 2)


def position_of(kind, half, block_rows):
    chip, core = whereabouts()
    return ((chip ^ kind) * CORES + (core ^ half)) * block_rows


def positions_along(first, shape, axis, block_rows):
    chip, core = whereabouts()
    bits = block_rows.bit_length() - 1
    place = first + lax.broadcasted_iota(jnp.int32, shape, axis)
    stand = place >> (bits + 1)
    kind = jnp.where(stand == 1, ORDER[1], jnp.maximum(stand - 1, 0))
    half = (place >> bits) & 1
    return ((((chip ^ kind) << 1) | (core ^ half)) << bits) | (place & (block_rows - 1))


def normalize(blocks, gain_refs, normed_refs, place=0):
    piece = 16
    gains = [gain_ref[...] for gain_ref in gain_refs]
    for number, block_ref in enumerate(blocks):
        block_rows = block_ref.shape[0]
        for part in range(0, block_rows, piece):
            floats = block_ref[part : part + piece, :].astype(jnp.float32)
            center = jnp.mean(floats, axis=-1, keepdims=True)
            shifted = floats - center
            spread = jnp.mean(shifted * shifted, axis=-1, keepdims=True)
            scaled = shifted * lax.rsqrt(spread + epsilon)
            first = place + number * block_rows + part
            for gain, normed_ref in zip(gains, normed_refs):
                normed_ref[first : first + piece, :] = (scaled * gain).astype(jnp.bfloat16)


def project(normed_ref, heads_ref, table_refs, places, joined_ref, first):
    block_rows = normed_ref.shape[0] // (4 if len(places) == 3 else len(places))
    rows = block_rows * len(places)
    own = slice(first, first + rows)
    cosine, sine_down, sine_up = [
        jnp.concatenate(
            [
                table_ref[pl.ds(pl.multiple_of(place, block_rows), block_rows), :]
                for place in places
            ],
            0,
        )
        for table_ref in table_refs
    ]
    for begin in range(0, heads_ref.shape[1], HD):
        columns = slice(begin, begin + HD)
        joined = jnp.dot(
            normed_ref[...], heads_ref[:, columns], preferred_element_type=jnp.float32
        )
        joined_ref[own, columns] = joined[:rows].astype(jnp.bfloat16)
    for begin in (0, HD):
        columns = slice(begin, begin + 128)
        turning = joined_ref[own, columns].astype(jnp.float32)
        turned = (
            turning * cosine
            + pltpu.roll(turning, 128 - ROT // 2, 1) * sine_down
            + pltpu.roll(turning, ROT // 2, 1) * sine_up
        )
        joined_ref[own, columns] = turned.astype(jnp.bfloat16)


def hide(normed_ref, upward_ref, hidden_ref, place, chunk=256):
    count = min(normed_ref.shape[0], hidden_ref.shape[0] - place)
    rows = slice(place, place + count)
    for first in range(0, upward_ref.shape[1], chunk):
        columns = slice(first, first + chunk)
        upward = jnp.dot(
            normed_ref[...], upward_ref[:, columns], preferred_element_type=jnp.float32
        )
        hidden = 0.5 * upward * (1.0 + lax.erf(upward * (0.5**0.5)))
        hidden_ref[rows, columns] = hidden[:count].astype(jnp.bfloat16)


def attend(joined_ref, offsets_ref, first, rows, block_rows):
    tokens = joined_ref.shape[0]
    starts = [
        position_of(ORDER[place // (2 * block_rows)], (place // block_rows) % 2, block_rows)
        for place in range(first, first + rows, block_rows)
    ]
    reach = jnp.concatenate(
        [
            offsets_ref[pl.ds(pl.multiple_of(start, block_rows), block_rows), :]
            for start in starts
        ],
        0,
    )[:, :1].astype(jnp.int32)
    row = positions_along(first, (rows, 1), 0, block_rows)
    column = positions_along(0, (1, tokens), 1, block_rows)
    allowed = (column <= row) & (column >= row - reach)
    scores = lax.dot_general(
        joined_ref[first : first + rows, :HD],
        joined_ref[:, HD : 2 * HD],
        (((1,), (1,)), ((), ())),
        preferred_element_type=jnp.float32,
    ) * (HD ** (-0.5))
    peak = jnp.max(jnp.where(allowed, scores, -jnp.inf), axis=1, keepdims=True)
    weights = jnp.where(allowed, jnp.exp(scores - peak), 0.0)
    weight_sum = jnp.sum(weights, axis=1, keepdims=True)
    mixed = jnp.dot(
        weights.astype(jnp.bfloat16), joined_ref[:, 2 * HD :], preferred_element_type=jnp.float32
    )
    return (mixed / weight_sum).astype(jnp.bfloat16)


def make_tables(segments_ref, offsets_ref, cosine_ref, sine_down_ref, sine_up_ref):
    tokens = segments_ref.shape[1]
    shape = (tokens, tokens)
    rows = lax.broadcasted_iota(jnp.int32, shape, 0)
    columns = lax.broadcasted_iota(jnp.int32, shape, 1)
    across = jnp.broadcast_to(segments_ref[...], shape).astype(jnp.float32)
    down = jnp.sum(jnp.where(rows == columns, across, 0.0), axis=1, keepdims=True)
    earlier = (across == down) & (columns < rows)
    offsets = jnp.sum(jnp.where(earlier, 1.0, 0.0), axis=1, keepdims=True)
    offsets_ref[...] = jnp.broadcast_to(offsets, offsets_ref.shape)
    half = ROT // 2
    lane = lax.broadcasted_iota(jnp.int32, (tokens, 128), 1)
    step = (lane & (half - 1)).astype(jnp.float32)
    frequency = jnp.exp(step * (-2.0 * math.log(rotary_base) / ROT))
    angles = offsets * frequency
    sine = jnp.sin(angles)
    cosine_ref[...] = jnp.where(lane < ROT, jnp.cos(angles), 1.0)
    sine_down_ref[...] = jnp.where(lane < half, -sine, 0.0)
    sine_up_ref[...] = jnp.where((lane >= half) & (lane < ROT), sine, 0.0)


def make_destinations(targets_ref, destinations_ref, replica_count, block_rows):
    page_count = targets_ref.shape[1]
    tokens = destinations_ref.shape[1]
    capacity = 2 * page_count // replica_count
    square = (page_count, page_count)
    rows = lax.broadcasted_iota(jnp.int32, square, 0)
    columns = lax.broadcasted_iota(jnp.int32, square, 1)
    across = jnp.broadcast_to(targets_ref[...], square).astype(jnp.float32)
    down = jnp.sum(jnp.where(rows == columns, across, 0.0), axis=1, keepdims=True)
    earlier = jnp.where((across == down) & (columns < rows), 1.0, 0.0)
    slots = jnp.sum(earlier, axis=1, keepdims=True).astype(jnp.int32)
    slots = (down.astype(jnp.int32) ^ lax.axis_index("dp")) * capacity + slots
    positions = positions_along(0, (1, tokens), 1, block_rows)
    bits = PAGE.bit_length() - 1
    pages = lax.broadcasted_iota(jnp.int32, (page_count, tokens), 0)
    chosen = jnp.where(pages == positions >> bits, slots.astype(jnp.float32), 0.0)
    slot = jnp.sum(chosen, axis=0, keepdims=True).astype(jnp.int32)
    destinations_ref[...] = slot * PAGE + (positions & (PAGE - 1))


def copies_in(sources, targets, sems):
    copies = []
    for number, (source, target) in enumerate(zip(sources, targets)):
        parts = 4 if source.shape[0] >= 256 else 1
        rows = source.shape[0] // parts
        places = [pl.ds(part * rows, rows) for part in range(parts)]
        copies.append(
            [
                pltpu.make_async_copy(source.at[place], target.at[place], sems.at[number, part])
                for part, place in enumerate(places)
            ]
        )
    for copy in sum(copies, []):
        copy.start()
    return copies


def wait_for(copies):
    for copy in copies:
        copy.wait()


def own_kernel(count, replica_count, *refs):
    sources, targets = refs[:count], refs[count : 2 * count]
    offsets_ref, *table_refs, destinations_ref, joined_ref, hidden_ref = refs[2 * count : -3]
    attention_scr, feedforward_scr, sems = refs[-3:]
    copies = copies_in(sources, targets, sems)
    segments_ref, targets_ref, states_ref, *gain_refs, heads_ref, upward_ref, _ = targets
    block_rows = states_ref.shape[0]
    wait_for(copies[0])
    make_tables(segments_ref, offsets_ref, *table_refs)
    wait_for(copies[1])
    make_destinations(targets_ref, destinations_ref, replica_count, block_rows)
    for number in (2, 3, 4):
        wait_for(copies[number])
    normalize([states_ref], gain_refs, [attention_scr, feedforward_scr])
    wait_for(copies[5])
    places = [position_of(0, 0, block_rows)]
    project(attention_scr, heads_ref, table_refs, places, joined_ref, 0)
    wait_for(copies[6])
    hide(feedforward_scr, upward_ref, hidden_ref, 0)
    wait_for(copies[7])


def own_rows(staged, replica_count):
    tokens = staged[0].shape[1]
    rows, width = staged[2].shape
    hidden_width = staged[6].shape[1]
    shapes = [pltpu.VMEM(array.shape, array.dtype) for array in staged]
    shapes += [pltpu.VMEM((tokens, 128), jnp.float32)] * 4
    shapes += [
        pltpu.VMEM((1, tokens), jnp.int32),
        pltpu.VMEM((rows, 3 * HD), jnp.bfloat16),
        pltpu.VMEM((rows, hidden_width), jnp.bfloat16),
    ]
    count = len(staged)
    return pl.pallas_call(
        functools.partial(own_kernel, count, replica_count),
        out_shape=shapes,
        in_specs=[pl.BlockSpec(memory_space=pltpu.HBM)] * count,
        out_specs=vmem_specs(len(shapes)),
        scratch_shapes=[
            pltpu.VMEM((rows, width), jnp.bfloat16),
            pltpu.VMEM((rows, width), jnp.bfloat16),
            pltpu.SemaphoreType.DMA((count, 4)),
        ],
        compiler_params=parameters(12),
        cost_estimate=pl.CostEstimate(
            flops=2 * rows * width * (3 * HD + hidden_width),
            bytes_accessed=sum(array.nbytes for array in staged),
            transcendentals=rows * hidden_width,
        ),
        name="own_rows",
    )(*[in_hbm(array) for array in staged])


def middle_kernel(origins, *refs):
    count = len(origins)
    blocks, (gain_a, gain_f, heads_ref, upward_ref) = refs[:count], refs[count : count + 4]
    table_refs, refs = refs[count + 4 : count + 7], refs[count + 7 :]
    staged = (len(refs) - 5) // 2
    sources, (joined_ref, hidden_ref), refs = refs[:staged], refs[staged:][:2], refs[staged + 2 :]
    targets, (attention_scr, feedforward_scr, sems) = refs[:staged], refs[staged:]
    copies = copies_in(sources, targets, sems)
    block_rows = blocks[0].shape[0]
    normalize(blocks, [gain_a, gain_f], [attention_scr, feedforward_scr])
    for normed_scr in (attention_scr, feedforward_scr):
        normed_scr[count * block_rows :, :] = jnp.zeros((block_rows, normed_scr.shape[1]), jnp.bfloat16)
    places = [position_of(kind, half, block_rows) for kind, half in origins]
    project(attention_scr, heads_ref, table_refs, places, joined_ref, 0)
    hide(feedforward_scr, upward_ref, hidden_ref, 0)
    wait_for(sum(copies, []))


def middle_rows(name, origins, blocks, gains, weights, tables, *staged):
    block_rows, width = blocks[0].shape
    rows = len(blocks) * block_rows
    hidden_width = weights[1].shape[1]
    return pl.pallas_call(
        functools.partial(middle_kernel, origins),
        out_shape=[
            pltpu.VMEM((rows, 3 * HD), jnp.bfloat16),
            pltpu.VMEM((rows, hidden_width), jnp.bfloat16),
        ]
        + [pltpu.VMEM(array.shape, array.dtype) for array in staged],
        in_specs=vmem_specs(len(blocks) + 2 + 2 + 3)
        + [pl.BlockSpec(memory_space=pltpu.HBM)] * len(staged),
        out_specs=vmem_specs(2 + len(staged)),
        scratch_shapes=[
            pltpu.VMEM((rows + block_rows, width), jnp.bfloat16),
            pltpu.VMEM((rows + block_rows, width), jnp.bfloat16),
            pltpu.SemaphoreType.DMA((max(len(staged), 1), 4)),
        ],
        compiler_params=parameters(12),
        cost_estimate=pl.CostEstimate(
            flops=2 * rows * width * (3 * HD + hidden_width),
            bytes_accessed=MIB,
            transcendentals=rows * hidden_width,
        ),
        name=name,
    )(*blocks, *gains, *weights, *tables, *[in_hbm(array) for array in staged])


def last_kernel(*refs):
    block_ref, *normed_refs = refs[:3]
    gain_a, gain_f, heads_ref, upward_ref, downward_ref, output_ref = refs[3:9]
    offsets_ref, *table_refs = refs[9:13]
    own_joined_ref, middle_joined_ref, early_ref = refs[13:16]
    joined_ref, fed_ref, sibling_ref, own_ref = refs[16:20]
    attention_scr, feedforward_scr, hidden_scr = refs[20:]
    block_rows = block_ref.shape[0]
    tokens = joined_ref.shape[0]
    first = tokens - attention_scr.shape[0]
    count = normed_refs[0].shape[0]
    normalize([block_ref], [gain_a, gain_f], [attention_scr, feedforward_scr], count)
    for normed_ref, normed_scr in zip(normed_refs, (attention_scr, feedforward_scr)):
        normed_scr[:count, :] = normed_ref[...]
    early = 3 * block_rows
    middle = early + block_rows
    joined_ref[:block_rows, :] = own_joined_ref[...]
    joined_ref[block_rows:early, :] = middle_joined_ref[: 2 * block_rows, :]
    origins = ((3, 1), (1, 1), (2, 0), (2, 1))
    places = [position_of(kind, half, block_rows) for kind, half in origins]
    project(attention_scr, heads_ref, table_refs, places, joined_ref, first)
    joined_ref[early:middle, :] = joined_ref[first : first + block_rows, :]
    joined_ref[middle : middle + block_rows, :] = middle_joined_ref[2 * block_rows :, :]
    rows = CORES * block_rows
    hide(feedforward_scr, upward_ref, hidden_scr, 0, 512)
    attended = attend(joined_ref, offsets_ref, early - block_rows, rows, block_rows)
    chunk = 512
    for begin in range(0, downward_ref.shape[1], chunk):
        columns = slice(begin, begin + chunk)
        fed = jnp.dot(hidden_scr[...], downward_ref[:, columns], preferred_element_type=jnp.float32)
        fed_ref[:, columns] = fed[block_rows:]
        product = jnp.dot(attended, output_ref[:, columns], preferred_element_type=jnp.float32)
        own_ref[:, columns] = early_ref[early - block_rows : early, columns] + product[:block_rows]
        sibling = fed[:block_rows] + product[block_rows:]
        sibling_ref[:, columns] = sibling.astype(jnp.bfloat16)


def last_rows(block, normed, gains, weights, tables, own_joined, middle_joined, early):
    block_rows, width = block.shape
    rows = normed[0].shape[0] + block_rows
    hidden_width = weights[1].shape[1]
    tokens = CHIPS * CORES * block_rows
    return pl.pallas_call(
        last_kernel,
        out_shape=[
            pltpu.VMEM((tokens, 3 * HD), jnp.bfloat16),
            pltpu.VMEM((rows - block_rows, width), jnp.float32),
            pltpu.VMEM((block_rows, width), jnp.bfloat16),
            pltpu.VMEM((block_rows, width), jnp.float32),
        ],
        in_specs=vmem_specs(1 + 2 + 2 + 4 + 4 + 3),
        out_specs=vmem_specs(4),
        scratch_shapes=[
            pltpu.VMEM((rows, width), jnp.bfloat16),
            pltpu.VMEM((rows, width), jnp.bfloat16),
            pltpu.VMEM((rows, hidden_width), jnp.bfloat16),
        ],
        compiler_params=parameters(12),
        cost_estimate=pl.CostEstimate(
            flops=2 * rows * width * (3 * HD + HD + 2 * hidden_width),
            bytes_accessed=MIB,
            transcendentals=rows * hidden_width,
        ),
        name="last_rows",
    )(block, *normed, *gains, *weights, *tables, own_joined, middle_joined, early)


def fed_kernel(own_hidden_ref, middle_hidden_ref, downward_ref, *refs):
    blocks, gain_refs, (fed_ref, *normed_refs) = refs[:-5], refs[-5:-3], refs[-3:]
    normalize(blocks, gain_refs, normed_refs)
    hidden = jnp.concatenate([own_hidden_ref[...], middle_hidden_ref[...]], 0)
    chunk = 512
    for begin in range(0, downward_ref.shape[1], chunk):
        columns = slice(begin, begin + chunk)
        fed_ref[:, columns] = jnp.dot(
            hidden, downward_ref[:, columns], preferred_element_type=jnp.float32
        )


def fed_rows(own_hidden, middle_hidden, downward_weight, blocks, gains):
    rows = own_hidden.shape[0] + middle_hidden.shape[0]
    depth, width = downward_weight.shape
    normed = pltpu.VMEM((len(blocks) * blocks[0].shape[0], width), jnp.bfloat16)
    return pl.pallas_call(
        fed_kernel,
        out_shape=[pltpu.VMEM((rows, width), jnp.float32), normed, normed],
        in_specs=vmem_specs(5 + len(blocks)),
        out_specs=vmem_specs(3),
        compiler_params=parameters(12),
        cost_estimate=pl.CostEstimate(
            flops=2 * rows * depth * width, bytes_accessed=MIB, transcendentals=0
        ),
        name="fed_rows",
    )(own_hidden, middle_hidden, downward_weight, *blocks, *gains)


def rest_kernel(joined_ref, offsets_ref, output_ref, early_ref, late_ref, *refs):
    near_ref, far_ref, *owns = refs
    block_rows = far_ref.shape[0]
    tokens = joined_ref.shape[0]
    early = CORES * block_rows
    attended = attend(joined_ref, offsets_ref, 0, tokens, block_rows)
    attended = jnp.concatenate([attended[:early], attended[2 * early :]], 0)
    chunk = 512
    for begin in range(0, output_ref.shape[1], chunk):
        columns = slice(begin, begin + chunk)
        fed = jnp.concatenate(
            [
                early_ref[:early, columns],
                early_ref[early + block_rows :, columns],
                late_ref[:, columns],
            ],
            0,
        )
        partial = fed + jnp.dot(
            attended, output_ref[:, columns], preferred_element_type=jnp.float32
        )
        for number, own_ref in enumerate(owns):
            first = CORES * number * block_rows
            middle = first + block_rows
            own_ref[:, columns] = partial[first:middle]
            sibling = partial[middle : middle + block_rows].astype(jnp.bfloat16)
            if number < near_ref.shape[0]:
                near_ref[number, :, columns] = sibling
            else:
                far_ref[:, columns] = sibling


def rest_rows(joined, offsets, output_weight, early, late):
    width = early.shape[1]
    count = CHIPS - 1
    shape = (joined.shape[0] // (CORES * CHIPS), width)
    rows = CORES * count * shape[0]
    shapes = [pltpu.VMEM((count - 1, *shape), jnp.bfloat16), pltpu.VMEM(shape, jnp.bfloat16)]
    shapes += [pltpu.VMEM(shape, jnp.float32)] * count
    return pl.pallas_call(
        rest_kernel,
        out_shape=shapes,
        in_specs=vmem_specs(5),
        out_specs=vmem_specs(2 + count),
        compiler_params=parameters(12),
        cost_estimate=pl.CostEstimate(
            flops=2 * rows * width * HD,
            bytes_accessed=MIB,
            transcendentals=rows * joined.shape[0],
        ),
        name="rest_rows",
    )(joined, offsets, output_weight, early, late)


def pages_kernel(joined_ref, destinations_ref, *page_refs):
    tokens = joined_ref.shape[0]
    slot_rows = page_refs[0].shape[0] * PAGE
    for number, page_ref in enumerate(page_refs):
        shape = (slot_rows, tokens)
        row = number * slot_rows + lax.broadcasted_iota(jnp.int32, shape, 0)
        placing = jnp.where(row == destinations_ref[...], 1.0, 0.0).astype(jnp.bfloat16)
        rows = jnp.dot(placing, joined_ref[:, HD:], preferred_element_type=jnp.float32)
        page_ref[...] = rows.astype(jnp.bfloat16).reshape(page_ref.shape)


def cached_pages(joined, destinations, replica_count):
    tokens = joined.shape[0]
    capacity = 2 * (tokens // PAGE) // replica_count
    shapes = [pltpu.VMEM((capacity, PAGE, 2 * HD), jnp.bfloat16)] * replica_count
    return pl.pallas_call(
        pages_kernel,
        out_shape=shapes,
        in_specs=vmem_specs(2),
        out_specs=vmem_specs(len(shapes)),
        compiler_params=parameters(8),
        cost_estimate=pl.CostEstimate(flops=0, bytes_accessed=MIB, transcendentals=0),
        name="cached_pages",
    )(joined, destinations)


def add_kernel(*refs):
    total = refs[0][...].astype(jnp.float32)
    for ref in refs[1:-1]:
        total = total + ref[...].astype(jnp.float32)
    refs[-1][...] = total.astype(refs[-1].dtype)


def added(name, *parts):
    return pl.pallas_call(
        add_kernel,
        out_shape=pltpu.VMEM(parts[0].shape, jnp.bfloat16),
        in_specs=vmem_specs(len(parts)),
        out_specs=pl.BlockSpec(memory_space=pltpu.VMEM),
        compiler_params=parameters(4),
        name=name,
    )(*parts)


def near_kernel(received_ref, zero_ref, one_ref, hidden_ref, first_ref, base_ref):
    first_ref[...] = (one_ref[...] + received_ref[1].astype(jnp.float32)).astype(jnp.bfloat16)
    zero = zero_ref[...] + received_ref[0].astype(jnp.float32)
    base_ref[...] = zero + hidden_ref[...].astype(jnp.float32)


def near_sums(received, owns, hidden):
    shape = hidden.shape
    return pl.pallas_call(
        near_kernel,
        out_shape=[pltpu.VMEM(shape, jnp.bfloat16), pltpu.VMEM(shape, jnp.float32)],
        in_specs=vmem_specs(4),
        out_specs=vmem_specs(2),
        compiler_params=parameters(4),
        name="near_sums",
    )(received, *owns, hidden)


def place_kernel(masks, *refs):
    group = lax.axis_index("dp")
    count = len(masks)
    pages, (part_ref, base_ref) = refs[:count], refs[count : count + 2]
    cache_ref, total_ref, sems = refs[count + 2 :]
    copies = [
        pltpu.make_async_copy(page_ref, cache_ref.at[0, group ^ mask], sems.at[number])
        for number, (mask, page_ref) in enumerate(zip(masks, pages))
    ]
    for copy in copies:
        copy.start()
    total_ref[...] = base_ref[...] + part_ref[...].astype(jnp.float32)
    for copy in copies:
        copy.wait()


def placed(masks, pages, part, base, replica_count):
    count = len(pages)
    return pl.pallas_call(
        functools.partial(place_kernel, masks),
        out_shape=[
            jax.ShapeDtypeStruct((1, replica_count) + pages[0].shape, pages[0].dtype),
            pltpu.VMEM(base.shape, base.dtype),
        ],
        in_specs=[pl.BlockSpec(memory_space=pl.ANY)] * count + vmem_specs(2),
        out_specs=[pl.BlockSpec(memory_space=pltpu.HBM)] + vmem_specs(1),
        scratch_shapes=[pltpu.SemaphoreType.DMA((count,))],
        compiler_params=parameters(4),
        name="placed",
    )(*pages, part, base)


def finish_kernel(masks, base_ref, *refs):
    count = len(masks)
    *parts, _, output_ref, cache_ref, total_scr, sems = refs
    parts, pages = parts[:-count], parts[-count:]
    group = lax.axis_index("dp")
    copies = [
        pltpu.make_async_copy(page_ref, cache_ref.at[0, group ^ mask], sems.at[number])
        for number, (mask, page_ref) in enumerate(zip(masks, pages))
    ]
    for copy in copies:
        copy.start()
    total = base_ref[...]
    for part_ref in parts:
        total = total + part_ref[...].astype(jnp.float32)
    total_scr[...] = total
    copies.append(pltpu.make_async_copy(total_scr, output_ref, sems.at[count]))
    copies[-1].start()
    for copy in copies:
        copy.wait()


def finished(base, parts, masks, pages, cache):
    count = len(pages)
    return pl.pallas_call(
        functools.partial(finish_kernel, masks),
        out_shape=[
            jax.ShapeDtypeStruct(base.shape, base.dtype),
            jax.ShapeDtypeStruct(cache.shape, cache.dtype),
        ],
        in_specs=vmem_specs(1 + len(parts))
        + [pl.BlockSpec(memory_space=pl.ANY)] * count
        + [pl.BlockSpec(memory_space=pltpu.HBM)],
        out_specs=[pl.BlockSpec(memory_space=pltpu.HBM)] * 2,
        scratch_shapes=[
            pltpu.VMEM(base.shape, base.dtype),
            pltpu.SemaphoreType.DMA((count + 1,)),
        ],
        input_output_aliases={1 + len(parts) + count: 1},
        compiler_params=parameters(4),
        name="finished",
    )(base, *parts, *pages, cache)


def shards_whole_heads(
    hidden_states,
    attention_gain,
    feedforward_gain,
    heads_weight,
    output_weight,
    upward_weight,
    downward_weight,
    segments,
    page_targets,
):
    replica_count = lax.axis_size("dp")
    to_chip = [mask * CORES for mask in range(CHIPS)]
    third = exchanged(hidden_states, "tensor", to_chip[3])
    first = exchanged(hidden_states, "tensor", to_chip[1])
    beside = exchanged(hidden_states, "tensor", 1)
    staged = (
        segments,
        page_targets.reshape(1, -1),
        hidden_states,
        attention_gain[None],
        feedforward_gain[None],
        heads_weight,
        upward_weight,
        downward_weight,
    )
    staged = own_rows(staged, replica_count)
    hidden, gains, weights, tables = staged[2], staged[3:5], staged[5:8], staged[8:12]
    heads, upward, downward = weights
    destinations, own_joined, own_hidden = staged[12:]

    third, own_joined = lax.optimization_barrier((third, own_joined))
    second = exchanged(third, "tensor", to_chip[1])
    middle_joined, middle_hidden, output = middle_rows(
        "middle_rows",
        ((0, 1), (3, 0), (1, 0)),
        (beside, third, first),
        gains,
        (heads, upward),
        tables[1:],
        output_weight,
    )
    third, first, middle_joined = lax.optimization_barrier((third, first, middle_joined))
    first_beside = exchanged(first, "tensor", 1)
    third_beside = exchanged(third, "tensor", 1)
    second, first_beside, third_beside, middle_joined, middle_hidden = lax.optimization_barrier(
        (second, first_beside, third_beside, middle_joined, middle_hidden)
    )
    second_beside = exchanged(second, "tensor", 1)
    fed, *normed = fed_rows(
        own_hidden, middle_hidden, downward, (third_beside, first_beside, second), gains
    )
    joined, fed_late, sibling, own = last_rows(
        second_beside,
        normed,
        gains,
        (heads, upward, downward, output),
        tables,
        own_joined,
        middle_joined,
        fed,
    )

    received = exchanged(sibling, "tensor", 1)
    partials = rest_rows(joined, tables[0], output, fed, fed_late)
    near_sibling, far_sibling, *owns = partials
    near_received = exchanged(near_sibling, "tensor", 1)
    third_sum = added("third_added", own, received)
    third_sum, far_sibling, joined = lax.optimization_barrier((third_sum, far_sibling, joined))
    passing = exchanged(third_sum, "tensor", to_chip[1])
    pages = cached_pages(joined, destinations, replica_count)
    far_sibling, pages = lax.optimization_barrier((far_sibling, pages))
    far_received = exchanged(far_sibling, "tensor", 1)
    early, late = (3,), (2, 1)
    arriving = [exchanged(pages[mask], "dp", mask) for mask in early]
    first_sum, base = near_sums(near_received, owns[:2], hidden)
    from_first = exchanged(first_sum, "tensor", to_chip[1])
    second_sum = added("second_added", owns[2], passing, far_received)
    second_sum, late_pages = lax.optimization_barrier(
        (second_sum, [pages[mask] for mask in late])
    )
    from_second = exchanged(second_sum, "tensor", to_chip[2])
    late_pages = [exchanged(page, "dp", mask) for mask, page in zip(late, late_pages)]
    cache_pages, base = placed((0,) + early, [pages[0]] + arriving, from_first, base, replica_count)
    return tuple(finished(base, (from_second,), late, late_pages, cache_pages))


def solution(mesh):
    whole_heads = mesh.shape["tensor"] == H and mesh.shape["dp"] == 4
    shards = shards_whole_heads if whole_heads else shards_split_heads
    in_specs = (
        P(("dp", "tensor"), None),
        P(),
        P(),
        P(None, "tensor"),
        P("tensor", None),
        P(None, "tensor"),
        P("tensor", None),
        P("dp", None),
        P("dp", None),
    )
    out_specs = (P(("dp", "tensor"), None), P("dp", None, None, None, "tensor"))
    return jax.shard_map(shards, mesh=mesh, in_specs=in_specs, out_specs=out_specs, check_vma=False)
```
